32 devices in a mesh: row: 2 (over core), col: 16 (over z, y, x).
Axes of the slice: x: 2, y: 2, z: 4, core: 2. Of those that a mesh axis runs over, the one named last changes fastest.
Arguments:
- signal: bfloat16 [65536, 512], P(('row', 'col')), may hold values from -6 to 6
- features: bfloat16 [65536, 80], P(('row', 'col')), may hold values from -6 to 6
- position: int32 [65536], P(('row', 'col')), may hold values from 0 to 15999, as said below
- valid: int32 [65536], P(('row', 'col')), may hold values 0 or 1
- w_past: bfloat16 [512, 1024], replicated, may hold values from -0.1875 to 0.1875
- w_now: bfloat16 [512, 1024], replicated, may hold values from -0.1875 to 0.1875
- b_conv: float32 [1024], replicated, may hold values from -2 to 2
- w_cond: bfloat16 [80, 1024], replicated, may hold values from -0.3125 to 0.3125
- w_res: bfloat16 [512, 512], replicated, may hold values from -0.75 to 0.75
- b_res: float32 [512], replicated, may hold values from -2 to 2
- w_skip: bfloat16 [512, 512], replicated, may hold values from -0.75 to 0.75
- b_skip: float32 [512], replicated, may hold values from -2 to 2
- grad_out: bfloat16 [65536, 512], P(('row', 'col')), may hold values from -6 to 6
- grad_skip: bfloat16 [65536, 512], P(('row', 'col')), may hold values from -6 to 6
Outputs:
- output: bfloat16 [65536, 512], P(('row', 'col'))
- skip_out: bfloat16 [65536, 512], P(('row', 'col'))
- grad_signal: float32 [65536, 512], P(('row', 'col'))
- grad_features: float32 [65536, 80], P(('row', 'col'))
- grad_w_past: float32 [512, 1024], replicated
- grad_w_now: float32 [512, 1024], replicated
- grad_b_conv: float32 [1024], replicated
- grad_w_cond: float32 [80, 1024], replicated
- grad_w_res: float32 [512, 512], replicated
- grad_b_res: float32 [512], replicated
- grad_w_skip: float32 [512, 512], replicated
- grad_b_skip: float32 [512], replicated
The draws below stay inside these ranges and needn't reach their ends.
Inputs may be any that keep to these rules, and one draw needn't show every extreme that they name: position counts up by one from sample to sample and falls to 0 where a clip begins; clips hold 2000 to 16000 samples, except the first and last, which may be cut; one clip has exactly 16000.
All inputs are finite; a program needn't handle non-finite values. No bound on the sum of `valid` on one device may be relied on, other than what follows from the above.
Results may differ from the reference program's by a relative error of at most 0.0047.
Values may be sent and summed in bfloat16 or wider, within the bound.
No kernel may reach another device: no remote copies, remote signals or barrier semaphores. Data moves between devices by JAX's collectives and lax.ppermute only.
A program may use at most 128 MiB of HBM per device.

```python
import jax
import jax.numpy as jnp
from jax import lax

RESIDUAL_WIDTH = 512
G = 1024
H = 512
S = 512
C = 80
DILATION_STEP = 256
CLIP_MIN = 2000
CLIP_MAX = 16000
TOKENS = 65536


def draw_position(key, part):
    key = jax.random.fold_in(key, 11)
    first_key, length_key = jax.random.split(key)
    count = TOKENS // CLIP_MIN + 2
    lengths = jax.random.randint(length_key, (count,), CLIP_MIN, CLIP_MAX + 1, dtype=jnp.int32)
    lengths = lengths.at[1].set(CLIP_MAX)
    lengths = lengths.at[0].set(jax.random.randint(first_key, (), 1, CLIP_MAX + 1, dtype=jnp.int32))
    starts = jnp.cumsum(lengths) - lengths
    marks = jnp.zeros((TOKENS,), jnp.int32).at[starts].set(1, mode='drop')
    marks = marks.at[0].set(1)
    index = jnp.arange(TOKENS, dtype=jnp.int32)
    begins = lax.cummax(jnp.where(marks > 0, index, 0), axis=0)
    return index - begins


def place_ends(drawn, rng, low, top_value):
    dims = drawn.shape
    spot = [jax.random.randint(jax.random.fold_in(rng, axis), (), 0, dims[axis]) for axis in range(len(dims))]
    drawn = drawn.at[tuple(spot)].set(low)
    longest = dims.index(max(dims))
    spot[longest] = (spot[longest] + 1) % dims[longest]
    return drawn.at[tuple(spot)].set(top_value)


def shard_levels(rng, extent, shards, least, largest):
    def one(dim, parts):
        draws = jax.random.uniform(jax.random.fold_in(jax.random.fold_in(rng, 6), dim), (parts,), jnp.float32, least / len(shards), largest / len(shards))
        return jnp.repeat(jnp.exp(draws), extent[dim] // parts).reshape((-1,) + (1,) * (len(extent) - dim - 1))

    gain = one(*shards[0])
    for cut in shards[1:]:
        gain = gain * one(*cut)
    return gain


def bell_draw(stream_key, dims, scale, bound, pieces=(), kind=jnp.bfloat16):
    level = shard_levels(stream_key, dims, pieces, -0.22, 0.18) if pieces else 1.0
    result = jax.random.normal(stream_key, dims, jnp.float32) * scale * level
    return jnp.minimum(jnp.maximum(result, -bound), bound).astype(kind)


def setup_inputs(seed: int = 0) -> dict:
    arg_keys = jax.random.split(jax.random.key(seed), 15)
    return {
        "signal": bell_draw(arg_keys[0], (TOKENS, RESIDUAL_WIDTH), 1.0, 6.0, ((0, 32),)),
        "features": bell_draw(arg_keys[1], (TOKENS, C), 1.0, 6.0, ((0, 32),)),
        "position": draw_position(jax.random.fold_in(arg_keys[14], 71), 0),
        "valid": place_ends((jax.random.randint(arg_keys[3], (TOKENS,), 0, 8) < 7).astype(jnp.int32), jax.random.fold_in(arg_keys[3], 1), 0, 1),
        "w_past": bell_draw(arg_keys[4], (RESIDUAL_WIDTH, G), (2 * RESIDUAL_WIDTH) ** -0.5, 0.1875),
        "w_now": bell_draw(arg_keys[5], (RESIDUAL_WIDTH, G), (2 * RESIDUAL_WIDTH) ** -0.5, 0.1875),
        "b_conv": bell_draw(arg_keys[6], (G,), 0.3, 2.0, (), jnp.float32),
        "w_cond": bell_draw(arg_keys[7], (C, G), (4 * C) ** -0.5, 0.3125),
        "w_res": bell_draw(arg_keys[8], (H, RESIDUAL_WIDTH), (H // 8) ** -0.5, 0.75),
        "b_res": bell_draw(arg_keys[9], (RESIDUAL_WIDTH,), 0.3, 2.0, (), jnp.float32),
        "w_skip": bell_draw(arg_keys[10], (H, S), (H // 8) ** -0.5, 0.75),
        "b_skip": bell_draw(arg_keys[11], (S,), 0.3, 2.0, (), jnp.float32),
        "grad_out": bell_draw(arg_keys[12], (TOKENS, RESIDUAL_WIDTH), 1.0, 6.0, ((0, 32),)),
        "grad_skip": bell_draw(arg_keys[13], (TOKENS, S), 1.0, 6.0, ((0, 32),)),
    }


@jax.custom_vjp
def low(v):
    return lax.optimization_barrier(v.astype(jnp.bfloat16)).astype(jnp.float32)

@jax.custom_vjp
def low_back(v):
    return v

def low_keep(v):
    return (low(v), None)

def low_pass(kept, grad):
    return (grad,)

def back_keep(v):
    return (v, None)

def back_low(kept, grad):
    return (low(grad),)
low.defvjp(low_keep, low_pass)
low_back.defvjp(back_keep, back_low)

def matmul(left, right):
    return jnp.dot(left, right, precision=lax.Precision.HIGHEST, preferred_element_type=jnp.float32)

def reference(signal, features, position, valid, w_past, w_now, b_conv, w_cond, w_res, b_res, w_skip, b_skip, grad_out, grad_skip):
    past_sample = (position >= DILATION_STEP).astype(jnp.float32)[:, None]
    mask = valid.astype(jnp.float32)[:, None]

    def forward(signal_input, feat, wp, wn, bc, wc, wr, br, ws, bs):
        delayed_input = jnp.concatenate([jnp.zeros((DILATION_STEP, RESIDUAL_WIDTH), jnp.float32), signal_input[:-DILATION_STEP]], axis=0)
        past = past_sample * delayed_input
        pre = low_back(matmul(past, wp) + matmul(signal_input, wn) + matmul(feat, wc) + bc)
        act = jnp.tanh(pre[:, :H])
        gate = jax.nn.sigmoid(pre[:, H:])
        gated = low(act * gate)
        branch = low_back(matmul(gated, wr) + br)
        side = low_back(matmul(gated, ws) + bs)
        return (signal_input + mask * branch, mask * side)
    inputs = (signal.astype(jnp.float32), features.astype(jnp.float32), w_past.astype(jnp.float32), w_now.astype(jnp.float32), b_conv, w_cond.astype(jnp.float32), w_res.astype(jnp.float32), b_res, w_skip.astype(jnp.float32), b_skip)
    outs, pullback = jax.vjp(forward, *inputs)
    grads = pullback((grad_out.astype(jnp.float32), grad_skip.astype(jnp.float32)))
    return (outs[0].astype(jnp.bfloat16), outs[1].astype(jnp.bfloat16), grads[0], grads[1], grads[2], grads[3], grads[4], grads[5], grads[6], grads[7], grads[8], grads[9])
```

```python
import jax
import jax.numpy as jnp
from jax import lax
from jax.sharding import PartitionSpec as P

DILATION_STEP = 256
AXES = ("row", "col")
LANES = 256
TILE = 16


def passed_along(x, axis, by):
    peers = lax.axis_size(axis)
    pairs = [(i, i + by) for i in range(peers) if 0 <= i + by < peers]
    return lax.ppermute(x, axis, pairs)


def across(left, right):
    return lax.dot_general(
        left, right, (((0,), (0,)), ((), ())), preferred_element_type=jnp.float32
    )


def against(left, weight):
    return lax.dot_general(
        left, weight, (((1,), (1,)), ((), ())), preferred_element_type=jnp.float32
    )


def bit_orders():
    chip_bits = (lax.axis_size("col") - 1).bit_length()
    row_bits = (lax.axis_size("row") - 1).bit_length()
    core = chip_bits
    rest = list(range(chip_bits)) + list(range(chip_bits + 1, chip_bits + row_bits))
    return [[core] + rest[k:] + rest[:k] for k in (0, 1, 2)]


def scatter_sum(total, bits):
    me = lax.axis_index(AXES)
    peers = lax.axis_size(AXES)
    for bit in bits:
        half = total.shape[0] // 2
        mine = (me >> bit) & 1
        theirs = lax.dynamic_slice_in_dim(total, (1 - mine) * half, half, 0)
        kept = lax.dynamic_slice_in_dim(total, mine * half, half, 0)
        pairs = [(i, i ^ (1 << bit)) for i in range(peers)]
        got = lax.ppermute(theirs.astype(jnp.bfloat16), AXES, pairs)
        total = kept + got.astype(jnp.float32)
    return total.astype(jnp.bfloat16)


def in_order(gathered, bits):
    count = len(bits)
    rows = gathered.shape[0] >> count
    cube = gathered.reshape((2,) * count + (rows, LANES))
    order = [count - 1 - bit for bit in bits]
    return cube.transpose(order + [count, count + 1]).reshape(-1, LANES)


def summed(arrays):
    peers = lax.axis_size(AXES)
    pieces = []
    for array in arrays:
        flat = array.reshape(-1, array.shape[-1])
        pieces += [flat[:, k : k + LANES] for k in range(0, flat.shape[1], LANES)]
    used = sum(piece.shape[0] for piece in pieces)
    unit = peers * TILE
    units = max(3, -(-used // unit))
    pieces.append(jnp.zeros((units * unit - used, LANES), jnp.float32))
    packed = jnp.concatenate(pieces, axis=0)
    sizes = [(units + 2 - k) // 3 * unit for k in range(3)]
    orders = bit_orders()
    parts, at = [], 0
    for size in sizes:
        parts.append(packed[at : at + size])
        at += size
    shards = [scatter_sum(part, bits) for part, bits in zip(parts, orders)]
    both = lax.all_gather(jnp.concatenate(shards, axis=0), AXES, axis=0)
    ends, at = [], 0
    for size, bits in zip(sizes, orders):
        rows = size // peers
        ends.append(in_order(both[:, at : at + rows].reshape(-1, LANES), bits))
        at += rows
    whole = jnp.concatenate(ends, axis=0).astype(jnp.float32)
    results, at = [], 0
    for array in arrays:
        rows = array.size // array.shape[-1]
        columns = []
        for _ in range(0, array.shape[-1], LANES):
            columns.append(whole[at : at + rows])
            at += rows
        results.append(jnp.concatenate(columns, axis=1).reshape(array.shape))
    return results


def body(
    signal,
    features,
    position,
    valid,
    w_past,
    w_now,
    b_conv,
    w_cond,
    w_res,
    b_res,
    w_skip,
    b_skip,
    grad_out,
    grad_skip,
):
    width = w_res.shape[0]
    frame_rows = signal.shape[0]
    earlier_state = passed_along(signal[frame_rows - DILATION_STEP :], AXES, 1)
    delayed_input = jnp.concatenate([earlier_state, signal[: frame_rows - DILATION_STEP]], axis=0)
    past_valid_mask = (position >= DILATION_STEP)[:, None]
    past = jnp.where(past_valid_mask, delayed_input, jnp.zeros_like(delayed_input))
    pre = (
        jnp.dot(past, w_past, preferred_element_type=jnp.float32)
        + jnp.dot(signal, w_now, preferred_element_type=jnp.float32)
        + jnp.dot(features, w_cond, preferred_element_type=jnp.float32)
        + b_conv
    )
    act = jnp.tanh(pre[:, :width])
    gate = jax.nn.sigmoid(pre[:, width:])
    gated = (act * gate).astype(jnp.bfloat16)
    mask = valid.astype(jnp.float32)[:, None]
    branch = jnp.dot(gated, w_res, preferred_element_type=jnp.float32) + b_res
    output = (signal.astype(jnp.float32) + mask * branch).astype(jnp.bfloat16)
    side = jnp.dot(gated, w_skip, preferred_element_type=jnp.float32) + b_skip
    skip_out = (mask * side).astype(jnp.bfloat16)
    g_res = (mask * grad_out.astype(jnp.float32)).astype(jnp.bfloat16)
    g_side = (mask * grad_skip.astype(jnp.float32)).astype(jnp.bfloat16)
    outer_grads = (
        across(gated, g_res),
        jnp.sum(g_res.astype(jnp.float32), axis=0),
        across(gated, g_side),
        jnp.sum(g_side.astype(jnp.float32), axis=0),
    )
    d_gated = against(g_res, w_res) + against(g_side, w_skip)
    d_pre = jnp.concatenate(
        [d_gated * gate * (1.0 - act * act), d_gated * act * gate * (1.0 - gate)], axis=1
    ).astype(jnp.bfloat16)
    inner_grads = (
        across(past, d_pre),
        across(signal, d_pre),
        jnp.sum(d_pre.astype(jnp.float32), axis=0),
        across(features, d_pre),
    )
    sums = summed(inner_grads + outer_grads)
    grad_features = against(d_pre, w_cond)
    tapped = jnp.where(past_valid_mask, d_pre, jnp.zeros_like(d_pre))
    past_gradient = against(tapped, w_past)
    received_rows = passed_along(
        past_gradient[:DILATION_STEP].astype(jnp.bfloat16), AXES, -1
    ).astype(jnp.float32)
    local_gradient = past_gradient[DILATION_STEP:]
    grad_signal = (
        grad_out.astype(jnp.float32)
        + against(d_pre, w_now)
        + jnp.concatenate([local_gradient, received_rows], axis=0)
    )
    return (output, skip_out, grad_signal, grad_features, *sums)


def solution(mesh):
    rows = P(AXES, None)
    line = P(AXES)
    return jax.shard_map(
        body,
        mesh=mesh,
        in_specs=(rows, rows, line, line) + (P(),) * 8 + (rows, rows),
        out_specs=(rows,) * 4 + (P(),) * 8,
        check_vma=False,
    )
```

```python
import jax
import jax.numpy as jnp
from jax import lax
from jax.sharding import Mesh
from jax.sharding import PartitionSpec as P

DILATION_STEP = 256
AXES = ("outer", "core", "far", "near")
STEPS = ("core", "near", "far", "outer")
LANES = 256
TILE = 16


def passed_along(x, axis, by):
    peers = lax.axis_size(axis)
    pairs = [(i, i + by) for i in range(peers) if 0 <= i + by < peers]
    return lax.ppermute(x, axis, pairs)


def across(left, right):
    return lax.dot_general(
        left, right, (((0,), (0,)), ((), ())), preferred_element_type=jnp.float32
    )


def against(left, weight):
    return lax.dot_general(
        left, weight, (((1,), (1,)), ((), ())), preferred_element_type=jnp.float32
    )


def swapped(x, axis):
    return lax.all_to_all(x, axis, 0, 0, tiled=True)


def scatter_sum(total, axis):
    peers = lax.axis_size(axis)
    got = swapped(total.astype(jnp.bfloat16), axis).reshape(peers, -1, LANES)
    return jnp.sum(got.astype(jnp.float32), axis=0)


def gathered(block, axis):
    peers = lax.axis_size(axis)
    return swapped(jnp.tile(block, (peers, 1)), axis)


def summed(arrays):
    peers = lax.axis_size(AXES)
    pieces = []
    for array in arrays:
        flat = array.reshape(-1, array.shape[-1])
        pieces += [flat[:, k : k + LANES].astype(jnp.bfloat16) for k in range(0, flat.shape[1], LANES)]
    used = sum(piece.shape[0] for piece in pieces)
    unit = peers * TILE
    size = -(-used // unit) * unit
    pieces.append(jnp.zeros((size - used, LANES), jnp.bfloat16))
    total = jnp.concatenate(pieces, axis=0)
    steps = [axis for axis in STEPS if lax.axis_size(axis) > 1]
    for axis in steps:
        total = scatter_sum(total, axis)
    whole = total.astype(jnp.bfloat16)
    for axis in reversed(steps):
        whole = gathered(whole, axis)
    results, at = [], 0
    for array in arrays:
        rows = array.size // array.shape[-1]
        columns = []
        for _ in range(0, array.shape[-1], LANES):
            columns.append(whole[at : at + rows].astype(jnp.float32))
            at += rows
        results.append(jnp.concatenate(columns, axis=1).reshape(array.shape))
    return results


def body(
    signal,
    features,
    position,
    valid,
    w_past,
    w_now,
    b_conv,
    w_cond,
    w_res,
    b_res,
    w_skip,
    b_skip,
    grad_out,
    grad_skip,
):
    width = w_res.shape[0]
    frame_rows = signal.shape[0]
    earlier_state = passed_along(signal[frame_rows - DILATION_STEP :], AXES, 1)
    delayed_input = jnp.concatenate([earlier_state, signal[: frame_rows - DILATION_STEP]], axis=0)
    past_valid_mask = (position >= DILATION_STEP)[:, None]
    past = jnp.where(past_valid_mask, delayed_input, jnp.zeros_like(delayed_input))
    pre = (
        jnp.dot(past, w_past, preferred_element_type=jnp.float32)
        + jnp.dot(signal, w_now, preferred_element_type=jnp.float32)
        + jnp.dot(features, w_cond, preferred_element_type=jnp.float32)
        + b_conv
    )
    act = jnp.tanh(pre[:, :width])
    gate = jax.nn.sigmoid(pre[:, width:])
    gated = (act * gate).astype(jnp.bfloat16)
    mask = valid.astype(jnp.float32)[:, None]
    branch = jnp.dot(gated, w_res, preferred_element_type=jnp.float32) + b_res
    output = (signal.astype(jnp.float32) + mask * branch).astype(jnp.bfloat16)
    side = jnp.dot(gated, w_skip, preferred_element_type=jnp.float32) + b_skip
    skip_out = (mask * side).astype(jnp.bfloat16)
    g_res = (mask * grad_out.astype(jnp.float32)).astype(jnp.bfloat16)
    g_side = (mask * grad_skip.astype(jnp.float32)).astype(jnp.bfloat16)
    outer_grads = (
        across(gated, g_res),
        jnp.sum(g_res.astype(jnp.float32), axis=0),
        across(gated, g_side),
        jnp.sum(g_side.astype(jnp.float32), axis=0),
    )
    d_gated = against(g_res, w_res) + against(g_side, w_skip)
    d_pre = jnp.concatenate(
        [d_gated * gate * (1.0 - act * act), d_gated * act * gate * (1.0 - gate)], axis=1
    ).astype(jnp.bfloat16)
    inner_grads = (
        across(past, d_pre),
        across(signal, d_pre),
        jnp.sum(d_pre.astype(jnp.float32), axis=0),
        across(features, d_pre),
    )
    sums = summed(inner_grads + outer_grads)
    grad_features = against(d_pre, w_cond)
    tapped = jnp.where(past_valid_mask, d_pre, jnp.zeros_like(d_pre))
    past_gradient = against(tapped, w_past)
    received_rows = passed_along(
        past_gradient[:DILATION_STEP].astype(jnp.bfloat16), AXES, -1
    ).astype(jnp.float32)
    local_gradient = past_gradient[DILATION_STEP:]
    grad_signal = (
        grad_out.astype(jnp.float32)
        + against(d_pre, w_now)
        + jnp.concatenate([local_gradient, received_rows], axis=0)
    )
    return (output, skip_out, grad_signal, grad_features, *sums)


def solution(mesh):
    row, col = mesh.shape["row"], mesh.shape["col"]
    fine = Mesh(mesh.devices.reshape(row // 2, 2, col // 4, 4), AXES)
    rows = P(AXES, None)
    line = P(AXES)
    return jax.shard_map(
        body,
        mesh=fine,
        in_specs=(rows, rows, line, line) + (P(),) * 8 + (rows, rows),
        out_specs=(rows,) * 4 + (P(),) * 8,
        check_vma=False,
    )
```

```python
import functools

import jax
import jax.numpy as jnp
from jax import lax
from jax.experimental import pallas as pl
from jax.experimental.pallas import tpu as pltpu
from jax.sharding import Mesh
from jax.sharding import PartitionSpec as P

DILATION_STEP = 256
AXES = ("outer", "core", "far", "near")
HALVES = 2
NEAR = 4
LANES = 128
ROWS = 512
F32 = jnp.float32
BF16 = jnp.bfloat16
MEGA = 1 << 20


def dot(left, right):
    return jnp.dot(left, right, preferred_element_type=F32)


def across(left, right):
    return lax.dot_general(left, right, (((0,), (0,)), ((), ())), preferred_element_type=F32)


def against(left, weight):
    return lax.dot_general(left, weight, (((1,), (1,)), ((), ())), preferred_element_type=F32)


def column(lines):
    turned = lines.astype(F32).T
    return jnp.concatenate([turned[:, k : k + 1] for k in range(lines.shape[0])], axis=0)


def tap_of(lines):
    return column(jnp.where(lines >= DILATION_STEP, 1, 0))


def call(kernel, grid, name, in_specs, out_specs, out_shape, scratch=(), aliases=None, cost=None, vmem=32):
    return pl.pallas_call(
        kernel,
        grid=grid,
        in_specs=in_specs,
        out_specs=out_specs,
        out_shape=out_shape,
        scratch_shapes=list(scratch),
        input_output_aliases=aliases or {},
        cost_estimate=cost,
        name=name,
        compiler_params=pltpu.CompilerParams(
            dimension_semantics=("arbitrary",) * len(grid), vmem_limit_bytes=vmem * MEGA
        ),
    )


def whole(*shape):
    return pl.BlockSpec(shape, lambda *i: (0,) * len(shape))


def tiles(rows, width, at=lambda i: i, column_block=0):
    return pl.BlockSpec((rows, width), lambda i: (at(i), column_block))


def line_tiles(at=lambda i: i):
    return pl.BlockSpec((1, ROWS // LANES, LANES), lambda i: (at(i), 0, 0))


SCALARS = pl.BlockSpec(memory_space=pltpu.SMEM)


def k0_body(gout, gskip, valid, w_res, w_skip, dgated, sums):
    step = pl.program_id(0)
    mask = column(valid[0])

    @pl.when(step == 0)
    def _():
        sums[...] = jnp.zeros_like(sums)

    res, skip = gout[...], gskip[...]
    dgated[...] = mask * (against(res, w_res[...]) + against(skip, w_skip[...]))
    sums[0:1, :] += jnp.sum(mask * res.astype(F32), axis=0, keepdims=True)
    sums[1:2, :] += jnp.sum(mask * skip.astype(F32), axis=0, keepdims=True)


def k0(gout, gskip, valid, w_res, w_skip):
    rows, width = gout.shape
    skip_width = gskip.shape[1]
    hidden = w_res.shape[0]
    return call(
        k0_body,
        (rows // ROWS,),
        "d_gated",
        [tiles(ROWS, width), tiles(ROWS, skip_width), line_tiles(), whole(hidden, width), whole(hidden, skip_width)],
        [tiles(ROWS, hidden), whole(8, width)],
        [jax.ShapeDtypeStruct((rows, hidden), F32), jax.ShapeDtypeStruct((8, width), F32)],
        cost=pl.CostEstimate(flops=4 * rows * width * hidden, bytes_accessed=9 * MEGA, transcendentals=0),
    )(gout, gskip, valid, w_res, w_skip)


def k1_body(
    far, block, half,
    place, halo, sig, feat, pos, valid, dgated, gout, gskip,
    wpa, wps, wna, wns, wca, wcs, bca, bcs, sums,
    gated_out, dpre_out, theirs, mine,
    acc, bias, carry,
):
    step = pl.program_id(0)
    width = sig.shape[1]
    cond = feat.shape[1]
    part = wpa.shape[1]
    top = 2 * width

    @pl.when(step == 0)
    def _():
        acc[...] = jnp.zeros_like(acc)
        bias[...] = jnp.zeros_like(bias)
        carry[...] = halo[...]

    now = sig[...]
    delayed = jnp.concatenate([carry[...], now[: ROWS - DILATION_STEP]], axis=0)
    carry[...] = now[ROWS - DILATION_STEP :]
    past = delayed * tap_of(pos[0]).astype(BF16)
    feats = feat[...]
    pre_a = dot(past, wpa[...]) + dot(now, wna[...]) + dot(feats, wca[...]) + bca[...]
    pre_s = dot(past, wps[...]) + dot(now, wns[...]) + dot(feats, wcs[...]) + bcs[...]
    act = jnp.tanh(pre_a)
    gate = 0.5 + 0.5 * jnp.tanh(0.5 * pre_s)
    gated = (act * gate).astype(BF16)
    gated_out[...] = gated
    slope = dgated[...] * gate
    dpre = jnp.concatenate(
        [slope * (1.0 - act * act), slope * act * (1.0 - gate)], axis=1
    ).astype(BF16)
    dpre_out[...] = dpre
    kept = gated * column(valid[0]).astype(BF16)
    acc[0:width, :] += across(past, dpre)
    acc[width:top, :] += across(now, dpre)
    acc[top : top + part, :] += across(kept, gout[...])
    acc[top + part : top + 2 * part, :] += across(kept, gskip[...])
    acc[top + 2 * part : top + 2 * part + cond, :] += across(feats, dpre)
    bias[...] += jnp.sum(dpre.astype(F32).reshape(ROWS // 8, 8, 2 * part), axis=0)

    @pl.when(step == pl.num_programs(0) - 1)
    def _():
        at = top + 2 * part + cond
        acc[at : at + 1, :] = jnp.sum(bias[...], axis=0, keepdims=True)
        acc[at + 1 : at + 2, :] = sums[half : half + 1, :]
        core, z, xy = place[0], place[1], place[2]
        for r in range(far):
            for c in range(NEAR):
                here = pl.ds(c * LANES, LANES)
                for k, out in ((1 - core, theirs), (core, mine)):
                    rows = pl.ds(pl.multiple_of((k * far + r) * block, 16), block)
                    out[c ^ xy, r ^ z] = acc[rows, here].astype(out.dtype)


def k1(half, far, block, place, halo, sig, feat, pos, valid, dgated, gout, gskip, w_past, w_now, w_cond, b_conv, sums):
    rows, width = sig.shape
    cond = feat.shape[1]
    gates = w_past.shape[1]
    hidden = gates // 2
    part = hidden // HALVES
    first, second = half, HALVES + half
    weight = [
        pl.BlockSpec((size, part), functools.partial(lambda b, i: (0, b), b))
        for size in (width, width, cond, 1)
        for b in (first, second)
    ]
    packed = (NEAR, far, block, LANES)
    return call(
        functools.partial(k1_body, far, block, half),
        (rows // ROWS,),
        f"gradients_{half}",
        [
            SCALARS,
            whole(DILATION_STEP, width),
            tiles(ROWS, width),
            tiles(ROWS, cond),
            line_tiles(),
            line_tiles(),
            tiles(ROWS, part, column_block=half),
            tiles(ROWS, gout.shape[1]),
            tiles(ROWS, gskip.shape[1]),
            *weight,
            whole(*sums.shape),
        ],
        [tiles(ROWS, part), tiles(ROWS, 2 * part), whole(*packed), whole(*packed)],
        [
            jax.ShapeDtypeStruct((rows, part), BF16),
            jax.ShapeDtypeStruct((rows, 2 * part), BF16),
            jax.ShapeDtypeStruct(packed, BF16),
            jax.ShapeDtypeStruct(packed, F32),
        ],
        scratch=[
            pltpu.VMEM((2 * far * block, 2 * part), F32),
            pltpu.VMEM((8, 2 * part), F32),
            pltpu.VMEM((DILATION_STEP, width), BF16),
        ],
        cost=pl.CostEstimate(
            flops=2 * rows * (2 * width + cond) * 4 * part + 8 * rows * width * part,
            bytes_accessed=18 * MEGA,
            transcendentals=2 * rows * part,
        ),
    )(
        place, halo, sig, feat, pos, valid, dgated, gout, gskip,
        w_past, w_past, w_now, w_now, w_cond, w_cond, b_conv, b_conv, sums,
    )


def k2a_body(sig, valid, pos, gated_0, gated_1, dpre_0, dpre_1, w_res, b_res, w_skip, b_skip, w_past, out, skip, early):
    part = gated_0.shape[1]
    mask = column(valid[0])

    @pl.when(pl.program_id(0) == 0)
    def _():
        tap = tap_of(pos[0, : DILATION_STEP // LANES])
        early[...] = (tap * past_term(dpre_0[...], dpre_1[...], w_past, part)).astype(BF16)

    left, right = gated_0[...], gated_1[...]
    branch = dot(left, w_res[:part]) + dot(right, w_res[part:]) + b_res[...]
    out[...] = (sig[...].astype(F32) + mask * branch).astype(BF16)
    side = dot(left, w_skip[:part]) + dot(right, w_skip[part:]) + b_skip[...]
    skip[...] = (mask * side).astype(BF16)


def past_term(dpre_0, dpre_1, weight, part):
    hidden = 2 * part
    total = against(dpre_0[:, :part], weight[:, :part])
    total += against(dpre_1[:, :part], weight[:, part:hidden])
    total += against(dpre_0[:, part:], weight[:, hidden : hidden + part])
    return total + against(dpre_1[:, part:], weight[:, hidden + part :])


def k2a(sig, valid, pos, gated, dpre, w_res, b_res, w_skip, b_skip, w_past):
    rows, width = sig.shape
    part = gated[0].shape[1]
    hidden = 2 * part
    return call(
        k2a_body,
        (rows // ROWS,),
        "outputs",
        [
            tiles(ROWS, width),
            line_tiles(),
            line_tiles(),
            tiles(ROWS, part),
            tiles(ROWS, part),
            whole(DILATION_STEP, 2 * part),
            whole(DILATION_STEP, 2 * part),
            whole(hidden, width),
            whole(1, width),
            whole(*w_skip.shape),
            whole(1, w_skip.shape[1]),
            whole(*w_past.shape),
        ],
        [tiles(ROWS, width), tiles(ROWS, w_skip.shape[1]), whole(DILATION_STEP, width)],
        [
            jax.ShapeDtypeStruct((rows, width), BF16),
            jax.ShapeDtypeStruct((rows, w_skip.shape[1]), BF16),
            jax.ShapeDtypeStruct((DILATION_STEP, width), BF16),
        ],
        cost=pl.CostEstimate(flops=4 * rows * width * hidden, bytes_accessed=11 * MEGA, transcendentals=0),
    )(sig, valid, pos, *gated, *dpre, w_res, b_res, w_skip, b_skip, w_past)


def k2b_body(received, gout, pos, dpre_0, dpre_1, w_past, w_now, w_cond, gsig, gfeat, carry):
    part = dpre_0.shape[1] // 2

    @pl.when(pl.program_id(0) == 0)
    def _():
        carry[...] = received[...].astype(F32)

    left, right = dpre_0[...], dpre_1[...]
    tail = tap_of(pos[0]) * past_term(left, right, w_past, part)
    here = gout[...].astype(F32) + past_term(left, right, w_now, part)
    gsig[: ROWS - DILATION_STEP] = here[: ROWS - DILATION_STEP] + tail[DILATION_STEP:]
    gsig[ROWS - DILATION_STEP :] = here[ROWS - DILATION_STEP :] + carry[...]
    carry[...] = tail[:DILATION_STEP]
    gfeat[...] = past_term(left, right, w_cond, part)


def k2b(received, gout, pos, dpre, w_past, w_now, w_cond):
    rows, width = gout.shape
    cond = w_cond.shape[0]
    steps = rows // ROWS

    def back(i):
        return steps - 1 - i

    return call(
        k2b_body,
        (steps,),
        "input_gradients",
        [
            whole(DILATION_STEP, width),
            tiles(ROWS, width, back),
            line_tiles(back),
            tiles(ROWS, dpre[0].shape[1], back),
            tiles(ROWS, dpre[1].shape[1], back),
            whole(*w_past.shape),
            whole(*w_now.shape),
            whole(*w_cond.shape),
        ],
        [tiles(ROWS, width, back), tiles(ROWS, cond, back)],
        [jax.ShapeDtypeStruct((rows, width), F32), jax.ShapeDtypeStruct((rows, cond), F32)],
        scratch=[pltpu.VMEM((DILATION_STEP, width), F32)],
        cost=pl.CostEstimate(
            flops=2 * rows * (2 * width + cond) * w_past.shape[1], bytes_accessed=14 * MEGA, transcendentals=0
        ),
    )(received, gout, pos, *dpre, w_past, w_now, w_cond)


def unpack_body(far, block, half, width, cond, place, mine, theirs, *refs):
    past, now, res, skip, conds, b_conv, b_own = refs[-8:-1]
    room = refs[-1]
    part = res.shape[0]
    core, z, xy = place[0], place[1], place[2]

    @pl.when(pl.program_id(0) == 0)
    def _():
        for k, ref in ((core, mine), (1 - core, theirs)):
            for c in range(NEAR):
                for r in range(far):
                    rows = pl.ds(pl.multiple_of((k * far + (r ^ z)) * block, 16), block)
                    room[c ^ xy, rows, :] = ref[c, r]

    for j in range(NEAR // 2):
        c = pl.program_id(0) * (NEAR // 2) + j
        here = pl.ds(j * LANES, LANES)
        top = 0
        for ref in (past, now, res, skip, conds):
            count = ref.shape[0]
            ref[:, here] = room[c, top : top + count, :].astype(F32)
            top += count
        last = room[c, top : top + 16, :].astype(F32)
        b_conv[:, here] = last[0:1]
        b_own[:, here] = last[1:2]


def unpack(half, far, block, place, mine, theirs, width, cond, hidden, skip_width, before):
    part = hidden // HALVES
    gates = 2 * hidden
    wide = [
        pl.BlockSpec((size, part), lambda s: (0, HALVES * s + half)) for size in (width, width)
    ]
    tall = [pl.BlockSpec((part, size // 2), lambda s: (half, s)) for size in (width, skip_width)]
    rest = [
        pl.BlockSpec((cond, part), lambda s: (0, HALVES * s + half)),
        pl.BlockSpec((1, part), lambda s: (0, HALVES * s + half)),
        pl.BlockSpec((1, (width, skip_width)[half] // 2), lambda s: (0, s)),
    ]
    shapes = [
        (width, gates), (width, gates), (hidden, width), (hidden, skip_width), (cond, gates), (1, gates),
        (1, (width, skip_width)[half]),
    ]
    packed = (NEAR, far, block, LANES)
    return call(
        functools.partial(unpack_body, far, block, half, width, cond),
        (2,),
        f"unpack_{half}",
        [SCALARS, whole(*packed), whole(*packed)] + [pl.BlockSpec(memory_space=pl.ANY)] * len(before),
        wide + tall + rest,
        [jax.ShapeDtypeStruct(shape, F32) for shape in shapes],
        scratch=[pltpu.VMEM((NEAR, 2 * far * block, LANES), BF16)],
        aliases={3 + k: k for k in range(len(before))},
        cost=pl.CostEstimate(flops=0, bytes_accessed=6 * MEGA, transcendentals=0),
    )(place, mine, theirs, *before)


def swapped(x, axis, k):
    return lax.ppermute(x, axis, [(i, i ^ k) for i in range(lax.axis_size(axis))])


def scattered(total, axis):
    got = [swapped(total[k].astype(BF16), axis, k) for k in range(1, lax.axis_size(axis))]
    result = total[0]
    for part in got:
        result = result + part.astype(F32)
    return result


def reduced(theirs, mine):
    total = mine + swapped(theirs, "core", 1).astype(F32)
    total = scattered(scattered(total, "near"), "far")
    shard = total.astype(BF16)
    rest = [swapped(shard, "outer", k) for k in range(1, lax.axis_size("outer"))]
    for part in rest:
        total = total + part.astype(F32)
    return total.astype(BF16)


def gathered(shard):
    blocks = jnp.stack([shard] + [swapped(shard, "far", k) for k in range(1, lax.axis_size("far"))])
    blocks = jnp.stack([blocks] + [swapped(blocks, "near", k) for k in range(1, NEAR)])
    return blocks, swapped(blocks, "core", 1)


def passed_along(x, by):
    peers = lax.axis_size(AXES)
    pairs = [(i, i + by) for i in range(peers) if 0 <= i + by < peers]
    return lax.ppermute(x, AXES, pairs)


def body(
    signal,
    features,
    position,
    valid,
    w_past,
    w_now,
    b_conv,
    w_cond,
    w_res,
    b_res,
    w_skip,
    b_skip,
    grad_out,
    grad_skip,
):
    rows, width = signal.shape
    cond = features.shape[1]
    hidden = w_res.shape[0]
    skip_width = w_skip.shape[1]
    far = lax.axis_size("far")
    used = 2 * width + 2 * (hidden // HALVES) + cond + 2
    block = -(-used // (2 * far * 16)) * 16
    place = jnp.stack([lax.axis_index(name) for name in ("core", "far", "near")]).astype(jnp.int32)
    lines = (rows // ROWS, ROWS // LANES, LANES)
    pos, val = position.reshape(lines), valid.reshape(lines)
    b_conv, b_res, b_skip = (b.reshape(1, -1) for b in (b_conv, b_res, b_skip))

    halo = passed_along(signal[rows - DILATION_STEP :], 1)
    dgated, sums = k0(grad_out, grad_skip, val, w_res, w_skip)
    gated, dpre, shards = [], [], []
    for half in range(HALVES):
        one, other, theirs, mine = k1(
            half, far, block, place, halo, signal, features, pos, val, dgated, grad_out, grad_skip,
            w_past, w_now, w_cond, b_conv, sums,
        )
        gated.append(one)
        dpre.append(other)
        shards.append(reduced(theirs, mine))
    output, skip_out, early = k2a(signal, val, pos, gated, dpre, w_res, b_res, w_skip, b_skip, w_past)
    received = passed_along(early, -1)
    grad_signal, grad_features = k2b(received, grad_out, pos, dpre, w_past, w_now, w_cond)
    done, own = [], []
    for half in range(HALVES):
        blocks, others = gathered(shards[half])
        *done, last = unpack(half, far, block, place, blocks, others, width, cond, hidden, skip_width, done)
        own.append(last)
    g_past, g_now, g_res, g_skip, g_cond, g_bias = done
    return (
        output,
        skip_out,
        grad_signal,
        grad_features,
        g_past,
        g_now,
        g_bias.reshape(-1),
        g_cond,
        g_res,
        own[0].reshape(-1),
        g_skip,
        own[1].reshape(-1),
    )


def solution(mesh):
    row, col = mesh.shape["row"], mesh.shape["col"]
    fine = Mesh(mesh.devices.reshape(row // 2, 2, col // NEAR, NEAR), AXES)
    rows = P(AXES, None)
    line = P(AXES)
    return jax.shard_map(
        body,
        mesh=fine,
        in_specs=(rows, rows, line, line) + (P(),) * 8 + (rows, rows),
        out_specs=(rows,) * 4 + (P(),) * 8,
        check_vma=False,
    )
```

```python
import functools

import jax
import jax.numpy as jnp
from jax import lax
from jax.experimental import pallas as pl
from jax.experimental.pallas import tpu as pltpu
from jax.sharding import Mesh
from jax.sharding import PartitionSpec as P

DILATION_STEP = 256
AXES = ("outer", "core", "far", "near")
HALVES = 2
NEAR = 4
LANES = 128
ROWS = 512
F32 = jnp.float32
BF16 = jnp.bfloat16
MEGA = 1 << 20
LITTLE = pl.CostEstimate(flops=1, bytes_accessed=1, transcendentals=0)


def dot(left, right):
    return jnp.dot(left, right, preferred_element_type=F32)


def across(left, right):
    return lax.dot_general(left, right, (((0,), (0,)), ((), ())), preferred_element_type=F32)


def against(left, weight):
    return lax.dot_general(left, weight, (((1,), (1,)), ((), ())), preferred_element_type=F32)


def column(lines):
    turned = lines.astype(F32).T
    return jnp.concatenate([turned[:, k : k + 1] for k in range(lines.shape[0])], axis=0)


def tap_of(lines):
    return column(jnp.where(lines >= DILATION_STEP, 1, 0))


def call(kernel, grid, name, in_specs, out_specs, out_shape, scratch=(), aliases=None, vmem=32):
    return pl.pallas_call(
        kernel,
        grid=grid,
        in_specs=in_specs,
        out_specs=out_specs,
        out_shape=out_shape,
        scratch_shapes=list(scratch),
        input_output_aliases=aliases or {},
        cost_estimate=LITTLE,
        name=name,
        compiler_params=pltpu.CompilerParams(
            dimension_semantics=("arbitrary",) * len(grid), vmem_limit_bytes=vmem * MEGA
        ),
    )


def whole(*shape):
    return pl.BlockSpec(shape, lambda *i: (0,) * len(shape))


def tiles(rows, width, at=lambda i: i, column_block=0):
    return pl.BlockSpec((rows, width), lambda i: (at(i), column_block))


def line_tiles(at=lambda i: i):
    return pl.BlockSpec((1, ROWS // LANES, LANES), lambda i: (at(i), 0, 0))


ANYWHERE = pl.BlockSpec(memory_space=pl.ANY)
SCALARS = pl.BlockSpec(memory_space=pltpu.SMEM)


def k0_body(gout, gskip, valid, w_res, w_skip, dgated, sums):
    step = pl.program_id(0)
    mask = column(valid[0])

    @pl.when(step == 0)
    def _():
        sums[...] = jnp.zeros_like(sums)

    res, skip = gout[...], gskip[...]
    dgated[...] = mask * (against(res, w_res[...]) + against(skip, w_skip[...]))
    sums[0:1, :] += jnp.sum(mask * res.astype(F32), axis=0, keepdims=True)
    sums[1:2, :] += jnp.sum(mask * skip.astype(F32), axis=0, keepdims=True)


def k0(gout, gskip, valid, w_res, w_skip):
    rows, width = gout.shape
    skip_width = gskip.shape[1]
    hidden = w_res.shape[0]
    return call(
        k0_body,
        (rows // ROWS,),
        "d_gated",
        [tiles(ROWS, width), tiles(ROWS, skip_width), line_tiles(), whole(hidden, width), whole(hidden, skip_width)],
        [tiles(ROWS, hidden), whole(8, width)],
        [jax.ShapeDtypeStruct((rows, hidden), F32), jax.ShapeDtypeStruct((8, width), F32)],
    )(gout, gskip, valid, w_res, w_skip)


def k1_body(
    far, block, half,
    place, halo, sig, feat, pos, valid, dgated, gout, gskip,
    wpa, wps, wna, wns, wca, wcs, bca, bcs, sums,
    gated_out, dpre_out, theirs, mine,
    acc, bias, carry,
):
    step = pl.program_id(0)
    width = sig.shape[1]
    cond = feat.shape[0]
    part = wpa.shape[1]
    top = 2 * width

    @pl.when(step == 0)
    def _():
        acc[...] = jnp.zeros_like(acc)
        bias[...] = jnp.zeros_like(bias)
        carry[...] = halo[...]

    now = sig[...]
    delayed = jnp.concatenate([carry[...], now[: ROWS - DILATION_STEP]], axis=0)
    carry[...] = now[ROWS - DILATION_STEP :]
    past = delayed * tap_of(pos[0]).astype(BF16)
    feats = feat[...]
    pre_a = dot(past, wpa[...]) + dot(now, wna[...]) + across(feats, wca[...]) + bca[...]
    pre_s = dot(past, wps[...]) + dot(now, wns[...]) + across(feats, wcs[...]) + bcs[...]
    act = jnp.tanh(pre_a)
    gate = 0.5 + 0.5 * jnp.tanh(0.5 * pre_s)
    gated = (act * gate).astype(BF16)
    gated_out[...] = gated
    slope = dgated[...] * gate
    dpre = jnp.concatenate(
        [slope * (1.0 - act * act), slope * act * (1.0 - gate)], axis=1
    ).astype(BF16)
    dpre_out[...] = dpre
    kept = gated * column(valid[0]).astype(BF16)
    acc[0:width, :] += across(past, dpre)
    acc[width:top, :] += across(now, dpre)
    acc[top : top + part, :] += across(kept, gout[...])
    acc[top + part : top + 2 * part, :] += across(kept, gskip[...])
    acc[top + 2 * part : top + 2 * part + cond, :] += dot(feats, dpre)
    bias[...] += jnp.sum(dpre.astype(F32).reshape(ROWS // 8, 8, 2 * part), axis=0)

    @pl.when(step == pl.num_programs(0) - 1)
    def _():
        at = top + 2 * part + cond
        acc[at : at + 1, :] = jnp.sum(bias[...], axis=0, keepdims=True)
        acc[at + 1 : at + 2, :] = sums[half : half + 1, :]
        core, z, xy = place[0], place[1], place[2]
        for r in range(far):
            for c in range(NEAR):
                here = pl.ds(c * LANES, LANES)
                for k, out in ((1 - core, theirs), (core, mine)):
                    rows = pl.ds(pl.multiple_of((k * far + r) * block, 16), block)
                    out[c ^ xy, r ^ z] = acc[rows, here].astype(out.dtype)


def k1(half, far, block, place, halo, sig, feat, pos, valid, dgated, gout, gskip, w_past, w_now, w_cond, b_conv, sums):
    rows, width = sig.shape
    cond = feat.shape[0]
    gates = w_past.shape[1]
    hidden = gates // 2
    part = hidden // HALVES
    first, second = half, HALVES + half
    weight = [
        pl.BlockSpec((size, part), functools.partial(lambda b, i: (0, b), b))
        for size in (width, width, cond, 1)
        for b in (first, second)
    ]
    packed = (NEAR, far, block, LANES)
    return call(
        functools.partial(k1_body, far, block, half),
        (rows // ROWS,),
        f"gradients_{half}",
        [
            SCALARS,
            whole(DILATION_STEP, width),
            tiles(ROWS, width),
            pl.BlockSpec((cond, ROWS), lambda i: (0, i)),
            line_tiles(),
            line_tiles(),
            tiles(ROWS, part, column_block=half),
            tiles(ROWS, gout.shape[1]),
            tiles(ROWS, gskip.shape[1]),
            *weight,
            whole(*sums.shape),
        ],
        [tiles(ROWS, part), tiles(ROWS, 2 * part), whole(*packed), whole(*packed)],
        [
            jax.ShapeDtypeStruct((rows, part), BF16),
            jax.ShapeDtypeStruct((rows, 2 * part), BF16),
            jax.ShapeDtypeStruct(packed, BF16),
            jax.ShapeDtypeStruct(packed, F32),
        ],
        scratch=[
            pltpu.VMEM((2 * far * block, 2 * part), F32),
            pltpu.VMEM((8, 2 * part), F32),
            pltpu.VMEM((DILATION_STEP, width), BF16),
        ],
    )(
        place, halo, sig, feat, pos, valid, dgated, gout, gskip,
        w_past, w_past, w_now, w_now, w_cond, w_cond, b_conv, b_conv, sums,
    )


def k2a_body(token, sig, valid, pos, gated_0, gated_1, dpre_0, dpre_1, w_res, b_res, w_skip, b_skip, w_past, out, skip, early):
    part = gated_0.shape[1]
    mask = column(valid[0])

    @pl.when(pl.program_id(0) == 0)
    def _():
        tap = tap_of(pos[0, : DILATION_STEP // LANES])
        early[...] = (tap * past_term(dpre_0[...], dpre_1[...], w_past, part)).astype(BF16)

    left, right = gated_0[...], gated_1[...]
    branch = dot(left, w_res[:part]) + dot(right, w_res[part:]) + b_res[...]
    out[...] = (sig[...].astype(F32) + mask * branch).astype(BF16)
    side = dot(left, w_skip[:part]) + dot(right, w_skip[part:]) + b_skip[...]
    skip[...] = (mask * side).astype(BF16)


def past_term(dpre_0, dpre_1, weight, part):
    hidden = 2 * part
    total = against(dpre_0[:, :part], weight[:, :part])
    total += against(dpre_1[:, :part], weight[:, part:hidden])
    total += against(dpre_0[:, part:], weight[:, hidden : hidden + part])
    return total + against(dpre_1[:, part:], weight[:, hidden + part :])


def k2a(token, sig, valid, pos, gated, dpre, w_res, b_res, w_skip, b_skip, w_past):
    rows, width = sig.shape
    part = gated[0].shape[1]
    hidden = 2 * part
    return call(
        k2a_body,
        (rows // ROWS,),
        "outputs",
        [
            ANYWHERE,
            tiles(ROWS, width),
            line_tiles(),
            line_tiles(),
            tiles(ROWS, part),
            tiles(ROWS, part),
            whole(DILATION_STEP, 2 * part),
            whole(DILATION_STEP, 2 * part),
            whole(hidden, width),
            whole(1, width),
            whole(*w_skip.shape),
            whole(1, w_skip.shape[1]),
            whole(*w_past.shape),
        ],
        [tiles(ROWS, width), tiles(ROWS, w_skip.shape[1]), whole(DILATION_STEP, width)],
        [
            jax.ShapeDtypeStruct((rows, width), BF16),
            jax.ShapeDtypeStruct((rows, w_skip.shape[1]), BF16),
            jax.ShapeDtypeStruct((DILATION_STEP, width), BF16),
        ],
    )(token, sig, valid, pos, *gated, *dpre, w_res, b_res, w_skip, b_skip, w_past)


def k2b_body(token, received, gout, pos, dpre_0, dpre_1, w_past, w_now, w_cond, gsig, gfeat, carry):
    part = dpre_0.shape[1] // 2

    @pl.when(pl.program_id(0) == 0)
    def _():
        carry[...] = received[...].astype(F32)

    left, right = dpre_0[...], dpre_1[...]
    tail = tap_of(pos[0]) * past_term(left, right, w_past, part)
    here = gout[...].astype(F32) + past_term(left, right, w_now, part)
    gsig[: ROWS - DILATION_STEP] = here[: ROWS - DILATION_STEP] + tail[DILATION_STEP:]
    gsig[ROWS - DILATION_STEP :] = here[ROWS - DILATION_STEP :] + carry[...]
    carry[...] = tail[:DILATION_STEP]
    hidden = 2 * part
    total = against(w_cond[:, :part], left[:, :part])
    total += against(w_cond[:, part:hidden], right[:, :part])
    total += against(w_cond[:, hidden : hidden + part], left[:, part:])
    gfeat[...] = total + against(w_cond[:, hidden + part :], right[:, part:])


def k2b(token, received, gout, pos, dpre, w_past, w_now, w_cond):
    rows, width = gout.shape
    cond = w_cond.shape[0]
    steps = rows // ROWS

    def back(i):
        return steps - 1 - i

    return call(
        k2b_body,
        (steps,),
        "input_gradients",
        [
            ANYWHERE,
            whole(DILATION_STEP, width),
            tiles(ROWS, width, back),
            line_tiles(back),
            tiles(ROWS, dpre[0].shape[1], back),
            tiles(ROWS, dpre[1].shape[1], back),
            whole(*w_past.shape),
            whole(*w_now.shape),
            whole(*w_cond.shape),
        ],
        [tiles(ROWS, width, back), pl.BlockSpec((cond, ROWS), lambda i: (0, back(i)))],
        [jax.ShapeDtypeStruct((rows, width), F32), jax.ShapeDtypeStruct((cond, rows), F32)],
        scratch=[pltpu.VMEM((DILATION_STEP, width), F32)],
    )(token, received, gout, pos, *dpre, w_past, w_now, w_cond)


def unpack_body(far, block, half, width, cond, place, mine, theirs, *refs):
    past, now, res, skip, conds, b_conv, b_own = refs[-8:-1]
    room = refs[-1]
    part = res.shape[0]
    core, z, xy = place[0], place[1], place[2]

    @pl.when(pl.program_id(0) == 0)
    def _():
        for k, ref in ((core, mine), (1 - core, theirs)):
            for c in range(NEAR):
                for r in range(far):
                    rows = pl.ds(pl.multiple_of((k * far + (r ^ z)) * block, 16), block)
                    room[c ^ xy, rows, :] = ref[c, r]

    for j in range(NEAR // 2):
        c = pl.program_id(0) * (NEAR // 2) + j
        here = pl.ds(j * LANES, LANES)
        top = 0
        for ref in (past, now, res, skip, conds):
            count = ref.shape[0]
            ref[:, here] = room[c, top : top + count, :].astype(F32)
            top += count
        last = room[c, top : top + 16, :].astype(F32)
        b_conv[:, here] = last[0:1]
        b_own[:, here] = last[1:2]


def unpack(half, far, block, place, mine, theirs, width, cond, hidden, skip_width, before):
    part = hidden // HALVES
    gates = 2 * hidden
    wide = [
        pl.BlockSpec((size, part), lambda s: (0, HALVES * s + half)) for size in (width, width)
    ]
    tall = [pl.BlockSpec((part, size // 2), lambda s: (half, s)) for size in (width, skip_width)]
    rest = [
        pl.BlockSpec((cond, part), lambda s: (0, HALVES * s + half)),
        pl.BlockSpec((1, part), lambda s: (0, HALVES * s + half)),
        pl.BlockSpec((1, (width, skip_width)[half] // 2), lambda s: (0, s)),
    ]
    shapes = [
        (width, gates), (width, gates), (hidden, width), (hidden, skip_width), (cond, gates), (1, gates),
        (1, (width, skip_width)[half]),
    ]
    packed = (NEAR, far, block, LANES)
    return call(
        functools.partial(unpack_body, far, block, half, width, cond),
        (2,),
        f"unpack_{half}",
        [SCALARS, whole(*packed), whole(*packed)] + [pl.BlockSpec(memory_space=pl.ANY)] * len(before),
        wide + tall + rest,
        [jax.ShapeDtypeStruct(shape, F32) for shape in shapes],
        scratch=[pltpu.VMEM((NEAR, 2 * far * block, LANES), BF16)],
        aliases={3 + k: k for k in range(len(before))},
    )(place, mine, theirs, *before)


def swapped(x, axis, k):
    return lax.ppermute(x, axis, [(i, i ^ k) for i in range(lax.axis_size(axis))])


def exchanged(blocks, axis):
    return [swapped(block, axis, k + 1) for k, block in enumerate(blocks)]


def add_body(token, kept, *refs):
    count = kept.shape[0]
    got, outs = refs[:-count], refs[-count:]
    for k in range(count):
        total = kept[k]
        for ref in got:
            total = total + ref[k].astype(F32)
        outs[k][...] = total.astype(outs[k].dtype)


def added(token, kept, got, name, final=BF16):
    count, *block = kept.shape
    vmem = pl.BlockSpec(memory_space=pltpu.VMEM)
    first, *rest = pl.pallas_call(
        add_body,
        in_specs=[ANYWHERE, vmem] + [vmem] * len(got),
        out_specs=[vmem] * count,
        out_shape=[jax.ShapeDtypeStruct(block, final)] + [jax.ShapeDtypeStruct(block, BF16)] * (count - 1),
        name=name,
        cost_estimate=LITTLE,
        compiler_params=pltpu.CompilerParams(vmem_limit_bytes=16 * MEGA),
    )(token, kept, *got)
    return first, rest


def over_outer(total):
    shard = total.astype(BF16)
    for k in range(1, lax.axis_size("outer")):
        total = total + swapped(shard, "outer", k).astype(F32)
    return total.astype(BF16)


def gathered(block, axis):
    return jnp.stack([block] + [swapped(block, axis, k) for k in range(1, lax.axis_size(axis))])


def in_hbm(x):
    return pltpu.with_memory_space_constraint(x, pltpu.HBM)


def passed_along(x, by):
    peers = lax.axis_size(AXES)
    pairs = [(i, i + by) for i in range(peers) if 0 <= i + by < peers]
    return lax.ppermute(x, AXES, pairs)


def body(
    signal,
    features,
    position,
    valid,
    w_past,
    w_now,
    b_conv,
    w_cond,
    w_res,
    b_res,
    w_skip,
    b_skip,
    grad_out,
    grad_skip,
):
    rows, width = signal.shape
    features = features.T
    cond = features.shape[0]
    hidden = w_res.shape[0]
    skip_width = w_skip.shape[1]
    far = lax.axis_size("far")
    used = 2 * width + 2 * (hidden // HALVES) + cond + 2
    block = -(-used // (2 * far * 16)) * 16
    place = jnp.stack([lax.axis_index(name) for name in ("core", "far", "near")]).astype(jnp.int32)
    lines = (rows // ROWS, ROWS // LANES, LANES)
    pos, val = position.reshape(lines), valid.reshape(lines)
    b_conv, b_res, b_skip = (b.reshape(1, -1) for b in (b_conv, b_res, b_skip))

    halo = passed_along(signal[rows - DILATION_STEP :], 1)
    signal, grad_out, grad_skip = (in_hbm(x) for x in (signal, grad_out, grad_skip))
    dgated, sums = k0(grad_out, grad_skip, val, in_hbm(w_res), in_hbm(w_skip))
    gated, dpre, packed = [], [], []
    for half in range(HALVES):
        one, other, *both = k1(
            half, far, block, place, halo, signal, features, pos, val, dgated, grad_out, grad_skip,
            w_past, w_now, w_cond, b_conv, sums,
        )
        gated.append(one)
        dpre.append(other)
        packed.append(both)
    crossed = [swapped(theirs, "core", 1) for theirs, _ in packed]
    kept_0, sent_0 = added(place, packed[0][1], [crossed[0]], "core_sum_0", F32)
    near_0 = exchanged(sent_0, "near")
    output, skip_out, early = k2a(sent_0[0], signal, val, pos, gated, dpre, w_res, b_res, w_skip, b_skip, w_past)
    received = passed_along(early, -1)
    kept_1, sent_1 = added(early, packed[1][1], [crossed[1]], "core_sum_1", F32)
    near_1 = exchanged(sent_1, "near")
    kept_0, sent_0 = added(sent_1[0], kept_0, near_0, "near_sum_0", F32)
    far_0 = exchanged(sent_0, "far")
    grad_signal, grad_features = k2b(sent_0[0], received, grad_out, pos, dpre, w_past, w_now, w_cond)
    shard_0, _ = added(grad_features, kept_0[None], [x[None] for x in far_0], "far_sum_0", F32)
    ends_0 = gathered(over_outer(shard_0), "far")
    kept_1, sent_1 = added(shard_0, kept_1, near_1, "near_sum_1", F32)
    far_1 = exchanged(sent_1, "far")
    whole_0 = gathered(ends_0, "near")
    shard_1, _ = added(ends_0, kept_1[None], [x[None] for x in far_1], "far_sum_1", F32)
    ends_1 = gathered(over_outer(shard_1), "far")
    whole_1 = gathered(ends_1, "near")
    done, own = [], []
    for half, blocks in enumerate((whole_0, whole_1)):
        others = swapped(blocks, "core", 1)
        *done, last = unpack(half, far, block, place, blocks, others, width, cond, hidden, skip_width, done)
        own.append(last)
    g_past, g_now, g_res, g_skip, g_cond, g_bias = done
    return (
        output,
        skip_out,
        grad_signal,
        grad_features.T,
        g_past,
        g_now,
        g_bias.reshape(-1),
        g_cond,
        g_res,
        own[0].reshape(-1),
        g_skip,
        own[1].reshape(-1),
    )


def solution(mesh):
    row, col = mesh.shape["row"], mesh.shape["col"]
    fine = Mesh(mesh.devices.reshape(row // 2, 2, col // NEAR, NEAR), AXES)
    rows = P(AXES, None)
    line = P(AXES)
    return jax.shard_map(
        body,
        mesh=fine,
        in_specs=(rows, rows, line, line) + (P(),) * 8 + (rows, rows),
        out_specs=(rows,) * 4 + (P(),) * 8,
        check_vma=False,
    )
```

```python
import functools

import jax
import jax.numpy as jnp
from jax import lax
from jax.experimental import pallas as pl
from jax.experimental.pallas import tpu as pltpu
from jax.sharding import Mesh
from jax.sharding import PartitionSpec as P

DILATION_STEP = 256
AXES = ("outer", "core", "far", "near")
HALVES = 2
NEAR = 4
LANES = 128
ROWS = 512
F32 = jnp.float32
BF16 = jnp.bfloat16
MEGA = 1 << 20
LITTLE = pl.CostEstimate(flops=1, bytes_accessed=1, transcendentals=0)


def dot(left, right):
    return jnp.dot(left, right, preferred_element_type=F32)


def across(left, right):
    return lax.dot_general(left, right, (((0,), (0,)), ((), ())), preferred_element_type=F32)


def against(left, weight):
    return lax.dot_general(left, weight, (((1,), (1,)), ((), ())), preferred_element_type=F32)


def column(lines):
    turned = lines.astype(F32).T
    return jnp.concatenate([turned[:, k : k + 1] for k in range(lines.shape[0])], axis=0)


def tap_of(lines):
    return column(jnp.where(lines >= DILATION_STEP, 1, 0))


def call(kernel, grid, name, in_specs, out_specs, out_shape, scratch=(), aliases=None, vmem=32):
    return pl.pallas_call(
        kernel,
        grid=grid,
        in_specs=in_specs,
        out_specs=out_specs,
        out_shape=out_shape,
        scratch_shapes=list(scratch),
        input_output_aliases=aliases or {},
        cost_estimate=LITTLE,
        name=name,
        compiler_params=pltpu.CompilerParams(
            dimension_semantics=("arbitrary",) * len(grid), vmem_limit_bytes=vmem * MEGA
        ),
    )


def whole(*shape):
    return pl.BlockSpec(shape, lambda *i: (0,) * len(shape))


def tiles(rows, width, at=lambda i: i, column_block=0):
    return pl.BlockSpec((rows, width), lambda i: (at(i), column_block))


def line_tiles(at=lambda i: i):
    return pl.BlockSpec((1, ROWS // LANES, LANES), lambda i: (at(i), 0, 0))


VMEM = pl.BlockSpec(memory_space=pltpu.VMEM)
ANYWHERE = pl.BlockSpec(memory_space=pl.ANY)
SCALARS = pl.BlockSpec(memory_space=pltpu.SMEM)


def k0_body(gout, gskip, valid, w_res, w_skip, dgated, sums):
    step = pl.program_id(0)
    mask = column(valid[0])

    @pl.when(step == 0)
    def _():
        sums[...] = jnp.zeros_like(sums)

    res, skip = gout[...], gskip[...]
    dgated[...] = mask * (against(res, w_res[...]) + against(skip, w_skip[...]))
    sums[0:1, :] += jnp.sum(mask * res.astype(F32), axis=0, keepdims=True)
    sums[1:2, :] += jnp.sum(mask * skip.astype(F32), axis=0, keepdims=True)


def k0(gout, gskip, valid, w_res, w_skip):
    rows, width = gout.shape
    skip_width = gskip.shape[1]
    hidden = w_res.shape[0]
    return call(
        k0_body,
        (rows // ROWS,),
        "d_gated",
        [tiles(ROWS, width), tiles(ROWS, skip_width), line_tiles(), whole(hidden, width), whole(hidden, skip_width)],
        [tiles(ROWS, hidden), whole(8, width)],
        [jax.ShapeDtypeStruct((rows, hidden), F32), jax.ShapeDtypeStruct((8, width), F32)],
    )(gout, gskip, valid, w_res, w_skip)


def place_blocks(far, block, place, acc, theirs, mine):
    core, z, xy = place[0], place[1], place[2]
    for r in range(far):
        for c in range(NEAR):
            here = pl.ds(c * LANES, LANES)
            for k, out in ((1 - core, theirs), (core, mine)):
                rows = pl.ds(pl.multiple_of((k * far + r) * block, 16), block)
                out[c ^ xy, turned(r ^ z, far)] = acc[rows, here].astype(out.dtype)


def turned(index, count):
    bits = (count - 1).bit_length()
    result = 0
    for bit in range(bits):
        result = result | (((index >> bit) & 1) << (bits - 1 - bit))
    return result


def gates(past, now, feats, w_past, w_now, w_cond, b_conv, at, part):
    here = slice(at, at + part)
    return dot(past, w_past[:, here]) + dot(now, w_now[:, here]) + across(feats, w_cond[:, here]) + b_conv[:, here]


def slopes(pre_a, pre_s, dgated):
    act = jnp.tanh(pre_a)
    gate = 0.5 + 0.5 * jnp.tanh(0.5 * pre_s)
    slope = dgated * gate
    dpre = jnp.concatenate([slope * (1.0 - act * act), slope * act * (1.0 - gate)], axis=1)
    return (act * gate).astype(BF16), dpre.astype(BF16)


def k1_body(
    far, block, half,
    place, halo, sig, feat, pos, valid, dgated, gout, gskip, w_past, w_now, w_cond, b_conv, sums,
    gated_out, dpre_out, theirs, mine,
    acc, bias, carry,
):
    step = pl.program_id(0)
    count, width = sig.shape
    cond = feat.shape[0]
    part = gated_out.shape[1]
    top = 2 * width
    first = half * part
    second = (HALVES + half) * part

    @pl.when(step == 0)
    def _():
        acc[...] = jnp.zeros_like(acc)
        bias[...] = jnp.zeros_like(bias)
        carry[...] = halo[...]

    now = sig[...]
    delayed = jnp.concatenate([carry[...], now[: count - DILATION_STEP]], axis=0)
    carry[...] = now[count - DILATION_STEP :]
    past = delayed * tap_of(pos[0]).astype(BF16)
    feats = feat[...]
    weights = (w_past, w_now, w_cond, b_conv)
    pre_a = gates(past, now, feats, *weights, first, part)
    pre_s = gates(past, now, feats, *weights, second, part)
    gated, dpre = slopes(pre_a, pre_s, dgated[...])
    gated_out[...] = gated
    dpre_out[...] = dpre
    kept = gated * column(valid[0]).astype(BF16)
    acc[0:width, :] += across(past, dpre)
    acc[width:top, :] += across(now, dpre)
    acc[top : top + part, :] += across(kept, gout[...])
    acc[top + part : top + 2 * part, :] += across(kept, gskip[...])
    acc[top + 2 * part : top + 2 * part + cond, :] += dot(feats, dpre)
    bias[...] += jnp.sum(dpre.astype(F32).reshape(count // 8, 8, 2 * part), axis=0)

    @pl.when(step == pl.num_programs(0) - 1)
    def _():
        at = top + 2 * part + cond
        acc[at : at + 1, :] = jnp.sum(bias[...], axis=0, keepdims=True)
        acc[at + 1 : at + 2, :] = sums[half : half + 1, :]
        place_blocks(far, block, place, acc, theirs, mine)


def k1_whole_body(
    far, block, half,
    place, halo, sig, feat, pos, valid, dgated, gout, gskip, w_past, w_now, w_cond, b_conv, sums,
    gated_out, dpre_out, theirs, mine,
    acc, past_all, kept_all,
):
    rows, width = sig.shape
    cond = feat.shape[0]
    part = gated_out.shape[1]
    top = 2 * width
    first = half * part
    second = (HALVES + half) * part
    weights = (w_past, w_now, w_cond, b_conv)
    bias = jnp.zeros((8, 2 * part), F32)
    for i in range(rows // ROWS):
        here = slice(i * ROWS, (i + 1) * ROWS)
        if i == 0:
            delayed = jnp.concatenate([halo[...], sig[: ROWS - DILATION_STEP, :]], axis=0)
        else:
            delayed = sig[i * ROWS - DILATION_STEP : (i + 1) * ROWS - DILATION_STEP, :]
        past = delayed * tap_of(pos[i]).astype(BF16)
        past_all[here, :] = past
        now, feats = sig[here, :], feat[:, here]
        pre_a = gates(past, now, feats, *weights, first, part)
        pre_s = gates(past, now, feats, *weights, second, part)
        gated, dpre = slopes(pre_a, pre_s, dgated[here, first : first + part])
        gated_out[here, :] = gated
        dpre_out[here, :] = dpre
        kept_all[here, :] = gated * column(valid[i]).astype(BF16)
        bias += jnp.sum(dpre.astype(F32).reshape(ROWS // 8, 8, 2 * part), axis=0)
    at = top + 2 * part
    acc[0:width, :] = across(past_all[...], dpre_out[...])
    acc[width:top, :] = across(sig[...], dpre_out[...])
    acc[top : top + part, :] = across(kept_all[...], gout[...])
    acc[top + part : at, :] = across(kept_all[...], gskip[...])
    acc[at : at + cond, :] = dot(feat[...], dpre_out[...])
    at += cond
    acc[at : at + 1, :] = jnp.sum(bias, axis=0, keepdims=True)
    acc[at + 1 : at + 2, :] = sums[half : half + 1, :]
    acc[at + 2 :, :] = jnp.zeros((acc.shape[0] - at - 2, acc.shape[1]), F32)
    place_blocks(far, block, place, acc, theirs, mine)


def k1(half, count, far, block, place, halo, sig, feat, pos, valid, dgated, gout, gskip, w_past, w_now, w_cond, b_conv, sums):
    rows, width = sig.shape
    cond = feat.shape[0]
    hidden = w_past.shape[1] // 2
    part = hidden // HALVES
    packed = (NEAR, far, block, LANES)
    shapes = [
        jax.ShapeDtypeStruct((rows, part), BF16),
        jax.ShapeDtypeStruct((rows, 2 * part), BF16),
        jax.ShapeDtypeStruct(packed, BF16),
        jax.ShapeDtypeStruct(packed, F32),
    ]
    room = pltpu.VMEM((2 * far * block, 2 * part), F32)
    args = (place, halo, sig, feat, pos, valid, dgated, gout, gskip, w_past, w_now, w_cond, b_conv, sums)
    if count == rows:
        return call(
            functools.partial(k1_whole_body, far, block, half),
            (),
            f"gradients_{half}",
            [SCALARS] + [VMEM] * (len(args) - 1),
            [VMEM] * len(shapes),
            shapes,
            scratch=[room, pltpu.VMEM((rows, width), BF16), pltpu.VMEM((rows, part), BF16)],
            vmem=24,
        )(*args)
    lines = pl.BlockSpec((1, count // LANES, LANES), lambda i: (i, 0, 0))
    args = (*args[:4], *(x.reshape(rows // count, count // LANES, LANES) for x in args[4:6]), *args[6:])
    return call(
        functools.partial(k1_body, far, block, half),
        (rows // count,),
        f"gradients_{half}",
        [
            SCALARS,
            whole(DILATION_STEP, width),
            tiles(count, width),
            pl.BlockSpec((cond, count), lambda i: (0, i)),
            lines,
            lines,
            tiles(count, part, column_block=half),
            tiles(count, gout.shape[1]),
            tiles(count, gskip.shape[1]),
            *(whole(*w.shape) for w in (w_past, w_now, w_cond, b_conv, sums)),
        ],
        [tiles(count, part), tiles(count, 2 * part), whole(*packed), whole(*packed)],
        shapes,
        scratch=[
            room,
            pltpu.VMEM((8, 2 * part), F32),
            pltpu.VMEM((DILATION_STEP, width), BF16),
        ],
        vmem=40,
    )(*args)


def k2a_body(token, sig, valid, pos, gated_0, gated_1, dpre_0, dpre_1, w_res, b_res, w_skip, b_skip, w_past, out, skip, early):
    part = gated_0.shape[1]
    mask = column(valid[0])

    @pl.when(pl.program_id(0) == 0)
    def _():
        tap = tap_of(pos[0, : DILATION_STEP // LANES])
        early[...] = (tap * past_term(dpre_0[...], dpre_1[...], w_past, part)).astype(BF16)

    left, right = gated_0[...], gated_1[...]
    branch = dot(left, w_res[:part]) + dot(right, w_res[part:]) + b_res[...]
    out[...] = (sig[...].astype(F32) + mask * branch).astype(BF16)
    side = dot(left, w_skip[:part]) + dot(right, w_skip[part:]) + b_skip[...]
    skip[...] = (mask * side).astype(BF16)


def past_term(dpre_0, dpre_1, weight, part):
    hidden = 2 * part
    total = against(dpre_0[:, :part], weight[:, :part])
    total += against(dpre_1[:, :part], weight[:, part:hidden])
    total += against(dpre_0[:, part:], weight[:, hidden : hidden + part])
    return total + against(dpre_1[:, part:], weight[:, hidden + part :])


def k2a(token, sig, valid, pos, gated, dpre, w_res, b_res, w_skip, b_skip, w_past):
    rows, width = sig.shape
    part = gated[0].shape[1]
    hidden = 2 * part
    return call(
        k2a_body,
        (rows // ROWS,),
        "outputs",
        [
            ANYWHERE,
            tiles(ROWS, width),
            line_tiles(),
            line_tiles(),
            tiles(ROWS, part),
            tiles(ROWS, part),
            whole(DILATION_STEP, 2 * part),
            whole(DILATION_STEP, 2 * part),
            whole(hidden, width),
            whole(1, width),
            whole(*w_skip.shape),
            whole(1, w_skip.shape[1]),
            whole(*w_past.shape),
        ],
        [tiles(ROWS, width), tiles(ROWS, w_skip.shape[1]), whole(DILATION_STEP, width)],
        [
            jax.ShapeDtypeStruct((rows, width), BF16),
            jax.ShapeDtypeStruct((rows, w_skip.shape[1]), BF16),
            jax.ShapeDtypeStruct((DILATION_STEP, width), BF16),
        ],
    )(token, sig, valid, pos, *gated, *dpre, w_res, b_res, w_skip, b_skip, w_past)


def k2b_body(token, received, gout, pos, dpre_0, dpre_1, w_past, w_now, w_cond, gsig, gfeat, carry):
    part = dpre_0.shape[1] // 2

    @pl.when(pl.program_id(0) == 0)
    def _():
        carry[...] = received[...].astype(F32)

    left, right = dpre_0[...], dpre_1[...]
    tail = tap_of(pos[0]) * past_term(left, right, w_past, part)
    here = gout[...].astype(F32) + past_term(left, right, w_now, part)
    gsig[: ROWS - DILATION_STEP] = here[: ROWS - DILATION_STEP] + tail[DILATION_STEP:]
    gsig[ROWS - DILATION_STEP :] = here[ROWS - DILATION_STEP :] + carry[...]
    carry[...] = tail[:DILATION_STEP]
    hidden = 2 * part
    total = against(w_cond[:, :part], left[:, :part])
    total += against(w_cond[:, part:hidden], right[:, :part])
    total += against(w_cond[:, hidden : hidden + part], left[:, part:])
    gfeat[...] = total + against(w_cond[:, hidden + part :], right[:, part:])


def k2b(token, received, gout, pos, dpre, w_past, w_now, w_cond):
    rows, width = gout.shape
    cond = w_cond.shape[0]
    steps = rows // ROWS

    def back(i):
        return steps - 1 - i

    return call(
        k2b_body,
        (steps,),
        "input_gradients",
        [
            ANYWHERE,
            whole(DILATION_STEP, width),
            tiles(ROWS, width, back),
            line_tiles(back),
            tiles(ROWS, dpre[0].shape[1], back),
            tiles(ROWS, dpre[1].shape[1], back),
            whole(*w_past.shape),
            whole(*w_now.shape),
            whole(*w_cond.shape),
        ],
        [tiles(ROWS, width, back), pl.BlockSpec((cond, ROWS), lambda i: (0, back(i)))],
        [jax.ShapeDtypeStruct((rows, width), F32), jax.ShapeDtypeStruct((cond, rows), F32)],
        scratch=[pltpu.VMEM((DILATION_STEP, width), F32)],
    )(token, received, gout, pos, *dpre, w_past, w_now, w_cond)


def unpack_body(far, block, half, width, cond, place, mine, theirs, *refs):
    past, now, res, skip, conds, b_conv, b_own = refs[-8:-1]
    room = refs[-1]
    part = res.shape[0]
    core, z, xy = place[0], place[1], place[2]

    @pl.when(pl.program_id(0) == 0)
    def _():
        for k, ref in ((core, mine), (1 - core, theirs)):
            for c in range(NEAR):
                for r in range(far):
                    rows = pl.ds(pl.multiple_of((k * far + (r ^ z)) * block, 16), block)
                    room[c ^ xy, rows, :] = ref[c, turned(r, far)]

    for j in range(NEAR // 2):
        c = pl.program_id(0) * (NEAR // 2) + j
        here = pl.ds(j * LANES, LANES)
        top = 0
        for ref in (past, now, res, skip, conds):
            count = ref.shape[0]
            ref[:, here] = room[c, top : top + count, :].astype(F32)
            top += count
        last = room[c, top : top + 16, :].astype(F32)
        b_conv[:, here] = last[0:1]
        b_own[:, here] = last[1:2]


def unpack(half, far, block, place, mine, theirs, width, cond, hidden, skip_width, before):
    part = hidden // HALVES
    gates = 2 * hidden
    wide = [
        pl.BlockSpec((size, part), lambda s: (0, HALVES * s + half)) for size in (width, width)
    ]
    tall = [pl.BlockSpec((part, size // 2), lambda s: (half, s)) for size in (width, skip_width)]
    rest = [
        pl.BlockSpec((cond, part), lambda s: (0, HALVES * s + half)),
        pl.BlockSpec((1, part), lambda s: (0, HALVES * s + half)),
        pl.BlockSpec((1, (width, skip_width)[half] // 2), lambda s: (0, s)),
    ]
    shapes = [
        (width, gates), (width, gates), (hidden, width), (hidden, skip_width), (cond, gates), (1, gates),
        (1, (width, skip_width)[half]),
    ]
    packed = (NEAR, far, block, LANES)
    return call(
        functools.partial(unpack_body, far, block, half, width, cond),
        (2,),
        f"unpack_{half}",
        [SCALARS, whole(*packed), whole(*packed)] + [pl.BlockSpec(memory_space=pl.ANY)] * len(before),
        wide + tall + rest,
        [jax.ShapeDtypeStruct(shape, F32) for shape in shapes],
        scratch=[pltpu.VMEM((NEAR, 2 * far * block, LANES), BF16)],
        aliases={3 + k: k for k in range(len(before))},
    )(place, mine, theirs, *before)


def swapped(x, axis, k):
    return lax.ppermute(x, axis, [(i, i ^ k) for i in range(lax.axis_size(axis))])


def exchanged(blocks, axis):
    return [swapped(block, axis, k + 1) for k, block in enumerate(blocks)]


def add_body(token, kept, *refs):
    count = kept.shape[0]
    got, outs = refs[:-count], refs[-count:]
    for k in range(count):
        total = kept[k]
        for ref in got:
            total = total + ref[k].astype(F32)
        outs[k][...] = total.astype(outs[k].dtype)


def added(token, kept, got, name, final=BF16):
    count, *block = kept.shape
    first, *rest = pl.pallas_call(
        add_body,
        in_specs=[ANYWHERE, VMEM] + [VMEM] * len(got),
        out_specs=[VMEM] * count,
        out_shape=[jax.ShapeDtypeStruct(block, final)] + [jax.ShapeDtypeStruct(block, BF16)] * (count - 1),
        name=name,
        cost_estimate=LITTLE,
        compiler_params=pltpu.CompilerParams(vmem_limit_bytes=16 * MEGA),
    )(token, kept, *got)
    return first, rest


def doubled(total, axis, bit):
    mine = total.astype(BF16)
    return mine, swapped(mine, axis, 1 << bit)


def far_summed(kept, got):
    bits = (lax.axis_size("far") - 1).bit_length()
    total = kept + got.astype(F32)
    for bit in range(1, bits - 1):
        half = total.shape[0] // 2
        total = total[:half] + swapped(total[half:].astype(BF16), "far", 1 << bit).astype(F32)
    mine, got = doubled(total, "far", bits - 1)
    total = mine.astype(F32) + got[::-1].astype(F32)
    for bit in range((lax.axis_size("outer") - 1).bit_length()):
        mine, got = doubled(total, "outer", bit)
        total = mine.astype(F32) + got.astype(F32)
    total = total.astype(BF16)
    for bit in reversed(range(bits - 1)):
        total = jnp.concatenate([total, swapped(total, "far", 1 << bit)])
    return total


def halves(x):
    return x.reshape(2, x.shape[0] // 2, *x.shape[1:])


def gathered(block, axis):
    return jnp.stack([block] + [swapped(block, axis, k) for k in range(1, lax.axis_size(axis))])


def in_hbm(x):
    return pltpu.with_memory_space_constraint(x, pltpu.HBM)


def passed_along(x, by):
    peers = lax.axis_size(AXES)
    pairs = [(i, i + by) for i in range(peers) if 0 <= i + by < peers]
    return lax.ppermute(x, AXES, pairs)


def body(
    signal,
    features,
    position,
    valid,
    w_past,
    w_now,
    b_conv,
    w_cond,
    w_res,
    b_res,
    w_skip,
    b_skip,
    grad_out,
    grad_skip,
):
    rows, width = signal.shape
    features = features.T
    cond = features.shape[0]
    hidden = w_res.shape[0]
    skip_width = w_skip.shape[1]
    far = lax.axis_size("far")
    used = 2 * width + 2 * (hidden // HALVES) + cond + 2
    block = -(-used // (2 * far * 16)) * 16
    place = jnp.stack([lax.axis_index(name) for name in ("core", "far", "near")]).astype(jnp.int32)
    lines = (rows // ROWS, ROWS // LANES, LANES)
    pos, val = position.reshape(lines), valid.reshape(lines)
    b_conv, b_res, b_skip = (b.reshape(1, -1) for b in (b_conv, b_res, b_skip))

    halo = passed_along(signal[rows - DILATION_STEP :], 1)
    dgated, sums = k0(in_hbm(grad_out), in_hbm(grad_skip), val, in_hbm(w_res), in_hbm(w_skip))
    gated, dpre, packed = [], [], []
    for half in range(HALVES):
        held = (signal, grad_out, grad_skip, w_past, w_now)
        if half == 0:
            held = tuple(in_hbm(x) for x in held)
        one, other, *both = k1(
            half, (1024, rows)[half], far, block, place, halo, held[0], features, pos, val, dgated, *held[1:],
            w_cond, b_conv, sums,
        )
        gated.append(one)
        dpre.append(other)
        packed.append(both)
    crossed = [swapped(theirs, "core", 1) for theirs, _ in packed]
    kept_0, sent_0 = added(place, packed[0][1], [crossed[0]], "core_sum_0", F32)
    near_0 = exchanged(sent_0, "near")
    output, skip_out, early = k2a(sent_0[0], signal, val, pos, gated, dpre, w_res, b_res, w_skip, b_skip, w_past)
    received = passed_along(early, -1)
    kept_1, sent_1 = added(early, packed[1][1], [crossed[1]], "core_sum_1", F32)
    near_1 = exchanged(sent_1, "near")
    kept_0, sent_0 = added(sent_1[0], halves(kept_0), [halves(x) for x in near_0], "near_sum_0", F32)
    far_0 = swapped(sent_0[0], "far", 1)
    grad_signal, grad_features = k2b(sent_0[0], received, in_hbm(grad_out), pos, dpre, w_past, w_now, w_cond)
    ends_0 = far_summed(kept_0, far_0)
    kept_1, sent_1 = added(grad_features, halves(kept_1), [halves(x) for x in near_1], "near_sum_1", F32)
    far_1 = swapped(sent_1[0], "far", 1)
    whole_0 = gathered(ends_0, "near")
    ends_1 = far_summed(kept_1, far_1)
    whole_1 = gathered(ends_1, "near")
    done, own = [], []
    for half, blocks in enumerate((whole_0, whole_1)):
        others = swapped(blocks, "core", 1)
        *done, last = unpack(half, far, block, place, blocks, others, width, cond, hidden, skip_width, done)
        own.append(last)
    g_past, g_now, g_res, g_skip, g_cond, g_bias = done
    return (
        output,
        skip_out,
        grad_signal,
        grad_features.T,
        g_past,
        g_now,
        g_bias.reshape(-1),
        g_cond,
        g_res,
        own[0].reshape(-1),
        g_skip,
        own[1].reshape(-1),
    )


def solution(mesh):
    row, col = mesh.shape["row"], mesh.shape["col"]
    fine = Mesh(mesh.devices.reshape(row // 2, 2, col // NEAR, NEAR), AXES)
    rows = P(AXES, None)
    line = P(AXES)
    return jax.shard_map(
        body,
        mesh=fine,
        in_specs=(rows, rows, line, line) + (P(),) * 8 + (rows, rows),
        out_specs=(rows,) * 4 + (P(),) * 8,
        check_vma=False,
    )
```

```python
import functools

import jax
import jax.numpy as jnp
from jax import lax
from jax.experimental import pallas as pl
from jax.experimental.pallas import tpu as pltpu
from jax.sharding import Mesh
from jax.sharding import PartitionSpec as P

DILATION_STEP = 256
AXES = ("outer", "core", "far", "near")
HALVES = 2
NEAR = 4
LANES = 128
ROWS = 512
F32 = jnp.float32
BF16 = jnp.bfloat16
MEGA = 1 << 20
LITTLE = pl.CostEstimate(flops=1, bytes_accessed=1, transcendentals=0)


def dot(left, right):
    return jnp.dot(left, right, preferred_element_type=F32)


def across(left, right):
    return lax.dot_general(left, right, (((0,), (0,)), ((), ())), preferred_element_type=F32)


def against(left, weight):
    return lax.dot_general(left, weight, (((1,), (1,)), ((), ())), preferred_element_type=F32)


def column(lines):
    turned = lines.astype(F32).T
    return jnp.concatenate([turned[:, k : k + 1] for k in range(lines.shape[0])], axis=0)


def tap_of(lines):
    return column(jnp.where(lines >= DILATION_STEP, 1, 0))


def call(kernel, name, in_specs, out_specs, out_shape, scratch=(), aliases=None, grid=(), vmem=24):
    return pl.pallas_call(
        kernel,
        grid=grid,
        in_specs=in_specs,
        out_specs=out_specs,
        out_shape=out_shape,
        scratch_shapes=list(scratch),
        input_output_aliases=aliases or {},
        cost_estimate=LITTLE,
        name=name,
        compiler_params=pltpu.CompilerParams(vmem_limit_bytes=vmem * MEGA),
    )


def whole(*shape):
    return pl.BlockSpec(shape, lambda *i: (0,) * len(shape))


VMEM = pl.BlockSpec(memory_space=pltpu.VMEM)
ANYWHERE = pl.BlockSpec(memory_space=pl.ANY)
SCALARS = pl.BlockSpec(memory_space=pltpu.SMEM)


def k0_body(*refs):
    count = (len(refs) - 3) // 2
    sources, here = refs[:count], refs[count : 2 * count]
    dgated, sums, sems = refs[2 * count :]
    valid, w_res, w_skip, gout, gskip = here[:5]
    tiled = (3, 4)
    steps = gout.shape[0] // ROWS
    used = 0
    copies = {}

    def start(k, i=None):
        nonlocal used
        at = (slice(None),) if i is None else (pl.ds(i * ROWS, ROWS),)
        copies[k, i] = pltpu.make_async_copy(sources[k].at[at], here[k].at[at], sems.at[used])
        copies[k, i].start()
        used += 1

    for k in range(3):
        start(k)
    for i in range(steps):
        for k in tiled:
            start(k, i)
    for k in range(5, count):
        start(k)
    for k in range(3):
        copies.pop((k, None)).wait()
    total = [jnp.zeros((8, gout.shape[1]), F32), jnp.zeros((8, gskip.shape[1]), F32)]
    for i in range(steps):
        for k in tiled:
            copies.pop((k, i)).wait()
        rows = slice(i * ROWS, (i + 1) * ROWS)
        mask = column(valid[i])
        res, skip = gout[rows, :], gskip[rows, :]
        dgated[rows, :] = mask * (against(res, w_res[...]) + against(skip, w_skip[...]))
        for k, x in enumerate((res, skip)):
            total[k] += jnp.sum((mask * x.astype(F32)).reshape(ROWS // 8, 8, x.shape[1]), axis=0)
    for k in range(2):
        sums[k : k + 1, :] = jnp.sum(total[k], axis=0, keepdims=True)
    for copy in copies.values():
        copy.wait()


def k0(valid, w_res, w_skip, gout, gskip, *others):
    rows, width = gout.shape
    sources = [in_hbm(x) for x in (valid, w_res, w_skip, gout, gskip, *others)]
    shapes = [jax.ShapeDtypeStruct(x.shape, x.dtype) for x in sources]
    shapes += [jax.ShapeDtypeStruct((rows, w_res.shape[0]), F32), jax.ShapeDtypeStruct((8, width), F32)]
    count = len(sources) + 2 * (rows // ROWS - 1)
    return call(
        k0_body,
        "load",
        [ANYWHERE] * len(sources),
        [VMEM] * len(shapes),
        shapes,
        scratch=[pltpu.SemaphoreType.DMA((count,))],
    )(*sources)


def place_blocks(far, block, place, acc, theirs, mine):
    core, z, xy = place[0], place[1], place[2]
    for r in range(far):
        for c in range(NEAR):
            here = pl.ds(c * LANES, LANES)
            for k, out in ((1 - core, theirs), (core, mine)):
                rows = pl.ds(pl.multiple_of((k * far + r) * block, 16), block)
                out[c ^ xy, turned(r ^ z, far)] = acc[rows, here].astype(out.dtype)


def turned(index, count):
    bits = (count - 1).bit_length()
    result = 0
    for bit in range(bits):
        result = result | (((index >> bit) & 1) << (bits - 1 - bit))
    return result


def gates(past, now, feats, w_past, w_now, w_cond, b_conv, at, part):
    here = slice(at, at + part)
    return dot(past, w_past[:, here]) + dot(now, w_now[:, here]) + across(feats, w_cond[:, here]) + b_conv[:, here]


def slopes(pre_a, pre_s, dgated):
    act = jnp.tanh(pre_a)
    gate = 0.5 + 0.5 * jnp.tanh(0.5 * pre_s)
    slope = dgated * gate
    dpre = jnp.concatenate([slope * (1.0 - act * act), slope * act * (1.0 - gate)], axis=1)
    return (act * gate).astype(BF16), dpre.astype(BF16)


def k1_body(
    far, block, half,
    place, halo, sig, feat, pos, valid, dgated, gout, gskip, w_past, w_now, w_cond, b_conv, sums,
    gated_out, dpre_out, theirs, mine,
    acc, past_all, kept_all,
):
    rows, width = sig.shape
    cond = feat.shape[0]
    part = gated_out.shape[1]
    top = 2 * width
    first = half * part
    second = (HALVES + half) * part
    weights = (w_past, w_now, w_cond, b_conv)
    bias = jnp.zeros((8, 2 * part), F32)
    for i in range(rows // ROWS):
        here = slice(i * ROWS, (i + 1) * ROWS)
        if i == 0:
            delayed = jnp.concatenate([halo[...], sig[: ROWS - DILATION_STEP, :]], axis=0)
        else:
            delayed = sig[i * ROWS - DILATION_STEP : (i + 1) * ROWS - DILATION_STEP, :]
        past = delayed * tap_of(pos[i]).astype(BF16)
        past_all[here, :] = past
        now, feats = sig[here, :], feat[:, here]
        pre_a = gates(past, now, feats, *weights, first, part)
        pre_s = gates(past, now, feats, *weights, second, part)
        gated, dpre = slopes(pre_a, pre_s, dgated[here, first : first + part])
        gated_out[here, :] = gated
        dpre_out[here, :] = dpre
        kept_all[here, :] = gated * column(valid[i]).astype(BF16)
        bias += jnp.sum(dpre.astype(F32).reshape(ROWS // 8, 8, 2 * part), axis=0)
    at = top + 2 * part
    acc[0:width, :] = across(past_all[...], dpre_out[...])
    acc[width:top, :] = across(sig[...], dpre_out[...])
    acc[top : top + part, :] = across(kept_all[...], gout[...])
    acc[top + part : at, :] = across(kept_all[...], gskip[...])
    acc[at : at + cond, :] = dot(feat[...], dpre_out[...])
    at += cond
    acc[at : at + 1, :] = jnp.sum(bias, axis=0, keepdims=True)
    acc[at + 1 : at + 2, :] = sums[half : half + 1, :]
    acc[at + 2 :, :] = jnp.zeros((acc.shape[0] - at - 2, acc.shape[1]), F32)
    place_blocks(far, block, place, acc, theirs, mine)


def k1(half, far, block, place, halo, sig, feat, pos, valid, dgated, gout, gskip, w_past, w_now, w_cond, b_conv, sums):
    rows, width = sig.shape
    part = w_past.shape[1] // 2 // HALVES
    packed = (NEAR, far, block, LANES)
    args = (place, halo, sig, feat, pos, valid, dgated, gout, gskip, w_past, w_now, w_cond, b_conv, sums)
    return call(
        functools.partial(k1_body, far, block, half),
        f"gradients_{half}",
        [SCALARS] + [VMEM] * (len(args) - 1),
        [VMEM] * 4,
        [
            jax.ShapeDtypeStruct((rows, part), BF16),
            jax.ShapeDtypeStruct((rows, 2 * part), BF16),
            jax.ShapeDtypeStruct(packed, BF16),
            jax.ShapeDtypeStruct(packed, F32),
        ],
        scratch=[
            pltpu.VMEM((2 * far * block, 2 * part), F32),
            pltpu.VMEM((rows, width), BF16),
            pltpu.VMEM((rows, part), BF16),
        ],
    )(*args)


def past_term(dpre_0, dpre_1, weight, part):
    hidden = 2 * part
    total = against(dpre_0[:, :part], weight[:, :part])
    total += against(dpre_1[:, :part], weight[:, part:hidden])
    total += against(dpre_0[:, part:], weight[:, hidden : hidden + part])
    return total + against(dpre_1[:, part:], weight[:, hidden + part :])


def k2a_body(
    token, sig, valid, pos, gated_0, gated_1, dpre_0, dpre_1, w_res, b_res, w_skip, b_skip, w_past,
    out, skip, early, rooms, sems,
):
    part = gated_0.shape[1]
    tap = tap_of(pos[0, : DILATION_STEP // LANES])
    first = slice(0, DILATION_STEP)
    early[...] = (tap * past_term(dpre_0[first, :], dpre_1[first, :], w_past, part)).astype(BF16)
    copies = []
    for i in range(sig.shape[0] // ROWS):
        rows = slice(i * ROWS, (i + 1) * ROWS)
        mask = column(valid[i])
        left, right = gated_0[rows, :], gated_1[rows, :]
        branch = dot(left, w_res[:part, :]) + dot(right, w_res[part:, :]) + b_res[...]
        rooms[i, 0] = (sig[rows, :].astype(F32) + mask * branch).astype(BF16)
        side = dot(left, w_skip[:part, :]) + dot(right, w_skip[part:, :]) + b_skip[...]
        rooms[i, 1] = (mask * side).astype(BF16)
        for k, ref in enumerate((out, skip)):
            copies.append(pltpu.make_async_copy(rooms.at[i, k], ref.at[pl.ds(i * ROWS, ROWS)], sems.at[i, k]))
            copies[-1].start()
    for copy in copies:
        copy.wait()


def k2a(token, sig, valid, pos, gated, dpre, w_res, b_res, w_skip, b_skip, w_past):
    rows, width = sig.shape
    return call(
        k2a_body,
        "outputs",
        [ANYWHERE] + [VMEM] * 12,
        [ANYWHERE, ANYWHERE, VMEM],
        [
            jax.ShapeDtypeStruct((rows, width), BF16),
            jax.ShapeDtypeStruct((rows, w_skip.shape[1]), BF16),
            jax.ShapeDtypeStruct((DILATION_STEP, width), BF16),
        ],
        scratch=[
            pltpu.VMEM((rows // ROWS, 2, ROWS, width), BF16),
            pltpu.SemaphoreType.DMA((rows // ROWS, 2)),
        ],
    )(token, sig, valid, pos, *gated, *dpre, w_res, b_res, w_skip, b_skip, w_past)


def k2b_body(step, token, received, gout, pos, dpre_0, dpre_1, w_past, w_now, w_cond, *refs):
    gsig, gfeat, mark, room, room_feat, sems = refs[-6:]
    rows, width = gout.shape
    part = dpre_0.shape[1] // 2
    hidden = 2 * part
    begin = step * ROWS
    here = slice(begin, begin + ROWS)
    left, right = dpre_0[here, :], dpre_1[here, :]
    after = slice(begin + DILATION_STEP, min(begin + DILATION_STEP + ROWS, rows))
    lines = jnp.concatenate([pos[step, DILATION_STEP // LANES :], pos[min(step + 1, rows // ROWS - 1), : DILATION_STEP // LANES]])
    tap = tap_of(lines)[: after.stop - after.start]
    copies = []
    wide = 2 * LANES
    for k in range(width // wide):
        some = slice(k * wide, (k + 1) * wide)
        tail = tap * past_term(dpre_0[after, :], dpre_1[after, :], w_past[some, :], part)
        if tail.shape[0] < ROWS:
            tail = jnp.concatenate([tail, received[:, some].astype(F32)], axis=0)
        room[k] = gout[here, some].astype(F32) + past_term(left, right, w_now[some, :], part) + tail
        copies.append(pltpu.make_async_copy(room.at[k], gsig.at[pl.ds(begin, ROWS), pl.ds(k * wide, wide)], sems.at[k]))
        copies[-1].start()
    total = against(w_cond[:, :part], left[:, :part])
    total += against(w_cond[:, part:hidden], right[:, :part])
    total += against(w_cond[:, hidden : hidden + part], left[:, part:])
    room_feat[...] = total + against(w_cond[:, hidden + part :], right[:, part:])
    copies.append(pltpu.make_async_copy(room_feat, gfeat.at[:, pl.ds(begin, ROWS)], sems.at[width // wide]))
    copies[-1].start()
    mark[...] = jnp.zeros_like(mark)
    for copy in copies:
        copy.wait()


def k2b(step, token, received, gout, pos, dpre, w_past, w_now, w_cond, before):
    rows, width = gout.shape
    cond = w_cond.shape[0]
    count = width // (2 * LANES)
    return call(
        functools.partial(k2b_body, step),
        f"input_gradients_{step}",
        [ANYWHERE] + [VMEM] * 8 + [ANYWHERE] * len(before),
        [ANYWHERE, ANYWHERE, VMEM],
        [
            jax.ShapeDtypeStruct((rows, width), F32),
            jax.ShapeDtypeStruct((cond, rows), F32),
            jax.ShapeDtypeStruct((8, LANES), F32),
        ],
        scratch=[
            pltpu.VMEM((count, ROWS, 2 * LANES), F32),
            pltpu.VMEM((cond, ROWS), F32),
            pltpu.SemaphoreType.DMA((count + 1,)),
        ],
        aliases={9 + k: k for k in range(len(before))},
    )(token, received, gout, pos, *dpre, w_past, w_now, w_cond, *before)


def unpack_body(far, block, half, width, cond, token, place, mine, theirs, *refs):
    past, now, res, skip, conds, b_conv, b_own = refs[-8:-1]
    room = refs[-1]
    part = res.shape[0]
    core, z, xy = place[0], place[1], place[2]

    @pl.when(pl.program_id(0) == 0)
    def _():
        for k, ref in ((core, mine), (1 - core, theirs)):
            for c in range(NEAR):
                for r in range(far):
                    rows = pl.ds(pl.multiple_of((k * far + (r ^ z)) * block, 16), block)
                    room[c ^ xy, rows, :] = ref[c, turned(r, far)]

    for j in range(NEAR // 2):
        c = pl.program_id(0) * (NEAR // 2) + j
        here = pl.ds(j * LANES, LANES)
        top = 0
        for ref in (past, now, res, skip, conds):
            count = ref.shape[0]
            ref[:, here] = room[c, top : top + count, :].astype(F32)
            top += count
        last = room[c, top : top + 16, :].astype(F32)
        b_conv[:, here] = last[0:1]
        b_own[:, here] = last[1:2]


def unpack(half, token, far, block, place, mine, theirs, width, cond, hidden, skip_width, before):
    part = hidden // HALVES
    gates = 2 * hidden
    wide = [
        pl.BlockSpec((size, part), lambda s: (0, HALVES * s + half)) for size in (width, width)
    ]
    tall = [pl.BlockSpec((part, size // 2), lambda s: (half, s)) for size in (width, skip_width)]
    rest = [
        pl.BlockSpec((cond, part), lambda s: (0, HALVES * s + half)),
        pl.BlockSpec((1, part), lambda s: (0, HALVES * s + half)),
        pl.BlockSpec((1, (width, skip_width)[half] // 2), lambda s: (0, s)),
    ]
    shapes = [
        (width, gates), (width, gates), (hidden, width), (hidden, skip_width), (cond, gates), (1, gates),
        (1, (width, skip_width)[half]),
    ]
    packed = (NEAR, far, block, LANES)
    return call(
        functools.partial(unpack_body, far, block, half, width, cond),
        f"unpack_{half}",
        [ANYWHERE, SCALARS, whole(*packed), whole(*packed)] + [pl.BlockSpec(memory_space=pl.ANY)] * len(before),
        wide + tall + rest,
        [jax.ShapeDtypeStruct(shape, F32) for shape in shapes],
        scratch=[pltpu.VMEM((NEAR, 2 * far * block, LANES), BF16)],
        aliases={4 + k: k for k in range(len(before))},
        grid=(2,),
    )(token, place, mine, theirs, *before)


def swapped(x, axis, k):
    return lax.ppermute(x, axis, [(i, i ^ k) for i in range(lax.axis_size(axis))])


def exchanged(blocks):
    return [swapped(block, "near", k + 1) for k, block in enumerate(blocks)]


def add_body(sizes, token, *refs):
    count = len(sizes)
    kept, got, outs = refs[0], refs[1:-count], refs[-count:]
    at = 0
    for out, size in zip(outs, sizes):
        for k in range(size):
            total = kept[at + k].astype(F32)
            for ref in got:
                total = total + ref[at + k].astype(F32)
            out[k] = total.astype(out.dtype)
        at += size


def added(name, token, kept, got, outs):
    sizes = [size for size, _ in outs]
    result = call(
        functools.partial(add_body, sizes),
        name,
        [ANYWHERE] + [VMEM] * (1 + len(got)),
        [VMEM] * len(outs),
        [jax.ShapeDtypeStruct((size, *kept.shape[1:]), dtype) for size, dtype in outs],
    )(token, kept, *got)
    return result


def mirror_body(token, mine, got, out):
    count = mine.shape[0]
    for k in range(count):
        out[k] = (mine[k].astype(F32) + got[count - 1 - k].astype(F32)).astype(out.dtype)


def mirrored(name, token, mine, got):
    return call(
        mirror_body,
        name,
        [ANYWHERE, VMEM, VMEM],
        VMEM,
        jax.ShapeDtypeStruct(mine.shape, BF16),
    )(token, mine, got)


def join_body(token, *refs):
    out = refs[-1]
    at = 0
    for ref in refs[:-1]:
        out[at : at + ref.shape[0]] = ref[...]
        at += ref.shape[0]


def joined(name, token, parts):
    count = sum(part.shape[0] for part in parts)
    return call(
        join_body,
        name,
        [ANYWHERE] + [VMEM] * len(parts),
        VMEM,
        jax.ShapeDtypeStruct((count, *parts[0].shape[1:]), BF16),
    )(token, *parts)


def over_outer(total):
    for bit in range((lax.axis_size("outer") - 1).bit_length()):
        total = (total.astype(F32) + swapped(total, "outer", 1 << bit).astype(F32)).astype(BF16)
    return total


def passed_along(x, by):
    peers = lax.axis_size(AXES)
    pairs = [(i, i + by) for i in range(peers) if 0 <= i + by < peers]
    return lax.ppermute(x, AXES, pairs)


def in_hbm(x):
    return pltpu.with_memory_space_constraint(x, pltpu.HBM)


def body(
    signal,
    features,
    position,
    valid,
    w_past,
    w_now,
    b_conv,
    w_cond,
    w_res,
    b_res,
    w_skip,
    b_skip,
    grad_out,
    grad_skip,
):
    rows, width = signal.shape
    features = features.T
    cond = features.shape[0]
    hidden = w_res.shape[0]
    skip_width = w_skip.shape[1]
    far = lax.axis_size("far")
    far_bits = (far - 1).bit_length()
    used = 2 * width + 2 * (hidden // HALVES) + cond + 2
    block = -(-used // (2 * far * 16)) * 16
    place = jnp.stack([lax.axis_index(name) for name in ("core", "far", "near")]).astype(jnp.int32)
    lines = (rows // ROWS, ROWS // LANES, LANES)
    pos, val = position.reshape(lines), valid.reshape(lines)
    b_conv, b_res, b_skip = (b.reshape(1, -1) for b in (b_conv, b_res, b_skip))

    halo = passed_along(signal[rows - DILATION_STEP :], 1)
    (
        val, w_res, w_skip, grad_out, grad_skip, pos, b_conv, features, w_cond, signal, w_past, w_now,
        b_res, b_skip, dgated, sums,
    ) = k0(
        val, w_res, w_skip, grad_out, grad_skip, pos, b_conv, features, w_cond, signal, w_past, w_now, b_res, b_skip
    )
    gated, dpre, packed = [], [], []
    for half in range(HALVES):
        one, other, *both = k1(
            half, far, block, place, halo, signal, features, pos, val, dgated, grad_out, grad_skip,
            w_past, w_now, w_cond, b_conv, sums,
        )
        gated.append(one)
        dpre.append(other)
        packed.append(both)

    def core_sum(half, token):
        theirs, mine = packed[half]
        kept, *sent = added(
            f"core_sum_{half}", token, mine, [swapped(theirs, "core", 1)], [(1, F32)] + [(1, BF16)] * (NEAR - 1)
        )
        return kept[0], exchanged([x[0] for x in sent])

    def near_sum(half, token, kept, got):
        kept, sent = added(f"near_sum_{half}", token, kept, got, [(far // 2, F32), (far // 2, BF16)])
        return kept, swapped(sent, "far", 1)

    def far_sum(half, token, kept, got):
        for bit in range(1, far_bits - 1):
            size = kept.shape[0] // 2
            kept, sent = added(f"far_sum_{half}_{bit}", token, kept, [got], [(size, F32), (size, BF16)])
            got = swapped(sent, "far", 1 << bit)
        (mine,) = added(f"far_sum_{half}", token, kept, [got], [(kept.shape[0], BF16)])
        return mine, swapped(mine, "far", 1 << (far_bits - 1))

    def far_end(half, token, mine, got):
        total = over_outer(mirrored(f"far_end_{half}", token, mine, got))
        return total, swapped(total, "far", 1 << (far_bits - 2))

    def far_join(half, token, mine, got):
        total = joined(f"far_join_{half}", token, [mine, got])
        for bit in reversed(range(far_bits - 2)):
            total = joined(f"far_join_{half}_{bit}", token, [total, swapped(total, "far", 1 << bit)])
        return total, exchanged([total] * (NEAR - 1))

    def near_join(half, token, mine, got):
        total = joined(f"near_join_{half}", token, [mine[None]] + [x[None] for x in got])
        return total, swapped(total, "core", 1)

    def input_gradients(step, token, before):
        return k2b(step, token, received, grad_out, pos, dpre, w_past, w_now, w_cond, before)

    kept_0, got_0 = core_sum(0, place)
    output, skip_out, early = k2a(kept_0, signal, val, pos, gated, dpre, w_res, b_res, w_skip, b_skip, w_past)
    received = passed_along(early, -1)
    kept_1, got_1 = core_sum(1, early)
    kept_0, got_0 = near_sum(0, kept_1, kept_0, got_0)
    *grads, mark = input_gradients(0, kept_0, [])
    mine_0, got_0 = far_sum(0, mark, kept_0, got_0)
    *grads, mark = input_gradients(1, mine_0, grads)
    *grads, mark = input_gradients(2, mark, grads)
    kept_1, got_1 = near_sum(1, mark, kept_1, got_1)
    mine_0, got_0 = far_end(0, kept_1, mine_0, got_0)
    *grads, mark = input_gradients(3, mine_0, grads)
    mine_1, got_1 = far_sum(1, mark, kept_1, got_1)
    mine_0, got_0 = far_join(0, mine_1, mine_0, got_0)
    mine_1, got_1 = far_end(1, mine_0, mine_1, got_1)
    mine_1, got_1 = far_join(1, mine_1, mine_1, got_1)
    mine_0, got_0 = near_join(0, mine_1, mine_0, got_0)
    *done, own_0 = unpack(0, mine_1, far, block, place, mine_0, got_0, width, cond, hidden, skip_width, [])
    mine_1, got_1 = near_join(1, own_0, mine_1, got_1)
    *done, own_1 = unpack(1, own_0, far, block, place, mine_1, got_1, width, cond, hidden, skip_width, done)
    grad_signal, grad_features = grads
    own = [own_0, own_1]
    g_past, g_now, g_res, g_skip, g_cond, g_bias = done
    return (
        output,
        skip_out,
        grad_signal,
        grad_features.T,
        g_past,
        g_now,
        g_bias.reshape(-1),
        g_cond,
        g_res,
        own[0].reshape(-1),
        g_skip,
        own[1].reshape(-1),
    )


def solution(mesh):
    row, col = mesh.shape["row"], mesh.shape["col"]
    fine = Mesh(mesh.devices.reshape(row // 2, 2, col // NEAR, NEAR), AXES)
    rows = P(AXES, None)
    line = P(AXES)
    return jax.shard_map(
        body,
        mesh=fine,
        in_specs=(rows, rows, line, line) + (P(),) * 8 + (rows, rows),
        out_specs=(rows,) * 4 + (P(),) * 8,
        check_vma=False,
    )
```

```python
import functools

import jax
import jax.numpy as jnp
from jax import lax
from jax.experimental import pallas as pl
from jax.experimental.pallas import tpu as pltpu
from jax.sharding import Mesh
from jax.sharding import PartitionSpec as P

DILATION_STEP = 256
AXES = ("outer", "core", "far", "near")
HALVES = 2
NEAR = 4
LANES = 128
ROWS = 512
F32 = jnp.float32
BF16 = jnp.bfloat16
MEGA = 1 << 20
LITTLE = pl.CostEstimate(flops=1, bytes_accessed=1, transcendentals=0)


def dot(left, right):
    return jnp.dot(left, right, preferred_element_type=F32)


def across(left, right):
    return lax.dot_general(left, right, (((0,), (0,)), ((), ())), preferred_element_type=F32)


def against(left, weight):
    return lax.dot_general(left, weight, (((1,), (1,)), ((), ())), preferred_element_type=F32)


def column(lines):
    turned = lines.astype(F32).T
    return jnp.concatenate([turned[:, k : k + 1] for k in range(lines.shape[0])], axis=0)


def tap_of(lines):
    return column(jnp.where(lines >= DILATION_STEP, 1, 0))


def call(kernel, name, in_specs, out_specs, out_shape, scratch=(), aliases=None, grid=(), vmem=24):
    return pl.pallas_call(
        kernel,
        grid=grid,
        in_specs=in_specs,
        out_specs=out_specs,
        out_shape=out_shape,
        scratch_shapes=list(scratch),
        input_output_aliases=aliases or {},
        cost_estimate=LITTLE,
        name=name,
        compiler_params=pltpu.CompilerParams(vmem_limit_bytes=vmem * MEGA),
    )


def whole(*shape):
    return pl.BlockSpec(shape, lambda *i: (0,) * len(shape))


VMEM = pl.BlockSpec(memory_space=pltpu.VMEM)
ANYWHERE = pl.BlockSpec(memory_space=pl.ANY)


def k0_body(*refs):
    count = (len(refs) - 3) // 2
    sources, here = refs[:count], refs[count : 2 * count]
    dgated, sums, sems = refs[2 * count :]
    valid, w_res, w_skip, gout, gskip = here[:5]
    tiled = (3, 4)
    steps = gout.shape[0] // ROWS
    used = 0
    copies = {}

    def start(k, i=None):
        nonlocal used
        at = (slice(None),) if i is None else (pl.ds(i * ROWS, ROWS),)
        copies[k, i] = pltpu.make_async_copy(sources[k].at[at], here[k].at[at], sems.at[used])
        copies[k, i].start()
        used += 1

    for k in range(3):
        start(k)
    for i in range(steps):
        for k in tiled:
            start(k, i)
    for k in range(5, count):
        start(k)
    for k in range(3):
        copies.pop((k, None)).wait()
    total = [jnp.zeros((8, gout.shape[1]), F32), jnp.zeros((8, gskip.shape[1]), F32)]
    for i in range(steps):
        for k in tiled:
            copies.pop((k, i)).wait()
        rows = slice(i * ROWS, (i + 1) * ROWS)
        mask = column(valid[i])
        res, skip = gout[rows, :], gskip[rows, :]
        dgated[rows, :] = mask * (against(res, w_res[...]) + against(skip, w_skip[...]))
        for k, x in enumerate((res, skip)):
            total[k] += jnp.sum((mask * x.astype(F32)).reshape(ROWS // 8, 8, x.shape[1]), axis=0)
    for k in range(2):
        sums[k : k + 1, :] = jnp.sum(total[k], axis=0, keepdims=True)
    for copy in copies.values():
        copy.wait()


def k0(valid, w_res, w_skip, gout, gskip, *others):
    rows, width = gout.shape
    sources = [in_hbm(x) for x in (valid, w_res, w_skip, gout, gskip, *others)]
    shapes = [jax.ShapeDtypeStruct(x.shape, x.dtype) for x in sources]
    shapes += [jax.ShapeDtypeStruct((rows, w_res.shape[0]), F32), jax.ShapeDtypeStruct((8, width), F32)]
    count = len(sources) + 2 * (rows // ROWS - 1)
    return call(
        k0_body,
        "load",
        [ANYWHERE] * len(sources),
        [VMEM] * len(shapes),
        shapes,
        scratch=[pltpu.SemaphoreType.DMA((count,))],
    )(*sources)


def own_place():
    return [lax.axis_index(name) for name in ("core", "far", "near")]


def place_blocks(far, block, acc, theirs, mine):
    core, z, xy = own_place()
    for r in range(far):
        for c in range(NEAR):
            here = pl.ds(c * LANES, LANES)
            for k, out in ((1 - core, theirs), (core, mine)):
                rows = pl.ds(pl.multiple_of((k * far + r) * block, 16), block)
                out[c ^ xy, turned(r ^ z, far)] = acc[rows, here].astype(out.dtype)


def turned(index, count):
    bits = (count - 1).bit_length()
    result = 0
    for bit in range(bits):
        result = result | (((index >> bit) & 1) << (bits - 1 - bit))
    return result


def gates(past, now, feats, w_past, w_now, w_cond, b_conv, at, part):
    here = slice(at, at + part)
    return dot(past, w_past[:, here]) + dot(now, w_now[:, here]) + across(feats, w_cond[:, here]) + b_conv[:, here]


def slopes(pre_a, pre_s, dgated):
    act = jnp.tanh(pre_a)
    gate = 0.5 + 0.5 * jnp.tanh(0.5 * pre_s)
    slope = dgated * gate
    dpre = jnp.concatenate([slope * (1.0 - act * act), slope * act * (1.0 - gate)], axis=1)
    return (act * gate).astype(BF16), dpre.astype(BF16)


def k1_body(
    far, block, half,
    halo, sig, feat, pos, valid, dgated, gout, gskip, w_past, w_now, w_cond, b_conv, sums,
    gated_out, dpre_out, theirs, mine,
    acc, past_all, kept_all,
):
    rows, width = sig.shape
    cond = feat.shape[0]
    part = gated_out.shape[1]
    top = 2 * width
    first = half * part
    second = (HALVES + half) * part
    weights = (w_past, w_now, w_cond, b_conv)
    bias = jnp.zeros((8, 2 * part), F32)
    for i in range(rows // ROWS):
        here = slice(i * ROWS, (i + 1) * ROWS)
        if i == 0:
            delayed = jnp.concatenate([halo[...], sig[: ROWS - DILATION_STEP, :]], axis=0)
        else:
            delayed = sig[i * ROWS - DILATION_STEP : (i + 1) * ROWS - DILATION_STEP, :]
        past = delayed * tap_of(pos[i]).astype(BF16)
        past_all[here, :] = past
        now, feats = sig[here, :], feat[:, here]
        pre_a = gates(past, now, feats, *weights, first, part)
        pre_s = gates(past, now, feats, *weights, second, part)
        gated, dpre = slopes(pre_a, pre_s, dgated[here, first : first + part])
        gated_out[here, :] = gated
        dpre_out[here, :] = dpre
        kept_all[here, :] = gated * column(valid[i]).astype(BF16)
        bias += jnp.sum(dpre.astype(F32).reshape(ROWS // 8, 8, 2 * part), axis=0)
    at = top + 2 * part
    acc[0:width, :] = across(past_all[...], dpre_out[...])
    acc[width:top, :] = across(sig[...], dpre_out[...])
    acc[top : top + part, :] = across(kept_all[...], gout[...])
    acc[top + part : at, :] = across(kept_all[...], gskip[...])
    acc[at : at + cond, :] = dot(feat[...], dpre_out[...])
    at += cond
    acc[at : at + 1, :] = jnp.sum(bias, axis=0, keepdims=True)
    acc[at + 1 : at + 2, :] = sums[half : half + 1, :]
    acc[at + 2 :, :] = jnp.zeros((acc.shape[0] - at - 2, acc.shape[1]), F32)
    place_blocks(far, block, acc, theirs, mine)


def k1(half, far, block, halo, sig, feat, pos, valid, dgated, gout, gskip, w_past, w_now, w_cond, b_conv, sums):
    rows, width = sig.shape
    part = w_past.shape[1] // 2 // HALVES
    packed = (NEAR, far, block, LANES)
    args = (halo, sig, feat, pos, valid, dgated, gout, gskip, w_past, w_now, w_cond, b_conv, sums)
    return call(
        functools.partial(k1_body, far, block, half),
        f"gradients_{half}",
        [VMEM] * len(args),
        [VMEM] * 4,
        [
            jax.ShapeDtypeStruct((rows, part), BF16),
            jax.ShapeDtypeStruct((rows, 2 * part), BF16),
            jax.ShapeDtypeStruct(packed, BF16),
            jax.ShapeDtypeStruct(packed, F32),
        ],
        scratch=[
            pltpu.VMEM((2 * far * block, 2 * part), F32),
            pltpu.VMEM((rows, width), BF16),
            pltpu.VMEM((rows, part), BF16),
        ],
    )(*args)


def past_term(dpre_0, dpre_1, weight, part):
    hidden = 2 * part
    total = against(dpre_0[:, :part], weight[:, :part])
    total += against(dpre_1[:, :part], weight[:, part:hidden])
    total += against(dpre_0[:, part:], weight[:, hidden : hidden + part])
    return total + against(dpre_1[:, part:], weight[:, hidden + part :])


def k2a_body(
    token, sig, valid, pos, gated_0, gated_1, dpre_0, dpre_1, w_res, b_res, w_skip, b_skip, w_past,
    out, skip, early, rooms, sems,
):
    part = gated_0.shape[1]
    tap = tap_of(pos[0, : DILATION_STEP // LANES])
    first = slice(0, DILATION_STEP)
    early[...] = (tap * past_term(dpre_0[first, :], dpre_1[first, :], w_past, part)).astype(BF16)
    copies = []
    for i in range(sig.shape[0] // ROWS):
        rows = slice(i * ROWS, (i + 1) * ROWS)
        mask = column(valid[i])
        left, right = gated_0[rows, :], gated_1[rows, :]
        branch = dot(left, w_res[:part, :]) + dot(right, w_res[part:, :]) + b_res[...]
        rooms[i, 0] = (sig[rows, :].astype(F32) + mask * branch).astype(BF16)
        side = dot(left, w_skip[:part, :]) + dot(right, w_skip[part:, :]) + b_skip[...]
        rooms[i, 1] = (mask * side).astype(BF16)
        for k, ref in enumerate((out, skip)):
            copies.append(pltpu.make_async_copy(rooms.at[i, k], ref.at[pl.ds(i * ROWS, ROWS)], sems.at[i, k]))
            copies[-1].start()
    for copy in copies:
        copy.wait()


def k2a(token, sig, valid, pos, gated, dpre, w_res, b_res, w_skip, b_skip, w_past):
    rows, width = sig.shape
    return call(
        k2a_body,
        "outputs",
        [ANYWHERE] + [VMEM] * 12,
        [ANYWHERE, ANYWHERE, VMEM],
        [
            jax.ShapeDtypeStruct((rows, width), BF16),
            jax.ShapeDtypeStruct((rows, w_skip.shape[1]), BF16),
            jax.ShapeDtypeStruct((DILATION_STEP, width), BF16),
        ],
        scratch=[
            pltpu.VMEM((rows // ROWS, 2, ROWS, width), BF16),
            pltpu.SemaphoreType.DMA((rows // ROWS, 2)),
        ],
    )(token, sig, valid, pos, *gated, *dpre, w_res, b_res, w_skip, b_skip, w_past)


def k2b_body(step, token, received, gout, pos, dpre_0, dpre_1, w_past, w_now, w_cond, *refs):
    gsig, gfeat, mark, room, room_feat, sems = refs[-6:]
    rows, width = gout.shape
    part = dpre_0.shape[1] // 2
    hidden = 2 * part
    begin = step * ROWS
    here = slice(begin, begin + ROWS)
    left, right = dpre_0[here, :], dpre_1[here, :]
    after = slice(begin + DILATION_STEP, min(begin + DILATION_STEP + ROWS, rows))
    lines = jnp.concatenate([pos[step, DILATION_STEP // LANES :], pos[min(step + 1, rows // ROWS - 1), : DILATION_STEP // LANES]])
    tap = tap_of(lines)[: after.stop - after.start]
    copies = []
    wide = 2 * LANES
    for k in range(width // wide):
        some = slice(k * wide, (k + 1) * wide)
        tail = tap * past_term(dpre_0[after, :], dpre_1[after, :], w_past[some, :], part)
        if tail.shape[0] < ROWS:
            tail = jnp.concatenate([tail, received[:, some].astype(F32)], axis=0)
        room[k] = gout[here, some].astype(F32) + past_term(left, right, w_now[some, :], part) + tail
        copies.append(pltpu.make_async_copy(room.at[k], gsig.at[pl.ds(begin, ROWS), pl.ds(k * wide, wide)], sems.at[k]))
        copies[-1].start()
    total = against(w_cond[:, :part], left[:, :part])
    total += against(w_cond[:, part:hidden], right[:, :part])
    total += against(w_cond[:, hidden : hidden + part], left[:, part:])
    room_feat[...] = total + against(w_cond[:, hidden + part :], right[:, part:])
    copies.append(pltpu.make_async_copy(room_feat, gfeat.at[:, pl.ds(begin, ROWS)], sems.at[width // wide]))
    copies[-1].start()
    mark[...] = jnp.zeros_like(mark)
    for copy in copies:
        copy.wait()


def k2b(step, token, received, gout, pos, dpre, w_past, w_now, w_cond, before):
    rows, width = gout.shape
    cond = w_cond.shape[0]
    count = width // (2 * LANES)
    return call(
        functools.partial(k2b_body, step),
        f"input_gradients_{step}",
        [ANYWHERE] + [VMEM] * 8 + [ANYWHERE] * len(before),
        [ANYWHERE, ANYWHERE, VMEM],
        [
            jax.ShapeDtypeStruct((rows, width), F32),
            jax.ShapeDtypeStruct((cond, rows), F32),
            jax.ShapeDtypeStruct((8, LANES), F32),
        ],
        scratch=[
            pltpu.VMEM((count, ROWS, 2 * LANES), F32),
            pltpu.VMEM((cond, ROWS), F32),
            pltpu.SemaphoreType.DMA((count + 1,)),
        ],
        aliases={9 + k: k for k in range(len(before))},
    )(token, received, gout, pos, *dpre, w_past, w_now, w_cond, *before)


def unpack_body(far, block, half, width, cond, token, mine, theirs, *refs):
    past, now, res, skip, conds, b_conv, b_own = refs[-8:-1]
    room = refs[-1]
    part = res.shape[0]
    core, z, xy = own_place()

    @pl.when(pl.program_id(0) == 0)
    def _():
        for k, ref in ((core, mine), (1 - core, theirs)):
            for c in range(NEAR):
                for r in range(far):
                    rows = pl.ds(pl.multiple_of((k * far + (r ^ z)) * block, 16), block)
                    room[c ^ xy, rows, :] = ref[c, turned(r, far)]

    for j in range(NEAR // 2):
        c = pl.program_id(0) * (NEAR // 2) + j
        here = pl.ds(j * LANES, LANES)
        top = 0
        for ref in (past, now, res, skip, conds):
            count = ref.shape[0]
            ref[:, here] = room[c, top : top + count, :].astype(F32)
            top += count
        last = room[c, top : top + 16, :].astype(F32)
        b_conv[:, here] = last[0:1]
        b_own[:, here] = last[1:2]


def unpack(half, token, far, block, mine, theirs, width, cond, hidden, skip_width, before):
    part = hidden // HALVES
    gates = 2 * hidden
    wide = [
        pl.BlockSpec((size, part), lambda s: (0, HALVES * s + half)) for size in (width, width)
    ]
    tall = [pl.BlockSpec((part, size // 2), lambda s: (half, s)) for size in (width, skip_width)]
    rest = [
        pl.BlockSpec((cond, part), lambda s: (0, HALVES * s + half)),
        pl.BlockSpec((1, part), lambda s: (0, HALVES * s + half)),
        pl.BlockSpec((1, (width, skip_width)[half] // 2), lambda s: (0, s)),
    ]
    shapes = [
        (width, gates), (width, gates), (hidden, width), (hidden, skip_width), (cond, gates), (1, gates),
        (1, (width, skip_width)[half]),
    ]
    packed = (NEAR, far, block, LANES)
    return call(
        functools.partial(unpack_body, far, block, half, width, cond),
        f"unpack_{half}",
        [ANYWHERE, whole(*packed), whole(*packed)] + [pl.BlockSpec(memory_space=pl.ANY)] * len(before),
        wide + tall + rest,
        [jax.ShapeDtypeStruct(shape, F32) for shape in shapes],
        scratch=[pltpu.VMEM((NEAR, 2 * far * block, LANES), BF16)],
        aliases={3 + k: k for k in range(len(before))},
        grid=(2,),
    )(token, mine, theirs, *before)


def swapped(x, axis, k):
    return lax.ppermute(x, axis, [(i, i ^ k) for i in range(lax.axis_size(axis))])


def exchanged(blocks):
    return [swapped(block, "near", k + 1) for k, block in enumerate(blocks)]


def add_body(sizes, token, *refs):
    count = len(sizes)
    kept, got, outs = refs[0], refs[1:-count], refs[-count:]
    at = 0
    for out, size in zip(outs, sizes):
        for k in range(size):
            total = kept[at + k].astype(F32)
            for ref in got:
                total = total + ref[at + k].astype(F32)
            out[k] = total.astype(out.dtype)
        at += size


def added(name, token, kept, got, outs):
    sizes = [size for size, _ in outs]
    result = call(
        functools.partial(add_body, sizes),
        name,
        [ANYWHERE] + [VMEM] * (1 + len(got)),
        [VMEM] * len(outs),
        [jax.ShapeDtypeStruct((size, *kept.shape[1:]), dtype) for size, dtype in outs],
    )(token, kept, *got)
    return result


def mirror_body(token, mine, got, out):
    count = mine.shape[0]
    for k in range(count):
        out[k] = (mine[k].astype(F32) + got[count - 1 - k].astype(F32)).astype(out.dtype)


def mirrored(name, token, mine, got):
    return call(
        mirror_body,
        name,
        [ANYWHERE, VMEM, VMEM],
        VMEM,
        jax.ShapeDtypeStruct(mine.shape, BF16),
    )(token, mine, got)


def join_body(token, *refs):
    out = refs[-1]
    at = 0
    for ref in refs[:-1]:
        out[at : at + ref.shape[0]] = ref[...]
        at += ref.shape[0]


def joined(name, token, parts):
    count = sum(part.shape[0] for part in parts)
    return call(
        join_body,
        name,
        [ANYWHERE] + [VMEM] * len(parts),
        VMEM,
        jax.ShapeDtypeStruct((count, *parts[0].shape[1:]), BF16),
    )(token, *parts)


def over_outer(total):
    for bit in range((lax.axis_size("outer") - 1).bit_length()):
        total = (total.astype(F32) + swapped(total, "outer", 1 << bit).astype(F32)).astype(BF16)
    return total


def passed_along(x, by):
    peers = lax.axis_size(AXES)
    pairs = [(i, i + by) for i in range(peers) if 0 <= i + by < peers]
    return lax.ppermute(x, AXES, pairs)


def in_hbm(x):
    return pltpu.with_memory_space_constraint(x, pltpu.HBM)


def body(
    signal,
    features,
    position,
    valid,
    w_past,
    w_now,
    b_conv,
    w_cond,
    w_res,
    b_res,
    w_skip,
    b_skip,
    grad_out,
    grad_skip,
):
    rows, width = signal.shape
    features = features.T
    cond = features.shape[0]
    hidden = w_res.shape[0]
    skip_width = w_skip.shape[1]
    far = lax.axis_size("far")
    far_bits = (far - 1).bit_length()
    used = 2 * width + 2 * (hidden // HALVES) + cond + 2
    block = -(-used // (2 * far * 16)) * 16
    lines = (rows // ROWS, ROWS // LANES, LANES)
    pos, val = position.reshape(lines), valid.reshape(lines)
    b_conv, b_res, b_skip = (b.reshape(1, -1) for b in (b_conv, b_res, b_skip))

    halo = passed_along(signal[rows - DILATION_STEP :], 1)
    (
        val, w_res, w_skip, grad_out, grad_skip, pos, b_conv, features, w_cond, signal, w_past, w_now,
        b_res, b_skip, dgated, sums,
    ) = k0(
        val, w_res, w_skip, grad_out, grad_skip, pos, b_conv, features, w_cond, signal, w_past, w_now, b_res, b_skip
    )
    gated, dpre, packed = [], [], []
    for half in range(HALVES):
        one, other, *both = k1(
            half, far, block, halo, signal, features, pos, val, dgated, grad_out, grad_skip,
            w_past, w_now, w_cond, b_conv, sums,
        )
        gated.append(one)
        dpre.append(other)
        packed.append(both)

    def core_sum(half, token):
        theirs, mine = packed[half]
        kept, *sent = added(
            f"core_sum_{half}", token, mine, [swapped(theirs, "core", 1)], [(1, F32)] + [(1, BF16)] * (NEAR - 1)
        )
        return kept[0], exchanged([x[0] for x in sent])

    def near_sum(half, token, kept, got):
        kept, sent = added(f"near_sum_{half}", token, kept, got, [(far // 2, F32), (far // 2, BF16)])
        return kept, swapped(sent, "far", 1)

    def far_sum(half, token, kept, got):
        for bit in range(1, far_bits - 1):
            size = kept.shape[0] // 2
            kept, sent = added(f"far_sum_{half}_{bit}", token, kept, [got], [(size, F32), (size, BF16)])
            got = swapped(sent, "far", 1 << bit)
        (mine,) = added(f"far_sum_{half}", token, kept, [got], [(kept.shape[0], BF16)])
        return mine, swapped(mine, "far", 1 << (far_bits - 1))

    def far_end(half, token, mine, got):
        total = over_outer(mirrored(f"far_end_{half}", token, mine, got))
        return total, swapped(total, "far", 1 << (far_bits - 2))

    def far_join(half, token, mine, got):
        total = joined(f"far_join_{half}", token, [mine, got])
        for bit in reversed(range(far_bits - 2)):
            total = joined(f"far_join_{half}_{bit}", token, [total, swapped(total, "far", 1 << bit)])
        return total, exchanged([total] * (NEAR - 1))

    def near_join(half, token, mine, got):
        total = joined(f"near_join_{half}", token, [mine[None]] + [x[None] for x in got])
        return total, swapped(total, "core", 1)

    def input_gradients(step, token, before):
        return k2b(step, token, received, grad_out, pos, dpre, w_past, w_now, w_cond, before)

    kept_0, got_0 = core_sum(0, dpre[1])
    output, skip_out, early = k2a(kept_0, signal, val, pos, gated, dpre, w_res, b_res, w_skip, b_skip, w_past)
    received = passed_along(early, -1)
    kept_1, got_1 = core_sum(1, early)
    kept_0, got_0 = near_sum(0, kept_1, kept_0, got_0)
    *grads, mark = input_gradients(0, kept_0, [])
    mine_0, got_0 = far_sum(0, mark, kept_0, got_0)
    *grads, mark = input_gradients(1, mine_0, grads)
    *grads, mark = input_gradients(2, mark, grads)
    kept_1, got_1 = near_sum(1, mark, kept_1, got_1)
    mine_0, got_0 = far_end(0, kept_1, mine_0, got_0)
    *grads, mark = input_gradients(3, mine_0, grads)
    mine_1, got_1 = far_sum(1, mark, kept_1, got_1)
    mine_0, got_0 = far_join(0, mine_1, mine_0, got_0)
    mine_1, got_1 = far_end(1, mine_0, mine_1, got_1)
    mine_1, got_1 = far_join(1, mine_1, mine_1, got_1)
    mine_0, got_0 = near_join(0, mine_1, mine_0, got_0)
    *done, own_0 = unpack(0, mine_1, far, block, mine_0, got_0, width, cond, hidden, skip_width, [])
    mine_1, got_1 = near_join(1, own_0, mine_1, got_1)
    *done, own_1 = unpack(1, own_0, far, block, mine_1, got_1, width, cond, hidden, skip_width, done)
    grad_signal, grad_features = grads
    own = [own_0, own_1]
    g_past, g_now, g_res, g_skip, g_cond, g_bias = done
    return (
        output,
        skip_out,
        grad_signal,
        grad_features.T,
        g_past,
        g_now,
        g_bias.reshape(-1),
        g_cond,
        g_res,
        own[0].reshape(-1),
        g_skip,
        own[1].reshape(-1),
    )


def solution(mesh):
    row, col = mesh.shape["row"], mesh.shape["col"]
    fine = Mesh(mesh.devices.reshape(row // 2, 2, col // NEAR, NEAR), AXES)
    rows = P(AXES, None)
    line = P(AXES)
    return jax.shard_map(
        body,
        mesh=fine,
        in_specs=(rows, rows, line, line) + (P(),) * 8 + (rows, rows),
        out_specs=(rows,) * 4 + (P(),) * 8,
        check_vma=False,
    )
```

```python
import functools

import jax
import jax.numpy as jnp
from jax import lax
from jax.experimental import pallas as pl
from jax.experimental.pallas import tpu as pltpu
from jax.sharding import Mesh
from jax.sharding import PartitionSpec as P

DILATION_STEP = 256
AXES = ("outer", "core", "far", "near")
HALVES = 2
NEAR = 4
LANES = 128
ROWS = 512
F32 = jnp.float32
BF16 = jnp.bfloat16
MEGA = 1 << 20
COSTS = {
    "load": 8, "head": 2, "gradients_0": 0, "forward_1": 0, "gradients_1": 4, "outputs": 4, "near_sum_0": 8,
    "input": 2, "unpack": 1,
}
FLOPS = 10**9


def dot(left, right):
    return jnp.dot(left, right, preferred_element_type=F32)


def across(left, right):
    return lax.dot_general(left, right, (((0,), (0,)), ((), ())), preferred_element_type=F32)


def against(left, weight):
    return lax.dot_general(left, weight, (((1,), (1,)), ((), ())), preferred_element_type=F32)


def column(lines):
    turned = lines.astype(F32).T
    return jnp.concatenate([turned[:, k : k + 1] for k in range(lines.shape[0])], axis=0)


def tap_of(lines):
    return column(jnp.where(lines >= DILATION_STEP, 1, 0))


def lines_of(ref, rows):
    return ref[rows.start // LANES : rows.stop // LANES, :]


def picked(head, rest, rows):
    cut = DILATION_STEP
    low = head[rows.start : min(rows.stop, cut), :] if rows.start < cut else None
    high = rest[max(rows.start, cut) - cut : rows.stop - cut, :] if rows.stop > cut else None
    if low is None:
        return high
    return low if high is None else jnp.concatenate([low, high], axis=0)


def call(kernel, name, in_specs, out_specs, out_shape, scratch=(), aliases=None, vmem=24):
    return pl.pallas_call(
        kernel,
        in_specs=in_specs,
        out_specs=out_specs,
        out_shape=out_shape,
        scratch_shapes=list(scratch),
        input_output_aliases=aliases or {},
        cost_estimate=pl.CostEstimate(
            flops=1 + FLOPS * COSTS.get(name, COSTS.get(name.split("_")[0], 0)), bytes_accessed=1, transcendentals=0
        ),
        name=name,
        compiler_params=pltpu.CompilerParams(vmem_limit_bytes=vmem * MEGA),
    )


VMEM = pl.BlockSpec(memory_space=pltpu.VMEM)
ANYWHERE = pl.BlockSpec(memory_space=pl.ANY)


def gates(past, now, feats, w_past, w_now, w_cond, b_conv, at, part):
    here = slice(at, at + part)
    return dot(past, w_past[:, here]) + dot(now, w_now[:, here]) + across(feats, w_cond[:, here]) + b_conv[:, here]


def slopes(pre_a, pre_s, dgated):
    act = jnp.tanh(pre_a)
    gate = 0.5 + 0.5 * jnp.tanh(0.5 * pre_s)
    slope = dgated * gate
    dpre = jnp.concatenate([slope * (1.0 - act * act), slope * act * (1.0 - gate)], axis=1)
    return (act * gate).astype(BF16), dpre.astype(BF16)


def forward(half, rows, past, sig, feat, dgated, mask, weights):
    part = dgated.shape[1] // HALVES
    args = (past, sig[rows, :], feat[:, rows], *weights)
    pre_a = gates(*args, half * part, part)
    pre_s = gates(*args, (HALVES + half) * part, part)
    gated, dpre = slopes(pre_a, pre_s, dgated[rows, half * part : (half + 1) * part])
    return gated, gated * mask, dpre


def rest_rows(rows):
    cuts = [DILATION_STEP, *range(ROWS, rows + 1, ROWS)]
    return [slice(a, b) for a, b in zip(cuts, cuts[1:])]


def moved(rows, by):
    return slice(rows.start + by, rows.stop + by)


LOADED = ("valid", "w_res", "w_skip", "gout", "gskip", "pos", "b_conv", "feat", "w_cond", "sig", "w_past", "w_now")


def load_body(count, *refs):
    sources, here = refs[:count], refs[count : 2 * count]
    dgated, sums, past_rest, gated_rest, kept_rest, dpre_rest, sems = refs[2 * count :]
    valid, w_res, w_skip, gout, gskip, pos, b_conv, feat, w_cond, sig, w_past, w_now = here[: len(LOADED)]
    steps = gout.shape[0] // ROWS
    copies = {}

    def start(k, i=None):
        at = (slice(None),) if i is None else (pl.ds(i * ROWS, ROWS),)
        copies[k, i] = pltpu.make_async_copy(sources[k].at[at], here[k].at[at], sems.at[len(copies)])
        copies[k, i].start()

    def wait(k, i=None):
        copies[k, i].wait()

    for k in range(3):
        start(k)
    for i in range(steps):
        start(3, i)
        start(4, i)
    for k in range(5, count):
        start(k)
    for k in range(3):
        wait(k)
    total = [jnp.zeros((8, gout.shape[1]), F32), jnp.zeros((8, gskip.shape[1]), F32)]
    for i in range(steps):
        wait(3, i)
        wait(4, i)
        rows = slice(i * ROWS, (i + 1) * ROWS)
        mask = column(lines_of(valid, rows))
        res, skip = gout[rows, :], gskip[rows, :]
        dgated[rows, :] = mask * (against(res, w_res[...]) + against(skip, w_skip[...]))
        for k, x in enumerate((res, skip)):
            total[k] += jnp.sum((mask * x.astype(F32)).reshape(ROWS // 8, 8, x.shape[1]), axis=0)
    for k in range(2):
        sums[k : k + 1, :] = jnp.sum(total[k], axis=0, keepdims=True)
    for k in range(5, count):
        wait(k)
    for rows in rest_rows(gout.shape[0]):
        there = moved(rows, -DILATION_STEP)
        past = sig[there, :] * tap_of(lines_of(pos, rows)).astype(BF16)
        mask = column(lines_of(valid, rows)).astype(BF16)
        past_rest[there, :] = past
        gated_rest[there, :], kept_rest[there, :], dpre_rest[there, :] = forward(
            0, rows, past, sig, feat, dgated, mask, (w_past, w_now, w_cond, b_conv)
        )


def load(*arrays):
    sources = [in_hbm(x) for x in arrays]
    named = dict(zip(LOADED, arrays))
    rows, width = named["gout"].shape
    hidden = named["w_res"].shape[0]
    rest = rows - DILATION_STEP
    part = hidden // HALVES
    shapes = [jax.ShapeDtypeStruct(x.shape, x.dtype) for x in sources] + [
        jax.ShapeDtypeStruct((rows, hidden), F32),
        jax.ShapeDtypeStruct((8, width), F32),
        jax.ShapeDtypeStruct((rest, width), BF16),
        jax.ShapeDtypeStruct((rest, part), BF16),
        jax.ShapeDtypeStruct((rest, part), BF16),
        jax.ShapeDtypeStruct((rest, 2 * part), BF16),
    ]
    count = len(sources)
    result = call(
        functools.partial(load_body, count),
        "load",
        [ANYWHERE] * count,
        [VMEM] * len(shapes),
        shapes,
        scratch=[pltpu.SemaphoreType.DMA((count + 2 * (rows // ROWS - 1),))],
    )(*sources)
    return result[:count], result[count:]


def past_term(dpre_0, dpre_1, weight, part):
    hidden = 2 * part
    total = against(dpre_0[:, :part], weight[:, :part])
    total += against(dpre_1[:, :part], weight[:, part:hidden])
    total += against(dpre_0[:, part:], weight[:, hidden : hidden + part])
    return total + against(dpre_1[:, part:], weight[:, hidden + part :])


def head_body(halo, sig, feat, pos, valid, dgated, w_past, w_now, w_cond, b_conv, past_out, early, *outs):
    rows = slice(0, DILATION_STEP)
    tap = tap_of(lines_of(pos, rows))
    mask = column(lines_of(valid, rows)).astype(BF16)
    past = halo[...] * tap.astype(BF16)
    past_out[...] = past
    dpres = []
    for half in range(HALVES):
        parts = forward(half, rows, past, sig, feat, dgated, mask, (w_past, w_now, w_cond, b_conv))
        for ref, x in zip(outs[3 * half :], parts):
            ref[...] = x
        dpres.append(parts[2])
    early[...] = (tap * past_term(*dpres, w_past, dpres[0].shape[1] // 2)).astype(BF16)


def head(halo, sig, feat, pos, valid, dgated, w_past, w_now, w_cond, b_conv):
    width = sig.shape[1]
    part = dgated.shape[1] // HALVES
    first, *others = [
        jax.ShapeDtypeStruct((DILATION_STEP, size), BF16) for size in (width, part, part, 2 * part)
    ]
    past, early, *parts = call(
        head_body,
        "head",
        [VMEM] * 10,
        [VMEM] * (2 + 3 * HALVES),
        [first, first] + others * HALVES,
    )(halo, sig, feat, pos, valid, dgated, w_past, w_now, w_cond, b_conv)
    return past, early, parts[:3], parts[3:]


def forward_body(token, past, sig, feat, valid, dgated, w_past, w_now, w_cond, b_conv, gated_out, kept_out, dpre_out):
    for rows in rest_rows(sig.shape[0]):
        there = moved(rows, -DILATION_STEP)
        mask = column(lines_of(valid, rows)).astype(BF16)
        gated_out[there, :], kept_out[there, :], dpre_out[there, :] = forward(
            1, rows, past[rows, :], sig, feat, dgated, mask, (w_past, w_now, w_cond, b_conv)
        )


def forward_rest(token, past, sig, feat, valid, dgated, w_past, w_now, w_cond, b_conv):
    rest = sig.shape[0] - DILATION_STEP
    part = dgated.shape[1] // HALVES
    return call(
        forward_body,
        "forward_1",
        [ANYWHERE] + [VMEM] * 9,
        [VMEM] * 3,
        [jax.ShapeDtypeStruct((rest, size), BF16) for size in (part, part, 2 * part)],
    )(token, past, sig, feat, valid, dgated, w_past, w_now, w_cond, b_conv)


def own_place():
    return [lax.axis_index(name) for name in ("core", "far", "near")]


def turned(index, count):
    bits = (count - 1).bit_length()
    result = 0
    for bit in range(bits):
        result = result | (((index >> bit) & 1) << (bits - 1 - bit))
    return result


def place_blocks(far, block, acc, theirs, mine):
    core, z, xy = own_place()
    for r in range(far):
        for c in range(NEAR):
            here = pl.ds(c * LANES, LANES)
            for k, out in ((1 - core, theirs), (core, mine)):
                rows = pl.ds(pl.multiple_of((k * far + r) * block, 16), block)
                out[c ^ xy, turned(r ^ z, far)] = acc[rows, here].astype(out.dtype)


def gradients_body(
    far, block, half, token, sig, feat, gout, gskip, sums, past_head, past_rest, kept_head, kept_rest, dpre_head, dpre_rest,
    theirs, mine, dpre, past, acc, kept,
):
    rows, width = sig.shape
    cond = feat.shape[0]
    part = kept.shape[1]
    cut = DILATION_STEP
    for whole, low, high in ((past, past_head, past_rest), (kept, kept_head, kept_rest), (dpre, dpre_head, dpre_rest)):
        whole[:cut, :] = low[...]
        whole[cut:, :] = high[...]
    bias = jnp.zeros((8, dpre.shape[1]), F32)
    for i in range(0, rows, ROWS):
        bias += jnp.sum(dpre[i : i + ROWS, :].astype(F32).reshape(ROWS // 8, 8, dpre.shape[1]), axis=0)
    at = 0
    for left, right in ((past, dpre), (sig, dpre), (kept, gout), (kept, gskip)):
        acc[at : at + left.shape[1], :] = across(left[...], right[...])
        at += left.shape[1]
    acc[at : at + cond, :] = dot(feat[...], dpre[...])
    at += cond
    acc[at : at + 1, :] = jnp.sum(bias, axis=0, keepdims=True)
    acc[at + 1 : at + 2, :] = sums[half : half + 1, :]
    acc[at + 2 :, :] = jnp.zeros((acc.shape[0] - at - 2, acc.shape[1]), F32)
    place_blocks(far, block, acc, theirs, mine)


def gradients(half, token, far, block, sig, feat, gout, gskip, sums, past, kept, dpre):
    rows, width = sig.shape
    part = kept[0].shape[1]
    packed = (NEAR, far, block, LANES)
    return call(
        functools.partial(gradients_body, far, block, half),
        f"gradients_{half}",
        [ANYWHERE] + [VMEM] * 11,
        [VMEM] * 4,
        [
            jax.ShapeDtypeStruct(packed, BF16),
            jax.ShapeDtypeStruct(packed, F32),
            jax.ShapeDtypeStruct((rows, 2 * part), BF16),
            jax.ShapeDtypeStruct((rows, width), BF16),
        ],
        scratch=[pltpu.VMEM((2 * far * block, 2 * part), F32), pltpu.VMEM((rows, part), BF16)],
    )(token, sig, feat, gout, gskip, sums, *past, *kept, *dpre)


def outputs_body(
    token, other, sig, valid, head_0, rest_0, head_1, rest_1, w_res, b_res, w_skip, b_skip, out, skip, mark, rooms, sems
):
    part = head_0.shape[1]
    copies = []
    for i in range(sig.shape[0] // ROWS):
        rows = slice(i * ROWS, (i + 1) * ROWS)
        mask = column(lines_of(valid, rows))
        left, right = picked(head_0, rest_0, rows), picked(head_1, rest_1, rows)
        branch = dot(left, w_res[:part, :]) + dot(right, w_res[part:, :]) + b_res[...]
        rooms[i, 0] = (sig[rows, :].astype(F32) + mask * branch).astype(BF16)
        side = dot(left, w_skip[:part, :]) + dot(right, w_skip[part:, :]) + b_skip[...]
        rooms[i, 1] = (mask * side).astype(BF16)
        for k, ref in enumerate((out, skip)):
            copies.append(pltpu.make_async_copy(rooms.at[i, k], ref.at[pl.ds(i * ROWS, ROWS)], sems.at[i, k]))
            copies[-1].start()
    mark[...] = jnp.zeros_like(mark)
    for copy in copies:
        copy.wait()


MARK = jax.ShapeDtypeStruct((8, LANES), F32)


def outputs(token, other, sig, valid, gated_0, gated_1, w_res, b_res, w_skip, b_skip):
    rows, width = sig.shape
    return call(
        outputs_body,
        "outputs",
        [ANYWHERE] * 2 + [VMEM] * 10,
        [ANYWHERE, ANYWHERE, VMEM],
        [
            jax.ShapeDtypeStruct((rows, width), BF16),
            jax.ShapeDtypeStruct((rows, w_skip.shape[1]), BF16),
            MARK,
        ],
        scratch=[
            pltpu.VMEM((rows // ROWS, 2, ROWS, width), BF16),
            pltpu.SemaphoreType.DMA((rows // ROWS, 2)),
        ],
    )(token, other, sig, valid, *gated_0, *gated_1, w_res, b_res, w_skip, b_skip)


def k2b_body(step, token, received, gout, pos, dpre_0, dpre_1, w_past, w_now, w_cond, *refs):
    gsig, gfeat, mark, room, room_feat, sems = refs[-6:]
    rows, width = gout.shape
    part = dpre_0.shape[1] // 2
    hidden = 2 * part
    begin = step * ROWS
    here = slice(begin, begin + ROWS)
    left, right = dpre_0[here, :], dpre_1[here, :]
    after = slice(begin + DILATION_STEP, min(begin + DILATION_STEP + ROWS, rows))
    tap = tap_of(lines_of(pos, after))
    copies = []
    wide = 2 * LANES
    for k in range(width // wide):
        some = slice(k * wide, (k + 1) * wide)
        tail = tap * past_term(dpre_0[after, :], dpre_1[after, :], w_past[some, :], part)
        if tail.shape[0] < ROWS:
            tail = jnp.concatenate([tail, received[:, some].astype(F32)], axis=0)
        room[k] = gout[here, some].astype(F32) + past_term(left, right, w_now[some, :], part) + tail
        copies.append(pltpu.make_async_copy(room.at[k], gsig.at[pl.ds(begin, ROWS), pl.ds(k * wide, wide)], sems.at[k]))
        copies[-1].start()
    total = against(w_cond[:, :part], left[:, :part])
    total += against(w_cond[:, part:hidden], right[:, :part])
    total += against(w_cond[:, hidden : hidden + part], left[:, part:])
    room_feat[...] = total + against(w_cond[:, hidden + part :], right[:, part:])
    copies.append(pltpu.make_async_copy(room_feat, gfeat.at[:, pl.ds(begin, ROWS)], sems.at[width // wide]))
    copies[-1].start()
    mark[...] = jnp.zeros_like(mark)
    for copy in copies:
        copy.wait()


def k2b(step, token, received, gout, pos, dpre, w_past, w_now, w_cond, before):
    rows, width = gout.shape
    cond = w_cond.shape[0]
    count = width // (2 * LANES)
    return call(
        functools.partial(k2b_body, step),
        f"input_gradients_{step}",
        [ANYWHERE] + [VMEM] * 8 + [ANYWHERE] * len(before),
        [ANYWHERE, ANYWHERE, VMEM],
        [
            jax.ShapeDtypeStruct((rows, width), F32),
            jax.ShapeDtypeStruct((cond, rows), F32),
            MARK,
        ],
        scratch=[
            pltpu.VMEM((count, ROWS, 2 * LANES), F32),
            pltpu.VMEM((cond, ROWS), F32),
            pltpu.SemaphoreType.DMA((count + 1,)),
        ],
        aliases={9 + k: k for k in range(len(before))},
    )(token, received, gout, pos, *dpre, w_past, w_now, w_cond, *before)


def regions(half, far, block, width, hidden, cond, k):
    part = hidden // HALVES
    found = []
    at = 0
    for array, first, count in ((0, 0, width), (1, 0, width), (2, half * part, part), (3, half * part, part), (4, 0, cond)):
        low, high = max(at, k * far * block), min(at + count, (k + 1) * far * block)
        if low < high:
            found.append((array, first + low - at, low - k * far * block, high - low))
        at += count
    return found, at - k * far * block


def unpack_body(half, own, far, block, hidden, cond, token, blocks, *refs):
    outs, (room, bias, own_bias, sems) = refs[-12:-4], refs[-4:]
    part = hidden // HALVES
    core, z, xy = own_place()
    which = core if own else 1 - core
    for p in range(NEAR):
        for r in range(far):
            rows = pl.ds(pl.multiple_of((r ^ z) * block, 16), block)
            room[p, rows, :] = blocks[p, turned(r, far)].astype(F32)
    for k in range(2):
        found, last = regions(half, far, block, outs[0].shape[0], hidden, cond, k)

        @pl.when(which == k)
        def _(found=found, last=last):
            copies = []

            def copy(source, target):
                copies.append(pltpu.make_async_copy(source, target, sems.at[len(copies)]))
                copies[-1].start()

            for p in range(NEAR):
                c = p ^ xy
                wide = pl.multiple_of((c >> 1) * hidden + half * part + (c & 1) * LANES, LANES)
                tall = pl.multiple_of(c * LANES, LANES)
                for array, first, at, count in found:
                    here = pl.ds(tall if array in (2, 3) else wide, LANES)
                    copy(room.at[p, pl.ds(at, count)], outs[array].at[pl.ds(first, count), here])
                if 0 <= last < room.shape[1]:
                    pair = room[p, last : last + 8, :]
                    bias[:, pl.ds(tall, LANES)] = pair[0:1]
                    own_bias[:, pl.ds(tall, LANES)] = pair[1:2]
            if 0 <= last < room.shape[1]:
                for j in range(2):
                    copy(bias.at[:, pl.ds(j * part, part)], outs[5].at[:, pl.ds(j * hidden + half * part, part)])
                copy(own_bias, outs[6 + half])
            for one in copies:
                one.wait()


def unpack(half, own, token, far, block, blocks, shapes, before):
    hidden, cond = shapes[2][0], shapes[4][0]
    return call(
        functools.partial(unpack_body, half, own, far, block, hidden, cond),
        f"unpack_{half}_{own:d}",
        [ANYWHERE, VMEM] + [ANYWHERE] * len(before),
        [ANYWHERE] * len(shapes),
        [jax.ShapeDtypeStruct(shape, F32) for shape in shapes],
        scratch=[
            pltpu.VMEM((NEAR, far * block, LANES), F32),
            pltpu.VMEM((1, NEAR * LANES), F32),
            pltpu.VMEM((1, NEAR * LANES), F32),
            pltpu.SemaphoreType.DMA((6 * NEAR,)),
        ],
        aliases={2 + k: k for k in range(len(before))},
    )(token, blocks, *before)


def swapped(x, axis, k):
    return lax.ppermute(x, axis, [(i, i ^ k) for i in range(lax.axis_size(axis))])


def exchanged(blocks):
    return [swapped(block, "near", k + 1) for k, block in enumerate(blocks)]


def add_body(sizes, token, *refs):
    count = len(sizes)
    kept, got, outs = refs[0], refs[1:-count], refs[-count:]
    at = 0
    for out, size in zip(outs, sizes):
        for k in range(size):
            total = kept[at + k].astype(F32)
            for ref in got:
                total = total + ref[at + k].astype(F32)
            out[k] = total.astype(out.dtype)
        at += size


def added(name, token, kept, got, outs):
    sizes = [size for size, _ in outs]
    result = call(
        functools.partial(add_body, sizes),
        name,
        [ANYWHERE] + [VMEM] * (1 + len(got)),
        [VMEM] * len(outs),
        [jax.ShapeDtypeStruct((size, *kept.shape[1:]), dtype) for size, dtype in outs],
    )(token, kept, *got)
    return result


def mirror_body(token, mine, got, out):
    count = mine.shape[0]
    for k in range(count):
        out[k] = (mine[k].astype(F32) + got[count - 1 - k].astype(F32)).astype(out.dtype)


def mirrored(name, token, mine, got):
    return call(
        mirror_body,
        name,
        [ANYWHERE, VMEM, VMEM],
        VMEM,
        jax.ShapeDtypeStruct(mine.shape, BF16),
    )(token, mine, got)


def join_body(token, *refs):
    out = refs[-1]
    at = 0
    for ref in refs[:-1]:
        out[at : at + ref.shape[0]] = ref[...]
        at += ref.shape[0]


def joined(name, token, parts):
    count = sum(part.shape[0] for part in parts)
    return call(
        join_body,
        name,
        [ANYWHERE] + [VMEM] * len(parts),
        VMEM,
        jax.ShapeDtypeStruct((count, *parts[0].shape[1:]), BF16),
    )(token, *parts)


def over_outer(total):
    for bit in range((lax.axis_size("outer") - 1).bit_length()):
        total = (total.astype(F32) + swapped(total, "outer", 1 << bit).astype(F32)).astype(BF16)
    return total


def passed_along(x, by):
    peers = lax.axis_size(AXES)
    pairs = [(i, i + by) for i in range(peers) if 0 <= i + by < peers]
    return lax.ppermute(x, AXES, pairs)


def in_hbm(x):
    return pltpu.with_memory_space_constraint(x, pltpu.HBM)


def body(
    signal,
    features,
    position,
    valid,
    w_past,
    w_now,
    b_conv,
    w_cond,
    w_res,
    b_res,
    w_skip,
    b_skip,
    grad_out,
    grad_skip,
):
    rows, width = signal.shape
    features = features.T
    cond = features.shape[0]
    hidden = w_res.shape[0]
    skip_width = w_skip.shape[1]
    far = lax.axis_size("far")
    far_bits = (far - 1).bit_length()
    used = 2 * width + 2 * (hidden // HALVES) + cond + 2
    block = -(-used // (2 * far * 16)) * 16
    lines = (rows // LANES, LANES)
    pos, val = position.reshape(lines), valid.reshape(lines)
    b_conv, b_res, b_skip = (b.reshape(1, -1) for b in (b_conv, b_res, b_skip))
    shapes = [
        (width, 2 * hidden), (width, 2 * hidden), (hidden, width), (hidden, skip_width), (cond, 2 * hidden),
        (1, 2 * hidden), (1, width), (1, skip_width),
    ]

    def core_sum(half, token, theirs, mine):
        kept, *sent = added(
            f"core_sum_{half}", token, mine, [swapped(theirs, "core", 1)], [(1, F32)] + [(1, BF16)] * (NEAR - 1)
        )
        return kept[0], exchanged([x[0] for x in sent])

    def near_sum(half, token, kept, got):
        kept, sent = added(f"near_sum_{half}", token, kept, got, [(far // 2, F32), (far // 2, BF16)])
        return kept, swapped(sent, "far", 1)

    def far_sum(half, token, kept, got):
        for bit in range(1, far_bits - 1):
            size = kept.shape[0] // 2
            kept, sent = added(f"far_sum_{half}_{bit}", token, kept, [got], [(size, F32), (size, BF16)])
            got = swapped(sent, "far", 1 << bit)
        (mine,) = added(f"far_sum_{half}", token, kept, [got], [(kept.shape[0], BF16)])
        return mine, swapped(mine, "far", 1 << (far_bits - 1))

    def far_end(half, token, mine, got):
        total = over_outer(mirrored(f"far_end_{half}", token, mine, got))
        return total, swapped(total, "far", 1 << (far_bits - 2))

    def far_join(half, token, mine, got):
        total = joined(f"far_join_{half}", token, [mine, got])
        for bit in reversed(range(far_bits - 2)):
            total = joined(f"far_join_{half}_{bit}", token, [total, swapped(total, "far", 1 << bit)])
        return total, exchanged([total] * (NEAR - 1))

    def near_join(half, token, mine, got):
        total = joined(f"near_join_{half}", token, [mine[None]] + [x[None] for x in got])
        return total, swapped(total, "core", 1)

    def input_gradients(step, token, before):
        last = (step + 1) * ROWS == rows
        return k2b(step, token, received if last else early, grad_out, pos, dpre, w_past, w_now, w_cond, before)

    halo = passed_along(signal[rows - DILATION_STEP :], 1)
    loaded, parts = load(
        val, w_res, w_skip, grad_out, grad_skip, pos, b_conv, features, w_cond, signal, w_past, w_now, b_res, b_skip
    )
    val, w_res, w_skip, grad_out, grad_skip, pos, b_conv, features, w_cond, signal, w_past, w_now, b_res, b_skip = loaded
    dgated, sums, past_rest, gated_rest_0, kept_rest_0, dpre_rest_0 = parts
    weights = (w_past, w_now, w_cond, b_conv)
    past_head, early, head_0, head_1 = head(halo, signal, features, pos, val, dgated, *weights)
    received = passed_along(early, -1)
    common = (signal, features, grad_out, grad_skip, sums)
    theirs_0, mine_0, dpre_0, past = gradients(
        0, early, far, block, *common, (past_head, past_rest), (head_0[1], kept_rest_0), (head_0[2], dpre_rest_0)
    )
    gated_rest_1, kept_rest_1, dpre_rest_1 = forward_rest(dpre_0, past, signal, features, val, dgated, *weights)
    kept_0, got_0 = core_sum(0, gated_rest_1, theirs_0, mine_0)
    output, skip_out, mark = outputs(
        kept_0, received, signal, val, (head_0[0], gated_rest_0), (head_1[0], gated_rest_1), w_res, b_res, w_skip, b_skip
    )
    theirs_1, mine_1, dpre_1, _ = gradients(
        1, mark, far, block, *common, (past_head, past_rest), (head_1[1], kept_rest_1), (head_1[2], dpre_rest_1)
    )
    dpre = (dpre_0, dpre_1)
    kept_0, got_0 = near_sum(0, dpre_1, kept_0, got_0)
    kept_1, got_1 = core_sum(1, kept_0, theirs_1, mine_1)
    *grads, mark = input_gradients(0, kept_1, [])
    ends_0, got_0 = far_sum(0, mark, kept_0, got_0)
    *grads, mark = input_gradients(1, ends_0, grads)
    *grads, mark = input_gradients(2, mark, grads)
    kept_1, got_1 = near_sum(1, mark, kept_1, got_1)
    ends_0, got_0 = far_end(0, kept_1, ends_0, got_0)
    ends_1, got_1 = far_sum(1, ends_0, kept_1, got_1)
    ends_0, got_0 = far_join(0, ends_1, ends_0, got_0)
    *grads, mark = input_gradients(3, ends_0, grads)
    ends_1, got_1 = far_end(1, mark, ends_1, got_1)
    ends_1, got_1 = far_join(1, ends_1, ends_1, got_1)
    blocks_0, others_0 = near_join(0, ends_1, ends_0, got_0)
    blocks_1, others_1 = near_join(1, blocks_0, ends_1, got_1)
    done = unpack(0, True, blocks_1, far, block, blocks_0, shapes, [])
    done = unpack(0, False, blocks_1, far, block, others_0, shapes, done)
    done = unpack(1, True, blocks_1, far, block, blocks_1, shapes, done)
    done = unpack(1, False, blocks_1, far, block, others_1, shapes, done)
    g_past, g_now, g_res, g_skip, g_cond, g_bias, g_bias_res, g_bias_skip = done
    grad_signal, grad_features = grads
    return (
        output,
        skip_out,
        grad_signal,
        grad_features.T,
        g_past,
        g_now,
        g_bias.reshape(-1),
        g_cond,
        g_res,
        g_bias_res.reshape(-1),
        g_skip,
        g_bias_skip.reshape(-1),
    )


def solution(mesh):
    row, col = mesh.shape["row"], mesh.shape["col"]
    fine = Mesh(mesh.devices.reshape(row // 2, 2, col // NEAR, NEAR), AXES)
    rows = P(AXES, None)
    line = P(AXES)
    return jax.shard_map(
        body,
        mesh=fine,
        in_specs=(rows, rows, line, line) + (P(),) * 8 + (rows, rows),
        out_specs=(rows,) * 4 + (P(),) * 8,
        check_vma=False,
    )
```

```python
import functools

import jax
import jax.numpy as jnp
from jax import lax
from jax.experimental import pallas as pl
from jax.experimental.pallas import tpu as pltpu
from jax.sharding import Mesh
from jax.sharding import PartitionSpec as P

DILATION_STEP = 256
AXES = ("outer", "core", "far", "near")
HALVES = 2
NEAR = 4
LANES = 128
ROWS = 512
F32 = jnp.float32
BF16 = jnp.bfloat16
MEGA = 1 << 20
COSTS = {
    "load": 8, "head": 2, "gradients_0": 4, "forward_1": 12, "gradients_1": 4, "outputs": 4, "near_sum_0": 8,
    "far_sum_0": 8, "input": 1, "unpack": 0,
}
FLOPS = 10**9


def dot(left, right):
    return jnp.dot(left, right, preferred_element_type=F32)


def across(left, right):
    return lax.dot_general(left, right, (((0,), (0,)), ((), ())), preferred_element_type=F32)


def against(left, weight):
    return lax.dot_general(left, weight, (((1,), (1,)), ((), ())), preferred_element_type=F32)


def column(lines):
    turned = lines.astype(F32).T
    return jnp.concatenate([turned[:, k : k + 1] for k in range(lines.shape[0])], axis=0)


def tap_of(lines):
    return column(jnp.where(lines >= DILATION_STEP, 1, 0))


def lines_of(ref, rows):
    return ref[rows.start // LANES : rows.stop // LANES, :]


def picked(head, rest, rows):
    cut = DILATION_STEP
    low = head[rows.start : min(rows.stop, cut), :] if rows.start < cut else None
    high = rest[max(rows.start, cut) - cut : rows.stop - cut, :] if rows.stop > cut else None
    if low is None:
        return high
    return low if high is None else jnp.concatenate([low, high], axis=0)


def call(kernel, name, in_specs, out_specs, out_shape, scratch=(), aliases=None, vmem=24):
    return pl.pallas_call(
        kernel,
        in_specs=in_specs,
        out_specs=out_specs,
        out_shape=out_shape,
        scratch_shapes=list(scratch),
        input_output_aliases=aliases or {},
        cost_estimate=pl.CostEstimate(
            flops=1 + FLOPS * COSTS.get(name, COSTS.get(name.split("_")[0], 0)), bytes_accessed=1, transcendentals=0
        ),
        name=name,
        compiler_params=pltpu.CompilerParams(vmem_limit_bytes=vmem * MEGA),
    )


VMEM = pl.BlockSpec(memory_space=pltpu.VMEM)
ANYWHERE = pl.BlockSpec(memory_space=pl.ANY)


def gates(past, now, feats, w_past, w_now, w_cond, b_conv, at, part):
    here = slice(at, at + part)
    return dot(past, w_past[:, here]) + dot(now, w_now[:, here]) + across(feats, w_cond[:, here]) + b_conv[:, here]


def slopes(pre_a, pre_s, dgated):
    act = jnp.tanh(pre_a)
    gate = 0.5 + 0.5 * jnp.tanh(0.5 * pre_s)
    slope = dgated * gate
    dpre = jnp.concatenate([slope * (1.0 - act * act), slope * act * (1.0 - gate)], axis=1)
    return (act * gate).astype(BF16), dpre.astype(BF16)


def forward(half, rows, past, sig, feat, dgated, mask, weights):
    part = dgated.shape[1] // HALVES
    args = (past, sig[rows, :], feat[:, rows], *weights)
    pre_a = gates(*args, half * part, part)
    pre_s = gates(*args, (HALVES + half) * part, part)
    gated, dpre = slopes(pre_a, pre_s, dgated[rows, half * part : (half + 1) * part])
    return gated, gated * mask, dpre


def rest_rows(rows):
    cuts = [DILATION_STEP, *range(ROWS, rows + 1, ROWS)]
    return [slice(a, b) for a, b in zip(cuts, cuts[1:])]


def moved(rows, by):
    return slice(rows.start + by, rows.stop + by)


LOADED = ("valid", "w_res", "w_skip", "gout", "gskip", "pos", "b_conv", "feat", "w_cond", "sig", "w_past", "w_now")


def load_body(count, *refs):
    sources, here = refs[:count], refs[count : 2 * count]
    dgated, sums, past_rest, gated_rest, kept_rest, dpre_rest, sems = refs[2 * count :]
    valid, w_res, w_skip, gout, gskip, pos, b_conv, feat, w_cond, sig, w_past, w_now = here[: len(LOADED)]
    steps = gout.shape[0] // ROWS
    copies = {}

    def start(k, i=None):
        at = (slice(None),) if i is None else (pl.ds(i * ROWS, ROWS),)
        copies[k, i] = pltpu.make_async_copy(sources[k].at[at], here[k].at[at], sems.at[len(copies)])
        copies[k, i].start()

    def wait(k, i=None):
        copies[k, i].wait()

    for k in range(3):
        start(k)
    for i in range(steps):
        start(3, i)
        start(4, i)
    for k in range(5, count):
        start(k)
    for k in range(3):
        wait(k)
    total = [jnp.zeros((8, gout.shape[1]), F32), jnp.zeros((8, gskip.shape[1]), F32)]
    for i in range(steps):
        wait(3, i)
        wait(4, i)
        rows = slice(i * ROWS, (i + 1) * ROWS)
        mask = column(lines_of(valid, rows))
        res, skip = gout[rows, :], gskip[rows, :]
        dgated[rows, :] = mask * (against(res, w_res[...]) + against(skip, w_skip[...]))
        for k, x in enumerate((res, skip)):
            total[k] += jnp.sum((mask * x.astype(F32)).reshape(ROWS // 8, 8, x.shape[1]), axis=0)
    for k in range(2):
        sums[k : k + 1, :] = jnp.sum(total[k], axis=0, keepdims=True)
    for k in range(5, count):
        wait(k)
    for rows in rest_rows(gout.shape[0]):
        there = moved(rows, -DILATION_STEP)
        past = sig[there, :] * tap_of(lines_of(pos, rows)).astype(BF16)
        mask = column(lines_of(valid, rows)).astype(BF16)
        past_rest[there, :] = past
        gated_rest[there, :], kept_rest[there, :], dpre_rest[there, :] = forward(
            0, rows, past, sig, feat, dgated, mask, (w_past, w_now, w_cond, b_conv)
        )


def load(*arrays):
    sources = [in_hbm(x) for x in arrays]
    named = dict(zip(LOADED, arrays))
    rows, width = named["gout"].shape
    hidden = named["w_res"].shape[0]
    rest = rows - DILATION_STEP
    part = hidden // HALVES
    shapes = [jax.ShapeDtypeStruct(x.shape, x.dtype) for x in sources] + [
        jax.ShapeDtypeStruct((rows, hidden), F32),
        jax.ShapeDtypeStruct((8, width), F32),
        jax.ShapeDtypeStruct((rest, width), BF16),
        jax.ShapeDtypeStruct((rest, part), BF16),
        jax.ShapeDtypeStruct((rest, part), BF16),
        jax.ShapeDtypeStruct((rest, 2 * part), BF16),
    ]
    count = len(sources)
    result = call(
        functools.partial(load_body, count),
        "load",
        [ANYWHERE] * count,
        [VMEM] * len(shapes),
        shapes,
        scratch=[pltpu.SemaphoreType.DMA((count + 2 * (rows // ROWS - 1),))],
    )(*sources)
    return result[:count], result[count:]


def past_term(dpre_0, dpre_1, weight, part):
    hidden = 2 * part
    total = against(dpre_0[:, :part], weight[:, :part])
    total += against(dpre_1[:, :part], weight[:, part:hidden])
    total += against(dpre_0[:, part:], weight[:, hidden : hidden + part])
    return total + against(dpre_1[:, part:], weight[:, hidden + part :])


def head_body(halo, sig, feat, pos, valid, dgated, w_past, w_now, w_cond, b_conv, past_out, early, *outs):
    rows = slice(0, DILATION_STEP)
    tap = tap_of(lines_of(pos, rows))
    mask = column(lines_of(valid, rows)).astype(BF16)
    past = halo[...] * tap.astype(BF16)
    past_out[...] = past
    dpres = []
    for half in range(HALVES):
        parts = forward(half, rows, past, sig, feat, dgated, mask, (w_past, w_now, w_cond, b_conv))
        for ref, x in zip(outs[3 * half :], parts):
            ref[...] = x
        dpres.append(parts[2])
    early[...] = (tap * past_term(*dpres, w_past, dpres[0].shape[1] // 2)).astype(BF16)


def head(halo, sig, feat, pos, valid, dgated, w_past, w_now, w_cond, b_conv):
    width = sig.shape[1]
    part = dgated.shape[1] // HALVES
    first, *others = [
        jax.ShapeDtypeStruct((DILATION_STEP, size), BF16) for size in (width, part, part, 2 * part)
    ]
    past, early, *parts = call(
        head_body,
        "head",
        [VMEM] * 10,
        [VMEM] * (2 + 3 * HALVES),
        [first, first] + others * HALVES,
    )(halo, sig, feat, pos, valid, dgated, w_past, w_now, w_cond, b_conv)
    return past, early, parts[:3], parts[3:]


def forward_body(token, past, sig, feat, valid, dgated, w_past, w_now, w_cond, b_conv, gated_out, kept_out, dpre_out):
    for rows in rest_rows(sig.shape[0]):
        there = moved(rows, -DILATION_STEP)
        mask = column(lines_of(valid, rows)).astype(BF16)
        gated_out[there, :], kept_out[there, :], dpre_out[there, :] = forward(
            1, rows, past[rows, :], sig, feat, dgated, mask, (w_past, w_now, w_cond, b_conv)
        )


def forward_rest(token, past, sig, feat, valid, dgated, w_past, w_now, w_cond, b_conv):
    rest = sig.shape[0] - DILATION_STEP
    part = dgated.shape[1] // HALVES
    return call(
        forward_body,
        "forward_1",
        [ANYWHERE] + [VMEM] * 9,
        [VMEM] * 3,
        [jax.ShapeDtypeStruct((rest, size), BF16) for size in (part, part, 2 * part)],
    )(token, past, sig, feat, valid, dgated, w_past, w_now, w_cond, b_conv)


def own_place():
    return [lax.axis_index(name) for name in ("core", "far", "near")]


def turned(index, count):
    bits = (count - 1).bit_length()
    result = 0
    for bit in range(bits):
        result = result | (((index >> bit) & 1) << (bits - 1 - bit))
    return result


def place_blocks(far, block, acc, theirs, mine):
    core, z, xy = own_place()
    for r in range(far):
        for c in range(NEAR):
            here = pl.ds(c * LANES, LANES)
            for k, out in ((1 - core, theirs), (core, mine)):
                rows = pl.ds(pl.multiple_of((k * far + r) * block, 16), block)
                out[c ^ xy, turned(r ^ z, far)] = acc[rows, here].astype(out.dtype)


def gradients_body(
    far, block, half, token, sig, feat, gout, gskip, sums, past_head, past_rest, kept_head, kept_rest, dpre_head, dpre_rest,
    theirs, mine, dpre, past, acc, kept,
):
    rows, width = sig.shape
    cond = feat.shape[0]
    part = kept.shape[1]
    cut = DILATION_STEP
    for whole, low, high in ((past, past_head, past_rest), (kept, kept_head, kept_rest), (dpre, dpre_head, dpre_rest)):
        whole[:cut, :] = low[...]
        whole[cut:, :] = high[...]
    bias = jnp.zeros((8, dpre.shape[1]), F32)
    for i in range(0, rows, ROWS):
        bias += jnp.sum(dpre[i : i + ROWS, :].astype(F32).reshape(ROWS // 8, 8, dpre.shape[1]), axis=0)
    at = 0
    for left, right in ((past, dpre), (sig, dpre), (kept, gout), (kept, gskip)):
        acc[at : at + left.shape[1], :] = across(left[...], right[...])
        at += left.shape[1]
    acc[at : at + cond, :] = dot(feat[...], dpre[...])
    at += cond
    acc[at : at + 1, :] = jnp.sum(bias, axis=0, keepdims=True)
    acc[at + 1 : at + 2, :] = sums[half : half + 1, :]
    acc[at + 2 :, :] = jnp.zeros((acc.shape[0] - at - 2, acc.shape[1]), F32)
    place_blocks(far, block, acc, theirs, mine)


def gradients(half, token, far, block, sig, feat, gout, gskip, sums, past, kept, dpre):
    rows, width = sig.shape
    part = kept[0].shape[1]
    packed = (NEAR, far, block, LANES)
    return call(
        functools.partial(gradients_body, far, block, half),
        f"gradients_{half}",
        [ANYWHERE] + [VMEM] * 11,
        [VMEM] * 4,
        [
            jax.ShapeDtypeStruct(packed, BF16),
            jax.ShapeDtypeStruct(packed, F32),
            jax.ShapeDtypeStruct((rows, 2 * part), BF16),
            jax.ShapeDtypeStruct((rows, width), BF16),
        ],
        scratch=[pltpu.VMEM((2 * far * block, 2 * part), F32), pltpu.VMEM((rows, part), BF16)],
    )(token, sig, feat, gout, gskip, sums, *past, *kept, *dpre)


def outputs_body(
    token, sig, valid, head_0, rest_0, head_1, rest_1, w_res, b_res, w_skip, b_skip, out, skip, mark, rooms, sems
):
    part = head_0.shape[1]
    copies = []
    for i in range(sig.shape[0] // ROWS):
        rows = slice(i * ROWS, (i + 1) * ROWS)
        mask = column(lines_of(valid, rows))
        left, right = picked(head_0, rest_0, rows), picked(head_1, rest_1, rows)
        branch = dot(left, w_res[:part, :]) + dot(right, w_res[part:, :]) + b_res[...]
        rooms[i, 0] = (sig[rows, :].astype(F32) + mask * branch).astype(BF16)
        side = dot(left, w_skip[:part, :]) + dot(right, w_skip[part:, :]) + b_skip[...]
        rooms[i, 1] = (mask * side).astype(BF16)
        for k, ref in enumerate((out, skip)):
            copies.append(pltpu.make_async_copy(rooms.at[i, k], ref.at[pl.ds(i * ROWS, ROWS)], sems.at[i, k]))
            copies[-1].start()
    mark[...] = jnp.zeros_like(mark)
    for copy in copies:
        copy.wait()


MARK = jax.ShapeDtypeStruct((8, LANES), F32)


def outputs(token, sig, valid, gated_0, gated_1, w_res, b_res, w_skip, b_skip):
    rows, width = sig.shape
    return call(
        outputs_body,
        "outputs",
        [ANYWHERE] + [VMEM] * 10,
        [ANYWHERE, ANYWHERE, VMEM],
        [
            jax.ShapeDtypeStruct((rows, width), BF16),
            jax.ShapeDtypeStruct((rows, w_skip.shape[1]), BF16),
            MARK,
        ],
        scratch=[
            pltpu.VMEM((rows // ROWS, 2, ROWS, width), BF16),
            pltpu.SemaphoreType.DMA((rows // ROWS, 2)),
        ],
    )(token, sig, valid, *gated_0, *gated_1, w_res, b_res, w_skip, b_skip)


def k2b_body(step, token, received, gout, pos, dpre_0, dpre_1, w_past, w_now, w_cond, *refs):
    gsig, gfeat, mark, room, room_feat, sems = refs[-6:]
    rows, width = gout.shape
    part = dpre_0.shape[1] // 2
    hidden = 2 * part
    begin = step * ROWS
    here = slice(begin, begin + ROWS)
    left, right = dpre_0[here, :], dpre_1[here, :]
    after = slice(begin + DILATION_STEP, min(begin + DILATION_STEP + ROWS, rows))
    tap = tap_of(lines_of(pos, after))
    copies = []
    wide = 2 * LANES
    for k in range(width // wide):
        some = slice(k * wide, (k + 1) * wide)
        tail = tap * past_term(dpre_0[after, :], dpre_1[after, :], w_past[some, :], part)
        if tail.shape[0] < ROWS:
            tail = jnp.concatenate([tail, received[:, some].astype(F32)], axis=0)
        room[k] = gout[here, some].astype(F32) + past_term(left, right, w_now[some, :], part) + tail
        copies.append(pltpu.make_async_copy(room.at[k], gsig.at[pl.ds(begin, ROWS), pl.ds(k * wide, wide)], sems.at[k]))
        copies[-1].start()
    total = against(w_cond[:, :part], left[:, :part])
    total += against(w_cond[:, part:hidden], right[:, :part])
    total += against(w_cond[:, hidden : hidden + part], left[:, part:])
    room_feat[...] = total + against(w_cond[:, hidden + part :], right[:, part:])
    copies.append(pltpu.make_async_copy(room_feat, gfeat.at[:, pl.ds(begin, ROWS)], sems.at[width // wide]))
    copies[-1].start()
    mark[...] = jnp.zeros_like(mark)
    for copy in copies:
        copy.wait()


def k2b(step, token, received, gout, pos, dpre, w_past, w_now, w_cond, before):
    rows, width = gout.shape
    cond = w_cond.shape[0]
    count = width // (2 * LANES)
    return call(
        functools.partial(k2b_body, step),
        f"input_gradients_{step}",
        [ANYWHERE] + [VMEM] * 8 + [ANYWHERE] * len(before),
        [ANYWHERE, ANYWHERE, VMEM],
        [
            jax.ShapeDtypeStruct((rows, width), F32),
            jax.ShapeDtypeStruct((cond, rows), F32),
            MARK,
        ],
        scratch=[
            pltpu.VMEM((count, ROWS, 2 * LANES), F32),
            pltpu.VMEM((cond, ROWS), F32),
            pltpu.SemaphoreType.DMA((count + 1,)),
        ],
        aliases={9 + k: k for k in range(len(before))},
    )(token, received, gout, pos, *dpre, w_past, w_now, w_cond, *before)


def regions(half, far, block, width, hidden, cond, k):
    part = hidden // HALVES
    found = []
    at = 0
    for array, first, count in ((0, 0, width), (1, 0, width), (2, half * part, part), (3, half * part, part), (4, 0, cond)):
        low, high = max(at, k * far * block), min(at + count, (k + 1) * far * block)
        if low < high:
            found.append((array, first + low - at, low - k * far * block, high - low))
        at += count
    return found, at - k * far * block


def unpack_body(half, own, far, block, hidden, cond, token, blocks, *refs):
    outs, (mark, room, bias, own_bias, sems) = refs[-13:-5], refs[-5:]
    mark[...] = jnp.zeros_like(mark)
    part = hidden // HALVES
    core, z, xy = own_place()
    which = core if own else 1 - core
    for p in range(NEAR):
        for r in range(far):
            rows = pl.ds(pl.multiple_of((r ^ z) * block, 16), block)
            room[p, rows, :] = blocks[p, turned(r, far)].astype(F32)
    for k in range(2):
        found, last = regions(half, far, block, outs[0].shape[0], hidden, cond, k)

        @pl.when(which == k)
        def _(found=found, last=last):
            copies = []

            def copy(source, target):
                copies.append(pltpu.make_async_copy(source, target, sems.at[len(copies)]))
                copies[-1].start()

            for p in range(NEAR):
                c = p ^ xy
                wide = pl.multiple_of((c >> 1) * hidden + half * part + (c & 1) * LANES, LANES)
                tall = pl.multiple_of(c * LANES, LANES)
                for array, first, at, count in found:
                    here = pl.ds(tall if array in (2, 3) else wide, LANES)
                    copy(room.at[p, pl.ds(at, count)], outs[array].at[pl.ds(first, count), here])
                if 0 <= last < room.shape[1]:
                    pair = room[p, last : last + 8, :]
                    bias[:, pl.ds(tall, LANES)] = pair[0:1]
                    own_bias[:, pl.ds(tall, LANES)] = pair[1:2]
            if 0 <= last < room.shape[1]:
                for j in range(2):
                    copy(bias.at[:, pl.ds(j * part, part)], outs[5].at[:, pl.ds(j * hidden + half * part, part)])
                copy(own_bias, outs[6 + half])
            for one in copies:
                one.wait()


def unpack(half, own, token, far, block, blocks, shapes, before):
    hidden, cond = shapes[2][0], shapes[4][0]
    return call(
        functools.partial(unpack_body, half, own, far, block, hidden, cond),
        f"unpack_{half}_{own:d}",
        [ANYWHERE, VMEM] + [ANYWHERE] * len(before),
        [ANYWHERE] * len(shapes) + [VMEM],
        [jax.ShapeDtypeStruct(shape, F32) for shape in shapes] + [MARK],
        scratch=[
            pltpu.VMEM((NEAR, far * block, LANES), F32),
            pltpu.VMEM((1, NEAR * LANES), F32),
            pltpu.VMEM((1, NEAR * LANES), F32),
            pltpu.SemaphoreType.DMA((6 * NEAR,)),
        ],
        aliases={2 + k: k for k in range(len(before))},
    )(token, blocks, *before)


def swapped(x, axis, k):
    return lax.ppermute(x, axis, [(i, i ^ k) for i in range(lax.axis_size(axis))])


def exchanged(blocks):
    return [swapped(block, "near", k + 1) for k, block in enumerate(blocks)]


def add_body(sizes, token, *refs):
    count = len(sizes)
    kept, got, outs = refs[0], refs[1:-count], refs[-count:]
    at = 0
    for out, size in zip(outs, sizes):
        for k in range(size):
            total = kept[at + k].astype(F32)
            for ref in got:
                total = total + ref[at + k].astype(F32)
            out[k] = total.astype(out.dtype)
        at += size


def added(name, token, kept, got, outs):
    sizes = [size for size, _ in outs]
    result = call(
        functools.partial(add_body, sizes),
        name,
        [ANYWHERE] + [VMEM] * (1 + len(got)),
        [VMEM] * len(outs),
        [jax.ShapeDtypeStruct((size, *kept.shape[1:]), dtype) for size, dtype in outs],
    )(token, kept, *got)
    return result


def mirror_body(token, mine, got, out):
    count = mine.shape[0]
    for k in range(count):
        out[k] = (mine[k].astype(F32) + got[count - 1 - k].astype(F32)).astype(out.dtype)


def mirrored(name, token, mine, got):
    return call(
        mirror_body,
        name,
        [ANYWHERE, VMEM, VMEM],
        VMEM,
        jax.ShapeDtypeStruct(mine.shape, BF16),
    )(token, mine, got)


def join_body(token, *refs):
    out = refs[-1]
    at = 0
    for ref in refs[:-1]:
        out[at : at + ref.shape[0]] = ref[...]
        at += ref.shape[0]


def joined(name, token, parts):
    count = sum(part.shape[0] for part in parts)
    return call(
        join_body,
        name,
        [ANYWHERE] + [VMEM] * len(parts),
        VMEM,
        jax.ShapeDtypeStruct((count, *parts[0].shape[1:]), BF16),
    )(token, *parts)


def over_outer(total):
    for bit in range((lax.axis_size("outer") - 1).bit_length()):
        total = (total.astype(F32) + swapped(total, "outer", 1 << bit).astype(F32)).astype(BF16)
    return total


def passed_along(x, by):
    peers = lax.axis_size(AXES)
    pairs = [(i, i + by) for i in range(peers) if 0 <= i + by < peers]
    return lax.ppermute(x, AXES, pairs)


def in_hbm(x):
    return pltpu.with_memory_space_constraint(x, pltpu.HBM)


def body(
    signal,
    features,
    position,
    valid,
    w_past,
    w_now,
    b_conv,
    w_cond,
    w_res,
    b_res,
    w_skip,
    b_skip,
    grad_out,
    grad_skip,
):
    rows, width = signal.shape
    features = features.T
    cond = features.shape[0]
    hidden = w_res.shape[0]
    skip_width = w_skip.shape[1]
    far = lax.axis_size("far")
    far_bits = (far - 1).bit_length()
    used = 2 * width + 2 * (hidden // HALVES) + cond + 2
    block = -(-used // (2 * far * 16)) * 16
    lines = (rows // LANES, LANES)
    pos, val = position.reshape(lines), valid.reshape(lines)
    b_conv, b_res, b_skip = (b.reshape(1, -1) for b in (b_conv, b_res, b_skip))
    shapes = [
        (width, 2 * hidden), (width, 2 * hidden), (hidden, width), (hidden, skip_width), (cond, 2 * hidden),
        (1, 2 * hidden), (1, width), (1, skip_width),
    ]

    def core_sum(half, token, theirs, mine):
        kept, *sent = added(
            f"core_sum_{half}", token, mine, [swapped(theirs, "core", 1)], [(1, F32)] + [(1, BF16)] * (NEAR - 1)
        )
        return kept[0], exchanged([x[0] for x in sent])

    def near_sum(half, token, kept, got):
        kept, sent = added(f"near_sum_{half}", token, kept, got, [(far // 2, F32), (far // 2, BF16)])
        return kept, swapped(sent, "far", 1)

    def far_sum(half, token, kept, got):
        for bit in range(1, far_bits - 1):
            size = kept.shape[0] // 2
            kept, sent = added(f"far_sum_{half}_{bit}", token, kept, [got], [(size, F32), (size, BF16)])
            got = swapped(sent, "far", 1 << bit)
        (mine,) = added(f"far_sum_{half}", token, kept, [got], [(kept.shape[0], BF16)])
        return mine, swapped(mine, "far", 1 << (far_bits - 1))

    def far_end(half, token, mine, got):
        total = over_outer(mirrored(f"far_end_{half}", token, mine, got))
        return total, swapped(total, "far", 1 << (far_bits - 2))

    def far_join(half, token, mine, got):
        total = joined(f"far_join_{half}", token, [mine, got])
        for bit in reversed(range(far_bits - 2)):
            total = joined(f"far_join_{half}_{bit}", token, [total, swapped(total, "far", 1 << bit)])
        return total, exchanged([total] * (NEAR - 1))

    def near_join(half, token, mine, got):
        total = joined(f"near_join_{half}", token, [mine[None]] + [x[None] for x in got])
        return total, swapped(total, "core", 1)

    def input_gradients(step, token, before):
        last = (step + 1) * ROWS == rows
        return k2b(step, token, received if last else early, grad_out, pos, dpre, w_past, w_now, w_cond, before)

    halo = passed_along(signal[rows - DILATION_STEP :], 1)
    loaded, parts = load(
        val, w_res, w_skip, grad_out, grad_skip, pos, b_conv, features, w_cond, signal, w_past, w_now, b_res, b_skip
    )
    val, w_res, w_skip, grad_out, grad_skip, pos, b_conv, features, w_cond, signal, w_past, w_now, b_res, b_skip = loaded
    dgated, sums, past_rest, gated_rest_0, kept_rest_0, dpre_rest_0 = parts
    weights = (w_past, w_now, w_cond, b_conv)
    past_head, early, head_0, head_1 = head(halo, signal, features, pos, val, dgated, *weights)
    received = passed_along(early, -1)
    common = (signal, features, grad_out, grad_skip, sums)
    theirs_0, mine_0, dpre_0, past = gradients(
        0, early, far, block, *common, (past_head, past_rest), (head_0[1], kept_rest_0), (head_0[2], dpre_rest_0)
    )
    gated_rest_1, kept_rest_1, dpre_rest_1 = forward_rest(received, past, signal, features, val, dgated, *weights)
    kept_0, got_0 = core_sum(0, gated_rest_1, theirs_0, mine_0)
    theirs_1, mine_1, dpre_1, _ = gradients(
        1, kept_0, far, block, *common, (past_head, past_rest), (head_1[1], kept_rest_1), (head_1[2], dpre_rest_1)
    )
    dpre = (dpre_0, dpre_1)
    output, skip_out, mark = outputs(
        dpre_1, signal, val, (head_0[0], gated_rest_0), (head_1[0], gated_rest_1), w_res, b_res, w_skip, b_skip
    )
    kept_0, got_0 = near_sum(0, mark, kept_0, got_0)
    kept_1, got_1 = core_sum(1, kept_0, theirs_1, mine_1)
    ends_0, got_0 = far_sum(0, kept_1, kept_0, got_0)
    *grads, mark = input_gradients(0, ends_0, [])
    ends_0, got_0 = far_end(0, mark, ends_0, got_0)
    *grads, mark = input_gradients(1, ends_0, grads)
    kept_1, got_1 = near_sum(1, mark, kept_1, got_1)
    ends_0, got_0 = far_join(0, kept_1, ends_0, got_0)
    *grads, mark = input_gradients(2, ends_0, grads)
    ends_1, got_1 = far_sum(1, mark, kept_1, got_1)
    *grads, mark = input_gradients(3, ends_1, grads)
    ends_1, got_1 = far_end(1, mark, ends_1, got_1)
    blocks_0, others_0 = near_join(0, ends_1, ends_0, got_0)
    ends_1, got_1 = far_join(1, blocks_0, ends_1, got_1)
    *done, mark = unpack(0, True, ends_1, far, block, blocks_0, shapes, [])
    blocks_1, others_1 = near_join(1, mark, ends_1, got_1)
    *done, mark = unpack(0, False, blocks_1, far, block, others_0, shapes, done)
    *done, mark = unpack(1, True, mark, far, block, blocks_1, shapes, done)
    *done, mark = unpack(1, False, mark, far, block, others_1, shapes, done)
    grad_signal, grad_features = grads
    g_past, g_now, g_res, g_skip, g_cond, g_bias, g_bias_res, g_bias_skip = done
    return (
        output,
        skip_out,
        grad_signal,
        grad_features.T,
        g_past,
        g_now,
        g_bias.reshape(-1),
        g_cond,
        g_res,
        g_bias_res.reshape(-1),
        g_skip,
        g_bias_skip.reshape(-1),
    )


def solution(mesh):
    row, col = mesh.shape["row"], mesh.shape["col"]
    fine = Mesh(mesh.devices.reshape(row // 2, 2, col // NEAR, NEAR), AXES)
    rows = P(AXES, None)
    line = P(AXES)
    return jax.shard_map(
        body,
        mesh=fine,
        in_specs=(rows, rows, line, line) + (P(),) * 8 + (rows, rows),
        out_specs=(rows,) * 4 + (P(),) * 8,
        check_vma=False,
    )
```

```python
import functools

import jax
import jax.numpy as jnp
from jax import lax
from jax.experimental import pallas as pl
from jax.experimental.pallas import tpu as pltpu
from jax.sharding import Mesh
from jax.sharding import PartitionSpec as P

DILATION_STEP = 256
AXES = ("outer", "core", "far", "near")
HALVES = 2
NEAR = 4
LANES = 128
ROWS = 512
F32 = jnp.float32
BF16 = jnp.bfloat16
MEGA = 1 << 20
COSTS = {
    "load": 8, "head": 2, "gradients_0": 4, "forward_1": 12, "gradients_1": 4, "outputs": 4, "near_sum_0": 8,
    "far_sum_0": 8, "far_end_1": 3, "near_sum_1": 4, "near_join_0": 1, "near_join_1": 4,
}
FLOPS = 10**9


def dot(left, right):
    return jnp.dot(left, right, preferred_element_type=F32)


def across(left, right):
    return lax.dot_general(left, right, (((0,), (0,)), ((), ())), preferred_element_type=F32)


def against(left, weight):
    return lax.dot_general(left, weight, (((1,), (1,)), ((), ())), preferred_element_type=F32)


def column(lines):
    turned = lines.astype(F32).T
    return jnp.concatenate([turned[:, k : k + 1] for k in range(lines.shape[0])], axis=0)


def tap_of(lines):
    return column(jnp.where(lines >= DILATION_STEP, 1, 0))


def lines_of(ref, rows):
    return ref[rows.start // LANES : rows.stop // LANES, :]


def picked(head, rest, rows):
    cut = DILATION_STEP
    low = head[rows.start : min(rows.stop, cut), :] if rows.start < cut else None
    high = rest[max(rows.start, cut) - cut : rows.stop - cut, :] if rows.stop > cut else None
    if low is None:
        return high
    return low if high is None else jnp.concatenate([low, high], axis=0)


def call(kernel, name, in_specs, out_specs, out_shape, scratch=(), aliases=None, vmem=24):
    return pl.pallas_call(
        kernel,
        in_specs=in_specs,
        out_specs=out_specs,
        out_shape=out_shape,
        scratch_shapes=list(scratch),
        input_output_aliases=aliases or {},
        cost_estimate=pl.CostEstimate(
            flops=1 + int(FLOPS * COSTS.get(name, COSTS.get(name.split("_")[0], 0))), bytes_accessed=1, transcendentals=0
        ),
        name=name,
        compiler_params=pltpu.CompilerParams(vmem_limit_bytes=vmem * MEGA),
    )


VMEM = pl.BlockSpec(memory_space=pltpu.VMEM)
ANYWHERE = pl.BlockSpec(memory_space=pl.ANY)


def beside(*parts):
    return jnp.concatenate(parts, axis=1)


def forward(half, rows, past, sig, feat, gout, gskip, mask, w_in, w_cond, b_conv, w_out):
    part = w_out.shape[0] // HALVES
    both = beside(past, sig[rows, :])
    feats = feat[:, rows]

    def pre(at):
        here = slice(at, at + part)
        return dot(both, w_in[:, here]) + across(feats, w_cond[:, here]) + b_conv[:, here]

    first = half * part
    dgated = mask * against(beside(gout[rows, :], gskip[rows, :]), w_out[first : first + part, :])
    act = jnp.tanh(pre(first))
    gate = 0.5 + 0.5 * jnp.tanh(0.5 * pre(HALVES * part + first))
    slope = dgated * gate
    dpre = beside(slope * (1.0 - act * act), slope * act * (1.0 - gate)).astype(BF16)
    gated = (act * gate).astype(BF16)
    return gated, gated * mask.astype(BF16), dpre


def rest_rows(rows):
    cuts = [DILATION_STEP, *range(ROWS, rows + 1, ROWS)]
    return [slice(a, b) for a, b in zip(cuts, cuts[1:])]


def moved(rows, by):
    return slice(rows.start + by, rows.stop + by)


def load_body(
    valid, pos, b_conv, b_res, b_skip, feat, w_cond, w_res, w_skip, w_past, w_now, sig, gout, gskip,
    valid_to, pos_to, b_conv_to, b_res_to, b_skip_to, feat_to, w_cond_to, w_out, w_in, sig_to, gout_to, gskip_to,
    past_rest, gated_rest, kept_rest, dpre_rest, sems,
):
    width = sig.shape[1]
    copies = []

    def start(source, target):
        copies.append(pltpu.make_async_copy(source, target, sems.at[len(copies)]))
        copies[-1].start()
        return copies[-1]

    def tile(i):
        rows = pl.ds(i * ROWS, ROWS)
        return [start(x.at[rows], y.at[rows]) for x, y in ((sig, sig_to), (gout, gout_to), (gskip, gskip_to))]

    start(valid, valid_to)
    start(pos, pos_to)
    start(b_conv, b_conv_to)
    start(w_cond, w_cond_to)
    start(feat, feat_to)
    start(w_past, w_in.at[pl.ds(0, width)])
    start(w_now, w_in.at[pl.ds(width, width)])
    start(w_res, w_out.at[:, pl.ds(0, width)])
    start(w_skip, w_out.at[:, pl.ds(width, gskip.shape[1])])
    tiled = [tile(i) for i in range(sig.shape[0] // ROWS)]
    last = [start(b_res, b_res_to), start(b_skip, b_skip_to)]
    for copy in copies[:9]:
        copy.wait()
    for rows in rest_rows(sig.shape[0]):
        for copy in tiled[rows.start // ROWS]:
            copy.wait()
        there = moved(rows, -DILATION_STEP)
        past = sig_to[there, :] * tap_of(lines_of(pos_to, rows)).astype(BF16)
        past_rest[there, :] = past
        gated_rest[there, :], kept_rest[there, :], dpre_rest[there, :] = forward(
            0, rows, past, sig_to, feat_to, gout_to, gskip_to, column(lines_of(valid_to, rows)), w_in, w_cond_to, b_conv_to, w_out
        )
    for copy in last:
        copy.wait()


def load(valid, pos, b_conv, b_res, b_skip, feat, w_cond, w_res, w_skip, w_past, w_now, sig, gout, gskip):
    sources = [
        in_hbm(x) for x in (valid, pos, b_conv, b_res, b_skip, feat, w_cond, w_res, w_skip, w_past, w_now, sig, gout, gskip)
    ]
    rows, width = sig.shape
    hidden = w_res.shape[0]
    rest = rows - DILATION_STEP
    part = hidden // HALVES
    shapes = [jax.ShapeDtypeStruct(x.shape, x.dtype) for x in sources[:7]] + [
        jax.ShapeDtypeStruct(shape, BF16)
        for shape in (
            (hidden, width + gskip.shape[1]), (2 * width, 2 * hidden), sig.shape, gout.shape, gskip.shape,
            (rest, width), (rest, part), (rest, part), (rest, 2 * part),
        )
    ]
    return call(
        load_body,
        "load",
        [ANYWHERE] * len(sources),
        [VMEM] * len(shapes),
        shapes,
        scratch=[pltpu.SemaphoreType.DMA((11 + 3 * (rows // ROWS),))],
    )(*sources)


def side_by_side(dpre_0, dpre_1):
    part = dpre_0.shape[1] // 2
    return beside(dpre_0[:, :part], dpre_1[:, :part], dpre_0[:, part:], dpre_1[:, part:])


def head_body(halo, pos, valid, sig, feat, gout, gskip, w_in, w_cond, b_conv, w_out, past_out, early, *outs):
    rows = slice(0, DILATION_STEP)
    tap = tap_of(lines_of(pos, rows))
    mask = column(lines_of(valid, rows))
    past = halo[...] * tap.astype(BF16)
    past_out[...] = past
    dpres = []
    for half in range(HALVES):
        parts = forward(half, rows, past, sig, feat, gout, gskip, mask, w_in, w_cond, b_conv, w_out)
        for ref, x in zip(outs[3 * half :], parts):
            ref[...] = x
        dpres.append(parts[2])
    early[...] = (tap * against(side_by_side(*dpres), w_in[: sig.shape[1], :])).astype(BF16)


def head(*args):
    width = args[3].shape[1]
    part = args[-1].shape[0] // HALVES
    first, *others = [
        jax.ShapeDtypeStruct((DILATION_STEP, size), BF16) for size in (width, part, part, 2 * part)
    ]
    past, early, *parts = call(
        head_body,
        "head",
        [VMEM] * len(args),
        [VMEM] * (2 + 3 * HALVES),
        [first, first] + others * HALVES,
    )(*args)
    return past, early, parts[:3], parts[3:]


def forward_body(token, past, valid, sig, feat, gout, gskip, w_in, w_cond, b_conv, w_out, gated_out, kept_out, dpre_out):
    for rows in rest_rows(sig.shape[0]):
        there = moved(rows, -DILATION_STEP)
        gated_out[there, :], kept_out[there, :], dpre_out[there, :] = forward(
            1, rows, past[there, :], sig, feat, gout, gskip, column(lines_of(valid, rows)), w_in, w_cond, b_conv, w_out
        )


def forward_rest(token, *args):
    rest = args[0].shape[0]
    part = args[-1].shape[0] // HALVES
    return call(
        forward_body,
        "forward_1",
        [ANYWHERE] + [VMEM] * len(args),
        [VMEM] * 3,
        [jax.ShapeDtypeStruct((rest, size), BF16) for size in (part, part, 2 * part)],
    )(token, *args)


def own_place():
    return [lax.axis_index(name) for name in ("core", "far", "near")]


def turned(index, count):
    bits = (count - 1).bit_length()
    result = 0
    for bit in range(bits):
        result = result | (((index >> bit) & 1) << (bits - 1 - bit))
    return result


def place_blocks(far, block, acc, theirs, mine):
    core, z, xy = own_place()
    for r in range(far):
        for c in range(NEAR):
            here = pl.ds(c * LANES, LANES)
            for k, out in ((1 - core, theirs), (core, mine)):
                rows = pl.ds(pl.multiple_of((k * far + r) * block, 16), block)
                out[c ^ xy, turned(r ^ z, far)] = acc[rows, here].astype(out.dtype)


def gradients_body(
    far, block, half, token, valid, sig, feat, gout, gskip, past_head, past_rest, kept_head, kept_rest, dpre_head, dpre_rest,
    theirs, mine, dpre, past, acc, kept,
):
    rows, width = sig.shape
    cond = feat.shape[0]
    part = kept.shape[1]
    cut = DILATION_STEP
    for whole, low, high in ((past, past_head, past_rest), (kept, kept_head, kept_rest), (dpre, dpre_head, dpre_rest)):
        whole[:cut, :] = low[...]
        whole[cut:, :] = high[...]
    bias = jnp.zeros((8, dpre.shape[1]), F32)
    own = jnp.zeros((8, dpre.shape[1]), F32)
    for i in range(0, rows, ROWS):
        here = slice(i, i + ROWS)
        mask = column(lines_of(valid, here))
        bias += jnp.sum(dpre[here, :].astype(F32).reshape(ROWS // 8, 8, dpre.shape[1]), axis=0)
        given = mask * (gout, gskip)[half][here, :].astype(F32)
        own += jnp.sum(given.reshape(ROWS // 8, 8, dpre.shape[1]), axis=0)
    at = 0
    for left, right in ((past, dpre), (sig, dpre), (kept, gout), (kept, gskip)):
        acc[at : at + left.shape[1], :] = across(left[...], right[...])
        at += left.shape[1]
    acc[at : at + cond, :] = dot(feat[...], dpre[...])
    at += cond
    acc[at : at + 1, :] = jnp.sum(bias, axis=0, keepdims=True)
    acc[at + 1 : at + 2, :] = jnp.sum(own, axis=0, keepdims=True)
    acc[at + 2 :, :] = jnp.zeros((acc.shape[0] - at - 2, acc.shape[1]), F32)
    place_blocks(far, block, acc, theirs, mine)


def gradients(half, token, far, block, valid, sig, feat, gout, gskip, past, kept, dpre):
    rows, width = sig.shape
    part = kept[0].shape[1]
    packed = (NEAR, far, block, LANES)
    return call(
        functools.partial(gradients_body, far, block, half),
        f"gradients_{half}",
        [ANYWHERE] + [VMEM] * 11,
        [VMEM] * 4,
        [
            jax.ShapeDtypeStruct(packed, BF16),
            jax.ShapeDtypeStruct(packed, F32),
            jax.ShapeDtypeStruct((rows, 2 * part), BF16),
            jax.ShapeDtypeStruct((rows, width), BF16),
        ],
        scratch=[pltpu.VMEM((2 * far * block, 2 * part), F32), pltpu.VMEM((rows, part), BF16)],
    )(token, valid, sig, feat, gout, gskip, *past, *kept, *dpre)


def outputs_body(
    token, valid, sig, head_0, rest_0, head_1, rest_1, w_out, b_res, b_skip, out, skip, mark, rooms, sems
):
    width = sig.shape[1]
    copies = []
    for i in range(sig.shape[0] // ROWS):
        rows = slice(i * ROWS, (i + 1) * ROWS)
        mask = column(lines_of(valid, rows))
        gated = beside(picked(head_0, rest_0, rows), picked(head_1, rest_1, rows))
        branch = dot(gated, w_out[:, :width]) + b_res[...]
        rooms[i, 0] = (sig[rows, :].astype(F32) + mask * branch).astype(BF16)
        side = dot(gated, w_out[:, width:]) + b_skip[...]
        rooms[i, 1] = (mask * side).astype(BF16)
        for k, ref in enumerate((out, skip)):
            copies.append(pltpu.make_async_copy(rooms.at[i, k], ref.at[pl.ds(i * ROWS, ROWS)], sems.at[i, k]))
            copies[-1].start()
    mark[...] = jnp.zeros_like(mark)
    for copy in copies:
        copy.wait()


MARK = jax.ShapeDtypeStruct((8, LANES), F32)


def outputs(token, valid, sig, gated_0, gated_1, w_out, b_res, b_skip):
    rows, width = sig.shape
    return call(
        outputs_body,
        "outputs",
        [ANYWHERE] + [VMEM] * 9,
        [ANYWHERE, ANYWHERE, VMEM],
        [
            jax.ShapeDtypeStruct((rows, width), BF16),
            jax.ShapeDtypeStruct((rows, w_out.shape[1] - width), BF16),
            MARK,
        ],
        scratch=[
            pltpu.VMEM((rows // ROWS, 2, ROWS, width), BF16),
            pltpu.SemaphoreType.DMA((rows // ROWS, 2)),
        ],
    )(token, valid, sig, *gated_0, *gated_1, w_out, b_res, b_skip)


def k2b_body(step, token, received, gout, pos, dpre_0, dpre_1, w_in, w_cond, *refs):
    gsig, gfeat, mark, room, room_feat, sems = refs[-6:]
    rows, width = gout.shape
    begin = step * ROWS
    here = slice(begin, begin + ROWS)
    after = slice(begin + DILATION_STEP, min(begin + DILATION_STEP + ROWS, rows))
    now = side_by_side(dpre_0[here, :], dpre_1[here, :])
    later = side_by_side(dpre_0[after, :], dpre_1[after, :])
    tap = tap_of(lines_of(pos, after))
    copies = []
    wide = 2 * LANES
    for k in range(width // wide):
        some = slice(k * wide, (k + 1) * wide)
        tail = tap * against(later, w_in[some, :])
        if tail.shape[0] < ROWS:
            tail = jnp.concatenate([tail, received[:, some].astype(F32)], axis=0)
        room[k] = gout[here, some].astype(F32) + against(now, w_in[width + k * wide : width + (k + 1) * wide, :]) + tail
        copies.append(pltpu.make_async_copy(room.at[k], gsig.at[pl.ds(begin, ROWS), pl.ds(k * wide, wide)], sems.at[k]))
        copies[-1].start()
    room_feat[...] = against(w_cond[...], now)
    copies.append(pltpu.make_async_copy(room_feat, gfeat.at[:, pl.ds(begin, ROWS)], sems.at[width // wide]))
    copies[-1].start()
    mark[...] = jnp.zeros_like(mark)
    for copy in copies:
        copy.wait()


def k2b(step, token, received, gout, pos, dpre, w_in, w_cond, before):
    rows, width = gout.shape
    cond = w_cond.shape[0]
    count = width // (2 * LANES)
    return call(
        functools.partial(k2b_body, step),
        f"input_gradients_{step}",
        [ANYWHERE] + [VMEM] * 7 + [ANYWHERE] * len(before),
        [ANYWHERE, ANYWHERE, VMEM],
        [
            jax.ShapeDtypeStruct((rows, width), F32),
            jax.ShapeDtypeStruct((cond, rows), F32),
            MARK,
        ],
        scratch=[
            pltpu.VMEM((count, ROWS, 2 * LANES), F32),
            pltpu.VMEM((cond, ROWS), F32),
            pltpu.SemaphoreType.DMA((count + 1,)),
        ],
        aliases={8 + k: k for k in range(len(before))},
    )(token, received, gout, pos, *dpre, w_in, w_cond, *before)


def regions(half, far, block, width, hidden, cond, k):
    part = hidden // HALVES
    found = []
    at = 0
    for array, first, count in ((0, 0, width), (1, 0, width), (2, half * part, part), (3, half * part, part), (4, 0, cond)):
        low, high = max(at, k * far * block), min(at + count, (k + 1) * far * block)
        if low < high:
            found.append((array, first + low - at, low - k * far * block, high - low))
        at += count
    return found, at - k * far * block


def unpack_body(half, own, first_place, far, block, hidden, cond, token, blocks, *refs):
    outs, (mark, room, bias, own_bias, sems) = refs[-13:-5], refs[-5:]
    mark[...] = jnp.zeros_like(mark)
    part = hidden // HALVES
    core, z, xy = own_place()
    which = core if own else 1 - core
    for p in range(room.shape[0]):
        for r in range(far):
            rows = pl.ds(pl.multiple_of((r ^ z) * block, 16), block)
            room[p, rows, :] = blocks[p, turned(r, far)].astype(F32)
    for k in range(2):
        found, last = regions(half, far, block, outs[0].shape[0], hidden, cond, k)

        @pl.when(which == k)
        def _(found=found, last=last):
            copies = []

            def copy(source, target):
                copies.append(pltpu.make_async_copy(source, target, sems.at[len(copies)]))
                copies[-1].start()

            for p in range(room.shape[0]):
                c = (p + first_place) ^ xy
                wide = pl.multiple_of((c >> 1) * hidden + half * part + (c & 1) * LANES, LANES)
                tall = pl.multiple_of(c * LANES, LANES)
                for array, first, at, count in found:
                    here = pl.ds(tall if array in (2, 3) else wide, LANES)
                    copy(room.at[p, pl.ds(at, count)], outs[array].at[pl.ds(first, count), here])
                if 0 <= last < room.shape[1]:
                    pair = room[p, last : last + 8, :]
                    bias[p] = pair[0:1]
                    own_bias[p] = pair[1:2]
                    copy(bias.at[p], outs[5].at[:, pl.ds(wide, LANES)])
                    copy(own_bias.at[p], outs[6 + half].at[:, pl.ds(tall, LANES)])
            for one in copies:
                one.wait()


def unpack(half, own, first_place, token, far, block, blocks, shapes, before):
    count = blocks.shape[0]
    hidden, cond = shapes[2][0], shapes[4][0]
    return call(
        functools.partial(unpack_body, half, own, first_place, far, block, hidden, cond),
        f"unpack_{half}_{own:d}_{first_place}",
        [ANYWHERE, VMEM] + [ANYWHERE] * len(before),
        [ANYWHERE] * len(shapes) + [VMEM],
        [jax.ShapeDtypeStruct(shape, F32) for shape in shapes] + [MARK],
        scratch=[
            pltpu.VMEM((count, far * block, LANES), F32),
            pltpu.VMEM((count, 1, LANES), F32),
            pltpu.VMEM((count, 1, LANES), F32),
            pltpu.SemaphoreType.DMA((8 * count,)),
        ],
        aliases={2 + k: k for k in range(len(before))},
    )(token, blocks, *before)


def swapped(x, axis, k):
    return lax.ppermute(x, axis, [(i, i ^ k) for i in range(lax.axis_size(axis))])


def exchanged(blocks):
    return [swapped(block, "near", k + 1) for k, block in enumerate(blocks)]


def add_body(sizes, token, *refs):
    count = len(sizes)
    kept, got, outs = refs[0], refs[1:-count], refs[-count:]
    at = 0
    for out, size in zip(outs, sizes):
        for k in range(size):
            total = kept[at + k].astype(F32)
            for ref in got:
                total = total + ref[at + k].astype(F32)
            out[k] = total.astype(out.dtype)
        at += size


def added(name, token, kept, got, outs):
    sizes = [size for size, _ in outs]
    result = call(
        functools.partial(add_body, sizes),
        name,
        [ANYWHERE] + [VMEM] * (1 + len(got)),
        [VMEM] * len(outs),
        [jax.ShapeDtypeStruct((size, *kept.shape[1:]), dtype) for size, dtype in outs],
    )(token, kept, *got)
    return result


def mirror_body(token, mine, got, out):
    count = mine.shape[0]
    for k in range(count):
        out[k] = (mine[k].astype(F32) + got[count - 1 - k].astype(F32)).astype(out.dtype)


def mirrored(name, token, mine, got):
    return call(
        mirror_body,
        name,
        [ANYWHERE, VMEM, VMEM],
        VMEM,
        jax.ShapeDtypeStruct(mine.shape, BF16),
    )(token, mine, got)


def join_body(token, *refs):
    out = refs[-1]
    at = 0
    for ref in refs[:-1]:
        out[at : at + ref.shape[0]] = ref[...]
        at += ref.shape[0]


def joined(name, token, parts):
    count = sum(part.shape[0] for part in parts)
    return call(
        join_body,
        name,
        [ANYWHERE] + [VMEM] * len(parts),
        VMEM,
        jax.ShapeDtypeStruct((count, *parts[0].shape[1:]), BF16),
    )(token, *parts)


def over_outer(total):
    for bit in range((lax.axis_size("outer") - 1).bit_length()):
        total = (total.astype(F32) + swapped(total, "outer", 1 << bit).astype(F32)).astype(BF16)
    return total


def passed_along(x, by):
    peers = lax.axis_size(AXES)
    pairs = [(i, i + by) for i in range(peers) if 0 <= i + by < peers]
    return lax.ppermute(x, AXES, pairs)


def in_hbm(x):
    return pltpu.with_memory_space_constraint(x, pltpu.HBM)


def body(
    signal,
    features,
    position,
    valid,
    w_past,
    w_now,
    b_conv,
    w_cond,
    w_res,
    b_res,
    w_skip,
    b_skip,
    grad_out,
    grad_skip,
):
    rows, width = signal.shape
    features = features.T
    cond = features.shape[0]
    hidden = w_res.shape[0]
    skip_width = w_skip.shape[1]
    far = lax.axis_size("far")
    far_bits = (far - 1).bit_length()
    used = 2 * width + 2 * (hidden // HALVES) + cond + 2
    block = -(-used // (2 * far * 16)) * 16
    lines = (rows // LANES, LANES)
    pos, val = position.reshape(lines), valid.reshape(lines)
    b_conv, b_res, b_skip = (b.reshape(1, -1) for b in (b_conv, b_res, b_skip))
    shapes = [
        (width, 2 * hidden), (width, 2 * hidden), (hidden, width), (hidden, skip_width), (cond, 2 * hidden),
        (1, 2 * hidden), (1, width), (1, skip_width),
    ]

    def core_sum(half, token, theirs, mine):
        kept, *sent = added(
            f"core_sum_{half}", token, mine, [swapped(theirs, "core", 1)], [(1, F32)] + [(1, BF16)] * (NEAR - 1)
        )
        return kept[0], exchanged([x[0] for x in sent])

    def near_sum(half, token, kept, got):
        kept, sent = added(f"near_sum_{half}", token, kept, got, [(far // 2, F32), (far // 2, BF16)])
        return kept, swapped(sent, "far", 1)

    def far_sum(half, token, kept, got):
        for bit in range(1, far_bits - 1):
            size = kept.shape[0] // 2
            kept, sent = added(f"far_sum_{half}_{bit}", token, kept, [got], [(size, F32), (size, BF16)])
            got = swapped(sent, "far", 1 << bit)
        (mine,) = added(f"far_sum_{half}", token, kept, [got], [(kept.shape[0], BF16)])
        return mine, swapped(mine, "far", 1 << (far_bits - 1))

    def far_end(half, token, mine, got):
        total = over_outer(mirrored(f"far_end_{half}", token, mine, got))
        return total, swapped(total, "far", 1 << (far_bits - 2))

    def far_join(half, token, mine, got):
        total = joined(f"far_join_{half}", token, [mine, got])
        for bit in reversed(range(far_bits - 2)):
            total = joined(f"far_join_{half}_{bit}", token, [total, swapped(total, "far", 1 << bit)])
        return total, exchanged([total] * (NEAR - 1))

    def input_gradients(step, token, before):
        last = (step + 1) * ROWS == rows
        return k2b(step, token, received if last else early, grad_out, pos, dpre, w_in, w_cond, before)

    halo = passed_along(signal[rows - DILATION_STEP :], 1)
    (
        val, pos, b_conv, b_res, b_skip, features, w_cond, w_out, w_in, signal, grad_out, grad_skip,
        past_rest, gated_rest_0, kept_rest_0, dpre_rest_0,
    ) = load(
        val, pos, b_conv, b_res, b_skip, features, w_cond, w_res, w_skip, w_past, w_now, signal, grad_out, grad_skip
    )
    common = (val, signal, features, grad_out, grad_skip)
    weights = (w_in, w_cond, b_conv, w_out)
    past_head, early, head_0, head_1 = head(halo, pos, *common, *weights)
    received = passed_along(early, -1)
    theirs_0, mine_0, dpre_0, past = gradients(
        0, early, far, block, *common, (past_head, past_rest), (head_0[1], kept_rest_0), (head_0[2], dpre_rest_0)
    )
    gated_rest_1, kept_rest_1, dpre_rest_1 = forward_rest(dpre_0, past_rest, *common, *weights)
    kept_0, got_0 = core_sum(0, gated_rest_1, theirs_0, mine_0)
    theirs_1, mine_1, dpre_1, _ = gradients(
        1, kept_0, far, block, *common, (past_head, past_rest), (head_1[1], kept_rest_1), (head_1[2], dpre_rest_1)
    )
    dpre = (dpre_0, dpre_1)
    output, skip_out, mark = outputs(
        dpre_1, val, signal, (head_0[0], gated_rest_0), (head_1[0], gated_rest_1), w_out, b_res, b_skip
    )
    kept_0, got_0 = near_sum(0, mark, kept_0, got_0)
    kept_1, got_1 = core_sum(1, kept_0, theirs_1, mine_1)
    ends_0, got_0 = far_sum(0, kept_1, kept_0, got_0)
    *grads, mark = input_gradients(0, ends_0, [])
    *grads, mark = input_gradients(1, mark, grads)
    ends_0, got_0 = far_end(0, mark, ends_0, got_0)
    *grads, mark = input_gradients(2, ends_0, grads)
    kept_1, got_1 = near_sum(1, mark, kept_1, got_1)
    ends_0, got_0 = far_join(0, kept_1, ends_0, got_0)
    ends_1, got_1 = far_sum(1, ends_0, kept_1, got_1)
    blocks_0 = joined("near_join_0", ends_1, [ends_0[None]] + [x[None] for x in got_0])
    ends_1, got_1 = far_end(1, blocks_0, ends_1, got_1)
    ends_1, got_1 = far_join(1, received, ends_1, got_1)
    others_0 = swapped(blocks_0, "core", 1)
    early_1 = swapped(ends_1[None], "core", 1)
    *grads, mark = input_gradients(3, ends_1, grads)
    *done, mark = unpack(0, True, 0, mark, far, block, blocks_0, shapes, [])
    *done, mark = unpack(1, True, 0, mark, far, block, ends_1[None], shapes, done)
    blocks_1 = joined("near_join_1", mark, [x[None] for x in got_1])
    others_1 = swapped(blocks_1, "core", 1)
    *done, mark = unpack(0, False, 0, blocks_1, far, block, others_0, shapes, done)
    *done, mark = unpack(1, False, 0, mark, far, block, early_1, shapes, done)
    *done, mark = unpack(1, True, 1, mark, far, block, blocks_1, shapes, done)
    *done, mark = unpack(1, False, 1, mark, far, block, others_1, shapes, done)
    grad_signal, grad_features = grads
    g_past, g_now, g_res, g_skip, g_cond, g_bias, g_bias_res, g_bias_skip = done
    return (
        output,
        skip_out,
        grad_signal,
        grad_features.T,
        g_past,
        g_now,
        g_bias.reshape(-1),
        g_cond,
        g_res,
        g_bias_res.reshape(-1),
        g_skip,
        g_bias_skip.reshape(-1),
    )


def solution(mesh):
    row, col = mesh.shape["row"], mesh.shape["col"]
    fine = Mesh(mesh.devices.reshape(row // 2, 2, col // NEAR, NEAR), AXES)
    rows = P(AXES, None)
    line = P(AXES)
    return jax.shard_map(
        body,
        mesh=fine,
        in_specs=(rows, rows, line, line) + (P(),) * 8 + (rows, rows),
        out_specs=(rows,) * 4 + (P(),) * 8,
        check_vma=False,
    )
```

```python
import functools

import jax
import jax.numpy as jnp
from jax import lax
from jax.experimental import pallas as pl
from jax.experimental.pallas import tpu as pltpu
from jax.sharding import Mesh
from jax.sharding import PartitionSpec as P

DILATION_STEP = 256
AXES = ("outer", "core", "far", "near")
HALVES = 2
NEAR = 4
LANES = 128
ROWS = 512
ONES = 16
F32 = jnp.float32
BF16 = jnp.bfloat16
MEGA = 1 << 20
COSTS = {
    "load": 8, "head": 2, "gradients_0": 0, "forward_1": 0, "gradients_1": 4, "outputs": 4, "near_sum_0": 8,
    "far_sum_0": 8, "far_end_1": 3, "near_sum_1": 4, "near_join_0": 1, "near_join_1": 4,
}
FLOPS = 10**9


def dot(left, right):
    return jnp.dot(left, right, preferred_element_type=F32)


def across(left, right):
    return lax.dot_general(left, right, (((0,), (0,)), ((), ())), preferred_element_type=F32)


def against(left, weight):
    return lax.dot_general(left, weight, (((1,), (1,)), ((), ())), preferred_element_type=F32)


def column(lines):
    turned = lines.astype(F32).T
    return jnp.concatenate([turned[:, k : k + 1] for k in range(lines.shape[0])], axis=0)


def row(lines):
    return jnp.concatenate([lines[k : k + 1] for k in range(lines.shape[0])], axis=1)


def tap_of(lines):
    return jnp.where(lines >= DILATION_STEP, 1, 0)


def lines_of(ref, rows):
    return ref[rows.start // LANES : rows.stop // LANES, :]


def picked(head, rest, rows):
    cut = DILATION_STEP
    low = head[rows.start : min(rows.stop, cut), :] if rows.start < cut else None
    high = rest[max(rows.start, cut) - cut : rows.stop - cut, :] if rows.stop > cut else None
    if low is None:
        return high
    return low if high is None else jnp.concatenate([low, high], axis=0)


def call(kernel, name, in_specs, out_specs, out_shape, scratch=(), aliases=None, grid=(), vmem=24):
    return pl.pallas_call(
        kernel,
        grid=grid,
        in_specs=in_specs,
        out_specs=out_specs,
        out_shape=out_shape,
        scratch_shapes=list(scratch),
        input_output_aliases=aliases or {},
        cost_estimate=pl.CostEstimate(
            flops=1 + int(FLOPS * COSTS.get(name, COSTS.get(name.split("_")[0], 0))), bytes_accessed=1, transcendentals=0
        ),
        name=name,
        compiler_params=pltpu.CompilerParams(vmem_limit_bytes=vmem * MEGA),
    )


VMEM = pl.BlockSpec(memory_space=pltpu.VMEM)
ANYWHERE = pl.BlockSpec(memory_space=pl.ANY)
MARK = jax.ShapeDtypeStruct((8, LANES), F32)


def beside(*parts):
    return jnp.concatenate(parts, axis=1)


def below(*parts):
    return jnp.concatenate(parts, axis=0)


def products(half, x, feats, given, w_in, w_cond, b_conv, w_out):
    part = w_out.shape[0] // HALVES

    def pre(at):
        here = slice(at, at + part)
        return dot(x, w_in[:, here]) + across(feats, w_cond[:, here]) + b_conv[:, here]

    first = half * part
    return pre(first), pre(HALVES * part + first), against(given, w_out[first : first + part, :])


def finish(pre_a, pre_s, dgated, valid_lines):
    act = jnp.tanh(pre_a)
    gate = 0.5 + 0.5 * jnp.tanh(0.5 * pre_s)
    slope = (column(valid_lines) * dgated) * gate
    dpre = beside(slope * (1.0 - act * act), slope * act * (1.0 - gate)).astype(BF16)
    gated = (act * gate).astype(BF16)
    return gated, gated.T * row(valid_lines.astype(BF16)), dpre


def forward_tiles(half, tiles, prepare, valid, xs, x_turned, given, weights, gated_out, kept_out, dpre_out):
    cond = weights[1].shape[0]
    width = xs.shape[1] // 2

    def done(rows, *made):
        there = slice(rows.start - DILATION_STEP, rows.stop - DILATION_STEP)
        gated_out[there, :], kept_out[:, there], dpre_out[there, :] = finish(*made, lines_of(valid, rows))

    waiting = None
    for rows in tiles:
        prepare(rows)
        feats = x_turned[2 * width : 2 * width + cond, rows]
        made = products(half, xs[rows, :], feats, given[rows, :], *weights)
        if waiting:
            done(*waiting)
        waiting = (rows, *made)
    done(*waiting)


def rest_rows(rows):
    cuts = [DILATION_STEP, *range(ROWS, rows + 1, ROWS)]
    return [slice(a, b) for a, b in zip(cuts, cuts[1:])]


def load_body(
    valid, pos, b_conv, b_res, b_skip, feat, w_cond, w_res, w_skip, w_past, w_now, sig, gout, gskip,
    valid_to, pos_to, b_conv_to, b_res_to, b_skip_to, w_cond_to, w_out, w_in, xs, x_turned, given,
    gated_rest, kept_rest, dpre_rest, sems,
):
    rows_all, width = sig.shape
    skip_width = gskip.shape[1]
    cond = feat.shape[0]
    part = w_res.shape[0] // HALVES
    count = 0

    def start(source, target):
        nonlocal count
        copy = pltpu.make_async_copy(source, target, sems.at[count])
        copy.start()
        count += 1
        return copy

    def weights(half):
        copies = []
        for k, ref in enumerate((w_past, w_now)):
            for at in (half * part, (HALVES + half) * part):
                here = pl.ds(at, part)
                copies.append(start(ref.at[:, here], w_in.at[pl.ds(k * width, width), here]))
        here = pl.ds(half * part, part)
        copies.append(start(w_res.at[here], w_out.at[here, pl.ds(0, width)]))
        copies.append(start(w_skip.at[here], w_out.at[here, pl.ds(width, skip_width)]))
        return copies

    def tile(i):
        rows = pl.ds(i * ROWS, ROWS)
        return [
            start(sig.at[rows], xs.at[rows, pl.ds(width, width)]),
            start(gout.at[rows], given.at[rows, pl.ds(0, width)]),
            start(gskip.at[rows], given.at[rows, pl.ds(width, skip_width)]),
        ]

    tiles = {0: tile(0)}
    first = [
        start(valid, valid_to),
        start(pos, pos_to),
        start(b_conv, b_conv_to),
        start(w_cond, w_cond_to),
        start(feat, x_turned.at[pl.ds(2 * width, cond)]),
    ] + weights(0)
    last = []

    def prepare(rows):
        i = rows.start // ROWS
        for copy in tiles[i]:
            copy.wait()
        if i == 0:
            for copy in first:
                copy.wait()
        for k in (i + 1, i + 2):
            if k < rows_all // ROWS and k not in tiles:
                tiles[k] = tile(k)
        if i == 1:
            last.extend(weights(1) + [start(b_res, b_res_to), start(b_skip, b_skip_to)])
        whole = slice(i * ROWS, (i + 1) * ROWS)
        before = slice(rows.start - DILATION_STEP, rows.stop - DILATION_STEP)
        tap = tap_of(lines_of(pos_to, rows)).astype(F32)
        x_turned[width : 2 * width, whole] = xs[whole, width:].T
        x_turned[:width, rows] = x_turned[width : 2 * width, before] * row(tap).astype(BF16)
        xs[rows, :width] = xs[before, width:] * column(tap).astype(BF16)

    x_turned[2 * width + cond :, :] = jnp.ones((x_turned.shape[0] - 2 * width - cond, rows_all), BF16)
    forward_tiles(
        0, rest_rows(rows_all), prepare, valid_to, xs, x_turned, given, (w_in, w_cond_to, b_conv_to, w_out),
        gated_rest, kept_rest, dpre_rest,
    )
    for copy in last:
        copy.wait()


def rest_shapes(rest, part):
    return [jax.ShapeDtypeStruct(shape, BF16) for shape in ((rest, part), (part, rest), (rest, 2 * part))]


def load(*arrays):
    sources = [in_hbm(x) for x in arrays]
    feat, w_cond, w_res, w_skip, w_past, w_now, sig, gout, gskip = arrays[5:]
    rows, width = sig.shape
    hidden = w_res.shape[0]
    wide = gout.shape[1] + gskip.shape[1]
    shapes = [jax.ShapeDtypeStruct(x.shape, x.dtype) for x in arrays[:5] + (w_cond,)] + [
        jax.ShapeDtypeStruct(shape, BF16)
        for shape in (
            (hidden, wide), (2 * width, 2 * hidden), (rows, 2 * width), (2 * width + feat.shape[0] + ONES, rows), (rows, wide),
        )
    ]
    shapes += rest_shapes(rows - DILATION_STEP, hidden // HALVES)
    return call(
        load_body,
        "load",
        [ANYWHERE] * len(sources),
        [VMEM] * len(shapes),
        shapes,
        scratch=[pltpu.SemaphoreType.DMA((7 + 6 * HALVES + 3 * (rows // ROWS),))],
    )(*sources)


def side_by_side(dpre_0, dpre_1):
    part = dpre_0.shape[1] // 2
    return beside(dpre_0[:, :part], dpre_1[:, :part], dpre_0[:, part:], dpre_1[:, part:])


def head_body(halo, pos, valid, xs, x_turned, given, w_in, w_cond, b_conv, w_out, past_out, early, *outs):
    rows = slice(0, DILATION_STEP)
    width = halo.shape[1]
    cond = w_cond.shape[0]
    tap = tap_of(lines_of(pos, rows)).astype(F32)
    past_out[...] = halo[...].T * row(tap).astype(BF16)
    x = beside(halo[...] * column(tap).astype(BF16), xs[rows, width:])
    feats = x_turned[2 * width : 2 * width + cond, rows]
    dpres = []
    made = [products(half, x, feats, given[rows, :], w_in, w_cond, b_conv, w_out) for half in range(HALVES)]
    for half in range(HALVES):
        parts = finish(*made[half], lines_of(valid, rows))
        for ref, value in zip(outs[3 * half :], parts):
            ref[...] = value
        dpres.append(parts[2])
    early[...] = (column(tap) * against(side_by_side(*dpres), w_in[:width, :])).astype(BF16)


def head(halo, *args):
    width = halo.shape[1]
    part = args[-1].shape[0] // HALVES
    shapes = [jax.ShapeDtypeStruct(shape, BF16) for shape in ((width, DILATION_STEP), (DILATION_STEP, width))]
    past, early, *parts = call(
        head_body,
        "head",
        [VMEM] * (1 + len(args)),
        [VMEM] * (2 + 3 * HALVES),
        shapes + rest_shapes(DILATION_STEP, part) * HALVES,
    )(halo, *args)
    return past, early, parts[:3], parts[3:]


def forward_body(token, valid, xs, x_turned, given, w_in, w_cond, b_conv, w_out, gated_out, kept_out, dpre_out):
    forward_tiles(
        1, rest_rows(xs.shape[0]), lambda rows: None, valid, xs, x_turned, given, (w_in, w_cond, b_conv, w_out),
        gated_out, kept_out, dpre_out,
    )


def forward_rest(token, *args):
    return call(
        forward_body,
        "forward_1",
        [ANYWHERE] + [VMEM] * len(args),
        [VMEM] * 3,
        rest_shapes(args[0].shape[0] * LANES - DILATION_STEP, args[-1].shape[0] // HALVES),
    )(token, *args)


def own_place():
    return [lax.axis_index(name) for name in ("core", "far", "near")]


def turned(index, count):
    bits = (count - 1).bit_length()
    result = 0
    for bit in range(bits):
        result = result | (((index >> bit) & 1) << (bits - 1 - bit))
    return result


def place_blocks(far, block, acc, theirs, mine):
    core, z, xy = own_place()
    for r in range(far):
        for c in range(NEAR):
            here = pl.ds(c * LANES, LANES)
            for k, out in ((1 - core, theirs), (core, mine)):
                rows = pl.ds(pl.multiple_of((k * far + r) * block, 16), block)
                out[c ^ xy, turned(r ^ z, far)] = acc[rows, here].astype(out.dtype)


def gradients_body(
    far, block, half, token, other, valid, x_turned, given, past_head, kept_head, kept_rest, dpre_head, dpre_rest,
    theirs, mine, acc,
):
    cut = DILATION_STEP
    width = past_head.shape[0]
    part = kept_head.shape[0]
    wide = dpre_rest.shape[1]
    mask = jnp.broadcast_to(row(valid[...].astype(F32)).astype(BF16), (ONES, valid.shape[0] * LANES))
    ends = x_turned.shape[0]
    outer = dot(below(kept_rest[...], mask[:, cut:]), given[cut:, :])
    outer += dot(below(kept_head[...], mask[:, :cut]), given[:cut, :])
    at = ends
    for k in range(2):
        acc[at : at + part, :] = outer[:part, k * width : (k + 1) * width]
        at += part
    acc[at : at + ONES, :] = outer[part:, half * width : (half + 1) * width]
    at += ONES
    acc[at:, :] = jnp.zeros((acc.shape[0] - at, wide), F32)
    inner = dot(x_turned[:, cut:], dpre_rest[...])
    inner += dot(below(past_head[...], x_turned[width:, :cut]), dpre_head[...])
    acc[:ends, :] = inner
    place_blocks(far, block, acc, theirs, mine)


def gradients(half, token, other, far, block, valid, x_turned, given, past_head, head_parts, rest_parts):
    packed = (NEAR, far, block, LANES)
    wide = rest_parts[2].shape[1]
    return call(
        functools.partial(gradients_body, far, block, half),
        f"gradients_{half}",
        [ANYWHERE] * 2 + [VMEM] * 8,
        [VMEM] * 2,
        [jax.ShapeDtypeStruct(packed, BF16), jax.ShapeDtypeStruct(packed, F32)],
        scratch=[pltpu.VMEM((2 * far * block, wide), F32)],
    )(token, other, valid, x_turned, given, past_head, head_parts[1], rest_parts[1], head_parts[2], rest_parts[2])


def outputs_body(token, valid, xs, head_0, rest_0, head_1, rest_1, w_out, b_res, b_skip, out, skip, mark, rooms, sems):
    width = xs.shape[1] // 2
    copies = []
    for i in range(xs.shape[0] // ROWS):
        rows = slice(i * ROWS, (i + 1) * ROWS)
        mask = column(lines_of(valid, rows))
        gated = beside(picked(head_0, rest_0, rows), picked(head_1, rest_1, rows))
        branch = dot(gated, w_out[:, :width]) + b_res[...]
        rooms[i, 0] = (xs[rows, width:].astype(F32) + mask * branch).astype(BF16)
        side = dot(gated, w_out[:, width:]) + b_skip[...]
        rooms[i, 1] = (mask * side).astype(BF16)
        for k, ref in enumerate((out, skip)):
            copies.append(pltpu.make_async_copy(rooms.at[i, k], ref.at[pl.ds(i * ROWS, ROWS)], sems.at[i, k]))
            copies[-1].start()
    mark[...] = jnp.zeros_like(mark)
    for copy in copies:
        copy.wait()


def outputs(token, valid, xs, gated_0, gated_1, w_out, b_res, b_skip):
    rows, width = xs.shape[0], xs.shape[1] // 2
    return call(
        outputs_body,
        "outputs",
        [ANYWHERE] + [VMEM] * 9,
        [ANYWHERE, ANYWHERE, VMEM],
        [
            jax.ShapeDtypeStruct((rows, width), BF16),
            jax.ShapeDtypeStruct((rows, w_out.shape[1] - width), BF16),
            MARK,
        ],
        scratch=[
            pltpu.VMEM((rows // ROWS, 2, ROWS, width), BF16),
            pltpu.SemaphoreType.DMA((rows // ROWS, 2)),
        ],
    )(token, valid, xs, *gated_0, *gated_1, w_out, b_res, b_skip)


def inputs_body(steps, token, received, given, pos, head_0, rest_0, head_1, rest_1, w_in, w_cond, *refs):
    gsig, gfeat, mark, room, room_feat, sems = refs[-6:]
    rows, width = given.shape[0], w_in.shape[0] // 2
    copies = []
    wide = 2 * LANES

    def copy(source, target):
        copies.append(pltpu.make_async_copy(source, target, sems.at[len(copies)]))
        copies[-1].start()

    for i, step in enumerate(steps):
        begin = step * ROWS
        here = slice(begin, begin + ROWS)
        after = slice(begin + DILATION_STEP, min(begin + DILATION_STEP + ROWS, rows))
        now = side_by_side(picked(head_0, rest_0, here), picked(head_1, rest_1, here))
        later = side_by_side(picked(head_0, rest_0, after), picked(head_1, rest_1, after))
        tap = column(tap_of(lines_of(pos, after)))
        room_feat[i] = against(w_cond[...], now)
        copy(room_feat.at[i], gfeat.at[:, pl.ds(begin, ROWS)])
        for k in range(width // wide):
            some = slice(k * wide, (k + 1) * wide)
            tail = tap * against(later, w_in[some, :])
            if tail.shape[0] < ROWS:
                tail = below(tail, received[:, some].astype(F32))
            room[i, k] = given[here, some].astype(F32) + against(now, w_in[width + k * wide : width + (k + 1) * wide, :]) + tail
            copy(room.at[i, k], gsig.at[pl.ds(begin, ROWS), pl.ds(k * wide, wide)])
    mark[...] = jnp.zeros_like(mark)
    for one in copies:
        one.wait()


def inputs(steps, token, received, given, pos, dpre_0, dpre_1, w_in, w_cond, before):
    rows, width = given.shape[0], w_in.shape[0] // 2
    cond = w_cond.shape[0]
    count = width // (2 * LANES)
    return call(
        functools.partial(inputs_body, steps),
        f"inputs_{steps[0]}",
        [ANYWHERE] + [VMEM] * 9 + [ANYWHERE] * len(before),
        [ANYWHERE, ANYWHERE, VMEM],
        [
            jax.ShapeDtypeStruct((rows, width), F32),
            jax.ShapeDtypeStruct((cond, rows), F32),
            MARK,
        ],
        scratch=[
            pltpu.VMEM((len(steps), count, ROWS, 2 * LANES), F32),
            pltpu.VMEM((len(steps), cond, ROWS), F32),
            pltpu.SemaphoreType.DMA((len(steps) * (count + 1),)),
        ],
        aliases={10 + k: k for k in range(len(before))},
    )(token, received, given, pos, *dpre_0, *dpre_1, w_in, w_cond, *before)


def unpack_body(far, block, token, mine, theirs, *refs):
    arrays, (mark, room) = refs[-9:-2], refs[-2:]
    mark[...] = jnp.zeros_like(mark)
    core, z, xy = own_place()

    @pl.when(pl.program_id(0) == 0)
    def _():
        for k, ref in ((core, mine), (1 - core, theirs)):
            for c in range(NEAR):
                for r in range(far):
                    rows = pl.ds(pl.multiple_of((k * far + (r ^ z)) * block, 16), block)
                    room[c ^ xy, rows, :] = ref[c, turned(r, far)]

    for j in range(NEAR // 2):
        c = pl.program_id(0) * (NEAR // 2) + j
        here = pl.ds(j * LANES, LANES)
        top = 0
        for ref in arrays:
            count = ref.shape[0]
            size = max(count, ONES)
            ref[:, here] = room[c, top : top + size, :].astype(F32)[:count]
            top += size


def unpack(half, token, far, block, mine, theirs, width, cond, hidden, skip_width, before):
    part = hidden // HALVES
    gates = 2 * hidden
    own = (width, skip_width)[half]

    def wide(size):
        return pl.BlockSpec((size, part), lambda s: (0, HALVES * s + half))

    def tall(size):
        return pl.BlockSpec((part, size // 2), lambda s: (half, s))

    specs = [wide(width), wide(width), wide(cond), wide(1), tall(width), tall(skip_width), pl.BlockSpec((1, own // 2), lambda s: (0, s))]
    shapes = [(width, gates), (width, gates), (cond, gates), (1, gates), (hidden, width), (hidden, skip_width), (1, own)]
    packed = (NEAR, far, block, LANES)
    blocks = pl.BlockSpec(packed, lambda s: (0,) * len(packed))
    return call(
        functools.partial(unpack_body, far, block),
        f"unpack_{half}",
        [ANYWHERE, blocks, blocks] + [ANYWHERE] * len(before),
        specs + [pl.BlockSpec(MARK.shape, lambda s: (0, 0))],
        [jax.ShapeDtypeStruct(shape, F32) for shape in shapes] + [MARK],
        scratch=[pltpu.VMEM((NEAR, 2 * far * block, LANES), BF16)],
        aliases={3 + k: k for k in range(len(before))},
        grid=(2,),
    )(token, mine, theirs, *before)


def swapped(x, axis, k):
    return lax.ppermute(x, axis, [(i, i ^ k) for i in range(lax.axis_size(axis))])


def exchanged(blocks):
    return [swapped(block, "near", k + 1) for k, block in enumerate(blocks)]


def add_body(sizes, token, *refs):
    count = len(sizes)
    kept, got, outs = refs[0], refs[1:-count], refs[-count:]
    at = 0
    for out, size in zip(outs, sizes):
        for k in range(size):
            total = kept[at + k].astype(F32)
            for ref in got:
                total = total + ref[at + k].astype(F32)
            out[k] = total.astype(out.dtype)
        at += size


def added(name, token, kept, got, outs):
    sizes = [size for size, _ in outs]
    result = call(
        functools.partial(add_body, sizes),
        name,
        [ANYWHERE] + [VMEM] * (1 + len(got)),
        [VMEM] * len(outs),
        [jax.ShapeDtypeStruct((size, *kept.shape[1:]), dtype) for size, dtype in outs],
    )(token, kept, *got)
    return result


def mirror_body(token, mine, got, out):
    count = mine.shape[0]
    for k in range(count):
        out[k] = (mine[k].astype(F32) + got[count - 1 - k].astype(F32)).astype(out.dtype)


def mirrored(name, token, mine, got):
    return call(
        mirror_body,
        name,
        [ANYWHERE, VMEM, VMEM],
        VMEM,
        jax.ShapeDtypeStruct(mine.shape, BF16),
    )(token, mine, got)


def join_body(token, *refs):
    out = refs[-1]
    at = 0
    for ref in refs[:-1]:
        out[at : at + ref.shape[0]] = ref[...]
        at += ref.shape[0]


def joined(name, token, parts):
    count = sum(part.shape[0] for part in parts)
    return call(
        join_body,
        name,
        [ANYWHERE] + [VMEM] * len(parts),
        VMEM,
        jax.ShapeDtypeStruct((count, *parts[0].shape[1:]), BF16),
    )(token, *parts)


def over_outer(total):
    for bit in range((lax.axis_size("outer") - 1).bit_length()):
        total = (total.astype(F32) + swapped(total, "outer", 1 << bit).astype(F32)).astype(BF16)
    return total


def passed_along(x, by):
    peers = lax.axis_size(AXES)
    pairs = [(i, i + by) for i in range(peers) if 0 <= i + by < peers]
    return lax.ppermute(x, AXES, pairs)


def in_hbm(x):
    return pltpu.with_memory_space_constraint(x, pltpu.HBM)


def body(
    signal,
    features,
    position,
    valid,
    w_past,
    w_now,
    b_conv,
    w_cond,
    w_res,
    b_res,
    w_skip,
    b_skip,
    grad_out,
    grad_skip,
):
    rows, width = signal.shape
    features = features.T
    cond = features.shape[0]
    hidden = w_res.shape[0]
    skip_width = w_skip.shape[1]
    far = lax.axis_size("far")
    far_bits = (far - 1).bit_length()
    used = 2 * width + cond + ONES + 2 * (hidden // HALVES) + ONES
    block = -(-used // (2 * far * 16)) * 16
    lines = (rows // LANES, LANES)
    pos, val = position.reshape(lines), valid.reshape(lines)
    b_conv, b_res, b_skip = (b.reshape(1, -1) for b in (b_conv, b_res, b_skip))

    def core_sum(half, token, theirs, mine):
        kept, *sent = added(
            f"core_sum_{half}", token, mine, [swapped(theirs, "core", 1)], [(1, F32)] + [(1, BF16)] * (NEAR - 1)
        )
        return kept[0], exchanged([x[0] for x in sent])

    def near_sum(half, token, kept, got):
        kept, sent = added(f"near_sum_{half}", token, kept, got, [(far // 2, F32), (far // 2, BF16)])
        return kept, swapped(sent, "far", 1)

    def far_sum(half, token, kept, got):
        for bit in range(1, far_bits - 1):
            size = kept.shape[0] // 2
            kept, sent = added(f"far_sum_{half}_{bit}", token, kept, [got], [(size, F32), (size, BF16)])
            got = swapped(sent, "far", 1 << bit)
        (mine,) = added(f"far_sum_{half}", token, kept, [got], [(kept.shape[0], BF16)])
        return mine, swapped(mine, "far", 1 << (far_bits - 1))

    def far_end(half, token, mine, got):
        total = over_outer(mirrored(f"far_end_{half}", token, mine, got))
        return total, swapped(total, "far", 1 << (far_bits - 2))

    def far_join(half, token, mine, got):
        total = joined(f"far_join_{half}", token, [mine, got])
        for bit in reversed(range(far_bits - 2)):
            total = joined(f"far_join_{half}_{bit}", token, [total, swapped(total, "far", 1 << bit)])
        return total, exchanged([total] * (NEAR - 1))

    def near_join(half, token, mine, got):
        total = joined(f"near_join_{half}", token, [mine[None]] + [x[None] for x in got])
        return total, swapped(total, "core", 1)

    def input_gradients(steps, token, before):
        last = (steps[-1] + 1) * ROWS == rows
        return inputs(steps, token, received if last else early, given, pos, dpre_0, dpre_1, w_in, w_cond, before)

    halo = passed_along(signal[rows - DILATION_STEP :], 1)
    val, pos, b_conv, b_res, b_skip, w_cond, w_out, w_in, xs, x_turned, given, *rest_0 = load(
        val, pos, b_conv, b_res, b_skip, features, w_cond, w_res, w_skip, w_past, w_now, signal, grad_out, grad_skip
    )
    common = (val, xs, x_turned, given, w_in, w_cond, b_conv, w_out)
    past_head, early, head_0, head_1 = head(halo, pos, *common)
    received = passed_along(early, -1)
    theirs_0, mine_0 = gradients(0, early, early, far, block, val, x_turned, given, past_head, head_0, rest_0)
    rest_1 = forward_rest(theirs_0, *common)
    dpre_0, dpre_1 = (head_0[2], rest_0[2]), (head_1[2], rest_1[2])
    kept_0, got_0 = core_sum(0, rest_1[0], theirs_0, mine_0)
    theirs_1, mine_1 = gradients(1, kept_0, received, far, block, val, x_turned, given, past_head, head_1, rest_1)
    output, skip_out, mark = outputs(
        theirs_1, val, xs, (head_0[0], rest_0[0]), (head_1[0], rest_1[0]), w_out, b_res, b_skip
    )
    kept_0, got_0 = near_sum(0, mark, kept_0, got_0)
    kept_1, got_1 = core_sum(1, kept_0, theirs_1, mine_1)
    ends_0, got_0 = far_sum(0, kept_1, kept_0, got_0)
    *grads, mark = input_gradients((0, 1), ends_0, [])
    ends_0, got_0 = far_end(0, mark, ends_0, got_0)
    kept_1, got_1 = near_sum(1, ends_0, kept_1, got_1)
    ends_0, got_0 = far_join(0, kept_1, ends_0, got_0)
    *grads, mark = input_gradients((2,), ends_0, grads)
    ends_1, got_1 = far_sum(1, mark, kept_1, got_1)
    *grads, mark = input_gradients((3,), ends_1, grads)
    blocks_0, others_0 = near_join(0, mark, ends_0, got_0)
    ends_1, got_1 = far_end(1, blocks_0, ends_1, got_1)
    ends_1, got_1 = far_join(1, ends_1, ends_1, got_1)
    blocks_1, others_1 = near_join(1, ends_1, ends_1, got_1)
    *done, own_0, mark = unpack(0, blocks_1, far, block, blocks_0, others_0, width, cond, hidden, skip_width, [])
    *done, own_1, _ = unpack(1, mark, far, block, blocks_1, others_1, width, cond, hidden, skip_width, done)
    g_past, g_now, g_cond, g_bias, g_res, g_skip = done
    grad_signal, grad_features = grads
    return (
        output,
        skip_out,
        grad_signal,
        grad_features.T,
        g_past,
        g_now,
        g_bias.reshape(-1),
        g_cond,
        g_res,
        own_0.reshape(-1),
        g_skip,
        own_1.reshape(-1),
    )


def solution(mesh):
    row, col = mesh.shape["row"], mesh.shape["col"]
    fine = Mesh(mesh.devices.reshape(row // 2, 2, col // NEAR, NEAR), AXES)
    rows = P(AXES, None)
    line = P(AXES)
    return jax.shard_map(
        body,
        mesh=fine,
        in_specs=(rows, rows, line, line) + (P(),) * 8 + (rows, rows),
        out_specs=(rows,) * 4 + (P(),) * 8,
        check_vma=False,
    )
```

```python
import functools

import jax
import jax.numpy as jnp
from jax import lax
from jax.experimental import pallas as pl
from jax.experimental.pallas import tpu as pltpu
from jax.sharding import Mesh
from jax.sharding import PartitionSpec as P

DILATION_STEP = 256
AXES = ("outer", "core", "far", "near")
HALVES = 2
NEAR = 4
LANES = 128
ROWS = 512
ONES = 16
F32 = jnp.float32
BF16 = jnp.bfloat16
MEGA = 1 << 20
COSTS = {
    "load": 8, "head": 2, "gradients_0": 0, "forward_1": 0, "gradients_1": 4, "outputs": 4, "near_sum_0": 8,
    "far_end_1": 3, "inputs": 1, "near_sum_1": 4, "near_join_0": 1, "near_join_1": 4,
}
FLOPS = 10**9


def dot(left, right):
    return jnp.dot(left, right, preferred_element_type=F32)


def across(left, right):
    return lax.dot_general(left, right, (((0,), (0,)), ((), ())), preferred_element_type=F32)


def against(left, weight):
    return lax.dot_general(left, weight, (((1,), (1,)), ((), ())), preferred_element_type=F32)


def column(lines):
    turned = lines.astype(F32).T
    return jnp.concatenate([turned[:, k : k + 1] for k in range(lines.shape[0])], axis=0)


def row(lines):
    return jnp.concatenate([lines[k : k + 1] for k in range(lines.shape[0])], axis=1)


def tap_of(lines):
    return jnp.where(lines >= DILATION_STEP, 1, 0)


def lines_of(ref, rows):
    return ref[rows.start // LANES : rows.stop // LANES, :]


def picked(head, rest, rows):
    cut = DILATION_STEP
    low = head[rows.start : min(rows.stop, cut), :] if rows.start < cut else None
    high = rest[max(rows.start, cut) - cut : rows.stop - cut, :] if rows.stop > cut else None
    if low is None:
        return high
    return low if high is None else jnp.concatenate([low, high], axis=0)


def call(kernel, name, in_specs, out_specs, out_shape, scratch=(), aliases=None, grid=(), vmem=24):
    return pl.pallas_call(
        kernel,
        grid=grid,
        in_specs=in_specs,
        out_specs=out_specs,
        out_shape=out_shape,
        scratch_shapes=list(scratch),
        input_output_aliases=aliases or {},
        cost_estimate=pl.CostEstimate(
            flops=1 + int(FLOPS * COSTS.get(name, COSTS.get(name.split("_")[0], 0))), bytes_accessed=1, transcendentals=0
        ),
        name=name,
        compiler_params=pltpu.CompilerParams(vmem_limit_bytes=vmem * MEGA),
    )


VMEM = pl.BlockSpec(memory_space=pltpu.VMEM)
ANYWHERE = pl.BlockSpec(memory_space=pl.ANY)
MARK = jax.ShapeDtypeStruct((8, LANES), F32)


def beside(*parts):
    return jnp.concatenate(parts, axis=1)


def below(*parts):
    return jnp.concatenate(parts, axis=0)


def products(half, rows, x, feats, given, w_in, w_cond, b_conv, w_out, arrive=None):
    part = w_out.shape[0] // HALVES
    first = half * part
    made = []
    for k, at in enumerate((first, HALVES * part + first)):
        here = slice(at, at + part)
        if arrive:
            arrive(rows, k)
        made.append(dot(x, w_in[:, here]) + across(feats, w_cond[:, here]) + b_conv[:, here])
    if arrive:
        arrive(rows, 2)
    return *made, against(given[rows, :], w_out[first : first + part, :])


def finish(pre_a, pre_s, dgated, valid_lines):
    act = jnp.tanh(pre_a)
    gate = 0.5 + 0.5 * jnp.tanh(0.5 * pre_s)
    slope = (column(valid_lines) * dgated) * gate
    dpre = beside(slope * (1.0 - act * act), slope * act * (1.0 - gate)).astype(BF16)
    gated = (act * gate).astype(BF16)
    return gated, gated.T * row(valid_lines.astype(BF16)), dpre


def forward_tiles(half, tiles, prepare, arrive, valid, xs, x_turned, given, weights, gated_out, kept_out, dpre_out):
    cond = weights[1].shape[0]
    width = xs.shape[1] // 2

    def done(rows, *made):
        there = slice(rows.start - DILATION_STEP, rows.stop - DILATION_STEP)
        gated_out[there, :], kept_out[:, there], dpre_out[there, :] = finish(*made, lines_of(valid, rows))

    waiting = None
    for rows in tiles:
        if prepare:
            prepare(rows)
        feats = x_turned[2 * width : 2 * width + cond, rows]
        made = products(half, rows, xs[rows, :], feats, given, *weights, arrive=arrive)
        if waiting:
            done(*waiting)
        waiting = (rows, *made)
    done(*waiting)


def rest_rows(rows):
    cuts = [DILATION_STEP, *range(ROWS, rows + 1, ROWS)]
    return [slice(a, b) for a, b in zip(cuts, cuts[1:])]


def load_body(
    valid, pos, b_conv, b_res, b_skip, feat, w_cond, w_res, w_skip, w_past, w_now, sig, gout, gskip,
    valid_to, pos_to, b_conv_to, b_res_to, b_skip_to, w_cond_to, w_out, w_in, xs, x_turned, given,
    gated_rest, kept_rest, dpre_rest, sems,
):
    rows_all, width = sig.shape
    skip_width = gskip.shape[1]
    cond = feat.shape[0]
    part = w_res.shape[0] // HALVES
    count = 0

    def start(source, target):
        nonlocal count
        copy = pltpu.make_async_copy(source, target, sems.at[count])
        copy.start()
        count += 1
        return copy

    def inner(half, at):
        here = pl.ds(at + half * part, part)
        return [start(ref.at[:, here], w_in.at[pl.ds(k * width, width), here]) for k, ref in enumerate((w_past, w_now))]

    def outer(half):
        here = pl.ds(half * part, part)
        return [
            start(w_res.at[here], w_out.at[here, pl.ds(0, width)]),
            start(w_skip.at[here], w_out.at[here, pl.ds(width, skip_width)]),
        ]

    def signals(i):
        rows = pl.ds(i * ROWS, ROWS)
        return [start(sig.at[rows], xs.at[rows, pl.ds(width, width)])]

    def cotangents(i):
        rows = pl.ds(i * ROWS, ROWS)
        return [
            start(gout.at[rows], given.at[rows, pl.ds(0, width)]),
            start(gskip.at[rows], given.at[rows, pl.ds(width, skip_width)]),
        ]

    here = {0: signals(0)}
    needs = [
        [start(pos, pos_to)] + inner(0, 0) + [
            start(feat, x_turned.at[pl.ds(2 * width, cond)]), start(w_cond, w_cond_to), start(b_conv, b_conv_to)
        ],
        inner(0, HALVES * part),
        [start(valid, valid_to)] + outer(0),
    ]
    given_here = {0: cotangents(0)}
    last = []

    def wait(copies):
        for copy in copies:
            copy.wait()
        copies.clear()

    def prepare(rows):
        i = rows.start // ROWS
        wait(here[i])
        if i == 0:
            wait(needs[0])
        for k in (i + 1, i + 2):
            if k < rows_all // ROWS and k not in here:
                here[k] = signals(k)
                given_here[k] = cotangents(k)
        if i == 1:
            for at in (0, HALVES * part):
                last.extend(inner(1, at))
            last.extend(outer(1) + [start(b_res, b_res_to), start(b_skip, b_skip_to)])
        whole = slice(i * ROWS, (i + 1) * ROWS)
        before = slice(rows.start - DILATION_STEP, rows.stop - DILATION_STEP)
        tap = tap_of(lines_of(pos_to, rows)).astype(F32)
        xs[rows, :width] = xs[before, width:] * column(tap).astype(BF16)
        x_turned[width : 2 * width, whole] = xs[whole, width:].T
        x_turned[:width, rows] = x_turned[width : 2 * width, before] * row(tap).astype(BF16)

    def arrive(rows, k):
        wait(needs[k])
        if k == 2:
            wait(given_here[rows.start // ROWS])

    x_turned[2 * width + cond :, :] = jnp.ones((x_turned.shape[0] - 2 * width - cond, rows_all), BF16)
    forward_tiles(
        0, rest_rows(rows_all), prepare, arrive, valid_to, xs, x_turned, given, (w_in, w_cond_to, b_conv_to, w_out),
        gated_rest, kept_rest, dpre_rest,
    )
    wait(last)


def rest_shapes(rest, part):
    return [jax.ShapeDtypeStruct(shape, BF16) for shape in ((rest, part), (part, rest), (rest, 2 * part))]


def load(*arrays):
    sources = [in_hbm(x) for x in arrays]
    feat, w_cond, w_res, w_skip, w_past, w_now, sig, gout, gskip = arrays[5:]
    rows, width = sig.shape
    hidden = w_res.shape[0]
    wide = gout.shape[1] + gskip.shape[1]
    shapes = [jax.ShapeDtypeStruct(x.shape, x.dtype) for x in arrays[:5] + (w_cond,)] + [
        jax.ShapeDtypeStruct(shape, BF16)
        for shape in (
            (hidden, wide), (2 * width, 2 * hidden), (rows, 2 * width), (2 * width + feat.shape[0] + ONES, rows), (rows, wide),
        )
    ]
    shapes += rest_shapes(rows - DILATION_STEP, hidden // HALVES)
    return call(
        load_body,
        "load",
        [ANYWHERE] * len(sources),
        [VMEM] * len(shapes),
        shapes,
        scratch=[pltpu.SemaphoreType.DMA((7 + 6 * HALVES + 3 * (rows // ROWS),))],
    )(*sources)


def side_by_side(dpre_0, dpre_1):
    part = dpre_0.shape[1] // 2
    return beside(dpre_0[:, :part], dpre_1[:, :part], dpre_0[:, part:], dpre_1[:, part:])


def head_body(halo, pos, valid, xs, x_turned, given, w_in, w_cond, b_conv, w_out, past_out, early, *outs):
    rows = slice(0, DILATION_STEP)
    width = halo.shape[1]
    cond = w_cond.shape[0]
    tap = tap_of(lines_of(pos, rows)).astype(F32)
    past_out[...] = halo[...].T * row(tap).astype(BF16)
    x = beside(halo[...] * column(tap).astype(BF16), xs[rows, width:])
    feats = x_turned[2 * width : 2 * width + cond, rows]
    dpres = []
    made = [products(half, rows, x, feats, given, w_in, w_cond, b_conv, w_out) for half in range(HALVES)]
    for half in range(HALVES):
        parts = finish(*made[half], lines_of(valid, rows))
        for ref, value in zip(outs[3 * half :], parts):
            ref[...] = value
        dpres.append(parts[2])
    early[...] = (column(tap) * against(side_by_side(*dpres), w_in[:width, :])).astype(BF16)


def head(halo, *args):
    width = halo.shape[1]
    part = args[-1].shape[0] // HALVES
    shapes = [jax.ShapeDtypeStruct(shape, BF16) for shape in ((width, DILATION_STEP), (DILATION_STEP, width))]
    past, early, *parts = call(
        head_body,
        "head",
        [VMEM] * (1 + len(args)),
        [VMEM] * (2 + 3 * HALVES),
        shapes + rest_shapes(DILATION_STEP, part) * HALVES,
    )(halo, *args)
    return past, early, parts[:3], parts[3:]


def forward_body(token, valid, xs, x_turned, given, w_in, w_cond, b_conv, w_out, gated_out, kept_out, dpre_out):
    forward_tiles(
        1, rest_rows(xs.shape[0]), None, None, valid, xs, x_turned, given, (w_in, w_cond, b_conv, w_out),
        gated_out, kept_out, dpre_out,
    )


def forward_rest(token, *args):
    return call(
        forward_body,
        "forward_1",
        [ANYWHERE] + [VMEM] * len(args),
        [VMEM] * 3,
        rest_shapes(args[0].shape[0] * LANES - DILATION_STEP, args[-1].shape[0] // HALVES),
    )(token, *args)


def own_place():
    return [lax.axis_index(name) for name in ("core", "far", "near")]


def turned(index, count):
    bits = (count - 1).bit_length()
    result = 0
    for bit in range(bits):
        result = result | (((index >> bit) & 1) << (bits - 1 - bit))
    return result


def place_blocks(far, block, acc, theirs, mine):
    core, z, xy = own_place()
    for r in range(far):
        for c in range(NEAR):
            here = pl.ds(c * LANES, LANES)
            for k, out in ((1 - core, theirs), (core, mine)):
                rows = pl.ds(pl.multiple_of((k * far + r) * block, 16), block)
                out[c ^ xy, turned(r ^ z, far)] = acc[rows, here].astype(out.dtype)


def gradients_body(
    far, block, half, token, other, valid, x_turned, given, past_head, kept_head, kept_rest, dpre_head, dpre_rest,
    theirs, mine, acc,
):
    cut = DILATION_STEP
    width = past_head.shape[0]
    part = kept_head.shape[0]
    wide = dpre_rest.shape[1]
    mask = jnp.broadcast_to(row(valid[...].astype(F32)).astype(BF16), (ONES, valid.shape[0] * LANES))
    ends = x_turned.shape[0]
    outer = dot(below(kept_rest[...], mask[:, cut:]), given[cut:, :])
    outer += dot(below(kept_head[...], mask[:, :cut]), given[:cut, :])
    at = ends
    for k in range(2):
        acc[at : at + part, :] = outer[:part, k * width : (k + 1) * width]
        at += part
    acc[at : at + ONES, :] = outer[part:, half * width : (half + 1) * width]
    at += ONES
    acc[at:, :] = jnp.zeros((acc.shape[0] - at, wide), F32)
    inner = dot(x_turned[:, cut:], dpre_rest[...])
    inner += dot(below(past_head[...], x_turned[width:, :cut]), dpre_head[...])
    acc[:ends, :] = inner
    place_blocks(far, block, acc, theirs, mine)


def gradients(half, token, other, far, block, valid, x_turned, given, past_head, head_parts, rest_parts):
    packed = (NEAR, far, block, LANES)
    wide = rest_parts[2].shape[1]
    return call(
        functools.partial(gradients_body, far, block, half),
        f"gradients_{half}",
        [ANYWHERE] * 2 + [VMEM] * 8,
        [VMEM] * 2,
        [jax.ShapeDtypeStruct(packed, BF16), jax.ShapeDtypeStruct(packed, F32)],
        scratch=[pltpu.VMEM((2 * far * block, wide), F32)],
    )(token, other, valid, x_turned, given, past_head, head_parts[1], rest_parts[1], head_parts[2], rest_parts[2])


def outputs_body(token, valid, xs, head_0, rest_0, head_1, rest_1, w_out, b_res, b_skip, out, skip, mark, rooms, sems):
    width = xs.shape[1] // 2
    copies = []
    for i in range(xs.shape[0] // ROWS):
        rows = slice(i * ROWS, (i + 1) * ROWS)
        mask = column(lines_of(valid, rows))
        gated = beside(picked(head_0, rest_0, rows), picked(head_1, rest_1, rows))
        branch = dot(gated, w_out[:, :width]) + b_res[...]
        rooms[i, 0] = (xs[rows, width:].astype(F32) + mask * branch).astype(BF16)
        side = dot(gated, w_out[:, width:]) + b_skip[...]
        rooms[i, 1] = (mask * side).astype(BF16)
        for k, ref in enumerate((out, skip)):
            copies.append(pltpu.make_async_copy(rooms.at[i, k], ref.at[pl.ds(i * ROWS, ROWS)], sems.at[i, k]))
            copies[-1].start()
    mark[...] = jnp.zeros_like(mark)
    for copy in copies:
        copy.wait()


def outputs(token, valid, xs, gated_0, gated_1, w_out, b_res, b_skip):
    rows, width = xs.shape[0], xs.shape[1] // 2
    return call(
        outputs_body,
        "outputs",
        [ANYWHERE] + [VMEM] * 9,
        [ANYWHERE, ANYWHERE, VMEM],
        [
            jax.ShapeDtypeStruct((rows, width), BF16),
            jax.ShapeDtypeStruct((rows, w_out.shape[1] - width), BF16),
            MARK,
        ],
        scratch=[
            pltpu.VMEM((rows // ROWS, 2, ROWS, width), BF16),
            pltpu.SemaphoreType.DMA((rows // ROWS, 2)),
        ],
    )(token, valid, xs, *gated_0, *gated_1, w_out, b_res, b_skip)


def inputs_body(steps, token, received, given, pos, head_0, rest_0, head_1, rest_1, w_in, w_cond, *refs):
    gsig, gfeat, mark, room, room_feat, sems = refs[-6:]
    rows, width = given.shape[0], w_in.shape[0] // 2
    copies = []
    wide = 2 * LANES

    def copy(source, target):
        copies.append(pltpu.make_async_copy(source, target, sems.at[len(copies)]))
        copies[-1].start()

    for i, step in enumerate(steps):
        begin = step * ROWS
        here = slice(begin, begin + ROWS)
        after = slice(begin + DILATION_STEP, min(begin + DILATION_STEP + ROWS, rows))
        now = side_by_side(picked(head_0, rest_0, here), picked(head_1, rest_1, here))
        later = side_by_side(picked(head_0, rest_0, after), picked(head_1, rest_1, after))
        tap = column(tap_of(lines_of(pos, after)))
        room_feat[i] = against(w_cond[...], now)
        copy(room_feat.at[i], gfeat.at[:, pl.ds(begin, ROWS)])
        for k in range(width // wide):
            some = slice(k * wide, (k + 1) * wide)
            tail = tap * against(later, w_in[some, :])
            if tail.shape[0] < ROWS:
                tail = below(tail, received[:, some].astype(F32))
            room[i, k] = given[here, some].astype(F32) + against(now, w_in[width + k * wide : width + (k + 1) * wide, :]) + tail
            copy(room.at[i, k], gsig.at[pl.ds(begin, ROWS), pl.ds(k * wide, wide)])
    mark[...] = jnp.zeros_like(mark)
    for one in copies:
        one.wait()


def inputs(steps, token, received, given, pos, dpre_0, dpre_1, w_in, w_cond, before):
    rows, width = given.shape[0], w_in.shape[0] // 2
    cond = w_cond.shape[0]
    count = width // (2 * LANES)
    return call(
        functools.partial(inputs_body, steps),
        f"inputs_{steps[0]}",
        [ANYWHERE] + [VMEM] * 9 + [ANYWHERE] * len(before),
        [ANYWHERE, ANYWHERE, VMEM],
        [
            jax.ShapeDtypeStruct((rows, width), F32),
            jax.ShapeDtypeStruct((cond, rows), F32),
            MARK,
        ],
        scratch=[
            pltpu.VMEM((len(steps), count, ROWS, 2 * LANES), F32),
            pltpu.VMEM((len(steps), cond, ROWS), F32),
            pltpu.SemaphoreType.DMA((len(steps) * (count + 1),)),
        ],
        aliases={10 + k: k for k in range(len(before))},
    )(token, received, given, pos, *dpre_0, *dpre_1, w_in, w_cond, *before)


def unpack_body(far, block, token, mine, theirs, *refs):
    arrays, (mark, room) = refs[-9:-2], refs[-2:]
    mark[...] = jnp.zeros_like(mark)
    core, z, xy = own_place()

    @pl.when(pl.program_id(0) == 0)
    def _():
        for k, ref in ((core, mine), (1 - core, theirs)):
            for c in range(NEAR):
                for r in range(far):
                    rows = pl.ds(pl.multiple_of((k * far + (r ^ z)) * block, 16), block)
                    room[c ^ xy, rows, :] = ref[c, turned(r, far)]

    for j in range(NEAR // 2):
        c = pl.program_id(0) * (NEAR // 2) + j
        here = pl.ds(j * LANES, LANES)
        top = 0
        for ref in arrays:
            count = ref.shape[0]
            size = max(count, ONES)
            ref[:, here] = room[c, top : top + size, :].astype(F32)[:count]
            top += size


def unpack(half, token, far, block, mine, theirs, width, cond, hidden, skip_width, before):
    part = hidden // HALVES
    gates = 2 * hidden
    own = (width, skip_width)[half]

    def wide(size):
        return pl.BlockSpec((size, part), lambda s: (0, HALVES * s + half))

    def tall(size):
        return pl.BlockSpec((part, size // 2), lambda s: (half, s))

    specs = [wide(width), wide(width), wide(cond), wide(1), tall(width), tall(skip_width), pl.BlockSpec((1, own // 2), lambda s: (0, s))]
    shapes = [(width, gates), (width, gates), (cond, gates), (1, gates), (hidden, width), (hidden, skip_width), (1, own)]
    packed = (NEAR, far, block, LANES)
    blocks = pl.BlockSpec(packed, lambda s: (0,) * len(packed))
    return call(
        functools.partial(unpack_body, far, block),
        f"unpack_{half}",
        [ANYWHERE, blocks, blocks] + [ANYWHERE] * len(before),
        specs + [pl.BlockSpec(MARK.shape, lambda s: (0, 0))],
        [jax.ShapeDtypeStruct(shape, F32) for shape in shapes] + [MARK],
        scratch=[pltpu.VMEM((NEAR, 2 * far * block, LANES), BF16)],
        aliases={3 + k: k for k in range(len(before))},
        grid=(2,),
    )(token, mine, theirs, *before)


def swapped(x, axis, k):
    return lax.ppermute(x, axis, [(i, i ^ k) for i in range(lax.axis_size(axis))])


def exchanged(blocks):
    return [swapped(block, "near", k + 1) for k, block in enumerate(blocks)]


def add_body(sizes, token, *refs):
    count = len(sizes)
    kept, got, outs = refs[0], refs[1:-count], refs[-count:]
    at = 0
    for out, size in zip(outs, sizes):
        for k in range(size):
            total = kept[at + k].astype(F32)
            for ref in got:
                total = total + ref[at + k].astype(F32)
            out[k] = total.astype(out.dtype)
        at += size


def added(name, token, kept, got, outs):
    sizes = [size for size, _ in outs]
    result = call(
        functools.partial(add_body, sizes),
        name,
        [ANYWHERE] + [VMEM] * (1 + len(got)),
        [VMEM] * len(outs),
        [jax.ShapeDtypeStruct((size, *kept.shape[1:]), dtype) for size, dtype in outs],
    )(token, kept, *got)
    return result


def mirror_body(token, mine, got, out):
    count = mine.shape[0]
    for k in range(count):
        out[k] = (mine[k].astype(F32) + got[count - 1 - k].astype(F32)).astype(out.dtype)


def mirrored(name, token, mine, got):
    return call(
        mirror_body,
        name,
        [ANYWHERE, VMEM, VMEM],
        VMEM,
        jax.ShapeDtypeStruct(mine.shape, BF16),
    )(token, mine, got)


def join_body(token, *refs):
    out = refs[-1]
    at = 0
    for ref in refs[:-1]:
        out[at : at + ref.shape[0]] = ref[...]
        at += ref.shape[0]


def joined(name, token, parts):
    count = sum(part.shape[0] for part in parts)
    return call(
        join_body,
        name,
        [ANYWHERE] + [VMEM] * len(parts),
        VMEM,
        jax.ShapeDtypeStruct((count, *parts[0].shape[1:]), BF16),
    )(token, *parts)


def over_outer(total):
    for bit in range((lax.axis_size("outer") - 1).bit_length()):
        total = (total.astype(F32) + swapped(total, "outer", 1 << bit).astype(F32)).astype(BF16)
    return total


def passed_along(x, by):
    peers = lax.axis_size(AXES)
    pairs = [(i, i + by) for i in range(peers) if 0 <= i + by < peers]
    return lax.ppermute(x, AXES, pairs)


def in_hbm(x):
    return pltpu.with_memory_space_constraint(x, pltpu.HBM)


def body(
    signal,
    features,
    position,
    valid,
    w_past,
    w_now,
    b_conv,
    w_cond,
    w_res,
    b_res,
    w_skip,
    b_skip,
    grad_out,
    grad_skip,
):
    rows, width = signal.shape
    features = features.T
    cond = features.shape[0]
    hidden = w_res.shape[0]
    skip_width = w_skip.shape[1]
    far = lax.axis_size("far")
    far_bits = (far - 1).bit_length()
    used = 2 * width + cond + ONES + 2 * (hidden // HALVES) + ONES
    block = -(-used // (2 * far * 16)) * 16
    lines = (rows // LANES, LANES)
    pos, val = position.reshape(lines), valid.reshape(lines)
    b_conv, b_res, b_skip = (b.reshape(1, -1) for b in (b_conv, b_res, b_skip))

    def core_sum(half, token, theirs, mine):
        kept, *sent = added(
            f"core_sum_{half}", token, mine, [swapped(theirs, "core", 1)], [(1, F32)] + [(1, BF16)] * (NEAR - 1)
        )
        return kept[0], exchanged([x[0] for x in sent])

    def near_sum(half, token, kept, got):
        kept, sent = added(f"near_sum_{half}", token, kept, got, [(far // 2, F32), (far // 2, BF16)])
        return kept, swapped(sent, "far", 1)

    def far_sum(half, token, kept, got):
        for bit in range(1, far_bits - 1):
            size = kept.shape[0] // 2
            kept, sent = added(f"far_sum_{half}_{bit}", token, kept, [got], [(size, F32), (size, BF16)])
            got = swapped(sent, "far", 1 << bit)
        (mine,) = added(f"far_sum_{half}", token, kept, [got], [(kept.shape[0], BF16)])
        return mine, swapped(mine, "far", 1 << (far_bits - 1))

    def far_end(half, token, mine, got):
        total = over_outer(mirrored(f"far_end_{half}", token, mine, got))
        return total, swapped(total, "far", 1 << (far_bits - 2))

    def far_join(half, token, mine, got):
        total = joined(f"far_join_{half}", token, [mine, got])
        for bit in reversed(range(far_bits - 2)):
            total = joined(f"far_join_{half}_{bit}", token, [total, swapped(total, "far", 1 << bit)])
        return total, exchanged([total] * (NEAR - 1))

    def near_join(half, token, mine, got):
        total = joined(f"near_join_{half}", token, [mine[None]] + [x[None] for x in got])
        return total, swapped(total, "core", 1)

    def input_gradients(steps, token, before):
        last = (steps[-1] + 1) * ROWS == rows
        return inputs(steps, token, received if last else early, given, pos, dpre_0, dpre_1, w_in, w_cond, before)

    halo = passed_along(signal[rows - DILATION_STEP :], 1)
    val, pos, b_conv, b_res, b_skip, w_cond, w_out, w_in, xs, x_turned, given, *rest_0 = load(
        val, pos, b_conv, b_res, b_skip, features, w_cond, w_res, w_skip, w_past, w_now, signal, grad_out, grad_skip
    )
    common = (val, xs, x_turned, given, w_in, w_cond, b_conv, w_out)
    past_head, early, head_0, head_1 = head(halo, pos, *common)
    received = passed_along(early, -1)
    theirs_0, mine_0 = gradients(0, early, early, far, block, val, x_turned, given, past_head, head_0, rest_0)
    rest_1 = forward_rest(theirs_0, *common)
    dpre_0, dpre_1 = (head_0[2], rest_0[2]), (head_1[2], rest_1[2])
    kept_0, got_0 = core_sum(0, rest_1[0], theirs_0, mine_0)
    theirs_1, mine_1 = gradients(1, kept_0, received, far, block, val, x_turned, given, past_head, head_1, rest_1)
    output, skip_out, mark = outputs(
        theirs_1, val, xs, (head_0[0], rest_0[0]), (head_1[0], rest_1[0]), w_out, b_res, b_skip
    )
    kept_0, got_0 = near_sum(0, mark, kept_0, got_0)
    kept_1, got_1 = core_sum(1, kept_0, theirs_1, mine_1)
    *grads, mark = input_gradients((0, 1), kept_1, [])
    ends_0, got_0 = far_sum(0, mark, kept_0, got_0)
    *grads, mark = input_gradients((2,), ends_0, grads)
    kept_1, got_1 = near_sum(1, mark, kept_1, got_1)
    ends_0, got_0 = far_end(0, kept_1, ends_0, got_0)
    ends_1, got_1 = far_sum(1, ends_0, kept_1, got_1)
    ends_0, got_0 = far_join(0, ends_1, ends_0, got_0)
    *grads, mark = input_gradients((3,), ends_0, grads)
    ends_1, got_1 = far_end(1, mark, ends_1, got_1)
    blocks_0, others_0 = near_join(0, ends_1, ends_0, got_0)
    ends_1, got_1 = far_join(1, blocks_0, ends_1, got_1)
    blocks_1, others_1 = near_join(1, ends_1, ends_1, got_1)
    *done, own_0, mark = unpack(0, blocks_1, far, block, blocks_0, others_0, width, cond, hidden, skip_width, [])
    *done, own_1, _ = unpack(1, mark, far, block, blocks_1, others_1, width, cond, hidden, skip_width, done)
    g_past, g_now, g_cond, g_bias, g_res, g_skip = done
    grad_signal, grad_features = grads
    return (
        output,
        skip_out,
        grad_signal,
        grad_features.T,
        g_past,
        g_now,
        g_bias.reshape(-1),
        g_cond,
        g_res,
        own_0.reshape(-1),
        g_skip,
        own_1.reshape(-1),
    )


def solution(mesh):
    row, col = mesh.shape["row"], mesh.shape["col"]
    fine = Mesh(mesh.devices.reshape(row // 2, 2, col // NEAR, NEAR), AXES)
    rows = P(AXES, None)
    line = P(AXES)
    return jax.shard_map(
        body,
        mesh=fine,
        in_specs=(rows, rows, line, line) + (P(),) * 8 + (rows, rows),
        out_specs=(rows,) * 4 + (P(),) * 8,
        check_vma=False,
    )
```

```python
import functools

import jax
import jax.numpy as jnp
from jax import lax
from jax.experimental import pallas as pl
from jax.experimental.pallas import tpu as pltpu
from jax.sharding import Mesh
from jax.sharding import PartitionSpec as P

DILATION_STEP = 256
AXES = ("outer", "core", "far", "near")
HALVES = 2
NEAR = 4
LANES = 128
ROWS = 512
ONES = 16
F32 = jnp.float32
BF16 = jnp.bfloat16
MEGA = 1 << 20
COSTS = {
    "load": 8, "head": 2, "gradients_0": 0, "forward_1": 0, "gradients_1": 4, "outputs": 4, "near_sum_0": 8,
    "far_end_1": 3, "inputs": 1, "near_sum_1": 4, "near_join_0": 1, "near_join_1": 4, "far_join_0": 4,
}
FLOPS = 10**9


def dot(left, right):
    return jnp.dot(left, right, preferred_element_type=F32)


def across(left, right):
    return lax.dot_general(left, right, (((0,), (0,)), ((), ())), preferred_element_type=F32)


def against(left, weight):
    return lax.dot_general(left, weight, (((1,), (1,)), ((), ())), preferred_element_type=F32)


def column(lines):
    turned = lines.astype(F32).T
    return jnp.concatenate([turned[:, k : k + 1] for k in range(lines.shape[0])], axis=0)


def row(lines):
    return jnp.concatenate([lines[k : k + 1] for k in range(lines.shape[0])], axis=1)


def tap_of(lines):
    return jnp.where(lines >= DILATION_STEP, 1, 0)


def lines_of(ref, rows):
    return ref[rows.start // LANES : rows.stop // LANES, :]


def picked(head, rest, rows):
    cut = DILATION_STEP
    low = head[rows.start : min(rows.stop, cut), :] if rows.start < cut else None
    high = rest[max(rows.start, cut) - cut : rows.stop - cut, :] if rows.stop > cut else None
    if low is None:
        return high
    return low if high is None else jnp.concatenate([low, high], axis=0)


def call(kernel, name, in_specs, out_specs, out_shape, scratch=(), aliases=None, grid=(), vmem=24):
    return pl.pallas_call(
        kernel,
        grid=grid,
        in_specs=in_specs,
        out_specs=out_specs,
        out_shape=out_shape,
        scratch_shapes=list(scratch),
        input_output_aliases=aliases or {},
        cost_estimate=pl.CostEstimate(
            flops=1 + int(FLOPS * COSTS.get(name, COSTS.get(name.split("_")[0], 0))), bytes_accessed=1, transcendentals=0
        ),
        name=name,
        compiler_params=pltpu.CompilerParams(vmem_limit_bytes=vmem * MEGA),
    )


VMEM = pl.BlockSpec(memory_space=pltpu.VMEM)
ANYWHERE = pl.BlockSpec(memory_space=pl.ANY)
MARK = jax.ShapeDtypeStruct((8, LANES), F32)


def beside(*parts):
    return jnp.concatenate(parts, axis=1)


def below(*parts):
    return jnp.concatenate(parts, axis=0)


def products(half, rows, x, feats, given, w_in, w_cond, b_conv, w_out, arrive=None):
    part = w_out.shape[0] // HALVES
    first = half * part
    made = []
    for k, at in enumerate((first, HALVES * part + first)):
        here = slice(at, at + part)
        if arrive:
            arrive(rows, k)
        made.append(dot(x, w_in[:, here]) + across(feats, w_cond[:, here]) + b_conv[:, here])
    if arrive:
        arrive(rows, 2)
    return *made, against(given[rows, :], w_out[first : first + part, :])


def finish(pre_a, pre_s, dgated, valid_lines):
    act = jnp.tanh(pre_a)
    gate = 0.5 + 0.5 * jnp.tanh(0.5 * pre_s)
    slope = (column(valid_lines) * dgated) * gate
    dpre = beside(slope * (1.0 - act * act), slope * act * (1.0 - gate)).astype(BF16)
    gated = (act * gate).astype(BF16)
    return gated, gated.T * row(valid_lines.astype(BF16)), dpre


def forward_tiles(half, tiles, prepare, arrive, valid, xs, x_turned, given, weights, gated_out, kept_out, dpre_out):
    cond = weights[1].shape[0]
    width = xs.shape[1] // 2

    def done(rows, *made):
        there = slice(rows.start - DILATION_STEP, rows.stop - DILATION_STEP)
        gated_out[there, :], kept_out[:, there], dpre_out[there, :] = finish(*made, lines_of(valid, rows))

    waiting = None
    for rows in tiles:
        if prepare:
            prepare(rows)
        feats = x_turned[2 * width : 2 * width + cond, rows]
        made = products(half, rows, xs[rows, :], feats, given, *weights, arrive=arrive)
        if waiting:
            done(*waiting)
        waiting = (rows, *made)
    done(*waiting)


def rest_rows(rows):
    cuts = [DILATION_STEP, *range(ROWS, rows + 1, ROWS)]
    return [slice(a, b) for a, b in zip(cuts, cuts[1:])]


def load_body(
    valid, pos, b_conv, b_res, b_skip, feat, w_cond, w_res, w_skip, w_past, w_now, sig, gout, gskip,
    valid_to, pos_to, b_conv_to, b_res_to, b_skip_to, w_cond_to, w_out, w_in, xs, x_turned, given,
    gated_rest, kept_rest, dpre_rest, sems,
):
    rows_all, width = sig.shape
    skip_width = gskip.shape[1]
    cond = feat.shape[0]
    part = w_res.shape[0] // HALVES
    count = 0

    def start(source, target):
        nonlocal count
        copy = pltpu.make_async_copy(source, target, sems.at[count])
        copy.start()
        count += 1
        return copy

    def inner(half, at):
        here = pl.ds(at + half * part, part)
        return [start(ref.at[:, here], w_in.at[pl.ds(k * width, width), here]) for k, ref in enumerate((w_past, w_now))]

    def outer(half):
        here = pl.ds(half * part, part)
        return [
            start(w_res.at[here], w_out.at[here, pl.ds(0, width)]),
            start(w_skip.at[here], w_out.at[here, pl.ds(width, skip_width)]),
        ]

    def signals(i):
        rows = pl.ds(i * ROWS, ROWS)
        return [start(sig.at[rows], xs.at[rows, pl.ds(width, width)])]

    def cotangents(i):
        rows = pl.ds(i * ROWS, ROWS)
        return [
            start(gout.at[rows], given.at[rows, pl.ds(0, width)]),
            start(gskip.at[rows], given.at[rows, pl.ds(width, skip_width)]),
        ]

    here, given_here = {}, {}

    def tile(i):
        if i < rows_all // ROWS and i not in here:
            here[i], given_here[i] = signals(i), cotangents(i)

    here[0] = signals(0)
    needs = [
        [start(pos, pos_to)] + inner(0, 0) + [
            start(feat, x_turned.at[pl.ds(2 * width, cond)]), start(w_cond, w_cond_to), start(b_conv, b_conv_to)
        ],
        inner(0, HALVES * part),
        [start(valid, valid_to)] + outer(0),
    ]
    given_here[0] = cotangents(0)
    tile(1)
    last = []

    def wait(copies):
        for copy in copies:
            copy.wait()
        copies.clear()

    def prepare(rows):
        i = rows.start // ROWS
        wait(here[i])
        if i == 0:
            wait(needs[0])
        tile(i + 2)
        if i == 1:
            for at in (0, HALVES * part):
                last.extend(inner(1, at))
            last.extend(outer(1) + [start(b_res, b_res_to), start(b_skip, b_skip_to)])
        whole = slice(i * ROWS, (i + 1) * ROWS)
        before = slice(rows.start - DILATION_STEP, rows.stop - DILATION_STEP)
        tap = tap_of(lines_of(pos_to, rows)).astype(F32)
        xs[rows, :width] = xs[before, width:] * column(tap).astype(BF16)
        x_turned[width : 2 * width, whole] = xs[whole, width:].T
        x_turned[:width, rows] = x_turned[width : 2 * width, before] * row(tap).astype(BF16)

    def arrive(rows, k):
        wait(needs[k])
        if k == 2:
            wait(given_here[rows.start // ROWS])
            tile(rows.start // ROWS + 3)

    x_turned[2 * width + cond :, :] = jnp.ones((x_turned.shape[0] - 2 * width - cond, rows_all), BF16)
    forward_tiles(
        0, rest_rows(rows_all), prepare, arrive, valid_to, xs, x_turned, given, (w_in, w_cond_to, b_conv_to, w_out),
        gated_rest, kept_rest, dpre_rest,
    )
    wait(last)


def rest_shapes(rest, part):
    return [jax.ShapeDtypeStruct(shape, BF16) for shape in ((rest, part), (part, rest), (rest, 2 * part))]


def load(*arrays):
    sources = [in_hbm(x) for x in arrays]
    feat, w_cond, w_res, w_skip, w_past, w_now, sig, gout, gskip = arrays[5:]
    rows, width = sig.shape
    hidden = w_res.shape[0]
    wide = gout.shape[1] + gskip.shape[1]
    shapes = [jax.ShapeDtypeStruct(x.shape, x.dtype) for x in arrays[:5] + (w_cond,)] + [
        jax.ShapeDtypeStruct(shape, BF16)
        for shape in (
            (hidden, wide), (2 * width, 2 * hidden), (rows, 2 * width), (2 * width + feat.shape[0] + ONES, rows), (rows, wide),
        )
    ]
    shapes += rest_shapes(rows - DILATION_STEP, hidden // HALVES)
    return call(
        load_body,
        "load",
        [ANYWHERE] * len(sources),
        [VMEM] * len(shapes),
        shapes,
        scratch=[pltpu.SemaphoreType.DMA((7 + 6 * HALVES + 3 * (rows // ROWS),))],
    )(*sources)


def side_by_side(dpre_0, dpre_1):
    part = dpre_0.shape[1] // 2
    return beside(dpre_0[:, :part], dpre_1[:, :part], dpre_0[:, part:], dpre_1[:, part:])


def head_body(halo, pos, valid, xs, x_turned, given, w_in, w_cond, b_conv, w_out, past_out, *outs):
    rows = slice(0, DILATION_STEP)
    width = halo.shape[1]
    cond = w_cond.shape[0]
    tap = tap_of(lines_of(pos, rows)).astype(F32)
    past_out[...] = halo[...].T * row(tap).astype(BF16)
    x = beside(halo[...] * column(tap).astype(BF16), xs[rows, width:])
    feats = x_turned[2 * width : 2 * width + cond, rows]
    made = [products(half, rows, x, feats, given, w_in, w_cond, b_conv, w_out) for half in range(HALVES)]
    for half in range(HALVES):
        parts = finish(*made[half], lines_of(valid, rows))
        for ref, value in zip(outs[3 * half :], parts):
            ref[...] = value


def head(halo, *args):
    width = halo.shape[1]
    part = args[-1].shape[0] // HALVES
    past, *parts = call(
        head_body,
        "head",
        [VMEM] * (1 + len(args)),
        [VMEM] * (1 + 3 * HALVES),
        [jax.ShapeDtypeStruct((width, DILATION_STEP), BF16)] + rest_shapes(DILATION_STEP, part) * HALVES,
    )(halo, *args)
    return past, parts[:3], parts[3:]


def early_body(token, pos, dpre_0, dpre_1, w_in, early):
    tap = column(tap_of(lines_of(pos, slice(0, DILATION_STEP))))
    early[...] = (tap * against(side_by_side(dpre_0[...], dpre_1[...]), w_in[: early.shape[1], :])).astype(BF16)


def early_rows(token, pos, dpre_0, dpre_1, w_in):
    return call(
        early_body,
        "early",
        [ANYWHERE] + [VMEM] * 4,
        VMEM,
        jax.ShapeDtypeStruct((DILATION_STEP, w_in.shape[0] // 2), BF16),
    )(token, pos, dpre_0, dpre_1, w_in)


def forward_body(token, valid, xs, x_turned, given, w_in, w_cond, b_conv, w_out, gated_out, kept_out, dpre_out):
    forward_tiles(
        1, rest_rows(xs.shape[0]), None, None, valid, xs, x_turned, given, (w_in, w_cond, b_conv, w_out),
        gated_out, kept_out, dpre_out,
    )


def forward_rest(token, *args):
    return call(
        forward_body,
        "forward_1",
        [ANYWHERE] + [VMEM] * len(args),
        [VMEM] * 3,
        rest_shapes(args[0].shape[0] * LANES - DILATION_STEP, args[-1].shape[0] // HALVES),
    )(token, *args)


def own_place():
    return [lax.axis_index(name) for name in ("core", "far", "near")]


def turned(index, count):
    bits = (count - 1).bit_length()
    result = 0
    for bit in range(bits):
        result = result | (((index >> bit) & 1) << (bits - 1 - bit))
    return result


def place_blocks(far, block, acc, theirs, mine):
    core, z, xy = own_place()
    for r in range(far):
        for c in range(NEAR):
            here = pl.ds(c * LANES, LANES)
            for k, out in ((1 - core, theirs), (core, mine)):
                rows = pl.ds(pl.multiple_of((k * far + r) * block, 16), block)
                out[c ^ xy, turned(r ^ z, far)] = acc[rows, here].astype(out.dtype)


def gradients_body(
    far, block, half, token, valid, x_turned, given, past_head, kept_head, kept_rest, dpre_head, dpre_rest,
    theirs, mine, acc,
):
    cut = DILATION_STEP
    width = past_head.shape[0]
    part = kept_head.shape[0]
    wide = dpre_rest.shape[1]
    mask = jnp.broadcast_to(row(valid[...].astype(F32)).astype(BF16), (ONES, valid.shape[0] * LANES))
    ends = x_turned.shape[0]
    outer = dot(below(kept_rest[...], mask[:, cut:]), given[cut:, :])
    outer += dot(below(kept_head[...], mask[:, :cut]), given[:cut, :])
    at = ends
    for k in range(2):
        acc[at : at + part, :] = outer[:part, k * width : (k + 1) * width]
        at += part
    acc[at : at + ONES, :] = outer[part:, half * width : (half + 1) * width]
    at += ONES
    acc[at:, :] = jnp.zeros((acc.shape[0] - at, wide), F32)
    inner = dot(x_turned[:, cut:], dpre_rest[...])
    inner += dot(below(past_head[...], x_turned[width:, :cut]), dpre_head[...])
    acc[:ends, :] = inner
    place_blocks(far, block, acc, theirs, mine)


def gradients(half, token, far, block, valid, x_turned, given, past_head, head_parts, rest_parts):
    packed = (NEAR, far, block, LANES)
    wide = rest_parts[2].shape[1]
    return call(
        functools.partial(gradients_body, far, block, half),
        f"gradients_{half}",
        [ANYWHERE] + [VMEM] * 8,
        [VMEM] * 2,
        [jax.ShapeDtypeStruct(packed, BF16), jax.ShapeDtypeStruct(packed, F32)],
        scratch=[pltpu.VMEM((2 * far * block, wide), F32)],
    )(token, valid, x_turned, given, past_head, head_parts[1], rest_parts[1], head_parts[2], rest_parts[2])


def outputs_body(token, valid, xs, head_0, rest_0, head_1, rest_1, w_out, b_res, b_skip, out, skip, mark, rooms, sems):
    width = xs.shape[1] // 2
    copies = []
    for i in range(xs.shape[0] // ROWS):
        rows = slice(i * ROWS, (i + 1) * ROWS)
        mask = column(lines_of(valid, rows))
        gated = beside(picked(head_0, rest_0, rows), picked(head_1, rest_1, rows))
        branch = dot(gated, w_out[:, :width]) + b_res[...]
        rooms[i, 0] = (xs[rows, width:].astype(F32) + mask * branch).astype(BF16)
        side = dot(gated, w_out[:, width:]) + b_skip[...]
        rooms[i, 1] = (mask * side).astype(BF16)
        for k, ref in enumerate((out, skip)):
            copies.append(pltpu.make_async_copy(rooms.at[i, k], ref.at[pl.ds(i * ROWS, ROWS)], sems.at[i, k]))
            copies[-1].start()
    mark[...] = jnp.zeros_like(mark)
    for copy in copies:
        copy.wait()


def outputs(token, valid, xs, gated_0, gated_1, w_out, b_res, b_skip):
    rows, width = xs.shape[0], xs.shape[1] // 2
    return call(
        outputs_body,
        "outputs",
        [ANYWHERE] + [VMEM] * 9,
        [ANYWHERE, ANYWHERE, VMEM],
        [
            jax.ShapeDtypeStruct((rows, width), BF16),
            jax.ShapeDtypeStruct((rows, w_out.shape[1] - width), BF16),
            MARK,
        ],
        scratch=[
            pltpu.VMEM((rows // ROWS, 2, ROWS, width), BF16),
            pltpu.SemaphoreType.DMA((rows // ROWS, 2)),
        ],
    )(token, valid, xs, *gated_0, *gated_1, w_out, b_res, b_skip)


def inputs_body(steps, token, received, given, pos, head_0, rest_0, head_1, rest_1, w_in, w_cond, *refs):
    gsig, gfeat, mark, room, room_feat, sems = refs[-6:]
    rows, width = given.shape[0], w_in.shape[0] // 2
    copies = []
    wide = 2 * LANES

    def copy(source, target):
        copies.append(pltpu.make_async_copy(source, target, sems.at[len(copies)]))
        copies[-1].start()

    for i, step in enumerate(steps):
        begin = step * ROWS
        here = slice(begin, begin + ROWS)
        after = slice(begin + DILATION_STEP, min(begin + DILATION_STEP + ROWS, rows))
        now = side_by_side(picked(head_0, rest_0, here), picked(head_1, rest_1, here))
        later = side_by_side(picked(head_0, rest_0, after), picked(head_1, rest_1, after))
        tap = column(tap_of(lines_of(pos, after)))
        room_feat[i] = against(w_cond[...], now)
        copy(room_feat.at[i], gfeat.at[:, pl.ds(begin, ROWS)])
        for k in range(width // wide):
            some = slice(k * wide, (k + 1) * wide)
            tail = tap * against(later, w_in[some, :])
            if tail.shape[0] < ROWS:
                tail = below(tail, received[:, some].astype(F32))
            room[i, k] = given[here, some].astype(F32) + against(now, w_in[width + k * wide : width + (k + 1) * wide, :]) + tail
            copy(room.at[i, k], gsig.at[pl.ds(begin, ROWS), pl.ds(k * wide, wide)])
    mark[...] = jnp.zeros_like(mark)
    for one in copies:
        one.wait()


def inputs(steps, token, received, given, pos, dpre_0, dpre_1, w_in, w_cond, before):
    rows, width = given.shape[0], w_in.shape[0] // 2
    cond = w_cond.shape[0]
    count = width // (2 * LANES)
    return call(
        functools.partial(inputs_body, steps),
        f"inputs_{steps[0]}",
        [ANYWHERE] + [VMEM] * 9 + [ANYWHERE] * len(before),
        [ANYWHERE, ANYWHERE, VMEM],
        [
            jax.ShapeDtypeStruct((rows, width), F32),
            jax.ShapeDtypeStruct((cond, rows), F32),
            MARK,
        ],
        scratch=[
            pltpu.VMEM((len(steps), count, ROWS, 2 * LANES), F32),
            pltpu.VMEM((len(steps), cond, ROWS), F32),
            pltpu.SemaphoreType.DMA((len(steps) * (count + 1),)),
        ],
        aliases={10 + k: k for k in range(len(before))},
    )(token, received, given, pos, *dpre_0, *dpre_1, w_in, w_cond, *before)


def unpack_body(far, block, token, mine, theirs, *refs):
    arrays, (mark, room) = refs[-9:-2], refs[-2:]
    mark[...] = jnp.zeros_like(mark)
    core, z, xy = own_place()

    @pl.when(pl.program_id(0) == 0)
    def _():
        for k, ref in ((core, mine), (1 - core, theirs)):
            for c in range(NEAR):
                for r in range(far):
                    rows = pl.ds(pl.multiple_of((k * far + (r ^ z)) * block, 16), block)
                    room[c ^ xy, rows, :] = ref[c, turned(r, far)]

    for j in range(NEAR // 2):
        c = pl.program_id(0) * (NEAR // 2) + j
        here = pl.ds(j * LANES, LANES)
        top = 0
        for ref in arrays:
            count = ref.shape[0]
            size = max(count, ONES)
            ref[:, here] = room[c, top : top + size, :].astype(F32)[:count]
            top += size


def unpack(half, token, far, block, mine, theirs, width, cond, hidden, skip_width, before):
    part = hidden // HALVES
    gates = 2 * hidden
    own = (width, skip_width)[half]

    def wide(size):
        return pl.BlockSpec((size, part), lambda s: (0, HALVES * s + half))

    def tall(size):
        return pl.BlockSpec((part, size // 2), lambda s: (half, s))

    specs = [wide(width), wide(width), wide(cond), wide(1), tall(width), tall(skip_width), pl.BlockSpec((1, own // 2), lambda s: (0, s))]
    shapes = [(width, gates), (width, gates), (cond, gates), (1, gates), (hidden, width), (hidden, skip_width), (1, own)]
    packed = (NEAR, far, block, LANES)
    blocks = pl.BlockSpec(packed, lambda s: (0,) * len(packed))
    return call(
        functools.partial(unpack_body, far, block),
        f"unpack_{half}",
        [ANYWHERE, blocks, blocks] + [ANYWHERE] * len(before),
        specs + [pl.BlockSpec(MARK.shape, lambda s: (0, 0))],
        [jax.ShapeDtypeStruct(shape, F32) for shape in shapes] + [MARK],
        scratch=[pltpu.VMEM((NEAR, 2 * far * block, LANES), BF16)],
        aliases={3 + k: k for k in range(len(before))},
        grid=(2,),
    )(token, mine, theirs, *before)


def swapped(x, axis, k):
    return lax.ppermute(x, axis, [(i, i ^ k) for i in range(lax.axis_size(axis))])


def exchanged(blocks):
    return [swapped(block, "near", k + 1) for k, block in enumerate(blocks)]


def add_body(sizes, token, *refs):
    count = len(sizes)
    kept, got, outs = refs[0], refs[1:-count], refs[-count:]
    at = 0
    for out, size in zip(outs, sizes):
        for k in range(size):
            total = kept[at + k].astype(F32)
            for ref in got:
                total = total + ref[at + k].astype(F32)
            out[k] = total.astype(out.dtype)
        at += size


def added(name, token, kept, got, outs):
    sizes = [size for size, _ in outs]
    result = call(
        functools.partial(add_body, sizes),
        name,
        [ANYWHERE] + [VMEM] * (1 + len(got)),
        [VMEM] * len(outs),
        [jax.ShapeDtypeStruct((size, *kept.shape[1:]), dtype) for size, dtype in outs],
    )(token, kept, *got)
    return result


def mirror_body(token, mine, got, out):
    count = mine.shape[0]
    for k in range(count):
        out[k] = (mine[k].astype(F32) + got[count - 1 - k].astype(F32)).astype(out.dtype)


def mirrored(name, token, mine, got):
    return call(
        mirror_body,
        name,
        [ANYWHERE, VMEM, VMEM],
        VMEM,
        jax.ShapeDtypeStruct(mine.shape, BF16),
    )(token, mine, got)


def join_body(token, *refs):
    out = refs[-1]
    at = 0
    for ref in refs[:-1]:
        out[at : at + ref.shape[0]] = ref[...]
        at += ref.shape[0]


def joined(name, token, parts):
    count = sum(part.shape[0] for part in parts)
    return call(
        join_body,
        name,
        [ANYWHERE] + [VMEM] * len(parts),
        VMEM,
        jax.ShapeDtypeStruct((count, *parts[0].shape[1:]), BF16),
    )(token, *parts)


def over_outer(total):
    for bit in range((lax.axis_size("outer") - 1).bit_length()):
        total = (total.astype(F32) + swapped(total, "outer", 1 << bit).astype(F32)).astype(BF16)
    return total


def passed_along(x, by):
    peers = lax.axis_size(AXES)
    pairs = [(i, i + by) for i in range(peers) if 0 <= i + by < peers]
    return lax.ppermute(x, AXES, pairs)


def in_hbm(x):
    return pltpu.with_memory_space_constraint(x, pltpu.HBM)


def body(
    signal,
    features,
    position,
    valid,
    w_past,
    w_now,
    b_conv,
    w_cond,
    w_res,
    b_res,
    w_skip,
    b_skip,
    grad_out,
    grad_skip,
):
    rows, width = signal.shape
    features = features.T
    cond = features.shape[0]
    hidden = w_res.shape[0]
    skip_width = w_skip.shape[1]
    far = lax.axis_size("far")
    far_bits = (far - 1).bit_length()
    used = 2 * width + cond + ONES + 2 * (hidden // HALVES) + ONES
    block = -(-used // (2 * far * 16)) * 16
    lines = (rows // LANES, LANES)
    pos, val = position.reshape(lines), valid.reshape(lines)
    b_conv, b_res, b_skip = (b.reshape(1, -1) for b in (b_conv, b_res, b_skip))

    def core_sum(half, token, theirs, mine):
        kept, *sent = added(
            f"core_sum_{half}", token, mine, [swapped(theirs, "core", 1)], [(1, F32)] + [(1, BF16)] * (NEAR - 1)
        )
        return kept[0], exchanged([x[0] for x in sent])

    def near_sum(half, token, kept, got):
        kept, sent = added(f"near_sum_{half}", token, kept, got, [(far // 2, F32), (far // 2, BF16)])
        return kept, swapped(sent, "far", 1)

    def far_sum(half, token, kept, got):
        for bit in range(1, far_bits - 1):
            size = kept.shape[0] // 2
            kept, sent = added(f"far_sum_{half}_{bit}", token, kept, [got], [(size, F32), (size, BF16)])
            got = swapped(sent, "far", 1 << bit)
        (mine,) = added(f"far_sum_{half}", token, kept, [got], [(kept.shape[0], BF16)])
        return mine, swapped(mine, "far", 1 << (far_bits - 1))

    def far_end(half, token, mine, got):
        total = over_outer(mirrored(f"far_end_{half}", token, mine, got))
        return total, swapped(total, "far", 1 << (far_bits - 2))

    def far_join(half, token, mine, got):
        total = joined(f"far_join_{half}", token, [mine, got])
        for bit in reversed(range(far_bits - 2)):
            total = joined(f"far_join_{half}_{bit}", token, [total, swapped(total, "far", 1 << bit)])
        return total, exchanged([total] * (NEAR - 1))

    def near_join(half, token, mine, got):
        total = joined(f"near_join_{half}", token, [mine[None]] + [x[None] for x in got])
        return total, swapped(total, "core", 1)

    def input_gradients(steps, token, before):
        last = (steps[-1] + 1) * ROWS == rows
        return inputs(steps, token, received if last else head_0[0], given, pos, dpre_0, dpre_1, w_in, w_cond, before)

    halo = passed_along(signal[rows - DILATION_STEP :], 1)
    val, pos, b_conv, b_res, b_skip, w_cond, w_out, w_in, xs, x_turned, given, *rest_0 = load(
        val, pos, b_conv, b_res, b_skip, features, w_cond, w_res, w_skip, w_past, w_now, signal, grad_out, grad_skip
    )
    common = (val, xs, x_turned, given, w_in, w_cond, b_conv, w_out)
    past_head, head_0, head_1 = head(halo, pos, *common)
    theirs_0, mine_0 = gradients(0, past_head, far, block, val, x_turned, given, past_head, head_0, rest_0)
    rest_1 = forward_rest(theirs_0, *common)
    dpre_0, dpre_1 = (head_0[2], rest_0[2]), (head_1[2], rest_1[2])
    kept_0, got_0 = core_sum(0, rest_1[0], theirs_0, mine_0)
    theirs_1, mine_1 = gradients(1, kept_0, far, block, val, x_turned, given, past_head, head_1, rest_1)
    output, skip_out, mark = outputs(
        theirs_1, val, xs, (head_0[0], rest_0[0]), (head_1[0], rest_1[0]), w_out, b_res, b_skip
    )
    kept_0, got_0 = near_sum(0, mark, kept_0, got_0)
    kept_1, got_1 = core_sum(1, kept_0, theirs_1, mine_1)
    *grads, mark = input_gradients((0, 1), kept_1, [])
    ends_0, got_0 = far_sum(0, mark, kept_0, got_0)
    *grads, mark = input_gradients((2,), ends_0, grads)
    kept_1, got_1 = near_sum(1, mark, kept_1, got_1)
    ends_0, got_0 = far_end(0, kept_1, ends_0, got_0)
    early = early_rows(ends_0, pos, head_0[2], head_1[2], w_in)
    received = passed_along(early, -1)
    ends_1, got_1 = far_sum(1, early, kept_1, got_1)
    ends_0, got_0 = far_join(0, ends_1, ends_0, got_0)
    *grads, mark = input_gradients((3,), ends_0, grads)
    ends_1, got_1 = far_end(1, mark, ends_1, got_1)
    blocks_0, others_0 = near_join(0, ends_1, ends_0, got_0)
    ends_1, got_1 = far_join(1, blocks_0, ends_1, got_1)
    blocks_1, others_1 = near_join(1, ends_1, ends_1, got_1)
    *done, own_0, mark = unpack(0, blocks_1, far, block, blocks_0, others_0, width, cond, hidden, skip_width, [])
    *done, own_1, _ = unpack(1, mark, far, block, blocks_1, others_1, width, cond, hidden, skip_width, done)
    g_past, g_now, g_cond, g_bias, g_res, g_skip = done
    grad_signal, grad_features = grads
    return (
        output,
        skip_out,
        grad_signal,
        grad_features.T,
        g_past,
        g_now,
        g_bias.reshape(-1),
        g_cond,
        g_res,
        own_0.reshape(-1),
        g_skip,
        own_1.reshape(-1),
    )


def solution(mesh):
    row, col = mesh.shape["row"], mesh.shape["col"]
    fine = Mesh(mesh.devices.reshape(row // 2, 2, col // NEAR, NEAR), AXES)
    rows = P(AXES, None)
    line = P(AXES)
    return jax.shard_map(
        body,
        mesh=fine,
        in_specs=(rows, rows, line, line) + (P(),) * 8 + (rows, rows),
        out_specs=(rows,) * 4 + (P(),) * 8,
        check_vma=False,
    )
```

```python
import functools

import jax
import jax.numpy as jnp
from jax import lax
from jax.experimental import pallas as pl
from jax.experimental.pallas import tpu as pltpu
from jax.sharding import Mesh
from jax.sharding import PartitionSpec as P

DILATION_STEP = 256
AXES = ("outer", "core", "far", "near")
HALVES = 2
NEAR = 4
LANES = 128
ROWS = 512
ONES = 16
F32 = jnp.float32
BF16 = jnp.bfloat16
MEGA = 1 << 20
COSTS = {
    "load": 8, "head": 2, "gradients_0": 0, "forward_1": 0, "gradients_1": 4, "outputs": 4, "near_sum_0": 8,
    "inputs": 1, "near_sum_1": 4, "near_join_0": 1, "near_join_1": 4, "far_join_0": 4,
}
FLOPS = 10**9


def dot(left, right):
    return jnp.dot(left, right, preferred_element_type=F32)


def across(left, right):
    return lax.dot_general(left, right, (((0,), (0,)), ((), ())), preferred_element_type=F32)


def against(left, weight):
    return lax.dot_general(left, weight, (((1,), (1,)), ((), ())), preferred_element_type=F32)


def column(lines):
    turned = lines.astype(F32).T
    return jnp.concatenate([turned[:, k : k + 1] for k in range(lines.shape[0])], axis=0)


def row(lines):
    return jnp.concatenate([lines[k : k + 1] for k in range(lines.shape[0])], axis=1)


def tap_of(lines):
    return jnp.where(lines >= DILATION_STEP, 1, 0)


def lines_of(ref, rows):
    return ref[rows.start // LANES : rows.stop // LANES, :]


def picked(head, rest, rows):
    cut = DILATION_STEP
    low = head[rows.start : min(rows.stop, cut), :] if rows.start < cut else None
    high = rest[max(rows.start, cut) - cut : rows.stop - cut, :] if rows.stop > cut else None
    if low is None:
        return high
    return low if high is None else jnp.concatenate([low, high], axis=0)


def call(kernel, name, in_specs, out_specs, out_shape, scratch=(), aliases=None, grid=(), vmem=24):
    return pl.pallas_call(
        kernel,
        grid=grid,
        in_specs=in_specs,
        out_specs=out_specs,
        out_shape=out_shape,
        scratch_shapes=list(scratch),
        input_output_aliases=aliases or {},
        cost_estimate=pl.CostEstimate(
            flops=1 + int(FLOPS * COSTS.get(name, COSTS.get(name.split("_")[0], 0))), bytes_accessed=1, transcendentals=0
        ),
        name=name,
        compiler_params=pltpu.CompilerParams(vmem_limit_bytes=vmem * MEGA),
    )


VMEM = pl.BlockSpec(memory_space=pltpu.VMEM)
ANYWHERE = pl.BlockSpec(memory_space=pl.ANY)
MARK = jax.ShapeDtypeStruct((8, LANES), F32)


def beside(*parts):
    return jnp.concatenate(parts, axis=1)


def below(*parts):
    return jnp.concatenate(parts, axis=0)


def products(half, rows, x, feats, given, w_in, w_cond, b_conv, w_out, arrive=None):
    part = w_out.shape[0] // HALVES
    first = half * part
    made = []
    for k, at in enumerate((first, HALVES * part + first)):
        here = slice(at, at + part)
        if arrive:
            arrive(rows, k)
        made.append(dot(x, w_in[:, here]) + across(feats, w_cond[:, here]) + b_conv[:, here])
    if arrive:
        arrive(rows, 2)
    return *made, against(given[rows, :], w_out[first : first + part, :])


def finish(pre_a, pre_s, dgated, valid_lines):
    act = jnp.tanh(pre_a)
    gate = 0.5 + 0.5 * jnp.tanh(0.5 * pre_s)
    slope = (column(valid_lines) * dgated) * gate
    dpre = beside(slope * (1.0 - act * act), slope * act * (1.0 - gate)).astype(BF16)
    gated = (act * gate).astype(BF16)
    return gated, gated.T * row(valid_lines.astype(BF16)), dpre


def forward_tiles(half, tiles, prepare, arrive, valid, xs, x_turned, given, weights, gated_out, kept_out, dpre_out):
    cond = weights[1].shape[0]
    width = xs.shape[1] // 2

    def done(rows, *made):
        there = slice(rows.start - DILATION_STEP, rows.stop - DILATION_STEP)
        gated_out[there, :], kept_out[:, there], dpre_out[there, :] = finish(*made, lines_of(valid, rows))

    waiting = None
    for rows in tiles:
        if prepare:
            prepare(rows)
        feats = x_turned[2 * width : 2 * width + cond, rows]
        made = products(half, rows, xs[rows, :], feats, given, *weights, arrive=arrive)
        if waiting:
            done(*waiting)
        waiting = (rows, *made)
    done(*waiting)


def rest_rows(rows, tile=ROWS):
    cuts = sorted({DILATION_STEP, *range(tile, rows + 1, tile)})
    return [slice(a, b) for a, b in zip(cuts, cuts[1:])]


def load_body(
    valid, pos, b_conv, b_res, b_skip, feat, w_cond, w_res, w_skip, w_past, w_now, sig, gout, gskip,
    valid_to, pos_to, b_conv_to, b_res_to, b_skip_to, w_cond_to, w_out, w_in, xs, x_turned, given,
    gated_rest, kept_rest, dpre_rest, sems,
):
    rows_all, width = sig.shape
    skip_width = gskip.shape[1]
    cond = feat.shape[0]
    part = w_res.shape[0] // HALVES
    count = 0

    def start(source, target):
        nonlocal count
        copy = pltpu.make_async_copy(source, target, sems.at[count])
        copy.start()
        count += 1
        return copy

    def inner(half, at):
        here = pl.ds(at + half * part, part)
        return [start(ref.at[:, here], w_in.at[pl.ds(k * width, width), here]) for k, ref in enumerate((w_past, w_now))]

    def outer(half):
        here = pl.ds(half * part, part)
        return [
            start(w_res.at[here], w_out.at[here, pl.ds(0, width)]),
            start(w_skip.at[here], w_out.at[here, pl.ds(width, skip_width)]),
        ]

    def signals(i):
        rows = pl.ds(i * ROWS, ROWS)
        return [start(sig.at[rows], xs.at[rows, pl.ds(width, width)])]

    def cotangents(i):
        rows = pl.ds(i * ROWS, ROWS)
        return [
            start(gout.at[rows], given.at[rows, pl.ds(0, width)]),
            start(gskip.at[rows], given.at[rows, pl.ds(width, skip_width)]),
        ]

    here, given_here = {}, {}

    def tile(i):
        if i < rows_all // ROWS and i not in here:
            here[i], given_here[i] = signals(i), cotangents(i)

    here[0] = signals(0)
    needs = [
        [start(pos, pos_to)] + inner(0, 0) + [
            start(feat, x_turned.at[pl.ds(2 * width, cond)]), start(w_cond, w_cond_to), start(b_conv, b_conv_to)
        ],
        inner(0, HALVES * part),
        [start(valid, valid_to)] + outer(0),
    ]
    given_here[0] = cotangents(0)
    tile(1)
    last = []

    def wait(copies):
        for copy in copies:
            copy.wait()
        copies.clear()

    def prepare(rows):
        i = rows.start // ROWS
        wait(here[i])
        if i == 0:
            wait(needs[0])
        tile(i + 2)
        if i == 1:
            for at in (0, HALVES * part):
                last.extend(inner(1, at))
            last.extend(outer(1) + [start(b_res, b_res_to), start(b_skip, b_skip_to)])
        whole = slice(i * ROWS, (i + 1) * ROWS)
        before = slice(rows.start - DILATION_STEP, rows.stop - DILATION_STEP)
        tap = tap_of(lines_of(pos_to, rows)).astype(F32)
        xs[rows, :width] = xs[before, width:] * column(tap).astype(BF16)
        x_turned[width : 2 * width, whole] = xs[whole, width:].T
        x_turned[:width, rows] = x_turned[width : 2 * width, before] * row(tap).astype(BF16)

    def arrive(rows, k):
        wait(needs[k])
        if k == 2:
            wait(given_here[rows.start // ROWS])
            tile(rows.start // ROWS + 3)

    x_turned[2 * width + cond :, :] = jnp.ones((x_turned.shape[0] - 2 * width - cond, rows_all), BF16)
    forward_tiles(
        0, rest_rows(rows_all), prepare, arrive, valid_to, xs, x_turned, given, (w_in, w_cond_to, b_conv_to, w_out),
        gated_rest, kept_rest, dpre_rest,
    )
    wait(last)


def rest_shapes(rest, part):
    return [jax.ShapeDtypeStruct(shape, BF16) for shape in ((rest, part), (part, rest), (rest, 2 * part))]


def load(*arrays):
    sources = [in_hbm(x) for x in arrays]
    feat, w_cond, w_res, w_skip, w_past, w_now, sig, gout, gskip = arrays[5:]
    rows, width = sig.shape
    hidden = w_res.shape[0]
    wide = gout.shape[1] + gskip.shape[1]
    shapes = [jax.ShapeDtypeStruct(x.shape, x.dtype) for x in arrays[:5] + (w_cond,)] + [
        jax.ShapeDtypeStruct(shape, BF16)
        for shape in (
            (hidden, wide), (2 * width, 2 * hidden), (rows, 2 * width), (2 * width + feat.shape[0] + ONES, rows), (rows, wide),
        )
    ]
    shapes += rest_shapes(rows - DILATION_STEP, hidden // HALVES)
    return call(
        load_body,
        "load",
        [ANYWHERE] * len(sources),
        [VMEM] * len(shapes),
        shapes,
        scratch=[pltpu.SemaphoreType.DMA((7 + 6 * HALVES + 3 * (rows // ROWS),))],
    )(*sources)


def side_by_side(dpre_0, dpre_1):
    part = dpre_0.shape[1] // 2
    return beside(dpre_0[:, :part], dpre_1[:, :part], dpre_0[:, part:], dpre_1[:, part:])


def head_body(halo, pos, valid, xs, x_turned, given, w_in, w_cond, b_conv, w_out, past_out, *outs):
    rows = slice(0, DILATION_STEP)
    width = halo.shape[1]
    cond = w_cond.shape[0]
    tap = tap_of(lines_of(pos, rows)).astype(F32)
    past_out[...] = halo[...].T * row(tap).astype(BF16)
    x = beside(halo[...] * column(tap).astype(BF16), xs[rows, width:])
    feats = x_turned[2 * width : 2 * width + cond, rows]
    made = [products(half, rows, x, feats, given, w_in, w_cond, b_conv, w_out) for half in range(HALVES)]
    for half in range(HALVES):
        parts = finish(*made[half], lines_of(valid, rows))
        for ref, value in zip(outs[3 * half :], parts):
            ref[...] = value


def head(halo, *args):
    width = halo.shape[1]
    part = args[-1].shape[0] // HALVES
    past, *parts = call(
        head_body,
        "head",
        [VMEM] * (1 + len(args)),
        [VMEM] * (1 + 3 * HALVES),
        [jax.ShapeDtypeStruct((width, DILATION_STEP), BF16)] + rest_shapes(DILATION_STEP, part) * HALVES,
    )(halo, *args)
    return past, parts[:3], parts[3:]


def early_body(token, pos, dpre_0, dpre_1, w_in, early):
    tap = column(tap_of(lines_of(pos, slice(0, DILATION_STEP))))
    early[...] = (tap * against(side_by_side(dpre_0[...], dpre_1[...]), w_in[: early.shape[1], :])).astype(BF16)


def early_rows(token, pos, dpre_0, dpre_1, w_in):
    return call(
        early_body,
        "early",
        [ANYWHERE] + [VMEM] * 4,
        VMEM,
        jax.ShapeDtypeStruct((DILATION_STEP, w_in.shape[0] // 2), BF16),
    )(token, pos, dpre_0, dpre_1, w_in)


def forward_body(token, valid, xs, x_turned, given, w_in, w_cond, b_conv, w_out, gated_out, kept_out, dpre_out):
    forward_tiles(
        1, rest_rows(xs.shape[0], ROWS // 2), None, None, valid, xs, x_turned, given, (w_in, w_cond, b_conv, w_out),
        gated_out, kept_out, dpre_out,
    )


def forward_rest(token, *args):
    return call(
        forward_body,
        "forward_1",
        [ANYWHERE] + [VMEM] * len(args),
        [VMEM] * 3,
        rest_shapes(args[0].shape[0] * LANES - DILATION_STEP, args[-1].shape[0] // HALVES),
    )(token, *args)


def own_place():
    return [lax.axis_index(name) for name in ("core", "far", "near")]


def turned(index, count):
    bits = (count - 1).bit_length()
    result = 0
    for bit in range(bits):
        result = result | (((index >> bit) & 1) << (bits - 1 - bit))
    return result


def place_blocks(far, block, acc, theirs, mine):
    core, z, xy = own_place()
    for r in range(far):
        for c in range(NEAR):
            here = pl.ds(c * LANES, LANES)
            for k, out in ((1 - core, theirs), (core, mine)):
                rows = pl.ds(pl.multiple_of((k * far + r) * block, 16), block)
                out[c ^ xy, turned(r ^ z, far)] = acc[rows, here].astype(out.dtype)


def gradients_body(
    far, block, half, token, valid, x_turned, given, past_head, kept_head, kept_rest, dpre_head, dpre_rest,
    theirs, mine, acc,
):
    cut = DILATION_STEP
    width = past_head.shape[0]
    part = kept_head.shape[0]
    wide = dpre_rest.shape[1]
    mask = jnp.broadcast_to(row(valid[...].astype(F32)).astype(BF16), (ONES, valid.shape[0] * LANES))
    ends = x_turned.shape[0]
    outer = dot(below(kept_rest[...], mask[:, cut:]), given[cut:, :])
    outer += dot(below(kept_head[...], mask[:, :cut]), given[:cut, :])
    at = ends
    for k in range(2):
        acc[at : at + part, :] = outer[:part, k * width : (k + 1) * width]
        at += part
    acc[at : at + ONES, :] = outer[part:, half * width : (half + 1) * width]
    at += ONES
    acc[at:, :] = jnp.zeros((acc.shape[0] - at, wide), F32)
    inner = dot(x_turned[:, cut:], dpre_rest[...])
    inner += dot(below(past_head[...], x_turned[width:, :cut]), dpre_head[...])
    acc[:ends, :] = inner
    place_blocks(far, block, acc, theirs, mine)


def gradients(half, token, far, block, valid, x_turned, given, past_head, head_parts, rest_parts):
    packed = (NEAR, far, block, LANES)
    wide = rest_parts[2].shape[1]
    return call(
        functools.partial(gradients_body, far, block, half),
        f"gradients_{half}",
        [ANYWHERE] + [VMEM] * 8,
        [VMEM] * 2,
        [jax.ShapeDtypeStruct(packed, BF16), jax.ShapeDtypeStruct(packed, F32)],
        scratch=[pltpu.VMEM((2 * far * block, wide), F32)],
    )(token, valid, x_turned, given, past_head, head_parts[1], rest_parts[1], head_parts[2], rest_parts[2])


def outputs_body(token, valid, xs, head_0, rest_0, head_1, rest_1, w_out, b_res, b_skip, out, skip, mark, rooms, sems):
    width = xs.shape[1] // 2
    copies = []
    for i in range(xs.shape[0] // ROWS):
        rows = slice(i * ROWS, (i + 1) * ROWS)
        mask = column(lines_of(valid, rows))
        gated = beside(picked(head_0, rest_0, rows), picked(head_1, rest_1, rows))
        branch = dot(gated, w_out[:, :width]) + b_res[...]
        rooms[i, 0] = (xs[rows, width:].astype(F32) + mask * branch).astype(BF16)
        side = dot(gated, w_out[:, width:]) + b_skip[...]
        rooms[i, 1] = (mask * side).astype(BF16)
        for k, ref in enumerate((out, skip)):
            copies.append(pltpu.make_async_copy(rooms.at[i, k], ref.at[pl.ds(i * ROWS, ROWS)], sems.at[i, k]))
            copies[-1].start()
    mark[...] = jnp.zeros_like(mark)
    for copy in copies:
        copy.wait()


def outputs(token, valid, xs, gated_0, gated_1, w_out, b_res, b_skip):
    rows, width = xs.shape[0], xs.shape[1] // 2
    return call(
        outputs_body,
        "outputs",
        [ANYWHERE] + [VMEM] * 9,
        [ANYWHERE, ANYWHERE, VMEM],
        [
            jax.ShapeDtypeStruct((rows, width), BF16),
            jax.ShapeDtypeStruct((rows, w_out.shape[1] - width), BF16),
            MARK,
        ],
        scratch=[
            pltpu.VMEM((rows // ROWS, 2, ROWS, width), BF16),
            pltpu.SemaphoreType.DMA((rows // ROWS, 2)),
        ],
    )(token, valid, xs, *gated_0, *gated_1, w_out, b_res, b_skip)


def inputs_body(steps, token, received, given, pos, head_0, rest_0, head_1, rest_1, w_in, w_cond, *refs):
    gsig, gfeat, mark, room, room_feat, sems = refs[-6:]
    rows, width = given.shape[0], w_in.shape[0] // 2
    copies = []
    wide = 2 * LANES

    def copy(source, target):
        copies.append(pltpu.make_async_copy(source, target, sems.at[len(copies)]))
        copies[-1].start()

    for i, step in enumerate(steps):
        begin = step * ROWS
        here = slice(begin, begin + ROWS)
        after = slice(begin + DILATION_STEP, min(begin + DILATION_STEP + ROWS, rows))
        now = side_by_side(picked(head_0, rest_0, here), picked(head_1, rest_1, here))
        later = side_by_side(picked(head_0, rest_0, after), picked(head_1, rest_1, after))
        tap = column(tap_of(lines_of(pos, after)))
        room_feat[i] = against(w_cond[...], now)
        copy(room_feat.at[i], gfeat.at[:, pl.ds(begin, ROWS)])
        for k in range(width // wide):
            some = slice(k * wide, (k + 1) * wide)
            tail = tap * against(later, w_in[some, :])
            if tail.shape[0] < ROWS:
                tail = below(tail, received[:, some].astype(F32))
            room[i, k] = given[here, some].astype(F32) + against(now, w_in[width + k * wide : width + (k + 1) * wide, :]) + tail
            copy(room.at[i, k], gsig.at[pl.ds(begin, ROWS), pl.ds(k * wide, wide)])
    mark[...] = jnp.zeros_like(mark)
    for one in copies:
        one.wait()


def inputs(steps, token, received, given, pos, dpre_0, dpre_1, w_in, w_cond, before):
    rows, width = given.shape[0], w_in.shape[0] // 2
    cond = w_cond.shape[0]
    count = width // (2 * LANES)
    return call(
        functools.partial(inputs_body, steps),
        f"inputs_{steps[0]}",
        [ANYWHERE] + [VMEM] * 9 + [ANYWHERE] * len(before),
        [ANYWHERE, ANYWHERE, VMEM],
        [
            jax.ShapeDtypeStruct((rows, width), F32),
            jax.ShapeDtypeStruct((cond, rows), F32),
            MARK,
        ],
        scratch=[
            pltpu.VMEM((len(steps), count, ROWS, 2 * LANES), F32),
            pltpu.VMEM((len(steps), cond, ROWS), F32),
            pltpu.SemaphoreType.DMA((len(steps) * (count + 1),)),
        ],
        aliases={10 + k: k for k in range(len(before))},
    )(token, received, given, pos, *dpre_0, *dpre_1, w_in, w_cond, *before)


def unpack_body(far, block, token, mine, theirs, *refs):
    arrays, (mark, room) = refs[-9:-2], refs[-2:]
    mark[...] = jnp.zeros_like(mark)
    core, z, xy = own_place()

    @pl.when(pl.program_id(0) == 0)
    def _():
        for k, ref in ((core, mine), (1 - core, theirs)):
            for c in range(NEAR):
                for r in range(far):
                    rows = pl.ds(pl.multiple_of((k * far + (r ^ z)) * block, 16), block)
                    room[c ^ xy, rows, :] = ref[c, turned(r, far)]

    for j in range(NEAR // 2):
        c = pl.program_id(0) * (NEAR // 2) + j
        here = pl.ds(j * LANES, LANES)
        top = 0
        for ref in arrays:
            count = ref.shape[0]
            size = max(count, ONES)
            ref[:, here] = room[c, top : top + size, :].astype(F32)[:count]
            top += size


def unpack(half, token, far, block, mine, theirs, width, cond, hidden, skip_width, before):
    part = hidden // HALVES
    gates = 2 * hidden
    own = (width, skip_width)[half]

    def wide(size):
        return pl.BlockSpec((size, part), lambda s: (0, HALVES * s + half))

    def tall(size):
        return pl.BlockSpec((part, size // 2), lambda s: (half, s))

    specs = [wide(width), wide(width), wide(cond), wide(1), tall(width), tall(skip_width), pl.BlockSpec((1, own // 2), lambda s: (0, s))]
    shapes = [(width, gates), (width, gates), (cond, gates), (1, gates), (hidden, width), (hidden, skip_width), (1, own)]
    packed = (NEAR, far, block, LANES)
    blocks = pl.BlockSpec(packed, lambda s: (0,) * len(packed))
    return call(
        functools.partial(unpack_body, far, block),
        f"unpack_{half}",
        [ANYWHERE, blocks, blocks] + [ANYWHERE] * len(before),
        specs + [pl.BlockSpec(MARK.shape, lambda s: (0, 0))],
        [jax.ShapeDtypeStruct(shape, F32) for shape in shapes] + [MARK],
        scratch=[pltpu.VMEM((NEAR, 2 * far * block, LANES), BF16)],
        aliases={3 + k: k for k in range(len(before))},
        grid=(2,),
    )(token, mine, theirs, *before)


def swapped(x, axis, k):
    return lax.ppermute(x, axis, [(i, i ^ k) for i in range(lax.axis_size(axis))])


def exchanged(blocks):
    return [swapped(block, "near", k + 1) for k, block in enumerate(blocks)]


def add_body(sizes, token, *refs):
    count = len(sizes)
    kept, got, outs = refs[0], refs[1:-count], refs[-count:]
    at = 0
    for out, size in zip(outs, sizes):
        for k in range(size):
            total = kept[at + k].astype(F32)
            for ref in got:
                total = total + ref[at + k].astype(F32)
            out[k] = total.astype(out.dtype)
        at += size


def added(name, token, kept, got, outs):
    sizes = [size for size, _ in outs]
    result = call(
        functools.partial(add_body, sizes),
        name,
        [ANYWHERE] + [VMEM] * (1 + len(got)),
        [VMEM] * len(outs),
        [jax.ShapeDtypeStruct((size, *kept.shape[1:]), dtype) for size, dtype in outs],
    )(token, kept, *got)
    return result


def mirror_body(token, mine, got, out):
    count = mine.shape[0]
    for k in range(count):
        out[k] = (mine[k].astype(F32) + got[count - 1 - k].astype(F32)).astype(out.dtype)


def mirrored(name, token, mine, got):
    return call(
        mirror_body,
        name,
        [ANYWHERE, VMEM, VMEM],
        VMEM,
        jax.ShapeDtypeStruct(mine.shape, BF16),
    )(token, mine, got)


def join_body(token, *refs):
    out = refs[-1]
    at = 0
    for ref in refs[:-1]:
        out[at : at + ref.shape[0]] = ref[...]
        at += ref.shape[0]


def joined(name, token, parts):
    count = sum(part.shape[0] for part in parts)
    return call(
        join_body,
        name,
        [ANYWHERE] + [VMEM] * len(parts),
        VMEM,
        jax.ShapeDtypeStruct((count, *parts[0].shape[1:]), BF16),
    )(token, *parts)


def over_outer(total):
    for bit in range((lax.axis_size("outer") - 1).bit_length()):
        total = (total.astype(F32) + swapped(total, "outer", 1 << bit).astype(F32)).astype(BF16)
    return total


def passed_along(x, by):
    peers = lax.axis_size(AXES)
    pairs = [(i, i + by) for i in range(peers) if 0 <= i + by < peers]
    return lax.ppermute(x, AXES, pairs)


def in_hbm(x):
    return pltpu.with_memory_space_constraint(x, pltpu.HBM)


def body(
    signal,
    features,
    position,
    valid,
    w_past,
    w_now,
    b_conv,
    w_cond,
    w_res,
    b_res,
    w_skip,
    b_skip,
    grad_out,
    grad_skip,
):
    rows, width = signal.shape
    features = features.T
    cond = features.shape[0]
    hidden = w_res.shape[0]
    skip_width = w_skip.shape[1]
    far = lax.axis_size("far")
    far_bits = (far - 1).bit_length()
    used = 2 * width + cond + ONES + 2 * (hidden // HALVES) + ONES
    block = -(-used // (2 * far * 16)) * 16
    lines = (rows // LANES, LANES)
    pos, val = position.reshape(lines), valid.reshape(lines)
    b_conv, b_res, b_skip = (b.reshape(1, -1) for b in (b_conv, b_res, b_skip))

    def core_sum(half, token, theirs, mine):
        kept, *sent = added(
            f"core_sum_{half}", token, mine, [swapped(theirs, "core", 1)], [(1, F32)] + [(1, BF16)] * (NEAR - 1)
        )
        return kept[0], exchanged([x[0] for x in sent])

    def near_sum(half, token, kept, got):
        kept, sent = added(f"near_sum_{half}", token, kept, got, [(far // 2, F32), (far // 2, BF16)])
        return kept, swapped(sent, "far", 1)

    def far_sum(half, token, kept, got):
        for bit in range(1, far_bits - 1):
            size = kept.shape[0] // 2
            kept, sent = added(f"far_sum_{half}_{bit}", token, kept, [got], [(size, F32), (size, BF16)])
            got = swapped(sent, "far", 1 << bit)
        (mine,) = added(f"far_sum_{half}", token, kept, [got], [(kept.shape[0], BF16)])
        return mine, swapped(mine, "far", 1 << (far_bits - 1))

    def far_end(half, token, mine, got):
        total = over_outer(mirrored(f"far_end_{half}", token, mine, got))
        return total, swapped(total, "far", 1 << (far_bits - 2))

    def far_join(half, token, mine, got):
        total = joined(f"far_join_{half}", token, [mine, got])
        for bit in reversed(range(far_bits - 2)):
            total = joined(f"far_join_{half}_{bit}", token, [total, swapped(total, "far", 1 << bit)])
        return total, exchanged([total] * (NEAR - 1))

    def near_join(half, token, mine, got):
        total = joined(f"near_join_{half}", token, [mine[None]] + [x[None] for x in got])
        return total, swapped(total, "core", 1)

    def input_gradients(steps, token, before):
        last = (steps[-1] + 1) * ROWS == rows
        return inputs(steps, token, received if last else head_0[0], given, pos, dpre_0, dpre_1, w_in, w_cond, before)

    halo = passed_along(signal[rows - DILATION_STEP :], 1)
    val, pos, b_conv, b_res, b_skip, w_cond, w_out, w_in, xs, x_turned, given, *rest_0 = load(
        val, pos, b_conv, b_res, b_skip, features, w_cond, w_res, w_skip, w_past, w_now, signal, grad_out, grad_skip
    )
    common = (val, xs, x_turned, given, w_in, w_cond, b_conv, w_out)
    past_head, head_0, head_1 = head(halo, pos, *common)
    theirs_0, mine_0 = gradients(0, past_head, far, block, val, x_turned, given, past_head, head_0, rest_0)
    early = early_rows(theirs_0, pos, head_0[2], head_1[2], w_in)
    received = passed_along(early, -1)
    kept_0, got_0 = core_sum(0, early, theirs_0, mine_0)
    rest_1 = forward_rest(kept_0, *common)
    dpre_0, dpre_1 = (head_0[2], rest_0[2]), (head_1[2], rest_1[2])
    theirs_1, mine_1 = gradients(1, received, far, block, val, x_turned, given, past_head, head_1, rest_1)
    kept_0, got_0 = near_sum(0, theirs_1, kept_0, got_0)
    output, skip_out, mark = outputs(
        kept_0, val, xs, (head_0[0], rest_0[0]), (head_1[0], rest_1[0]), w_out, b_res, b_skip
    )
    kept_1, got_1 = core_sum(1, mark, theirs_1, mine_1)
    ends_0, got_0 = far_sum(0, kept_1, kept_0, got_0)
    *grads, mark = input_gradients((0, 1), ends_0, [])
    ends_0, got_0 = far_end(0, mark, ends_0, got_0)
    kept_1, got_1 = near_sum(1, ends_0, kept_1, got_1)
    ends_0, got_0 = far_join(0, kept_1, ends_0, got_0)
    *grads, mark = input_gradients((2,), ends_0, grads)
    ends_1, got_1 = far_sum(1, mark, kept_1, got_1)
    ends_1, got_1 = far_end(1, ends_1, ends_1, got_1)
    blocks_0, others_0 = near_join(0, ends_1, ends_0, got_0)
    ends_1, got_1 = far_join(1, blocks_0, ends_1, got_1)
    *grads, mark = input_gradients((3,), ends_1, grads)
    blocks_1, others_1 = near_join(1, mark, ends_1, got_1)
    *done, own_0, mark = unpack(0, blocks_1, far, block, blocks_0, others_0, width, cond, hidden, skip_width, [])
    *done, own_1, _ = unpack(1, mark, far, block, blocks_1, others_1, width, cond, hidden, skip_width, done)
    g_past, g_now, g_cond, g_bias, g_res, g_skip = done
    grad_signal, grad_features = grads
    return (
        output,
        skip_out,
        grad_signal,
        grad_features.T,
        g_past,
        g_now,
        g_bias.reshape(-1),
        g_cond,
        g_res,
        own_0.reshape(-1),
        g_skip,
        own_1.reshape(-1),
    )


def solution(mesh):
    row, col = mesh.shape["row"], mesh.shape["col"]
    fine = Mesh(mesh.devices.reshape(row // 2, 2, col // NEAR, NEAR), AXES)
    rows = P(AXES, None)
    line = P(AXES)
    return jax.shard_map(
        body,
        mesh=fine,
        in_specs=(rows, rows, line, line) + (P(),) * 8 + (rows, rows),
        out_specs=(rows,) * 4 + (P(),) * 8,
        check_vma=False,
    )
```

```python
import functools

import jax
import jax.numpy as jnp
from jax import lax
from jax.experimental import pallas as pl
from jax.experimental.pallas import tpu as pltpu
from jax.sharding import Mesh
from jax.sharding import PartitionSpec as P

DILATION_STEP = 256
AXES = ("outer", "core", "far", "near")
HALVES = 2
NEAR = 4
LANES = 128
ROWS = 512
ONES = 16
F32 = jnp.float32
BF16 = jnp.bfloat16
MEGA = 1 << 20
COSTS = {
    "load": 8, "head": 2, "gradients_0": 0, "forward_1": 0, "gradients_1": 4, "outputs": 4, "near_sum_0": 8,
    "far_end_1": 3, "inputs": 1, "near_sum_1": 4, "near_join_0": 2, "near_join_1": 4, "far_join_0": 4,
}
FLOPS = 10**9


def dot(left, right):
    return jnp.dot(left, right, preferred_element_type=F32)


def across(left, right):
    return lax.dot_general(left, right, (((0,), (0,)), ((), ())), preferred_element_type=F32)


def against(left, weight):
    return lax.dot_general(left, weight, (((1,), (1,)), ((), ())), preferred_element_type=F32)


def column(lines):
    turned = lines.astype(F32).T
    return jnp.concatenate([turned[:, k : k + 1] for k in range(lines.shape[0])], axis=0)


def row(lines):
    return jnp.concatenate([lines[k : k + 1] for k in range(lines.shape[0])], axis=1)


def tap_of(lines):
    return jnp.where(lines >= DILATION_STEP, 1, 0)


def lines_of(ref, rows):
    return ref[rows.start // LANES : rows.stop // LANES, :]


def picked(head, rest, rows):
    cut = DILATION_STEP
    low = head[rows.start : min(rows.stop, cut), :] if rows.start < cut else None
    high = rest[max(rows.start, cut) - cut : rows.stop - cut, :] if rows.stop > cut else None
    if low is None:
        return high
    return low if high is None else jnp.concatenate([low, high], axis=0)


def call(kernel, name, in_specs, out_specs, out_shape, scratch=(), aliases=None, grid=(), vmem=24):
    return pl.pallas_call(
        kernel,
        grid=grid,
        in_specs=in_specs,
        out_specs=out_specs,
        out_shape=out_shape,
        scratch_shapes=list(scratch),
        input_output_aliases=aliases or {},
        cost_estimate=pl.CostEstimate(
            flops=1 + int(FLOPS * COSTS.get(name, COSTS.get(name.split("_")[0], 0))), bytes_accessed=1, transcendentals=0
        ),
        name=name,
        compiler_params=pltpu.CompilerParams(vmem_limit_bytes=vmem * MEGA),
    )


VMEM = pl.BlockSpec(memory_space=pltpu.VMEM)
ANYWHERE = pl.BlockSpec(memory_space=pl.ANY)
MARK = jax.ShapeDtypeStruct((8, LANES), F32)


def beside(*parts):
    return jnp.concatenate(parts, axis=1)


def below(*parts):
    return jnp.concatenate(parts, axis=0)


def products(half, rows, x, feats, given, w_in, w_cond, b_conv, w_out, arrive=None):
    part = w_out.shape[0] // HALVES
    first = half * part
    made = []
    for k, at in enumerate((first, HALVES * part + first)):
        here = slice(at, at + part)
        if arrive:
            arrive(rows, k)
        made.append(dot(x, w_in[:, here]) + across(feats, w_cond[:, here]) + b_conv[:, here])
    if arrive:
        arrive(rows, 2)
    return *made, against(given[rows, :], w_out[first : first + part, :])


def finish(pre_a, pre_s, dgated, valid_lines):
    act = jnp.tanh(pre_a)
    gate = 0.5 + 0.5 * jnp.tanh(0.5 * pre_s)
    slope = (column(valid_lines) * dgated) * gate
    dpre = beside(slope * (1.0 - act * act), slope * act * (1.0 - gate)).astype(BF16)
    gated = (act * gate).astype(BF16)
    return gated, gated.T * row(valid_lines.astype(BF16)), dpre


def forward_tiles(half, tiles, prepare, arrive, valid, xs, x_turned, given, weights, gated_out, kept_out, dpre_out):
    cond = weights[1].shape[0]
    width = xs.shape[1] // 2

    def done(rows, *made):
        there = slice(rows.start - DILATION_STEP, rows.stop - DILATION_STEP)
        gated_out[there, :], kept_out[:, there], dpre_out[there, :] = finish(*made, lines_of(valid, rows))

    waiting = None
    for rows in tiles:
        if prepare:
            prepare(rows)
        feats = x_turned[2 * width : 2 * width + cond, rows]
        made = products(half, rows, xs[rows, :], feats, given, *weights, arrive=arrive)
        if waiting:
            done(*waiting)
        waiting = (rows, *made)
    done(*waiting)


def rest_rows(rows, tile=ROWS):
    cuts = sorted({DILATION_STEP, *range(tile, rows + 1, tile)})
    return [slice(a, b) for a, b in zip(cuts, cuts[1:])]


def load_body(
    valid, pos, b_conv, b_res, b_skip, feat, w_cond, w_res, w_skip, w_past, w_now, sig, gout, gskip,
    valid_to, pos_to, b_conv_to, b_res_to, b_skip_to, w_cond_to, w_out, w_in, xs, x_turned, given,
    gated_rest, kept_rest, dpre_rest, sems,
):
    rows_all, width = sig.shape
    skip_width = gskip.shape[1]
    cond = feat.shape[0]
    part = w_res.shape[0] // HALVES
    count = 0

    def start(source, target):
        nonlocal count
        copy = pltpu.make_async_copy(source, target, sems.at[count])
        copy.start()
        count += 1
        return copy

    def inner(half, at):
        here = pl.ds(at + half * part, part)
        return [start(ref.at[:, here], w_in.at[pl.ds(k * width, width), here]) for k, ref in enumerate((w_past, w_now))]

    def outer(half):
        here = pl.ds(half * part, part)
        return [
            start(w_res.at[here], w_out.at[here, pl.ds(0, width)]),
            start(w_skip.at[here], w_out.at[here, pl.ds(width, skip_width)]),
        ]

    def signals(i):
        rows = pl.ds(i * ROWS, ROWS)
        return [start(sig.at[rows], xs.at[rows, pl.ds(width, width)])]

    def cotangents(i):
        rows = pl.ds(i * ROWS, ROWS)
        return [
            start(gout.at[rows], given.at[rows, pl.ds(0, width)]),
            start(gskip.at[rows], given.at[rows, pl.ds(width, skip_width)]),
        ]

    here, given_here = {}, {}

    def tile(i):
        if i < rows_all // ROWS and i not in here:
            here[i], given_here[i] = signals(i), cotangents(i)

    here[0] = signals(0)
    needs = [
        [start(pos, pos_to)] + inner(0, 0) + [
            start(feat, x_turned.at[pl.ds(2 * width, cond)]), start(w_cond, w_cond_to), start(b_conv, b_conv_to)
        ],
        inner(0, HALVES * part),
        [start(valid, valid_to)] + outer(0),
    ]
    given_here[0] = cotangents(0)
    tile(1)
    last = []

    def wait(copies):
        for copy in copies:
            copy.wait()
        copies.clear()

    def prepare(rows):
        i = rows.start // ROWS
        wait(here[i])
        if i == 0:
            wait(needs[0])
        tile(i + 2)
        if i == 1:
            for at in (0, HALVES * part):
                last.extend(inner(1, at))
            last.extend(outer(1) + [start(b_res, b_res_to), start(b_skip, b_skip_to)])
        whole = slice(i * ROWS, (i + 1) * ROWS)
        before = slice(rows.start - DILATION_STEP, rows.stop - DILATION_STEP)
        tap = tap_of(lines_of(pos_to, rows)).astype(F32)
        xs[rows, :width] = xs[before, width:] * column(tap).astype(BF16)
        x_turned[width : 2 * width, whole] = xs[whole, width:].T
        x_turned[:width, rows] = x_turned[width : 2 * width, before] * row(tap).astype(BF16)

    def arrive(rows, k):
        wait(needs[k])
        if k == 2:
            wait(given_here[rows.start // ROWS])
            tile(rows.start // ROWS + 3)

    x_turned[2 * width + cond :, :] = jnp.ones((x_turned.shape[0] - 2 * width - cond, rows_all), BF16)
    forward_tiles(
        0, rest_rows(rows_all), prepare, arrive, valid_to, xs, x_turned, given, (w_in, w_cond_to, b_conv_to, w_out),
        gated_rest, kept_rest, dpre_rest,
    )
    wait(last)


def rest_shapes(rest, part):
    return [jax.ShapeDtypeStruct(shape, BF16) for shape in ((rest, part), (part, rest), (rest, 2 * part))]


def load(*arrays):
    sources = [in_hbm(x) for x in arrays]
    feat, w_cond, w_res, w_skip, w_past, w_now, sig, gout, gskip = arrays[5:]
    rows, width = sig.shape
    hidden = w_res.shape[0]
    wide = gout.shape[1] + gskip.shape[1]
    shapes = [jax.ShapeDtypeStruct(x.shape, x.dtype) for x in arrays[:5] + (w_cond,)] + [
        jax.ShapeDtypeStruct(shape, BF16)
        for shape in (
            (hidden, wide), (2 * width, 2 * hidden), (rows, 2 * width), (2 * width + feat.shape[0] + ONES, rows), (rows, wide),
        )
    ]
    shapes += rest_shapes(rows - DILATION_STEP, hidden // HALVES)
    return call(
        load_body,
        "load",
        [ANYWHERE] * len(sources),
        [VMEM] * len(shapes),
        shapes,
        scratch=[pltpu.SemaphoreType.DMA((7 + 6 * HALVES + 3 * (rows // ROWS),))],
    )(*sources)


def side_by_side(dpre_0, dpre_1):
    part = dpre_0.shape[1] // 2
    return beside(dpre_0[:, :part], dpre_1[:, :part], dpre_0[:, part:], dpre_1[:, part:])


def head_body(halo, pos, valid, xs, x_turned, given, w_in, w_cond, b_conv, w_out, past_out, *outs):
    rows = slice(0, DILATION_STEP)
    width = halo.shape[1]
    cond = w_cond.shape[0]
    tap = tap_of(lines_of(pos, rows)).astype(F32)
    past_out[...] = halo[...].T * row(tap).astype(BF16)
    x = beside(halo[...] * column(tap).astype(BF16), xs[rows, width:])
    feats = x_turned[2 * width : 2 * width + cond, rows]
    made = [products(half, rows, x, feats, given, w_in, w_cond, b_conv, w_out) for half in range(HALVES)]
    for half in range(HALVES):
        parts = finish(*made[half], lines_of(valid, rows))
        for ref, value in zip(outs[3 * half :], parts):
            ref[...] = value


def head(halo, *args):
    width = halo.shape[1]
    part = args[-1].shape[0] // HALVES
    past, *parts = call(
        head_body,
        "head",
        [VMEM] * (1 + len(args)),
        [VMEM] * (1 + 3 * HALVES),
        [jax.ShapeDtypeStruct((width, DILATION_STEP), BF16)] + rest_shapes(DILATION_STEP, part) * HALVES,
    )(halo, *args)
    return past, parts[:3], parts[3:]


def early_body(token, pos, dpre_0, dpre_1, w_in, early):
    tap = column(tap_of(lines_of(pos, slice(0, DILATION_STEP))))
    early[...] = (tap * against(side_by_side(dpre_0[...], dpre_1[...]), w_in[: early.shape[1], :])).astype(BF16)


def early_rows(token, pos, dpre_0, dpre_1, w_in):
    return call(
        early_body,
        "early",
        [ANYWHERE] + [VMEM] * 4,
        VMEM,
        jax.ShapeDtypeStruct((DILATION_STEP, w_in.shape[0] // 2), BF16),
    )(token, pos, dpre_0, dpre_1, w_in)


def forward_body(token, valid, xs, x_turned, given, w_in, w_cond, b_conv, w_out, gated_out, kept_out, dpre_out):
    forward_tiles(
        1, rest_rows(xs.shape[0], ROWS // 2), None, None, valid, xs, x_turned, given, (w_in, w_cond, b_conv, w_out),
        gated_out, kept_out, dpre_out,
    )


def forward_rest(token, *args):
    return call(
        forward_body,
        "forward_1",
        [ANYWHERE] + [VMEM] * len(args),
        [VMEM] * 3,
        rest_shapes(args[0].shape[0] * LANES - DILATION_STEP, args[-1].shape[0] // HALVES),
    )(token, *args)


def own_place():
    return [lax.axis_index(name) for name in ("core", "far", "near")]


def turned(index, count):
    bits = (count - 1).bit_length()
    result = 0
    for bit in range(bits):
        result = result | (((index >> bit) & 1) << (bits - 1 - bit))
    return result


def place_blocks(far, block, acc, theirs, mine):
    core, z, xy = own_place()
    for r in range(far):
        for c in range(NEAR):
            here = pl.ds(c * LANES, LANES)
            for k, out in ((1 - core, theirs), (core, mine)):
                rows = pl.ds(pl.multiple_of((k * far + r) * block, 16), block)
                out[c ^ xy, turned(r ^ z, far)] = acc[rows, here].astype(out.dtype)


def gradients_body(
    far, block, half, token, valid, x_turned, given, past_head, kept_head, kept_rest, dpre_head, dpre_rest,
    theirs, mine, acc,
):
    cut = DILATION_STEP
    width = past_head.shape[0]
    part = kept_head.shape[0]
    wide = dpre_rest.shape[1]
    mask = jnp.broadcast_to(row(valid[...].astype(F32)).astype(BF16), (ONES, valid.shape[0] * LANES))
    ends = x_turned.shape[0]
    outer = dot(below(kept_rest[...], mask[:, cut:]), given[cut:, :])
    outer += dot(below(kept_head[...], mask[:, :cut]), given[:cut, :])
    at = ends
    for k in range(2):
        acc[at : at + part, :] = outer[:part, k * width : (k + 1) * width]
        at += part
    acc[at : at + ONES, :] = outer[part:, half * width : (half + 1) * width]
    at += ONES
    acc[at:, :] = jnp.zeros((acc.shape[0] - at, wide), F32)
    inner = dot(x_turned[:, cut:], dpre_rest[...])
    inner += dot(below(past_head[...], x_turned[width:, :cut]), dpre_head[...])
    acc[:ends, :] = inner
    place_blocks(far, block, acc, theirs, mine)


def gradients(half, token, far, block, valid, x_turned, given, past_head, head_parts, rest_parts):
    packed = (NEAR, far, block, LANES)
    wide = rest_parts[2].shape[1]
    return call(
        functools.partial(gradients_body, far, block, half),
        f"gradients_{half}",
        [ANYWHERE] + [VMEM] * 8,
        [VMEM] * 2,
        [jax.ShapeDtypeStruct(packed, BF16), jax.ShapeDtypeStruct(packed, F32)],
        scratch=[pltpu.VMEM((2 * far * block, wide), F32)],
    )(token, valid, x_turned, given, past_head, head_parts[1], rest_parts[1], head_parts[2], rest_parts[2])


def outputs_body(token, valid, xs, head_0, rest_0, head_1, rest_1, w_out, b_res, b_skip, out, skip, mark, rooms, sems):
    width = xs.shape[1] // 2
    copies = []
    for i in range(xs.shape[0] // ROWS):
        rows = slice(i * ROWS, (i + 1) * ROWS)
        mask = column(lines_of(valid, rows))
        gated = beside(picked(head_0, rest_0, rows), picked(head_1, rest_1, rows))
        branch = dot(gated, w_out[:, :width]) + b_res[...]
        rooms[i, 0] = (xs[rows, width:].astype(F32) + mask * branch).astype(BF16)
        side = dot(gated, w_out[:, width:]) + b_skip[...]
        rooms[i, 1] = (mask * side).astype(BF16)
        for k, ref in enumerate((out, skip)):
            copies.append(pltpu.make_async_copy(rooms.at[i, k], ref.at[pl.ds(i * ROWS, ROWS)], sems.at[i, k]))
            copies[-1].start()
    mark[...] = jnp.zeros_like(mark)
    for copy in copies:
        copy.wait()


def outputs(token, valid, xs, gated_0, gated_1, w_out, b_res, b_skip):
    rows, width = xs.shape[0], xs.shape[1] // 2
    return call(
        outputs_body,
        "outputs",
        [ANYWHERE] + [VMEM] * 9,
        [ANYWHERE, ANYWHERE, VMEM],
        [
            jax.ShapeDtypeStruct((rows, width), BF16),
            jax.ShapeDtypeStruct((rows, w_out.shape[1] - width), BF16),
            MARK,
        ],
        scratch=[
            pltpu.VMEM((rows // ROWS, 2, ROWS, width), BF16),
            pltpu.SemaphoreType.DMA((rows // ROWS, 2)),
        ],
    )(token, valid, xs, *gated_0, *gated_1, w_out, b_res, b_skip)


def inputs_body(steps, token, received, given, pos, head_0, rest_0, head_1, rest_1, w_in, w_cond, *refs):
    gsig, gfeat, mark, room, room_feat, sems = refs[-6:]
    rows, width = given.shape[0], w_in.shape[0] // 2
    copies = []
    wide = 2 * LANES

    def copy(source, target):
        copies.append(pltpu.make_async_copy(source, target, sems.at[len(copies)]))
        copies[-1].start()

    for i, step in enumerate(steps):
        begin = step * ROWS
        here = slice(begin, begin + ROWS)
        after = slice(begin + DILATION_STEP, min(begin + DILATION_STEP + ROWS, rows))
        now = side_by_side(picked(head_0, rest_0, here), picked(head_1, rest_1, here))
        later = side_by_side(picked(head_0, rest_0, after), picked(head_1, rest_1, after))
        tap = column(tap_of(lines_of(pos, after)))
        room_feat[i] = against(w_cond[...], now)
        copy(room_feat.at[i], gfeat.at[:, pl.ds(begin, ROWS)])
        for k in range(width // wide):
            some = slice(k * wide, (k + 1) * wide)
            tail = tap * against(later, w_in[some, :])
            if tail.shape[0] < ROWS:
                tail = below(tail, received[:, some].astype(F32))
            room[i, k] = given[here, some].astype(F32) + against(now, w_in[width + k * wide : width + (k + 1) * wide, :]) + tail
            copy(room.at[i, k], gsig.at[pl.ds(begin, ROWS), pl.ds(k * wide, wide)])
    mark[...] = jnp.zeros_like(mark)
    for one in copies:
        one.wait()


def inputs(steps, token, received, given, pos, dpre_0, dpre_1, w_in, w_cond, before):
    rows, width = given.shape[0], w_in.shape[0] // 2
    cond = w_cond.shape[0]
    count = width // (2 * LANES)
    return call(
        functools.partial(inputs_body, steps),
        f"inputs_{steps[0]}",
        [ANYWHERE] + [VMEM] * 9 + [ANYWHERE] * len(before),
        [ANYWHERE, ANYWHERE, VMEM],
        [
            jax.ShapeDtypeStruct((rows, width), F32),
            jax.ShapeDtypeStruct((cond, rows), F32),
            MARK,
        ],
        scratch=[
            pltpu.VMEM((len(steps), count, ROWS, 2 * LANES), F32),
            pltpu.VMEM((len(steps), cond, ROWS), F32),
            pltpu.SemaphoreType.DMA((len(steps) * (count + 1),)),
        ],
        aliases={10 + k: k for k in range(len(before))},
    )(token, received, given, pos, *dpre_0, *dpre_1, w_in, w_cond, *before)


def unpack_body(far, block, token, mine, theirs, *refs):
    arrays, (mark, room) = refs[-9:-2], refs[-2:]
    mark[...] = jnp.zeros_like(mark)
    core, z, xy = own_place()

    @pl.when(pl.program_id(0) == 0)
    def _():
        for k, ref in ((core, mine), (1 - core, theirs)):
            for c in range(NEAR):
                for r in range(far):
                    rows = pl.ds(pl.multiple_of((k * far + (r ^ z)) * block, 16), block)
                    room[c ^ xy, rows, :] = ref[c, turned(r, far)]

    for j in range(NEAR // 2):
        c = pl.program_id(0) * (NEAR // 2) + j
        here = pl.ds(j * LANES, LANES)
        top = 0
        for ref in arrays:
            count = ref.shape[0]
            size = max(count, ONES)
            ref[:, here] = room[c, top : top + size, :].astype(F32)[:count]
            top += size


def unpack(half, token, far, block, mine, theirs, width, cond, hidden, skip_width, before):
    part = hidden // HALVES
    gates = 2 * hidden
    own = (width, skip_width)[half]

    def wide(size):
        return pl.BlockSpec((size, part), lambda s: (0, HALVES * s + half))

    def tall(size):
        return pl.BlockSpec((part, size // 2), lambda s: (half, s))

    specs = [wide(width), wide(width), wide(cond), wide(1), tall(width), tall(skip_width), pl.BlockSpec((1, own // 2), lambda s: (0, s))]
    shapes = [(width, gates), (width, gates), (cond, gates), (1, gates), (hidden, width), (hidden, skip_width), (1, own)]
    packed = (NEAR, far, block, LANES)
    blocks = pl.BlockSpec(packed, lambda s: (0,) * len(packed))
    return call(
        functools.partial(unpack_body, far, block),
        f"unpack_{half}",
        [ANYWHERE, blocks, blocks] + [ANYWHERE] * len(before),
        specs + [pl.BlockSpec(MARK.shape, lambda s: (0, 0))],
        [jax.ShapeDtypeStruct(shape, F32) for shape in shapes] + [MARK],
        scratch=[pltpu.VMEM((NEAR, 2 * far * block, LANES), BF16)],
        aliases={3 + k: k for k in range(len(before))},
        grid=(2,),
    )(token, mine, theirs, *before)


def swapped(x, axis, k):
    return lax.ppermute(x, axis, [(i, i ^ k) for i in range(lax.axis_size(axis))])


def exchanged(blocks):
    return [swapped(block, "near", k + 1) for k, block in enumerate(blocks)]


def add_body(sizes, token, *refs):
    count = len(sizes)
    kept, got, outs = refs[0], refs[1:-count], refs[-count:]
    at = 0
    for out, size in zip(outs, sizes):
        for k in range(size):
            total = kept[at + k].astype(F32)
            for ref in got:
                total = total + ref[at + k].astype(F32)
            out[k] = total.astype(out.dtype)
        at += size


def added(name, token, kept, got, outs):
    sizes = [size for size, _ in outs]
    result = call(
        functools.partial(add_body, sizes),
        name,
        [ANYWHERE] + [VMEM] * (1 + len(got)),
        [VMEM] * len(outs),
        [jax.ShapeDtypeStruct((size, *kept.shape[1:]), dtype) for size, dtype in outs],
    )(token, kept, *got)
    return result


def mirror_body(token, mine, got, out):
    count = mine.shape[0]
    for k in range(count):
        out[k] = (mine[k].astype(F32) + got[count - 1 - k].astype(F32)).astype(out.dtype)


def mirrored(name, token, mine, got):
    return call(
        mirror_body,
        name,
        [ANYWHERE, VMEM, VMEM],
        VMEM,
        jax.ShapeDtypeStruct(mine.shape, BF16),
    )(token, mine, got)


def join_body(token, *refs):
    out = refs[-1]
    at = 0
    for ref in refs[:-1]:
        out[at : at + ref.shape[0]] = ref[...]
        at += ref.shape[0]


def joined(name, token, parts):
    count = sum(part.shape[0] for part in parts)
    return call(
        join_body,
        name,
        [ANYWHERE] + [VMEM] * len(parts),
        VMEM,
        jax.ShapeDtypeStruct((count, *parts[0].shape[1:]), BF16),
    )(token, *parts)


def over_outer(total):
    for bit in range((lax.axis_size("outer") - 1).bit_length()):
        total = (total.astype(F32) + swapped(total, "outer", 1 << bit).astype(F32)).astype(BF16)
    return total


def passed_along(x, by):
    peers = lax.axis_size(AXES)
    pairs = [(i, i + by) for i in range(peers) if 0 <= i + by < peers]
    return lax.ppermute(x, AXES, pairs)


def in_hbm(x):
    return pltpu.with_memory_space_constraint(x, pltpu.HBM)


def body(
    signal,
    features,
    position,
    valid,
    w_past,
    w_now,
    b_conv,
    w_cond,
    w_res,
    b_res,
    w_skip,
    b_skip,
    grad_out,
    grad_skip,
):
    rows, width = signal.shape
    features = features.T
    cond = features.shape[0]
    hidden = w_res.shape[0]
    skip_width = w_skip.shape[1]
    far = lax.axis_size("far")
    far_bits = (far - 1).bit_length()
    used = 2 * width + cond + ONES + 2 * (hidden // HALVES) + ONES
    block = -(-used // (2 * far * 16)) * 16
    lines = (rows // LANES, LANES)
    pos, val = position.reshape(lines), valid.reshape(lines)
    b_conv, b_res, b_skip = (b.reshape(1, -1) for b in (b_conv, b_res, b_skip))

    def core_sum(half, token, theirs, mine):
        kept, *sent = added(
            f"core_sum_{half}", token, mine, [swapped(theirs, "core", 1)], [(1, F32)] + [(1, BF16)] * (NEAR - 1)
        )
        return kept[0], exchanged([x[0] for x in sent])

    def near_sum(half, token, kept, got):
        kept, sent = added(f"near_sum_{half}", token, kept, got, [(far // 2, F32), (far // 2, BF16)])
        return kept, swapped(sent, "far", 1)

    def far_sum(half, token, kept, got):
        for bit in range(1, far_bits - 1):
            size = kept.shape[0] // 2
            kept, sent = added(f"far_sum_{half}_{bit}", token, kept, [got], [(size, F32), (size, BF16)])
            got = swapped(sent, "far", 1 << bit)
        (mine,) = added(f"far_sum_{half}", token, kept, [got], [(kept.shape[0], BF16)])
        return mine, swapped(mine, "far", 1 << (far_bits - 1))

    def far_end(half, token, mine, got):
        total = over_outer(mirrored(f"far_end_{half}", token, mine, got))
        return total, swapped(total, "far", 1 << (far_bits - 2))

    def far_join(half, token, mine, got):
        total = joined(f"far_join_{half}", token, [mine, got])
        for bit in reversed(range(far_bits - 2)):
            total = joined(f"far_join_{half}_{bit}", token, [total, swapped(total, "far", 1 << bit)])
        return total, exchanged([total] * (NEAR - 1))

    def near_join(half, token, mine, got):
        total = joined(f"near_join_{half}", token, [mine[None]] + [x[None] for x in got])
        return total, swapped(total, "core", 1)

    def input_gradients(steps, token, before):
        last = (steps[-1] + 1) * ROWS == rows
        return inputs(steps, token, received if last else head_0[0], given, pos, dpre_0, dpre_1, w_in, w_cond, before)

    halo = passed_along(signal[rows - DILATION_STEP :], 1)
    val, pos, b_conv, b_res, b_skip, w_cond, w_out, w_in, xs, x_turned, given, *rest_0 = load(
        val, pos, b_conv, b_res, b_skip, features, w_cond, w_res, w_skip, w_past, w_now, signal, grad_out, grad_skip
    )
    common = (val, xs, x_turned, given, w_in, w_cond, b_conv, w_out)
    past_head, head_0, head_1 = head(halo, pos, *common)
    theirs_0, mine_0 = gradients(0, past_head, far, block, val, x_turned, given, past_head, head_0, rest_0)
    rest_1 = forward_rest(theirs_0, *common)
    dpre_0, dpre_1 = (head_0[2], rest_0[2]), (head_1[2], rest_1[2])
    kept_0, got_0 = core_sum(0, rest_1[0], theirs_0, mine_0)
    theirs_1, mine_1 = gradients(1, kept_0, far, block, val, x_turned, given, past_head, head_1, rest_1)
    output, skip_out, mark = outputs(
        theirs_1, val, xs, (head_0[0], rest_0[0]), (head_1[0], rest_1[0]), w_out, b_res, b_skip
    )
    kept_0, got_0 = near_sum(0, mark, kept_0, got_0)
    kept_1, got_1 = core_sum(1, kept_0, theirs_1, mine_1)
    *grads, mark = input_gradients((0, 1), kept_1, [])
    ends_0, got_0 = far_sum(0, mark, kept_0, got_0)
    *grads, mark = input_gradients((2,), ends_0, grads)
    kept_1, got_1 = near_sum(1, mark, kept_1, got_1)
    ends_0, got_0 = far_end(0, kept_1, ends_0, got_0)
    ends_1, got_1 = far_sum(1, ends_0, kept_1, got_1)
    ends_0, got_0 = far_join(0, ends_1, ends_0, got_0)
    ends_1, got_1 = far_end(1, ends_0, ends_1, got_1)
    early = early_rows(ends_1, pos, head_0[2], head_1[2], w_in)
    received = passed_along(early, -1)
    blocks_0, others_0 = near_join(0, early, ends_0, got_0)
    ends_1, got_1 = far_join(1, blocks_0, ends_1, got_1)
    *grads, mark = input_gradients((3,), ends_1, grads)
    blocks_1, others_1 = near_join(1, mark, ends_1, got_1)
    *done, own_0, mark = unpack(0, blocks_1, far, block, blocks_0, others_0, width, cond, hidden, skip_width, [])
    *done, own_1, _ = unpack(1, mark, far, block, blocks_1, others_1, width, cond, hidden, skip_width, done)
    g_past, g_now, g_cond, g_bias, g_res, g_skip = done
    grad_signal, grad_features = grads
    return (
        output,
        skip_out,
        grad_signal,
        grad_features.T,
        g_past,
        g_now,
        g_bias.reshape(-1),
        g_cond,
        g_res,
        own_0.reshape(-1),
        g_skip,
        own_1.reshape(-1),
    )


def solution(mesh):
    row, col = mesh.shape["row"], mesh.shape["col"]
    fine = Mesh(mesh.devices.reshape(row // 2, 2, col // NEAR, NEAR), AXES)
    rows = P(AXES, None)
    line = P(AXES)
    return jax.shard_map(
        body,
        mesh=fine,
        in_specs=(rows, rows, line, line) + (P(),) * 8 + (rows, rows),
        out_specs=(rows,) * 4 + (P(),) * 8,
        check_vma=False,
    )
```

```python
import functools

import jax
import jax.numpy as jnp
from jax import lax
from jax.experimental import pallas as pl
from jax.experimental.pallas import tpu as pltpu
from jax.sharding import Mesh
from jax.sharding import PartitionSpec as P

DILATION_STEP = 256
AXES = ("outer", "core", "far", "near")
HALVES = 2
NEAR = 4
LANES = 128
ROWS = 512
ONES = 16
F32 = jnp.float32
BF16 = jnp.bfloat16
MEGA = 1 << 20
COSTS = {
    "load": 8, "head": 2, "gradients_0": 0, "forward_1": 0, "gradients_1": 4, "outputs": 4, "near_sum_0": 8,
    "far_sum_0": 8, "near_sum_1": 4, "near_join_0": 2, "near_join_1": 4, "far_join_0": 4,
}
FLOPS = 10**9


def dot(left, right):
    return jnp.dot(left, right, preferred_element_type=F32)


def across(left, right):
    return lax.dot_general(left, right, (((0,), (0,)), ((), ())), preferred_element_type=F32)


def against(left, weight):
    return lax.dot_general(left, weight, (((1,), (1,)), ((), ())), preferred_element_type=F32)


def column(lines):
    turned = lines.astype(F32).T
    return jnp.concatenate([turned[:, k : k + 1] for k in range(lines.shape[0])], axis=0)


def row(lines):
    return jnp.concatenate([lines[k : k + 1] for k in range(lines.shape[0])], axis=1)


def tap_of(lines):
    return jnp.where(lines >= DILATION_STEP, 1, 0)


def lines_of(ref, rows):
    return ref[rows.start // LANES : rows.stop // LANES, :]


def picked(head, rest, rows):
    cut = DILATION_STEP
    low = head[rows.start : min(rows.stop, cut), :] if rows.start < cut else None
    high = rest[max(rows.start, cut) - cut : rows.stop - cut, :] if rows.stop > cut else None
    if low is None:
        return high
    return low if high is None else jnp.concatenate([low, high], axis=0)


def call(kernel, name, in_specs, out_specs, out_shape, scratch=(), aliases=None, grid=(), vmem=24):
    return pl.pallas_call(
        kernel,
        grid=grid,
        in_specs=in_specs,
        out_specs=out_specs,
        out_shape=out_shape,
        scratch_shapes=list(scratch),
        input_output_aliases=aliases or {},
        cost_estimate=pl.CostEstimate(
            flops=1 + int(FLOPS * COSTS.get(name, COSTS.get(name.split("_")[0], 0))), bytes_accessed=1, transcendentals=0
        ),
        name=name,
        compiler_params=pltpu.CompilerParams(vmem_limit_bytes=vmem * MEGA),
    )


VMEM = pl.BlockSpec(memory_space=pltpu.VMEM)
ANYWHERE = pl.BlockSpec(memory_space=pl.ANY)
MARK = jax.ShapeDtypeStruct((8, LANES), F32)


def beside(*parts):
    return jnp.concatenate(parts, axis=1)


def below(*parts):
    return jnp.concatenate(parts, axis=0)


def products(half, rows, x, feats, given, w_in, w_cond, b_conv, w_out, arrive=None):
    part = w_out.shape[0] // HALVES
    first = half * part
    made = []
    for k, at in enumerate((first, HALVES * part + first)):
        here = slice(at, at + part)
        if arrive:
            arrive(rows, k)
        made.append(dot(x, w_in[:, here]) + across(feats, w_cond[:, here]) + b_conv[:, here])
    if arrive:
        arrive(rows, 2)
    return *made, against(given[rows, :], w_out[first : first + part, :])


def finish(pre_a, pre_s, dgated, valid_lines):
    act = jnp.tanh(pre_a)
    gate = 0.5 + 0.5 * jnp.tanh(0.5 * pre_s)
    slope = (column(valid_lines) * dgated) * gate
    dpre = beside(slope * (1.0 - act * act), slope * act * (1.0 - gate)).astype(BF16)
    gated = (act * gate).astype(BF16)
    return gated, gated.T * row(valid_lines.astype(BF16)), dpre


def forward_tiles(half, tiles, prepare, arrive, valid, xs, x_turned, given, weights, gated_out, kept_out, dpre_out):
    cond = weights[1].shape[0]
    width = xs.shape[1] // 2

    def done(rows, *made):
        there = slice(rows.start - DILATION_STEP, rows.stop - DILATION_STEP)
        gated_out[there, :], kept_out[:, there], dpre_out[there, :] = finish(*made, lines_of(valid, rows))

    waiting = None
    for rows in tiles:
        if prepare:
            prepare(rows)
        feats = x_turned[2 * width : 2 * width + cond, rows]
        made = products(half, rows, xs[rows, :], feats, given, *weights, arrive=arrive)
        if waiting:
            done(*waiting)
        waiting = (rows, *made)
    done(*waiting)


def rest_rows(rows, tile=ROWS):
    cuts = sorted({DILATION_STEP, *range(tile, rows + 1, tile)})
    return [slice(a, b) for a, b in zip(cuts, cuts[1:])]


def load_body(
    valid, pos, b_conv, b_res, b_skip, feat, w_cond, w_res, w_skip, w_past, w_now, sig, gout, gskip,
    valid_to, pos_to, b_conv_to, b_res_to, b_skip_to, w_cond_to, w_out, w_in, xs, x_turned, given,
    gated_rest, kept_rest, dpre_rest, sems,
):
    rows_all, width = sig.shape
    skip_width = gskip.shape[1]
    cond = feat.shape[0]
    part = w_res.shape[0] // HALVES
    count = 0

    def start(source, target):
        nonlocal count
        copy = pltpu.make_async_copy(source, target, sems.at[count])
        copy.start()
        count += 1
        return copy

    def inner(half, at):
        here = pl.ds(at + half * part, part)
        return [start(ref.at[:, here], w_in.at[pl.ds(k * width, width), here]) for k, ref in enumerate((w_past, w_now))]

    def outer(half):
        here = pl.ds(half * part, part)
        return [
            start(w_res.at[here], w_out.at[here, pl.ds(0, width)]),
            start(w_skip.at[here], w_out.at[here, pl.ds(width, skip_width)]),
        ]

    def signals(i):
        rows = pl.ds(i * ROWS, ROWS)
        return [start(sig.at[rows], xs.at[rows, pl.ds(width, width)])]

    def cotangents(i):
        rows = pl.ds(i * ROWS, ROWS)
        return [
            start(gout.at[rows], given.at[rows, pl.ds(0, width)]),
            start(gskip.at[rows], given.at[rows, pl.ds(width, skip_width)]),
        ]

    here, given_here = {}, {}

    def tile(i):
        if i < rows_all // ROWS and i not in here:
            here[i], given_here[i] = signals(i), cotangents(i)

    here[0] = signals(0)
    needs = [
        [start(pos, pos_to)] + inner(0, 0) + [
            start(feat, x_turned.at[pl.ds(2 * width, cond)]), start(w_cond, w_cond_to), start(b_conv, b_conv_to)
        ],
        inner(0, HALVES * part),
        [start(valid, valid_to)] + outer(0),
    ]
    given_here[0] = cotangents(0)
    for i in range(1, rows_all // ROWS):
        tile(i)
    last = []

    def wait(copies):
        for copy in copies:
            copy.wait()
        copies.clear()

    def prepare(rows):
        i = rows.start // ROWS
        wait(here[i])
        if i == 0:
            wait(needs[0])
        if i == 1:
            for at in (0, HALVES * part):
                last.extend(inner(1, at))
            last.extend(outer(1) + [start(b_res, b_res_to), start(b_skip, b_skip_to)])
        whole = slice(i * ROWS, (i + 1) * ROWS)
        before = slice(rows.start - DILATION_STEP, rows.stop - DILATION_STEP)
        tap = tap_of(lines_of(pos_to, rows)).astype(F32)
        xs[rows, :width] = xs[before, width:] * column(tap).astype(BF16)
        x_turned[width : 2 * width, whole] = xs[whole, width:].T
        x_turned[:width, rows] = x_turned[width : 2 * width, before] * row(tap).astype(BF16)

    def arrive(rows, k):
        wait(needs[k])
        if k == 2:
            wait(given_here[rows.start // ROWS])

    x_turned[2 * width + cond :, :] = jnp.ones((x_turned.shape[0] - 2 * width - cond, rows_all), BF16)
    forward_tiles(
        0, rest_rows(rows_all), prepare, arrive, valid_to, xs, x_turned, given, (w_in, w_cond_to, b_conv_to, w_out),
        gated_rest, kept_rest, dpre_rest,
    )
    wait(last)


def rest_shapes(rest, part):
    return [jax.ShapeDtypeStruct(shape, BF16) for shape in ((rest, part), (part, rest), (rest, 2 * part))]


def load(*arrays):
    sources = [in_hbm(x) for x in arrays]
    feat, w_cond, w_res, w_skip, w_past, w_now, sig, gout, gskip = arrays[5:]
    rows, width = sig.shape
    hidden = w_res.shape[0]
    wide = gout.shape[1] + gskip.shape[1]
    shapes = [jax.ShapeDtypeStruct(x.shape, x.dtype) for x in arrays[:5] + (w_cond,)] + [
        jax.ShapeDtypeStruct(shape, BF16)
        for shape in (
            (hidden, wide), (2 * width, 2 * hidden), (rows, 2 * width), (2 * width + feat.shape[0] + ONES, rows), (rows, wide),
        )
    ]
    shapes += rest_shapes(rows - DILATION_STEP, hidden // HALVES)
    return call(
        load_body,
        "load",
        [ANYWHERE] * len(sources),
        [VMEM] * len(shapes),
        shapes,
        scratch=[pltpu.SemaphoreType.DMA((7 + 6 * HALVES + 3 * (rows // ROWS),))],
    )(*sources)


def side_by_side(dpre_0, dpre_1):
    part = dpre_0.shape[1] // 2
    return beside(dpre_0[:, :part], dpre_1[:, :part], dpre_0[:, part:], dpre_1[:, part:])


def head_body(halo, pos, valid, xs, x_turned, given, w_in, w_cond, b_conv, w_out, past_out, *outs):
    rows = slice(0, DILATION_STEP)
    width = halo.shape[1]
    cond = w_cond.shape[0]
    tap = tap_of(lines_of(pos, rows)).astype(F32)
    past_out[...] = halo[...].T * row(tap).astype(BF16)
    x = beside(halo[...] * column(tap).astype(BF16), xs[rows, width:])
    feats = x_turned[2 * width : 2 * width + cond, rows]
    made = [products(half, rows, x, feats, given, w_in, w_cond, b_conv, w_out) for half in range(HALVES)]
    for half in range(HALVES):
        parts = finish(*made[half], lines_of(valid, rows))
        for ref, value in zip(outs[3 * half :], parts):
            ref[...] = value


def head(halo, *args):
    width = halo.shape[1]
    part = args[-1].shape[0] // HALVES
    past, *parts = call(
        head_body,
        "head",
        [VMEM] * (1 + len(args)),
        [VMEM] * (1 + 3 * HALVES),
        [jax.ShapeDtypeStruct((width, DILATION_STEP), BF16)] + rest_shapes(DILATION_STEP, part) * HALVES,
    )(halo, *args)
    return past, parts[:3], parts[3:]


def early_body(token, pos, dpre_0, dpre_1, w_in, early):
    tap = column(tap_of(lines_of(pos, slice(0, DILATION_STEP))))
    early[...] = (tap * against(side_by_side(dpre_0[...], dpre_1[...]), w_in[: early.shape[1], :])).astype(BF16)


def early_rows(token, pos, dpre_0, dpre_1, w_in):
    return call(
        early_body,
        "early",
        [ANYWHERE] + [VMEM] * 4,
        VMEM,
        jax.ShapeDtypeStruct((DILATION_STEP, w_in.shape[0] // 2), BF16),
    )(token, pos, dpre_0, dpre_1, w_in)


def forward_body(token, valid, xs, x_turned, given, w_in, w_cond, b_conv, w_out, gated_out, kept_out, dpre_out):
    forward_tiles(
        1, rest_rows(xs.shape[0], ROWS // 2), None, None, valid, xs, x_turned, given, (w_in, w_cond, b_conv, w_out),
        gated_out, kept_out, dpre_out,
    )


def forward_rest(token, *args):
    return call(
        forward_body,
        "forward_1",
        [ANYWHERE] + [VMEM] * len(args),
        [VMEM] * 3,
        rest_shapes(args[0].shape[0] * LANES - DILATION_STEP, args[-1].shape[0] // HALVES),
    )(token, *args)


def own_place():
    return [lax.axis_index(name) for name in ("core", "far", "near")]


def turned(index, count):
    bits = (count - 1).bit_length()
    result = 0
    for bit in range(bits):
        result = result | (((index >> bit) & 1) << (bits - 1 - bit))
    return result


def place_blocks(far, block, acc, theirs, mine):
    core, z, xy = own_place()
    for r in range(far):
        for c in range(NEAR):
            here = pl.ds(c * LANES, LANES)
            for k, out in ((1 - core, theirs), (core, mine)):
                rows = pl.ds(pl.multiple_of((k * far + r) * block, 16), block)
                out[c ^ xy, turned(r ^ z, far)] = acc[rows, here].astype(out.dtype)


def gradients_body(
    far, block, half, token, valid, x_turned, given, past_head, kept_head, kept_rest, dpre_head, dpre_rest,
    theirs, mine, acc,
):
    cut = DILATION_STEP
    width = past_head.shape[0]
    part = kept_head.shape[0]
    wide = dpre_rest.shape[1]
    mask = jnp.broadcast_to(row(valid[...].astype(F32)).astype(BF16), (ONES, valid.shape[0] * LANES))
    ends = x_turned.shape[0]
    outer = dot(below(kept_rest[...], mask[:, cut:]), given[cut:, :])
    outer += dot(below(kept_head[...], mask[:, :cut]), given[:cut, :])
    at = ends
    for k in range(2):
        acc[at : at + part, :] = outer[:part, k * width : (k + 1) * width]
        at += part
    acc[at : at + ONES, :] = outer[part:, half * width : (half + 1) * width]
    at += ONES
    acc[at:, :] = jnp.zeros((acc.shape[0] - at, wide), F32)
    inner = dot(x_turned[:, cut:], dpre_rest[...])
    inner += dot(below(past_head[...], x_turned[width:, :cut]), dpre_head[...])
    acc[:ends, :] = inner
    place_blocks(far, block, acc, theirs, mine)


def gradients(half, token, far, block, valid, x_turned, given, past_head, head_parts, rest_parts):
    packed = (NEAR, far, block, LANES)
    wide = rest_parts[2].shape[1]
    return call(
        functools.partial(gradients_body, far, block, half),
        f"gradients_{half}",
        [ANYWHERE] + [VMEM] * 8,
        [VMEM] * 2,
        [jax.ShapeDtypeStruct(packed, BF16), jax.ShapeDtypeStruct(packed, F32)],
        scratch=[pltpu.VMEM((2 * far * block, wide), F32)],
    )(token, valid, x_turned, given, past_head, head_parts[1], rest_parts[1], head_parts[2], rest_parts[2])


def outputs_body(token, valid, xs, head_0, rest_0, head_1, rest_1, w_out, b_res, b_skip, out, skip, mark, rooms, sems):
    width = xs.shape[1] // 2
    copies = []
    for i in range(xs.shape[0] // ROWS):
        rows = slice(i * ROWS, (i + 1) * ROWS)
        mask = column(lines_of(valid, rows))
        gated = beside(picked(head_0, rest_0, rows), picked(head_1, rest_1, rows))
        branch = dot(gated, w_out[:, :width]) + b_res[...]
        rooms[i, 0] = (xs[rows, width:].astype(F32) + mask * branch).astype(BF16)
        side = dot(gated, w_out[:, width:]) + b_skip[...]
        rooms[i, 1] = (mask * side).astype(BF16)
        for k, ref in enumerate((out, skip)):
            copies.append(pltpu.make_async_copy(rooms.at[i, k], ref.at[pl.ds(i * ROWS, ROWS)], sems.at[i, k]))
            copies[-1].start()
    mark[...] = jnp.zeros_like(mark)
    for copy in copies:
        copy.wait()


def outputs(token, valid, xs, gated_0, gated_1, w_out, b_res, b_skip):
    rows, width = xs.shape[0], xs.shape[1] // 2
    return call(
        outputs_body,
        "outputs",
        [ANYWHERE] + [VMEM] * 9,
        [ANYWHERE, ANYWHERE, VMEM],
        [
            jax.ShapeDtypeStruct((rows, width), BF16),
            jax.ShapeDtypeStruct((rows, w_out.shape[1] - width), BF16),
            MARK,
        ],
        scratch=[
            pltpu.VMEM((rows // ROWS, 2, ROWS, width), BF16),
            pltpu.SemaphoreType.DMA((rows // ROWS, 2)),
        ],
    )(token, valid, xs, *gated_0, *gated_1, w_out, b_res, b_skip)


def inputs_body(steps, token, received, given, pos, head_0, rest_0, head_1, rest_1, w_in, w_cond, *refs):
    gsig, gfeat, mark, room, room_feat, sems = refs[-6:]
    rows, width = given.shape[0], w_in.shape[0] // 2
    copies = []
    wide = 2 * LANES

    def copy(source, target):
        copies.append(pltpu.make_async_copy(source, target, sems.at[len(copies)]))
        copies[-1].start()

    for i, step in enumerate(steps):
        begin = step * ROWS
        here = slice(begin, begin + ROWS)
        after = slice(begin + DILATION_STEP, min(begin + DILATION_STEP + ROWS, rows))
        now = side_by_side(picked(head_0, rest_0, here), picked(head_1, rest_1, here))
        later = side_by_side(picked(head_0, rest_0, after), picked(head_1, rest_1, after))
        tap = column(tap_of(lines_of(pos, after)))
        room_feat[i] = against(w_cond[...], now)
        copy(room_feat.at[i], gfeat.at[:, pl.ds(begin, ROWS)])
        for k in range(width // wide):
            some = slice(k * wide, (k + 1) * wide)
            tail = tap * against(later, w_in[some, :])
            if tail.shape[0] < ROWS:
                tail = below(tail, received[:, some].astype(F32))
            room[i, k] = given[here, some].astype(F32) + against(now, w_in[width + k * wide : width + (k + 1) * wide, :]) + tail
            copy(room.at[i, k], gsig.at[pl.ds(begin, ROWS), pl.ds(k * wide, wide)])
    mark[...] = jnp.zeros_like(mark)
    for one in copies:
        one.wait()


def inputs(steps, token, received, given, pos, dpre_0, dpre_1, w_in, w_cond, before):
    rows, width = given.shape[0], w_in.shape[0] // 2
    cond = w_cond.shape[0]
    count = width // (2 * LANES)
    return call(
        functools.partial(inputs_body, steps),
        f"inputs_{steps[0]}",
        [ANYWHERE] + [VMEM] * 9 + [ANYWHERE] * len(before),
        [ANYWHERE, ANYWHERE, VMEM],
        [
            jax.ShapeDtypeStruct((rows, width), F32),
            jax.ShapeDtypeStruct((cond, rows), F32),
            MARK,
        ],
        scratch=[
            pltpu.VMEM((len(steps), count, ROWS, 2 * LANES), F32),
            pltpu.VMEM((len(steps), cond, ROWS), F32),
            pltpu.SemaphoreType.DMA((len(steps) * (count + 1),)),
        ],
        aliases={10 + k: k for k in range(len(before))},
    )(token, received, given, pos, *dpre_0, *dpre_1, w_in, w_cond, *before)


def unpack_body(far, block, token, mine, theirs, *refs):
    arrays, (mark, room) = refs[-9:-2], refs[-2:]
    mark[...] = jnp.zeros_like(mark)
    core, z, xy = own_place()

    @pl.when(pl.program_id(0) == 0)
    def _():
        for k, ref in ((core, mine), (1 - core, theirs)):
            for c in range(NEAR):
                for r in range(far):
                    rows = pl.ds(pl.multiple_of((k * far + (r ^ z)) * block, 16), block)
                    room[c ^ xy, rows, :] = ref[c, turned(r, far)]

    for j in range(NEAR // 2):
        c = pl.program_id(0) * (NEAR // 2) + j
        here = pl.ds(j * LANES, LANES)
        top = 0
        for ref in arrays:
            count = ref.shape[0]
            size = max(count, ONES)
            ref[:, here] = room[c, top : top + size, :].astype(F32)[:count]
            top += size


def unpack(half, token, far, block, mine, theirs, width, cond, hidden, skip_width, before):
    part = hidden // HALVES
    gates = 2 * hidden
    own = (width, skip_width)[half]

    def wide(size):
        return pl.BlockSpec((size, part), lambda s: (0, HALVES * s + half))

    def tall(size):
        return pl.BlockSpec((part, size // 2), lambda s: (half, s))

    specs = [wide(width), wide(width), wide(cond), wide(1), tall(width), tall(skip_width), pl.BlockSpec((1, own // 2), lambda s: (0, s))]
    shapes = [(width, gates), (width, gates), (cond, gates), (1, gates), (hidden, width), (hidden, skip_width), (1, own)]
    packed = (NEAR, far, block, LANES)
    blocks = pl.BlockSpec(packed, lambda s: (0,) * len(packed))
    return call(
        functools.partial(unpack_body, far, block),
        f"unpack_{half}",
        [ANYWHERE, blocks, blocks] + [ANYWHERE] * len(before),
        specs + [pl.BlockSpec(MARK.shape, lambda s: (0, 0))],
        [jax.ShapeDtypeStruct(shape, F32) for shape in shapes] + [MARK],
        scratch=[pltpu.VMEM((NEAR, 2 * far * block, LANES), BF16)],
        aliases={3 + k: k for k in range(len(before))},
        grid=(2,),
    )(token, mine, theirs, *before)


def swapped(x, axis, k):
    return lax.ppermute(x, axis, [(i, i ^ k) for i in range(lax.axis_size(axis))])


def exchanged(blocks):
    return [swapped(block, "near", k + 1) for k, block in enumerate(blocks)]


def add_body(sizes, token, *refs):
    count = len(sizes)
    kept, got, outs = refs[0], refs[1:-count], refs[-count:]
    at = 0
    for out, size in zip(outs, sizes):
        for k in range(size):
            total = kept[at + k].astype(F32)
            for ref in got:
                total = total + ref[at + k].astype(F32)
            out[k] = total.astype(out.dtype)
        at += size


def added(name, token, kept, got, outs):
    sizes = [size for size, _ in outs]
    result = call(
        functools.partial(add_body, sizes),
        name,
        [ANYWHERE] + [VMEM] * (1 + len(got)),
        [VMEM] * len(outs),
        [jax.ShapeDtypeStruct((size, *kept.shape[1:]), dtype) for size, dtype in outs],
    )(token, kept, *got)
    return result


def mirror_body(token, mine, got, out):
    count = mine.shape[0]
    for k in range(count):
        out[k] = (mine[k].astype(F32) + got[count - 1 - k].astype(F32)).astype(out.dtype)


def mirrored(name, token, mine, got):
    return call(
        mirror_body,
        name,
        [ANYWHERE, VMEM, VMEM],
        VMEM,
        jax.ShapeDtypeStruct(mine.shape, BF16),
    )(token, mine, got)


def join_body(token, *refs):
    out = refs[-1]
    at = 0
    for ref in refs[:-1]:
        out[at : at + ref.shape[0]] = ref[...]
        at += ref.shape[0]


def joined(name, token, parts):
    count = sum(part.shape[0] for part in parts)
    return call(
        join_body,
        name,
        [ANYWHERE] + [VMEM] * len(parts),
        VMEM,
        jax.ShapeDtypeStruct((count, *parts[0].shape[1:]), BF16),
    )(token, *parts)


def over_outer(total):
    for bit in range((lax.axis_size("outer") - 1).bit_length()):
        total = (total.astype(F32) + swapped(total, "outer", 1 << bit).astype(F32)).astype(BF16)
    return total


def passed_along(x, by):
    peers = lax.axis_size(AXES)
    pairs = [(i, i + by) for i in range(peers) if 0 <= i + by < peers]
    return lax.ppermute(x, AXES, pairs)


def in_hbm(x):
    return pltpu.with_memory_space_constraint(x, pltpu.HBM)


def body(
    signal,
    features,
    position,
    valid,
    w_past,
    w_now,
    b_conv,
    w_cond,
    w_res,
    b_res,
    w_skip,
    b_skip,
    grad_out,
    grad_skip,
):
    rows, width = signal.shape
    features = features.T
    cond = features.shape[0]
    hidden = w_res.shape[0]
    skip_width = w_skip.shape[1]
    far = lax.axis_size("far")
    far_bits = (far - 1).bit_length()
    used = 2 * width + cond + ONES + 2 * (hidden // HALVES) + ONES
    block = -(-used // (2 * far * 16)) * 16
    lines = (rows // LANES, LANES)
    pos, val = position.reshape(lines), valid.reshape(lines)
    b_conv, b_res, b_skip = (b.reshape(1, -1) for b in (b_conv, b_res, b_skip))

    def core_sum(half, token, theirs, mine):
        kept, *sent = added(
            f"core_sum_{half}", token, mine, [swapped(theirs, "core", 1)], [(1, F32)] + [(1, BF16)] * (NEAR - 1)
        )
        return kept[0], exchanged([x[0] for x in sent])

    def near_sum(half, token, kept, got):
        kept, sent = added(f"near_sum_{half}", token, kept, got, [(far // 2, F32), (far // 2, BF16)])
        return kept, swapped(sent, "far", 1)

    def far_sum(half, token, kept, got):
        for bit in range(1, far_bits - 1):
            size = kept.shape[0] // 2
            kept, sent = added(f"far_sum_{half}_{bit}", token, kept, [got], [(size, F32), (size, BF16)])
            got = swapped(sent, "far", 1 << bit)
        (mine,) = added(f"far_sum_{half}", token, kept, [got], [(kept.shape[0], BF16)])
        return mine, swapped(mine, "far", 1 << (far_bits - 1))

    def far_end(half, token, mine, got):
        total = over_outer(mirrored(f"far_end_{half}", token, mine, got))
        return total, swapped(total, "far", 1 << (far_bits - 2))

    def far_join(half, token, mine, got):
        total = joined(f"far_join_{half}", token, [mine, got])
        for bit in reversed(range(far_bits - 2)):
            total = joined(f"far_join_{half}_{bit}", token, [total, swapped(total, "far", 1 << bit)])
        return total, exchanged([total] * (NEAR - 1))

    def near_join(half, token, mine, got):
        total = joined(f"near_join_{half}", token, [mine[None]] + [x[None] for x in got])
        return total, swapped(total, "core", 1)

    def input_gradients(steps, token, before):
        last = (steps[-1] + 1) * ROWS == rows
        return inputs(steps, token, received if last else head_0[0], given, pos, dpre_0, dpre_1, w_in, w_cond, before)

    halo = passed_along(signal[rows - DILATION_STEP :], 1)
    val, pos, b_conv, b_res, b_skip, w_cond, w_out, w_in, xs, x_turned, given, *rest_0 = load(
        val, pos, b_conv, b_res, b_skip, features, w_cond, w_res, w_skip, w_past, w_now, signal, grad_out, grad_skip
    )
    common = (val, xs, x_turned, given, w_in, w_cond, b_conv, w_out)
    past_head, head_0, head_1 = head(halo, pos, *common)
    theirs_0, mine_0 = gradients(0, past_head, far, block, val, x_turned, given, past_head, head_0, rest_0)
    rest_1 = forward_rest(theirs_0, *common)
    dpre_0, dpre_1 = (head_0[2], rest_0[2]), (head_1[2], rest_1[2])
    kept_0, got_0 = core_sum(0, rest_1[0], theirs_0, mine_0)
    theirs_1, mine_1 = gradients(1, kept_0, far, block, val, x_turned, given, past_head, head_1, rest_1)
    output, skip_out, mark = outputs(
        theirs_1, val, xs, (head_0[0], rest_0[0]), (head_1[0], rest_1[0]), w_out, b_res, b_skip
    )
    kept_0, got_0 = near_sum(0, mark, kept_0, got_0)
    kept_1, got_1 = core_sum(1, kept_0, theirs_1, mine_1)
    ends_0, got_0 = far_sum(0, kept_1, kept_0, got_0)
    *grads, mark = input_gradients((0, 1), ends_0, [])
    ends_0, got_0 = far_end(0, mark, ends_0, got_0)
    kept_1, got_1 = near_sum(1, ends_0, kept_1, got_1)
    ends_0, got_0 = far_join(0, kept_1, ends_0, got_0)
    ends_1, got_1 = far_sum(1, ends_0, kept_1, got_1)
    *grads, mark = input_gradients((2,), ends_1, grads)
    ends_1, got_1 = far_end(1, mark, ends_1, got_1)
    early = early_rows(ends_1, pos, head_0[2], head_1[2], w_in)
    received = passed_along(early, -1)
    blocks_0, others_0 = near_join(0, early, ends_0, got_0)
    ends_1, got_1 = far_join(1, blocks_0, ends_1, got_1)
    *grads, mark = input_gradients((3,), ends_1, grads)
    blocks_1, others_1 = near_join(1, mark, ends_1, got_1)
    *done, own_0, mark = unpack(0, blocks_1, far, block, blocks_0, others_0, width, cond, hidden, skip_width, [])
    *done, own_1, _ = unpack(1, mark, far, block, blocks_1, others_1, width, cond, hidden, skip_width, done)
    g_past, g_now, g_cond, g_bias, g_res, g_skip = done
    grad_signal, grad_features = grads
    return (
        output,
        skip_out,
        grad_signal,
        grad_features.T,
        g_past,
        g_now,
        g_bias.reshape(-1),
        g_cond,
        g_res,
        own_0.reshape(-1),
        g_skip,
        own_1.reshape(-1),
    )


def solution(mesh):
    row, col = mesh.shape["row"], mesh.shape["col"]
    fine = Mesh(mesh.devices.reshape(row // 2, 2, col // NEAR, NEAR), AXES)
    rows = P(AXES, None)
    line = P(AXES)
    return jax.shard_map(
        body,
        mesh=fine,
        in_specs=(rows, rows, line, line) + (P(),) * 8 + (rows, rows),
        out_specs=(rows,) * 4 + (P(),) * 8,
        check_vma=False,
    )
```

```python
import functools

import jax
import jax.numpy as jnp
from jax import lax
from jax.experimental import pallas as pl
from jax.experimental.pallas import tpu as pltpu
from jax.sharding import Mesh
from jax.sharding import PartitionSpec as P

DILATION_STEP = 256
AXES = ("outer", "core", "far", "near")
HALVES = 2
NEAR = 4
LANES = 128
ROWS = 512
ONES = 16
F32 = jnp.float32
BF16 = jnp.bfloat16
MEGA = 1 << 20
COSTS = {
    "load": 8, "head": 2, "gradients_0": 0, "forward_1": 0, "gradients_1": 4, "outputs": 4, "near_sum_0": 8,
    "far_sum_0": 8, "near_sum_1": 4, "near_join_0": 2, "near_join_1": 4, "far_join_0": 4,
}
FLOPS = 10**9


def dot(left, right):
    return jnp.dot(left, right, preferred_element_type=F32)


def across(left, right):
    return lax.dot_general(left, right, (((0,), (0,)), ((), ())), preferred_element_type=F32)


def against(left, weight):
    return lax.dot_general(left, weight, (((1,), (1,)), ((), ())), preferred_element_type=F32)


def column(lines):
    turned = lines.astype(F32).T
    return jnp.concatenate([turned[:, k : k + 1] for k in range(lines.shape[0])], axis=0)


def row(lines):
    return jnp.concatenate([lines[k : k + 1] for k in range(lines.shape[0])], axis=1)


def tap_of(lines):
    return jnp.where(lines >= DILATION_STEP, 1, 0)


def lines_of(ref, rows):
    return ref[rows.start // LANES : rows.stop // LANES, :]


def picked(head, rest, rows):
    cut = DILATION_STEP
    low = head[rows.start : min(rows.stop, cut), :] if rows.start < cut else None
    high = rest[max(rows.start, cut) - cut : rows.stop - cut, :] if rows.stop > cut else None
    if low is None:
        return high
    return low if high is None else jnp.concatenate([low, high], axis=0)


def call(kernel, name, in_specs, out_specs, out_shape, scratch=(), aliases=None, grid=(), vmem=24):
    return pl.pallas_call(
        kernel,
        grid=grid,
        in_specs=in_specs,
        out_specs=out_specs,
        out_shape=out_shape,
        scratch_shapes=list(scratch),
        input_output_aliases=aliases or {},
        cost_estimate=pl.CostEstimate(
            flops=1 + int(FLOPS * COSTS.get(name, COSTS.get(name.split("_")[0], 0))), bytes_accessed=1, transcendentals=0
        ),
        name=name,
        compiler_params=pltpu.CompilerParams(vmem_limit_bytes=vmem * MEGA),
    )


VMEM = pl.BlockSpec(memory_space=pltpu.VMEM)
ANYWHERE = pl.BlockSpec(memory_space=pl.ANY)
MARK = jax.ShapeDtypeStruct((8, LANES), F32)


def beside(*parts):
    return jnp.concatenate(parts, axis=1)


def below(*parts):
    return jnp.concatenate(parts, axis=0)


def products(half, rows, x, feats, given, w_in, w_cond, b_conv, w_out, arrive=None):
    part = w_out.shape[0] // HALVES
    first = half * part
    made = []
    for k, at in enumerate((first, HALVES * part + first)):
        here = slice(at, at + part)
        if arrive:
            arrive(rows, k)
        made.append(dot(x, w_in[:, here]) + across(feats, w_cond[:, here]) + b_conv[:, here])
    if arrive:
        arrive(rows, 2)
    return *made, against(given[rows, :], w_out[first : first + part, :])


def finish(pre_a, pre_s, dgated, valid_lines):
    act = jnp.tanh(pre_a)
    gate = 0.5 + 0.5 * jnp.tanh(0.5 * pre_s)
    slope = (column(valid_lines) * dgated) * gate
    dpre = beside(slope * (1.0 - act * act), slope * act * (1.0 - gate)).astype(BF16)
    gated = (act * gate).astype(BF16)
    return gated, gated.T * row(valid_lines.astype(BF16)), dpre


def forward_tiles(half, tiles, prepare, arrive, valid, xs, x_turned, given, weights, gated_out, kept_out, dpre_out):
    cond = weights[1].shape[0]
    width = xs.shape[1] // 2

    def done(rows, *made):
        there = slice(rows.start - DILATION_STEP, rows.stop - DILATION_STEP)
        gated_out[there, :], kept_out[:, there], dpre_out[there, :] = finish(*made, lines_of(valid, rows))

    waiting = None
    for rows in tiles:
        if prepare:
            prepare(rows)
        feats = x_turned[2 * width : 2 * width + cond, rows]
        made = products(half, rows, xs[rows, :], feats, given, *weights, arrive=arrive)
        if waiting:
            done(*waiting)
        waiting = (rows, *made)
    done(*waiting)


def rest_rows(rows, tile=ROWS):
    cuts = sorted({DILATION_STEP, *range(tile, rows + 1, tile)})
    return [slice(a, b) for a, b in zip(cuts, cuts[1:])]


def load_body(
    valid, pos, b_conv, b_res, b_skip, feat, w_cond, w_res, w_skip, w_past, w_now, sig, gout, gskip,
    valid_to, pos_to, b_conv_to, b_res_to, b_skip_to, w_cond_to, w_out, w_in, xs, x_turned, given,
    gated_rest, kept_rest, dpre_rest, sems,
):
    rows_all, width = sig.shape
    skip_width = gskip.shape[1]
    cond = feat.shape[0]
    part = w_res.shape[0] // HALVES
    count = 0

    def start(source, target):
        nonlocal count
        copy = pltpu.make_async_copy(source, target, sems.at[count])
        copy.start()
        count += 1
        return copy

    def inner(half, at):
        here = pl.ds(at + half * part, part)
        return [start(ref.at[:, here], w_in.at[pl.ds(k * width, width), here]) for k, ref in enumerate((w_past, w_now))]

    def outer(half):
        here = pl.ds(half * part, part)
        return [
            start(w_res.at[here], w_out.at[here, pl.ds(0, width)]),
            start(w_skip.at[here], w_out.at[here, pl.ds(width, skip_width)]),
        ]

    def signals(i):
        rows = pl.ds(i * ROWS, ROWS)
        return [start(sig.at[rows], xs.at[rows, pl.ds(width, width)])]

    def cotangents(i):
        rows = pl.ds(i * ROWS, ROWS)
        return [
            start(gout.at[rows], given.at[rows, pl.ds(0, width)]),
            start(gskip.at[rows], given.at[rows, pl.ds(width, skip_width)]),
        ]

    here, given_here = {}, {}

    def tile(i):
        if i < rows_all // ROWS and i not in here:
            here[i], given_here[i] = signals(i), cotangents(i)

    here[0] = signals(0)
    needs = [
        [start(pos, pos_to)] + inner(0, 0) + [
            start(feat, x_turned.at[pl.ds(2 * width, cond)]), start(w_cond, w_cond_to), start(b_conv, b_conv_to)
        ],
        inner(0, HALVES * part),
        [start(valid, valid_to)] + outer(0),
    ]
    given_here[0] = cotangents(0)
    for i in range(1, rows_all // ROWS):
        tile(i)
    last = []

    def wait(copies):
        for copy in copies:
            copy.wait()
        copies.clear()

    def prepare(rows):
        i = rows.start // ROWS
        wait(here[i])
        if i == 0:
            wait(needs[0])
        if i == 1:
            for at in (0, HALVES * part):
                last.extend(inner(1, at))
            last.extend(outer(1) + [start(b_res, b_res_to), start(b_skip, b_skip_to)])
        whole = slice(i * ROWS, (i + 1) * ROWS)
        before = slice(rows.start - DILATION_STEP, rows.stop - DILATION_STEP)
        tap = tap_of(lines_of(pos_to, rows)).astype(F32)
        xs[rows, :width] = xs[before, width:] * column(tap).astype(BF16)
        x_turned[width : 2 * width, whole] = xs[whole, width:].T
        x_turned[:width, rows] = x_turned[width : 2 * width, before] * row(tap).astype(BF16)

    def arrive(rows, k):
        wait(needs[k])
        if k == 2:
            wait(given_here[rows.start // ROWS])

    x_turned[2 * width + cond :, :] = jnp.ones((x_turned.shape[0] - 2 * width - cond, rows_all), BF16)
    forward_tiles(
        0, rest_rows(rows_all), prepare, arrive, valid_to, xs, x_turned, given, (w_in, w_cond_to, b_conv_to, w_out),
        gated_rest, kept_rest, dpre_rest,
    )
    wait(last)


def rest_shapes(rest, part):
    return [jax.ShapeDtypeStruct(shape, BF16) for shape in ((rest, part), (part, rest), (rest, 2 * part))]


def load(*arrays):
    sources = [in_hbm(x) for x in arrays]
    feat, w_cond, w_res, w_skip, w_past, w_now, sig, gout, gskip = arrays[5:]
    rows, width = sig.shape
    hidden = w_res.shape[0]
    wide = gout.shape[1] + gskip.shape[1]
    shapes = [jax.ShapeDtypeStruct(x.shape, x.dtype) for x in arrays[:5] + (w_cond,)] + [
        jax.ShapeDtypeStruct(shape, BF16)
        for shape in (
            (hidden, wide), (2 * width, 2 * hidden), (rows, 2 * width), (2 * width + feat.shape[0] + ONES, rows), (rows, wide),
        )
    ]
    shapes += rest_shapes(rows - DILATION_STEP, hidden // HALVES)
    return call(
        load_body,
        "load",
        [ANYWHERE] * len(sources),
        [VMEM] * len(shapes),
        shapes,
        scratch=[pltpu.SemaphoreType.DMA((7 + 6 * HALVES + 3 * (rows // ROWS),))],
    )(*sources)


def side_by_side(dpre_0, dpre_1):
    part = dpre_0.shape[1] // 2
    return beside(dpre_0[:, :part], dpre_1[:, :part], dpre_0[:, part:], dpre_1[:, part:])


def head_body(halo, pos, valid, xs, x_turned, given, w_in, w_cond, b_conv, w_out, past_out, early, *outs):
    rows = slice(0, DILATION_STEP)
    width = halo.shape[1]
    cond = w_cond.shape[0]
    tap = tap_of(lines_of(pos, rows)).astype(F32)
    past_out[...] = halo[...].T * row(tap).astype(BF16)
    x = beside(halo[...] * column(tap).astype(BF16), xs[rows, width:])
    feats = x_turned[2 * width : 2 * width + cond, rows]
    dpres = []
    made = [products(half, rows, x, feats, given, w_in, w_cond, b_conv, w_out) for half in range(HALVES)]
    for half in range(HALVES):
        parts = finish(*made[half], lines_of(valid, rows))
        for ref, value in zip(outs[3 * half :], parts):
            ref[...] = value
        dpres.append(parts[2])
    early[...] = (column(tap) * against(side_by_side(*dpres), w_in[:width, :])).astype(BF16)


def head(halo, *args):
    width = halo.shape[1]
    part = args[-1].shape[0] // HALVES
    shapes = [jax.ShapeDtypeStruct(shape, BF16) for shape in ((width, DILATION_STEP), (DILATION_STEP, width))]
    past, early, *parts = call(
        head_body,
        "head",
        [VMEM] * (1 + len(args)),
        [VMEM] * (2 + 3 * HALVES),
        shapes + rest_shapes(DILATION_STEP, part) * HALVES,
    )(halo, *args)
    return past, early, parts[:3], parts[3:]


def forward_body(token, valid, xs, x_turned, given, w_in, w_cond, b_conv, w_out, gated_out, kept_out, dpre_out):
    forward_tiles(
        1, rest_rows(xs.shape[0], ROWS // 2), None, None, valid, xs, x_turned, given, (w_in, w_cond, b_conv, w_out),
        gated_out, kept_out, dpre_out,
    )


def forward_rest(token, *args):
    return call(
        forward_body,
        "forward_1",
        [ANYWHERE] + [VMEM] * len(args),
        [VMEM] * 3,
        rest_shapes(args[0].shape[0] * LANES - DILATION_STEP, args[-1].shape[0] // HALVES),
    )(token, *args)


def own_place():
    return [lax.axis_index(name) for name in ("core", "far", "near")]


def turned(index, count):
    bits = (count - 1).bit_length()
    result = 0
    for bit in range(bits):
        result = result | (((index >> bit) & 1) << (bits - 1 - bit))
    return result


def place_blocks(far, block, acc, theirs, mine):
    core, z, xy = own_place()
    for r in range(far):
        for c in range(NEAR):
            here = pl.ds(c * LANES, LANES)
            for k, out in ((1 - core, theirs), (core, mine)):
                rows = pl.ds(pl.multiple_of((k * far + r) * block, 16), block)
                out[c ^ xy, turned(r ^ z, far)] = acc[rows, here].astype(out.dtype)


def gradients_body(
    far, block, half, token, valid, x_turned, given, past_head, kept_head, kept_rest, dpre_head, dpre_rest,
    theirs, mine, acc,
):
    cut = DILATION_STEP
    width = past_head.shape[0]
    part = kept_head.shape[0]
    wide = dpre_rest.shape[1]
    mask = jnp.broadcast_to(row(valid[...].astype(F32)).astype(BF16), (ONES, valid.shape[0] * LANES))
    ends = x_turned.shape[0]
    outer = dot(below(kept_rest[...], mask[:, cut:]), given[cut:, :])
    outer += dot(below(kept_head[...], mask[:, :cut]), given[:cut, :])
    at = ends
    for k in range(2):
        acc[at : at + part, :] = outer[:part, k * width : (k + 1) * width]
        at += part
    acc[at : at + ONES, :] = outer[part:, half * width : (half + 1) * width]
    at += ONES
    acc[at:, :] = jnp.zeros((acc.shape[0] - at, wide), F32)
    inner = dot(x_turned[:, cut:], dpre_rest[...])
    inner += dot(below(past_head[...], x_turned[width:, :cut]), dpre_head[...])
    acc[:ends, :] = inner
    place_blocks(far, block, acc, theirs, mine)


def gradients(half, token, far, block, valid, x_turned, given, past_head, head_parts, rest_parts):
    packed = (NEAR, far, block, LANES)
    wide = rest_parts[2].shape[1]
    return call(
        functools.partial(gradients_body, far, block, half),
        f"gradients_{half}",
        [ANYWHERE] + [VMEM] * 8,
        [VMEM] * 2,
        [jax.ShapeDtypeStruct(packed, BF16), jax.ShapeDtypeStruct(packed, F32)],
        scratch=[pltpu.VMEM((2 * far * block, wide), F32)],
    )(token, valid, x_turned, given, past_head, head_parts[1], rest_parts[1], head_parts[2], rest_parts[2])


def outputs_body(token, valid, xs, head_0, rest_0, head_1, rest_1, w_out, b_res, b_skip, out, skip, mark, rooms, sems):
    width = xs.shape[1] // 2
    copies = []
    for i in range(xs.shape[0] // ROWS):
        rows = slice(i * ROWS, (i + 1) * ROWS)
        mask = column(lines_of(valid, rows))
        gated = beside(picked(head_0, rest_0, rows), picked(head_1, rest_1, rows))
        branch = dot(gated, w_out[:, :width]) + b_res[...]
        rooms[i, 0] = (xs[rows, width:].astype(F32) + mask * branch).astype(BF16)
        side = dot(gated, w_out[:, width:]) + b_skip[...]
        rooms[i, 1] = (mask * side).astype(BF16)
        for k, ref in enumerate((out, skip)):
            copies.append(pltpu.make_async_copy(rooms.at[i, k], ref.at[pl.ds(i * ROWS, ROWS)], sems.at[i, k]))
            copies[-1].start()
    mark[...] = jnp.zeros_like(mark)
    for copy in copies:
        copy.wait()


def outputs(token, valid, xs, gated_0, gated_1, w_out, b_res, b_skip):
    rows, width = xs.shape[0], xs.shape[1] // 2
    return call(
        outputs_body,
        "outputs",
        [ANYWHERE] + [VMEM] * 9,
        [ANYWHERE, ANYWHERE, VMEM],
        [
            jax.ShapeDtypeStruct((rows, width), BF16),
            jax.ShapeDtypeStruct((rows, w_out.shape[1] - width), BF16),
            MARK,
        ],
        scratch=[
            pltpu.VMEM((rows // ROWS, 2, ROWS, width), BF16),
            pltpu.SemaphoreType.DMA((rows // ROWS, 2)),
        ],
    )(token, valid, xs, *gated_0, *gated_1, w_out, b_res, b_skip)


def inputs_body(steps, token, received, relayed, given, pos, head_0, rest_0, head_1, rest_1, w_in, w_cond, *refs):
    gsig, gfeat, mark, room, room_feat, sems = refs[-6:]
    rows, width = given.shape[0], w_in.shape[0] // 2
    copies = []
    wide = 2 * LANES

    def copy(source, target):
        copies.append(pltpu.make_async_copy(source, target, sems.at[len(copies)]))
        copies[-1].start()

    for i, step in enumerate(steps):
        begin = step * ROWS
        here = slice(begin, begin + ROWS)
        after = slice(begin + DILATION_STEP, min(begin + DILATION_STEP + ROWS, rows))
        now = side_by_side(picked(head_0, rest_0, here), picked(head_1, rest_1, here))
        later = side_by_side(picked(head_0, rest_0, after), picked(head_1, rest_1, after))
        tap = column(tap_of(lines_of(pos, after)))
        room_feat[i] = against(w_cond[...], now)
        copy(room_feat.at[i], gfeat.at[:, pl.ds(begin, ROWS)])
        for k in range(width // wide):
            some = slice(k * wide, (k + 1) * wide)
            tail = tap * against(later, w_in[some, :])
            if tail.shape[0] < ROWS:
                tail = below(tail, received[:, some].astype(F32) + relayed[:, some].astype(F32))
            room[i, k] = given[here, some].astype(F32) + against(now, w_in[width + k * wide : width + (k + 1) * wide, :]) + tail
            copy(room.at[i, k], gsig.at[pl.ds(begin, ROWS), pl.ds(k * wide, wide)])
    mark[...] = jnp.zeros_like(mark)
    for one in copies:
        one.wait()


def inputs(steps, token, received, relayed, given, pos, dpre_0, dpre_1, w_in, w_cond, before):
    rows, width = given.shape[0], w_in.shape[0] // 2
    cond = w_cond.shape[0]
    count = width // (2 * LANES)
    return call(
        functools.partial(inputs_body, steps),
        f"inputs_{steps[0]}",
        [ANYWHERE] + [VMEM] * 10 + [ANYWHERE] * len(before),
        [ANYWHERE, ANYWHERE, VMEM],
        [
            jax.ShapeDtypeStruct((rows, width), F32),
            jax.ShapeDtypeStruct((cond, rows), F32),
            MARK,
        ],
        scratch=[
            pltpu.VMEM((len(steps), count, ROWS, 2 * LANES), F32),
            pltpu.VMEM((len(steps), cond, ROWS), F32),
            pltpu.SemaphoreType.DMA((len(steps) * (count + 1),)),
        ],
        aliases={11 + k: k for k in range(len(before))},
    )(token, received, relayed, given, pos, *dpre_0, *dpre_1, w_in, w_cond, *before)


def unpack_body(far, block, token, mine, theirs, *refs):
    arrays, (mark, room) = refs[-9:-2], refs[-2:]
    mark[...] = jnp.zeros_like(mark)
    core, z, xy = own_place()

    @pl.when(pl.program_id(0) == 0)
    def _():
        for k, ref in ((core, mine), (1 - core, theirs)):
            for c in range(NEAR):
                for r in range(far):
                    rows = pl.ds(pl.multiple_of((k * far + (r ^ z)) * block, 16), block)
                    room[c ^ xy, rows, :] = ref[c, turned(r, far)]

    for j in range(NEAR // 2):
        c = pl.program_id(0) * (NEAR // 2) + j
        here = pl.ds(j * LANES, LANES)
        top = 0
        for ref in arrays:
            count = ref.shape[0]
            size = max(count, ONES)
            ref[:, here] = room[c, top : top + size, :].astype(F32)[:count]
            top += size


def unpack(half, token, far, block, mine, theirs, width, cond, hidden, skip_width, before):
    part = hidden // HALVES
    gates = 2 * hidden
    own = (width, skip_width)[half]

    def wide(size):
        return pl.BlockSpec((size, part), lambda s: (0, HALVES * s + half))

    def tall(size):
        return pl.BlockSpec((part, size // 2), lambda s: (half, s))

    specs = [wide(width), wide(width), wide(cond), wide(1), tall(width), tall(skip_width), pl.BlockSpec((1, own // 2), lambda s: (0, s))]
    shapes = [(width, gates), (width, gates), (cond, gates), (1, gates), (hidden, width), (hidden, skip_width), (1, own)]
    packed = (NEAR, far, block, LANES)
    blocks = pl.BlockSpec(packed, lambda s: (0,) * len(packed))
    return call(
        functools.partial(unpack_body, far, block),
        f"unpack_{half}",
        [ANYWHERE, blocks, blocks] + [ANYWHERE] * len(before),
        specs + [pl.BlockSpec(MARK.shape, lambda s: (0, 0))],
        [jax.ShapeDtypeStruct(shape, F32) for shape in shapes] + [MARK],
        scratch=[pltpu.VMEM((NEAR, 2 * far * block, LANES), BF16)],
        aliases={3 + k: k for k in range(len(before))},
        grid=(2,),
    )(token, mine, theirs, *before)


def swapped(x, axis, k):
    return lax.ppermute(x, axis, [(i, i ^ k) for i in range(lax.axis_size(axis))])


def exchanged(blocks):
    return [swapped(block, "near", k + 1) for k, block in enumerate(blocks)]


def add_body(sizes, *refs):
    count = len(sizes)
    kept, got, outs = refs[0], refs[1:-count], refs[-count:]
    at = 0
    for out, size in zip(outs, sizes):
        for k in range(size):
            total = kept[at + k].astype(F32)
            for ref in got:
                total = total + ref[at + k].astype(F32)
            out[k] = total.astype(out.dtype)
        at += size


def many(token):
    return token if isinstance(token, tuple) else (token,)


def after(tokens, body):
    return lambda *refs: body(*refs[tokens:])


def added(name, token, kept, got, outs):
    sizes = [size for size, _ in outs]
    tokens = many(token)
    return call(
        after(len(tokens), functools.partial(add_body, sizes)),
        name,
        [ANYWHERE] * len(tokens) + [VMEM] * (1 + len(got)),
        [VMEM] * len(outs),
        [jax.ShapeDtypeStruct((size, *kept.shape[1:]), dtype) for size, dtype in outs],
    )(*tokens, kept, *got)


def mirror_body(mine, got, out):
    count = mine.shape[0]
    for k in range(count):
        out[k] = (mine[k].astype(F32) + got[count - 1 - k].astype(F32)).astype(out.dtype)


def mirrored(name, token, mine, got):
    tokens = many(token)
    return call(
        after(len(tokens), mirror_body),
        name,
        [ANYWHERE] * len(tokens) + [VMEM, VMEM],
        VMEM,
        jax.ShapeDtypeStruct(mine.shape, BF16),
    )(*tokens, mine, got)


def join_body(*refs):
    out = refs[-1]
    at = 0
    for ref in refs[:-1]:
        out[at : at + ref.shape[0]] = ref[...]
        at += ref.shape[0]


def joined(name, token, parts):
    count = sum(part.shape[0] for part in parts)
    tokens = many(token)
    return call(
        after(len(tokens), join_body),
        name,
        [ANYWHERE] * len(tokens) + [VMEM] * len(parts),
        VMEM,
        jax.ShapeDtypeStruct((count, *parts[0].shape[1:]), BF16),
    )(*tokens, *parts)


def over_outer(total):
    for bit in range((lax.axis_size("outer") - 1).bit_length()):
        total = (total.astype(F32) + swapped(total, "outer", 1 << bit).astype(F32)).astype(BF16)
    return total


def passed_along(x, by, inside=None):
    peers = lax.axis_size(AXES)
    pairs = [(i, i + by) for i in range(peers) if 0 <= i + by < peers]
    if inside:
        pairs = [(i, j) for i, j in pairs if i // inside == j // inside]
    return lax.ppermute(x, AXES, pairs)


def block_hops():
    sizes = [lax.axis_size(name) for name in AXES]
    block = sizes[2] * sizes[3]
    blocks = sizes[0] * sizes[1]
    marks = [0]
    size = sizes[2] // 2
    while size:
        marks.append(marks[-1] + size * sizes[3])
        size //= 2
    marks.append(block - 1)
    first = [(k * block, (k - 1) * block) for k in range(1, blocks)]
    return [first] + [
        [(k * block + a, k * block + b) for k in range(blocks - 1)] for a, b in zip(marks, marks[1:])
    ]


def in_hbm(x):
    return pltpu.with_memory_space_constraint(x, pltpu.HBM)


def body(
    signal,
    features,
    position,
    valid,
    w_past,
    w_now,
    b_conv,
    w_cond,
    w_res,
    b_res,
    w_skip,
    b_skip,
    grad_out,
    grad_skip,
):
    rows, width = signal.shape
    features = features.T
    cond = features.shape[0]
    hidden = w_res.shape[0]
    skip_width = w_skip.shape[1]
    far = lax.axis_size("far")
    far_bits = (far - 1).bit_length()
    used = 2 * width + cond + ONES + 2 * (hidden // HALVES) + ONES
    block = -(-used // (2 * far * 16)) * 16
    lines = (rows // LANES, LANES)
    pos, val = position.reshape(lines), valid.reshape(lines)
    b_conv, b_res, b_skip = (b.reshape(1, -1) for b in (b_conv, b_res, b_skip))

    def core_sum(half, token, theirs, mine):
        kept, *sent = added(
            f"core_sum_{half}", token, mine, [swapped(theirs, "core", 1)], [(1, F32)] + [(1, BF16)] * (NEAR - 1)
        )
        return kept[0], exchanged([x[0] for x in sent])

    def near_sum(half, token, kept, got):
        kept, sent = added(f"near_sum_{half}", token, kept, got, [(far // 2, F32), (far // 2, BF16)])
        return kept, swapped(sent, "far", 1)

    def far_sum(half, token, kept, got):
        for bit in range(1, far_bits - 1):
            size = kept.shape[0] // 2
            kept, sent = added(f"far_sum_{half}_{bit}", token, kept, [got], [(size, F32), (size, BF16)])
            got = swapped(sent, "far", 1 << bit)
        (mine,) = added(f"far_sum_{half}", token, kept, [got], [(kept.shape[0], BF16)])
        return mine, swapped(mine, "far", 1 << (far_bits - 1))

    def far_end(half, token, mine, got):
        total = over_outer(mirrored(f"far_end_{half}", token, mine, got))
        return total, swapped(total, "far", 1 << (far_bits - 2))

    def far_join(half, token, mine, got):
        total = joined(f"far_join_{half}", token, [mine, got])
        for bit in reversed(range(far_bits - 2)):
            total = joined(f"far_join_{half}_{bit}", token, [total, swapped(total, "far", 1 << bit)])
        return total, exchanged([total] * (NEAR - 1))

    def near_join(half, token, mine, got):
        total = joined(f"near_join_{half}", token, [mine[None]] + [x[None] for x in got])
        return total, swapped(total, "core", 1)

    def input_gradients(steps, token, before):
        last = (steps[-1] + 1) * ROWS == rows
        first, second = (received, relayed) if last else (head_0[0], head_0[0])
        return inputs(steps, token, first, second, given, pos, dpre_0, dpre_1, w_in, w_cond, before)

    halo = passed_along(signal[rows - DILATION_STEP :], 1)
    val, pos, b_conv, b_res, b_skip, w_cond, w_out, w_in, xs, x_turned, given, *rest_0 = load(
        val, pos, b_conv, b_res, b_skip, features, w_cond, w_res, w_skip, w_past, w_now, signal, grad_out, grad_skip
    )
    common = (val, xs, x_turned, given, w_in, w_cond, b_conv, w_out)
    past_head, early, head_0, head_1 = head(halo, pos, *common)
    hops = block_hops()
    theirs_0, mine_0 = gradients(0, past_head, far, block, val, x_turned, given, past_head, head_0, rest_0)
    relayed = joined("pass_0", theirs_0, [early])
    relayed = lax.ppermute(relayed, AXES, hops[0])
    rest_1 = forward_rest(theirs_0, *common)
    dpre_0, dpre_1 = (head_0[2], rest_0[2]), (head_1[2], rest_1[2])
    kept_0, got_0 = core_sum(0, (rest_1[0], relayed), theirs_0, mine_0)
    relayed = joined("pass_1", kept_0, [relayed])
    relayed_0 = relayed
    for pairs in hops[1:-2]:
        relayed = lax.ppermute(relayed, AXES, pairs)
    theirs_1, mine_1 = gradients(1, relayed_0, far, block, val, x_turned, given, past_head, head_1, rest_1)
    relayed = joined("pass_2", theirs_1, [relayed])
    relayed_0 = relayed
    relayed = lax.ppermute(relayed, AXES, hops[-2])
    output, skip_out, mark = outputs(
        relayed_0, val, xs, (head_0[0], rest_0[0]), (head_1[0], rest_1[0]), w_out, b_res, b_skip
    )
    kept_0, got_0 = near_sum(0, (mark, relayed), kept_0, got_0)
    kept_1, got_1 = core_sum(1, kept_0, theirs_1, mine_1)
    ends_0, got_0 = far_sum(0, kept_1, kept_0, got_0)
    *grads, mark = input_gradients((0, 1), ends_0, [])
    ends_0, got_0 = far_end(0, mark, ends_0, got_0)
    kept_1, got_1 = near_sum(1, ends_0, kept_1, got_1)
    ends_0, got_0 = far_join(0, kept_1, ends_0, got_0)
    ends_1, got_1 = far_sum(1, ends_0, kept_1, got_1)
    *grads, mark = input_gradients((2,), ends_1, grads)
    ends_1, got_1 = far_end(1, mark, ends_1, got_1)
    early = joined("pass_3", ends_1, [early])
    received = passed_along(early, -1, inside=far * NEAR)
    relayed = joined("pass_4", early, [relayed])
    blocks_0, others_0 = near_join(0, relayed, ends_0, got_0)
    relayed = lax.ppermute(relayed, AXES, hops[-1])
    ends_1, got_1 = far_join(1, blocks_0, ends_1, got_1)
    *grads, mark = input_gradients((3,), ends_1, grads)
    blocks_1, others_1 = near_join(1, mark, ends_1, got_1)
    *done, own_0, mark = unpack(0, blocks_1, far, block, blocks_0, others_0, width, cond, hidden, skip_width, [])
    *done, own_1, _ = unpack(1, mark, far, block, blocks_1, others_1, width, cond, hidden, skip_width, done)
    g_past, g_now, g_cond, g_bias, g_res, g_skip = done
    grad_signal, grad_features = grads
    return (
        output,
        skip_out,
        grad_signal,
        grad_features.T,
        g_past,
        g_now,
        g_bias.reshape(-1),
        g_cond,
        g_res,
        own_0.reshape(-1),
        g_skip,
        own_1.reshape(-1),
    )


def solution(mesh):
    row, col = mesh.shape["row"], mesh.shape["col"]
    fine = Mesh(mesh.devices.reshape(row // 2, 2, col // NEAR, NEAR), AXES)
    rows = P(AXES, None)
    line = P(AXES)
    return jax.shard_map(
        body,
        mesh=fine,
        in_specs=(rows, rows, line, line) + (P(),) * 8 + (rows, rows),
        out_specs=(rows,) * 4 + (P(),) * 8,
        check_vma=False,
    )
```

```python
import functools

import jax
import jax.numpy as jnp
from jax import lax
from jax.experimental import pallas as pl
from jax.experimental.pallas import tpu as pltpu
from jax.sharding import Mesh
from jax.sharding import PartitionSpec as P

DILATION_STEP = 256
AXES = ("outer", "core", "far", "near")
HALVES = 2
NEAR = 4
LANES = 128
ROWS = 512
ONES = 16
F32 = jnp.float32
BF16 = jnp.bfloat16
MEGA = 1 << 20
COSTS = {
    "load": 8, "head": 2, "gradients_0": 0, "forward_1": 0, "gradients_1": 4, "outputs": 4, "near_sum_0": 8,
    "far_sum_0": 8, "near_sum_1": 4, "near_join_0": 2, "near_join_1": 4, "far_join_0": 4,
}
FLOPS = 10**9


def dot(left, right):
    return jnp.dot(left, right, preferred_element_type=F32)


def across(left, right):
    return lax.dot_general(left, right, (((0,), (0,)), ((), ())), preferred_element_type=F32)


def against(left, weight):
    return lax.dot_general(left, weight, (((1,), (1,)), ((), ())), preferred_element_type=F32)


def column(lines):
    turned = lines.astype(F32).T
    return jnp.concatenate([turned[:, k : k + 1] for k in range(lines.shape[0])], axis=0)


def row(lines):
    return jnp.concatenate([lines[k : k + 1] for k in range(lines.shape[0])], axis=1)


def tap_of(lines):
    return jnp.where(lines >= DILATION_STEP, 1, 0)


def lines_of(ref, rows):
    return ref[rows.start // LANES : rows.stop // LANES, :]


def picked(head, rest, rows):
    cut = DILATION_STEP
    low = head[rows.start : min(rows.stop, cut), :] if rows.start < cut else None
    high = rest[max(rows.start, cut) - cut : rows.stop - cut, :] if rows.stop > cut else None
    if low is None:
        return high
    return low if high is None else jnp.concatenate([low, high], axis=0)


def call(kernel, name, in_specs, out_specs, out_shape, scratch=(), aliases=None, grid=(), vmem=24):
    return pl.pallas_call(
        kernel,
        grid=grid,
        in_specs=in_specs,
        out_specs=out_specs,
        out_shape=out_shape,
        scratch_shapes=list(scratch),
        input_output_aliases=aliases or {},
        cost_estimate=pl.CostEstimate(
            flops=1 + int(FLOPS * COSTS.get(name, COSTS.get(name.split("_")[0], 0))), bytes_accessed=1, transcendentals=0
        ),
        name=name,
        compiler_params=pltpu.CompilerParams(vmem_limit_bytes=vmem * MEGA),
    )


VMEM = pl.BlockSpec(memory_space=pltpu.VMEM)
ANYWHERE = pl.BlockSpec(memory_space=pl.ANY)
MARK = jax.ShapeDtypeStruct((8, LANES), F32)


def beside(*parts):
    return jnp.concatenate(parts, axis=1)


def below(*parts):
    return jnp.concatenate(parts, axis=0)


def products(half, rows, past, sig, feats, gout, gskip, w_in, w_cond, b_conv, w_res, w_skip, arrive=None):
    part = w_res.shape[0] // HALVES
    width = sig.shape[1]
    first = half * part
    made = []
    for k, at in enumerate((first, HALVES * part + first)):
        here = slice(at, at + part)
        if arrive:
            arrive(rows, k)
        own = dot(past, w_in[:width, here]) + dot(sig[rows, :], w_in[width:, here])
        made.append(own + across(feats, w_cond[:, here]) + b_conv[:, here])
    if arrive:
        arrive(rows, 2)
    here = slice(first, first + part)
    return *made, against(gout[rows, :], w_res[here, :]) + against(gskip[rows, :], w_skip[here, :])


def finish(pre_a, pre_s, dgated, valid_lines):
    act = jnp.tanh(pre_a)
    gate = 0.5 + 0.5 * jnp.tanh(0.5 * pre_s)
    slope = (column(valid_lines) * dgated) * gate
    dpre = beside(slope * (1.0 - act * act), slope * act * (1.0 - gate)).astype(BF16)
    gated = (act * gate).astype(BF16)
    return gated, gated.T * row(valid_lines.astype(BF16)), dpre


def forward_tiles(half, tiles, prepare, arrive, valid, past, sig, x_turned, gout, gskip, weights, gated_out, kept_out, dpre_out):
    cond = weights[1].shape[0]
    width = sig.shape[1]

    def done(rows, *made):
        there = slice(rows.start - DILATION_STEP, rows.stop - DILATION_STEP)
        gated_out[there, :], kept_out[:, there], dpre_out[there, :] = finish(*made, lines_of(valid, rows))

    waiting = None
    for rows in tiles:
        if prepare:
            prepare(rows)
        feats = x_turned[2 * width : 2 * width + cond, rows]
        made = products(half, rows, past[rows, :], sig, feats, gout, gskip, *weights, arrive=arrive)
        if waiting:
            done(*waiting)
        waiting = (rows, *made)
    done(*waiting)


def rest_rows(rows, tile=ROWS):
    cuts = sorted({DILATION_STEP, *range(tile, rows + 1, tile)})
    return [slice(a, b) for a, b in zip(cuts, cuts[1:])]


def load_body(
    valid, pos, b_conv, b_res, b_skip, feat, w_cond, w_res, w_skip, w_past, w_now, sig, gout, gskip,
    valid_to, pos_to, b_conv_to, b_res_to, b_skip_to, w_cond_to, w_res_to, w_skip_to, w_in, past, sig_to, x_turned,
    gout_to, gskip_to, gated_rest, kept_rest, dpre_rest, sems,
):
    rows_all, width = sig.shape
    cond = feat.shape[0]
    count = 0

    def start(source, target):
        nonlocal count
        copy = pltpu.make_async_copy(source, target, sems.at[count])
        copy.start()
        count += 1
        return copy

    def tile(i, source, target):
        rows = pl.ds(i * ROWS, ROWS)
        return start(source.at[rows], target.at[rows])

    signals = [tile(0, sig, sig_to)]
    needs = [
        [
            start(pos, pos_to),
            start(w_past, w_in.at[pl.ds(0, width)]),
            start(w_now, w_in.at[pl.ds(width, width)]),
            start(feat, x_turned.at[pl.ds(2 * width, cond)]),
            start(w_cond, w_cond_to),
            start(b_conv, b_conv_to),
        ],
        [],
        [start(valid, valid_to), start(w_res, w_res_to), start(w_skip, w_skip_to)],
    ]
    cotangents = [[tile(0, gout, gout_to), tile(0, gskip, gskip_to)]]
    for i in range(1, rows_all // ROWS):
        signals.append(tile(i, sig, sig_to))
        cotangents.append([tile(i, gout, gout_to), tile(i, gskip, gskip_to)])
    last = [start(b_res, b_res_to), start(b_skip, b_skip_to)]

    def wait(copies):
        for copy in copies:
            copy.wait()
        copies.clear()

    def prepare(rows):
        i = rows.start // ROWS
        signals[i].wait()
        wait(needs[0])
        whole = slice(i * ROWS, (i + 1) * ROWS)
        before = slice(rows.start - DILATION_STEP, rows.stop - DILATION_STEP)
        tap = tap_of(lines_of(pos_to, rows)).astype(F32)
        past[rows, :] = sig_to[before, :] * column(tap).astype(BF16)
        x_turned[width : 2 * width, whole] = sig_to[whole, :].T
        x_turned[:width, rows] = x_turned[width : 2 * width, before] * row(tap).astype(BF16)

    def arrive(rows, k):
        wait(needs[k])
        if k == 2:
            wait(cotangents[rows.start // ROWS])

    x_turned[2 * width + cond :, :] = jnp.ones((x_turned.shape[0] - 2 * width - cond, rows_all), BF16)
    forward_tiles(
        0, rest_rows(rows_all), prepare, arrive, valid_to, past, sig_to, x_turned, gout_to, gskip_to,
        (w_in, w_cond_to, b_conv_to, w_res_to, w_skip_to), gated_rest, kept_rest, dpre_rest,
    )
    wait(last)


def rest_shapes(rest, part):
    return [jax.ShapeDtypeStruct(shape, BF16) for shape in ((rest, part), (part, rest), (rest, 2 * part))]


def load(*arrays):
    sources = [in_hbm(x) for x in arrays]
    feat, w_cond, w_res, w_skip, w_past, w_now, sig, gout, gskip = arrays[5:]
    rows, width = sig.shape
    hidden = w_res.shape[0]
    shapes = [jax.ShapeDtypeStruct(x.shape, x.dtype) for x in arrays[:5] + (w_cond, w_res, w_skip)] + [
        jax.ShapeDtypeStruct(shape, BF16)
        for shape in (
            (2 * width, 2 * hidden), sig.shape, sig.shape, (2 * width + feat.shape[0] + ONES, rows), gout.shape, gskip.shape,
        )
    ]
    shapes += rest_shapes(rows - DILATION_STEP, hidden // HALVES)
    return call(
        load_body,
        "load",
        [ANYWHERE] * len(sources),
        [VMEM] * len(shapes),
        shapes,
        scratch=[pltpu.SemaphoreType.DMA((11 + 3 * (rows // ROWS),))],
    )(*sources)


def side_by_side(dpre_0, dpre_1):
    part = dpre_0.shape[1] // 2
    return beside(dpre_0[:, :part], dpre_1[:, :part], dpre_0[:, part:], dpre_1[:, part:])


def head_body(halo, pos, valid, sig, x_turned, gout, gskip, w_in, w_cond, b_conv, w_res, w_skip, past_out, *outs):
    rows = slice(0, DILATION_STEP)
    width = halo.shape[1]
    cond = w_cond.shape[0]
    tap = tap_of(lines_of(pos, rows)).astype(F32)
    past_out[...] = halo[...].T * row(tap).astype(BF16)
    past = halo[...] * column(tap).astype(BF16)
    feats = x_turned[2 * width : 2 * width + cond, rows]
    made = [
        products(half, rows, past, sig, feats, gout, gskip, w_in, w_cond, b_conv, w_res, w_skip) for half in range(HALVES)
    ]
    for half in range(HALVES):
        parts = finish(*made[half], lines_of(valid, rows))
        for ref, value in zip(outs[3 * half :], parts):
            ref[...] = value


def head(halo, *args):
    width = halo.shape[1]
    part = args[-1].shape[0] // HALVES
    past, *parts = call(
        head_body,
        "head",
        [VMEM] * (1 + len(args)),
        [VMEM] * (1 + 3 * HALVES),
        [jax.ShapeDtypeStruct((width, DILATION_STEP), BF16)] + rest_shapes(DILATION_STEP, part) * HALVES,
    )(halo, *args)
    return past, parts[:3], parts[3:]


def early_body(token, pos, dpre_0, dpre_1, w_in, early):
    tap = column(tap_of(lines_of(pos, slice(0, DILATION_STEP))))
    early[...] = (tap * against(side_by_side(dpre_0[...], dpre_1[...]), w_in[: early.shape[1], :])).astype(BF16)


def early_rows(token, pos, dpre_0, dpre_1, w_in):
    return call(
        early_body,
        "early",
        [ANYWHERE] + [VMEM] * 4,
        VMEM,
        jax.ShapeDtypeStruct((DILATION_STEP, w_in.shape[0] // 2), BF16),
    )(token, pos, dpre_0, dpre_1, w_in)


def forward_body(
    token, valid, past, sig, x_turned, gout, gskip, w_in, w_cond, b_conv, w_res, w_skip, gated_out, kept_out, dpre_out
):
    forward_tiles(
        1, rest_rows(sig.shape[0], ROWS // 2), None, None, valid, past, sig, x_turned, gout, gskip,
        (w_in, w_cond, b_conv, w_res, w_skip), gated_out, kept_out, dpre_out,
    )


def forward_rest(token, *args):
    return call(
        forward_body,
        "forward_1",
        [ANYWHERE] + [VMEM] * len(args),
        [VMEM] * 3,
        rest_shapes(args[0].shape[0] * LANES - DILATION_STEP, args[-1].shape[0] // HALVES),
    )(token, *args)


def own_place():
    return [lax.axis_index(name) for name in ("core", "far", "near")]


def turned(index, count):
    bits = (count - 1).bit_length()
    result = 0
    for bit in range(bits):
        result = result | (((index >> bit) & 1) << (bits - 1 - bit))
    return result


def place_blocks(far, block, acc, theirs, mine):
    core, z, xy = own_place()
    for r in range(far):
        for c in range(NEAR):
            here = pl.ds(c * LANES, LANES)
            for k, out in ((1 - core, theirs), (core, mine)):
                rows = pl.ds(pl.multiple_of((k * far + r) * block, 16), block)
                out[c ^ xy, turned(r ^ z, far)] = acc[rows, here].astype(out.dtype)


def gradients_body(
    far, block, half, token, valid, x_turned, gout, gskip, past_head, kept_head, kept_rest, dpre_head, dpre_rest,
    theirs, mine, acc,
):
    cut = DILATION_STEP
    width = past_head.shape[0]
    part = kept_head.shape[0]
    wide = dpre_rest.shape[1]
    mask = jnp.broadcast_to(row(valid[...].astype(F32)).astype(BF16), (ONES, valid.shape[0] * LANES))
    ends = x_turned.shape[0]
    rest = below(kept_rest[...], mask[:, cut:])
    first = below(kept_head[...], mask[:, :cut])
    at = ends
    for k, ref in enumerate((gout, gskip)):
        outer = dot(rest, ref[cut:, :]) + dot(first, ref[:cut, :])
        acc[at : at + part, :] = outer[:part]
        at += part
        if k == half:
            acc[ends + 2 * part : ends + 2 * part + ONES, :] = outer[part:]
    at += ONES
    acc[at:, :] = jnp.zeros((acc.shape[0] - at, wide), F32)
    inner = dot(x_turned[:, cut:], dpre_rest[...])
    inner += dot(below(past_head[...], x_turned[width:, :cut]), dpre_head[...])
    acc[:ends, :] = inner
    place_blocks(far, block, acc, theirs, mine)


def gradients(half, token, far, block, valid, x_turned, gout, gskip, past_head, head_parts, rest_parts):
    packed = (NEAR, far, block, LANES)
    wide = rest_parts[2].shape[1]
    return call(
        functools.partial(gradients_body, far, block, half),
        f"gradients_{half}",
        [ANYWHERE] + [VMEM] * 9,
        [VMEM] * 2,
        [jax.ShapeDtypeStruct(packed, BF16), jax.ShapeDtypeStruct(packed, F32)],
        scratch=[pltpu.VMEM((2 * far * block, wide), F32)],
    )(token, valid, x_turned, gout, gskip, past_head, head_parts[1], rest_parts[1], head_parts[2], rest_parts[2])


def outputs_body(
    token, valid, sig, head_0, rest_0, head_1, rest_1, w_res, w_skip, b_res, b_skip, out, skip, mark, rooms, sems
):
    copies = []
    for i in range(sig.shape[0] // ROWS):
        rows = slice(i * ROWS, (i + 1) * ROWS)
        mask = column(lines_of(valid, rows))
        gated = beside(picked(head_0, rest_0, rows), picked(head_1, rest_1, rows))
        branch = dot(gated, w_res[...]) + b_res[...]
        rooms[i, 0] = (sig[rows, :].astype(F32) + mask * branch).astype(BF16)
        side = dot(gated, w_skip[...]) + b_skip[...]
        rooms[i, 1] = (mask * side).astype(BF16)
        for k, ref in enumerate((out, skip)):
            copies.append(pltpu.make_async_copy(rooms.at[i, k], ref.at[pl.ds(i * ROWS, ROWS)], sems.at[i, k]))
            copies[-1].start()
    mark[...] = jnp.zeros_like(mark)
    for copy in copies:
        copy.wait()


def outputs(token, valid, sig, gated_0, gated_1, w_res, w_skip, b_res, b_skip):
    rows, width = sig.shape
    return call(
        outputs_body,
        "outputs",
        [ANYWHERE] + [VMEM] * 10,
        [ANYWHERE, ANYWHERE, VMEM],
        [
            jax.ShapeDtypeStruct((rows, width), BF16),
            jax.ShapeDtypeStruct((rows, w_skip.shape[1]), BF16),
            MARK,
        ],
        scratch=[
            pltpu.VMEM((rows // ROWS, 2, ROWS, width), BF16),
            pltpu.SemaphoreType.DMA((rows // ROWS, 2)),
        ],
    )(token, valid, sig, *gated_0, *gated_1, w_res, w_skip, b_res, b_skip)


def inputs_body(steps, token, received, gout, pos, head_0, rest_0, head_1, rest_1, w_in, w_cond, *refs):
    gsig, gfeat, mark, room, room_feat, sems = refs[-6:]
    rows, width = gout.shape
    copies = []
    wide = 2 * LANES

    def copy(source, target):
        copies.append(pltpu.make_async_copy(source, target, sems.at[len(copies)]))
        copies[-1].start()

    for i, step in enumerate(steps):
        begin = step * ROWS
        here = slice(begin, begin + ROWS)
        after = slice(begin + DILATION_STEP, min(begin + DILATION_STEP + ROWS, rows))
        now = side_by_side(picked(head_0, rest_0, here), picked(head_1, rest_1, here))
        later = side_by_side(picked(head_0, rest_0, after), picked(head_1, rest_1, after))
        tap = column(tap_of(lines_of(pos, after)))
        room_feat[i] = against(w_cond[...], now)
        copy(room_feat.at[i], gfeat.at[:, pl.ds(begin, ROWS)])
        for k in range(width // wide):
            some = slice(k * wide, (k + 1) * wide)
            tail = tap * against(later, w_in[some, :])
            if tail.shape[0] < ROWS:
                tail = below(tail, received[:, some].astype(F32))
            room[i, k] = gout[here, some].astype(F32) + against(now, w_in[width + k * wide : width + (k + 1) * wide, :]) + tail
            copy(room.at[i, k], gsig.at[pl.ds(begin, ROWS), pl.ds(k * wide, wide)])
    mark[...] = jnp.zeros_like(mark)
    for one in copies:
        one.wait()


def inputs(steps, token, received, gout, pos, dpre_0, dpre_1, w_in, w_cond, before):
    rows, width = gout.shape
    cond = w_cond.shape[0]
    count = width // (2 * LANES)
    return call(
        functools.partial(inputs_body, steps),
        f"inputs_{steps[0]}",
        [ANYWHERE] + [VMEM] * 9 + [ANYWHERE] * len(before),
        [ANYWHERE, ANYWHERE, VMEM],
        [
            jax.ShapeDtypeStruct((rows, width), F32),
            jax.ShapeDtypeStruct((cond, rows), F32),
            MARK,
        ],
        scratch=[
            pltpu.VMEM((len(steps), count, ROWS, 2 * LANES), F32),
            pltpu.VMEM((len(steps), cond, ROWS), F32),
            pltpu.SemaphoreType.DMA((len(steps) * (count + 1),)),
        ],
        aliases={10 + k: k for k in range(len(before))},
    )(token, received, gout, pos, *dpre_0, *dpre_1, w_in, w_cond, *before)


def unpack_body(far, block, token, mine, theirs, *refs):
    arrays, (mark, room) = refs[-9:-2], refs[-2:]
    mark[...] = jnp.zeros_like(mark)
    core, z, xy = own_place()

    @pl.when(pl.program_id(0) == 0)
    def _():
        for k, ref in ((core, mine), (1 - core, theirs)):
            for c in range(NEAR):
                for r in range(far):
                    rows = pl.ds(pl.multiple_of((k * far + (r ^ z)) * block, 16), block)
                    room[c ^ xy, rows, :] = ref[c, turned(r, far)]

    for j in range(NEAR // 2):
        c = pl.program_id(0) * (NEAR // 2) + j
        here = pl.ds(j * LANES, LANES)
        top = 0
        for ref in arrays:
            count = ref.shape[0]
            size = max(count, ONES)
            ref[:, here] = room[c, top : top + size, :].astype(F32)[:count]
            top += size


def unpack(half, token, far, block, mine, theirs, width, cond, hidden, skip_width, before):
    part = hidden // HALVES
    gates = 2 * hidden
    own = (width, skip_width)[half]

    def wide(size):
        return pl.BlockSpec((size, part), lambda s: (0, HALVES * s + half))

    def tall(size):
        return pl.BlockSpec((part, size // 2), lambda s: (half, s))

    specs = [wide(width), wide(width), wide(cond), wide(1), tall(width), tall(skip_width), pl.BlockSpec((1, own // 2), lambda s: (0, s))]
    shapes = [(width, gates), (width, gates), (cond, gates), (1, gates), (hidden, width), (hidden, skip_width), (1, own)]
    packed = (NEAR, far, block, LANES)
    blocks = pl.BlockSpec(packed, lambda s: (0,) * len(packed))
    return call(
        functools.partial(unpack_body, far, block),
        f"unpack_{half}",
        [ANYWHERE, blocks, blocks] + [ANYWHERE] * len(before),
        specs + [pl.BlockSpec(MARK.shape, lambda s: (0, 0))],
        [jax.ShapeDtypeStruct(shape, F32) for shape in shapes] + [MARK],
        scratch=[pltpu.VMEM((NEAR, 2 * far * block, LANES), BF16)],
        aliases={3 + k: k for k in range(len(before))},
        grid=(2,),
    )(token, mine, theirs, *before)


def swapped(x, axis, k):
    return lax.ppermute(x, axis, [(i, i ^ k) for i in range(lax.axis_size(axis))])


def exchanged(blocks):
    return [swapped(block, "near", k + 1) for k, block in enumerate(blocks)]


def add_body(sizes, token, *refs):
    count = len(sizes)
    kept, got, outs = refs[0], refs[1:-count], refs[-count:]
    at = 0
    for out, size in zip(outs, sizes):
        for k in range(size):
            total = kept[at + k].astype(F32)
            for ref in got:
                total = total + ref[at + k].astype(F32)
            out[k] = total.astype(out.dtype)
        at += size


def added(name, token, kept, got, outs):
    sizes = [size for size, _ in outs]
    result = call(
        functools.partial(add_body, sizes),
        name,
        [ANYWHERE] + [VMEM] * (1 + len(got)),
        [VMEM] * len(outs),
        [jax.ShapeDtypeStruct((size, *kept.shape[1:]), dtype) for size, dtype in outs],
    )(token, kept, *got)
    return result


def mirror_body(token, mine, got, out):
    count = mine.shape[0]
    for k in range(count):
        out[k] = (mine[k].astype(F32) + got[count - 1 - k].astype(F32)).astype(out.dtype)


def mirrored(name, token, mine, got):
    return call(
        mirror_body,
        name,
        [ANYWHERE, VMEM, VMEM],
        VMEM,
        jax.ShapeDtypeStruct(mine.shape, BF16),
    )(token, mine, got)


def join_body(token, *refs):
    out = refs[-1]
    at = 0
    for ref in refs[:-1]:
        out[at : at + ref.shape[0]] = ref[...]
        at += ref.shape[0]


def joined(name, token, parts):
    count = sum(part.shape[0] for part in parts)
    return call(
        join_body,
        name,
        [ANYWHERE] + [VMEM] * len(parts),
        VMEM,
        jax.ShapeDtypeStruct((count, *parts[0].shape[1:]), BF16),
    )(token, *parts)


def over_outer(total):
    for bit in range((lax.axis_size("outer") - 1).bit_length()):
        total = (total.astype(F32) + swapped(total, "outer", 1 << bit).astype(F32)).astype(BF16)
    return total


def passed_along(x, by):
    peers = lax.axis_size(AXES)
    pairs = [(i, i + by) for i in range(peers) if 0 <= i + by < peers]
    return lax.ppermute(x, AXES, pairs)


def in_hbm(x):
    return pltpu.with_memory_space_constraint(x, pltpu.HBM)


def body(
    signal,
    features,
    position,
    valid,
    w_past,
    w_now,
    b_conv,
    w_cond,
    w_res,
    b_res,
    w_skip,
    b_skip,
    grad_out,
    grad_skip,
):
    rows, width = signal.shape
    features = features.T
    cond = features.shape[0]
    hidden = w_res.shape[0]
    skip_width = w_skip.shape[1]
    far = lax.axis_size("far")
    far_bits = (far - 1).bit_length()
    used = 2 * width + cond + ONES + 2 * (hidden // HALVES) + ONES
    block = -(-used // (2 * far * 16)) * 16
    lines = (rows // LANES, LANES)
    pos, val = position.reshape(lines), valid.reshape(lines)
    b_conv, b_res, b_skip = (b.reshape(1, -1) for b in (b_conv, b_res, b_skip))

    def core_sum(half, token, theirs, mine):
        kept, *sent = added(
            f"core_sum_{half}", token, mine, [swapped(theirs, "core", 1)], [(1, F32)] + [(1, BF16)] * (NEAR - 1)
        )
        return kept[0], exchanged([x[0] for x in sent])

    def near_sum(half, token, kept, got):
        kept, sent = added(f"near_sum_{half}", token, kept, got, [(far // 2, F32), (far // 2, BF16)])
        return kept, swapped(sent, "far", 1)

    def far_sum(half, token, kept, got):
        for bit in range(1, far_bits - 1):
            size = kept.shape[0] // 2
            kept, sent = added(f"far_sum_{half}_{bit}", token, kept, [got], [(size, F32), (size, BF16)])
            got = swapped(sent, "far", 1 << bit)
        (mine,) = added(f"far_sum_{half}", token, kept, [got], [(kept.shape[0], BF16)])
        return mine, swapped(mine, "far", 1 << (far_bits - 1))

    def far_end(half, token, mine, got):
        total = over_outer(mirrored(f"far_end_{half}", token, mine, got))
        return total, swapped(total, "far", 1 << (far_bits - 2))

    def far_join(half, token, mine, got):
        total = joined(f"far_join_{half}", token, [mine, got])
        for bit in reversed(range(far_bits - 2)):
            total = joined(f"far_join_{half}_{bit}", token, [total, swapped(total, "far", 1 << bit)])
        return total, exchanged([total] * (NEAR - 1))

    def near_join(half, token, mine, got):
        total = joined(f"near_join_{half}", token, [mine[None]] + [x[None] for x in got])
        return total, swapped(total, "core", 1)

    def input_gradients(steps, token, before):
        last = (steps[-1] + 1) * ROWS == rows
        return inputs(steps, token, received if last else head_0[0], grad_out, pos, dpre_0, dpre_1, w_in, w_cond, before)

    halo = passed_along(signal[rows - DILATION_STEP :], 1)
    val, pos, b_conv, b_res, b_skip, w_cond, w_res, w_skip, w_in, past, signal, x_turned, grad_out, grad_skip, *rest_0 = load(
        val, pos, b_conv, b_res, b_skip, features, w_cond, w_res, w_skip, w_past, w_now, signal, grad_out, grad_skip
    )
    common = (signal, x_turned, grad_out, grad_skip, w_in, w_cond, b_conv, w_res, w_skip)
    past_head, head_0, head_1 = head(halo, pos, val, *common)
    theirs_0, mine_0 = gradients(0, past_head, far, block, val, x_turned, grad_out, grad_skip, past_head, head_0, rest_0)
    rest_1 = forward_rest(theirs_0, val, past, *common)
    dpre_0, dpre_1 = (head_0[2], rest_0[2]), (head_1[2], rest_1[2])
    kept_0, got_0 = core_sum(0, rest_1[0], theirs_0, mine_0)
    theirs_1, mine_1 = gradients(1, kept_0, far, block, val, x_turned, grad_out, grad_skip, past_head, head_1, rest_1)
    output, skip_out, mark = outputs(
        theirs_1, val, signal, (head_0[0], rest_0[0]), (head_1[0], rest_1[0]), w_res, w_skip, b_res, b_skip
    )
    kept_0, got_0 = near_sum(0, mark, kept_0, got_0)
    kept_1, got_1 = core_sum(1, kept_0, theirs_1, mine_1)
    ends_0, got_0 = far_sum(0, kept_1, kept_0, got_0)
    *grads, mark = input_gradients((0, 1), ends_0, [])
    ends_0, got_0 = far_end(0, mark, ends_0, got_0)
    kept_1, got_1 = near_sum(1, ends_0, kept_1, got_1)
    ends_0, got_0 = far_join(0, kept_1, ends_0, got_0)
    ends_1, got_1 = far_sum(1, ends_0, kept_1, got_1)
    *grads, mark = input_gradients((2,), ends_1, grads)
    ends_1, got_1 = far_end(1, mark, ends_1, got_1)
    early = early_rows(ends_1, pos, head_0[2], head_1[2], w_in)
    received = passed_along(early, -1)
    blocks_0, others_0 = near_join(0, early, ends_0, got_0)
    ends_1, got_1 = far_join(1, blocks_0, ends_1, got_1)
    *grads, mark = input_gradients((3,), ends_1, grads)
    blocks_1, others_1 = near_join(1, mark, ends_1, got_1)
    *done, own_0, mark = unpack(0, blocks_1, far, block, blocks_0, others_0, width, cond, hidden, skip_width, [])
    *done, own_1, _ = unpack(1, mark, far, block, blocks_1, others_1, width, cond, hidden, skip_width, done)
    g_past, g_now, g_cond, g_bias, g_res, g_skip = done
    grad_signal, grad_features = grads
    return (
        output,
        skip_out,
        grad_signal,
        grad_features.T,
        g_past,
        g_now,
        g_bias.reshape(-1),
        g_cond,
        g_res,
        own_0.reshape(-1),
        g_skip,
        own_1.reshape(-1),
    )


def solution(mesh):
    row, col = mesh.shape["row"], mesh.shape["col"]
    fine = Mesh(mesh.devices.reshape(row // 2, 2, col // NEAR, NEAR), AXES)
    rows = P(AXES, None)
    line = P(AXES)
    return jax.shard_map(
        body,
        mesh=fine,
        in_specs=(rows, rows, line, line) + (P(),) * 8 + (rows, rows),
        out_specs=(rows,) * 4 + (P(),) * 8,
        check_vma=False,
    )
```

```python
import functools

import jax
import jax.numpy as jnp
from jax import lax
from jax.experimental import pallas as pl
from jax.experimental.pallas import tpu as pltpu
from jax.sharding import Mesh
from jax.sharding import PartitionSpec as P

DILATION_STEP = 256
AXES = ("outer", "core", "far", "near")
HALVES = 2
NEAR = 4
LANES = 128
ROWS = 512
ONES = 16
F32 = jnp.float32
BF16 = jnp.bfloat16
MEGA = 1 << 20
COSTS = {
    "load": 8, "head": 2, "gradients_0": 0, "forward_1": 0, "gradients_1": 4, "outputs": 4, "near_sum_0": 8,
    "far_sum_0": 8, "near_sum_1": 4, "near_join_0": 2, "near_join_1": 4, "far_join_0": 4,
}
FLOPS = 10**9


def dot(left, right):
    return jnp.dot(left, right, preferred_element_type=F32)


def across(left, right):
    return lax.dot_general(left, right, (((0,), (0,)), ((), ())), preferred_element_type=F32)


def against(left, weight):
    return lax.dot_general(left, weight, (((1,), (1,)), ((), ())), preferred_element_type=F32)


def column(lines):
    turned = lines.astype(F32).T
    return jnp.concatenate([turned[:, k : k + 1] for k in range(lines.shape[0])], axis=0)


def row(lines):
    return jnp.concatenate([lines[k : k + 1] for k in range(lines.shape[0])], axis=1)


def tap_of(lines):
    return jnp.where(lines >= DILATION_STEP, 1, 0)


def lines_of(ref, rows):
    return ref[rows.start // LANES : rows.stop // LANES, :]


def picked(head, rest, rows):
    cut = DILATION_STEP
    low = head[rows.start : min(rows.stop, cut), :] if rows.start < cut else None
    high = rest[max(rows.start, cut) - cut : rows.stop - cut, :] if rows.stop > cut else None
    if low is None:
        return high
    return low if high is None else jnp.concatenate([low, high], axis=0)


def call(kernel, name, in_specs, out_specs, out_shape, scratch=(), aliases=None, grid=(), vmem=24):
    return pl.pallas_call(
        kernel,
        grid=grid,
        in_specs=in_specs,
        out_specs=out_specs,
        out_shape=out_shape,
        scratch_shapes=list(scratch),
        input_output_aliases=aliases or {},
        cost_estimate=pl.CostEstimate(
            flops=1 + int(FLOPS * COSTS.get(name, COSTS.get(name.split("_")[0], 0))), bytes_accessed=1, transcendentals=0
        ),
        name=name,
        compiler_params=pltpu.CompilerParams(vmem_limit_bytes=vmem * MEGA),
    )


VMEM = pl.BlockSpec(memory_space=pltpu.VMEM)
ANYWHERE = pl.BlockSpec(memory_space=pl.ANY)
MARK = jax.ShapeDtypeStruct((8, LANES), F32)


def beside(*parts):
    return jnp.concatenate(parts, axis=1)


def below(*parts):
    return jnp.concatenate(parts, axis=0)


def gates(half, rows, past, sig, feats, w_in, w_cond, b_conv):
    width = sig.shape[1]
    part = w_in.shape[1] // 2 // HALVES
    made = []
    for at in (half * part, (HALVES + half) * part):
        here = slice(at, at + part)
        own = dot(past, w_in[:width, here]) + dot(sig[rows, :], w_in[width:, here])
        made.append(own + across(feats, w_cond[:, here]) + b_conv[:, here])
    return made


def d_gated(half, rows, gout, gskip, w_res, w_skip):
    part = w_res.shape[0] // HALVES
    here = slice(half * part, (half + 1) * part)
    return against(gout[rows, :], w_res[here, :]) + against(gskip[rows, :], w_skip[here, :])


def activated(pre_a, pre_s):
    act = jnp.tanh(pre_a)
    gate = 0.5 + 0.5 * jnp.tanh(0.5 * pre_s)
    return act, gate, (act * gate).astype(BF16)


def slopes(act, gate, dgated, mask):
    slope = (mask * dgated) * gate
    return beside(slope * (1.0 - act * act), slope * act * (1.0 - gate)).astype(BF16)


def rest_rows(rows, tile=ROWS):
    cuts = sorted({DILATION_STEP, *range(tile, rows + 1, tile)})
    return [slice(a, b) for a, b in zip(cuts, cuts[1:])]


def moved(rows):
    return slice(rows.start - DILATION_STEP, rows.stop - DILATION_STEP)


def pipelined(items, first, second):
    waiting = None
    for item in items:
        made = first(item)
        if waiting:
            second(*waiting)
        waiting = (item, made)
    second(*waiting)


def load_body(
    valid, pos, b_conv, b_res, b_skip, feat, w_cond, w_res, w_skip, w_past, w_now, sig, gout, gskip,
    valid_to, pos_to, b_conv_to, b_res_to, b_skip_to, w_cond_to, w_res_to, w_skip_to, w_in, past, sig_to, feat_to,
    gout_to, gskip_to, gated_rest, kept_rest, dpre_rest, acts, gatings, sems,
):
    rows_all, width = sig.shape
    cond = feat.shape[0]
    count = 0

    def start(source, target):
        nonlocal count
        copy = pltpu.make_async_copy(source, target, sems.at[count])
        copy.start()
        count += 1
        return copy

    def tile(i, source, target):
        rows = pl.ds(i * ROWS, ROWS)
        return start(source.at[rows], target.at[rows])

    steps = rows_all // ROWS
    signals = [tile(0, sig, sig_to)]
    needs = [
        start(pos, pos_to),
        start(w_past, w_in.at[pl.ds(0, width)]),
        start(w_now, w_in.at[pl.ds(width, width)]),
        start(feat, feat_to.at[pl.ds(0, cond)]),
        start(w_cond, w_cond_to),
        start(b_conv, b_conv_to),
        start(valid, valid_to),
    ]
    signals += [tile(i, sig, sig_to) for i in range(1, steps)]
    feat_to[cond:, :] = jnp.ones((feat_to.shape[0] - cond, rows_all), BF16)
    later = []

    def produce(rows):
        i = rows.start // ROWS
        signals[i].wait()
        if i == 0:
            for copy in needs:
                copy.wait()
            later.extend([start(w_res, w_res_to), start(w_skip, w_skip_to)])
            for k in range(steps):
                later.extend([tile(k, gout, gout_to), tile(k, gskip, gskip_to)])
            later.extend([start(b_res, b_res_to), start(b_skip, b_skip_to)])
        there = moved(rows)
        tap = column(tap_of(lines_of(pos_to, rows)))
        past[rows, :] = sig_to[there, :] * tap.astype(BF16)
        return gates(0, rows, past[rows, :], sig_to, feat_to[:cond, rows], w_in, w_cond_to, b_conv_to)

    def activate(rows, made):
        there = moved(rows)
        acts[there, :], gatings[there, :], gated = activated(*made)
        gated_rest[there, :] = gated
        kept_rest[there, :] = gated * column(lines_of(valid_to, rows)).astype(BF16)

    def back(rows):
        if rows.start < ROWS:
            later[0].wait()
            later[1].wait()
        for copy in later[2 + 2 * (rows.start // ROWS) : 4 + 2 * (rows.start // ROWS)]:
            copy.wait()
        return d_gated(0, rows, gout_to, gskip_to, w_res_to, w_skip_to)

    def finish(rows, dgated):
        there = moved(rows)
        mask = column(lines_of(valid_to, rows))
        dpre_rest[there, :] = slopes(acts[there, :], gatings[there, :], dgated, mask)

    tiles = rest_rows(rows_all)
    pipelined(tiles, produce, activate)
    pipelined(tiles, back, finish)
    for copy in later[2 + 2 * steps :]:
        copy.wait()


def rest_shapes(rest, part):
    return [jax.ShapeDtypeStruct((rest, size), BF16) for size in (part, part, 2 * part)]


def load(*arrays):
    sources = [in_hbm(x) for x in arrays]
    feat, w_cond, w_res, w_skip, w_past, w_now, sig, gout, gskip = arrays[5:]
    rows, width = sig.shape
    hidden = w_res.shape[0]
    part = hidden // HALVES
    rest = rows - DILATION_STEP
    shapes = [jax.ShapeDtypeStruct(x.shape, x.dtype) for x in arrays[:5] + (w_cond, w_res, w_skip)] + [
        jax.ShapeDtypeStruct(shape, BF16)
        for shape in (
            (2 * width, 2 * hidden), sig.shape, sig.shape, (feat.shape[0] + ONES, rows), gout.shape, gskip.shape,
        )
    ]
    shapes += rest_shapes(rest, part)
    return call(
        load_body,
        "load",
        [ANYWHERE] * len(sources),
        [VMEM] * len(shapes),
        shapes,
        scratch=[
            pltpu.VMEM((rest, part), F32),
            pltpu.VMEM((rest, part), F32),
            pltpu.SemaphoreType.DMA((11 + 3 * (rows // ROWS),)),
        ],
    )(*sources)


def side_by_side(dpre_0, dpre_1):
    part = dpre_0.shape[1] // 2
    return beside(dpre_0[:, :part], dpre_1[:, :part], dpre_0[:, part:], dpre_1[:, part:])


def head_body(halo, pos, valid, sig, feat, gout, gskip, w_in, w_cond, b_conv, w_res, w_skip, past_out, *outs):
    rows = slice(0, DILATION_STEP)
    cond = w_cond.shape[0]
    mask = column(lines_of(valid, rows))
    past = halo[...] * column(tap_of(lines_of(pos, rows))).astype(BF16)
    past_out[...] = past
    made = [
        (gates(half, rows, past, sig, feat[:cond, rows], w_in, w_cond, b_conv), d_gated(half, rows, gout, gskip, w_res, w_skip))
        for half in range(HALVES)
    ]
    for half in range(HALVES):
        pre, dgated = made[half]
        act, gate, gated = activated(*pre)
        for ref, value in zip(outs[3 * half :], (gated, gated * mask.astype(BF16), slopes(act, gate, dgated, mask))):
            ref[...] = value


def head(halo, *args):
    width = halo.shape[1]
    part = args[-1].shape[0] // HALVES
    past, *parts = call(
        head_body,
        "head",
        [VMEM] * (1 + len(args)),
        [VMEM] * (1 + 3 * HALVES),
        [jax.ShapeDtypeStruct((DILATION_STEP, width), BF16)] + rest_shapes(DILATION_STEP, part) * HALVES,
    )(halo, *args)
    return past, parts[:3], parts[3:]


def early_body(token, pos, dpre_0, dpre_1, w_in, early):
    tap = column(tap_of(lines_of(pos, slice(0, DILATION_STEP))))
    early[...] = (tap * against(side_by_side(dpre_0[...], dpre_1[...]), w_in[: early.shape[1], :])).astype(BF16)


def early_rows(token, pos, dpre_0, dpre_1, w_in):
    return call(
        early_body,
        "early",
        [ANYWHERE] + [VMEM] * 4,
        VMEM,
        jax.ShapeDtypeStruct((DILATION_STEP, w_in.shape[0] // 2), BF16),
    )(token, pos, dpre_0, dpre_1, w_in)


def forward_body(
    token, valid, past, sig, feat, gout, gskip, w_in, w_cond, b_conv, w_res, w_skip, gated_out, kept_out, dpre_out
):
    cond = w_cond.shape[0]

    def produce(rows):
        pre = gates(1, rows, past[rows, :], sig, feat[:cond, rows], w_in, w_cond, b_conv)
        return pre, d_gated(1, rows, gout, gskip, w_res, w_skip)

    def finish(rows, made):
        there = moved(rows)
        mask = column(lines_of(valid, rows))
        act, gate, gated = activated(*made[0])
        gated_out[there, :] = gated
        kept_out[there, :] = gated * mask.astype(BF16)
        dpre_out[there, :] = slopes(act, gate, made[1], mask)

    pipelined(rest_rows(sig.shape[0], ROWS // 2), produce, finish)


def forward_rest(token, *args):
    return call(
        forward_body,
        "forward_1",
        [ANYWHERE] + [VMEM] * len(args),
        [VMEM] * 3,
        rest_shapes(args[0].shape[0] * LANES - DILATION_STEP, args[-1].shape[0] // HALVES),
    )(token, *args)


def own_place():
    return [lax.axis_index(name) for name in ("core", "far", "near")]


def turned(index, count):
    bits = (count - 1).bit_length()
    result = 0
    for bit in range(bits):
        result = result | (((index >> bit) & 1) << (bits - 1 - bit))
    return result


def place_blocks(far, block, acc, theirs, mine):
    core, z, xy = own_place()
    for r in range(far):
        for c in range(NEAR):
            here = pl.ds(c * LANES, LANES)
            for k, out in ((1 - core, theirs), (core, mine)):
                rows = pl.ds(pl.multiple_of((k * far + r) * block, 16), block)
                out[c ^ xy, turned(r ^ z, far)] = acc[rows, here].astype(out.dtype)


def gradients_body(
    far, block, half, token, valid, past, sig, feat, gout, gskip, past_head, kept_head, kept_rest, dpre_head, dpre_rest,
    theirs, mine, acc,
):
    cut = DILATION_STEP
    width = sig.shape[1]
    part = kept_head.shape[1]
    count = feat.shape[0]
    dpres = (dpre_head[...], dpre_rest[...])
    acc[:width, :] = across(past_head[...], dpres[0]) + across(past[cut:, :], dpres[1])
    acc[width : 2 * width, :] = across(sig[:cut, :], dpres[0]) + across(sig[cut:, :], dpres[1])
    acc[2 * width : 2 * width + count, :] = dot(feat[:, :cut], dpres[0]) + dot(feat[:, cut:], dpres[1])
    at = 2 * width + count
    for ref in (gout, gskip):
        acc[at : at + part, :] = across(kept_head[...], ref[:cut, :]) + across(kept_rest[...], ref[cut:, :])
        at += part
    mask = jnp.broadcast_to(row(valid[...].astype(F32)).astype(BF16), (ONES, valid.shape[0] * LANES))
    acc[at : at + ONES, :] = dot(mask, (gout, gskip)[half][...])
    at += ONES
    acc[at:, :] = jnp.zeros((acc.shape[0] - at, acc.shape[1]), F32)
    place_blocks(far, block, acc, theirs, mine)


def gradients(half, token, far, block, valid, past, sig, feat, gout, gskip, past_head, head_parts, rest_parts):
    packed = (NEAR, far, block, LANES)
    wide = rest_parts[2].shape[1]
    return call(
        functools.partial(gradients_body, far, block, half),
        f"gradients_{half}",
        [ANYWHERE] + [VMEM] * 11,
        [VMEM] * 2,
        [jax.ShapeDtypeStruct(packed, BF16), jax.ShapeDtypeStruct(packed, F32)],
        scratch=[pltpu.VMEM((2 * far * block, wide), F32)],
    )(
        token, valid, past, sig, feat, gout, gskip, past_head,
        head_parts[1], rest_parts[1], head_parts[2], rest_parts[2],
    )


def outputs_body(
    token, valid, sig, head_0, rest_0, head_1, rest_1, w_res, w_skip, b_res, b_skip, out, skip, mark, rooms, sems
):
    copies = []
    for i in range(sig.shape[0] // ROWS):
        rows = slice(i * ROWS, (i + 1) * ROWS)
        mask = column(lines_of(valid, rows))
        gated = beside(picked(head_0, rest_0, rows), picked(head_1, rest_1, rows))
        branch = dot(gated, w_res[...]) + b_res[...]
        rooms[i, 0] = (sig[rows, :].astype(F32) + mask * branch).astype(BF16)
        side = dot(gated, w_skip[...]) + b_skip[...]
        rooms[i, 1] = (mask * side).astype(BF16)
        for k, ref in enumerate((out, skip)):
            copies.append(pltpu.make_async_copy(rooms.at[i, k], ref.at[pl.ds(i * ROWS, ROWS)], sems.at[i, k]))
            copies[-1].start()
    mark[...] = jnp.zeros_like(mark)
    for copy in copies:
        copy.wait()


def outputs(token, valid, sig, gated_0, gated_1, w_res, w_skip, b_res, b_skip):
    rows, width = sig.shape
    return call(
        outputs_body,
        "outputs",
        [ANYWHERE] + [VMEM] * 10,
        [ANYWHERE, ANYWHERE, VMEM],
        [
            jax.ShapeDtypeStruct((rows, width), BF16),
            jax.ShapeDtypeStruct((rows, w_skip.shape[1]), BF16),
            MARK,
        ],
        scratch=[
            pltpu.VMEM((rows // ROWS, 2, ROWS, width), BF16),
            pltpu.SemaphoreType.DMA((rows // ROWS, 2)),
        ],
    )(token, valid, sig, *gated_0, *gated_1, w_res, w_skip, b_res, b_skip)


def inputs_body(steps, token, received, gout, pos, head_0, rest_0, head_1, rest_1, w_in, w_cond, *refs):
    gsig, gfeat, mark, room, room_feat, sems = refs[-6:]
    rows, width = gout.shape
    copies = []
    wide = 2 * LANES

    def copy(source, target):
        copies.append(pltpu.make_async_copy(source, target, sems.at[len(copies)]))
        copies[-1].start()

    for i, step in enumerate(steps):
        begin = step * ROWS
        here = slice(begin, begin + ROWS)
        after = slice(begin + DILATION_STEP, min(begin + DILATION_STEP + ROWS, rows))
        now = side_by_side(picked(head_0, rest_0, here), picked(head_1, rest_1, here))
        later = side_by_side(picked(head_0, rest_0, after), picked(head_1, rest_1, after))
        tap = column(tap_of(lines_of(pos, after)))
        room_feat[i] = against(w_cond[...], now)
        copy(room_feat.at[i], gfeat.at[:, pl.ds(begin, ROWS)])
        for k in range(width // wide):
            some = slice(k * wide, (k + 1) * wide)
            tail = tap * against(later, w_in[some, :])
            if tail.shape[0] < ROWS:
                tail = below(tail, received[:, some].astype(F32))
            room[i, k] = gout[here, some].astype(F32) + against(now, w_in[width + k * wide : width + (k + 1) * wide, :]) + tail
            copy(room.at[i, k], gsig.at[pl.ds(begin, ROWS), pl.ds(k * wide, wide)])
    mark[...] = jnp.zeros_like(mark)
    for one in copies:
        one.wait()


def inputs(steps, token, received, gout, pos, dpre_0, dpre_1, w_in, w_cond, before):
    rows, width = gout.shape
    cond = w_cond.shape[0]
    count = width // (2 * LANES)
    return call(
        functools.partial(inputs_body, steps),
        f"inputs_{steps[0]}",
        [ANYWHERE] + [VMEM] * 9 + [ANYWHERE] * len(before),
        [ANYWHERE, ANYWHERE, VMEM],
        [
            jax.ShapeDtypeStruct((rows, width), F32),
            jax.ShapeDtypeStruct((cond, rows), F32),
            MARK,
        ],
        scratch=[
            pltpu.VMEM((len(steps), count, ROWS, 2 * LANES), F32),
            pltpu.VMEM((len(steps), cond, ROWS), F32),
            pltpu.SemaphoreType.DMA((len(steps) * (count + 1),)),
        ],
        aliases={10 + k: k for k in range(len(before))},
    )(token, received, gout, pos, *dpre_0, *dpre_1, w_in, w_cond, *before)


def unpack_body(far, block, token, mine, theirs, *refs):
    arrays, (mark, room) = refs[-9:-2], refs[-2:]
    mark[...] = jnp.zeros_like(mark)
    core, z, xy = own_place()

    @pl.when(pl.program_id(0) == 0)
    def _():
        for k, ref in ((core, mine), (1 - core, theirs)):
            for c in range(NEAR):
                for r in range(far):
                    rows = pl.ds(pl.multiple_of((k * far + (r ^ z)) * block, 16), block)
                    room[c ^ xy, rows, :] = ref[c, turned(r, far)]

    for j in range(NEAR // 2):
        c = pl.program_id(0) * (NEAR // 2) + j
        here = pl.ds(j * LANES, LANES)
        top = 0
        for ref in arrays:
            count = ref.shape[0]
            size = max(count, ONES)
            ref[:, here] = room[c, top : top + size, :].astype(F32)[:count]
            top += size


def unpack(half, token, far, block, mine, theirs, width, cond, hidden, skip_width, before):
    part = hidden // HALVES
    gates = 2 * hidden
    own = (width, skip_width)[half]

    def wide(size):
        return pl.BlockSpec((size, part), lambda s: (0, HALVES * s + half))

    def tall(size):
        return pl.BlockSpec((part, size // 2), lambda s: (half, s))

    specs = [wide(width), wide(width), wide(cond), wide(1), tall(width), tall(skip_width), pl.BlockSpec((1, own // 2), lambda s: (0, s))]
    shapes = [(width, gates), (width, gates), (cond, gates), (1, gates), (hidden, width), (hidden, skip_width), (1, own)]
    packed = (NEAR, far, block, LANES)
    blocks = pl.BlockSpec(packed, lambda s: (0,) * len(packed))
    return call(
        functools.partial(unpack_body, far, block),
        f"unpack_{half}",
        [ANYWHERE, blocks, blocks] + [ANYWHERE] * len(before),
        specs + [pl.BlockSpec(MARK.shape, lambda s: (0, 0))],
        [jax.ShapeDtypeStruct(shape, F32) for shape in shapes] + [MARK],
        scratch=[pltpu.VMEM((NEAR, 2 * far * block, LANES), BF16)],
        aliases={3 + k: k for k in range(len(before))},
        grid=(2,),
    )(token, mine, theirs, *before)


def swapped(x, axis, k):
    return lax.ppermute(x, axis, [(i, i ^ k) for i in range(lax.axis_size(axis))])


def exchanged(blocks):
    return [swapped(block, "near", k + 1) for k, block in enumerate(blocks)]


def add_body(sizes, token, *refs):
    count = len(sizes)
    kept, got, outs = refs[0], refs[1:-count], refs[-count:]
    at = 0
    for out, size in zip(outs, sizes):
        for k in range(size):
            total = kept[at + k].astype(F32)
            for ref in got:
                total = total + ref[at + k].astype(F32)
            out[k] = total.astype(out.dtype)
        at += size


def added(name, token, kept, got, outs):
    sizes = [size for size, _ in outs]
    result = call(
        functools.partial(add_body, sizes),
        name,
        [ANYWHERE] + [VMEM] * (1 + len(got)),
        [VMEM] * len(outs),
        [jax.ShapeDtypeStruct((size, *kept.shape[1:]), dtype) for size, dtype in outs],
    )(token, kept, *got)
    return result


def mirror_body(token, mine, got, out):
    count = mine.shape[0]
    for k in range(count):
        out[k] = (mine[k].astype(F32) + got[count - 1 - k].astype(F32)).astype(out.dtype)


def mirrored(name, token, mine, got):
    return call(
        mirror_body,
        name,
        [ANYWHERE, VMEM, VMEM],
        VMEM,
        jax.ShapeDtypeStruct(mine.shape, BF16),
    )(token, mine, got)


def join_body(token, *refs):
    out = refs[-1]
    at = 0
    for ref in refs[:-1]:
        out[at : at + ref.shape[0]] = ref[...]
        at += ref.shape[0]


def joined(name, token, parts):
    count = sum(part.shape[0] for part in parts)
    return call(
        join_body,
        name,
        [ANYWHERE] + [VMEM] * len(parts),
        VMEM,
        jax.ShapeDtypeStruct((count, *parts[0].shape[1:]), BF16),
    )(token, *parts)


def over_outer(total):
    for bit in range((lax.axis_size("outer") - 1).bit_length()):
        total = (total.astype(F32) + swapped(total, "outer", 1 << bit).astype(F32)).astype(BF16)
    return total


def passed_along(x, by):
    peers = lax.axis_size(AXES)
    pairs = [(i, i + by) for i in range(peers) if 0 <= i + by < peers]
    return lax.ppermute(x, AXES, pairs)


def in_hbm(x):
    return pltpu.with_memory_space_constraint(x, pltpu.HBM)


def body(
    signal,
    features,
    position,
    valid,
    w_past,
    w_now,
    b_conv,
    w_cond,
    w_res,
    b_res,
    w_skip,
    b_skip,
    grad_out,
    grad_skip,
):
    rows, width = signal.shape
    features = features.T
    cond = features.shape[0]
    hidden = w_res.shape[0]
    skip_width = w_skip.shape[1]
    far = lax.axis_size("far")
    far_bits = (far - 1).bit_length()
    used = 2 * width + cond + ONES + 2 * (hidden // HALVES) + ONES
    block = -(-used // (2 * far * 16)) * 16
    lines = (rows // LANES, LANES)
    pos, val = position.reshape(lines), valid.reshape(lines)
    b_conv, b_res, b_skip = (b.reshape(1, -1) for b in (b_conv, b_res, b_skip))

    def core_sum(half, token, theirs, mine):
        kept, *sent = added(
            f"core_sum_{half}", token, mine, [swapped(theirs, "core", 1)], [(1, F32)] + [(1, BF16)] * (NEAR - 1)
        )
        return kept[0], exchanged([x[0] for x in sent])

    def near_sum(half, token, kept, got):
        kept, sent = added(f"near_sum_{half}", token, kept, got, [(far // 2, F32), (far // 2, BF16)])
        return kept, swapped(sent, "far", 1)

    def far_sum(half, token, kept, got):
        for bit in range(1, far_bits - 1):
            size = kept.shape[0] // 2
            kept, sent = added(f"far_sum_{half}_{bit}", token, kept, [got], [(size, F32), (size, BF16)])
            got = swapped(sent, "far", 1 << bit)
        (mine,) = added(f"far_sum_{half}", token, kept, [got], [(kept.shape[0], BF16)])
        return mine, swapped(mine, "far", 1 << (far_bits - 1))

    def far_end(half, token, mine, got):
        total = over_outer(mirrored(f"far_end_{half}", token, mine, got))
        return total, swapped(total, "far", 1 << (far_bits - 2))

    def far_join(half, token, mine, got):
        total = joined(f"far_join_{half}", token, [mine, got])
        for bit in reversed(range(far_bits - 2)):
            total = joined(f"far_join_{half}_{bit}", token, [total, swapped(total, "far", 1 << bit)])
        return total, exchanged([total] * (NEAR - 1))

    def near_join(half, token, mine, got):
        total = joined(f"near_join_{half}", token, [mine[None]] + [x[None] for x in got])
        return total, swapped(total, "core", 1)

    def input_gradients(steps, token, before):
        last = (steps[-1] + 1) * ROWS == rows
        return inputs(steps, token, received if last else head_0[0], grad_out, pos, dpre_0, dpre_1, w_in, w_cond, before)

    halo = passed_along(signal[rows - DILATION_STEP :], 1)
    val, pos, b_conv, b_res, b_skip, w_cond, w_res, w_skip, w_in, past, signal, features, grad_out, grad_skip, *rest_0 = load(
        val, pos, b_conv, b_res, b_skip, features, w_cond, w_res, w_skip, w_past, w_now, signal, grad_out, grad_skip
    )
    common = (signal, features, grad_out, grad_skip, w_in, w_cond, b_conv, w_res, w_skip)
    past_head, head_0, head_1 = head(halo, pos, val, *common)
    theirs_0, mine_0 = gradients(0, past_head, far, block, val, past, signal, features, grad_out, grad_skip, past_head, head_0, rest_0)
    rest_1 = forward_rest(theirs_0, val, past, *common)
    dpre_0, dpre_1 = (head_0[2], rest_0[2]), (head_1[2], rest_1[2])
    kept_0, got_0 = core_sum(0, rest_1[0], theirs_0, mine_0)
    theirs_1, mine_1 = gradients(1, kept_0, far, block, val, past, signal, features, grad_out, grad_skip, past_head, head_1, rest_1)
    output, skip_out, mark = outputs(
        theirs_1, val, signal, (head_0[0], rest_0[0]), (head_1[0], rest_1[0]), w_res, w_skip, b_res, b_skip
    )
    kept_0, got_0 = near_sum(0, mark, kept_0, got_0)
    kept_1, got_1 = core_sum(1, kept_0, theirs_1, mine_1)
    ends_0, got_0 = far_sum(0, kept_1, kept_0, got_0)
    *grads, mark = input_gradients((0, 1), ends_0, [])
    ends_0, got_0 = far_end(0, mark, ends_0, got_0)
    kept_1, got_1 = near_sum(1, ends_0, kept_1, got_1)
    ends_0, got_0 = far_join(0, kept_1, ends_0, got_0)
    ends_1, got_1 = far_sum(1, ends_0, kept_1, got_1)
    *grads, mark = input_gradients((2,), ends_1, grads)
    ends_1, got_1 = far_end(1, mark, ends_1, got_1)
    early = early_rows(ends_1, pos, head_0[2], head_1[2], w_in)
    received = passed_along(early, -1)
    blocks_0, others_0 = near_join(0, early, ends_0, got_0)
    ends_1, got_1 = far_join(1, blocks_0, ends_1, got_1)
    *grads, mark = input_gradients((3,), ends_1, grads)
    blocks_1, others_1 = near_join(1, mark, ends_1, got_1)
    *done, own_0, mark = unpack(0, blocks_1, far, block, blocks_0, others_0, width, cond, hidden, skip_width, [])
    *done, own_1, _ = unpack(1, mark, far, block, blocks_1, others_1, width, cond, hidden, skip_width, done)
    g_past, g_now, g_cond, g_bias, g_res, g_skip = done
    grad_signal, grad_features = grads
    return (
        output,
        skip_out,
        grad_signal,
        grad_features.T,
        g_past,
        g_now,
        g_bias.reshape(-1),
        g_cond,
        g_res,
        own_0.reshape(-1),
        g_skip,
        own_1.reshape(-1),
    )


def solution(mesh):
    row, col = mesh.shape["row"], mesh.shape["col"]
    fine = Mesh(mesh.devices.reshape(row // 2, 2, col // NEAR, NEAR), AXES)
    rows = P(AXES, None)
    line = P(AXES)
    return jax.shard_map(
        body,
        mesh=fine,
        in_specs=(rows, rows, line, line) + (P(),) * 8 + (rows, rows),
        out_specs=(rows,) * 4 + (P(),) * 8,
        check_vma=False,
    )
```

```python
import functools

import jax
import jax.numpy as jnp
from jax import lax
from jax.experimental import pallas as pl
from jax.experimental.pallas import tpu as pltpu
from jax.sharding import Mesh
from jax.sharding import PartitionSpec as P

DILATION_STEP = 256
AXES = ("outer", "core", "far", "near")
HALVES = 2
NEAR = 4
LANES = 128
ROWS = 512
ONES = 16
F32 = jnp.float32
BF16 = jnp.bfloat16
MEGA = 1 << 20
COSTS = {
    "load": 8, "head": 2, "gradients_0": 0, "forward_1": 0, "gradients_1": 4, "outputs": 4, "near_sum_0": 8,
    "far_sum_0": 8, "near_sum_1": 4, "near_join_0": 2, "near_join_1": 4, "far_join_0": 4,
}
FLOPS = 10**9


def dot(left, right):
    return jnp.dot(left, right, preferred_element_type=F32)


def across(left, right):
    return lax.dot_general(left, right, (((0,), (0,)), ((), ())), preferred_element_type=F32)


def against(left, weight):
    return lax.dot_general(left, weight, (((1,), (1,)), ((), ())), preferred_element_type=F32)


def column(lines):
    turned = lines.astype(F32).T
    return jnp.concatenate([turned[:, k : k + 1] for k in range(lines.shape[0])], axis=0)


def row(lines):
    return jnp.concatenate([lines[k : k + 1] for k in range(lines.shape[0])], axis=1)


def tap_of(lines):
    return jnp.where(lines >= DILATION_STEP, 1, 0)


def lines_of(ref, rows):
    return jnp.concatenate([ref[k] for k in range(rows.start // DILATION_STEP, rows.stop // DILATION_STEP)], axis=0)


def picked(head, rest, rows):
    cut = DILATION_STEP
    low = head[rows.start : min(rows.stop, cut), :] if rows.start < cut else None
    high = rest[max(rows.start, cut) - cut : rows.stop - cut, :] if rows.stop > cut else None
    if low is None:
        return high
    return low if high is None else jnp.concatenate([low, high], axis=0)


def call(kernel, name, in_specs, out_specs, out_shape, scratch=(), aliases=None, grid=(), vmem=24):
    return pl.pallas_call(
        kernel,
        grid=grid,
        in_specs=in_specs,
        out_specs=out_specs,
        out_shape=out_shape,
        scratch_shapes=list(scratch),
        input_output_aliases=aliases or {},
        cost_estimate=pl.CostEstimate(
            flops=1 + int(FLOPS * COSTS.get(name, COSTS.get(name.split("_")[0], 0))), bytes_accessed=1, transcendentals=0
        ),
        name=name,
        compiler_params=pltpu.CompilerParams(vmem_limit_bytes=vmem * MEGA),
    )


VMEM = pl.BlockSpec(memory_space=pltpu.VMEM)
ANYWHERE = pl.BlockSpec(memory_space=pl.ANY)
MARK = jax.ShapeDtypeStruct((8, LANES), F32)


def beside(*parts):
    return jnp.concatenate(parts, axis=1)


def below(*parts):
    return jnp.concatenate(parts, axis=0)


def products(half, rows, past, sig, feats, gout, gskip, w_in, w_cond, b_conv, w_res, w_skip, arrive=None):
    part = w_res.shape[0] // HALVES
    width = sig.shape[1]
    first = half * part
    made = []
    for k, at in enumerate((first, HALVES * part + first)):
        here = slice(at, at + part)
        if arrive:
            arrive(rows, k)
        own = dot(past, w_in[:width, here]) + dot(sig[rows, :], w_in[width:, here])
        made.append(own + across(feats, w_cond[:, here]) + b_conv[:, here])
    if arrive:
        arrive(rows, 2)
    here = slice(first, first + part)
    return *made, against(gout[rows, :], w_res[here, :]) + against(gskip[rows, :], w_skip[here, :])


def finish(pre_a, pre_s, dgated, valid_lines):
    act = jnp.tanh(pre_a)
    gate = 0.5 + 0.5 * jnp.tanh(0.5 * pre_s)
    slope = (column(valid_lines) * dgated) * gate
    dpre = beside(slope * (1.0 - act * act), slope * act * (1.0 - gate)).astype(BF16)
    gated = (act * gate).astype(BF16)
    return gated, gated.T * row(valid_lines.astype(BF16)), dpre


def forward_tiles(half, tiles, prepare, arrive, valid, past, sig, x_turned, gout, gskip, weights, gated_out, kept_out, dpre_out):
    cond = weights[1].shape[0]
    width = sig.shape[1]

    def done(rows, *made):
        there = slice(rows.start - DILATION_STEP, rows.stop - DILATION_STEP)
        gated_out[there, :], kept_out[:, there], dpre_out[there, :] = finish(*made, lines_of(valid, rows))

    waiting = None
    for rows in tiles:
        if prepare:
            prepare(rows)
        feats = x_turned[2 * width : 2 * width + cond, rows]
        made = products(half, rows, past[rows, :], sig, feats, gout, gskip, *weights, arrive=arrive)
        if waiting:
            done(*waiting)
        waiting = (rows, *made)
    done(*waiting)


def rest_rows(rows, tile=ROWS):
    cuts = sorted({DILATION_STEP, *range(tile, rows + 1, tile)})
    return [slice(a, b) for a, b in zip(cuts, cuts[1:])]


def load_body(
    valid, pos, b_conv, b_res, b_skip, feat, w_cond, w_res, w_skip, w_past, w_now, sig, gout, gskip,
    valid_to, pos_to, b_conv_to, b_res_to, b_skip_to, w_cond_to, w_res_to, w_skip_to, w_in, past, sig_to, x_turned,
    gout_to, gskip_to, gated_rest, kept_rest, dpre_rest, sems,
):
    rows_all, width = sig.shape
    cond = feat.shape[0]
    count = 0

    def start(source, target):
        nonlocal count
        copy = pltpu.make_async_copy(source, target, sems.at[count])
        copy.start()
        count += 1
        return copy

    def tile(i, source, target):
        rows = pl.ds(i * ROWS, ROWS)
        return start(source.at[rows], target.at[rows])

    signals = [tile(0, sig, sig_to)]
    needs = [
        [
            start(pos, pos_to),
            start(w_past, w_in.at[pl.ds(0, width)]),
            start(w_now, w_in.at[pl.ds(width, width)]),
            start(feat, x_turned.at[pl.ds(2 * width, cond)]),
            start(w_cond, w_cond_to),
            start(b_conv, b_conv_to),
        ],
        [],
        [start(valid, valid_to), start(w_res, w_res_to), start(w_skip, w_skip_to)],
    ]
    cotangents = [[tile(0, gout, gout_to), tile(0, gskip, gskip_to)]]
    for i in range(1, rows_all // ROWS):
        signals.append(tile(i, sig, sig_to))
        cotangents.append([tile(i, gout, gout_to), tile(i, gskip, gskip_to)])
    last = [start(b_res, b_res_to), start(b_skip, b_skip_to)]

    def wait(copies):
        for copy in copies:
            copy.wait()
        copies.clear()

    def prepare(rows):
        i = rows.start // ROWS
        signals[i].wait()
        wait(needs[0])
        whole = slice(i * ROWS, (i + 1) * ROWS)
        before = slice(rows.start - DILATION_STEP, rows.stop - DILATION_STEP)
        tap = tap_of(lines_of(pos_to, rows)).astype(F32)
        past[rows, :] = sig_to[before, :] * column(tap).astype(BF16)
        x_turned[width : 2 * width, whole] = sig_to[whole, :].T
        x_turned[:width, rows] = x_turned[width : 2 * width, before] * row(tap).astype(BF16)

    def arrive(rows, k):
        wait(needs[k])
        if k == 2:
            wait(cotangents[rows.start // ROWS])

    x_turned[2 * width + cond :, :] = jnp.ones((x_turned.shape[0] - 2 * width - cond, rows_all), BF16)
    forward_tiles(
        0, rest_rows(rows_all), prepare, arrive, valid_to, past, sig_to, x_turned, gout_to, gskip_to,
        (w_in, w_cond_to, b_conv_to, w_res_to, w_skip_to), gated_rest, kept_rest, dpre_rest,
    )
    wait(last)


def rest_shapes(rest, part):
    return [jax.ShapeDtypeStruct(shape, BF16) for shape in ((rest, part), (part, rest), (rest, 2 * part))]


def load(*arrays):
    sources = [in_hbm(x) for x in arrays]
    feat, w_cond, w_res, w_skip, w_past, w_now, sig, gout, gskip = arrays[5:]
    rows, width = sig.shape
    hidden = w_res.shape[0]
    shapes = [jax.ShapeDtypeStruct(x.shape, x.dtype) for x in arrays[:5] + (w_cond, w_res, w_skip)] + [
        jax.ShapeDtypeStruct(shape, BF16)
        for shape in (
            (2 * width, 2 * hidden), sig.shape, sig.shape, (2 * width + feat.shape[0] + ONES, rows), gout.shape, gskip.shape,
        )
    ]
    shapes += rest_shapes(rows - DILATION_STEP, hidden // HALVES)
    return call(
        load_body,
        "load",
        [ANYWHERE] * len(sources),
        [VMEM] * len(shapes),
        shapes,
        scratch=[pltpu.SemaphoreType.DMA((11 + 3 * (rows // ROWS),))],
    )(*sources)


def side_by_side(dpre_0, dpre_1):
    part = dpre_0.shape[1] // 2
    return beside(dpre_0[:, :part], dpre_1[:, :part], dpre_0[:, part:], dpre_1[:, part:])


def head_body(halo, pos, valid, sig, x_turned, gout, gskip, w_in, w_cond, b_conv, w_res, w_skip, past_out, *outs):
    rows = slice(0, DILATION_STEP)
    width = halo.shape[1]
    cond = w_cond.shape[0]
    tap = tap_of(lines_of(pos, rows)).astype(F32)
    past_out[...] = halo[...].T * row(tap).astype(BF16)
    past = halo[...] * column(tap).astype(BF16)
    feats = x_turned[2 * width : 2 * width + cond, rows]
    made = [
        products(half, rows, past, sig, feats, gout, gskip, w_in, w_cond, b_conv, w_res, w_skip) for half in range(HALVES)
    ]
    for half in range(HALVES):
        parts = finish(*made[half], lines_of(valid, rows))
        for ref, value in zip(outs[3 * half :], parts):
            ref[...] = value


def head(halo, *args):
    width = halo.shape[1]
    part = args[-1].shape[0] // HALVES
    past, *parts = call(
        head_body,
        "head",
        [VMEM] * (1 + len(args)),
        [VMEM] * (1 + 3 * HALVES),
        [jax.ShapeDtypeStruct((width, DILATION_STEP), BF16)] + rest_shapes(DILATION_STEP, part) * HALVES,
    )(halo, *args)
    return past, parts[:3], parts[3:]


def early_body(token, pos, dpre_0, dpre_1, w_in, early):
    tap = column(tap_of(lines_of(pos, slice(0, DILATION_STEP))))
    early[...] = (tap * against(side_by_side(dpre_0[...], dpre_1[...]), w_in[: early.shape[1], :])).astype(BF16)


def early_rows(token, pos, dpre_0, dpre_1, w_in):
    return call(
        early_body,
        "early",
        [ANYWHERE] + [VMEM] * 4,
        VMEM,
        jax.ShapeDtypeStruct((DILATION_STEP, w_in.shape[0] // 2), BF16),
    )(token, pos, dpre_0, dpre_1, w_in)


def forward_body(
    token, valid, past, sig, x_turned, gout, gskip, w_in, w_cond, b_conv, w_res, w_skip, gated_out, kept_out, dpre_out
):
    cond = w_cond.shape[0]
    width = sig.shape[1]
    size = DILATION_STEP

    def step(i, carry):
        rows = pl.ds(pl.multiple_of(i * size, size), size)
        there = pl.ds(pl.multiple_of((i - 1) * size, size), size)
        feats = x_turned[2 * width : 2 * width + cond, rows]
        made = products(1, rows, past[rows, :], sig, feats, gout, gskip, w_in, w_cond, b_conv, w_res, w_skip)
        gated_out[there, :], kept_out[:, there], dpre_out[there, :] = finish(*made, valid[i])
        return carry

    lax.fori_loop(1, sig.shape[0] // size, step, 0)


def forward_rest(token, *args):
    return call(
        forward_body,
        "forward_1",
        [ANYWHERE] + [VMEM] * len(args),
        [VMEM] * 3,
        rest_shapes(args[2].shape[0] - DILATION_STEP, args[-1].shape[0] // HALVES),
    )(token, *args)


def own_place():
    return [lax.axis_index(name) for name in ("core", "far", "near")]


def turned(index, count):
    bits = (count - 1).bit_length()
    result = 0
    for bit in range(bits):
        result = result | (((index >> bit) & 1) << (bits - 1 - bit))
    return result


def place_blocks(far, block, acc, theirs, mine):
    core, z, xy = own_place()
    for r in range(far):
        for c in range(NEAR):
            here = pl.ds(c * LANES, LANES)
            for k, out in ((1 - core, theirs), (core, mine)):
                rows = pl.ds(pl.multiple_of((k * far + r) * block, 16), block)
                out[c ^ xy, turned(r ^ z, far)] = acc[rows, here].astype(out.dtype)


def gradients_body(
    far, block, half, token, valid, x_turned, gout, gskip, past_head, kept_head, kept_rest, dpre_head, dpre_rest,
    theirs, mine, acc,
):
    cut = DILATION_STEP
    width = past_head.shape[0]
    part = kept_head.shape[0]
    wide = dpre_rest.shape[1]
    count = x_turned.shape[1]
    mask = jnp.broadcast_to(row(lines_of(valid, slice(0, count)).astype(F32)).astype(BF16), (ONES, count))
    ends = x_turned.shape[0]
    rest = below(kept_rest[...], mask[:, cut:])
    first = below(kept_head[...], mask[:, :cut])
    at = ends
    for k, ref in enumerate((gout, gskip)):
        outer = dot(rest, ref[cut:, :]) + dot(first, ref[:cut, :])
        acc[at : at + part, :] = outer[:part]
        at += part
        if k == half:
            acc[ends + 2 * part : ends + 2 * part + ONES, :] = outer[part:]
    at += ONES
    acc[at:, :] = jnp.zeros((acc.shape[0] - at, wide), F32)
    if half == 0:
        inner = dot(x_turned[:, cut:], dpre_rest[...])
        inner += dot(below(past_head[...], x_turned[width:, :cut]), dpre_head[...])
        acc[:ends, :] = inner
    else:
        size = ends // 2

        def step(i, carry):
            here = pl.ds(pl.multiple_of(i * size, 16), size)
            acc[here, :] = dot(x_turned[here, cut:], dpre_rest[...])
            return carry

        lax.fori_loop(0, 2, step, 0)
        acc[:ends, :] += dot(below(past_head[...], x_turned[width:, :cut]), dpre_head[...])
    place_blocks(far, block, acc, theirs, mine)


def gradients(half, token, far, block, valid, x_turned, gout, gskip, past_head, head_parts, rest_parts):
    packed = (NEAR, far, block, LANES)
    wide = rest_parts[2].shape[1]
    return call(
        functools.partial(gradients_body, far, block, half),
        f"gradients_{half}",
        [ANYWHERE] + [VMEM] * 9,
        [VMEM] * 2,
        [jax.ShapeDtypeStruct(packed, BF16), jax.ShapeDtypeStruct(packed, F32)],
        scratch=[pltpu.VMEM((2 * far * block, wide), F32)],
    )(token, valid, x_turned, gout, gskip, past_head, head_parts[1], rest_parts[1], head_parts[2], rest_parts[2])


def outputs_body(
    token, valid, sig, head_0, rest_0, head_1, rest_1, w_res, w_skip, b_res, b_skip, out, skip, mark, rooms, sems
):
    copies = []
    for i in range(sig.shape[0] // ROWS):
        rows = slice(i * ROWS, (i + 1) * ROWS)
        mask = column(lines_of(valid, rows))
        gated = beside(picked(head_0, rest_0, rows), picked(head_1, rest_1, rows))
        branch = dot(gated, w_res[...]) + b_res[...]
        rooms[i, 0] = (sig[rows, :].astype(F32) + mask * branch).astype(BF16)
        side = dot(gated, w_skip[...]) + b_skip[...]
        rooms[i, 1] = (mask * side).astype(BF16)
        for k, ref in enumerate((out, skip)):
            copies.append(pltpu.make_async_copy(rooms.at[i, k], ref.at[pl.ds(i * ROWS, ROWS)], sems.at[i, k]))
            copies[-1].start()
    mark[...] = jnp.zeros_like(mark)
    for copy in copies:
        copy.wait()


def outputs(token, valid, sig, gated_0, gated_1, w_res, w_skip, b_res, b_skip):
    rows, width = sig.shape
    return call(
        outputs_body,
        "outputs",
        [ANYWHERE] + [VMEM] * 10,
        [ANYWHERE, ANYWHERE, VMEM],
        [
            jax.ShapeDtypeStruct((rows, width), BF16),
            jax.ShapeDtypeStruct((rows, w_skip.shape[1]), BF16),
            MARK,
        ],
        scratch=[
            pltpu.VMEM((rows // ROWS, 2, ROWS, width), BF16),
            pltpu.SemaphoreType.DMA((rows // ROWS, 2)),
        ],
    )(token, valid, sig, *gated_0, *gated_1, w_res, w_skip, b_res, b_skip)


def inputs_body(steps, token, received, gout, pos, head_0, rest_0, head_1, rest_1, w_in, w_cond, *refs):
    gsig, gfeat, mark, room, room_feat, sems = refs[-6:]
    rows, width = gout.shape
    copies = []
    wide = 2 * LANES

    def copy(source, target):
        copies.append(pltpu.make_async_copy(source, target, sems.at[len(copies)]))
        copies[-1].start()

    for i, step in enumerate(steps):
        begin = step * ROWS
        here = slice(begin, begin + ROWS)
        after = slice(begin + DILATION_STEP, min(begin + DILATION_STEP + ROWS, rows))
        now = side_by_side(picked(head_0, rest_0, here), picked(head_1, rest_1, here))
        later = side_by_side(picked(head_0, rest_0, after), picked(head_1, rest_1, after))
        tap = column(tap_of(lines_of(pos, after)))
        room_feat[i] = against(w_cond[...], now)
        copy(room_feat.at[i], gfeat.at[:, pl.ds(begin, ROWS)])
        for k in range(width // wide):
            some = slice(k * wide, (k + 1) * wide)
            tail = tap * against(later, w_in[some, :])
            if tail.shape[0] < ROWS:
                tail = below(tail, received[:, some].astype(F32))
            room[i, k] = gout[here, some].astype(F32) + against(now, w_in[width + k * wide : width + (k + 1) * wide, :]) + tail
            copy(room.at[i, k], gsig.at[pl.ds(begin, ROWS), pl.ds(k * wide, wide)])
    mark[...] = jnp.zeros_like(mark)
    for one in copies:
        one.wait()


def inputs(steps, token, received, gout, pos, dpre_0, dpre_1, w_in, w_cond, before):
    rows, width = gout.shape
    cond = w_cond.shape[0]
    count = width // (2 * LANES)
    return call(
        functools.partial(inputs_body, steps),
        f"inputs_{steps[0]}",
        [ANYWHERE] + [VMEM] * 9 + [ANYWHERE] * len(before),
        [ANYWHERE, ANYWHERE, VMEM],
        [
            jax.ShapeDtypeStruct((rows, width), F32),
            jax.ShapeDtypeStruct((cond, rows), F32),
            MARK,
        ],
        scratch=[
            pltpu.VMEM((len(steps), count, ROWS, 2 * LANES), F32),
            pltpu.VMEM((len(steps), cond, ROWS), F32),
            pltpu.SemaphoreType.DMA((len(steps) * (count + 1),)),
        ],
        aliases={10 + k: k for k in range(len(before))},
    )(token, received, gout, pos, *dpre_0, *dpre_1, w_in, w_cond, *before)


def unpack_body(far, block, token, mine, theirs, *refs):
    arrays, (mark, room) = refs[-9:-2], refs[-2:]
    mark[...] = jnp.zeros_like(mark)
    core, z, xy = own_place()

    @pl.when(pl.program_id(0) == 0)
    def _():
        for k, ref in ((core, mine), (1 - core, theirs)):
            for c in range(NEAR):
                for r in range(far):
                    rows = pl.ds(pl.multiple_of((k * far + (r ^ z)) * block, 16), block)
                    room[c ^ xy, rows, :] = ref[c, turned(r, far)]

    for j in range(NEAR // 2):
        c = pl.program_id(0) * (NEAR // 2) + j
        here = pl.ds(j * LANES, LANES)
        top = 0
        for ref in arrays:
            count = ref.shape[0]
            size = max(count, ONES)
            ref[:, here] = room[c, top : top + size, :].astype(F32)[:count]
            top += size


def unpack(half, token, far, block, mine, theirs, width, cond, hidden, skip_width, before):
    part = hidden // HALVES
    gates = 2 * hidden
    own = (width, skip_width)[half]

    def wide(size):
        return pl.BlockSpec((size, part), lambda s: (0, HALVES * s + half))

    def tall(size):
        return pl.BlockSpec((part, size // 2), lambda s: (half, s))

    specs = [wide(width), wide(width), wide(cond), wide(1), tall(width), tall(skip_width), pl.BlockSpec((1, own // 2), lambda s: (0, s))]
    shapes = [(width, gates), (width, gates), (cond, gates), (1, gates), (hidden, width), (hidden, skip_width), (1, own)]
    packed = (NEAR, far, block, LANES)
    blocks = pl.BlockSpec(packed, lambda s: (0,) * len(packed))
    return call(
        functools.partial(unpack_body, far, block),
        f"unpack_{half}",
        [ANYWHERE, blocks, blocks] + [ANYWHERE] * len(before),
        specs + [pl.BlockSpec(MARK.shape, lambda s: (0, 0))],
        [jax.ShapeDtypeStruct(shape, F32) for shape in shapes] + [MARK],
        scratch=[pltpu.VMEM((NEAR, 2 * far * block, LANES), BF16)],
        aliases={3 + k: k for k in range(len(before))},
        grid=(2,),
    )(token, mine, theirs, *before)


def swapped(x, axis, k):
    return lax.ppermute(x, axis, [(i, i ^ k) for i in range(lax.axis_size(axis))])


def exchanged(blocks):
    return [swapped(block, "near", k + 1) for k, block in enumerate(blocks)]


def add_body(sizes, token, *refs):
    count = len(sizes)
    kept, got, outs = refs[0], refs[1:-count], refs[-count:]
    at = 0
    for out, size in zip(outs, sizes):
        for k in range(size):
            total = kept[at + k].astype(F32)
            for ref in got:
                total = total + ref[at + k].astype(F32)
            out[k] = total.astype(out.dtype)
        at += size


def added(name, token, kept, got, outs):
    sizes = [size for size, _ in outs]
    result = call(
        functools.partial(add_body, sizes),
        name,
        [ANYWHERE] + [VMEM] * (1 + len(got)),
        [VMEM] * len(outs),
        [jax.ShapeDtypeStruct((size, *kept.shape[1:]), dtype) for size, dtype in outs],
    )(token, kept, *got)
    return result


def mirror_body(token, mine, got, out):
    count = mine.shape[0]
    for k in range(count):
        out[k] = (mine[k].astype(F32) + got[count - 1 - k].astype(F32)).astype(out.dtype)


def mirrored(name, token, mine, got):
    return call(
        mirror_body,
        name,
        [ANYWHERE, VMEM, VMEM],
        VMEM,
        jax.ShapeDtypeStruct(mine.shape, BF16),
    )(token, mine, got)


def join_body(token, *refs):
    out = refs[-1]
    at = 0
    for ref in refs[:-1]:
        out[at : at + ref.shape[0]] = ref[...]
        at += ref.shape[0]


def joined(name, token, parts):
    count = sum(part.shape[0] for part in parts)
    return call(
        join_body,
        name,
        [ANYWHERE] + [VMEM] * len(parts),
        VMEM,
        jax.ShapeDtypeStruct((count, *parts[0].shape[1:]), BF16),
    )(token, *parts)


def over_outer(total):
    for bit in range((lax.axis_size("outer") - 1).bit_length()):
        total = (total.astype(F32) + swapped(total, "outer", 1 << bit).astype(F32)).astype(BF16)
    return total


def passed_along(x, by):
    peers = lax.axis_size(AXES)
    pairs = [(i, i + by) for i in range(peers) if 0 <= i + by < peers]
    return lax.ppermute(x, AXES, pairs)


def in_hbm(x):
    return pltpu.with_memory_space_constraint(x, pltpu.HBM)


def body(
    signal,
    features,
    position,
    valid,
    w_past,
    w_now,
    b_conv,
    w_cond,
    w_res,
    b_res,
    w_skip,
    b_skip,
    grad_out,
    grad_skip,
):
    rows, width = signal.shape
    features = features.T
    cond = features.shape[0]
    hidden = w_res.shape[0]
    skip_width = w_skip.shape[1]
    far = lax.axis_size("far")
    far_bits = (far - 1).bit_length()
    used = 2 * width + cond + ONES + 2 * (hidden // HALVES) + ONES
    block = -(-used // (2 * far * 16)) * 16
    lines = (rows // DILATION_STEP, DILATION_STEP // LANES, LANES)
    pos, val = position.reshape(lines), valid.reshape(lines)
    b_conv, b_res, b_skip = (b.reshape(1, -1) for b in (b_conv, b_res, b_skip))

    def core_sum(half, token, theirs, mine):
        kept, *sent = added(
            f"core_sum_{half}", token, mine, [swapped(theirs, "core", 1)], [(1, F32)] + [(1, BF16)] * (NEAR - 1)
        )
        return kept[0], exchanged([x[0] for x in sent])

    def near_sum(half, token, kept, got):
        kept, sent = added(f"near_sum_{half}", token, kept, got, [(far // 2, F32), (far // 2, BF16)])
        return kept, swapped(sent, "far", 1)

    def far_sum(half, token, kept, got):
        for bit in range(1, far_bits - 1):
            size = kept.shape[0] // 2
            kept, sent = added(f"far_sum_{half}_{bit}", token, kept, [got], [(size, F32), (size, BF16)])
            got = swapped(sent, "far", 1 << bit)
        (mine,) = added(f"far_sum_{half}", token, kept, [got], [(kept.shape[0], BF16)])
        return mine, swapped(mine, "far", 1 << (far_bits - 1))

    def far_end(half, token, mine, got):
        total = over_outer(mirrored(f"far_end_{half}", token, mine, got))
        return total, swapped(total, "far", 1 << (far_bits - 2))

    def far_join(half, token, mine, got):
        total = joined(f"far_join_{half}", token, [mine, got])
        for bit in reversed(range(far_bits - 2)):
            total = joined(f"far_join_{half}_{bit}", token, [total, swapped(total, "far", 1 << bit)])
        return total, exchanged([total] * (NEAR - 1))

    def near_join(half, token, mine, got):
        total = joined(f"near_join_{half}", token, [mine[None]] + [x[None] for x in got])
        return total, swapped(total, "core", 1)

    def input_gradients(steps, token, before):
        last = (steps[-1] + 1) * ROWS == rows
        return inputs(steps, token, received if last else head_0[0], grad_out, pos, dpre_0, dpre_1, w_in, w_cond, before)

    halo = passed_along(signal[rows - DILATION_STEP :], 1)
    val, pos, b_conv, b_res, b_skip, w_cond, w_res, w_skip, w_in, past, signal, x_turned, grad_out, grad_skip, *rest_0 = load(
        val, pos, b_conv, b_res, b_skip, features, w_cond, w_res, w_skip, w_past, w_now, signal, grad_out, grad_skip
    )
    common = (signal, x_turned, grad_out, grad_skip, w_in, w_cond, b_conv, w_res, w_skip)
    past_head, head_0, head_1 = head(halo, pos, val, *common)
    theirs_0, mine_0 = gradients(0, past_head, far, block, val, x_turned, grad_out, grad_skip, past_head, head_0, rest_0)
    rest_1 = forward_rest(theirs_0, val, past, *common)
    dpre_0, dpre_1 = (head_0[2], rest_0[2]), (head_1[2], rest_1[2])
    kept_0, got_0 = core_sum(0, rest_1[0], theirs_0, mine_0)
    theirs_1, mine_1 = gradients(1, kept_0, far, block, val, x_turned, grad_out, grad_skip, past_head, head_1, rest_1)
    output, skip_out, mark = outputs(
        theirs_1, val, signal, (head_0[0], rest_0[0]), (head_1[0], rest_1[0]), w_res, w_skip, b_res, b_skip
    )
    kept_0, got_0 = near_sum(0, mark, kept_0, got_0)
    kept_1, got_1 = core_sum(1, kept_0, theirs_1, mine_1)
    ends_0, got_0 = far_sum(0, kept_1, kept_0, got_0)
    *grads, mark = input_gradients((0, 1), ends_0, [])
    ends_0, got_0 = far_end(0, mark, ends_0, got_0)
    kept_1, got_1 = near_sum(1, ends_0, kept_1, got_1)
    ends_0, got_0 = far_join(0, kept_1, ends_0, got_0)
    ends_1, got_1 = far_sum(1, ends_0, kept_1, got_1)
    *grads, mark = input_gradients((2,), ends_1, grads)
    ends_1, got_1 = far_end(1, mark, ends_1, got_1)
    early = early_rows(ends_1, pos, head_0[2], head_1[2], w_in)
    received = passed_along(early, -1)
    blocks_0, others_0 = near_join(0, early, ends_0, got_0)
    ends_1, got_1 = far_join(1, blocks_0, ends_1, got_1)
    *grads, mark = input_gradients((3,), ends_1, grads)
    blocks_1, others_1 = near_join(1, mark, ends_1, got_1)
    *done, own_0, mark = unpack(0, blocks_1, far, block, blocks_0, others_0, width, cond, hidden, skip_width, [])
    *done, own_1, _ = unpack(1, mark, far, block, blocks_1, others_1, width, cond, hidden, skip_width, done)
    g_past, g_now, g_cond, g_bias, g_res, g_skip = done
    grad_signal, grad_features = grads
    return (
        output,
        skip_out,
        grad_signal,
        grad_features.T,
        g_past,
        g_now,
        g_bias.reshape(-1),
        g_cond,
        g_res,
        own_0.reshape(-1),
        g_skip,
        own_1.reshape(-1),
    )


def solution(mesh):
    row, col = mesh.shape["row"], mesh.shape["col"]
    fine = Mesh(mesh.devices.reshape(row // 2, 2, col // NEAR, NEAR), AXES)
    rows = P(AXES, None)
    line = P(AXES)
    return jax.shard_map(
        body,
        mesh=fine,
        in_specs=(rows, rows, line, line) + (P(),) * 8 + (rows, rows),
        out_specs=(rows,) * 4 + (P(),) * 8,
        check_vma=False,
    )
```

```python
import functools

import jax
import jax.numpy as jnp
from jax import lax
from jax.experimental import pallas as pl
from jax.experimental.pallas import tpu as pltpu
from jax.sharding import Mesh
from jax.sharding import PartitionSpec as P

DILATION_STEP = 256
AXES = ("outer", "core", "far", "near")
HALVES = 2
NEAR = 4
LANES = 128
ROWS = 512
ONES = 16
F32 = jnp.float32
BF16 = jnp.bfloat16
MEGA = 1 << 20
COSTS = {
    "load": 8, "head": 2, "gradients_0": 0, "forward_1": 0, "gradients_1": 4, "outputs": 4, "near_sum_0": 8,
    "far_sum_0": 8, "near_sum_1": 4, "near_join_0": 2, "near_join_1": 4, "far_join_0": 4,
}
FLOPS = 10**9


def dot(left, right):
    return jnp.dot(left, right, preferred_element_type=F32)


def across(left, right):
    return lax.dot_general(left, right, (((0,), (0,)), ((), ())), preferred_element_type=F32)


def against(left, weight):
    return lax.dot_general(left, weight, (((1,), (1,)), ((), ())), preferred_element_type=F32)


def column(lines):
    turned = lines.astype(F32).T
    return jnp.concatenate([turned[:, k : k + 1] for k in range(lines.shape[0])], axis=0)


def row(lines):
    return jnp.concatenate([lines[k : k + 1] for k in range(lines.shape[0])], axis=1)


def tap_of(lines):
    return jnp.where(lines >= DILATION_STEP, 1, 0)


def lines_of(ref, rows):
    return ref[rows.start // LANES : rows.stop // LANES, :]


def picked(head, rest, rows):
    cut = DILATION_STEP
    low = head[rows.start : min(rows.stop, cut), :] if rows.start < cut else None
    high = rest[max(rows.start, cut) - cut : rows.stop - cut, :] if rows.stop > cut else None
    if low is None:
        return high
    return low if high is None else jnp.concatenate([low, high], axis=0)


def call(kernel, name, in_specs, out_specs, out_shape, scratch=(), aliases=None, grid=(), vmem=24):
    return pl.pallas_call(
        kernel,
        grid=grid,
        in_specs=in_specs,
        out_specs=out_specs,
        out_shape=out_shape,
        scratch_shapes=list(scratch),
        input_output_aliases=aliases or {},
        cost_estimate=pl.CostEstimate(
            flops=1 + int(FLOPS * COSTS.get(name, COSTS.get(name.split("_")[0], 0))), bytes_accessed=1, transcendentals=0
        ),
        name=name,
        compiler_params=pltpu.CompilerParams(vmem_limit_bytes=vmem * MEGA),
    )


VMEM = pl.BlockSpec(memory_space=pltpu.VMEM)
ANYWHERE = pl.BlockSpec(memory_space=pl.ANY)
MARK = jax.ShapeDtypeStruct((8, LANES), F32)


def beside(*parts):
    return jnp.concatenate(parts, axis=1)


def below(*parts):
    return jnp.concatenate(parts, axis=0)


def gate_product(half, k, rows, past, sig, feats, w_in, w_cond, b_conv):
    width = sig.shape[1]
    part = w_in.shape[1] // 2 // HALVES
    at = (k * HALVES + half) * part
    here = slice(at, at + part)
    own = dot(past, w_in[:width, here]) + dot(sig[rows, :], w_in[width:, here])
    return own + across(feats, w_cond[:, here]) + b_conv[:, here]


def back_product(half, rows, gout, gskip, w_res, w_skip):
    part = w_res.shape[0] // HALVES
    here = slice(half * part, (half + 1) * part)
    return against(gout[rows, :], w_res[here, :]) + against(gskip[rows, :], w_skip[here, :])


def finish(pre_a, pre_s, dgated, valid_lines):
    act = jnp.tanh(pre_a)
    yield None
    gate = 0.5 + 0.5 * jnp.tanh(0.5 * pre_s)
    gated = (act * gate).astype(BF16)
    yield gated, gated.T * row(valid_lines.astype(BF16))
    slope = (column(valid_lines) * dgated) * gate
    yield beside(slope * (1.0 - act * act), slope * act * (1.0 - gate)).astype(BF16)


def forward_tiles(half, tiles, prepare, arrive, valid, past, sig, x_turned, gout, gskip, weights, gated_out, kept_out, dpre_out):
    w_in, w_cond, b_conv, w_res, w_skip = weights
    cond = w_cond.shape[0]
    width = sig.shape[1]

    def product(rows, k):
        if arrive:
            arrive(rows, k)
        if k == 2:
            return back_product(half, rows, gout, gskip, w_res, w_skip)
        feats = x_turned[2 * width : 2 * width + cond, rows]
        return gate_product(half, k, rows, past[rows, :], sig, feats, w_in, w_cond, b_conv)

    def store(rows, k, made):
        there = slice(rows.start - DILATION_STEP, rows.stop - DILATION_STEP)
        if k == 1:
            gated_out[there, :], kept_out[:, there] = made
        elif k == 2:
            dpre_out[there, :] = made

    ahead = None
    for rows in [*tiles, None]:
        if rows and prepare:
            prepare(rows)
        made = []
        for k in range(3):
            if rows:
                made.append(product(rows, k))
            if ahead:
                store(ahead[0], k, next(ahead[1]))
        ahead = (rows, finish(*made, lines_of(valid, rows))) if rows else None


def rest_rows(rows, tile=ROWS):
    cuts = sorted({DILATION_STEP, *range(tile, rows + 1, tile)})
    return [slice(a, b) for a, b in zip(cuts, cuts[1:])]


def load_body(
    valid, pos, b_conv, b_res, b_skip, feat, w_cond, w_res, w_skip, w_past, w_now, sig, gout, gskip,
    valid_to, pos_to, b_conv_to, b_res_to, b_skip_to, w_cond_to, w_res_to, w_skip_to, w_in, past, sig_to, x_turned,
    gout_to, gskip_to, gated_rest, kept_rest, dpre_rest, sems,
):
    rows_all, width = sig.shape
    cond = feat.shape[0]
    count = 0

    def start(source, target):
        nonlocal count
        copy = pltpu.make_async_copy(source, target, sems.at[count])
        copy.start()
        count += 1
        return copy

    def tile(i, source, target):
        rows = pl.ds(i * ROWS, ROWS)
        return start(source.at[rows], target.at[rows])

    signals = [[tile(0, sig, sig_to)]]
    needs = [
        [
            start(pos, pos_to),
            start(w_past, w_in.at[pl.ds(0, width)]),
            start(w_now, w_in.at[pl.ds(width, width)]),
            start(feat, x_turned.at[pl.ds(2 * width, cond)]),
            start(w_cond, w_cond_to),
            start(b_conv, b_conv_to),
        ],
        [],
        [start(valid, valid_to), start(w_res, w_res_to), start(w_skip, w_skip_to)],
    ]
    cotangents = [[tile(0, gout, gout_to), tile(0, gskip, gskip_to)]]
    for i in range(1, rows_all // ROWS):
        signals.append([tile(i, sig, sig_to)])
        cotangents.append([tile(i, gout, gout_to), tile(i, gskip, gskip_to)])
    last = [start(b_res, b_res_to), start(b_skip, b_skip_to)]

    def wait(copies):
        for copy in copies:
            copy.wait()
        copies.clear()

    def prepare(rows):
        i = rows.start // ROWS
        wait(signals[i])
        wait(needs[0])
        whole = rows if i else slice(0, rows.stop)
        before = slice(rows.start - DILATION_STEP, rows.stop - DILATION_STEP)
        tap = tap_of(lines_of(pos_to, rows)).astype(F32)
        past[rows, :] = sig_to[before, :] * column(tap).astype(BF16)
        x_turned[width : 2 * width, whole] = sig_to[whole, :].T
        x_turned[:width, rows] = x_turned[width : 2 * width, before] * row(tap).astype(BF16)

    def arrive(rows, k):
        wait(needs[k])
        if k == 2:
            wait(cotangents[rows.start // ROWS])

    x_turned[2 * width + cond :, :] = jnp.ones((x_turned.shape[0] - 2 * width - cond, rows_all), BF16)
    forward_tiles(
        0, rest_rows(rows_all, ROWS // 2), prepare, arrive, valid_to, past, sig_to, x_turned, gout_to, gskip_to,
        (w_in, w_cond_to, b_conv_to, w_res_to, w_skip_to), gated_rest, kept_rest, dpre_rest,
    )
    wait(last)


def rest_shapes(rest, part):
    return [jax.ShapeDtypeStruct(shape, BF16) for shape in ((rest, part), (part, rest), (rest, 2 * part))]


def load(*arrays):
    sources = [in_hbm(x) for x in arrays]
    feat, w_cond, w_res, w_skip, w_past, w_now, sig, gout, gskip = arrays[5:]
    rows, width = sig.shape
    hidden = w_res.shape[0]
    shapes = [jax.ShapeDtypeStruct(x.shape, x.dtype) for x in arrays[:5] + (w_cond, w_res, w_skip)] + [
        jax.ShapeDtypeStruct(shape, BF16)
        for shape in (
            (2 * width, 2 * hidden), sig.shape, sig.shape, (2 * width + feat.shape[0] + ONES, rows), gout.shape, gskip.shape,
        )
    ]
    shapes += rest_shapes(rows - DILATION_STEP, hidden // HALVES)
    return call(
        load_body,
        "load",
        [ANYWHERE] * len(sources),
        [VMEM] * len(shapes),
        shapes,
        scratch=[pltpu.SemaphoreType.DMA((11 + 3 * (rows // ROWS),))],
    )(*sources)


def side_by_side(dpre_0, dpre_1):
    part = dpre_0.shape[1] // 2
    return beside(dpre_0[:, :part], dpre_1[:, :part], dpre_0[:, part:], dpre_1[:, part:])


def head_body(halo, pos, valid, sig, x_turned, gout, gskip, w_in, w_cond, b_conv, w_res, w_skip, past_out, *outs):
    rows = slice(0, DILATION_STEP)
    width = halo.shape[1]
    cond = w_cond.shape[0]
    tap = tap_of(lines_of(pos, rows)).astype(F32)
    past_out[...] = halo[...].T * row(tap).astype(BF16)
    past = halo[...] * column(tap).astype(BF16)
    feats = x_turned[2 * width : 2 * width + cond, rows]
    made = [
        [gate_product(half, k, rows, past, sig, feats, w_in, w_cond, b_conv) for k in range(2)]
        + [back_product(half, rows, gout, gskip, w_res, w_skip)]
        for half in range(HALVES)
    ]
    for half in range(HALVES):
        _, pair, dpre = finish(*made[half], lines_of(valid, rows))
        for ref, value in zip(outs[3 * half :], (*pair, dpre)):
            ref[...] = value


def head(halo, *args):
    width = halo.shape[1]
    part = args[-1].shape[0] // HALVES
    past, *parts = call(
        head_body,
        "head",
        [VMEM] * (1 + len(args)),
        [VMEM] * (1 + 3 * HALVES),
        [jax.ShapeDtypeStruct((width, DILATION_STEP), BF16)] + rest_shapes(DILATION_STEP, part) * HALVES,
    )(halo, *args)
    return past, parts[:3], parts[3:]


def early_body(token, pos, dpre_0, dpre_1, w_in, early):
    tap = column(tap_of(lines_of(pos, slice(0, DILATION_STEP))))
    early[...] = (tap * against(side_by_side(dpre_0[...], dpre_1[...]), w_in[: early.shape[1], :])).astype(BF16)


def early_rows(token, pos, dpre_0, dpre_1, w_in):
    return call(
        early_body,
        "early",
        [ANYWHERE] + [VMEM] * 4,
        VMEM,
        jax.ShapeDtypeStruct((DILATION_STEP, w_in.shape[0] // 2), BF16),
    )(token, pos, dpre_0, dpre_1, w_in)


def forward_body(
    token, valid, past, sig, x_turned, gout, gskip, w_in, w_cond, b_conv, w_res, w_skip, gated_out, kept_out, dpre_out
):
    forward_tiles(
        1, rest_rows(sig.shape[0], ROWS // 2), None, None, valid, past, sig, x_turned, gout, gskip,
        (w_in, w_cond, b_conv, w_res, w_skip), gated_out, kept_out, dpre_out,
    )


def forward_rest(token, *args):
    return call(
        forward_body,
        "forward_1",
        [ANYWHERE] + [VMEM] * len(args),
        [VMEM] * 3,
        rest_shapes(args[0].shape[0] * LANES - DILATION_STEP, args[-1].shape[0] // HALVES),
    )(token, *args)


def own_place():
    return [lax.axis_index(name) for name in ("core", "far", "near")]


def turned(index, count):
    bits = (count - 1).bit_length()
    result = 0
    for bit in range(bits):
        result = result | (((index >> bit) & 1) << (bits - 1 - bit))
    return result


def place_blocks(far, block, acc, theirs, mine):
    core, z, xy = own_place()
    for r in range(far):
        for c in range(NEAR):
            here = pl.ds(c * LANES, LANES)
            for k, out in ((1 - core, theirs), (core, mine)):
                rows = pl.ds(pl.multiple_of((k * far + r) * block, 16), block)
                out[c ^ xy, turned(r ^ z, far)] = acc[rows, here].astype(out.dtype)


def gradients_body(
    far, block, half, token, valid, x_turned, gout, gskip, past_head, kept_head, kept_rest, dpre_head, dpre_rest,
    theirs, mine, acc,
):
    cut = DILATION_STEP
    width = past_head.shape[0]
    part = kept_head.shape[0]
    wide = dpre_rest.shape[1]
    mask = jnp.broadcast_to(row(valid[...].astype(F32)).astype(BF16), (ONES, valid.shape[0] * LANES))
    ends = x_turned.shape[0]
    rest = below(kept_rest[...], mask[:, cut:])
    first = below(kept_head[...], mask[:, :cut])
    at = ends
    for k, ref in enumerate((gout, gskip)):
        outer = dot(rest, ref[cut:, :]) + dot(first, ref[:cut, :])
        acc[at : at + part, :] = outer[:part]
        at += part
        if k == half:
            acc[ends + 2 * part : ends + 2 * part + ONES, :] = outer[part:]
    at += ONES
    acc[at:, :] = jnp.zeros((acc.shape[0] - at, wide), F32)
    inner = dot(x_turned[:, cut:], dpre_rest[...])
    inner += dot(below(past_head[...], x_turned[width:, :cut]), dpre_head[...])
    acc[:ends, :] = inner
    place_blocks(far, block, acc, theirs, mine)


def gradients(half, token, far, block, valid, x_turned, gout, gskip, past_head, head_parts, rest_parts):
    packed = (NEAR, far, block, LANES)
    wide = rest_parts[2].shape[1]
    return call(
        functools.partial(gradients_body, far, block, half),
        f"gradients_{half}",
        [ANYWHERE] + [VMEM] * 9,
        [VMEM] * 2,
        [jax.ShapeDtypeStruct(packed, BF16), jax.ShapeDtypeStruct(packed, F32)],
        scratch=[pltpu.VMEM((2 * far * block, wide), F32)],
    )(token, valid, x_turned, gout, gskip, past_head, head_parts[1], rest_parts[1], head_parts[2], rest_parts[2])


def outputs_body(
    token, valid, sig, head_0, rest_0, head_1, rest_1, w_res, w_skip, b_res, b_skip, out, skip, mark, rooms, sems
):
    copies = []
    for i in range(sig.shape[0] // ROWS):
        rows = slice(i * ROWS, (i + 1) * ROWS)
        mask = column(lines_of(valid, rows))
        gated = beside(picked(head_0, rest_0, rows), picked(head_1, rest_1, rows))
        branch = dot(gated, w_res[...]) + b_res[...]
        rooms[i, 0] = (sig[rows, :].astype(F32) + mask * branch).astype(BF16)
        side = dot(gated, w_skip[...]) + b_skip[...]
        rooms[i, 1] = (mask * side).astype(BF16)
        for k, ref in enumerate((out, skip)):
            copies.append(pltpu.make_async_copy(rooms.at[i, k], ref.at[pl.ds(i * ROWS, ROWS)], sems.at[i, k]))
            copies[-1].start()
    mark[...] = jnp.zeros_like(mark)
    for copy in copies:
        copy.wait()


def outputs(token, valid, sig, gated_0, gated_1, w_res, w_skip, b_res, b_skip):
    rows, width = sig.shape
    return call(
        outputs_body,
        "outputs",
        [ANYWHERE] + [VMEM] * 10,
        [ANYWHERE, ANYWHERE, VMEM],
        [
            jax.ShapeDtypeStruct((rows, width), BF16),
            jax.ShapeDtypeStruct((rows, w_skip.shape[1]), BF16),
            MARK,
        ],
        scratch=[
            pltpu.VMEM((rows // ROWS, 2, ROWS, width), BF16),
            pltpu.SemaphoreType.DMA((rows // ROWS, 2)),
        ],
    )(token, valid, sig, *gated_0, *gated_1, w_res, w_skip, b_res, b_skip)


def inputs_body(steps, token, received, gout, pos, head_0, rest_0, head_1, rest_1, w_in, w_cond, *refs):
    gsig, gfeat, mark, room, room_feat, sems = refs[-6:]
    rows, width = gout.shape
    copies = []
    wide = 2 * LANES

    def copy(source, target):
        copies.append(pltpu.make_async_copy(source, target, sems.at[len(copies)]))
        copies[-1].start()

    for i, step in enumerate(steps):
        begin = step * ROWS
        here = slice(begin, begin + ROWS)
        after = slice(begin + DILATION_STEP, min(begin + DILATION_STEP + ROWS, rows))
        now = side_by_side(picked(head_0, rest_0, here), picked(head_1, rest_1, here))
        later = side_by_side(picked(head_0, rest_0, after), picked(head_1, rest_1, after))
        tap = column(tap_of(lines_of(pos, after)))
        room_feat[i] = against(w_cond[...], now)
        copy(room_feat.at[i], gfeat.at[:, pl.ds(begin, ROWS)])
        for k in range(width // wide):
            some = slice(k * wide, (k + 1) * wide)
            tail = tap * against(later, w_in[some, :])
            if tail.shape[0] < ROWS:
                tail = below(tail, received[:, some].astype(F32))
            room[i, k] = gout[here, some].astype(F32) + against(now, w_in[width + k * wide : width + (k + 1) * wide, :]) + tail
            copy(room.at[i, k], gsig.at[pl.ds(begin, ROWS), pl.ds(k * wide, wide)])
    mark[...] = jnp.zeros_like(mark)
    for one in copies:
        one.wait()


def inputs(steps, token, received, gout, pos, dpre_0, dpre_1, w_in, w_cond, before):
    rows, width = gout.shape
    cond = w_cond.shape[0]
    count = width // (2 * LANES)
    return call(
        functools.partial(inputs_body, steps),
        f"inputs_{steps[0]}",
        [ANYWHERE] + [VMEM] * 9 + [ANYWHERE] * len(before),
        [ANYWHERE, ANYWHERE, VMEM],
        [
            jax.ShapeDtypeStruct((rows, width), F32),
            jax.ShapeDtypeStruct((cond, rows), F32),
            MARK,
        ],
        scratch=[
            pltpu.VMEM((len(steps), count, ROWS, 2 * LANES), F32),
            pltpu.VMEM((len(steps), cond, ROWS), F32),
            pltpu.SemaphoreType.DMA((len(steps) * (count + 1),)),
        ],
        aliases={10 + k: k for k in range(len(before))},
    )(token, received, gout, pos, *dpre_0, *dpre_1, w_in, w_cond, *before)


def unpack_body(far, block, token, mine, theirs, *refs):
    arrays, (mark, room) = refs[-9:-2], refs[-2:]
    mark[...] = jnp.zeros_like(mark)
    core, z, xy = own_place()

    @pl.when(pl.program_id(0) == 0)
    def _():
        for k, ref in ((core, mine), (1 - core, theirs)):
            for c in range(NEAR):
                for r in range(far):
                    rows = pl.ds(pl.multiple_of((k * far + (r ^ z)) * block, 16), block)
                    room[c ^ xy, rows, :] = ref[c, turned(r, far)]

    for j in range(NEAR // 2):
        c = pl.program_id(0) * (NEAR // 2) + j
        here = pl.ds(j * LANES, LANES)
        top = 0
        for ref in arrays:
            count = ref.shape[0]
            size = max(count, ONES)
            ref[:, here] = room[c, top : top + size, :].astype(F32)[:count]
            top += size


def unpack(half, token, far, block, mine, theirs, width, cond, hidden, skip_width, before):
    part = hidden // HALVES
    gates = 2 * hidden
    own = (width, skip_width)[half]

    def wide(size):
        return pl.BlockSpec((size, part), lambda s: (0, HALVES * s + half))

    def tall(size):
        return pl.BlockSpec((part, size // 2), lambda s: (half, s))

    specs = [wide(width), wide(width), wide(cond), wide(1), tall(width), tall(skip_width), pl.BlockSpec((1, own // 2), lambda s: (0, s))]
    shapes = [(width, gates), (width, gates), (cond, gates), (1, gates), (hidden, width), (hidden, skip_width), (1, own)]
    packed = (NEAR, far, block, LANES)
    blocks = pl.BlockSpec(packed, lambda s: (0,) * len(packed))
    return call(
        functools.partial(unpack_body, far, block),
        f"unpack_{half}",
        [ANYWHERE, blocks, blocks] + [ANYWHERE] * len(before),
        specs + [pl.BlockSpec(MARK.shape, lambda s: (0, 0))],
        [jax.ShapeDtypeStruct(shape, F32) for shape in shapes] + [MARK],
        scratch=[pltpu.VMEM((NEAR, 2 * far * block, LANES), BF16)],
        aliases={3 + k: k for k in range(len(before))},
        grid=(2,),
    )(token, mine, theirs, *before)


def swapped(x, axis, k):
    return lax.ppermute(x, axis, [(i, i ^ k) for i in range(lax.axis_size(axis))])


def exchanged(blocks):
    return [swapped(block, "near", k + 1) for k, block in enumerate(blocks)]


def add_body(sizes, token, *refs):
    count = len(sizes)
    kept, got, outs = refs[0], refs[1:-count], refs[-count:]
    at = 0
    for out, size in zip(outs, sizes):
        for k in range(size):
            total = kept[at + k].astype(F32)
            for ref in got:
                total = total + ref[at + k].astype(F32)
            out[k] = total.astype(out.dtype)
        at += size


def added(name, token, kept, got, outs):
    sizes = [size for size, _ in outs]
    result = call(
        functools.partial(add_body, sizes),
        name,
        [ANYWHERE] + [VMEM] * (1 + len(got)),
        [VMEM] * len(outs),
        [jax.ShapeDtypeStruct((size, *kept.shape[1:]), dtype) for size, dtype in outs],
    )(token, kept, *got)
    return result


def mirror_body(token, mine, got, out):
    count = mine.shape[0]
    for k in range(count):
        out[k] = (mine[k].astype(F32) + got[count - 1 - k].astype(F32)).astype(out.dtype)


def mirrored(name, token, mine, got):
    return call(
        mirror_body,
        name,
        [ANYWHERE, VMEM, VMEM],
        VMEM,
        jax.ShapeDtypeStruct(mine.shape, BF16),
    )(token, mine, got)


def join_body(token, *refs):
    out = refs[-1]
    at = 0
    for ref in refs[:-1]:
        out[at : at + ref.shape[0]] = ref[...]
        at += ref.shape[0]


def joined(name, token, parts):
    count = sum(part.shape[0] for part in parts)
    return call(
        join_body,
        name,
        [ANYWHERE] + [VMEM] * len(parts),
        VMEM,
        jax.ShapeDtypeStruct((count, *parts[0].shape[1:]), BF16),
    )(token, *parts)


def over_outer(total):
    for bit in range((lax.axis_size("outer") - 1).bit_length()):
        total = (total.astype(F32) + swapped(total, "outer", 1 << bit).astype(F32)).astype(BF16)
    return total


def passed_along(x, by):
    peers = lax.axis_size(AXES)
    pairs = [(i, i + by) for i in range(peers) if 0 <= i + by < peers]
    return lax.ppermute(x, AXES, pairs)


def in_hbm(x):
    return pltpu.with_memory_space_constraint(x, pltpu.HBM)


def body(
    signal,
    features,
    position,
    valid,
    w_past,
    w_now,
    b_conv,
    w_cond,
    w_res,
    b_res,
    w_skip,
    b_skip,
    grad_out,
    grad_skip,
):
    rows, width = signal.shape
    features = features.T
    cond = features.shape[0]
    hidden = w_res.shape[0]
    skip_width = w_skip.shape[1]
    far = lax.axis_size("far")
    far_bits = (far - 1).bit_length()
    used = 2 * width + cond + ONES + 2 * (hidden // HALVES) + ONES
    block = -(-used // (2 * far * 16)) * 16
    lines = (rows // LANES, LANES)
    pos, val = position.reshape(lines), valid.reshape(lines)
    b_conv, b_res, b_skip = (b.reshape(1, -1) for b in (b_conv, b_res, b_skip))

    def core_sum(half, token, theirs, mine):
        kept, *sent = added(
            f"core_sum_{half}", token, mine, [swapped(theirs, "core", 1)], [(1, F32)] + [(1, BF16)] * (NEAR - 1)
        )
        return kept[0], exchanged([x[0] for x in sent])

    def near_sum(half, token, kept, got):
        kept, sent = added(f"near_sum_{half}", token, kept, got, [(far // 2, F32), (far // 2, BF16)])
        return kept, swapped(sent, "far", 1)

    def far_sum(half, token, kept, got):
        for bit in range(1, far_bits - 1):
            size = kept.shape[0] // 2
            kept, sent = added(f"far_sum_{half}_{bit}", token, kept, [got], [(size, F32), (size, BF16)])
            got = swapped(sent, "far", 1 << bit)
        (mine,) = added(f"far_sum_{half}", token, kept, [got], [(kept.shape[0], BF16)])
        return mine, swapped(mine, "far", 1 << (far_bits - 1))

    def far_end(half, token, mine, got):
        total = over_outer(mirrored(f"far_end_{half}", token, mine, got))
        return total, swapped(total, "far", 1 << (far_bits - 2))

    def far_join(half, token, mine, got):
        total = joined(f"far_join_{half}", token, [mine, got])
        for bit in reversed(range(far_bits - 2)):
            total = joined(f"far_join_{half}_{bit}", token, [total, swapped(total, "far", 1 << bit)])
        return total, exchanged([total] * (NEAR - 1))

    def near_join(half, token, mine, got):
        total = joined(f"near_join_{half}", token, [mine[None]] + [x[None] for x in got])
        return total, swapped(total, "core", 1)

    def input_gradients(steps, token, before):
        last = (steps[-1] + 1) * ROWS == rows
        return inputs(steps, token, received if last else head_0[0], grad_out, pos, dpre_0, dpre_1, w_in, w_cond, before)

    halo = passed_along(signal[rows - DILATION_STEP :], 1)
    val, pos, b_conv, b_res, b_skip, w_cond, w_res, w_skip, w_in, past, signal, x_turned, grad_out, grad_skip, *rest_0 = load(
        val, pos, b_conv, b_res, b_skip, features, w_cond, w_res, w_skip, w_past, w_now, signal, grad_out, grad_skip
    )
    common = (signal, x_turned, grad_out, grad_skip, w_in, w_cond, b_conv, w_res, w_skip)
    past_head, head_0, head_1 = head(halo, pos, val, *common)
    theirs_0, mine_0 = gradients(0, past_head, far, block, val, x_turned, grad_out, grad_skip, past_head, head_0, rest_0)
    rest_1 = forward_rest(theirs_0, val, past, *common)
    dpre_0, dpre_1 = (head_0[2], rest_0[2]), (head_1[2], rest_1[2])
    kept_0, got_0 = core_sum(0, rest_1[0], theirs_0, mine_0)
    theirs_1, mine_1 = gradients(1, kept_0, far, block, val, x_turned, grad_out, grad_skip, past_head, head_1, rest_1)
    output, skip_out, mark = outputs(
        theirs_1, val, signal, (head_0[0], rest_0[0]), (head_1[0], rest_1[0]), w_res, w_skip, b_res, b_skip
    )
    kept_0, got_0 = near_sum(0, mark, kept_0, got_0)
    kept_1, got_1 = core_sum(1, kept_0, theirs_1, mine_1)
    ends_0, got_0 = far_sum(0, kept_1, kept_0, got_0)
    *grads, mark = input_gradients((0, 1), ends_0, [])
    ends_0, got_0 = far_end(0, mark, ends_0, got_0)
    kept_1, got_1 = near_sum(1, ends_0, kept_1, got_1)
    ends_0, got_0 = far_join(0, kept_1, ends_0, got_0)
    ends_1, got_1 = far_sum(1, ends_0, kept_1, got_1)
    *grads, mark = input_gradients((2,), ends_1, grads)
    ends_1, got_1 = far_end(1, mark, ends_1, got_1)
    early = early_rows(ends_1, pos, head_0[2], head_1[2], w_in)
    received = passed_along(early, -1)
    blocks_0, others_0 = near_join(0, early, ends_0, got_0)
    ends_1, got_1 = far_join(1, blocks_0, ends_1, got_1)
    *grads, mark = input_gradients((3,), ends_1, grads)
    blocks_1, others_1 = near_join(1, mark, ends_1, got_1)
    *done, own_0, mark = unpack(0, blocks_1, far, block, blocks_0, others_0, width, cond, hidden, skip_width, [])
    *done, own_1, _ = unpack(1, mark, far, block, blocks_1, others_1, width, cond, hidden, skip_width, done)
    g_past, g_now, g_cond, g_bias, g_res, g_skip = done
    grad_signal, grad_features = grads
    return (
        output,
        skip_out,
        grad_signal,
        grad_features.T,
        g_past,
        g_now,
        g_bias.reshape(-1),
        g_cond,
        g_res,
        own_0.reshape(-1),
        g_skip,
        own_1.reshape(-1),
    )


def solution(mesh):
    row, col = mesh.shape["row"], mesh.shape["col"]
    fine = Mesh(mesh.devices.reshape(row // 2, 2, col // NEAR, NEAR), AXES)
    rows = P(AXES, None)
    line = P(AXES)
    return jax.shard_map(
        body,
        mesh=fine,
        in_specs=(rows, rows, line, line) + (P(),) * 8 + (rows, rows),
        out_specs=(rows,) * 4 + (P(),) * 8,
        check_vma=False,
    )
```

```python
import functools

import jax
import jax.numpy as jnp
from jax import lax
from jax.experimental import pallas as pl
from jax.experimental.pallas import tpu as pltpu
from jax.sharding import Mesh
from jax.sharding import PartitionSpec as P

DILATION_STEP = 256
AXES = ("outer", "core", "far", "near")
HALVES = 2
NEAR = 4
LANES = 128
ROWS = 512
ONES = 16
F32 = jnp.float32
BF16 = jnp.bfloat16
MEGA = 1 << 20
COSTS = {
    "load": 8, "head": 2, "gradients_0": 0, "forward_1": 0, "gradients_1": 4, "outputs": 4, "near_sum_0": 8,
    "far_sum_0": 8, "near_sum_1": 4, "near_join_0": 2, "near_join_1": 4, "far_join_0": 4,
}
FLOPS = 10**9


def dot(left, right):
    return jnp.dot(left, right, preferred_element_type=F32)


def across(left, right):
    return lax.dot_general(left, right, (((0,), (0,)), ((), ())), preferred_element_type=F32)


def against(left, weight):
    return lax.dot_general(left, weight, (((1,), (1,)), ((), ())), preferred_element_type=F32)


def column(lines):
    turned = lines.astype(F32).T
    return jnp.concatenate([turned[:, k : k + 1] for k in range(lines.shape[0])], axis=0)


def row(lines):
    return jnp.concatenate([lines[k : k + 1] for k in range(lines.shape[0])], axis=1)


def tap_of(lines):
    return jnp.where(lines >= DILATION_STEP, 1, 0)


def lines_of(ref, rows):
    return ref[rows.start // LANES : rows.stop // LANES, :]


def picked(pieces, rows):
    found, at = [], 0
    for ref in pieces:
        low, high = max(rows.start, at), min(rows.stop, at + ref.shape[0])
        if low < high:
            found.append(ref[low - at : high - at, :])
        at += ref.shape[0]
    return found[0] if len(found) == 1 else jnp.concatenate(found, axis=0)


def call(kernel, name, in_specs, out_specs, out_shape, scratch=(), aliases=None, grid=(), vmem=24):
    return pl.pallas_call(
        kernel,
        grid=grid,
        in_specs=in_specs,
        out_specs=out_specs,
        out_shape=out_shape,
        scratch_shapes=list(scratch),
        input_output_aliases=aliases or {},
        cost_estimate=pl.CostEstimate(
            flops=1 + int(FLOPS * COSTS.get(name, COSTS.get(name.split("_")[0], 0))), bytes_accessed=1, transcendentals=0
        ),
        name=name,
        compiler_params=pltpu.CompilerParams(vmem_limit_bytes=vmem * MEGA),
    )


VMEM = pl.BlockSpec(memory_space=pltpu.VMEM)
ANYWHERE = pl.BlockSpec(memory_space=pl.ANY)
MARK = jax.ShapeDtypeStruct((8, LANES), F32)


def beside(*parts):
    return jnp.concatenate(parts, axis=1)


def below(*parts):
    return jnp.concatenate(parts, axis=0)


def gate_product(half, k, rows, past, sig, feats, w_in, w_cond, b_conv):
    width = sig.shape[1]
    part = w_in.shape[1] // 2 // HALVES
    at = (k * HALVES + half) * part
    here = slice(at, at + part)
    own = dot(past, w_in[:width, here]) + dot(sig[rows, :], w_in[width:, here])
    return own + across(feats, w_cond[:, here]) + b_conv[:, here]


def back_product(half, rows, gout, gskip, w_res, w_skip):
    part = w_res.shape[0] // HALVES
    here = slice(half * part, (half + 1) * part)
    return against(gout[rows, :], w_res[here, :]) + against(gskip[rows, :], w_skip[here, :])


def finish(pre_a, pre_s, dgated, valid_lines):
    act = jnp.tanh(pre_a)
    gate = 0.5 + 0.5 * jnp.tanh(0.5 * pre_s)
    slope = (column(valid_lines) * dgated) * gate
    dpre = beside(slope * (1.0 - act * act), slope * act * (1.0 - gate)).astype(BF16)
    gated = (act * gate).astype(BF16)
    return gated, gated.T * row(valid_lines.astype(BF16)), dpre


def forward_tiles(half, tiles, prepare, arrive, valid, past, sig, x_turned, gout, gskip, weights, outs, base):
    w_in, w_cond, b_conv, w_res, w_skip = weights
    gated_out, kept_out, dpre_out = outs
    cond = w_cond.shape[0]
    width = sig.shape[1]

    def product(rows, k):
        if arrive:
            arrive(rows, k)
        if k == 2:
            return back_product(half, rows, gout, gskip, w_res, w_skip)
        feats = x_turned[2 * width : 2 * width + cond, rows]
        return gate_product(half, k, rows, past[rows, :], sig, feats, w_in, w_cond, b_conv)

    def done(rows, made):
        there = slice(rows.start - base, rows.stop - base)
        gated_out[there, :], kept_out[:, there], dpre_out[there, :] = finish(*made, lines_of(valid, rows))

    ahead = None
    for rows in tiles:
        if prepare:
            prepare(rows)
        made = [product(rows, k) for k in range(3)]
        if ahead:
            done(*ahead)
        ahead = (rows, made)
    done(*ahead)


def tiles_of(start, stop):
    return [slice(a, a + DILATION_STEP) for a in range(start, stop, DILATION_STEP)]


def split_rows(rows):
    return rows - DILATION_STEP


def load_body(
    valid, pos, b_conv, b_res, b_skip, feat, w_cond, w_res, w_skip, w_past, w_now, sig, gout, gskip,
    valid_to, pos_to, b_conv_to, b_res_to, b_skip_to, w_cond_to, w_res_to, w_skip_to, w_in, past, sig_to, x_turned,
    gout_to, gskip_to, gated_rest, kept_rest, dpre_rest, sems,
):
    rows_all, width = sig.shape
    cond = feat.shape[0]
    count = 0

    def start(source, target):
        nonlocal count
        copy = pltpu.make_async_copy(source, target, sems.at[count])
        copy.start()
        count += 1
        return copy

    def tile(i, source, target):
        rows = pl.ds(i * ROWS, ROWS)
        return start(source.at[rows], target.at[rows])

    signals = [[tile(0, sig, sig_to)]]
    needs = [
        [
            start(pos, pos_to),
            start(w_past, w_in.at[pl.ds(0, width)]),
            start(w_now, w_in.at[pl.ds(width, width)]),
            start(feat, x_turned.at[pl.ds(2 * width, cond)]),
            start(w_cond, w_cond_to),
            start(b_conv, b_conv_to),
        ],
        [],
        [start(valid, valid_to), start(w_res, w_res_to), start(w_skip, w_skip_to)],
    ]
    cotangents = [[tile(0, gout, gout_to), tile(0, gskip, gskip_to)]]
    for i in range(1, rows_all // ROWS):
        signals.append([tile(i, sig, sig_to)])
        cotangents.append([tile(i, gout, gout_to), tile(i, gskip, gskip_to)])
    last = [start(b_res, b_res_to), start(b_skip, b_skip_to)]

    def wait(copies):
        for copy in copies:
            copy.wait()
        copies.clear()

    def prepare(rows):
        i = rows.start // ROWS
        wait(signals[i])
        wait(needs[0])
        whole = rows if i else slice(0, rows.stop)
        before = slice(rows.start - DILATION_STEP, rows.stop - DILATION_STEP)
        tap = tap_of(lines_of(pos_to, rows)).astype(F32)
        past[rows, :] = sig_to[before, :] * column(tap).astype(BF16)
        x_turned[width : 2 * width, whole] = sig_to[whole, :].T
        x_turned[:width, rows] = x_turned[width : 2 * width, before] * row(tap).astype(BF16)

    def arrive(rows, k):
        wait(needs[k])
        if k == 2:
            wait(cotangents[rows.start // ROWS])

    x_turned[2 * width + cond :, :] = jnp.ones((x_turned.shape[0] - 2 * width - cond, rows_all), BF16)
    forward_tiles(
        0, tiles_of(DILATION_STEP, rows_all), prepare, arrive, valid_to, past, sig_to, x_turned, gout_to, gskip_to,
        (w_in, w_cond_to, b_conv_to, w_res_to, w_skip_to), (gated_rest, kept_rest, dpre_rest), DILATION_STEP,
    )
    wait(last)


def rest_shapes(rest, part):
    return [jax.ShapeDtypeStruct(shape, BF16) for shape in ((rest, part), (part, rest), (rest, 2 * part))]


def load(*arrays):
    sources = [in_hbm(x) for x in arrays]
    feat, w_cond, w_res, w_skip, w_past, w_now, sig, gout, gskip = arrays[5:]
    rows, width = sig.shape
    hidden = w_res.shape[0]
    shapes = [jax.ShapeDtypeStruct(x.shape, x.dtype) for x in arrays[:5] + (w_cond, w_res, w_skip)] + [
        jax.ShapeDtypeStruct(shape, BF16)
        for shape in (
            (2 * width, 2 * hidden), sig.shape, sig.shape, (2 * width + feat.shape[0] + ONES, rows), gout.shape, gskip.shape,
        )
    ]
    shapes += rest_shapes(rows - DILATION_STEP, hidden // HALVES)
    return call(
        load_body,
        "load",
        [ANYWHERE] * len(sources),
        [VMEM] * len(shapes),
        shapes,
        scratch=[pltpu.SemaphoreType.DMA((11 + 3 * (rows // ROWS),))],
    )(*sources)


def side_by_side(dpre_0, dpre_1):
    part = dpre_0.shape[1] // 2
    return beside(dpre_0[:, :part], dpre_1[:, :part], dpre_0[:, part:], dpre_1[:, part:])


def head_rows(half, halo, pos, valid, sig, x_turned, gout, gskip, weights, outs):
    w_in, w_cond, b_conv, w_res, w_skip = weights
    rows = slice(0, DILATION_STEP)
    width = halo.shape[1]
    feats = x_turned[2 * width : 2 * width + w_cond.shape[0], rows]
    past = halo[...] * column(tap_of(lines_of(pos, rows)).astype(F32)).astype(BF16)
    made = [gate_product(half, k, rows, past, sig, feats, w_in, w_cond, b_conv) for k in range(2)]
    made.append(back_product(half, rows, gout, gskip, w_res, w_skip))
    for ref, value in zip(outs, finish(*made, lines_of(valid, rows))):
        ref[...] = value


def head_body(halo, pos, valid, sig, x_turned, gout, gskip, w_in, w_cond, b_conv, w_res, w_skip, past_out, *outs):
    tap = tap_of(lines_of(pos, slice(0, DILATION_STEP))).astype(F32)
    past_out[...] = halo[...].T * row(tap).astype(BF16)
    head_rows(0, halo, pos, valid, sig, x_turned, gout, gskip, (w_in, w_cond, b_conv, w_res, w_skip), outs)


def head(halo, *args):
    width = halo.shape[1]
    part = args[-1].shape[0] // HALVES
    past, *parts = call(
        head_body,
        "head",
        [VMEM] * (1 + len(args)),
        [VMEM] * 4,
        [jax.ShapeDtypeStruct((width, DILATION_STEP), BF16)] + rest_shapes(DILATION_STEP, part),
    )(halo, *args)
    return past, parts


def early_body(token, pos, dpre_0, dpre_1, w_in, early):
    tap = column(tap_of(lines_of(pos, slice(0, DILATION_STEP))))
    early[...] = (tap * against(side_by_side(dpre_0[...], dpre_1[...]), w_in[: early.shape[1], :])).astype(BF16)


def early_rows(token, pos, dpre_0, dpre_1, w_in):
    return call(
        early_body,
        "early",
        [ANYWHERE] + [VMEM] * 4,
        VMEM,
        jax.ShapeDtypeStruct((DILATION_STEP, w_in.shape[0] // 2), BF16),
    )(token, pos, dpre_0, dpre_1, w_in)


def most_body(token, valid, past, sig, x_turned, gout, gskip, w_in, w_cond, b_conv, w_res, w_skip, *outs):
    forward_tiles(
        1, tiles_of(DILATION_STEP, split_rows(sig.shape[0])), None, None, valid, past, sig, x_turned, gout, gskip,
        (w_in, w_cond, b_conv, w_res, w_skip), outs, DILATION_STEP,
    )


def forward_most(token, *args):
    part = args[-1].shape[0] // HALVES
    return call(
        most_body,
        "forward_1",
        [ANYWHERE] + [VMEM] * len(args),
        [VMEM] * 3,
        rest_shapes(split_rows(args[2].shape[0]) - DILATION_STEP, part),
    )(token, *args)


def ends_body(token, halo, pos, valid, past, sig, x_turned, gout, gskip, w_in, w_cond, b_conv, w_res, w_skip, *outs):
    weights = (w_in, w_cond, b_conv, w_res, w_skip)
    rows = sig.shape[0]
    head_rows(1, halo, pos, valid, sig, x_turned, gout, gskip, weights, outs[:3])
    forward_tiles(
        1, tiles_of(split_rows(rows), rows), None, None, valid, past, sig, x_turned, gout, gskip, weights, outs[3:],
        split_rows(rows),
    )


def forward_ends(token, *args):
    part = args[-1].shape[0] // HALVES
    rows = args[4].shape[0]
    parts = call(
        ends_body,
        "ends_1",
        [ANYWHERE] + [VMEM] * len(args),
        [VMEM] * 6,
        rest_shapes(DILATION_STEP, part) + rest_shapes(rows - split_rows(rows), part),
    )(token, *args)
    return parts[:3], parts[3:]


def own_place():
    return [lax.axis_index(name) for name in ("core", "far", "near")]


def turned(index, count):
    bits = (count - 1).bit_length()
    result = 0
    for bit in range(bits):
        result = result | (((index >> bit) & 1) << (bits - 1 - bit))
    return result


def place_blocks(far, block, acc, theirs, mine):
    core, z, xy = own_place()
    for r in range(far):
        for c in range(NEAR):
            here = pl.ds(c * LANES, LANES)
            for k, out in ((1 - core, theirs), (core, mine)):
                rows = pl.ds(pl.multiple_of((k * far + r) * block, 16), block)
                out[c ^ xy, turned(r ^ z, far)] = acc[rows, here].astype(out.dtype)


def gradients_body(far, block, half, count, token, valid, x_turned, gout, gskip, past_head, *refs):
    kepts, dpres, (theirs, mine, acc) = refs[:count], refs[count : 2 * count], refs[2 * count :]
    width = past_head.shape[0]
    part = kepts[0].shape[0]
    ends, rows = x_turned.shape
    mask = jnp.broadcast_to(row(lines_of(valid, slice(0, rows)).astype(F32)).astype(BF16), (ONES, rows))
    inner, outer, at = None, [None, None], 0
    for kept, dpre in zip(kepts, dpres):
        here = slice(at, at + dpre.shape[0])
        left = below(kept[...], mask[:, here])
        for k, ref in enumerate((gout, gskip)):
            made = dot(left, ref[here, :])
            outer[k] = made if at == 0 else outer[k] + made
        left = below(past_head[...], x_turned[width:, here]) if at == 0 else x_turned[:, here]
        made = dot(left, dpre[...])
        inner = made if at == 0 else inner + made
        at = here.stop
    acc[:ends, :] = inner
    at = ends
    for k in range(2):
        acc[at : at + part, :] = outer[k][:part]
        at += part
    acc[at : at + ONES, :] = outer[half][part:]
    at += ONES
    acc[at:, :] = jnp.zeros((acc.shape[0] - at, acc.shape[1]), F32)
    place_blocks(far, block, acc, theirs, mine)


def gradients(half, token, far, block, valid, x_turned, gout, gskip, past_head, pieces):
    packed = (NEAR, far, block, LANES)
    wide = pieces[0][2].shape[1]
    count = len(pieces)
    return call(
        functools.partial(gradients_body, far, block, half, count),
        f"gradients_{half}",
        [ANYWHERE] + [VMEM] * (5 + 2 * count),
        [VMEM] * 2,
        [jax.ShapeDtypeStruct(packed, BF16), jax.ShapeDtypeStruct(packed, F32)],
        scratch=[pltpu.VMEM((2 * far * block, wide), F32)],
    )(token, valid, x_turned, gout, gskip, past_head, *(p[1] for p in pieces), *(p[2] for p in pieces))


def outputs_body(counts, token, valid, sig, w_res, w_skip, b_res, b_skip, *refs):
    first, second = refs[: counts[0]], refs[counts[0] : sum(counts)]
    out, skip, mark, rooms, sems = refs[sum(counts) :]
    copies = []
    for i in range(sig.shape[0] // ROWS):
        rows = slice(i * ROWS, (i + 1) * ROWS)
        mask = column(lines_of(valid, rows))
        gated = beside(picked(first, rows), picked(second, rows))
        branch = dot(gated, w_res[...]) + b_res[...]
        rooms[i, 0] = (sig[rows, :].astype(F32) + mask * branch).astype(BF16)
        side = dot(gated, w_skip[...]) + b_skip[...]
        rooms[i, 1] = (mask * side).astype(BF16)
        for k, ref in enumerate((out, skip)):
            copies.append(pltpu.make_async_copy(rooms.at[i, k], ref.at[pl.ds(i * ROWS, ROWS)], sems.at[i, k]))
            copies[-1].start()
    mark[...] = jnp.zeros_like(mark)
    for copy in copies:
        copy.wait()


def outputs(token, valid, sig, gated_0, gated_1, w_res, w_skip, b_res, b_skip):
    rows, width = sig.shape
    counts = (len(gated_0), len(gated_1))
    return call(
        functools.partial(outputs_body, counts),
        "outputs",
        [ANYWHERE] + [VMEM] * (6 + sum(counts)),
        [ANYWHERE, ANYWHERE, VMEM],
        [
            jax.ShapeDtypeStruct((rows, width), BF16),
            jax.ShapeDtypeStruct((rows, w_skip.shape[1]), BF16),
            MARK,
        ],
        scratch=[
            pltpu.VMEM((rows // ROWS, 2, ROWS, width), BF16),
            pltpu.SemaphoreType.DMA((rows // ROWS, 2)),
        ],
    )(token, valid, sig, w_res, w_skip, b_res, b_skip, *gated_0, *gated_1)


def inputs_body(steps, counts, token, received, gout, pos, w_in, w_cond, *refs):
    first, second = refs[: counts[0]], refs[counts[0] : sum(counts)]
    gsig, gfeat, mark, room, room_feat, sems = refs[-6:]
    rows, width = gout.shape
    copies = []
    wide = 2 * LANES

    def copy(source, target):
        copies.append(pltpu.make_async_copy(source, target, sems.at[len(copies)]))
        copies[-1].start()

    for i, step in enumerate(steps):
        begin = step * ROWS
        here = slice(begin, begin + ROWS)
        after = slice(begin + DILATION_STEP, min(begin + DILATION_STEP + ROWS, rows))
        now = side_by_side(picked(first, here), picked(second, here))
        later = side_by_side(picked(first, after), picked(second, after))
        tap = column(tap_of(lines_of(pos, after)))
        room_feat[i] = against(w_cond[...], now)
        copy(room_feat.at[i], gfeat.at[:, pl.ds(begin, ROWS)])
        for k in range(width // wide):
            some = slice(k * wide, (k + 1) * wide)
            tail = tap * against(later, w_in[some, :])
            if tail.shape[0] < ROWS:
                tail = below(tail, received[:, some].astype(F32))
            room[i, k] = gout[here, some].astype(F32) + against(now, w_in[width + k * wide : width + (k + 1) * wide, :]) + tail
            copy(room.at[i, k], gsig.at[pl.ds(begin, ROWS), pl.ds(k * wide, wide)])
    mark[...] = jnp.zeros_like(mark)
    for one in copies:
        one.wait()


def inputs(steps, token, received, gout, pos, dpre_0, dpre_1, w_in, w_cond, before):
    rows, width = gout.shape
    cond = w_cond.shape[0]
    count = width // (2 * LANES)
    counts = (len(dpre_0), len(dpre_1))
    operands = 6 + sum(counts)
    return call(
        functools.partial(inputs_body, steps, counts),
        f"inputs_{steps[0]}",
        [ANYWHERE] + [VMEM] * (operands - 1) + [ANYWHERE] * len(before),
        [ANYWHERE, ANYWHERE, VMEM],
        [
            jax.ShapeDtypeStruct((rows, width), F32),
            jax.ShapeDtypeStruct((cond, rows), F32),
            MARK,
        ],
        scratch=[
            pltpu.VMEM((len(steps), count, ROWS, 2 * LANES), F32),
            pltpu.VMEM((len(steps), cond, ROWS), F32),
            pltpu.SemaphoreType.DMA((len(steps) * (count + 1),)),
        ],
        aliases={operands + k: k for k in range(len(before))},
    )(token, received, gout, pos, w_in, w_cond, *dpre_0, *dpre_1, *before)


def unpack_body(far, block, token, mine, theirs, *refs):
    arrays, (mark, room) = refs[-9:-2], refs[-2:]
    mark[...] = jnp.zeros_like(mark)
    core, z, xy = own_place()

    @pl.when(pl.program_id(0) == 0)
    def _():
        for k, ref in ((core, mine), (1 - core, theirs)):
            for c in range(NEAR):
                for r in range(far):
                    rows = pl.ds(pl.multiple_of((k * far + (r ^ z)) * block, 16), block)
                    room[c ^ xy, rows, :] = ref[c, turned(r, far)]

    for j in range(NEAR // 2):
        c = pl.program_id(0) * (NEAR // 2) + j
        here = pl.ds(j * LANES, LANES)
        top = 0
        for ref in arrays:
            count = ref.shape[0]
            size = max(count, ONES)
            ref[:, here] = room[c, top : top + size, :].astype(F32)[:count]
            top += size


def unpack(half, token, far, block, mine, theirs, width, cond, hidden, skip_width, before):
    part = hidden // HALVES
    gates = 2 * hidden
    own = (width, skip_width)[half]

    def wide(size):
        return pl.BlockSpec((size, part), lambda s: (0, HALVES * s + half))

    def tall(size):
        return pl.BlockSpec((part, size // 2), lambda s: (half, s))

    specs = [wide(width), wide(width), wide(cond), wide(1), tall(width), tall(skip_width), pl.BlockSpec((1, own // 2), lambda s: (0, s))]
    shapes = [(width, gates), (width, gates), (cond, gates), (1, gates), (hidden, width), (hidden, skip_width), (1, own)]
    packed = (NEAR, far, block, LANES)
    blocks = pl.BlockSpec(packed, lambda s: (0,) * len(packed))
    return call(
        functools.partial(unpack_body, far, block),
        f"unpack_{half}",
        [ANYWHERE, blocks, blocks] + [ANYWHERE] * len(before),
        specs + [pl.BlockSpec(MARK.shape, lambda s: (0, 0))],
        [jax.ShapeDtypeStruct(shape, F32) for shape in shapes] + [MARK],
        scratch=[pltpu.VMEM((NEAR, 2 * far * block, LANES), BF16)],
        aliases={3 + k: k for k in range(len(before))},
        grid=(2,),
    )(token, mine, theirs, *before)


def swapped(x, axis, k):
    return lax.ppermute(x, axis, [(i, i ^ k) for i in range(lax.axis_size(axis))])


def exchanged(blocks):
    return [swapped(block, "near", k + 1) for k, block in enumerate(blocks)]


def add_body(sizes, token, *refs):
    count = len(sizes)
    kept, got, outs = refs[0], refs[1:-count], refs[-count:]
    at = 0
    for out, size in zip(outs, sizes):
        for k in range(size):
            total = kept[at + k].astype(F32)
            for ref in got:
                total = total + ref[at + k].astype(F32)
            out[k] = total.astype(out.dtype)
        at += size


def added(name, token, kept, got, outs):
    sizes = [size for size, _ in outs]
    result = call(
        functools.partial(add_body, sizes),
        name,
        [ANYWHERE] + [VMEM] * (1 + len(got)),
        [VMEM] * len(outs),
        [jax.ShapeDtypeStruct((size, *kept.shape[1:]), dtype) for size, dtype in outs],
    )(token, kept, *got)
    return result


def mirror_body(token, mine, got, out):
    count = mine.shape[0]
    for k in range(count):
        out[k] = (mine[k].astype(F32) + got[count - 1 - k].astype(F32)).astype(out.dtype)


def mirrored(name, token, mine, got):
    return call(
        mirror_body,
        name,
        [ANYWHERE, VMEM, VMEM],
        VMEM,
        jax.ShapeDtypeStruct(mine.shape, BF16),
    )(token, mine, got)


def join_body(token, *refs):
    out = refs[-1]
    at = 0
    for ref in refs[:-1]:
        out[at : at + ref.shape[0]] = ref[...]
        at += ref.shape[0]


def joined(name, token, parts):
    count = sum(part.shape[0] for part in parts)
    return call(
        join_body,
        name,
        [ANYWHERE] + [VMEM] * len(parts),
        VMEM,
        jax.ShapeDtypeStruct((count, *parts[0].shape[1:]), BF16),
    )(token, *parts)


def over_outer(total):
    for bit in range((lax.axis_size("outer") - 1).bit_length()):
        total = (total.astype(F32) + swapped(total, "outer", 1 << bit).astype(F32)).astype(BF16)
    return total


def passed_along(x, by):
    peers = lax.axis_size(AXES)
    pairs = [(i, i + by) for i in range(peers) if 0 <= i + by < peers]
    return lax.ppermute(x, AXES, pairs)


def in_hbm(x):
    return pltpu.with_memory_space_constraint(x, pltpu.HBM)


def body(
    signal,
    features,
    position,
    valid,
    w_past,
    w_now,
    b_conv,
    w_cond,
    w_res,
    b_res,
    w_skip,
    b_skip,
    grad_out,
    grad_skip,
):
    rows, width = signal.shape
    features = features.T
    cond = features.shape[0]
    hidden = w_res.shape[0]
    skip_width = w_skip.shape[1]
    far = lax.axis_size("far")
    far_bits = (far - 1).bit_length()
    used = 2 * width + cond + ONES + 2 * (hidden // HALVES) + ONES
    block = -(-used // (2 * far * 16)) * 16
    lines = (rows // LANES, LANES)
    pos, val = position.reshape(lines), valid.reshape(lines)
    b_conv, b_res, b_skip = (b.reshape(1, -1) for b in (b_conv, b_res, b_skip))

    def core_sum(half, token, theirs, mine):
        kept, *sent = added(
            f"core_sum_{half}", token, mine, [swapped(theirs, "core", 1)], [(1, F32)] + [(1, BF16)] * (NEAR - 1)
        )
        return kept[0], exchanged([x[0] for x in sent])

    def near_sum(half, token, kept, got):
        kept, sent = added(f"near_sum_{half}", token, kept, got, [(far // 2, F32), (far // 2, BF16)])
        return kept, swapped(sent, "far", 1)

    def far_sum(half, token, kept, got):
        for bit in range(1, far_bits - 1):
            size = kept.shape[0] // 2
            kept, sent = added(f"far_sum_{half}_{bit}", token, kept, [got], [(size, F32), (size, BF16)])
            got = swapped(sent, "far", 1 << bit)
        (mine,) = added(f"far_sum_{half}", token, kept, [got], [(kept.shape[0], BF16)])
        return mine, swapped(mine, "far", 1 << (far_bits - 1))

    def far_end(half, token, mine, got):
        total = over_outer(mirrored(f"far_end_{half}", token, mine, got))
        return total, swapped(total, "far", 1 << (far_bits - 2))

    def far_join(half, token, mine, got):
        total = joined(f"far_join_{half}", token, [mine, got])
        for bit in reversed(range(far_bits - 2)):
            total = joined(f"far_join_{half}_{bit}", token, [total, swapped(total, "far", 1 << bit)])
        return total, exchanged([total] * (NEAR - 1))

    def near_join(half, token, mine, got):
        total = joined(f"near_join_{half}", token, [mine[None]] + [x[None] for x in got])
        return total, swapped(total, "core", 1)

    def input_gradients(steps, token, before):
        last = (steps[-1] + 1) * ROWS == rows
        return inputs(steps, token, received if last else head_0[0], grad_out, pos, dpre_0, dpre_1, w_in, w_cond, before)

    halo = passed_along(signal[rows - DILATION_STEP :], 1)
    val, pos, b_conv, b_res, b_skip, w_cond, w_res, w_skip, w_in, past, signal, x_turned, grad_out, grad_skip, *rest_0 = load(
        val, pos, b_conv, b_res, b_skip, features, w_cond, w_res, w_skip, w_past, w_now, signal, grad_out, grad_skip
    )
    common = (signal, x_turned, grad_out, grad_skip, w_in, w_cond, b_conv, w_res, w_skip)
    past_head, head_0 = head(halo, pos, val, *common)
    made_0 = (head_0, rest_0)
    theirs_0, mine_0 = gradients(0, past_head, far, block, val, x_turned, grad_out, grad_skip, past_head, made_0)
    most_1 = forward_most(theirs_0, val, past, *common)
    kept_0, got_0 = core_sum(0, most_1[0], theirs_0, mine_0)
    head_1, last_1 = forward_ends(kept_0, halo, pos, val, past, *common)
    made_1 = (head_1, most_1, last_1)
    dpre_0, dpre_1 = ([p[2] for p in made] for made in (made_0, made_1))
    theirs_1, mine_1 = gradients(1, kept_0, far, block, val, x_turned, grad_out, grad_skip, past_head, made_1)
    output, skip_out, mark = outputs(
        theirs_1, val, signal, [p[0] for p in made_0], [p[0] for p in made_1], w_res, w_skip, b_res, b_skip
    )
    kept_0, got_0 = near_sum(0, mark, kept_0, got_0)
    kept_1, got_1 = core_sum(1, kept_0, theirs_1, mine_1)
    ends_0, got_0 = far_sum(0, kept_1, kept_0, got_0)
    *grads, mark = input_gradients((0, 1), ends_0, [])
    ends_0, got_0 = far_end(0, mark, ends_0, got_0)
    kept_1, got_1 = near_sum(1, ends_0, kept_1, got_1)
    ends_0, got_0 = far_join(0, kept_1, ends_0, got_0)
    ends_1, got_1 = far_sum(1, ends_0, kept_1, got_1)
    *grads, mark = input_gradients((2,), ends_1, grads)
    ends_1, got_1 = far_end(1, mark, ends_1, got_1)
    early = early_rows(ends_1, pos, head_0[2], head_1[2], w_in)
    received = passed_along(early, -1)
    blocks_0, others_0 = near_join(0, early, ends_0, got_0)
    ends_1, got_1 = far_join(1, blocks_0, ends_1, got_1)
    *grads, mark = input_gradients((3,), ends_1, grads)
    blocks_1, others_1 = near_join(1, mark, ends_1, got_1)
    *done, own_0, mark = unpack(0, blocks_1, far, block, blocks_0, others_0, width, cond, hidden, skip_width, [])
    *done, own_1, _ = unpack(1, mark, far, block, blocks_1, others_1, width, cond, hidden, skip_width, done)
    g_past, g_now, g_cond, g_bias, g_res, g_skip = done
    grad_signal, grad_features = grads
    return (
        output,
        skip_out,
        grad_signal,
        grad_features.T,
        g_past,
        g_now,
        g_bias.reshape(-1),
        g_cond,
        g_res,
        own_0.reshape(-1),
        g_skip,
        own_1.reshape(-1),
    )


def solution(mesh):
    row, col = mesh.shape["row"], mesh.shape["col"]
    fine = Mesh(mesh.devices.reshape(row // 2, 2, col // NEAR, NEAR), AXES)
    rows = P(AXES, None)
    line = P(AXES)
    return jax.shard_map(
        body,
        mesh=fine,
        in_specs=(rows, rows, line, line) + (P(),) * 8 + (rows, rows),
        out_specs=(rows,) * 4 + (P(),) * 8,
        check_vma=False,
    )
```

```python
import functools

import jax
import jax.numpy as jnp
from jax import lax
from jax.experimental import pallas as pl
from jax.experimental.pallas import tpu as pltpu
from jax.sharding import Mesh
from jax.sharding import PartitionSpec as P

DILATION_STEP = 256
AXES = ("outer", "core", "far", "near")
HALVES = 2
NEAR = 4
LANES = 128
ROWS = 512
ONES = 16
F32 = jnp.float32
BF16 = jnp.bfloat16
MEGA = 1 << 20
COSTS = {
    "load": 8, "head": 2, "gradients_0": 0, "forward_1": 0, "gradients_1": 4, "outputs": 4, "near_sum_0": 8,
    "far_sum_0": 8, "near_sum_1": 4, "near_join_0_1": 2, "near_join_1_1": 4, "far_join_0": 4,
}
FLOPS = 10**9


def dot(left, right):
    return jnp.dot(left, right, preferred_element_type=F32)


def across(left, right):
    return lax.dot_general(left, right, (((0,), (0,)), ((), ())), preferred_element_type=F32)


def against(left, weight):
    return lax.dot_general(left, weight, (((1,), (1,)), ((), ())), preferred_element_type=F32)


def column(lines):
    turned = lines.astype(F32).T
    return jnp.concatenate([turned[:, k : k + 1] for k in range(lines.shape[0])], axis=0)


def row(lines):
    return jnp.concatenate([lines[k : k + 1] for k in range(lines.shape[0])], axis=1)


def tap_of(lines):
    return jnp.where(lines >= DILATION_STEP, 1, 0)


def lines_of(ref, rows):
    return ref[rows.start // LANES : rows.stop // LANES, :]


def picked(pieces, rows):
    found, at = [], 0
    for ref in pieces:
        low, high = max(rows.start, at), min(rows.stop, at + ref.shape[0])
        if low < high:
            found.append(ref[low - at : high - at, :])
        at += ref.shape[0]
    return found[0] if len(found) == 1 else jnp.concatenate(found, axis=0)


def call(kernel, name, in_specs, out_specs, out_shape, scratch=(), aliases=None, grid=(), vmem=24):
    return pl.pallas_call(
        kernel,
        grid=grid,
        in_specs=in_specs,
        out_specs=out_specs,
        out_shape=out_shape,
        scratch_shapes=list(scratch),
        input_output_aliases=aliases or {},
        cost_estimate=pl.CostEstimate(
            flops=1 + int(FLOPS * COSTS.get(name, COSTS.get(name.split("_")[0], 0))), bytes_accessed=1, transcendentals=0
        ),
        name=name,
        compiler_params=pltpu.CompilerParams(vmem_limit_bytes=vmem * MEGA),
    )


VMEM = pl.BlockSpec(memory_space=pltpu.VMEM)
ANYWHERE = pl.BlockSpec(memory_space=pl.ANY)
MARK = jax.ShapeDtypeStruct((8, LANES), F32)


def beside(*parts):
    return jnp.concatenate(parts, axis=1)


def below(*parts):
    return jnp.concatenate(parts, axis=0)


def gate_product(half, k, rows, past, sig, feats, w_in, w_cond, b_conv):
    width = sig.shape[1]
    part = w_in.shape[1] // 2 // HALVES
    at = (k * HALVES + half) * part
    here = slice(at, at + part)
    own = dot(past, w_in[:width, here]) + dot(sig[rows, :], w_in[width:, here])
    return own + across(feats, w_cond[:, here]) + b_conv[:, here]


def back_product(half, rows, gout, gskip, w_res, w_skip):
    part = w_res.shape[0] // HALVES
    here = slice(half * part, (half + 1) * part)
    return against(gout[rows, :], w_res[here, :]) + against(gskip[rows, :], w_skip[here, :])


def finish(pre_a, pre_s, dgated, valid_lines):
    act = jnp.tanh(pre_a)
    gate = 0.5 + 0.5 * jnp.tanh(0.5 * pre_s)
    slope = (column(valid_lines) * dgated) * gate
    dpre = beside(slope * (1.0 - act * act), slope * act * (1.0 - gate)).astype(BF16)
    gated = (act * gate).astype(BF16)
    return gated, gated.T * row(valid_lines.astype(BF16)), dpre


def forward_tiles(half, tiles, prepare, arrive, valid, past, sig, x_turned, gout, gskip, weights, outs, base):
    w_in, w_cond, b_conv, w_res, w_skip = weights
    gated_out, kept_out, dpre_out = outs
    cond = w_cond.shape[0]
    width = sig.shape[1]

    def product(rows, k):
        if arrive:
            arrive(rows, k)
        if k == 2:
            return back_product(half, rows, gout, gskip, w_res, w_skip)
        feats = x_turned[2 * width : 2 * width + cond, rows]
        return gate_product(half, k, rows, past[rows, :], sig, feats, w_in, w_cond, b_conv)

    def done(rows, made):
        there = slice(rows.start - base, rows.stop - base)
        gated_out[there, :], kept_out[:, there], dpre_out[there, :] = finish(*made, lines_of(valid, rows))

    ahead = None
    for rows in tiles:
        if prepare:
            prepare(rows)
        made = [product(rows, k) for k in range(3)]
        if ahead:
            done(*ahead)
        ahead = (rows, made)
    done(*ahead)


def tiles_of(start, stop):
    return [slice(a, a + DILATION_STEP) for a in range(start, stop, DILATION_STEP)]


def split_rows(rows):
    return rows - DILATION_STEP


def load_body(
    valid, pos, b_conv, b_res, b_skip, feat, w_cond, w_res, w_skip, w_past, w_now, sig, gout, gskip,
    valid_to, pos_to, b_conv_to, b_res_to, b_skip_to, w_cond_to, w_res_to, w_skip_to, w_in, past, sig_to, x_turned,
    gout_to, gskip_to, gated_rest, kept_rest, dpre_rest, sems,
):
    rows_all, width = sig.shape
    cond = feat.shape[0]
    count = 0

    def start(source, target):
        nonlocal count
        copy = pltpu.make_async_copy(source, target, sems.at[count])
        copy.start()
        count += 1
        return copy

    def tile(i, source, target):
        rows = pl.ds(i * ROWS, ROWS)
        return start(source.at[rows], target.at[rows])

    signals = [[tile(0, sig, sig_to)]]
    needs = [
        [
            start(pos, pos_to),
            start(w_past, w_in.at[pl.ds(0, width)]),
            start(w_now, w_in.at[pl.ds(width, width)]),
            start(feat, x_turned.at[pl.ds(2 * width, cond)]),
            start(w_cond, w_cond_to),
            start(b_conv, b_conv_to),
        ],
        [],
        [start(valid, valid_to), start(w_res, w_res_to), start(w_skip, w_skip_to)],
    ]
    cotangents = [[tile(0, gout, gout_to), tile(0, gskip, gskip_to)]]
    for i in range(1, rows_all // ROWS):
        signals.append([tile(i, sig, sig_to)])
        cotangents.append([tile(i, gout, gout_to), tile(i, gskip, gskip_to)])
    last = [start(b_res, b_res_to), start(b_skip, b_skip_to)]

    def wait(copies):
        for copy in copies:
            copy.wait()
        copies.clear()

    def prepare(rows):
        i = rows.start // ROWS
        wait(signals[i])
        wait(needs[0])
        whole = rows if i else slice(0, rows.stop)
        before = slice(rows.start - DILATION_STEP, rows.stop - DILATION_STEP)
        tap = tap_of(lines_of(pos_to, rows)).astype(F32)
        past[rows, :] = sig_to[before, :] * column(tap).astype(BF16)
        x_turned[width : 2 * width, whole] = sig_to[whole, :].T
        x_turned[:width, rows] = x_turned[width : 2 * width, before] * row(tap).astype(BF16)

    def arrive(rows, k):
        wait(needs[k])
        if k == 2:
            wait(cotangents[rows.start // ROWS])

    x_turned[2 * width + cond :, :] = jnp.ones((x_turned.shape[0] - 2 * width - cond, rows_all), BF16)
    forward_tiles(
        0, tiles_of(DILATION_STEP, rows_all), prepare, arrive, valid_to, past, sig_to, x_turned, gout_to, gskip_to,
        (w_in, w_cond_to, b_conv_to, w_res_to, w_skip_to), (gated_rest, kept_rest, dpre_rest), DILATION_STEP,
    )
    wait(last)


def rest_shapes(rest, part):
    return [jax.ShapeDtypeStruct(shape, BF16) for shape in ((rest, part), (part, rest), (rest, 2 * part))]


def load(*arrays):
    sources = [in_hbm(x) for x in arrays]
    feat, w_cond, w_res, w_skip, w_past, w_now, sig, gout, gskip = arrays[5:]
    rows, width = sig.shape
    hidden = w_res.shape[0]
    shapes = [jax.ShapeDtypeStruct(x.shape, x.dtype) for x in arrays[:5] + (w_cond, w_res, w_skip)] + [
        jax.ShapeDtypeStruct(shape, BF16)
        for shape in (
            (2 * width, 2 * hidden), sig.shape, sig.shape, (2 * width + feat.shape[0] + ONES, rows), gout.shape, gskip.shape,
        )
    ]
    shapes += rest_shapes(rows - DILATION_STEP, hidden // HALVES)
    return call(
        load_body,
        "load",
        [ANYWHERE] * len(sources),
        [VMEM] * len(shapes),
        shapes,
        scratch=[pltpu.SemaphoreType.DMA((11 + 3 * (rows // ROWS),))],
    )(*sources)


def side_by_side(dpre_0, dpre_1):
    part = dpre_0.shape[1] // 2
    return beside(dpre_0[:, :part], dpre_1[:, :part], dpre_0[:, part:], dpre_1[:, part:])


def head_rows(half, halo, pos, valid, sig, x_turned, gout, gskip, weights, outs):
    w_in, w_cond, b_conv, w_res, w_skip = weights
    rows = slice(0, DILATION_STEP)
    width = halo.shape[1]
    feats = x_turned[2 * width : 2 * width + w_cond.shape[0], rows]
    past = halo[...] * column(tap_of(lines_of(pos, rows)).astype(F32)).astype(BF16)
    made = [gate_product(half, k, rows, past, sig, feats, w_in, w_cond, b_conv) for k in range(2)]
    made.append(back_product(half, rows, gout, gskip, w_res, w_skip))
    for ref, value in zip(outs, finish(*made, lines_of(valid, rows))):
        ref[...] = value


def head_body(halo, pos, valid, sig, x_turned, gout, gskip, w_in, w_cond, b_conv, w_res, w_skip, past_out, *outs):
    tap = tap_of(lines_of(pos, slice(0, DILATION_STEP))).astype(F32)
    past_out[...] = halo[...].T * row(tap).astype(BF16)
    head_rows(0, halo, pos, valid, sig, x_turned, gout, gskip, (w_in, w_cond, b_conv, w_res, w_skip), outs)


def head(halo, *args):
    width = halo.shape[1]
    part = args[-1].shape[0] // HALVES
    past, *parts = call(
        head_body,
        "head",
        [VMEM] * (1 + len(args)),
        [VMEM] * 4,
        [jax.ShapeDtypeStruct((width, DILATION_STEP), BF16)] + rest_shapes(DILATION_STEP, part),
    )(halo, *args)
    return past, parts


def early_body(token, pos, dpre_0, dpre_1, w_in, early):
    tap = column(tap_of(lines_of(pos, slice(0, DILATION_STEP))))
    early[...] = (tap * against(side_by_side(dpre_0[...], dpre_1[...]), w_in[: early.shape[1], :])).astype(BF16)


def early_rows(token, pos, dpre_0, dpre_1, w_in):
    return call(
        early_body,
        "early",
        [ANYWHERE] + [VMEM] * 4,
        VMEM,
        jax.ShapeDtypeStruct((DILATION_STEP, w_in.shape[0] // 2), BF16),
    )(token, pos, dpre_0, dpre_1, w_in)


def most_body(token, valid, past, sig, x_turned, gout, gskip, w_in, w_cond, b_conv, w_res, w_skip, *outs):
    forward_tiles(
        1, tiles_of(DILATION_STEP, split_rows(sig.shape[0])), None, None, valid, past, sig, x_turned, gout, gskip,
        (w_in, w_cond, b_conv, w_res, w_skip), outs, DILATION_STEP,
    )


def forward_most(token, *args):
    part = args[-1].shape[0] // HALVES
    return call(
        most_body,
        "forward_1",
        [ANYWHERE] + [VMEM] * len(args),
        [VMEM] * 3,
        rest_shapes(split_rows(args[2].shape[0]) - DILATION_STEP, part),
    )(token, *args)


def ends_body(token, halo, pos, valid, past, sig, x_turned, gout, gskip, w_in, w_cond, b_conv, w_res, w_skip, *outs):
    weights = (w_in, w_cond, b_conv, w_res, w_skip)
    rows = sig.shape[0]
    head_rows(1, halo, pos, valid, sig, x_turned, gout, gskip, weights, outs[:3])
    forward_tiles(
        1, tiles_of(split_rows(rows), rows), None, None, valid, past, sig, x_turned, gout, gskip, weights, outs[3:],
        split_rows(rows),
    )


def forward_ends(token, *args):
    part = args[-1].shape[0] // HALVES
    rows = args[4].shape[0]
    parts = call(
        ends_body,
        "ends_1",
        [ANYWHERE] + [VMEM] * len(args),
        [VMEM] * 6,
        rest_shapes(DILATION_STEP, part) + rest_shapes(rows - split_rows(rows), part),
    )(token, *args)
    return parts[:3], parts[3:]


def own_place():
    return [lax.axis_index(name) for name in ("core", "far", "near")]


def turned(index, count):
    bits = (count - 1).bit_length()
    result = 0
    for bit in range(bits):
        result = result | (((index >> bit) & 1) << (bits - 1 - bit))
    return result


def place_blocks(far, block, acc, theirs, mine):
    core, z, xy = own_place()
    for r in range(far):
        for c in range(NEAR):
            here = pl.ds(c * LANES, LANES)
            for k, out in ((1 - core, theirs), (core, mine)):
                rows = pl.ds(pl.multiple_of((k * far + r) * block, 16), block)
                out[c ^ xy, turned(r ^ z, far)] = acc[rows, here].astype(out.dtype)


def gradients_body(far, block, half, count, token, valid, x_turned, gout, gskip, past_head, *refs):
    kepts, dpres, (theirs, mine, acc) = refs[:count], refs[count : 2 * count], refs[2 * count :]
    width = past_head.shape[0]
    part = kepts[0].shape[0]
    ends, rows = x_turned.shape
    mask = jnp.broadcast_to(row(lines_of(valid, slice(0, rows)).astype(F32)).astype(BF16), (ONES, rows))
    inner, outer, at = None, [None, None], 0
    for kept, dpre in zip(kepts, dpres):
        here = slice(at, at + dpre.shape[0])
        left = below(kept[...], mask[:, here])
        for k, ref in enumerate((gout, gskip)):
            made = dot(left, ref[here, :])
            outer[k] = made if at == 0 else outer[k] + made
        left = below(past_head[...], x_turned[width:, here]) if at == 0 else x_turned[:, here]
        made = dot(left, dpre[...])
        inner = made if at == 0 else inner + made
        at = here.stop
    acc[:ends, :] = inner
    at = ends
    for k in range(2):
        acc[at : at + part, :] = outer[k][:part]
        at += part
    acc[at : at + ONES, :] = outer[half][part:]
    at += ONES
    acc[at:, :] = jnp.zeros((acc.shape[0] - at, acc.shape[1]), F32)
    place_blocks(far, block, acc, theirs, mine)


def gradients(half, token, far, block, valid, x_turned, gout, gskip, past_head, pieces):
    packed = (NEAR, far, block, LANES)
    wide = pieces[0][2].shape[1]
    count = len(pieces)
    return call(
        functools.partial(gradients_body, far, block, half, count),
        f"gradients_{half}",
        [ANYWHERE] + [VMEM] * (5 + 2 * count),
        [VMEM] * 2,
        [jax.ShapeDtypeStruct(packed, BF16), jax.ShapeDtypeStruct(packed, F32)],
        scratch=[pltpu.VMEM((2 * far * block, wide), F32)],
    )(token, valid, x_turned, gout, gskip, past_head, *(p[1] for p in pieces), *(p[2] for p in pieces))


def outputs_body(counts, token, valid, sig, w_res, w_skip, b_res, b_skip, *refs):
    first, second = refs[: counts[0]], refs[counts[0] : sum(counts)]
    out, skip, mark, rooms, sems = refs[sum(counts) :]
    copies = []
    for i in range(sig.shape[0] // ROWS):
        rows = slice(i * ROWS, (i + 1) * ROWS)
        mask = column(lines_of(valid, rows))
        gated = beside(picked(first, rows), picked(second, rows))
        branch = dot(gated, w_res[...]) + b_res[...]
        rooms[i, 0] = (sig[rows, :].astype(F32) + mask * branch).astype(BF16)
        side = dot(gated, w_skip[...]) + b_skip[...]
        rooms[i, 1] = (mask * side).astype(BF16)
        for k, ref in enumerate((out, skip)):
            copies.append(pltpu.make_async_copy(rooms.at[i, k], ref.at[pl.ds(i * ROWS, ROWS)], sems.at[i, k]))
            copies[-1].start()
    mark[...] = jnp.zeros_like(mark)
    for copy in copies:
        copy.wait()


def outputs(token, valid, sig, gated_0, gated_1, w_res, w_skip, b_res, b_skip):
    rows, width = sig.shape
    counts = (len(gated_0), len(gated_1))
    return call(
        functools.partial(outputs_body, counts),
        "outputs",
        [ANYWHERE] + [VMEM] * (6 + sum(counts)),
        [ANYWHERE, ANYWHERE, VMEM],
        [
            jax.ShapeDtypeStruct((rows, width), BF16),
            jax.ShapeDtypeStruct((rows, w_skip.shape[1]), BF16),
            MARK,
        ],
        scratch=[
            pltpu.VMEM((rows // ROWS, 2, ROWS, width), BF16),
            pltpu.SemaphoreType.DMA((rows // ROWS, 2)),
        ],
    )(token, valid, sig, w_res, w_skip, b_res, b_skip, *gated_0, *gated_1)


def inputs_body(steps, counts, token, received, gout, pos, w_in, w_cond, *refs):
    first, second = refs[: counts[0]], refs[counts[0] : sum(counts)]
    gsig, gfeat, mark, room, room_feat, sems = refs[-6:]
    rows, width = gout.shape
    copies = []
    wide = 2 * LANES

    def copy(source, target):
        copies.append(pltpu.make_async_copy(source, target, sems.at[len(copies)]))
        copies[-1].start()

    for i, step in enumerate(steps):
        begin = step * ROWS
        here = slice(begin, begin + ROWS)
        after = slice(begin + DILATION_STEP, min(begin + DILATION_STEP + ROWS, rows))
        now = side_by_side(picked(first, here), picked(second, here))
        later = side_by_side(picked(first, after), picked(second, after))
        tap = column(tap_of(lines_of(pos, after)))
        room_feat[i] = against(w_cond[...], now)
        copy(room_feat.at[i], gfeat.at[:, pl.ds(begin, ROWS)])
        for k in range(width // wide):
            some = slice(k * wide, (k + 1) * wide)
            tail = tap * against(later, w_in[some, :])
            if tail.shape[0] < ROWS:
                tail = below(tail, received[:, some].astype(F32))
            room[i, k] = gout[here, some].astype(F32) + against(now, w_in[width + k * wide : width + (k + 1) * wide, :]) + tail
            copy(room.at[i, k], gsig.at[pl.ds(begin, ROWS), pl.ds(k * wide, wide)])
    mark[...] = jnp.zeros_like(mark)
    for one in copies:
        one.wait()


def inputs(steps, token, received, gout, pos, dpre_0, dpre_1, w_in, w_cond, before):
    rows, width = gout.shape
    cond = w_cond.shape[0]
    count = width // (2 * LANES)
    counts = (len(dpre_0), len(dpre_1))
    operands = 6 + sum(counts)
    return call(
        functools.partial(inputs_body, steps, counts),
        f"inputs_{steps[0]}",
        [ANYWHERE] + [VMEM] * (operands - 1) + [ANYWHERE] * len(before),
        [ANYWHERE, ANYWHERE, VMEM],
        [
            jax.ShapeDtypeStruct((rows, width), F32),
            jax.ShapeDtypeStruct((cond, rows), F32),
            MARK,
        ],
        scratch=[
            pltpu.VMEM((len(steps), count, ROWS, 2 * LANES), F32),
            pltpu.VMEM((len(steps), cond, ROWS), F32),
            pltpu.SemaphoreType.DMA((len(steps) * (count + 1),)),
        ],
        aliases={operands + k: k for k in range(len(before))},
    )(token, received, gout, pos, w_in, w_cond, *dpre_0, *dpre_1, *before)


SHARES = ((0, 3), (1, 2))


def unpack_body(far, block, token, *refs):
    blocks, arrays, (mark, room) = refs[: 2 * len(SHARES)], refs[-9:-2], refs[-2:]
    mine, theirs = blocks[: len(SHARES)], blocks[len(SHARES) :]
    mark[...] = jnp.zeros_like(mark)
    core, z, xy = own_place()

    @pl.when(pl.program_id(0) == 0)
    def _():
        for k, parts in ((core, mine), (1 - core, theirs)):
            for share, ref in zip(SHARES, parts):
                for i, c in enumerate(share):
                    for r in range(far):
                        rows = pl.ds(pl.multiple_of((k * far + (r ^ z)) * block, 16), block)
                        room[c ^ xy, rows, :] = ref[i, turned(r, far)]

    for j in range(NEAR // 2):
        c = pl.program_id(0) * (NEAR // 2) + j
        here = pl.ds(j * LANES, LANES)
        top = 0
        for ref in arrays:
            count = ref.shape[0]
            size = max(count, ONES)
            ref[:, here] = room[c, top : top + size, :].astype(F32)[:count]
            top += size


def unpack(half, token, far, block, mine, theirs, width, cond, hidden, skip_width, before):
    part = hidden // HALVES
    gates = 2 * hidden
    own = (width, skip_width)[half]

    def wide(size):
        return pl.BlockSpec((size, part), lambda s: (0, HALVES * s + half))

    def tall(size):
        return pl.BlockSpec((part, size // 2), lambda s: (half, s))

    specs = [wide(width), wide(width), wide(cond), wide(1), tall(width), tall(skip_width), pl.BlockSpec((1, own // 2), lambda s: (0, s))]
    shapes = [(width, gates), (width, gates), (cond, gates), (1, gates), (hidden, width), (hidden, skip_width), (1, own)]
    blocks = [pl.BlockSpec(x.shape, lambda s: (0,) * 4) for x in (*mine, *theirs)]
    return call(
        functools.partial(unpack_body, far, block),
        f"unpack_{half}",
        [ANYWHERE, *blocks] + [ANYWHERE] * len(before),
        specs + [pl.BlockSpec(MARK.shape, lambda s: (0, 0))],
        [jax.ShapeDtypeStruct(shape, F32) for shape in shapes] + [MARK],
        scratch=[pltpu.VMEM((NEAR, 2 * far * block, LANES), BF16)],
        aliases={1 + len(blocks) + k: k for k in range(len(before))},
        grid=(2,),
    )(token, *mine, *theirs, *before)


def swapped(x, axis, k):
    return lax.ppermute(x, axis, [(i, i ^ k) for i in range(lax.axis_size(axis))])


def exchanged(blocks):
    return [swapped(block, "near", k + 1) for k, block in enumerate(blocks)]


def add_body(sizes, token, *refs):
    count = len(sizes)
    kept, got, outs = refs[0], refs[1:-count], refs[-count:]
    at = 0
    for out, size in zip(outs, sizes):
        for k in range(size):
            total = kept[at + k].astype(F32)
            for ref in got:
                total = total + ref[at + k].astype(F32)
            out[k] = total.astype(out.dtype)
        at += size


def added(name, token, kept, got, outs):
    sizes = [size for size, _ in outs]
    result = call(
        functools.partial(add_body, sizes),
        name,
        [ANYWHERE] + [VMEM] * (1 + len(got)),
        [VMEM] * len(outs),
        [jax.ShapeDtypeStruct((size, *kept.shape[1:]), dtype) for size, dtype in outs],
    )(token, kept, *got)
    return result


def mirror_body(token, mine, got, out):
    count = mine.shape[0]
    for k in range(count):
        out[k] = (mine[k].astype(F32) + got[count - 1 - k].astype(F32)).astype(out.dtype)


def mirrored(name, token, mine, got):
    return call(
        mirror_body,
        name,
        [ANYWHERE, VMEM, VMEM],
        VMEM,
        jax.ShapeDtypeStruct(mine.shape, BF16),
    )(token, mine, got)


def join_body(token, *refs):
    out = refs[-1]
    at = 0
    for ref in refs[:-1]:
        out[at : at + ref.shape[0]] = ref[...]
        at += ref.shape[0]


def joined(name, token, parts):
    count = sum(part.shape[0] for part in parts)
    return call(
        join_body,
        name,
        [ANYWHERE] + [VMEM] * len(parts),
        VMEM,
        jax.ShapeDtypeStruct((count, *parts[0].shape[1:]), BF16),
    )(token, *parts)


def over_outer(total):
    for bit in range((lax.axis_size("outer") - 1).bit_length()):
        total = (total.astype(F32) + swapped(total, "outer", 1 << bit).astype(F32)).astype(BF16)
    return total


def passed_along(x, by):
    peers = lax.axis_size(AXES)
    pairs = [(i, i + by) for i in range(peers) if 0 <= i + by < peers]
    return lax.ppermute(x, AXES, pairs)


def in_hbm(x):
    return pltpu.with_memory_space_constraint(x, pltpu.HBM)


def body(
    signal,
    features,
    position,
    valid,
    w_past,
    w_now,
    b_conv,
    w_cond,
    w_res,
    b_res,
    w_skip,
    b_skip,
    grad_out,
    grad_skip,
):
    rows, width = signal.shape
    features = features.T
    cond = features.shape[0]
    hidden = w_res.shape[0]
    skip_width = w_skip.shape[1]
    far = lax.axis_size("far")
    far_bits = (far - 1).bit_length()
    used = 2 * width + cond + ONES + 2 * (hidden // HALVES) + ONES
    block = -(-used // (2 * far * 16)) * 16
    lines = (rows // LANES, LANES)
    pos, val = position.reshape(lines), valid.reshape(lines)
    b_conv, b_res, b_skip = (b.reshape(1, -1) for b in (b_conv, b_res, b_skip))

    def core_sum(half, token, theirs, mine):
        kept, *sent = added(
            f"core_sum_{half}", token, mine, [swapped(theirs, "core", 1)], [(1, F32)] + [(1, BF16)] * (NEAR - 1)
        )
        return kept[0], exchanged([x[0] for x in sent])

    def near_sum(half, token, kept, got):
        kept, sent = added(f"near_sum_{half}", token, kept, got, [(far // 2, F32), (far // 2, BF16)])
        return kept, swapped(sent, "far", 1)

    def far_sum(half, token, kept, got):
        for bit in range(1, far_bits - 1):
            size = kept.shape[0] // 2
            kept, sent = added(f"far_sum_{half}_{bit}", token, kept, [got], [(size, F32), (size, BF16)])
            got = swapped(sent, "far", 1 << bit)
        (mine,) = added(f"far_sum_{half}", token, kept, [got], [(kept.shape[0], BF16)])
        return mine, swapped(mine, "far", 1 << (far_bits - 1))

    def far_end(half, token, mine, got):
        total = over_outer(mirrored(f"far_end_{half}", token, mine, got))
        return total, swapped(total, "far", 1 << (far_bits - 2))

    def far_join(half, token, mine, got):
        total = joined(f"far_join_{half}", token, [mine, got])
        for bit in reversed(range(far_bits - 2)):
            total = joined(f"far_join_{half}_{bit}", token, [total, swapped(total, "far", 1 << bit)])
        return total, exchanged([total] * (NEAR - 1))

    def near_join(half, k, token, mine, got):
        blocks = [mine, *got]
        total = joined(f"near_join_{half}_{k}", token, [blocks[c][None] for c in SHARES[k]])
        return total, swapped(total, "core", 1)

    def input_gradients(steps, token, before):
        last = (steps[-1] + 1) * ROWS == rows
        return inputs(steps, token, received if last else head_0[0], grad_out, pos, dpre_0, dpre_1, w_in, w_cond, before)

    halo = passed_along(signal[rows - DILATION_STEP :], 1)
    val, pos, b_conv, b_res, b_skip, w_cond, w_res, w_skip, w_in, past, signal, x_turned, grad_out, grad_skip, *rest_0 = load(
        val, pos, b_conv, b_res, b_skip, features, w_cond, w_res, w_skip, w_past, w_now, signal, grad_out, grad_skip
    )
    common = (signal, x_turned, grad_out, grad_skip, w_in, w_cond, b_conv, w_res, w_skip)
    past_head, head_0 = head(halo, pos, val, *common)
    made_0 = (head_0, rest_0)
    theirs_0, mine_0 = gradients(0, past_head, far, block, val, x_turned, grad_out, grad_skip, past_head, made_0)
    most_1 = forward_most(theirs_0, val, past, *common)
    kept_0, got_0 = core_sum(0, most_1[0], theirs_0, mine_0)
    head_1, last_1 = forward_ends(kept_0, halo, pos, val, past, *common)
    made_1 = (head_1, most_1, last_1)
    dpre_0, dpre_1 = ([p[2] for p in made] for made in (made_0, made_1))
    theirs_1, mine_1 = gradients(1, kept_0, far, block, val, x_turned, grad_out, grad_skip, past_head, made_1)
    output, skip_out, mark = outputs(
        theirs_1, val, signal, [p[0] for p in made_0], [p[0] for p in made_1], w_res, w_skip, b_res, b_skip
    )
    kept_0, got_0 = near_sum(0, mark, kept_0, got_0)
    kept_1, got_1 = core_sum(1, kept_0, theirs_1, mine_1)
    ends_0, got_0 = far_sum(0, kept_1, kept_0, got_0)
    *grads, mark = input_gradients((0, 1), ends_0, [])
    ends_0, got_0 = far_end(0, mark, ends_0, got_0)
    kept_1, got_1 = near_sum(1, ends_0, kept_1, got_1)
    ends_0, got_0 = far_join(0, kept_1, ends_0, got_0)
    ends_1, got_1 = far_sum(1, ends_0, kept_1, got_1)
    *grads, mark = input_gradients((2,), ends_1, grads)
    ends_1, got_1 = far_end(1, mark, ends_1, got_1)
    early = early_rows(ends_1, pos, head_0[2], head_1[2], w_in)
    received = passed_along(early, -1)
    first = near_join(0, 0, early, ends_0, got_0)
    second = near_join(0, 1, first[0], ends_0, got_0)
    pairs_0 = [first, second]
    ends_1, got_1 = far_join(1, second[0], ends_1, got_1)
    *grads, mark = input_gradients((3,), ends_1, grads)
    first = near_join(1, 0, mark, ends_1, got_1)
    second = near_join(1, 1, first[0], ends_1, got_1)
    pairs_1 = [first, second]
    sizes = (width, cond, hidden, skip_width)
    *done, own_0, mark = unpack(0, first[1], far, block, *zip(*pairs_0), *sizes, [])
    *done, own_1, _ = unpack(1, mark, far, block, *zip(*pairs_1), *sizes, done)
    g_past, g_now, g_cond, g_bias, g_res, g_skip = done
    grad_signal, grad_features = grads
    return (
        output,
        skip_out,
        grad_signal,
        grad_features.T,
        g_past,
        g_now,
        g_bias.reshape(-1),
        g_cond,
        g_res,
        own_0.reshape(-1),
        g_skip,
        own_1.reshape(-1),
    )


def solution(mesh):
    row, col = mesh.shape["row"], mesh.shape["col"]
    fine = Mesh(mesh.devices.reshape(row // 2, 2, col // NEAR, NEAR), AXES)
    rows = P(AXES, None)
    line = P(AXES)
    return jax.shard_map(
        body,
        mesh=fine,
        in_specs=(rows, rows, line, line) + (P(),) * 8 + (rows, rows),
        out_specs=(rows,) * 4 + (P(),) * 8,
        check_vma=False,
    )
```

```python
import functools

import jax
import jax.numpy as jnp
from jax import lax
from jax.experimental import pallas as pl
from jax.experimental.pallas import tpu as pltpu
from jax.sharding import Mesh
from jax.sharding import PartitionSpec as P

DILATION_STEP = 256
AXES = ("outer", "core", "far", "near")
HALVES = 2
NEAR = 4
LANES = 128
ROWS = 512
ONES = 16
F32 = jnp.float32
BF16 = jnp.bfloat16
MEGA = 1 << 20
COSTS = {
    "load": 8, "head": 2, "gradients_0": 0, "forward_1": 0, "gradients_1": 4, "outputs": 4, "near_sum_0": 8,
    "far_sum_0": 8, "near_sum_1": 4, "near_join_0_1": 2, "near_join_1_1": 4, "far_join_0": 4,
}
FLOPS = 10**9


def dot(left, right):
    return jnp.dot(left, right, preferred_element_type=F32)


def across(left, right):
    return lax.dot_general(left, right, (((0,), (0,)), ((), ())), preferred_element_type=F32)


def against(left, weight):
    return lax.dot_general(left, weight, (((1,), (1,)), ((), ())), preferred_element_type=F32)


def column(lines):
    turned = lines.astype(F32).T
    return jnp.concatenate([turned[:, k : k + 1] for k in range(lines.shape[0])], axis=0)


def row(lines):
    return jnp.concatenate([lines[k : k + 1] for k in range(lines.shape[0])], axis=1)


def tap_of(lines):
    return jnp.where(lines >= DILATION_STEP, 1, 0)


def lines_of(ref, rows):
    return ref[rows.start // LANES : rows.stop // LANES, :]


def picked(pieces, rows):
    found, at = [], 0
    for ref in pieces:
        low, high = max(rows.start, at), min(rows.stop, at + ref.shape[0])
        if low < high:
            found.append(ref[low - at : high - at, :])
        at += ref.shape[0]
    return found[0] if len(found) == 1 else jnp.concatenate(found, axis=0)


def call(kernel, name, in_specs, out_specs, out_shape, scratch=(), aliases=None, grid=(), vmem=24):
    return pl.pallas_call(
        kernel,
        grid=grid,
        in_specs=in_specs,
        out_specs=out_specs,
        out_shape=out_shape,
        scratch_shapes=list(scratch),
        input_output_aliases=aliases or {},
        cost_estimate=pl.CostEstimate(
            flops=1 + int(FLOPS * COSTS.get(name, COSTS.get(name.split("_")[0], 0))), bytes_accessed=1, transcendentals=0
        ),
        name=name,
        compiler_params=pltpu.CompilerParams(vmem_limit_bytes=vmem * MEGA),
    )


VMEM = pl.BlockSpec(memory_space=pltpu.VMEM)
ANYWHERE = pl.BlockSpec(memory_space=pl.ANY)
MARK = jax.ShapeDtypeStruct((8, LANES), F32)


def beside(*parts):
    return jnp.concatenate(parts, axis=1)


def below(*parts):
    return jnp.concatenate(parts, axis=0)


def gate_product(half, k, rows, past, sig, feats, w_in, w_cond, b_conv):
    width = sig.shape[1]
    part = w_in.shape[1] // 2 // HALVES
    at = (k * HALVES + half) * part
    here = slice(at, at + part)
    own = dot(past, w_in[:width, here]) + dot(sig[rows, :], w_in[width:, here])
    return own + across(feats, w_cond[:, here]) + b_conv[:, here]


def back_product(half, rows, gout, gskip, w_res, w_skip):
    part = w_res.shape[0] // HALVES
    here = slice(half * part, (half + 1) * part)
    return against(gout[rows, :], w_res[here, :]) + against(gskip[rows, :], w_skip[here, :])


def finish(pre_a, pre_s, dgated, valid_lines):
    act = jnp.tanh(pre_a)
    gate = 0.5 + 0.5 * jnp.tanh(0.5 * pre_s)
    slope = (column(valid_lines) * dgated) * gate
    dpre = beside(slope * (1.0 - act * act), slope * act * (1.0 - gate)).astype(BF16)
    gated = (act * gate).astype(BF16)
    return gated, gated.T * row(valid_lines.astype(BF16)), dpre


def forward_tiles(half, tiles, prepare, arrive, valid, past, sig, x_turned, gout, gskip, weights, outs, base):
    w_in, w_cond, b_conv, w_res, w_skip = weights
    gated_out, kept_out, dpre_out = outs
    cond = w_cond.shape[0]
    width = sig.shape[1]

    def product(rows, k):
        if arrive:
            arrive(rows, k)
        if k == 2:
            return back_product(half, rows, gout, gskip, w_res, w_skip)
        feats = x_turned[2 * width : 2 * width + cond, rows]
        return gate_product(half, k, rows, past[rows, :], sig, feats, w_in, w_cond, b_conv)

    def done(rows, made):
        there = slice(rows.start - base, rows.stop - base)
        gated_out[there, :], kept_out[:, there], dpre_out[there, :] = finish(*made, lines_of(valid, rows))

    ahead = None
    for rows in tiles:
        if prepare:
            prepare(rows)
        made = [product(rows, k) for k in range(3)]
        if ahead:
            done(*ahead)
        ahead = (rows, made)
    done(*ahead)


def tiles_of(start, stop):
    return [slice(a, a + DILATION_STEP) for a in range(start, stop, DILATION_STEP)]


def split_rows(rows):
    return rows - DILATION_STEP


def load_body(
    valid, pos, b_conv, b_res, b_skip, feat, w_cond, w_res, w_skip, w_past, w_now, sig, gout, gskip,
    valid_to, pos_to, b_conv_to, b_res_to, b_skip_to, w_cond_to, w_res_to, w_skip_to, w_in, past, sig_to, x_turned,
    gout_to, gskip_to, gated_rest, kept_rest, dpre_rest, sems,
):
    rows_all, width = sig.shape
    cond = feat.shape[0]
    count = 0

    def start(source, target):
        nonlocal count
        copy = pltpu.make_async_copy(source, target, sems.at[count])
        copy.start()
        count += 1
        return copy

    def tile(i, source, target):
        rows = pl.ds(i * ROWS, ROWS)
        return start(source.at[rows], target.at[rows])

    signals = [[tile(0, sig, sig_to)]]
    needs = [
        [
            start(pos, pos_to),
            start(w_past, w_in.at[pl.ds(0, width)]),
            start(w_now, w_in.at[pl.ds(width, width)]),
            start(feat, x_turned.at[pl.ds(2 * width, cond)]),
            start(w_cond, w_cond_to),
            start(b_conv, b_conv_to),
        ],
        [],
        [start(valid, valid_to), start(w_res, w_res_to), start(w_skip, w_skip_to)],
    ]
    cotangents = [[tile(0, gout, gout_to), tile(0, gskip, gskip_to)]]
    for i in range(1, rows_all // ROWS):
        signals.append([tile(i, sig, sig_to)])
        cotangents.append([tile(i, gout, gout_to), tile(i, gskip, gskip_to)])
    last = [start(b_res, b_res_to), start(b_skip, b_skip_to)]

    def wait(copies):
        for copy in copies:
            copy.wait()
        copies.clear()

    def prepare(rows):
        i = rows.start // ROWS
        wait(signals[i])
        wait(needs[0])
        whole = rows if i else slice(0, rows.stop)
        before = slice(rows.start - DILATION_STEP, rows.stop - DILATION_STEP)
        tap = tap_of(lines_of(pos_to, rows)).astype(F32)
        past[rows, :] = sig_to[before, :] * column(tap).astype(BF16)
        x_turned[width : 2 * width, whole] = sig_to[whole, :].T
        x_turned[:width, rows] = x_turned[width : 2 * width, before] * row(tap).astype(BF16)

    def arrive(rows, k):
        wait(needs[k])
        if k == 2:
            wait(cotangents[rows.start // ROWS])

    x_turned[2 * width + cond :, :] = jnp.ones((x_turned.shape[0] - 2 * width - cond, rows_all), BF16)
    forward_tiles(
        0, tiles_of(DILATION_STEP, rows_all), prepare, arrive, valid_to, past, sig_to, x_turned, gout_to, gskip_to,
        (w_in, w_cond_to, b_conv_to, w_res_to, w_skip_to), (gated_rest, kept_rest, dpre_rest), DILATION_STEP,
    )
    wait(last)


def rest_shapes(rest, part):
    return [jax.ShapeDtypeStruct(shape, BF16) for shape in ((rest, part), (part, rest), (rest, 2 * part))]


def load(*arrays):
    sources = [in_hbm(x) for x in arrays]
    feat, w_cond, w_res, w_skip, w_past, w_now, sig, gout, gskip = arrays[5:]
    rows, width = sig.shape
    hidden = w_res.shape[0]
    shapes = [jax.ShapeDtypeStruct(x.shape, x.dtype) for x in arrays[:5] + (w_cond, w_res, w_skip)] + [
        jax.ShapeDtypeStruct(shape, BF16)
        for shape in (
            (2 * width, 2 * hidden), sig.shape, sig.shape, (2 * width + feat.shape[0] + ONES, rows), gout.shape, gskip.shape,
        )
    ]
    shapes += rest_shapes(rows - DILATION_STEP, hidden // HALVES)
    return call(
        load_body,
        "load",
        [ANYWHERE] * len(sources),
        [VMEM] * len(shapes),
        shapes,
        scratch=[pltpu.SemaphoreType.DMA((11 + 3 * (rows // ROWS),))],
    )(*sources)


def side_by_side(dpre_0, dpre_1):
    part = dpre_0.shape[1] // 2
    return beside(dpre_0[:, :part], dpre_1[:, :part], dpre_0[:, part:], dpre_1[:, part:])


def head_rows(half, halo, pos, valid, sig, x_turned, gout, gskip, weights, outs):
    w_in, w_cond, b_conv, w_res, w_skip = weights
    rows = slice(0, DILATION_STEP)
    width = halo.shape[1]
    feats = x_turned[2 * width : 2 * width + w_cond.shape[0], rows]
    past = halo[...] * column(tap_of(lines_of(pos, rows)).astype(F32)).astype(BF16)
    made = [gate_product(half, k, rows, past, sig, feats, w_in, w_cond, b_conv) for k in range(2)]
    made.append(back_product(half, rows, gout, gskip, w_res, w_skip))
    for ref, value in zip(outs, finish(*made, lines_of(valid, rows))):
        ref[...] = value


def head_body(halo, pos, valid, sig, x_turned, gout, gskip, w_in, w_cond, b_conv, w_res, w_skip, past_out, *outs):
    tap = tap_of(lines_of(pos, slice(0, DILATION_STEP))).astype(F32)
    past_out[...] = halo[...].T * row(tap).astype(BF16)
    head_rows(0, halo, pos, valid, sig, x_turned, gout, gskip, (w_in, w_cond, b_conv, w_res, w_skip), outs)


def head(halo, *args):
    width = halo.shape[1]
    part = args[-1].shape[0] // HALVES
    past, *parts = call(
        head_body,
        "head",
        [VMEM] * (1 + len(args)),
        [VMEM] * 4,
        [jax.ShapeDtypeStruct((width, DILATION_STEP), BF16)] + rest_shapes(DILATION_STEP, part),
    )(halo, *args)
    return past, parts


def early_body(token, pos, dpre_0, dpre_1, w_in, early):
    tap = column(tap_of(lines_of(pos, slice(0, DILATION_STEP))))
    early[...] = (tap * against(side_by_side(dpre_0[...], dpre_1[...]), w_in[: early.shape[1], :])).astype(BF16)


def early_rows(token, pos, dpre_0, dpre_1, w_in):
    return call(
        early_body,
        "early",
        [ANYWHERE] + [VMEM] * 4,
        VMEM,
        jax.ShapeDtypeStruct((DILATION_STEP, w_in.shape[0] // 2), BF16),
    )(token, pos, dpre_0, dpre_1, w_in)


def most_body(token, valid, past, sig, x_turned, gout, gskip, w_in, w_cond, b_conv, w_res, w_skip, *outs):
    forward_tiles(
        1, tiles_of(DILATION_STEP, split_rows(sig.shape[0])), None, None, valid, past, sig, x_turned, gout, gskip,
        (w_in, w_cond, b_conv, w_res, w_skip), outs, DILATION_STEP,
    )


def forward_most(token, *args):
    part = args[-1].shape[0] // HALVES
    return call(
        most_body,
        "forward_1",
        [ANYWHERE] + [VMEM] * len(args),
        [VMEM] * 3,
        rest_shapes(split_rows(args[2].shape[0]) - DILATION_STEP, part),
    )(token, *args)


def ends_body(token, halo, pos, valid, past, sig, x_turned, gout, gskip, w_in, w_cond, b_conv, w_res, w_skip, *outs):
    weights = (w_in, w_cond, b_conv, w_res, w_skip)
    rows = sig.shape[0]
    head_rows(1, halo, pos, valid, sig, x_turned, gout, gskip, weights, outs[:3])
    forward_tiles(
        1, tiles_of(split_rows(rows), rows), None, None, valid, past, sig, x_turned, gout, gskip, weights, outs[3:],
        split_rows(rows),
    )


def forward_ends(token, *args):
    part = args[-1].shape[0] // HALVES
    rows = args[4].shape[0]
    parts = call(
        ends_body,
        "ends_1",
        [ANYWHERE] + [VMEM] * len(args),
        [VMEM] * 6,
        rest_shapes(DILATION_STEP, part) + rest_shapes(rows - split_rows(rows), part),
    )(token, *args)
    return parts[:3], parts[3:]


def own_place():
    return [lax.axis_index(name) for name in ("core", "far", "near")]


def turned(index, count):
    bits = (count - 1).bit_length()
    result = 0
    for bit in range(bits):
        result = result | (((index >> bit) & 1) << (bits - 1 - bit))
    return result


def place_blocks(far, block, acc, theirs, mine):
    core, z, xy = own_place()
    for r in range(far):
        for c in range(NEAR):
            here = pl.ds(c * LANES, LANES)
            for k, out in ((1 - core, theirs), (core, mine)):
                rows = pl.ds(pl.multiple_of((k * far + r) * block, 16), block)
                out[c ^ xy, turned(r ^ z, far)] = acc[rows, here].astype(out.dtype)


def gradients_body(far, block, half, count, token, valid, x_turned, gout, gskip, past_head, *refs):
    kepts, dpres, (theirs, mine, acc) = refs[:count], refs[count : 2 * count], refs[2 * count :]
    width = past_head.shape[0]
    part = kepts[0].shape[0]
    ends, rows = x_turned.shape
    mask = jnp.broadcast_to(row(lines_of(valid, slice(0, rows)).astype(F32)).astype(BF16), (ONES, rows))
    inner, outer, at = None, [None, None], 0
    for kept, dpre in zip(kepts, dpres):
        here = slice(at, at + dpre.shape[0])
        left = below(kept[...], mask[:, here])
        for k, ref in enumerate((gout, gskip)):
            made = dot(left, ref[here, :])
            outer[k] = made if at == 0 else outer[k] + made
        left = below(past_head[...], x_turned[width:, here]) if at == 0 else x_turned[:, here]
        made = dot(left, dpre[...])
        inner = made if at == 0 else inner + made
        at = here.stop
    acc[:ends, :] = inner
    at = ends
    for k in range(2):
        acc[at : at + part, :] = outer[k][:part]
        at += part
    acc[at : at + ONES, :] = outer[half][part:]
    at += ONES
    acc[at:, :] = jnp.zeros((acc.shape[0] - at, acc.shape[1]), F32)
    place_blocks(far, block, acc, theirs, mine)


def gradients(half, token, far, block, valid, x_turned, gout, gskip, past_head, pieces):
    packed = (NEAR, far, block, LANES)
    wide = pieces[0][2].shape[1]
    count = len(pieces)
    return call(
        functools.partial(gradients_body, far, block, half, count),
        f"gradients_{half}",
        [ANYWHERE] + [VMEM] * (5 + 2 * count),
        [VMEM] * 2,
        [jax.ShapeDtypeStruct(packed, BF16), jax.ShapeDtypeStruct(packed, F32)],
        scratch=[pltpu.VMEM((2 * far * block, wide), F32)],
    )(token, valid, x_turned, gout, gskip, past_head, *(p[1] for p in pieces), *(p[2] for p in pieces))


def outputs_body(counts, token, valid, sig, w_res, w_skip, b_res, b_skip, *refs):
    first, second = refs[: counts[0]], refs[counts[0] : sum(counts)]
    out, skip, mark, rooms, sems = refs[sum(counts) :]
    copies = []
    for i in range(sig.shape[0] // ROWS):
        rows = slice(i * ROWS, (i + 1) * ROWS)
        mask = column(lines_of(valid, rows))
        gated = beside(picked(first, rows), picked(second, rows))
        branch = dot(gated, w_res[...]) + b_res[...]
        rooms[i, 0] = (sig[rows, :].astype(F32) + mask * branch).astype(BF16)
        side = dot(gated, w_skip[...]) + b_skip[...]
        rooms[i, 1] = (mask * side).astype(BF16)
        for k, ref in enumerate((out, skip)):
            copies.append(pltpu.make_async_copy(rooms.at[i, k], ref.at[pl.ds(i * ROWS, ROWS)], sems.at[i, k]))
            copies[-1].start()
    mark[...] = jnp.zeros_like(mark)
    for copy in copies:
        copy.wait()


def outputs(token, valid, sig, gated_0, gated_1, w_res, w_skip, b_res, b_skip):
    rows, width = sig.shape
    counts = (len(gated_0), len(gated_1))
    return call(
        functools.partial(outputs_body, counts),
        "outputs",
        [ANYWHERE] + [VMEM] * (6 + sum(counts)),
        [ANYWHERE, ANYWHERE, VMEM],
        [
            jax.ShapeDtypeStruct((rows, width), BF16),
            jax.ShapeDtypeStruct((rows, w_skip.shape[1]), BF16),
            MARK,
        ],
        scratch=[
            pltpu.VMEM((rows // ROWS, 2, ROWS, width), BF16),
            pltpu.SemaphoreType.DMA((rows // ROWS, 2)),
        ],
    )(token, valid, sig, w_res, w_skip, b_res, b_skip, *gated_0, *gated_1)


def inputs_body(steps, counts, only, token, received, gout, pos, w_in, w_cond, *refs):
    refs[-4][...] = jnp.zeros_like(refs[-4])
    if only is None:
        inputs_steps(steps, counts, received, gout, pos, w_in, w_cond, *refs)
        return

    @pl.when(lax.axis_index("core") == only)
    def _():
        inputs_steps(steps, counts, received, gout, pos, w_in, w_cond, *refs)


def inputs_steps(steps, counts, received, gout, pos, w_in, w_cond, *refs):
    first, second = refs[: counts[0]], refs[counts[0] : sum(counts)]
    gsig, gfeat, _, room, room_feat, sems = refs[-6:]
    rows, width = gout.shape
    copies = []
    wide = 2 * LANES

    def copy(source, target):
        copies.append(pltpu.make_async_copy(source, target, sems.at[len(copies)]))
        copies[-1].start()

    for i, step in enumerate(steps):
        begin = step * ROWS
        here = slice(begin, begin + ROWS)
        after = slice(begin + DILATION_STEP, min(begin + DILATION_STEP + ROWS, rows))
        now = side_by_side(picked(first, here), picked(second, here))
        later = side_by_side(picked(first, after), picked(second, after))
        tap = column(tap_of(lines_of(pos, after)))
        room_feat[i] = against(w_cond[...], now)
        copy(room_feat.at[i], gfeat.at[:, pl.ds(begin, ROWS)])
        for k in range(width // wide):
            some = slice(k * wide, (k + 1) * wide)
            tail = tap * against(later, w_in[some, :])
            if tail.shape[0] < ROWS:
                tail = below(tail, received[:, some].astype(F32))
            room[i, k] = gout[here, some].astype(F32) + against(now, w_in[width + k * wide : width + (k + 1) * wide, :]) + tail
            copy(room.at[i, k], gsig.at[pl.ds(begin, ROWS), pl.ds(k * wide, wide)])
    for one in copies:
        one.wait()


def inputs(steps, only, token, received, gout, pos, dpre_0, dpre_1, w_in, w_cond, before):
    rows, width = gout.shape
    cond = w_cond.shape[0]
    count = width // (2 * LANES)
    counts = (len(dpre_0), len(dpre_1))
    operands = 6 + sum(counts)
    return call(
        functools.partial(inputs_body, steps, counts, only),
        f"inputs_{steps[0]}" + ("" if only is None else f"_{only}"),
        [ANYWHERE] + [VMEM] * (operands - 1) + [ANYWHERE] * len(before),
        [ANYWHERE, ANYWHERE, VMEM],
        [
            jax.ShapeDtypeStruct((rows, width), F32),
            jax.ShapeDtypeStruct((cond, rows), F32),
            MARK,
        ],
        scratch=[
            pltpu.VMEM((len(steps), count, ROWS, 2 * LANES), F32),
            pltpu.VMEM((len(steps), cond, ROWS), F32),
            pltpu.SemaphoreType.DMA((len(steps) * (count + 1),)),
        ],
        aliases={operands + k: k for k in range(len(before))},
    )(token, received, gout, pos, w_in, w_cond, *dpre_0, *dpre_1, *before)


SHARES = ((0, 3), (1, 2))


def unpack_body(far, block, token, *refs):
    blocks, arrays, (mark, room) = refs[: 2 * len(SHARES)], refs[-9:-2], refs[-2:]
    mine, theirs = blocks[: len(SHARES)], blocks[len(SHARES) :]
    mark[...] = jnp.zeros_like(mark)
    core, z, xy = own_place()

    @pl.when(pl.program_id(0) == 0)
    def _():
        for k, parts in ((core, mine), (1 - core, theirs)):
            for share, ref in zip(SHARES, parts):
                for i, c in enumerate(share):
                    for r in range(far):
                        rows = pl.ds(pl.multiple_of((k * far + (r ^ z)) * block, 16), block)
                        room[c ^ xy, rows, :] = ref[i, turned(r, far)]

    for j in range(NEAR // 2):
        c = pl.program_id(0) * (NEAR // 2) + j
        here = pl.ds(j * LANES, LANES)
        top = 0
        for ref in arrays:
            count = ref.shape[0]
            size = max(count, ONES)
            ref[:, here] = room[c, top : top + size, :].astype(F32)[:count]
            top += size


def unpack(half, token, far, block, mine, theirs, width, cond, hidden, skip_width, before):
    part = hidden // HALVES
    gates = 2 * hidden
    own = (width, skip_width)[half]

    def wide(size):
        return pl.BlockSpec((size, part), lambda s: (0, HALVES * s + half))

    def tall(size):
        return pl.BlockSpec((part, size // 2), lambda s: (half, s))

    specs = [wide(width), wide(width), wide(cond), wide(1), tall(width), tall(skip_width), pl.BlockSpec((1, own // 2), lambda s: (0, s))]
    shapes = [(width, gates), (width, gates), (cond, gates), (1, gates), (hidden, width), (hidden, skip_width), (1, own)]
    blocks = [pl.BlockSpec(x.shape, lambda s: (0,) * 4) for x in (*mine, *theirs)]
    return call(
        functools.partial(unpack_body, far, block),
        f"unpack_{half}",
        [ANYWHERE, *blocks] + [ANYWHERE] * len(before),
        specs + [pl.BlockSpec(MARK.shape, lambda s: (0, 0))],
        [jax.ShapeDtypeStruct(shape, F32) for shape in shapes] + [MARK],
        scratch=[pltpu.VMEM((NEAR, 2 * far * block, LANES), BF16)],
        aliases={1 + len(blocks) + k: k for k in range(len(before))},
        grid=(2,),
    )(token, *mine, *theirs, *before)


def swapped(x, axis, k):
    return lax.ppermute(x, axis, [(i, i ^ k) for i in range(lax.axis_size(axis))])


def exchanged(blocks):
    return [swapped(block, "near", k + 1) for k, block in enumerate(blocks)]


def add_body(sizes, token, *refs):
    count = len(sizes)
    kept, got, outs = refs[0], refs[1:-count], refs[-count:]
    at = 0
    for out, size in zip(outs, sizes):
        for k in range(size):
            total = kept[at + k].astype(F32)
            for ref in got:
                total = total + ref[at + k].astype(F32)
            out[k] = total.astype(out.dtype)
        at += size


def added(name, token, kept, got, outs):
    sizes = [size for size, _ in outs]
    result = call(
        functools.partial(add_body, sizes),
        name,
        [ANYWHERE] + [VMEM] * (1 + len(got)),
        [VMEM] * len(outs),
        [jax.ShapeDtypeStruct((size, *kept.shape[1:]), dtype) for size, dtype in outs],
    )(token, kept, *got)
    return result


def mirror_body(token, mine, got, out):
    count = mine.shape[0]
    for k in range(count):
        out[k] = (mine[k].astype(F32) + got[count - 1 - k].astype(F32)).astype(out.dtype)


def mirrored(name, token, mine, got):
    return call(
        mirror_body,
        name,
        [ANYWHERE, VMEM, VMEM],
        VMEM,
        jax.ShapeDtypeStruct(mine.shape, BF16),
    )(token, mine, got)


def join_body(token, *refs):
    out = refs[-1]
    at = 0
    for ref in refs[:-1]:
        out[at : at + ref.shape[0]] = ref[...]
        at += ref.shape[0]


def joined(name, token, parts):
    count = sum(part.shape[0] for part in parts)
    return call(
        join_body,
        name,
        [ANYWHERE] + [VMEM] * len(parts),
        VMEM,
        jax.ShapeDtypeStruct((count, *parts[0].shape[1:]), BF16),
    )(token, *parts)


def over_outer(total):
    for bit in range((lax.axis_size("outer") - 1).bit_length()):
        total = (total.astype(F32) + swapped(total, "outer", 1 << bit).astype(F32)).astype(BF16)
    return total


def passed_along(x, by):
    peers = lax.axis_size(AXES)
    pairs = [(i, i + by) for i in range(peers) if 0 <= i + by < peers]
    return lax.ppermute(x, AXES, pairs)


def in_hbm(x):
    return pltpu.with_memory_space_constraint(x, pltpu.HBM)


def body(
    signal,
    features,
    position,
    valid,
    w_past,
    w_now,
    b_conv,
    w_cond,
    w_res,
    b_res,
    w_skip,
    b_skip,
    grad_out,
    grad_skip,
):
    rows, width = signal.shape
    features = features.T
    cond = features.shape[0]
    hidden = w_res.shape[0]
    skip_width = w_skip.shape[1]
    far = lax.axis_size("far")
    far_bits = (far - 1).bit_length()
    used = 2 * width + cond + ONES + 2 * (hidden // HALVES) + ONES
    block = -(-used // (2 * far * 16)) * 16
    lines = (rows // LANES, LANES)
    pos, val = position.reshape(lines), valid.reshape(lines)
    b_conv, b_res, b_skip = (b.reshape(1, -1) for b in (b_conv, b_res, b_skip))

    def core_sum(half, token, theirs, mine):
        kept, *sent = added(
            f"core_sum_{half}", token, mine, [swapped(theirs, "core", 1)], [(1, F32)] + [(1, BF16)] * (NEAR - 1)
        )
        return kept[0], exchanged([x[0] for x in sent])

    def near_sum(half, token, kept, got):
        kept, sent = added(f"near_sum_{half}", token, kept, got, [(far // 2, F32), (far // 2, BF16)])
        return kept, swapped(sent, "far", 1)

    def far_sum(half, token, kept, got):
        for bit in range(1, far_bits - 1):
            size = kept.shape[0] // 2
            kept, sent = added(f"far_sum_{half}_{bit}", token, kept, [got], [(size, F32), (size, BF16)])
            got = swapped(sent, "far", 1 << bit)
        (mine,) = added(f"far_sum_{half}", token, kept, [got], [(kept.shape[0], BF16)])
        return mine, swapped(mine, "far", 1 << (far_bits - 1))

    def far_end(half, token, mine, got):
        total = over_outer(mirrored(f"far_end_{half}", token, mine, got))
        return total, swapped(total, "far", 1 << (far_bits - 2))

    def far_join(half, token, mine, got):
        total = joined(f"far_join_{half}", token, [mine, got])
        for bit in reversed(range(far_bits - 2)):
            total = joined(f"far_join_{half}_{bit}", token, [total, swapped(total, "far", 1 << bit)])
        return total, exchanged([total] * (NEAR - 1))

    def near_join(half, k, token, mine, got):
        blocks = [mine, *got]
        total = joined(f"near_join_{half}_{k}", token, [blocks[c][None] for c in SHARES[k]])
        return total, swapped(total, "core", 1)

    def input_gradients(steps, token, before, only=None):
        last = (steps[-1] + 1) * ROWS == rows
        return inputs(steps, only, token, received if last else head_0[0], grad_out, pos, dpre_0, dpre_1, w_in, w_cond, before)

    halo = passed_along(signal[rows - DILATION_STEP :], 1)
    val, pos, b_conv, b_res, b_skip, w_cond, w_res, w_skip, w_in, past, signal, x_turned, grad_out, grad_skip, *rest_0 = load(
        val, pos, b_conv, b_res, b_skip, features, w_cond, w_res, w_skip, w_past, w_now, signal, grad_out, grad_skip
    )
    common = (signal, x_turned, grad_out, grad_skip, w_in, w_cond, b_conv, w_res, w_skip)
    past_head, head_0 = head(halo, pos, val, *common)
    made_0 = (head_0, rest_0)
    theirs_0, mine_0 = gradients(0, past_head, far, block, val, x_turned, grad_out, grad_skip, past_head, made_0)
    most_1 = forward_most(theirs_0, val, past, *common)
    kept_0, got_0 = core_sum(0, most_1[0], theirs_0, mine_0)
    head_1, last_1 = forward_ends(kept_0, halo, pos, val, past, *common)
    made_1 = (head_1, most_1, last_1)
    dpre_0, dpre_1 = ([p[2] for p in made] for made in (made_0, made_1))
    theirs_1, mine_1 = gradients(1, kept_0, far, block, val, x_turned, grad_out, grad_skip, past_head, made_1)
    output, skip_out, mark = outputs(
        theirs_1, val, signal, [p[0] for p in made_0], [p[0] for p in made_1], w_res, w_skip, b_res, b_skip
    )
    kept_0, got_0 = near_sum(0, mark, kept_0, got_0)
    *grads, mark = input_gradients((2,), kept_0, [], only=1)
    kept_1, got_1 = core_sum(1, mark, theirs_1, mine_1)
    ends_0, got_0 = far_sum(0, kept_1, kept_0, got_0)
    *grads, mark = input_gradients((0, 1), ends_0, grads)
    ends_0, got_0 = far_end(0, mark, ends_0, got_0)
    kept_1, got_1 = near_sum(1, ends_0, kept_1, got_1)
    ends_0, got_0 = far_join(0, kept_1, ends_0, got_0)
    ends_1, got_1 = far_sum(1, ends_0, kept_1, got_1)
    *grads, mark = input_gradients((2,), ends_1, grads, only=0)
    ends_1, got_1 = far_end(1, mark, ends_1, got_1)
    early = early_rows(ends_1, pos, head_0[2], head_1[2], w_in)
    received = passed_along(early, -1)
    first = near_join(0, 0, early, ends_0, got_0)
    second = near_join(0, 1, first[0], ends_0, got_0)
    pairs_0 = [first, second]
    ends_1, got_1 = far_join(1, second[0], ends_1, got_1)
    *grads, mark = input_gradients((3,), ends_1, grads)
    first = near_join(1, 0, mark, ends_1, got_1)
    second = near_join(1, 1, first[0], ends_1, got_1)
    pairs_1 = [first, second]
    sizes = (width, cond, hidden, skip_width)
    *done, own_0, mark = unpack(0, first[1], far, block, *zip(*pairs_0), *sizes, [])
    *done, own_1, _ = unpack(1, mark, far, block, *zip(*pairs_1), *sizes, done)
    g_past, g_now, g_cond, g_bias, g_res, g_skip = done
    grad_signal, grad_features = grads
    return (
        output,
        skip_out,
        grad_signal,
        grad_features.T,
        g_past,
        g_now,
        g_bias.reshape(-1),
        g_cond,
        g_res,
        own_0.reshape(-1),
        g_skip,
        own_1.reshape(-1),
    )


def solution(mesh):
    row, col = mesh.shape["row"], mesh.shape["col"]
    fine = Mesh(mesh.devices.reshape(row // 2, 2, col // NEAR, NEAR), AXES)
    rows = P(AXES, None)
    line = P(AXES)
    return jax.shard_map(
        body,
        mesh=fine,
        in_specs=(rows, rows, line, line) + (P(),) * 8 + (rows, rows),
        out_specs=(rows,) * 4 + (P(),) * 8,
        check_vma=False,
    )
```

```python
import functools

import jax
import jax.numpy as jnp
from jax import lax
from jax.experimental import pallas as pl
from jax.experimental.pallas import tpu as pltpu
from jax.sharding import Mesh
from jax.sharding import PartitionSpec as P

DILATION_STEP = 256
AXES = ("outer", "core", "far", "near")
HALVES = 2
NEAR = 4
LANES = 128
ROWS = 512
ONES = 16
F32 = jnp.float32
BF16 = jnp.bfloat16
MEGA = 1 << 20
COSTS = {
    "load": 8, "head": 2, "near_sum_0": 7, "mine_1": 2,
    "far_sum_0": 8, "near_sum_1": 4, "near_join_0_1": 2, "near_join_1_1": 4, "far_join_0": 4,
}
FLOPS = 10**9


def dot(left, right):
    return jnp.dot(left, right, preferred_element_type=F32)


def across(left, right):
    return lax.dot_general(left, right, (((0,), (0,)), ((), ())), preferred_element_type=F32)


def against(left, weight):
    return lax.dot_general(left, weight, (((1,), (1,)), ((), ())), preferred_element_type=F32)


def column(lines):
    turned = lines.astype(F32).T
    return jnp.concatenate([turned[:, k : k + 1] for k in range(lines.shape[0])], axis=0)


def row(lines):
    return jnp.concatenate([lines[k : k + 1] for k in range(lines.shape[0])], axis=1)


def tap_of(lines):
    return jnp.where(lines >= DILATION_STEP, 1, 0)


def lines_of(ref, rows):
    return ref[rows.start // LANES : rows.stop // LANES, :]


def picked(pieces, rows):
    found, at = [], 0
    for ref in pieces:
        low, high = max(rows.start, at), min(rows.stop, at + ref.shape[0])
        if low < high:
            found.append(ref[low - at : high - at, :])
        at += ref.shape[0]
    return found[0] if len(found) == 1 else jnp.concatenate(found, axis=0)


def call(kernel, name, in_specs, out_specs, out_shape, scratch=(), aliases=None, grid=(), vmem=24):
    return pl.pallas_call(
        kernel,
        grid=grid,
        in_specs=in_specs,
        out_specs=out_specs,
        out_shape=out_shape,
        scratch_shapes=list(scratch),
        input_output_aliases=aliases or {},
        cost_estimate=pl.CostEstimate(
            flops=1 + int(FLOPS * COSTS.get(name, COSTS.get(name.split("_")[0], 0))), bytes_accessed=1, transcendentals=0
        ),
        name=name,
        compiler_params=pltpu.CompilerParams(vmem_limit_bytes=vmem * MEGA),
    )


VMEM = pl.BlockSpec(memory_space=pltpu.VMEM)
ANYWHERE = pl.BlockSpec(memory_space=pl.ANY)
MARK = jax.ShapeDtypeStruct((8, LANES), F32)


def beside(*parts):
    return jnp.concatenate(parts, axis=1)


def below(*parts):
    return jnp.concatenate(parts, axis=0)


def gate_product(half, k, rows, past, sig, feats, w_in, w_cond, b_conv):
    width = sig.shape[1]
    part = w_in.shape[1] // 2 // HALVES
    at = (k * HALVES + half) * part
    here = slice(at, at + part)
    own = dot(past, w_in[:width, here]) + dot(sig[rows, :], w_in[width:, here])
    return own + across(feats, w_cond[:, here]) + b_conv[:, here]


def back_product(half, rows, gout, gskip, w_res, w_skip):
    part = w_res.shape[0] // HALVES
    here = slice(half * part, (half + 1) * part)
    return against(gout[rows, :], w_res[here, :]) + against(gskip[rows, :], w_skip[here, :])


def finish(pre_a, pre_s, dgated, valid_lines):
    act = jnp.tanh(pre_a)
    gate = 0.5 + 0.5 * jnp.tanh(0.5 * pre_s)
    slope = (column(valid_lines) * dgated) * gate
    dpre = beside(slope * (1.0 - act * act), slope * act * (1.0 - gate)).astype(BF16)
    gated = (act * gate).astype(BF16)
    return gated, gated.T * row(valid_lines.astype(BF16)), dpre


def forward_tiles(half, tiles, prepare, arrive, valid, past, sig, x_turned, gout, gskip, weights, outs, base):
    w_in, w_cond, b_conv, w_res, w_skip = weights
    gated_out, kept_out, dpre_out = outs
    cond = w_cond.shape[0]
    width = sig.shape[1]

    def product(rows, k):
        if arrive:
            arrive(rows, k)
        if k == 2:
            return back_product(half, rows, gout, gskip, w_res, w_skip)
        feats = x_turned[2 * width : 2 * width + cond, rows]
        return gate_product(half, k, rows, past[rows, :], sig, feats, w_in, w_cond, b_conv)

    def done(rows, made):
        there = slice(rows.start - base, rows.stop - base)
        gated_out[there, :], kept_out[:, there], dpre_out[there, :] = finish(*made, lines_of(valid, rows))

    ahead = None
    for rows in tiles:
        if prepare:
            prepare(rows)
        made = [product(rows, k) for k in range(3)]
        if ahead:
            done(*ahead)
        ahead = (rows, made)
    done(*ahead)


def tiles_of(start, stop):
    return [slice(a, a + DILATION_STEP) for a in range(start, stop, DILATION_STEP)]


def split_rows(rows):
    return rows // 2


def load_body(
    valid, pos, b_conv, b_res, b_skip, feat, w_cond, w_res, w_skip, w_past, w_now, sig, gout, gskip,
    valid_to, pos_to, b_conv_to, b_res_to, b_skip_to, w_cond_to, w_res_to, w_skip_to, w_in, past, sig_to, x_turned,
    gout_to, gskip_to, gated_rest, kept_rest, dpre_rest, sems,
):
    rows_all, width = sig.shape
    cond = feat.shape[0]
    count = 0

    def start(source, target):
        nonlocal count
        copy = pltpu.make_async_copy(source, target, sems.at[count])
        copy.start()
        count += 1
        return copy

    def tile(i, source, target):
        rows = pl.ds(i * ROWS, ROWS)
        return start(source.at[rows], target.at[rows])

    signals = [[tile(0, sig, sig_to)]]
    needs = [
        [
            start(pos, pos_to),
            start(w_past, w_in.at[pl.ds(0, width)]),
            start(w_now, w_in.at[pl.ds(width, width)]),
            start(feat, x_turned.at[pl.ds(2 * width, cond)]),
            start(w_cond, w_cond_to),
            start(b_conv, b_conv_to),
        ],
        [],
        [start(valid, valid_to), start(w_res, w_res_to), start(w_skip, w_skip_to)],
    ]
    cotangents = [[tile(0, gout, gout_to), tile(0, gskip, gskip_to)]]
    for i in range(1, rows_all // ROWS):
        signals.append([tile(i, sig, sig_to)])
        cotangents.append([tile(i, gout, gout_to), tile(i, gskip, gskip_to)])
    last = [start(b_res, b_res_to), start(b_skip, b_skip_to)]

    def wait(copies):
        for copy in copies:
            copy.wait()
        copies.clear()

    def prepare(rows):
        i = rows.start // ROWS
        wait(signals[i])
        wait(needs[0])
        whole = rows if i else slice(0, rows.stop)
        before = slice(rows.start - DILATION_STEP, rows.stop - DILATION_STEP)
        tap = tap_of(lines_of(pos_to, rows)).astype(F32)
        past[rows, :] = sig_to[before, :] * column(tap).astype(BF16)
        x_turned[width : 2 * width, whole] = sig_to[whole, :].T
        x_turned[:width, rows] = x_turned[width : 2 * width, before] * row(tap).astype(BF16)

    def arrive(rows, k):
        wait(needs[k])
        if k == 2:
            wait(cotangents[rows.start // ROWS])

    x_turned[2 * width + cond :, :] = jnp.ones((x_turned.shape[0] - 2 * width - cond, rows_all), BF16)
    forward_tiles(
        0, tiles_of(DILATION_STEP, rows_all), prepare, arrive, valid_to, past, sig_to, x_turned, gout_to, gskip_to,
        (w_in, w_cond_to, b_conv_to, w_res_to, w_skip_to), (gated_rest, kept_rest, dpre_rest), DILATION_STEP,
    )
    wait(last)


def rest_shapes(rest, part):
    return [jax.ShapeDtypeStruct(shape, BF16) for shape in ((rest, part), (part, rest), (rest, 2 * part))]


def load(*arrays):
    sources = [in_hbm(x) for x in arrays]
    feat, w_cond, w_res, w_skip, w_past, w_now, sig, gout, gskip = arrays[5:]
    rows, width = sig.shape
    hidden = w_res.shape[0]
    shapes = [jax.ShapeDtypeStruct(x.shape, x.dtype) for x in arrays[:5] + (w_cond, w_res, w_skip)] + [
        jax.ShapeDtypeStruct(shape, BF16)
        for shape in (
            (2 * width, 2 * hidden), sig.shape, sig.shape, (2 * width + feat.shape[0] + ONES, rows), gout.shape, gskip.shape,
        )
    ]
    shapes += rest_shapes(rows - DILATION_STEP, hidden // HALVES)
    return call(
        load_body,
        "load",
        [ANYWHERE] * len(sources),
        [VMEM] * len(shapes),
        shapes,
        scratch=[pltpu.SemaphoreType.DMA((11 + 3 * (rows // ROWS),))],
    )(*sources)


def side_by_side(dpre_0, dpre_1):
    part = dpre_0.shape[1] // 2
    return beside(dpre_0[:, :part], dpre_1[:, :part], dpre_0[:, part:], dpre_1[:, part:])


def head_rows(half, halo, pos, valid, sig, x_turned, gout, gskip, weights, outs):
    w_in, w_cond, b_conv, w_res, w_skip = weights
    rows = slice(0, DILATION_STEP)
    width = halo.shape[1]
    feats = x_turned[2 * width : 2 * width + w_cond.shape[0], rows]
    past = halo[...] * column(tap_of(lines_of(pos, rows)).astype(F32)).astype(BF16)
    made = [gate_product(half, k, rows, past, sig, feats, w_in, w_cond, b_conv) for k in range(2)]
    made.append(back_product(half, rows, gout, gskip, w_res, w_skip))
    for ref, value in zip(outs, finish(*made, lines_of(valid, rows))):
        ref[...] = value


def head_body(halo, pos, valid, sig, x_turned, gout, gskip, w_in, w_cond, b_conv, w_res, w_skip, past_out, *outs):
    tap = tap_of(lines_of(pos, slice(0, DILATION_STEP))).astype(F32)
    past_out[...] = halo[...].T * row(tap).astype(BF16)
    head_rows(0, halo, pos, valid, sig, x_turned, gout, gskip, (w_in, w_cond, b_conv, w_res, w_skip), outs)


def head(halo, *args):
    width = halo.shape[1]
    part = args[-1].shape[0] // HALVES
    past, *parts = call(
        head_body,
        "head",
        [VMEM] * (1 + len(args)),
        [VMEM] * 4,
        [jax.ShapeDtypeStruct((width, DILATION_STEP), BF16)] + rest_shapes(DILATION_STEP, part),
    )(halo, *args)
    return past, parts


def early_body(token, pos, dpre_0, dpre_1, w_in, early):
    tap = column(tap_of(lines_of(pos, slice(0, DILATION_STEP))))
    early[...] = (tap * against(side_by_side(dpre_0[...], dpre_1[...]), w_in[: early.shape[1], :])).astype(BF16)


def early_rows(token, pos, dpre_0, dpre_1, w_in):
    return call(
        early_body,
        "early",
        [ANYWHERE] + [VMEM] * 4,
        VMEM,
        jax.ShapeDtypeStruct((DILATION_STEP, w_in.shape[0] // 2), BF16),
    )(token, pos, dpre_0, dpre_1, w_in)


def most_body(token, valid, past, sig, x_turned, gout, gskip, w_in, w_cond, b_conv, w_res, w_skip, *outs):
    forward_tiles(
        1, tiles_of(DILATION_STEP, split_rows(sig.shape[0])), None, None, valid, past, sig, x_turned, gout, gskip,
        (w_in, w_cond, b_conv, w_res, w_skip), outs, DILATION_STEP,
    )


def forward_most(token, *args):
    part = args[-1].shape[0] // HALVES
    return call(
        most_body,
        "forward_1",
        [ANYWHERE] + [VMEM] * len(args),
        [VMEM] * 3,
        rest_shapes(split_rows(args[2].shape[0]) - DILATION_STEP, part),
    )(token, *args)


def ends_body(token, halo, pos, valid, past, sig, x_turned, gout, gskip, w_in, w_cond, b_conv, w_res, w_skip, *outs):
    weights = (w_in, w_cond, b_conv, w_res, w_skip)
    rows = sig.shape[0]
    head_rows(1, halo, pos, valid, sig, x_turned, gout, gskip, weights, outs[:3])
    forward_tiles(
        1, tiles_of(split_rows(rows), rows), None, None, valid, past, sig, x_turned, gout, gskip, weights, outs[3:],
        split_rows(rows),
    )


def forward_ends(token, *args):
    part = args[-1].shape[0] // HALVES
    rows = args[4].shape[0]
    parts = call(
        ends_body,
        "ends_1",
        [ANYWHERE] + [VMEM] * len(args),
        [VMEM] * 6,
        rest_shapes(DILATION_STEP, part) + rest_shapes(rows - split_rows(rows), part),
    )(token, *args)
    return parts[:3], parts[3:]


def own_place():
    return [lax.axis_index(name) for name in ("core", "far", "near")]


def turned(index, count):
    bits = (count - 1).bit_length()
    result = 0
    for bit in range(bits):
        result = result | (((index >> bit) & 1) << (bits - 1 - bit))
    return result


def gradients_body(far, block, half, own, count, token, valid, x_turned, gout, gskip, past_head, *refs):
    kepts, dpres, (out, acc) = refs[:count], refs[count : 2 * count], refs[2 * count :]
    width = past_head.shape[0]
    part = kepts[0].shape[0]
    ends, rows = x_turned.shape
    size = far * block
    core, z, xy = own_place()
    which = core if own else 1 - core

    def product(left_of, rights):
        total, at = None, 0
        for k, right in enumerate(rights):
            here = slice(at, at + right.shape[0])
            made = dot(left_of(here, k), right[...])
            total = made if at == 0 else total + made
            at = here.stop
        return total

    def region(k):
        low, high = k * size, min((k + 1) * size, ends)

        def turned_rows(here, piece):
            if piece == 0 and low < width:
                return below(past_head[low : min(high, width), :], x_turned[width : max(high, width), here])
            return x_turned[low:high, here]

        acc[: high - low, :] = product(turned_rows, dpres)
        at = high - low
        if high == ends:
            mask = jnp.broadcast_to(row(lines_of(valid, slice(0, rows)).astype(F32)).astype(BF16), (ONES, rows))

            def kept_rows(here, piece):
                return below(kepts[piece][...], mask[:, here])

            for i, ref in enumerate((gout, gskip)):
                cuts = [0]
                for kept in kepts:
                    cuts.append(cuts[-1] + kept.shape[1])
                made = product(kept_rows, [ref.at[pl.ds(a, b - a)] for a, b in zip(cuts, cuts[1:])])
                acc[at : at + part, :] = made[:part]
                at += part
                if i == half:
                    acc[high - low + 2 * part : high - low + 2 * part + ONES, :] = made[part:]
            at += ONES
            acc[at:, :] = jnp.zeros((size - at, acc.shape[1]), F32)
        for r in range(far):
            for c in range(NEAR):
                value = acc[r * block : (r + 1) * block, c * LANES : (c + 1) * LANES]
                out[c ^ xy, turned(r ^ z, far)] = value.astype(out.dtype)

    for k in range(2):
        pl.when(which == k)(functools.partial(region, k))


def gradients(half, own, token, far, block, valid, x_turned, gout, gskip, past_head, pieces):
    packed = (NEAR, far, block, LANES)
    wide = pieces[0][2].shape[1]
    count = len(pieces)
    return call(
        functools.partial(gradients_body, far, block, half, own, count),
        ("mine" if own else "theirs") + f"_{half}",
        [ANYWHERE] + [VMEM] * (5 + 2 * count),
        VMEM,
        jax.ShapeDtypeStruct(packed, F32 if own else BF16),
        scratch=[pltpu.VMEM((far * block, wide), F32)],
    )(token, valid, x_turned, gout, gskip, past_head, *(p[1] for p in pieces), *(p[2] for p in pieces))


def outputs_body(counts, token, valid, sig, w_res, w_skip, b_res, b_skip, *refs):
    first, second = refs[: counts[0]], refs[counts[0] : sum(counts)]
    out, skip, mark, rooms, sems = refs[sum(counts) :]
    copies = []
    for i in range(sig.shape[0] // ROWS):
        rows = slice(i * ROWS, (i + 1) * ROWS)
        mask = column(lines_of(valid, rows))
        gated = beside(picked(first, rows), picked(second, rows))
        branch = dot(gated, w_res[...]) + b_res[...]
        rooms[i, 0] = (sig[rows, :].astype(F32) + mask * branch).astype(BF16)
        side = dot(gated, w_skip[...]) + b_skip[...]
        rooms[i, 1] = (mask * side).astype(BF16)
        for k, ref in enumerate((out, skip)):
            copies.append(pltpu.make_async_copy(rooms.at[i, k], ref.at[pl.ds(i * ROWS, ROWS)], sems.at[i, k]))
            copies[-1].start()
    mark[...] = jnp.zeros_like(mark)
    for copy in copies:
        copy.wait()


def outputs(token, valid, sig, gated_0, gated_1, w_res, w_skip, b_res, b_skip):
    rows, width = sig.shape
    counts = (len(gated_0), len(gated_1))
    return call(
        functools.partial(outputs_body, counts),
        "outputs",
        [ANYWHERE] + [VMEM] * (6 + sum(counts)),
        [ANYWHERE, ANYWHERE, VMEM],
        [
            jax.ShapeDtypeStruct((rows, width), BF16),
            jax.ShapeDtypeStruct((rows, w_skip.shape[1]), BF16),
            MARK,
        ],
        scratch=[
            pltpu.VMEM((rows // ROWS, 2, ROWS, width), BF16),
            pltpu.SemaphoreType.DMA((rows // ROWS, 2)),
        ],
    )(token, valid, sig, w_res, w_skip, b_res, b_skip, *gated_0, *gated_1)


def inputs_body(steps, counts, token, received, gout, pos, w_in, w_cond, *refs):
    first, second = refs[: counts[0]], refs[counts[0] : sum(counts)]
    gsig, gfeat, mark, room, room_feat, sems = refs[-6:]
    rows, width = gout.shape
    copies = []
    wide = 2 * LANES

    def copy(source, target):
        copies.append(pltpu.make_async_copy(source, target, sems.at[len(copies)]))
        copies[-1].start()

    for i, step in enumerate(steps):
        begin = step * ROWS
        here = slice(begin, begin + ROWS)
        after = slice(begin + DILATION_STEP, min(begin + DILATION_STEP + ROWS, rows))
        now = side_by_side(picked(first, here), picked(second, here))
        later = side_by_side(picked(first, after), picked(second, after))
        tap = column(tap_of(lines_of(pos, after)))
        room_feat[i] = against(w_cond[...], now)
        copy(room_feat.at[i], gfeat.at[:, pl.ds(begin, ROWS)])
        for k in range(width // wide):
            some = slice(k * wide, (k + 1) * wide)
            tail = tap * against(later, w_in[some, :])
            if tail.shape[0] < ROWS:
                tail = below(tail, received[:, some].astype(F32))
            room[i, k] = gout[here, some].astype(F32) + against(now, w_in[width + k * wide : width + (k + 1) * wide, :]) + tail
            copy(room.at[i, k], gsig.at[pl.ds(begin, ROWS), pl.ds(k * wide, wide)])
    mark[...] = jnp.zeros_like(mark)
    for one in copies:
        one.wait()


def inputs(steps, token, received, gout, pos, dpre_0, dpre_1, w_in, w_cond, before):
    rows, width = gout.shape
    cond = w_cond.shape[0]
    count = width // (2 * LANES)
    counts = (len(dpre_0), len(dpre_1))
    operands = 6 + sum(counts)
    return call(
        functools.partial(inputs_body, steps, counts),
        f"inputs_{steps[0]}",
        [ANYWHERE] + [VMEM] * (operands - 1) + [ANYWHERE] * len(before),
        [ANYWHERE, ANYWHERE, VMEM],
        [
            jax.ShapeDtypeStruct((rows, width), F32),
            jax.ShapeDtypeStruct((cond, rows), F32),
            MARK,
        ],
        scratch=[
            pltpu.VMEM((len(steps), count, ROWS, 2 * LANES), F32),
            pltpu.VMEM((len(steps), cond, ROWS), F32),
            pltpu.SemaphoreType.DMA((len(steps) * (count + 1),)),
        ],
        aliases={operands + k: k for k in range(len(before))},
    )(token, received, gout, pos, w_in, w_cond, *dpre_0, *dpre_1, *before)


SHARES = ((0, 3), (1, 2))


def unpack_body(far, block, token, *refs):
    blocks, arrays, (mark, room) = refs[: 2 * len(SHARES)], refs[-9:-2], refs[-2:]
    mine, theirs = blocks[: len(SHARES)], blocks[len(SHARES) :]
    mark[...] = jnp.zeros_like(mark)
    core, z, xy = own_place()

    @pl.when(pl.program_id(0) == 0)
    def _():
        for k, parts in ((core, mine), (1 - core, theirs)):
            for share, ref in zip(SHARES, parts):
                for i, c in enumerate(share):
                    for r in range(far):
                        rows = pl.ds(pl.multiple_of((k * far + (r ^ z)) * block, 16), block)
                        room[c ^ xy, rows, :] = ref[i, turned(r, far)]

    for j in range(NEAR // 2):
        c = pl.program_id(0) * (NEAR // 2) + j
        here = pl.ds(j * LANES, LANES)
        top = 0
        for ref in arrays:
            count = ref.shape[0]
            size = max(count, ONES)
            ref[:, here] = room[c, top : top + size, :].astype(F32)[:count]
            top += size


def unpack(half, token, far, block, mine, theirs, width, cond, hidden, skip_width, before):
    part = hidden // HALVES
    gates = 2 * hidden
    own = (width, skip_width)[half]

    def wide(size):
        return pl.BlockSpec((size, part), lambda s: (0, HALVES * s + half))

    def tall(size):
        return pl.BlockSpec((part, size // 2), lambda s: (half, s))

    specs = [wide(width), wide(width), wide(cond), wide(1), tall(width), tall(skip_width), pl.BlockSpec((1, own // 2), lambda s: (0, s))]
    shapes = [(width, gates), (width, gates), (cond, gates), (1, gates), (hidden, width), (hidden, skip_width), (1, own)]
    blocks = [pl.BlockSpec(x.shape, lambda s: (0,) * 4) for x in (*mine, *theirs)]
    return call(
        functools.partial(unpack_body, far, block),
        f"unpack_{half}",
        [ANYWHERE, *blocks] + [ANYWHERE] * len(before),
        specs + [pl.BlockSpec(MARK.shape, lambda s: (0, 0))],
        [jax.ShapeDtypeStruct(shape, F32) for shape in shapes] + [MARK],
        scratch=[pltpu.VMEM((NEAR, 2 * far * block, LANES), BF16)],
        aliases={1 + len(blocks) + k: k for k in range(len(before))},
        grid=(2,),
    )(token, *mine, *theirs, *before)


def swapped(x, axis, k):
    return lax.ppermute(x, axis, [(i, i ^ k) for i in range(lax.axis_size(axis))])


def exchanged(blocks):
    return [swapped(block, "near", k + 1) for k, block in enumerate(blocks)]


def add_body(sizes, token, *refs):
    count = len(sizes)
    kept, got, outs = refs[0], refs[1:-count], refs[-count:]
    at = 0
    for out, size in zip(outs, sizes):
        for k in range(size):
            total = kept[at + k].astype(F32)
            for ref in got:
                total = total + ref[at + k].astype(F32)
            out[k] = total.astype(out.dtype)
        at += size


def added(name, token, kept, got, outs):
    sizes = [size for size, _ in outs]
    result = call(
        functools.partial(add_body, sizes),
        name,
        [ANYWHERE] + [VMEM] * (1 + len(got)),
        [VMEM] * len(outs),
        [jax.ShapeDtypeStruct((size, *kept.shape[1:]), dtype) for size, dtype in outs],
    )(token, kept, *got)
    return result


def mirror_body(token, mine, got, out):
    count = mine.shape[0]
    for k in range(count):
        out[k] = (mine[k].astype(F32) + got[count - 1 - k].astype(F32)).astype(out.dtype)


def mirrored(name, token, mine, got):
    return call(
        mirror_body,
        name,
        [ANYWHERE, VMEM, VMEM],
        VMEM,
        jax.ShapeDtypeStruct(mine.shape, BF16),
    )(token, mine, got)


def join_body(token, *refs):
    out = refs[-1]
    at = 0
    for ref in refs[:-1]:
        out[at : at + ref.shape[0]] = ref[...]
        at += ref.shape[0]


def joined(name, token, parts):
    count = sum(part.shape[0] for part in parts)
    return call(
        join_body,
        name,
        [ANYWHERE] + [VMEM] * len(parts),
        VMEM,
        jax.ShapeDtypeStruct((count, *parts[0].shape[1:]), BF16),
    )(token, *parts)


def over_outer(total):
    for bit in range((lax.axis_size("outer") - 1).bit_length()):
        total = (total.astype(F32) + swapped(total, "outer", 1 << bit).astype(F32)).astype(BF16)
    return total


def passed_along(x, by):
    peers = lax.axis_size(AXES)
    pairs = [(i, i + by) for i in range(peers) if 0 <= i + by < peers]
    return lax.ppermute(x, AXES, pairs)


def in_hbm(x):
    return pltpu.with_memory_space_constraint(x, pltpu.HBM)


def body(
    signal,
    features,
    position,
    valid,
    w_past,
    w_now,
    b_conv,
    w_cond,
    w_res,
    b_res,
    w_skip,
    b_skip,
    grad_out,
    grad_skip,
):
    rows, width = signal.shape
    features = features.T
    cond = features.shape[0]
    hidden = w_res.shape[0]
    skip_width = w_skip.shape[1]
    far = lax.axis_size("far")
    far_bits = (far - 1).bit_length()
    used = 2 * width + cond + ONES + 2 * (hidden // HALVES) + ONES
    block = -(-used // (2 * far * 16)) * 16
    lines = (rows // LANES, LANES)
    pos, val = position.reshape(lines), valid.reshape(lines)
    b_conv, b_res, b_skip = (b.reshape(1, -1) for b in (b_conv, b_res, b_skip))

    def core_sum(half, token, theirs, mine):
        kept, *sent = added(
            f"core_sum_{half}", token, mine, [swapped(theirs, "core", 1)], [(1, F32)] + [(1, BF16)] * (NEAR - 1)
        )
        return kept[0], exchanged([x[0] for x in sent])

    def near_sum(half, token, kept, got):
        kept, sent = added(f"near_sum_{half}", token, kept, got, [(far // 2, F32), (far // 2, BF16)])
        return kept, swapped(sent, "far", 1)

    def far_sum(half, token, kept, got):
        for bit in range(1, far_bits - 1):
            size = kept.shape[0] // 2
            kept, sent = added(f"far_sum_{half}_{bit}", token, kept, [got], [(size, F32), (size, BF16)])
            got = swapped(sent, "far", 1 << bit)
        (mine,) = added(f"far_sum_{half}", token, kept, [got], [(kept.shape[0], BF16)])
        return mine, swapped(mine, "far", 1 << (far_bits - 1))

    def far_end(half, token, mine, got):
        total = over_outer(mirrored(f"far_end_{half}", token, mine, got))
        return total, swapped(total, "far", 1 << (far_bits - 2))

    def far_join(half, token, mine, got):
        total = joined(f"far_join_{half}", token, [mine, got])
        for bit in reversed(range(far_bits - 2)):
            total = joined(f"far_join_{half}_{bit}", token, [total, swapped(total, "far", 1 << bit)])
        return total, exchanged([total] * (NEAR - 1))

    def near_join(half, k, token, mine, got):
        blocks = [mine, *got]
        total = joined(f"near_join_{half}_{k}", token, [blocks[c][None] for c in SHARES[k]])
        return total, swapped(total, "core", 1)

    def input_gradients(steps, token, before):
        last = (steps[-1] + 1) * ROWS == rows
        return inputs(steps, token, received if last else head_0[0], grad_out, pos, dpre_0, dpre_1, w_in, w_cond, before)

    halo = passed_along(signal[rows - DILATION_STEP :], 1)
    val, pos, b_conv, b_res, b_skip, w_cond, w_res, w_skip, w_in, past, signal, x_turned, grad_out, grad_skip, *rest_0 = load(
        val, pos, b_conv, b_res, b_skip, features, w_cond, w_res, w_skip, w_past, w_now, signal, grad_out, grad_skip
    )
    common = (signal, x_turned, grad_out, grad_skip, w_in, w_cond, b_conv, w_res, w_skip)
    past_head, head_0 = head(halo, pos, val, *common)
    made_0 = (head_0, rest_0)
    fixed = (far, block, val, x_turned, grad_out, grad_skip, past_head)
    theirs_0 = gradients(0, False, past_head, *fixed, made_0)
    mine_0 = gradients(0, True, theirs_0, *fixed, made_0)
    most_1 = forward_most(mine_0, val, past, *common)
    kept_0, got_0 = core_sum(0, most_1[0], theirs_0, mine_0)
    head_1, last_1 = forward_ends(kept_0, halo, pos, val, past, *common)
    made_1 = (head_1, most_1, last_1)
    dpre_0, dpre_1 = ([p[2] for p in made] for made in (made_0, made_1))
    theirs_1 = gradients(1, False, kept_0, *fixed, made_1)
    mine_1 = gradients(1, True, theirs_1, *fixed, made_1)
    kept_0, got_0 = near_sum(0, mine_1, kept_0, got_0)
    kept_1, got_1 = core_sum(1, kept_0, theirs_1, mine_1)
    ends_0, got_0 = far_sum(0, kept_1, kept_0, got_0)
    *grads, mark = input_gradients((0, 1), ends_0, [])
    ends_0, got_0 = far_end(0, mark, ends_0, got_0)
    kept_1, got_1 = near_sum(1, ends_0, kept_1, got_1)
    ends_0, got_0 = far_join(0, kept_1, ends_0, got_0)
    ends_1, got_1 = far_sum(1, ends_0, kept_1, got_1)
    output, skip_out, mark = outputs(
        ends_1, val, signal, [p[0] for p in made_0], [p[0] for p in made_1], w_res, w_skip, b_res, b_skip
    )
    ends_1, got_1 = far_end(1, mark, ends_1, got_1)
    early = early_rows(ends_1, pos, head_0[2], head_1[2], w_in)
    received = passed_along(early, -1)
    first = near_join(0, 0, early, ends_0, got_0)
    second = near_join(0, 1, first[0], ends_0, got_0)
    pairs_0 = [first, second]
    ends_1, got_1 = far_join(1, second[0], ends_1, got_1)
    *grads, mark = input_gradients((2, 3), ends_1, grads)
    first = near_join(1, 0, mark, ends_1, got_1)
    second = near_join(1, 1, first[0], ends_1, got_1)
    pairs_1 = [first, second]
    sizes = (width, cond, hidden, skip_width)
    *done, own_0, mark = unpack(0, first[1], far, block, *zip(*pairs_0), *sizes, [])
    *done, own_1, _ = unpack(1, mark, far, block, *zip(*pairs_1), *sizes, done)
    g_past, g_now, g_cond, g_bias, g_res, g_skip = done
    grad_signal, grad_features = grads
    return (
        output,
        skip_out,
        grad_signal,
        grad_features.T,
        g_past,
        g_now,
        g_bias.reshape(-1),
        g_cond,
        g_res,
        own_0.reshape(-1),
        g_skip,
        own_1.reshape(-1),
    )


def solution(mesh):
    row, col = mesh.shape["row"], mesh.shape["col"]
    fine = Mesh(mesh.devices.reshape(row // 2, 2, col // NEAR, NEAR), AXES)
    rows = P(AXES, None)
    line = P(AXES)
    return jax.shard_map(
        body,
        mesh=fine,
        in_specs=(rows, rows, line, line) + (P(),) * 8 + (rows, rows),
        out_specs=(rows,) * 4 + (P(),) * 8,
        check_vma=False,
    )
```

```python
import functools

import jax
import jax.numpy as jnp
from jax import lax
from jax.experimental import pallas as pl
from jax.experimental.pallas import tpu as pltpu
from jax.sharding import Mesh
from jax.sharding import PartitionSpec as P

DILATION_STEP = 256
AXES = ("outer", "core", "far", "near")
HALVES = 2
NEAR = 4
LANES = 128
ROWS = 512
ONES = 16
F32 = jnp.float32
BF16 = jnp.bfloat16
MEGA = 1 << 20
COSTS = {
    "load": 8, "head": 2, "near_sum_0": 7, "mine_1": 2,
    "far_sum_0": 8, "near_sum_1": 4, "near_join_0_1": 2, "near_join_1_1": 4, "far_join_0": 4,
}
FLOPS = 10**9


def dot(left, right):
    return jnp.dot(left, right, preferred_element_type=F32)


def across(left, right):
    return lax.dot_general(left, right, (((0,), (0,)), ((), ())), preferred_element_type=F32)


def against(left, weight):
    return lax.dot_general(left, weight, (((1,), (1,)), ((), ())), preferred_element_type=F32)


def column(lines):
    turned = lines.astype(F32).T
    return jnp.concatenate([turned[:, k : k + 1] for k in range(lines.shape[0])], axis=0)


def row(lines):
    return jnp.concatenate([lines[k : k + 1] for k in range(lines.shape[0])], axis=1)


def tap_of(lines):
    return jnp.where(lines >= DILATION_STEP, 1, 0)


def lines_of(ref, rows):
    return ref[rows.start // LANES : rows.stop // LANES, :]


def picked(pieces, rows):
    found, at = [], 0
    for ref in pieces:
        low, high = max(rows.start, at), min(rows.stop, at + ref.shape[0])
        if low < high:
            found.append(ref[low - at : high - at, :])
        at += ref.shape[0]
    return found[0] if len(found) == 1 else jnp.concatenate(found, axis=0)


def call(kernel, name, in_specs, out_specs, out_shape, scratch=(), aliases=None, grid=(), vmem=24):
    return pl.pallas_call(
        kernel,
        grid=grid,
        in_specs=in_specs,
        out_specs=out_specs,
        out_shape=out_shape,
        scratch_shapes=list(scratch),
        input_output_aliases=aliases or {},
        cost_estimate=pl.CostEstimate(
            flops=1 + int(FLOPS * COSTS.get(name, COSTS.get(name.split("_")[0], 0))), bytes_accessed=1, transcendentals=0
        ),
        name=name,
        compiler_params=pltpu.CompilerParams(vmem_limit_bytes=vmem * MEGA),
    )


VMEM = pl.BlockSpec(memory_space=pltpu.VMEM)
ANYWHERE = pl.BlockSpec(memory_space=pl.ANY)
MARK = jax.ShapeDtypeStruct((8, LANES), F32)


def beside(*parts):
    return jnp.concatenate(parts, axis=1)


def below(*parts):
    return jnp.concatenate(parts, axis=0)


def gate_product(half, k, rows, past, sig, feats, w_in, w_cond, b_conv):
    width = sig.shape[1]
    part = w_in.shape[1] // 2
    here = slice(k * part, (k + 1) * part)
    there = slice((k * HALVES + half) * part, (k * HALVES + half + 1) * part)
    own = dot(past, w_in[:width, here]) + dot(sig[rows, :], w_in[width:, here])
    return own + across(feats, w_cond[:, there]) + b_conv[:, there]


def back_product(rows, gout, gskip, w_res, w_skip):
    return against(gout[rows, :], w_res[...]) + against(gskip[rows, :], w_skip[...])


def weight_copies(half, w_past, w_now, w_res, w_skip, w_in_to, w_res_to, w_skip_to):
    width = w_past.shape[0]
    part = w_res_to.shape[0]
    pairs = []
    for k in range(2):
        here = pl.ds((k * HALVES + half) * part, part)
        for i, ref in enumerate((w_past, w_now)):
            pairs.append((ref.at[:, here], w_in_to.at[pl.ds(i * width, width), pl.ds(k * part, part)]))
    rows = pl.ds(half * part, part)
    return pairs + [(w_res.at[rows], w_res_to), (w_skip.at[rows], w_skip_to)]


def half_weights(w_past, w_res, w_skip):
    part = w_res.shape[0] // HALVES
    shapes = ((2 * w_past.shape[0], 2 * part), (part, w_res.shape[1]), (part, w_skip.shape[1]))
    return [jax.ShapeDtypeStruct(shape, BF16) for shape in shapes]


def finish(pre_a, pre_s, dgated, valid_lines):
    act = jnp.tanh(pre_a)
    gate = 0.5 + 0.5 * jnp.tanh(0.5 * pre_s)
    slope = (column(valid_lines) * dgated) * gate
    dpre = beside(slope * (1.0 - act * act), slope * act * (1.0 - gate)).astype(BF16)
    gated = (act * gate).astype(BF16)
    return gated, gated.T * row(valid_lines.astype(BF16)), dpre


def forward_tiles(half, tiles, prepare, arrive, valid, past, sig, x_turned, gout, gskip, weights, outs, base):
    w_in, w_cond, b_conv, w_res, w_skip = weights
    gated_out, kept_out, dpre_out = outs
    cond = w_cond.shape[0]
    width = sig.shape[1]

    def product(rows, k):
        if arrive:
            arrive(rows, k)
        if k == 2:
            return back_product(rows, gout, gskip, w_res, w_skip)
        feats = x_turned[2 * width : 2 * width + cond, rows]
        return gate_product(half, k, rows, past[rows, :], sig, feats, w_in, w_cond, b_conv)

    def done(rows, made):
        there = slice(rows.start - base, rows.stop - base)
        gated_out[there, :], kept_out[:, there], dpre_out[there, :] = finish(*made, lines_of(valid, rows))

    ahead = None
    for rows in tiles:
        if prepare:
            prepare(rows)
        made = [product(rows, k) for k in range(3)]
        if ahead:
            done(*ahead)
        ahead = (rows, made)
    done(*ahead)


def tiles_of(start, stop):
    return [slice(a, a + DILATION_STEP) for a in range(start, stop, DILATION_STEP)]


def split_rows(rows):
    return 3 * DILATION_STEP


def load_body(
    valid, pos, b_conv, feat, w_cond, w_res, w_skip, w_past, w_now, sig, gout, gskip,
    valid_to, pos_to, b_conv_to, w_cond_to, w_in, w_res_to, w_skip_to, past, sig_to, x_turned,
    gout_to, gskip_to, gated_rest, kept_rest, dpre_rest, sems,
):
    rows_all, width = sig.shape
    cond = feat.shape[0]
    count = 0

    def start(source, target):
        nonlocal count
        copy = pltpu.make_async_copy(source, target, sems.at[count])
        copy.start()
        count += 1
        return copy

    def tile(i, source, target):
        rows = pl.ds(i * ROWS, ROWS)
        return start(source.at[rows], target.at[rows])

    weights = weight_copies(0, w_past, w_now, w_res, w_skip, w_in, w_res_to, w_skip_to)
    signals = [[tile(0, sig, sig_to)]]
    needs = [
        [
            start(pos, pos_to),
            *(start(*pair) for pair in weights[:2]),
            start(feat, x_turned.at[pl.ds(2 * width, cond)]),
            start(w_cond, w_cond_to),
            start(b_conv, b_conv_to),
        ],
        [start(*pair) for pair in weights[2:4]],
        [start(valid, valid_to), *(start(*pair) for pair in weights[4:])],
    ]
    cotangents = [[tile(0, gout, gout_to), tile(0, gskip, gskip_to)]]
    for i in range(1, rows_all // ROWS):
        signals.append([tile(i, sig, sig_to)])
        cotangents.append([tile(i, gout, gout_to), tile(i, gskip, gskip_to)])

    def wait(copies):
        for copy in copies:
            copy.wait()
        copies.clear()

    def prepare(rows):
        i = rows.start // ROWS
        wait(signals[i])
        wait(needs[0])
        whole = rows if i else slice(0, rows.stop)
        before = slice(rows.start - DILATION_STEP, rows.stop - DILATION_STEP)
        tap = tap_of(lines_of(pos_to, rows)).astype(F32)
        past[rows, :] = sig_to[before, :] * column(tap).astype(BF16)
        x_turned[width : 2 * width, whole] = sig_to[whole, :].T
        x_turned[:width, rows] = x_turned[width : 2 * width, before] * row(tap).astype(BF16)

    def arrive(rows, k):
        wait(needs[k])
        if k == 2:
            wait(cotangents[rows.start // ROWS])

    x_turned[2 * width + cond :, :] = jnp.ones((x_turned.shape[0] - 2 * width - cond, rows_all), BF16)
    forward_tiles(
        0, tiles_of(DILATION_STEP, rows_all), prepare, arrive, valid_to, past, sig_to, x_turned, gout_to, gskip_to,
        (w_in, w_cond_to, b_conv_to, w_res_to, w_skip_to), (gated_rest, kept_rest, dpre_rest), DILATION_STEP,
    )


def rest_shapes(rest, part):
    return [jax.ShapeDtypeStruct(shape, BF16) for shape in ((rest, part), (part, rest), (rest, 2 * part))]


def load(*arrays):
    sources = [in_hbm(x) for x in arrays]
    feat, w_cond, w_res, w_skip, w_past, _, sig, gout, gskip = arrays[3:]
    rows, width = sig.shape
    hidden = w_res.shape[0]
    shapes = [jax.ShapeDtypeStruct(x.shape, x.dtype) for x in arrays[:3] + (w_cond,)]
    shapes += half_weights(w_past, w_res, w_skip) + [
        jax.ShapeDtypeStruct(shape, BF16)
        for shape in (
            sig.shape, sig.shape, (2 * width + feat.shape[0] + ONES, rows), gout.shape, gskip.shape,
        )
    ]
    shapes += rest_shapes(rows - DILATION_STEP, hidden // HALVES)
    return call(
        load_body,
        "load",
        [ANYWHERE] * len(sources),
        [VMEM] * len(shapes),
        shapes,
        scratch=[pltpu.SemaphoreType.DMA((11 + 3 * (rows // ROWS),))],
    )(*sources)


def side_by_side(dpre_0, dpre_1):
    part = dpre_0.shape[1] // 2
    return beside(dpre_0[:, :part], dpre_1[:, :part], dpre_0[:, part:], dpre_1[:, part:])


def head_rows(half, halo, pos, valid, sig, x_turned, gout, gskip, weights, outs):
    w_in, w_cond, b_conv, w_res, w_skip = weights
    rows = slice(0, DILATION_STEP)
    width = halo.shape[1]
    feats = x_turned[2 * width : 2 * width + w_cond.shape[0], rows]
    past = halo[...] * column(tap_of(lines_of(pos, rows)).astype(F32)).astype(BF16)
    made = [gate_product(half, k, rows, past, sig, feats, w_in, w_cond, b_conv) for k in range(2)]
    made.append(back_product(rows, gout, gskip, w_res, w_skip))
    for ref, value in zip(outs, finish(*made, lines_of(valid, rows))):
        ref[...] = value


def head_body(halo, pos, valid, sig, x_turned, gout, gskip, w_in, w_cond, b_conv, w_res, w_skip, past_out, *outs):
    tap = tap_of(lines_of(pos, slice(0, DILATION_STEP))).astype(F32)
    past_out[...] = halo[...].T * row(tap).astype(BF16)
    head_rows(0, halo, pos, valid, sig, x_turned, gout, gskip, (w_in, w_cond, b_conv, w_res, w_skip), outs)


def head(halo, *args):
    width = halo.shape[1]
    part = args[-1].shape[0]
    past, *parts = call(
        head_body,
        "head",
        [VMEM] * (1 + len(args)),
        [VMEM] * 4,
        [jax.ShapeDtypeStruct((width, DILATION_STEP), BF16)] + rest_shapes(DILATION_STEP, part),
    )(halo, *args)
    return past, parts


def early_body(token, pos, dpre_0, dpre_1, w_in_0, w_in_1, early):
    tap = column(tap_of(lines_of(pos, slice(0, DILATION_STEP))))
    some = slice(0, early.shape[1])
    early[...] = (tap * (against(dpre_0[...], w_in_0[some, :]) + against(dpre_1[...], w_in_1[some, :]))).astype(BF16)


def early_rows(token, pos, dpre_0, dpre_1, w_in_0, w_in_1):
    return call(
        early_body,
        "early",
        [ANYWHERE] + [VMEM] * 5,
        VMEM,
        jax.ShapeDtypeStruct((DILATION_STEP, w_in_0.shape[0] // 2), BF16),
    )(token, pos, dpre_0, dpre_1, w_in_0, w_in_1)


def most_body(token, valid, past, sig, x_turned, gout, gskip, w_in, w_cond, b_conv, w_res, w_skip, *outs):
    forward_tiles(
        1, tiles_of(DILATION_STEP, split_rows(sig.shape[0])), None, None, valid, past, sig, x_turned, gout, gskip,
        (w_in, w_cond, b_conv, w_res, w_skip), outs, DILATION_STEP,
    )


def forward_most(token, *args):
    part = args[-1].shape[0]
    return call(
        most_body,
        "forward_1",
        [ANYWHERE] + [VMEM] * len(args),
        [VMEM] * 3,
        rest_shapes(split_rows(args[2].shape[0]) - DILATION_STEP, part),
    )(token, *args)


def ends_body(token, halo, pos, valid, past, sig, x_turned, gout, gskip, w_in, w_cond, b_conv, w_res, w_skip, *outs):
    weights = (w_in, w_cond, b_conv, w_res, w_skip)
    rows = sig.shape[0]
    head_rows(1, halo, pos, valid, sig, x_turned, gout, gskip, weights, outs[:3])
    forward_tiles(
        1, tiles_of(split_rows(rows), rows), None, None, valid, past, sig, x_turned, gout, gskip, weights, outs[3:],
        split_rows(rows),
    )


def forward_ends(token, *args):
    part = args[-1].shape[0]
    rows = args[4].shape[0]
    parts = call(
        ends_body,
        "ends_1",
        [ANYWHERE] + [VMEM] * len(args),
        [VMEM] * 6,
        rest_shapes(DILATION_STEP, part) + rest_shapes(rows - split_rows(rows), part),
    )(token, *args)
    return parts[:3], parts[3:]


def own_place():
    return [lax.axis_index(name) for name in ("core", "far", "near")]


def turned(index, count):
    bits = (count - 1).bit_length()
    result = 0
    for bit in range(bits):
        result = result | (((index >> bit) & 1) << (bits - 1 - bit))
    return result


def gradients_body(far, block, half, own, count, extra, token, valid, x_turned, gout, gskip, past_head, *refs):
    kepts, dpres, refs = refs[:count], refs[count : 2 * count], refs[2 * count :]
    sources, (out, *targets) = refs[:extra], refs[extra : len(refs) - 1 - bool(extra)]
    acc = refs[-1 - bool(extra)]
    copies = []
    if extra:
        pairs = weight_copies(1, *sources[:4], *targets[:3]) + list(zip(sources[4:], targets[3:]))
        copies = [pltpu.make_async_copy(*pair, refs[-1].at[k]) for k, pair in enumerate(pairs)]
    for copy in copies:
        copy.start()
    width = past_head.shape[0]
    part = kepts[0].shape[0]
    ends, rows = x_turned.shape
    size = far * block
    core, z, xy = own_place()
    which = core if own else 1 - core

    def product(left_of, rights):
        total, at = None, 0
        for k, right in enumerate(rights):
            here = slice(at, at + right.shape[0])
            made = dot(left_of(here, k), right[...])
            total = made if at == 0 else total + made
            at = here.stop
        return total

    def region(k):
        low, high = k * size, min((k + 1) * size, ends)

        def turned_rows(here, piece):
            if piece == 0 and low < width:
                return below(past_head[low : min(high, width), :], x_turned[width : max(high, width), here])
            return x_turned[low:high, here]

        acc[: high - low, :] = product(turned_rows, dpres)
        at = high - low
        if high == ends:
            mask = jnp.broadcast_to(row(lines_of(valid, slice(0, rows)).astype(F32)).astype(BF16), (ONES, rows))

            def kept_rows(here, piece):
                return below(kepts[piece][...], mask[:, here])

            for i, ref in enumerate((gout, gskip)):
                cuts = [0]
                for kept in kepts:
                    cuts.append(cuts[-1] + kept.shape[1])
                made = product(kept_rows, [ref.at[pl.ds(a, b - a)] for a, b in zip(cuts, cuts[1:])])
                acc[at : at + part, :] = made[:part]
                at += part
                if i == half:
                    acc[high - low + 2 * part : high - low + 2 * part + ONES, :] = made[part:]
            at += ONES
            acc[at:, :] = jnp.zeros((size - at, acc.shape[1]), F32)
        for r in range(far):
            for c in range(NEAR):
                value = acc[r * block : (r + 1) * block, c * LANES : (c + 1) * LANES]
                out[c ^ xy, turned(r ^ z, far)] = value.astype(out.dtype)

    for k in range(2):
        pl.when(which == k)(functools.partial(region, k))
    for copy in copies:
        copy.wait()


def gradients(half, own, token, far, block, valid, x_turned, gout, gskip, past_head, pieces, loads=()):
    packed = (NEAR, far, block, LANES)
    wide = pieces[0][2].shape[1]
    count = len(pieces)
    sources = [in_hbm(x) for x in loads]
    outs = [jax.ShapeDtypeStruct(packed, F32 if own else BF16)]
    scratch = [pltpu.VMEM((far * block, wide), F32)]
    if loads:
        outs += half_weights(loads[0], *loads[2:4]) + [jax.ShapeDtypeStruct(x.shape, x.dtype) for x in loads[4:]]
        scratch.append(pltpu.SemaphoreType.DMA((6 + len(loads[4:]),)))
    return call(
        functools.partial(gradients_body, far, block, half, own, count, len(loads)),
        ("mine" if own else "theirs") + f"_{half}",
        [ANYWHERE] + [VMEM] * (5 + 2 * count) + [ANYWHERE] * len(loads),
        [VMEM] * len(outs),
        outs,
        scratch=scratch,
    )(token, valid, x_turned, gout, gskip, past_head, *(p[1] for p in pieces), *(p[2] for p in pieces), *sources)


def outputs_body(counts, token, valid, sig, w_res_0, w_skip_0, w_res_1, w_skip_1, b_res, b_skip, *refs):
    first, second = refs[: counts[0]], refs[counts[0] : sum(counts)]
    out, skip, mark, rooms, sems = refs[sum(counts) :]
    copies = []
    for i in range(sig.shape[0] // ROWS):
        rows = slice(i * ROWS, (i + 1) * ROWS)
        mask = column(lines_of(valid, rows))
        left, right = picked(first, rows), picked(second, rows)
        branch = dot(left, w_res_0[...]) + dot(right, w_res_1[...]) + b_res[...]
        rooms[i, 0] = (sig[rows, :].astype(F32) + mask * branch).astype(BF16)
        side = dot(left, w_skip_0[...]) + dot(right, w_skip_1[...]) + b_skip[...]
        rooms[i, 1] = (mask * side).astype(BF16)
        for k, ref in enumerate((out, skip)):
            copies.append(pltpu.make_async_copy(rooms.at[i, k], ref.at[pl.ds(i * ROWS, ROWS)], sems.at[i, k]))
            copies[-1].start()
    mark[...] = jnp.zeros_like(mark)
    for copy in copies:
        copy.wait()


def outputs(token, valid, sig, gated_0, gated_1, weights_0, weights_1, b_res, b_skip):
    rows, width = sig.shape
    counts = (len(gated_0), len(gated_1))
    return call(
        functools.partial(outputs_body, counts),
        "outputs",
        [ANYWHERE] + [VMEM] * (8 + sum(counts)),
        [ANYWHERE, ANYWHERE, VMEM],
        [
            jax.ShapeDtypeStruct((rows, width), BF16),
            jax.ShapeDtypeStruct((rows, weights_0[1].shape[1]), BF16),
            MARK,
        ],
        scratch=[
            pltpu.VMEM((rows // ROWS, 2, ROWS, width), BF16),
            pltpu.SemaphoreType.DMA((rows // ROWS, 2)),
        ],
    )(token, valid, sig, *weights_0, *weights_1, b_res, b_skip, *gated_0, *gated_1)


def inputs_body(steps, counts, token, received, gout, pos, w_in_0, w_in_1, w_cond, *refs):
    first, second = refs[: counts[0]], refs[counts[0] : sum(counts)]
    gsig, gfeat, mark, room, room_feat, sems = refs[-6:]
    rows, width = gout.shape
    copies = []
    wide = 2 * LANES

    def copy(source, target):
        copies.append(pltpu.make_async_copy(source, target, sems.at[len(copies)]))
        copies[-1].start()

    for i, step in enumerate(steps):
        begin = step * ROWS
        here = slice(begin, begin + ROWS)
        after = slice(begin + DILATION_STEP, min(begin + DILATION_STEP + ROWS, rows))
        now = [picked(pieces, here) for pieces in (first, second)]
        later = [picked(pieces, after) for pieces in (first, second)]
        tap = column(tap_of(lines_of(pos, after)))
        room_feat[i] = against(w_cond[...], side_by_side(*now))
        copy(room_feat.at[i], gfeat.at[:, pl.ds(begin, ROWS)])
        for k in range(width // wide):
            some = slice(k * wide, (k + 1) * wide)
            tail = tap * (against(later[0], w_in_0[some, :]) + against(later[1], w_in_1[some, :]))
            if tail.shape[0] < ROWS:
                tail = below(tail, received[:, some].astype(F32))
            below_past = slice(width + k * wide, width + (k + 1) * wide)
            own = against(now[0], w_in_0[below_past, :]) + against(now[1], w_in_1[below_past, :])
            room[i, k] = gout[here, some].astype(F32) + own + tail
            copy(room.at[i, k], gsig.at[pl.ds(begin, ROWS), pl.ds(k * wide, wide)])
    mark[...] = jnp.zeros_like(mark)
    for one in copies:
        one.wait()


def inputs(steps, token, received, gout, pos, dpre_0, dpre_1, w_in_0, w_in_1, w_cond, before):
    rows, width = gout.shape
    cond = w_cond.shape[0]
    count = width // (2 * LANES)
    counts = (len(dpre_0), len(dpre_1))
    operands = 7 + sum(counts)
    return call(
        functools.partial(inputs_body, steps, counts),
        f"inputs_{steps[0]}",
        [ANYWHERE] + [VMEM] * (operands - 1) + [ANYWHERE] * len(before),
        [ANYWHERE, ANYWHERE, VMEM],
        [
            jax.ShapeDtypeStruct((rows, width), F32),
            jax.ShapeDtypeStruct((cond, rows), F32),
            MARK,
        ],
        scratch=[
            pltpu.VMEM((len(steps), count, ROWS, 2 * LANES), F32),
            pltpu.VMEM((len(steps), cond, ROWS), F32),
            pltpu.SemaphoreType.DMA((len(steps) * (count + 1),)),
        ],
        aliases={operands + k: k for k in range(len(before))},
    )(token, received, gout, pos, w_in_0, w_in_1, w_cond, *dpre_0, *dpre_1, *before)


SHARES = ((0, 3), (1, 2))


def unpack_body(far, block, token, *refs):
    blocks, arrays, (mark, room) = refs[: 2 * len(SHARES)], refs[-9:-2], refs[-2:]
    mine, theirs = blocks[: len(SHARES)], blocks[len(SHARES) :]
    mark[...] = jnp.zeros_like(mark)
    core, z, xy = own_place()

    @pl.when(pl.program_id(0) == 0)
    def _():
        for k, parts in ((core, mine), (1 - core, theirs)):
            for share, ref in zip(SHARES, parts):
                for i, c in enumerate(share):
                    for r in range(far):
                        rows = pl.ds(pl.multiple_of((k * far + (r ^ z)) * block, 16), block)
                        room[c ^ xy, rows, :] = ref[i, turned(r, far)]

    for j in range(NEAR // 2):
        c = pl.program_id(0) * (NEAR // 2) + j
        here = pl.ds(j * LANES, LANES)
        top = 0
        for ref in arrays:
            count = ref.shape[0]
            size = max(count, ONES)
            ref[:, here] = room[c, top : top + size, :].astype(F32)[:count]
            top += size


def unpack(half, token, far, block, mine, theirs, width, cond, hidden, skip_width, before):
    part = hidden // HALVES
    gates = 2 * hidden
    own = (width, skip_width)[half]

    def wide(size):
        return pl.BlockSpec((size, part), lambda s: (0, HALVES * s + half))

    def tall(size):
        return pl.BlockSpec((part, size // 2), lambda s: (half, s))

    specs = [wide(width), wide(width), wide(cond), wide(1), tall(width), tall(skip_width), pl.BlockSpec((1, own // 2), lambda s: (0, s))]
    shapes = [(width, gates), (width, gates), (cond, gates), (1, gates), (hidden, width), (hidden, skip_width), (1, own)]
    blocks = [pl.BlockSpec(x.shape, lambda s: (0,) * 4) for x in (*mine, *theirs)]
    return call(
        functools.partial(unpack_body, far, block),
        f"unpack_{half}",
        [ANYWHERE, *blocks] + [ANYWHERE] * len(before),
        specs + [pl.BlockSpec(MARK.shape, lambda s: (0, 0))],
        [jax.ShapeDtypeStruct(shape, F32) for shape in shapes] + [MARK],
        scratch=[pltpu.VMEM((NEAR, 2 * far * block, LANES), BF16)],
        aliases={1 + len(blocks) + k: k for k in range(len(before))},
        grid=(2,),
    )(token, *mine, *theirs, *before)


def swapped(x, axis, k):
    return lax.ppermute(x, axis, [(i, i ^ k) for i in range(lax.axis_size(axis))])


def exchanged(blocks):
    return [swapped(block, "near", k + 1) for k, block in enumerate(blocks)]


def add_body(sizes, token, *refs):
    count = len(sizes)
    kept, got, outs = refs[0], refs[1:-count], refs[-count:]
    at = 0
    for out, size in zip(outs, sizes):
        for k in range(size):
            total = kept[at + k].astype(F32)
            for ref in got:
                total = total + ref[at + k].astype(F32)
            out[k] = total.astype(out.dtype)
        at += size


def added(name, token, kept, got, outs):
    sizes = [size for size, _ in outs]
    result = call(
        functools.partial(add_body, sizes),
        name,
        [ANYWHERE] + [VMEM] * (1 + len(got)),
        [VMEM] * len(outs),
        [jax.ShapeDtypeStruct((size, *kept.shape[1:]), dtype) for size, dtype in outs],
    )(token, kept, *got)
    return result


def mirror_body(token, mine, got, out):
    count = mine.shape[0]
    for k in range(count):
        out[k] = (mine[k].astype(F32) + got[count - 1 - k].astype(F32)).astype(out.dtype)


def mirrored(name, token, mine, got):
    return call(
        mirror_body,
        name,
        [ANYWHERE, VMEM, VMEM],
        VMEM,
        jax.ShapeDtypeStruct(mine.shape, BF16),
    )(token, mine, got)


def join_body(token, *refs):
    out = refs[-1]
    at = 0
    for ref in refs[:-1]:
        out[at : at + ref.shape[0]] = ref[...]
        at += ref.shape[0]


def joined(name, token, parts):
    count = sum(part.shape[0] for part in parts)
    return call(
        join_body,
        name,
        [ANYWHERE] + [VMEM] * len(parts),
        VMEM,
        jax.ShapeDtypeStruct((count, *parts[0].shape[1:]), BF16),
    )(token, *parts)


def over_outer(total):
    for bit in range((lax.axis_size("outer") - 1).bit_length()):
        total = (total.astype(F32) + swapped(total, "outer", 1 << bit).astype(F32)).astype(BF16)
    return total


def passed_along(x, by):
    peers = lax.axis_size(AXES)
    pairs = [(i, i + by) for i in range(peers) if 0 <= i + by < peers]
    return lax.ppermute(x, AXES, pairs)


def in_hbm(x):
    return pltpu.with_memory_space_constraint(x, pltpu.HBM)


def body(
    signal,
    features,
    position,
    valid,
    w_past,
    w_now,
    b_conv,
    w_cond,
    w_res,
    b_res,
    w_skip,
    b_skip,
    grad_out,
    grad_skip,
):
    rows, width = signal.shape
    features = features.T
    cond = features.shape[0]
    hidden = w_res.shape[0]
    skip_width = w_skip.shape[1]
    far = lax.axis_size("far")
    far_bits = (far - 1).bit_length()
    used = 2 * width + cond + ONES + 2 * (hidden // HALVES) + ONES
    block = -(-used // (2 * far * 16)) * 16
    lines = (rows // LANES, LANES)
    pos, val = position.reshape(lines), valid.reshape(lines)
    b_conv, b_res, b_skip = (b.reshape(1, -1) for b in (b_conv, b_res, b_skip))

    def core_sum(half, token, theirs, mine):
        kept, *sent = added(
            f"core_sum_{half}", token, mine, [swapped(theirs, "core", 1)], [(1, F32)] + [(1, BF16)] * (NEAR - 1)
        )
        return kept[0], exchanged([x[0] for x in sent])

    def near_sum(half, token, kept, got):
        kept, sent = added(f"near_sum_{half}", token, kept, got, [(far // 2, F32), (far // 2, BF16)])
        return kept, swapped(sent, "far", 1)

    def far_sum(half, token, kept, got):
        for bit in range(1, far_bits - 1):
            size = kept.shape[0] // 2
            kept, sent = added(f"far_sum_{half}_{bit}", token, kept, [got], [(size, F32), (size, BF16)])
            got = swapped(sent, "far", 1 << bit)
        (mine,) = added(f"far_sum_{half}", token, kept, [got], [(kept.shape[0], BF16)])
        return mine, swapped(mine, "far", 1 << (far_bits - 1))

    def far_end(half, token, mine, got):
        total = over_outer(mirrored(f"far_end_{half}", token, mine, got))
        return total, swapped(total, "far", 1 << (far_bits - 2))

    def far_join(half, token, mine, got):
        total = joined(f"far_join_{half}", token, [mine, got])
        for bit in reversed(range(far_bits - 2)):
            total = joined(f"far_join_{half}_{bit}", token, [total, swapped(total, "far", 1 << bit)])
        return total, exchanged([total] * (NEAR - 1))

    def near_join(half, k, token, mine, got):
        blocks = [mine, *got]
        total = joined(f"near_join_{half}_{k}", token, [blocks[c][None] for c in SHARES[k]])
        return total, swapped(total, "core", 1)

    def input_gradients(steps, token, before):
        last = (steps[-1] + 1) * ROWS == rows
        return inputs(steps, token, received if last else head_0[0], grad_out, pos, dpre_0, dpre_1, w_in_0, w_in_1, w_cond, before)

    halo = passed_along(signal[rows - DILATION_STEP :], 1)
    loads = (w_past, w_now, w_res, w_skip, b_res, b_skip)
    val, pos, b_conv, w_cond, w_in_0, *outer_0, past, signal, x_turned, grad_out, grad_skip, a, b, c = load(
        val, pos, b_conv, features, w_cond, w_res, w_skip, w_past, w_now, signal, grad_out, grad_skip
    )
    rest_0 = (a, b, c)
    common = (signal, x_turned, grad_out, grad_skip)
    past_head, head_0 = head(halo, pos, val, *common, w_in_0, w_cond, b_conv, *outer_0)
    made_0 = (head_0, rest_0)
    fixed = (far, block, val, x_turned, grad_out, grad_skip, past_head)
    theirs_0, w_in_1, *outer_1, b_res, b_skip = gradients(0, False, past_head, *fixed, made_0, loads)
    weights_1 = (w_in_1, w_cond, b_conv, *outer_1)
    (mine_0,) = gradients(0, True, theirs_0, *fixed, made_0)
    most_1 = forward_most(mine_0, val, past, *common, *weights_1)
    kept_0, got_0 = core_sum(0, most_1[0], theirs_0, mine_0)
    head_1, last_1 = forward_ends(kept_0, halo, pos, val, past, *common, *weights_1)
    made_1 = (head_1, most_1, last_1)
    dpre_0, dpre_1 = ([p[2] for p in made] for made in (made_0, made_1))
    (theirs_1,) = gradients(1, False, kept_0, *fixed, made_1)
    (mine_1,) = gradients(1, True, theirs_1, *fixed, made_1)
    kept_0, got_0 = near_sum(0, mine_1, kept_0, got_0)
    kept_1, got_1 = core_sum(1, kept_0, theirs_1, mine_1)
    ends_0, got_0 = far_sum(0, kept_1, kept_0, got_0)
    *grads, mark = input_gradients((0, 1), ends_0, [])
    ends_0, got_0 = far_end(0, mark, ends_0, got_0)
    kept_1, got_1 = near_sum(1, ends_0, kept_1, got_1)
    ends_0, got_0 = far_join(0, kept_1, ends_0, got_0)
    ends_1, got_1 = far_sum(1, ends_0, kept_1, got_1)
    output, skip_out, mark = outputs(
        ends_1, val, signal, [p[0] for p in made_0], [p[0] for p in made_1], outer_0, outer_1, b_res, b_skip
    )
    ends_1, got_1 = far_end(1, mark, ends_1, got_1)
    early = early_rows(ends_1, pos, head_0[2], head_1[2], w_in_0, w_in_1)
    received = passed_along(early, -1)
    first = near_join(0, 0, early, ends_0, got_0)
    second = near_join(0, 1, first[0], ends_0, got_0)
    pairs_0 = [first, second]
    ends_1, got_1 = far_join(1, second[0], ends_1, got_1)
    *grads, mark = input_gradients((2, 3), ends_1, grads)
    first = near_join(1, 0, mark, ends_1, got_1)
    second = near_join(1, 1, first[0], ends_1, got_1)
    pairs_1 = [first, second]
    sizes = (width, cond, hidden, skip_width)
    *done, own_0, mark = unpack(0, first[1], far, block, *zip(*pairs_0), *sizes, [])
    *done, own_1, _ = unpack(1, mark, far, block, *zip(*pairs_1), *sizes, done)
    g_past, g_now, g_cond, g_bias, g_res, g_skip = done
    grad_signal, grad_features = grads
    return (
        output,
        skip_out,
        grad_signal,
        grad_features.T,
        g_past,
        g_now,
        g_bias.reshape(-1),
        g_cond,
        g_res,
        own_0.reshape(-1),
        g_skip,
        own_1.reshape(-1),
    )


def solution(mesh):
    row, col = mesh.shape["row"], mesh.shape["col"]
    fine = Mesh(mesh.devices.reshape(row // 2, 2, col // NEAR, NEAR), AXES)
    rows = P(AXES, None)
    line = P(AXES)
    return jax.shard_map(
        body,
        mesh=fine,
        in_specs=(rows, rows, line, line) + (P(),) * 8 + (rows, rows),
        out_specs=(rows,) * 4 + (P(),) * 8,
        check_vma=False,
    )
```

```python
import functools

import jax
import jax.numpy as jnp
from jax import lax
from jax.experimental import pallas as pl
from jax.experimental.pallas import tpu as pltpu
from jax.sharding import Mesh
from jax.sharding import PartitionSpec as P

DILATION_STEP = 256
AXES = ("outer", "core", "far", "near")
HALVES = 2
NEAR = 4
LANES = 128
ROWS = 512
ONES = 16
F32 = jnp.float32
BF16 = jnp.bfloat16
MEGA = 1 << 20
COSTS = {
    "load": 8, "head": 2, "near_sum_0": 7, "mine_1": 2, "near_part_0": 1,
    "far_sum_0": 8, "near_sum_1": 4, "near_join_0_1": 2, "near_join_1_1": 4, "far_join_0": 4,
}
FLOPS = 10**9


def dot(left, right):
    return jnp.dot(left, right, preferred_element_type=F32)


def across(left, right):
    return lax.dot_general(left, right, (((0,), (0,)), ((), ())), preferred_element_type=F32)


def against(left, weight):
    return lax.dot_general(left, weight, (((1,), (1,)), ((), ())), preferred_element_type=F32)


def column(lines):
    turned = lines.astype(F32).T
    return jnp.concatenate([turned[:, k : k + 1] for k in range(lines.shape[0])], axis=0)


def row(lines):
    return jnp.concatenate([lines[k : k + 1] for k in range(lines.shape[0])], axis=1)


def tap_of(lines):
    return jnp.where(lines >= DILATION_STEP, 1, 0)


def lines_of(ref, rows):
    return ref[rows.start // LANES : rows.stop // LANES, :]


def picked(pieces, rows):
    found, at = [], 0
    for ref in pieces:
        low, high = max(rows.start, at), min(rows.stop, at + ref.shape[0])
        if low < high:
            found.append(ref[low - at : high - at, :])
        at += ref.shape[0]
    return found[0] if len(found) == 1 else jnp.concatenate(found, axis=0)


def call(kernel, name, in_specs, out_specs, out_shape, scratch=(), aliases=None, grid=(), vmem=24):
    return pl.pallas_call(
        kernel,
        grid=grid,
        in_specs=in_specs,
        out_specs=out_specs,
        out_shape=out_shape,
        scratch_shapes=list(scratch),
        input_output_aliases=aliases or {},
        cost_estimate=pl.CostEstimate(
            flops=1 + int(FLOPS * COSTS.get(name, COSTS.get(name.split("_")[0], 0))), bytes_accessed=1, transcendentals=0
        ),
        name=name,
        compiler_params=pltpu.CompilerParams(vmem_limit_bytes=vmem * MEGA),
    )


VMEM = pl.BlockSpec(memory_space=pltpu.VMEM)
ANYWHERE = pl.BlockSpec(memory_space=pl.ANY)
MARK = jax.ShapeDtypeStruct((8, LANES), F32)


def beside(*parts):
    return jnp.concatenate(parts, axis=1)


def below(*parts):
    return jnp.concatenate(parts, axis=0)


def gate_product(half, k, rows, past, sig, feats, w_in, w_cond, b_conv):
    width = sig.shape[1]
    part = w_in.shape[1] // 2
    here = slice(k * part, (k + 1) * part)
    there = slice((k * HALVES + half) * part, (k * HALVES + half + 1) * part)
    own = dot(past, w_in[:width, here]) + dot(sig[rows, :], w_in[width:, here])
    return own + across(feats, w_cond[:, there]) + b_conv[:, there]


def back_product(rows, gout, gskip, w_res, w_skip):
    return against(gout[rows, :], w_res[...]) + against(gskip[rows, :], w_skip[...])


def weight_copies(half, w_past, w_now, w_res, w_skip, w_in_to, w_res_to, w_skip_to):
    width = w_past.shape[0]
    part = w_res_to.shape[0]
    pairs = []
    for k in range(2):
        here = pl.ds((k * HALVES + half) * part, part)
        for i, ref in enumerate((w_past, w_now)):
            pairs.append((ref.at[:, here], w_in_to.at[pl.ds(i * width, width), pl.ds(k * part, part)]))
    rows = pl.ds(half * part, part)
    return pairs + [(w_res.at[rows], w_res_to), (w_skip.at[rows], w_skip_to)]


def half_weights(w_past, w_res, w_skip):
    part = w_res.shape[0] // HALVES
    shapes = ((2 * w_past.shape[0], 2 * part), (part, w_res.shape[1]), (part, w_skip.shape[1]))
    return [jax.ShapeDtypeStruct(shape, BF16) for shape in shapes]


def finish(pre_a, pre_s, dgated, valid_lines):
    act = jnp.tanh(pre_a)
    gate = 0.5 + 0.5 * jnp.tanh(0.5 * pre_s)
    slope = (column(valid_lines) * dgated) * gate
    dpre = beside(slope * (1.0 - act * act), slope * act * (1.0 - gate)).astype(BF16)
    gated = (act * gate).astype(BF16)
    return gated, gated.T * row(valid_lines.astype(BF16)), dpre


def forward_tiles(half, tiles, prepare, arrive, valid, past, sig, x_turned, gout, gskip, weights, outs, base):
    w_in, w_cond, b_conv, w_res, w_skip = weights
    gated_out, kept_out, dpre_out = outs
    cond = w_cond.shape[0]
    width = sig.shape[1]

    def product(rows, k):
        if arrive:
            arrive(rows, k)
        if k == 2:
            return back_product(rows, gout, gskip, w_res, w_skip)
        feats = x_turned[2 * width : 2 * width + cond, rows]
        return gate_product(half, k, rows, past[rows, :], sig, feats, w_in, w_cond, b_conv)

    def done(rows, made):
        there = slice(rows.start - base, rows.stop - base)
        gated_out[there, :], kept_out[:, there], dpre_out[there, :] = finish(*made, lines_of(valid, rows))

    ahead = None
    for rows in tiles:
        if prepare:
            prepare(rows)
        made = [product(rows, k) for k in range(3)]
        if ahead:
            done(*ahead)
        ahead = (rows, made)
    done(*ahead)


def tiles_of(start, stop):
    return [slice(a, a + DILATION_STEP) for a in range(start, stop, DILATION_STEP)]


def load_body(
    valid, pos, b_conv, feat, w_cond, w_res, w_skip, w_past, w_now, sig, gout, gskip,
    valid_to, pos_to, b_conv_to, w_cond_to, w_in, w_res_to, w_skip_to, past, sig_to, x_turned,
    gout_to, gskip_to, gated_rest, kept_rest, dpre_rest, sems,
):
    rows_all, width = sig.shape
    cond = feat.shape[0]
    count = 0

    def start(source, target):
        nonlocal count
        copy = pltpu.make_async_copy(source, target, sems.at[count])
        copy.start()
        count += 1
        return copy

    def tile(i, source, target):
        rows = pl.ds(i * ROWS, ROWS)
        return start(source.at[rows], target.at[rows])

    weights = weight_copies(0, w_past, w_now, w_res, w_skip, w_in, w_res_to, w_skip_to)
    signals = [[tile(0, sig, sig_to)]]
    needs = [
        [
            start(pos, pos_to),
            *(start(*pair) for pair in weights[:2]),
            start(feat, x_turned.at[pl.ds(2 * width, cond)]),
            start(w_cond, w_cond_to),
            start(b_conv, b_conv_to),
        ],
        [start(*pair) for pair in weights[2:4]],
        [start(valid, valid_to), *(start(*pair) for pair in weights[4:])],
    ]
    cotangents = [[tile(0, gout, gout_to), tile(0, gskip, gskip_to)]]
    for i in range(1, rows_all // ROWS):
        signals.append([tile(i, sig, sig_to)])
        cotangents.append([tile(i, gout, gout_to), tile(i, gskip, gskip_to)])

    def wait(copies):
        for copy in copies:
            copy.wait()
        copies.clear()

    def prepare(rows):
        i = rows.start // ROWS
        wait(signals[i])
        wait(needs[0])
        whole = rows if i else slice(0, rows.stop)
        before = slice(rows.start - DILATION_STEP, rows.stop - DILATION_STEP)
        tap = tap_of(lines_of(pos_to, rows)).astype(F32)
        past[rows, :] = sig_to[before, :] * column(tap).astype(BF16)
        x_turned[width : 2 * width, whole] = sig_to[whole, :].T
        x_turned[:width, rows] = x_turned[width : 2 * width, before] * row(tap).astype(BF16)

    def arrive(rows, k):
        wait(needs[k])
        if k == 2:
            wait(cotangents[rows.start // ROWS])

    x_turned[2 * width + cond :, :] = jnp.ones((x_turned.shape[0] - 2 * width - cond, rows_all), BF16)
    forward_tiles(
        0, tiles_of(DILATION_STEP, rows_all), prepare, arrive, valid_to, past, sig_to, x_turned, gout_to, gskip_to,
        (w_in, w_cond_to, b_conv_to, w_res_to, w_skip_to), (gated_rest, kept_rest, dpre_rest), DILATION_STEP,
    )


def rest_shapes(rest, part):
    return [jax.ShapeDtypeStruct(shape, BF16) for shape in ((rest, part), (part, rest), (rest, 2 * part))]


def load(*arrays):
    sources = [in_hbm(x) for x in arrays]
    feat, w_cond, w_res, w_skip, w_past, _, sig, gout, gskip = arrays[3:]
    rows, width = sig.shape
    hidden = w_res.shape[0]
    shapes = [jax.ShapeDtypeStruct(x.shape, x.dtype) for x in arrays[:3] + (w_cond,)]
    shapes += half_weights(w_past, w_res, w_skip) + [
        jax.ShapeDtypeStruct(shape, BF16)
        for shape in (
            sig.shape, sig.shape, (2 * width + feat.shape[0] + ONES, rows), gout.shape, gskip.shape,
        )
    ]
    shapes += rest_shapes(rows - DILATION_STEP, hidden // HALVES)
    return call(
        load_body,
        "load",
        [ANYWHERE] * len(sources),
        [VMEM] * len(shapes),
        shapes,
        scratch=[pltpu.SemaphoreType.DMA((11 + 3 * (rows // ROWS),))],
    )(*sources)


def side_by_side(dpre_0, dpre_1):
    part = dpre_0.shape[1] // 2
    return beside(dpre_0[:, :part], dpre_1[:, :part], dpre_0[:, part:], dpre_1[:, part:])


def head_rows(half, halo, pos, valid, sig, x_turned, gout, gskip, weights, outs):
    w_in, w_cond, b_conv, w_res, w_skip = weights
    rows = slice(0, DILATION_STEP)
    width = halo.shape[1]
    feats = x_turned[2 * width : 2 * width + w_cond.shape[0], rows]
    past = halo[...] * column(tap_of(lines_of(pos, rows)).astype(F32)).astype(BF16)
    made = [gate_product(half, k, rows, past, sig, feats, w_in, w_cond, b_conv) for k in range(2)]
    made.append(back_product(rows, gout, gskip, w_res, w_skip))
    for ref, value in zip(outs, finish(*made, lines_of(valid, rows))):
        ref[...] = value


def head_body(halo, pos, valid, sig, x_turned, gout, gskip, w_in, w_cond, b_conv, w_res, w_skip, past_out, *outs):
    tap = tap_of(lines_of(pos, slice(0, DILATION_STEP))).astype(F32)
    past_out[...] = halo[...].T * row(tap).astype(BF16)
    head_rows(0, halo, pos, valid, sig, x_turned, gout, gskip, (w_in, w_cond, b_conv, w_res, w_skip), outs)


def head(halo, *args):
    width = halo.shape[1]
    part = args[-1].shape[0]
    past, *parts = call(
        head_body,
        "head",
        [VMEM] * (1 + len(args)),
        [VMEM] * 4,
        [jax.ShapeDtypeStruct((width, DILATION_STEP), BF16)] + rest_shapes(DILATION_STEP, part),
    )(halo, *args)
    return past, parts


def early_body(token, pos, dpre_0, dpre_1, w_in_0, w_in_1, early):
    tap = column(tap_of(lines_of(pos, slice(0, DILATION_STEP))))
    some = slice(0, early.shape[1])
    early[...] = (tap * (against(dpre_0[...], w_in_0[some, :]) + against(dpre_1[...], w_in_1[some, :]))).astype(BF16)


def early_rows(token, pos, dpre_0, dpre_1, w_in_0, w_in_1):
    return call(
        early_body,
        "early",
        [ANYWHERE] + [VMEM] * 5,
        VMEM,
        jax.ShapeDtypeStruct((DILATION_STEP, w_in_0.shape[0] // 2), BF16),
    )(token, pos, dpre_0, dpre_1, w_in_0, w_in_1)


def forward_body(token, halo, pos, valid, past, sig, x_turned, gout, gskip, w_in, w_cond, b_conv, w_res, w_skip, *outs):
    weights = (w_in, w_cond, b_conv, w_res, w_skip)
    head_rows(1, halo, pos, valid, sig, x_turned, gout, gskip, weights, outs[:3])
    forward_tiles(
        1, tiles_of(DILATION_STEP, sig.shape[0]), None, None, valid, past, sig, x_turned, gout, gskip, weights, outs[3:],
        DILATION_STEP,
    )


def forward_1(token, *args):
    part = args[-1].shape[0]
    parts = call(
        forward_body,
        "forward_1",
        [ANYWHERE] + [VMEM] * len(args),
        [VMEM] * 6,
        rest_shapes(DILATION_STEP, part) + rest_shapes(args[4].shape[0] - DILATION_STEP, part),
    )(token, *args)
    return parts[:3], parts[3:]


GROUPS = (((3, 1), (2, 0)), ((1, 2, 3, 0),))


def own_place():
    return [lax.axis_index(name) for name in ("core", "far", "near")]


def turned(index, count):
    bits = (count - 1).bit_length()
    result = 0
    for bit in range(bits):
        result = result | (((index >> bit) & 1) << (bits - 1 - bit))
    return result


def gradients_body(far, block, half, own, count, extra, token, valid, x_turned, gout, gskip, past_head, *refs):
    kepts, dpres, refs = refs[:count], refs[count : 2 * count], refs[2 * count :]
    groups = GROUPS[half]
    sources, outs = refs[:extra], refs[extra : len(refs) - 1 - bool(extra)]
    outs, targets = outs[: len(groups)], outs[len(groups) :]
    acc = refs[-1 - bool(extra)]
    copies = []
    if extra:
        pairs = weight_copies(1, *sources[:4], *targets[:3]) + list(zip(sources[4:], targets[3:]))
        copies = [pltpu.make_async_copy(*pair, refs[-1].at[k]) for k, pair in enumerate(pairs)]
    for copy in copies:
        copy.start()
    width = past_head.shape[0]
    part = kepts[0].shape[0]
    ends, rows = x_turned.shape
    size = far * block
    core, z, xy = own_place()
    which = core if own else 1 - core

    def product(left_of, rights):
        total, at = None, 0
        for k, right in enumerate(rights):
            here = slice(at, at + right.shape[0])
            made = dot(left_of(here, k), right[...])
            total = made if at == 0 else total + made
            at = here.stop
        return total

    def region(k):
        low, high = k * size, min((k + 1) * size, ends)

        def turned_rows(here, piece):
            if piece == 0 and low < width:
                return below(past_head[low : min(high, width), :], x_turned[width : max(high, width), here])
            return x_turned[low:high, here]

        acc[: high - low, :] = product(turned_rows, dpres)
        at = high - low
        if high == ends:
            mask = jnp.broadcast_to(row(lines_of(valid, slice(0, rows)).astype(F32)).astype(BF16), (ONES, rows))

            def kept_rows(here, piece):
                return below(kepts[piece][...], mask[:, here])

            for i, ref in enumerate((gout, gskip)):
                cuts = [0]
                for kept in kepts:
                    cuts.append(cuts[-1] + kept.shape[1])
                made = product(kept_rows, [ref.at[pl.ds(a, b - a)] for a, b in zip(cuts, cuts[1:])])
                acc[at : at + part, :] = made[:part]
                at += part
                if i == half:
                    acc[high - low + 2 * part : high - low + 2 * part + ONES, :] = made[part:]
            at += ONES
            acc[at:, :] = jnp.zeros((size - at, acc.shape[1]), F32)
        for group, out in zip(groups, outs):
            for i, p in enumerate(group):
                here = pl.ds(pl.multiple_of((xy ^ p) * LANES, LANES), LANES)
                for r in range(far):
                    out[i, turned(r ^ z, far)] = acc[r * block : (r + 1) * block, here].astype(out.dtype)

    for k in range(2):
        pl.when(which == k)(functools.partial(region, k))
    for copy in copies:
        copy.wait()


def gradients(half, own, token, far, block, valid, x_turned, gout, gskip, past_head, pieces, loads=()):
    wide = pieces[0][2].shape[1]
    count = len(pieces)
    sources = [in_hbm(x) for x in loads]
    outs = [jax.ShapeDtypeStruct((len(group), far, block, LANES), F32 if own else BF16) for group in GROUPS[half]]
    scratch = [pltpu.VMEM((far * block, wide), F32)]
    if loads:
        outs += half_weights(loads[0], *loads[2:4]) + [jax.ShapeDtypeStruct(x.shape, x.dtype) for x in loads[4:]]
        scratch.append(pltpu.SemaphoreType.DMA((6 + len(loads[4:]),)))
    return call(
        functools.partial(gradients_body, far, block, half, own, count, len(loads)),
        ("mine" if own else "theirs") + f"_{half}",
        [ANYWHERE] + [VMEM] * (5 + 2 * count) + [ANYWHERE] * len(loads),
        [VMEM] * len(outs),
        outs,
        scratch=scratch,
    )(token, valid, x_turned, gout, gskip, past_head, *(p[1] for p in pieces), *(p[2] for p in pieces), *sources)


def outputs_body(counts, token, valid, sig, w_res_0, w_skip_0, w_res_1, w_skip_1, b_res, b_skip, *refs):
    first, second = refs[: counts[0]], refs[counts[0] : sum(counts)]
    out, skip, mark, rooms, sems = refs[sum(counts) :]
    copies = []
    for i in range(sig.shape[0] // ROWS):
        rows = slice(i * ROWS, (i + 1) * ROWS)
        mask = column(lines_of(valid, rows))
        left, right = picked(first, rows), picked(second, rows)
        branch = dot(left, w_res_0[...]) + dot(right, w_res_1[...]) + b_res[...]
        rooms[i, 0] = (sig[rows, :].astype(F32) + mask * branch).astype(BF16)
        side = dot(left, w_skip_0[...]) + dot(right, w_skip_1[...]) + b_skip[...]
        rooms[i, 1] = (mask * side).astype(BF16)
        for k, ref in enumerate((out, skip)):
            copies.append(pltpu.make_async_copy(rooms.at[i, k], ref.at[pl.ds(i * ROWS, ROWS)], sems.at[i, k]))
            copies[-1].start()
    mark[...] = jnp.zeros_like(mark)
    for copy in copies:
        copy.wait()


def outputs(token, valid, sig, gated_0, gated_1, weights_0, weights_1, b_res, b_skip):
    rows, width = sig.shape
    counts = (len(gated_0), len(gated_1))
    return call(
        functools.partial(outputs_body, counts),
        "outputs",
        [ANYWHERE] + [VMEM] * (8 + sum(counts)),
        [ANYWHERE, ANYWHERE, VMEM],
        [
            jax.ShapeDtypeStruct((rows, width), BF16),
            jax.ShapeDtypeStruct((rows, weights_0[1].shape[1]), BF16),
            MARK,
        ],
        scratch=[
            pltpu.VMEM((rows // ROWS, 2, ROWS, width), BF16),
            pltpu.SemaphoreType.DMA((rows // ROWS, 2)),
        ],
    )(token, valid, sig, *weights_0, *weights_1, b_res, b_skip, *gated_0, *gated_1)


def inputs_body(steps, counts, token, received, gout, pos, w_in_0, w_in_1, w_cond, *refs):
    first, second = refs[: counts[0]], refs[counts[0] : sum(counts)]
    gsig, gfeat, mark, room, room_feat, sems = refs[-6:]
    rows, width = gout.shape
    copies = []
    wide = 2 * LANES

    def copy(source, target):
        copies.append(pltpu.make_async_copy(source, target, sems.at[len(copies)]))
        copies[-1].start()

    for i, step in enumerate(steps):
        begin = step * ROWS
        here = slice(begin, begin + ROWS)
        after = slice(begin + DILATION_STEP, min(begin + DILATION_STEP + ROWS, rows))
        now = [picked(pieces, here) for pieces in (first, second)]
        later = [picked(pieces, after) for pieces in (first, second)]
        tap = column(tap_of(lines_of(pos, after)))
        room_feat[i] = against(w_cond[...], side_by_side(*now))
        copy(room_feat.at[i], gfeat.at[:, pl.ds(begin, ROWS)])
        for k in range(width // wide):
            some = slice(k * wide, (k + 1) * wide)
            tail = tap * (against(later[0], w_in_0[some, :]) + against(later[1], w_in_1[some, :]))
            if tail.shape[0] < ROWS:
                tail = below(tail, received[:, some].astype(F32))
            below_past = slice(width + k * wide, width + (k + 1) * wide)
            own = against(now[0], w_in_0[below_past, :]) + against(now[1], w_in_1[below_past, :])
            room[i, k] = gout[here, some].astype(F32) + own + tail
            copy(room.at[i, k], gsig.at[pl.ds(begin, ROWS), pl.ds(k * wide, wide)])
    mark[...] = jnp.zeros_like(mark)
    for one in copies:
        one.wait()


def inputs(steps, token, received, gout, pos, dpre_0, dpre_1, w_in_0, w_in_1, w_cond, before):
    rows, width = gout.shape
    cond = w_cond.shape[0]
    count = width // (2 * LANES)
    counts = (len(dpre_0), len(dpre_1))
    operands = 7 + sum(counts)
    return call(
        functools.partial(inputs_body, steps, counts),
        f"inputs_{steps[0]}",
        [ANYWHERE] + [VMEM] * (operands - 1) + [ANYWHERE] * len(before),
        [ANYWHERE, ANYWHERE, VMEM],
        [
            jax.ShapeDtypeStruct((rows, width), F32),
            jax.ShapeDtypeStruct((cond, rows), F32),
            MARK,
        ],
        scratch=[
            pltpu.VMEM((len(steps), count, ROWS, 2 * LANES), F32),
            pltpu.VMEM((len(steps), cond, ROWS), F32),
            pltpu.SemaphoreType.DMA((len(steps) * (count + 1),)),
        ],
        aliases={operands + k: k for k in range(len(before))},
    )(token, received, gout, pos, w_in_0, w_in_1, w_cond, *dpre_0, *dpre_1, *before)


SHARES = ((0, 3), (1, 2))


def unpack_body(far, block, token, *refs):
    blocks, arrays, (mark, room) = refs[: 2 * len(SHARES)], refs[-9:-2], refs[-2:]
    mine, theirs = blocks[: len(SHARES)], blocks[len(SHARES) :]
    mark[...] = jnp.zeros_like(mark)
    core, z, xy = own_place()

    @pl.when(pl.program_id(0) == 0)
    def _():
        for k, parts in ((core, mine), (1 - core, theirs)):
            for share, ref in zip(SHARES, parts):
                for i, c in enumerate(share):
                    for r in range(far):
                        rows = pl.ds(pl.multiple_of((k * far + (r ^ z)) * block, 16), block)
                        room[c ^ xy, rows, :] = ref[i, turned(r, far)]

    for j in range(NEAR // 2):
        c = pl.program_id(0) * (NEAR // 2) + j
        here = pl.ds(j * LANES, LANES)
        top = 0
        for ref in arrays:
            count = ref.shape[0]
            size = max(count, ONES)
            ref[:, here] = room[c, top : top + size, :].astype(F32)[:count]
            top += size


def unpack(half, token, far, block, mine, theirs, width, cond, hidden, skip_width, before):
    part = hidden // HALVES
    gates = 2 * hidden
    own = (width, skip_width)[half]

    def wide(size):
        return pl.BlockSpec((size, part), lambda s: (0, HALVES * s + half))

    def tall(size):
        return pl.BlockSpec((part, size // 2), lambda s: (half, s))

    specs = [wide(width), wide(width), wide(cond), wide(1), tall(width), tall(skip_width), pl.BlockSpec((1, own // 2), lambda s: (0, s))]
    shapes = [(width, gates), (width, gates), (cond, gates), (1, gates), (hidden, width), (hidden, skip_width), (1, own)]
    blocks = [pl.BlockSpec(x.shape, lambda s: (0,) * 4) for x in (*mine, *theirs)]
    return call(
        functools.partial(unpack_body, far, block),
        f"unpack_{half}",
        [ANYWHERE, *blocks] + [ANYWHERE] * len(before),
        specs + [pl.BlockSpec(MARK.shape, lambda s: (0, 0))],
        [jax.ShapeDtypeStruct(shape, F32) for shape in shapes] + [MARK],
        scratch=[pltpu.VMEM((NEAR, 2 * far * block, LANES), BF16)],
        aliases={1 + len(blocks) + k: k for k in range(len(before))},
        grid=(2,),
    )(token, *mine, *theirs, *before)


def swapped(x, axis, k):
    return lax.ppermute(x, axis, [(i, i ^ k) for i in range(lax.axis_size(axis))])


def exchanged(blocks):
    return [swapped(block, "near", k + 1) for k, block in enumerate(blocks)]


def add_body(sizes, token, *refs):
    count = len(sizes)
    kept, got, outs = refs[0], refs[1:-count], refs[-count:]
    at = 0
    for out, size in zip(outs, sizes):
        for k in range(size):
            total = kept[at + k].astype(F32)
            for ref in got:
                total = total + ref[at + k].astype(F32)
            out[k] = total.astype(out.dtype)
        at += size


def added(name, token, kept, got, outs):
    sizes = [size for size, _ in outs]
    result = call(
        functools.partial(add_body, sizes),
        name,
        [ANYWHERE] + [VMEM] * (1 + len(got)),
        [VMEM] * len(outs),
        [jax.ShapeDtypeStruct((size, *kept.shape[1:]), dtype) for size, dtype in outs],
    )(token, kept, *got)
    return result


def mirror_body(token, mine, got, out):
    count = mine.shape[0]
    for k in range(count):
        out[k] = (mine[k].astype(F32) + got[count - 1 - k].astype(F32)).astype(out.dtype)


def mirrored(name, token, mine, got):
    return call(
        mirror_body,
        name,
        [ANYWHERE, VMEM, VMEM],
        VMEM,
        jax.ShapeDtypeStruct(mine.shape, BF16),
    )(token, mine, got)


def join_body(token, *refs):
    out = refs[-1]
    at = 0
    for ref in refs[:-1]:
        out[at : at + ref.shape[0]] = ref[...]
        at += ref.shape[0]


def joined(name, token, parts):
    count = sum(part.shape[0] for part in parts)
    return call(
        join_body,
        name,
        [ANYWHERE] + [VMEM] * len(parts),
        VMEM,
        jax.ShapeDtypeStruct((count, *parts[0].shape[1:]), BF16),
    )(token, *parts)


def over_outer(total):
    for bit in range((lax.axis_size("outer") - 1).bit_length()):
        total = (total.astype(F32) + swapped(total, "outer", 1 << bit).astype(F32)).astype(BF16)
    return total


def passed_along(x, by):
    peers = lax.axis_size(AXES)
    pairs = [(i, i + by) for i in range(peers) if 0 <= i + by < peers]
    return lax.ppermute(x, AXES, pairs)


def in_hbm(x):
    return pltpu.with_memory_space_constraint(x, pltpu.HBM)


def body(
    signal,
    features,
    position,
    valid,
    w_past,
    w_now,
    b_conv,
    w_cond,
    w_res,
    b_res,
    w_skip,
    b_skip,
    grad_out,
    grad_skip,
):
    rows, width = signal.shape
    features = features.T
    cond = features.shape[0]
    hidden = w_res.shape[0]
    skip_width = w_skip.shape[1]
    far = lax.axis_size("far")
    far_bits = (far - 1).bit_length()
    used = 2 * width + cond + ONES + 2 * (hidden // HALVES) + ONES
    block = -(-used // (2 * far * 16)) * 16
    lines = (rows // LANES, LANES)
    pos, val = position.reshape(lines), valid.reshape(lines)
    b_conv, b_res, b_skip = (b.reshape(1, -1) for b in (b_conv, b_res, b_skip))

    def core_sum(half, token, theirs, mine):
        got = {}
        for k, group in enumerate(GROUPS[half]):
            blocks = added(
                f"core_sum_{half}_{k}", token, mine[k], [swapped(theirs[k], "core", 1)],
                [(1, BF16 if p else F32) for p in group],
            )
            token = blocks[0]
            for p, part in zip(group, blocks):
                got[p] = swapped(part[0], "near", p) if p else part[0]
        return got[0], [got[p] for p in range(1, NEAR)]

    def near_sum(half, token, kept, got):
        kept, sent = added(f"near_sum_{half}", token, kept, got, [(far // 2, F32), (far // 2, BF16)])
        return kept, swapped(sent, "far", 1)

    def far_sum(half, token, kept, got):
        for bit in range(1, far_bits - 1):
            size = kept.shape[0] // 2
            kept, sent = added(f"far_sum_{half}_{bit}", token, kept, [got], [(size, F32), (size, BF16)])
            got = swapped(sent, "far", 1 << bit)
        (mine,) = added(f"far_sum_{half}", token, kept, [got], [(kept.shape[0], BF16)])
        return mine, swapped(mine, "far", 1 << (far_bits - 1))

    def far_end(half, token, mine, got):
        total = over_outer(mirrored(f"far_end_{half}", token, mine, got))
        return total, swapped(total, "far", 1 << (far_bits - 2))

    def far_join(half, token, mine, got):
        total = joined(f"far_join_{half}", token, [mine, got])
        for bit in reversed(range(far_bits - 2)):
            total = joined(f"far_join_{half}_{bit}", token, [total, swapped(total, "far", 1 << bit)])
        return total, exchanged([total] * (NEAR - 1))

    def near_join(half, k, token, mine, got):
        blocks = [mine, *got]
        total = joined(f"near_join_{half}_{k}", token, [blocks[c][None] for c in SHARES[k]])
        return total, swapped(total, "core", 1)

    def input_gradients(steps, token, before):
        last = (steps[-1] + 1) * ROWS == rows
        return inputs(steps, token, received if last else head_0[0], grad_out, pos, dpre_0, dpre_1, w_in_0, w_in_1, w_cond, before)

    halo = passed_along(signal[rows - DILATION_STEP :], 1)
    loads = (w_past, w_now, w_res, w_skip, b_res, b_skip)
    val, pos, b_conv, w_cond, w_in_0, *outer_0, past, signal, x_turned, grad_out, grad_skip, a, b, c = load(
        val, pos, b_conv, features, w_cond, w_res, w_skip, w_past, w_now, signal, grad_out, grad_skip
    )
    rest_0 = (a, b, c)
    common = (signal, x_turned, grad_out, grad_skip)
    past_head, head_0 = head(halo, pos, val, *common, w_in_0, w_cond, b_conv, *outer_0)
    made_0 = (head_0, rest_0)
    fixed = (far, block, val, x_turned, grad_out, grad_skip, past_head)
    *theirs_0, w_in_1, w_res_1, w_skip_1, b_res, b_skip = gradients(0, False, past_head, *fixed, made_0, loads)
    outer_1 = (w_res_1, w_skip_1)
    weights_1 = (w_in_1, w_cond, b_conv, *outer_1)
    mine_0 = gradients(0, True, theirs_0[0], *fixed, made_0)
    kept_0, got_0 = core_sum(0, mine_0[0], theirs_0, mine_0)
    made_1 = forward_1(kept_0, halo, pos, val, past, *common, *weights_1)
    dpre_0, dpre_1 = ([p[2] for p in made] for made in (made_0, made_1))
    theirs_1 = gradients(1, False, kept_0, *fixed, made_1)
    mine_1 = gradients(1, True, theirs_1[0], *fixed, made_1)
    (part,) = added("near_part_0", mine_1[0], got_0[2], [got_0[0]], [(far, F32)])
    kept_0, got_0 = near_sum(0, part, kept_0, [part, got_0[1]])
    kept_1, got_1 = core_sum(1, kept_0, theirs_1, mine_1)
    ends_0, got_0 = far_sum(0, kept_1, kept_0, got_0)
    *grads, mark = input_gradients((0, 1), ends_0, [])
    ends_0, got_0 = far_end(0, mark, ends_0, got_0)
    kept_1, got_1 = near_sum(1, ends_0, kept_1, got_1)
    ends_0, got_0 = far_join(0, kept_1, ends_0, got_0)
    ends_1, got_1 = far_sum(1, ends_0, kept_1, got_1)
    output, skip_out, mark = outputs(
        ends_1, val, signal, [p[0] for p in made_0], [p[0] for p in made_1], outer_0, outer_1, b_res, b_skip
    )
    ends_1, got_1 = far_end(1, mark, ends_1, got_1)
    early = early_rows(ends_1, pos, dpre_0[0], dpre_1[0], w_in_0, w_in_1)
    received = passed_along(early, -1)
    first = near_join(0, 0, early, ends_0, got_0)
    second = near_join(0, 1, first[0], ends_0, got_0)
    pairs_0 = [first, second]
    ends_1, got_1 = far_join(1, second[0], ends_1, got_1)
    *grads, mark = input_gradients((2, 3), ends_1, grads)
    first = near_join(1, 0, mark, ends_1, got_1)
    second = near_join(1, 1, first[0], ends_1, got_1)
    pairs_1 = [first, second]
    sizes = (width, cond, hidden, skip_width)
    *done, own_0, mark = unpack(0, first[1], far, block, *zip(*pairs_0), *sizes, [])
    *done, own_1, _ = unpack(1, mark, far, block, *zip(*pairs_1), *sizes, done)
    g_past, g_now, g_cond, g_bias, g_res, g_skip = done
    grad_signal, grad_features = grads
    return (
        output,
        skip_out,
        grad_signal,
        grad_features.T,
        g_past,
        g_now,
        g_bias.reshape(-1),
        g_cond,
        g_res,
        own_0.reshape(-1),
        g_skip,
        own_1.reshape(-1),
    )


def solution(mesh):
    row, col = mesh.shape["row"], mesh.shape["col"]
    fine = Mesh(mesh.devices.reshape(row // 2, 2, col // NEAR, NEAR), AXES)
    rows = P(AXES, None)
    line = P(AXES)
    return jax.shard_map(
        body,
        mesh=fine,
        in_specs=(rows, rows, line, line) + (P(),) * 8 + (rows, rows),
        out_specs=(rows,) * 4 + (P(),) * 8,
        check_vma=False,
    )
```

```python
import functools

import jax
import jax.numpy as jnp
from jax import lax
from jax.experimental import pallas as pl
from jax.experimental.pallas import tpu as pltpu
from jax.sharding import Mesh
from jax.sharding import PartitionSpec as P

DILATION_STEP = 256
AXES = ("outer", "core", "far", "near")
HALVES = 2
NEAR = 4
LANES = 128
ROWS = 512
ONES = 16
F32 = jnp.float32
BF16 = jnp.bfloat16
MEGA = 1 << 20
COSTS = {
    "load": 8, "head": 2, "near_sum_0": 7, "mine_1": 2,
    "far_sum_0": 8, "near_sum_1": 4, "near_join_0_1": 2, "near_join_1_1": 4, "far_join_0": 4,
}
FLOPS = 10**9


def dot(left, right):
    return jnp.dot(left, right, preferred_element_type=F32)


def across(left, right):
    return lax.dot_general(left, right, (((0,), (0,)), ((), ())), preferred_element_type=F32)


def against(left, weight):
    return lax.dot_general(left, weight, (((1,), (1,)), ((), ())), preferred_element_type=F32)


def column(lines):
    turned = lines.astype(F32).T
    return jnp.concatenate([turned[:, k : k + 1] for k in range(lines.shape[0])], axis=0)


def row(lines):
    return jnp.concatenate([lines[k : k + 1] for k in range(lines.shape[0])], axis=1)


def tap_of(lines):
    return jnp.where(lines >= DILATION_STEP, 1, 0)


def lines_of(ref, rows):
    return ref[rows.start // LANES : rows.stop // LANES, :]


def picked(pieces, rows):
    found, at = [], 0
    for ref in pieces:
        low, high = max(rows.start, at), min(rows.stop, at + ref.shape[0])
        if low < high:
            found.append(ref[low - at : high - at, :])
        at += ref.shape[0]
    return found[0] if len(found) == 1 else jnp.concatenate(found, axis=0)


def call(kernel, name, in_specs, out_specs, out_shape, scratch=(), aliases=None, grid=(), vmem=24):
    return pl.pallas_call(
        kernel,
        grid=grid,
        in_specs=in_specs,
        out_specs=out_specs,
        out_shape=out_shape,
        scratch_shapes=list(scratch),
        input_output_aliases=aliases or {},
        cost_estimate=pl.CostEstimate(
            flops=1 + int(FLOPS * COSTS.get(name, COSTS.get(name.split("_")[0], 0))), bytes_accessed=1, transcendentals=0
        ),
        name=name,
        compiler_params=pltpu.CompilerParams(vmem_limit_bytes=vmem * MEGA),
    )


VMEM = pl.BlockSpec(memory_space=pltpu.VMEM)
ANYWHERE = pl.BlockSpec(memory_space=pl.ANY)
MARK = jax.ShapeDtypeStruct((8, LANES), F32)


def beside(*parts):
    return jnp.concatenate(parts, axis=1)


def below(*parts):
    return jnp.concatenate(parts, axis=0)


def gate_product(half, k, rows, past, sig, feats, w_in, w_cond, b_conv):
    width = sig.shape[1]
    part = w_in.shape[1] // 2
    here = slice(k * part, (k + 1) * part)
    there = slice((k * HALVES + half) * part, (k * HALVES + half + 1) * part)
    own = dot(past, w_in[:width, here]) + dot(sig[rows, :], w_in[width:, here])
    return own + across(feats, w_cond[:, there]) + b_conv[:, there]


def back_product(rows, gout, gskip, w_res, w_skip):
    return against(gout[rows, :], w_res[...]) + against(gskip[rows, :], w_skip[...])


def weight_copies(half, w_past, w_now, w_res, w_skip, w_in_to, w_res_to, w_skip_to):
    width = w_past.shape[0]
    part = w_res_to.shape[0]
    pairs = []
    for k in range(2):
        here = pl.ds((k * HALVES + half) * part, part)
        for i, ref in enumerate((w_past, w_now)):
            pairs.append((ref.at[:, here], w_in_to.at[pl.ds(i * width, width), pl.ds(k * part, part)]))
    rows = pl.ds(half * part, part)
    return pairs + [(w_res.at[rows], w_res_to), (w_skip.at[rows], w_skip_to)]


def half_weights(w_past, w_res, w_skip):
    part = w_res.shape[0] // HALVES
    shapes = ((2 * w_past.shape[0], 2 * part), (part, w_res.shape[1]), (part, w_skip.shape[1]))
    return [jax.ShapeDtypeStruct(shape, BF16) for shape in shapes]


def finish(pre_a, pre_s, dgated, valid_lines):
    act = jnp.tanh(pre_a)
    gate = 0.5 + 0.5 * jnp.tanh(0.5 * pre_s)
    slope = (column(valid_lines) * dgated) * gate
    dpre = beside(slope * (1.0 - act * act), slope * act * (1.0 - gate)).astype(BF16)
    gated = (act * gate).astype(BF16)
    return gated, gated.T * row(valid_lines.astype(BF16)), dpre


def forward_tiles(half, tiles, prepare, arrive, valid, past, sig, x_turned, gout, gskip, weights, outs, base):
    w_in, w_cond, b_conv, w_res, w_skip = weights
    gated_out, kept_out, dpre_out = outs
    cond = w_cond.shape[0]
    width = sig.shape[1]

    def product(rows, k):
        if arrive:
            arrive(rows, k)
        if k == 2:
            return back_product(rows, gout, gskip, w_res, w_skip)
        feats = x_turned[2 * width : 2 * width + cond, rows]
        return gate_product(half, k, rows, past[rows, :], sig, feats, w_in, w_cond, b_conv)

    def done(rows, made):
        there = slice(rows.start - base, rows.stop - base)
        gated_out[there, :], kept_out[:, there], dpre_out[there, :] = finish(*made, lines_of(valid, rows))

    ahead = None
    for rows in tiles:
        if prepare:
            prepare(rows)
        made = [product(rows, k) for k in range(3)]
        if ahead:
            done(*ahead)
        ahead = (rows, made)
    done(*ahead)


def tiles_of(start, stop):
    return [slice(a, a + DILATION_STEP) for a in range(start, stop, DILATION_STEP)]


def split_rows(rows):
    return 3 * DILATION_STEP


def load_body(
    valid, pos, b_conv, feat, w_cond, w_res, w_skip, w_past, w_now, sig, gout, gskip,
    valid_to, pos_to, b_conv_to, w_cond_to, w_in, w_res_to, w_skip_to, past, sig_to, x_turned,
    gout_to, gskip_to, gated_rest, kept_rest, dpre_rest, sems,
):
    rows_all, width = sig.shape
    cond = feat.shape[0]
    count = 0

    def start(source, target):
        nonlocal count
        copy = pltpu.make_async_copy(source, target, sems.at[count])
        copy.start()
        count += 1
        return copy

    def tile(i, source, target):
        rows = pl.ds(i * ROWS, ROWS)
        return start(source.at[rows], target.at[rows])

    weights = weight_copies(0, w_past, w_now, w_res, w_skip, w_in, w_res_to, w_skip_to)
    signals = [[tile(0, sig, sig_to)]]
    needs = [
        [
            start(pos, pos_to),
            *(start(*pair) for pair in weights[:2]),
            start(feat, x_turned.at[pl.ds(2 * width, cond)]),
            start(w_cond, w_cond_to),
            start(b_conv, b_conv_to),
        ],
        [start(*pair) for pair in weights[2:4]],
        [start(valid, valid_to), *(start(*pair) for pair in weights[4:])],
    ]
    cotangents = [[tile(0, gout, gout_to), tile(0, gskip, gskip_to)]]
    for i in range(1, rows_all // ROWS):
        signals.append([tile(i, sig, sig_to)])
        cotangents.append([tile(i, gout, gout_to), tile(i, gskip, gskip_to)])

    def wait(copies):
        for copy in copies:
            copy.wait()
        copies.clear()

    def prepare(rows):
        i = rows.start // ROWS
        wait(signals[i])
        wait(needs[0])
        whole = rows if i else slice(0, rows.stop)
        before = slice(rows.start - DILATION_STEP, rows.stop - DILATION_STEP)
        tap = tap_of(lines_of(pos_to, rows)).astype(F32)
        past[rows, :] = sig_to[before, :] * column(tap).astype(BF16)
        x_turned[width : 2 * width, whole] = sig_to[whole, :].T
        x_turned[:width, rows] = x_turned[width : 2 * width, before] * row(tap).astype(BF16)

    def arrive(rows, k):
        wait(needs[k])
        if k == 2:
            wait(cotangents[rows.start // ROWS])

    x_turned[2 * width + cond :, :] = jnp.ones((x_turned.shape[0] - 2 * width - cond, rows_all), BF16)
    forward_tiles(
        0, tiles_of(DILATION_STEP, rows_all), prepare, arrive, valid_to, past, sig_to, x_turned, gout_to, gskip_to,
        (w_in, w_cond_to, b_conv_to, w_res_to, w_skip_to), (gated_rest, kept_rest, dpre_rest), DILATION_STEP,
    )


def rest_shapes(rest, part):
    return [jax.ShapeDtypeStruct(shape, BF16) for shape in ((rest, part), (part, rest), (rest, 2 * part))]


def load(*arrays):
    sources = [in_hbm(x) for x in arrays]
    feat, w_cond, w_res, w_skip, w_past, _, sig, gout, gskip = arrays[3:]
    rows, width = sig.shape
    hidden = w_res.shape[0]
    shapes = [jax.ShapeDtypeStruct(x.shape, x.dtype) for x in arrays[:3] + (w_cond,)]
    shapes += half_weights(w_past, w_res, w_skip) + [
        jax.ShapeDtypeStruct(shape, BF16)
        for shape in (
            sig.shape, sig.shape, (2 * width + feat.shape[0] + ONES, rows), gout.shape, gskip.shape,
        )
    ]
    shapes += rest_shapes(rows - DILATION_STEP, hidden // HALVES)
    return call(
        load_body,
        "load",
        [ANYWHERE] * len(sources),
        [VMEM] * len(shapes),
        shapes,
        scratch=[pltpu.SemaphoreType.DMA((11 + 3 * (rows // ROWS),))],
    )(*sources)


def side_by_side(dpre_0, dpre_1):
    part = dpre_0.shape[1] // 2
    return beside(dpre_0[:, :part], dpre_1[:, :part], dpre_0[:, part:], dpre_1[:, part:])


def head_rows(half, halo, pos, valid, sig, x_turned, gout, gskip, weights, outs):
    w_in, w_cond, b_conv, w_res, w_skip = weights
    rows = slice(0, DILATION_STEP)
    width = halo.shape[1]
    feats = x_turned[2 * width : 2 * width + w_cond.shape[0], rows]
    past = halo[...] * column(tap_of(lines_of(pos, rows)).astype(F32)).astype(BF16)
    made = [gate_product(half, k, rows, past, sig, feats, w_in, w_cond, b_conv) for k in range(2)]
    made.append(back_product(rows, gout, gskip, w_res, w_skip))
    for ref, value in zip(outs, finish(*made, lines_of(valid, rows))):
        ref[...] = value


def head_body(halo, pos, valid, sig, x_turned, gout, gskip, w_in, w_cond, b_conv, w_res, w_skip, past_out, *outs):
    tap = tap_of(lines_of(pos, slice(0, DILATION_STEP))).astype(F32)
    past_out[...] = halo[...].T * row(tap).astype(BF16)
    head_rows(0, halo, pos, valid, sig, x_turned, gout, gskip, (w_in, w_cond, b_conv, w_res, w_skip), outs)


def head(halo, *args):
    width = halo.shape[1]
    part = args[-1].shape[0]
    past, *parts = call(
        head_body,
        "head",
        [VMEM] * (1 + len(args)),
        [VMEM] * 4,
        [jax.ShapeDtypeStruct((width, DILATION_STEP), BF16)] + rest_shapes(DILATION_STEP, part),
    )(halo, *args)
    return past, parts


def early_body(token, pos, dpre_0, dpre_1, w_in_0, w_in_1, early):
    tap = column(tap_of(lines_of(pos, slice(0, DILATION_STEP))))
    some = slice(0, early.shape[1])
    early[...] = (tap * (against(dpre_0[...], w_in_0[some, :]) + against(dpre_1[...], w_in_1[some, :]))).astype(BF16)


def early_rows(token, pos, dpre_0, dpre_1, w_in_0, w_in_1):
    return call(
        early_body,
        "early",
        [ANYWHERE] + [VMEM] * 5,
        VMEM,
        jax.ShapeDtypeStruct((DILATION_STEP, w_in_0.shape[0] // 2), BF16),
    )(token, pos, dpre_0, dpre_1, w_in_0, w_in_1)


def most_body(token, valid, past, sig, x_turned, gout, gskip, w_in, w_cond, b_conv, w_res, w_skip, *outs):
    forward_tiles(
        1, tiles_of(DILATION_STEP, split_rows(sig.shape[0])), None, None, valid, past, sig, x_turned, gout, gskip,
        (w_in, w_cond, b_conv, w_res, w_skip), outs, DILATION_STEP,
    )


def forward_most(token, *args):
    part = args[-1].shape[0]
    return call(
        most_body,
        "forward_1",
        [ANYWHERE] + [VMEM] * len(args),
        [VMEM] * 3,
        rest_shapes(split_rows(args[2].shape[0]) - DILATION_STEP, part),
    )(token, *args)


def ends_body(token, halo, pos, valid, past, sig, x_turned, gout, gskip, w_in, w_cond, b_conv, w_res, w_skip, *outs):
    weights = (w_in, w_cond, b_conv, w_res, w_skip)
    rows = sig.shape[0]
    head_rows(1, halo, pos, valid, sig, x_turned, gout, gskip, weights, outs[:3])
    forward_tiles(
        1, tiles_of(split_rows(rows), rows), None, None, valid, past, sig, x_turned, gout, gskip, weights, outs[3:],
        split_rows(rows),
    )


def forward_ends(token, *args):
    part = args[-1].shape[0]
    rows = args[4].shape[0]
    parts = call(
        ends_body,
        "ends_1",
        [ANYWHERE] + [VMEM] * len(args),
        [VMEM] * 6,
        rest_shapes(DILATION_STEP, part) + rest_shapes(rows - split_rows(rows), part),
    )(token, *args)
    return parts[:3], parts[3:]


def own_place():
    return [lax.axis_index(name) for name in ("core", "far", "near")]


def turned(index, count):
    bits = (count - 1).bit_length()
    result = 0
    for bit in range(bits):
        result = result | (((index >> bit) & 1) << (bits - 1 - bit))
    return result


def gradients_body(far, block, half, own, count, extra, token, valid, x_turned, gout, gskip, past_head, *refs):
    kepts, dpres, refs = refs[:count], refs[count : 2 * count], refs[2 * count :]
    sources, (out, *targets) = refs[:extra], refs[extra : len(refs) - 1 - bool(extra)]
    acc = refs[-1 - bool(extra)]
    copies = []
    if extra:
        pairs = weight_copies(1, *sources[:4], *targets[:3]) + list(zip(sources[4:], targets[3:]))
        copies = [pltpu.make_async_copy(*pair, refs[-1].at[k]) for k, pair in enumerate(pairs)]
    for copy in copies:
        copy.start()
    width = past_head.shape[0]
    part = kepts[0].shape[0]
    ends, rows = x_turned.shape
    size = far * block
    core, z, xy = own_place()
    which = core if own else 1 - core

    def product(left_of, rights):
        total, at = None, 0
        for k, right in enumerate(rights):
            here = slice(at, at + right.shape[0])
            made = dot(left_of(here, k), right[...])
            total = made if at == 0 else total + made
            at = here.stop
        return total

    def region(k):
        low, high = k * size, min((k + 1) * size, ends)

        def turned_rows(here, piece):
            if piece == 0 and low < width:
                return below(past_head[low : min(high, width), :], x_turned[width : max(high, width), here])
            return x_turned[low:high, here]

        acc[: high - low, :] = product(turned_rows, dpres)
        at = high - low
        if high == ends:
            mask = jnp.broadcast_to(row(lines_of(valid, slice(0, rows)).astype(F32)).astype(BF16), (ONES, rows))

            def kept_rows(here, piece):
                return below(kepts[piece][...], mask[:, here])

            for i, ref in enumerate((gout, gskip)):
                cuts = [0]
                for kept in kepts:
                    cuts.append(cuts[-1] + kept.shape[1])
                made = product(kept_rows, [ref.at[pl.ds(a, b - a)] for a, b in zip(cuts, cuts[1:])])
                acc[at : at + part, :] = made[:part]
                at += part
                if i == half:
                    acc[high - low + 2 * part : high - low + 2 * part + ONES, :] = made[part:]
            at += ONES
            acc[at:, :] = jnp.zeros((size - at, acc.shape[1]), F32)
        for r in range(far):
            for c in range(NEAR):
                value = acc[r * block : (r + 1) * block, c * LANES : (c + 1) * LANES]
                out[c ^ xy, turned(r ^ z, far)] = value.astype(out.dtype)

    for k in range(2):
        pl.when(which == k)(functools.partial(region, k))
    for copy in copies:
        copy.wait()


def gradients(half, own, token, far, block, valid, x_turned, gout, gskip, past_head, pieces, loads=()):
    packed = (NEAR, far, block, LANES)
    wide = pieces[0][2].shape[1]
    count = len(pieces)
    sources = [in_hbm(x) for x in loads]
    outs = [jax.ShapeDtypeStruct(packed, F32 if own else BF16)]
    scratch = [pltpu.VMEM((far * block, wide), F32)]
    if loads:
        outs += half_weights(loads[0], *loads[2:4]) + [jax.ShapeDtypeStruct(x.shape, x.dtype) for x in loads[4:]]
        scratch.append(pltpu.SemaphoreType.DMA((6 + len(loads[4:]),)))
    return call(
        functools.partial(gradients_body, far, block, half, own, count, len(loads)),
        ("mine" if own else "theirs") + f"_{half}",
        [ANYWHERE] + [VMEM] * (5 + 2 * count) + [ANYWHERE] * len(loads),
        [VMEM] * len(outs),
        outs,
        scratch=scratch,
    )(token, valid, x_turned, gout, gskip, past_head, *(p[1] for p in pieces), *(p[2] for p in pieces), *sources)


def outputs_body(counts, token, valid, sig, w_res_0, w_skip_0, w_res_1, w_skip_1, b_res, b_skip, *refs):
    first, second = refs[: counts[0]], refs[counts[0] : sum(counts)]
    out, skip, mark, rooms, sems = refs[sum(counts) :]
    copies = []
    for i in range(sig.shape[0] // ROWS):
        rows = slice(i * ROWS, (i + 1) * ROWS)
        mask = column(lines_of(valid, rows))
        left, right = picked(first, rows), picked(second, rows)
        branch = dot(left, w_res_0[...]) + dot(right, w_res_1[...]) + b_res[...]
        rooms[i, 0] = (sig[rows, :].astype(F32) + mask * branch).astype(BF16)
        side = dot(left, w_skip_0[...]) + dot(right, w_skip_1[...]) + b_skip[...]
        rooms[i, 1] = (mask * side).astype(BF16)
        for k, ref in enumerate((out, skip)):
            copies.append(pltpu.make_async_copy(rooms.at[i, k], ref.at[pl.ds(i * ROWS, ROWS)], sems.at[i, k]))
            copies[-1].start()
    mark[...] = jnp.zeros_like(mark)
    for copy in copies:
        copy.wait()


def outputs(token, valid, sig, gated_0, gated_1, weights_0, weights_1, b_res, b_skip):
    rows, width = sig.shape
    counts = (len(gated_0), len(gated_1))
    return call(
        functools.partial(outputs_body, counts),
        "outputs",
        [ANYWHERE] + [VMEM] * (8 + sum(counts)),
        [ANYWHERE, ANYWHERE, VMEM],
        [
            jax.ShapeDtypeStruct((rows, width), BF16),
            jax.ShapeDtypeStruct((rows, weights_0[1].shape[1]), BF16),
            MARK,
        ],
        scratch=[
            pltpu.VMEM((rows // ROWS, 2, ROWS, width), BF16),
            pltpu.SemaphoreType.DMA((rows // ROWS, 2)),
        ],
    )(token, valid, sig, *weights_0, *weights_1, b_res, b_skip, *gated_0, *gated_1)


def inputs_body(steps, counts, token, received, gout, pos, w_in_0, w_in_1, w_cond, *refs):
    first, second = refs[: counts[0]], refs[counts[0] : sum(counts)]
    gsig, gfeat, mark, room, room_feat, sems = refs[-6:]
    rows, width = gout.shape
    copies = []
    wide = 2 * LANES

    def copy(source, target):
        copies.append(pltpu.make_async_copy(source, target, sems.at[len(copies)]))
        copies[-1].start()

    for i, step in enumerate(steps):
        begin = step * ROWS
        here = slice(begin, begin + ROWS)
        after = slice(begin + DILATION_STEP, min(begin + DILATION_STEP + ROWS, rows))
        now = [picked(pieces, here) for pieces in (first, second)]
        later = [picked(pieces, after) for pieces in (first, second)]
        tap = column(tap_of(lines_of(pos, after)))
        room_feat[i] = against(w_cond[...], side_by_side(*now))
        copy(room_feat.at[i], gfeat.at[:, pl.ds(begin, ROWS)])
        for k in range(width // wide):
            some = slice(k * wide, (k + 1) * wide)
            tail = tap * (against(later[0], w_in_0[some, :]) + against(later[1], w_in_1[some, :]))
            if tail.shape[0] < ROWS:
                tail = below(tail, received[:, some].astype(F32))
            below_past = slice(width + k * wide, width + (k + 1) * wide)
            own = against(now[0], w_in_0[below_past, :]) + against(now[1], w_in_1[below_past, :])
            room[i, k] = gout[here, some].astype(F32) + own + tail
            copy(room.at[i, k], gsig.at[pl.ds(begin, ROWS), pl.ds(k * wide, wide)])
    mark[...] = jnp.zeros_like(mark)
    for one in copies:
        one.wait()


def inputs(steps, token, received, gout, pos, dpre_0, dpre_1, w_in_0, w_in_1, w_cond, before):
    rows, width = gout.shape
    cond = w_cond.shape[0]
    count = width // (2 * LANES)
    counts = (len(dpre_0), len(dpre_1))
    operands = 7 + sum(counts)
    return call(
        functools.partial(inputs_body, steps, counts),
        f"inputs_{steps[0]}",
        [ANYWHERE] + [VMEM] * (operands - 1) + [ANYWHERE] * len(before),
        [ANYWHERE, ANYWHERE, VMEM],
        [
            jax.ShapeDtypeStruct((rows, width), F32),
            jax.ShapeDtypeStruct((cond, rows), F32),
            MARK,
        ],
        scratch=[
            pltpu.VMEM((len(steps), count, ROWS, 2 * LANES), F32),
            pltpu.VMEM((len(steps), cond, ROWS), F32),
            pltpu.SemaphoreType.DMA((len(steps) * (count + 1),)),
        ],
        aliases={operands + k: k for k in range(len(before))},
    )(token, received, gout, pos, w_in_0, w_in_1, w_cond, *dpre_0, *dpre_1, *before)


SHARES = ((0, 3), (1, 2))


def unpack_body(far, block, token, *refs):
    blocks, arrays, (mark, room) = refs[: 2 * len(SHARES)], refs[-9:-2], refs[-2:]
    mine, theirs = blocks[: len(SHARES)], blocks[len(SHARES) :]
    mark[...] = jnp.zeros_like(mark)
    core, z, xy = own_place()

    @pl.when(pl.program_id(0) == 0)
    def _():
        for k, parts in ((core, mine), (1 - core, theirs)):
            for share, ref in zip(SHARES, parts):
                for i, c in enumerate(share):
                    for r in range(far):
                        rows = pl.ds(pl.multiple_of((k * far + (r ^ z)) * block, 16), block)
                        room[c ^ xy, rows, :] = ref[i, turned(r, far)]

    c = pl.program_id(0)
    top = 0
    for ref in arrays:
        count = ref.shape[0]
        size = max(count, ONES)
        ref[...] = room[c, top : top + size, :].astype(F32)[:count]
        top += size


def unpack(half, token, far, block, mine, theirs, width, cond, hidden, skip_width, before):
    part = hidden // HALVES
    gates = 2 * hidden
    own = (width, skip_width)[half]

    per = part // LANES

    def wide(size):
        return pl.BlockSpec((size, LANES), lambda s: (0, (s // per * HALVES + half) * per + s % per))

    def tall(size):
        return pl.BlockSpec((part, size // NEAR), lambda s: (half, s))

    specs = [wide(width), wide(width), wide(cond), wide(1), tall(width), tall(skip_width), pl.BlockSpec((1, own // NEAR), lambda s: (0, s))]
    shapes = [(width, gates), (width, gates), (cond, gates), (1, gates), (hidden, width), (hidden, skip_width), (1, own)]
    blocks = [VMEM] * (len(mine) + len(theirs))
    return call(
        functools.partial(unpack_body, far, block),
        f"unpack_{half}",
        [ANYWHERE, *blocks] + [ANYWHERE] * len(before),
        specs + [pl.BlockSpec(MARK.shape, lambda s: (0, 0))],
        [jax.ShapeDtypeStruct(shape, F32) for shape in shapes] + [MARK],
        scratch=[pltpu.VMEM((NEAR, 2 * far * block, LANES), BF16)],
        aliases={1 + len(blocks) + k: k for k in range(len(before))},
        grid=(NEAR,),
    )(token, *mine, *theirs, *before)


def swapped(x, axis, k):
    return lax.ppermute(x, axis, [(i, i ^ k) for i in range(lax.axis_size(axis))])


def exchanged(blocks):
    return [swapped(block, "near", k + 1) for k, block in enumerate(blocks)]


def add_body(sizes, token, *refs):
    count = len(sizes)
    kept, got, outs = refs[0], refs[1:-count], refs[-count:]
    at = 0
    for out, size in zip(outs, sizes):
        for k in range(size):
            total = kept[at + k].astype(F32)
            for ref in got:
                total = total + ref[at + k].astype(F32)
            out[k] = total.astype(out.dtype)
        at += size


def added(name, token, kept, got, outs):
    sizes = [size for size, _ in outs]
    result = call(
        functools.partial(add_body, sizes),
        name,
        [ANYWHERE] + [VMEM] * (1 + len(got)),
        [VMEM] * len(outs),
        [jax.ShapeDtypeStruct((size, *kept.shape[1:]), dtype) for size, dtype in outs],
    )(token, kept, *got)
    return result


def mirror_body(token, mine, got, out):
    count = mine.shape[0]
    for k in range(count):
        out[k] = (mine[k].astype(F32) + got[count - 1 - k].astype(F32)).astype(out.dtype)


def mirrored(name, token, mine, got):
    return call(
        mirror_body,
        name,
        [ANYWHERE, VMEM, VMEM],
        VMEM,
        jax.ShapeDtypeStruct(mine.shape, BF16),
    )(token, mine, got)


def join_body(token, *refs):
    out = refs[-1]
    at = 0
    for ref in refs[:-1]:
        out[at : at + ref.shape[0]] = ref[...]
        at += ref.shape[0]


def joined(name, token, parts):
    count = sum(part.shape[0] for part in parts)
    return call(
        join_body,
        name,
        [ANYWHERE] + [VMEM] * len(parts),
        VMEM,
        jax.ShapeDtypeStruct((count, *parts[0].shape[1:]), BF16),
    )(token, *parts)


def over_outer(total):
    for bit in range((lax.axis_size("outer") - 1).bit_length()):
        total = (total.astype(F32) + swapped(total, "outer", 1 << bit).astype(F32)).astype(BF16)
    return total


def passed_along(x, by):
    peers = lax.axis_size(AXES)
    pairs = [(i, i + by) for i in range(peers) if 0 <= i + by < peers]
    return lax.ppermute(x, AXES, pairs)


def in_hbm(x):
    return pltpu.with_memory_space_constraint(x, pltpu.HBM)


def body(
    signal,
    features,
    position,
    valid,
    w_past,
    w_now,
    b_conv,
    w_cond,
    w_res,
    b_res,
    w_skip,
    b_skip,
    grad_out,
    grad_skip,
):
    rows, width = signal.shape
    features = features.T
    cond = features.shape[0]
    hidden = w_res.shape[0]
    skip_width = w_skip.shape[1]
    far = lax.axis_size("far")
    far_bits = (far - 1).bit_length()
    used = 2 * width + cond + ONES + 2 * (hidden // HALVES) + ONES
    block = -(-used // (2 * far * 16)) * 16
    lines = (rows // LANES, LANES)
    pos, val = position.reshape(lines), valid.reshape(lines)
    b_conv, b_res, b_skip = (b.reshape(1, -1) for b in (b_conv, b_res, b_skip))

    def core_sum(half, token, theirs, mine):
        kept, *sent = added(
            f"core_sum_{half}", token, mine, [swapped(theirs, "core", 1)], [(1, F32)] + [(1, BF16)] * (NEAR - 1)
        )
        return kept[0], exchanged([x[0] for x in sent])

    def near_sum(half, token, kept, got):
        kept, sent = added(f"near_sum_{half}", token, kept, got, [(far // 2, F32), (far // 2, BF16)])
        return kept, swapped(sent, "far", 1)

    def far_sum(half, token, kept, got):
        for bit in range(1, far_bits - 1):
            size = kept.shape[0] // 2
            kept, sent = added(f"far_sum_{half}_{bit}", token, kept, [got], [(size, F32), (size, BF16)])
            got = swapped(sent, "far", 1 << bit)
        (mine,) = added(f"far_sum_{half}", token, kept, [got], [(kept.shape[0], BF16)])
        return mine, swapped(mine, "far", 1 << (far_bits - 1))

    def far_end(half, token, mine, got):
        total = over_outer(mirrored(f"far_end_{half}", token, mine, got))
        return total, swapped(total, "far", 1 << (far_bits - 2))

    def far_join(half, token, mine, got):
        total = joined(f"far_join_{half}", token, [mine, got])
        for bit in reversed(range(far_bits - 2)):
            total = joined(f"far_join_{half}_{bit}", token, [total, swapped(total, "far", 1 << bit)])
        return total, exchanged([total] * (NEAR - 1))

    def near_join(half, k, token, mine, got):
        blocks = [mine, *got]
        total = joined(f"near_join_{half}_{k}", token, [blocks[c][None] for c in SHARES[k]])
        return total, swapped(total, "core", 1)

    def input_gradients(steps, token, before):
        last = (steps[-1] + 1) * ROWS == rows
        return inputs(steps, token, received if last else head_0[0], grad_out, pos, dpre_0, dpre_1, w_in_0, w_in_1, w_cond, before)

    halo = passed_along(signal[rows - DILATION_STEP :], 1)
    loads = (w_past, w_now, w_res, w_skip, b_res, b_skip)
    val, pos, b_conv, w_cond, w_in_0, *outer_0, past, signal, x_turned, grad_out, grad_skip, a, b, c = load(
        val, pos, b_conv, features, w_cond, w_res, w_skip, w_past, w_now, signal, grad_out, grad_skip
    )
    rest_0 = (a, b, c)
    common = (signal, x_turned, grad_out, grad_skip)
    past_head, head_0 = head(halo, pos, val, *common, w_in_0, w_cond, b_conv, *outer_0)
    made_0 = (head_0, rest_0)
    fixed = (far, block, val, x_turned, grad_out, grad_skip, past_head)
    theirs_0, w_in_1, *outer_1, b_res, b_skip = gradients(0, False, past_head, *fixed, made_0, loads)
    weights_1 = (w_in_1, w_cond, b_conv, *outer_1)
    (mine_0,) = gradients(0, True, theirs_0, *fixed, made_0)
    most_1 = forward_most(mine_0, val, past, *common, *weights_1)
    kept_0, got_0 = core_sum(0, most_1[0], theirs_0, mine_0)
    head_1, last_1 = forward_ends(kept_0, halo, pos, val, past, *common, *weights_1)
    made_1 = (head_1, most_1, last_1)
    dpre_0, dpre_1 = ([p[2] for p in made] for made in (made_0, made_1))
    (theirs_1,) = gradients(1, False, kept_0, *fixed, made_1)
    (mine_1,) = gradients(1, True, theirs_1, *fixed, made_1)
    kept_0, got_0 = near_sum(0, mine_1, kept_0, got_0)
    kept_1, got_1 = core_sum(1, kept_0, theirs_1, mine_1)
    ends_0, got_0 = far_sum(0, kept_1, kept_0, got_0)
    *grads, mark = input_gradients((0, 1), ends_0, [])
    ends_0, got_0 = far_end(0, mark, ends_0, got_0)
    kept_1, got_1 = near_sum(1, ends_0, kept_1, got_1)
    ends_0, got_0 = far_join(0, kept_1, ends_0, got_0)
    ends_1, got_1 = far_sum(1, ends_0, kept_1, got_1)
    output, skip_out, mark = outputs(
        ends_1, val, signal, [p[0] for p in made_0], [p[0] for p in made_1], outer_0, outer_1, b_res, b_skip
    )
    ends_1, got_1 = far_end(1, mark, ends_1, got_1)
    early = early_rows(ends_1, pos, head_0[2], head_1[2], w_in_0, w_in_1)
    received = passed_along(early, -1)
    first = near_join(0, 0, early, ends_0, got_0)
    second = near_join(0, 1, first[0], ends_0, got_0)
    pairs_0 = [first, second]
    ends_1, got_1 = far_join(1, second[0], ends_1, got_1)
    *grads, mark = input_gradients((2, 3), ends_1, grads)
    first = near_join(1, 0, mark, ends_1, got_1)
    second = near_join(1, 1, first[0], ends_1, got_1)
    pairs_1 = [first, second]
    sizes = (width, cond, hidden, skip_width)
    *done, own_0, mark = unpack(0, first[1], far, block, *zip(*pairs_0), *sizes, [])
    *done, own_1, _ = unpack(1, mark, far, block, *zip(*pairs_1), *sizes, done)
    g_past, g_now, g_cond, g_bias, g_res, g_skip = done
    grad_signal, grad_features = grads
    return (
        output,
        skip_out,
        grad_signal,
        grad_features.T,
        g_past,
        g_now,
        g_bias.reshape(-1),
        g_cond,
        g_res,
        own_0.reshape(-1),
        g_skip,
        own_1.reshape(-1),
    )


def solution(mesh):
    row, col = mesh.shape["row"], mesh.shape["col"]
    fine = Mesh(mesh.devices.reshape(row // 2, 2, col // NEAR, NEAR), AXES)
    rows = P(AXES, None)
    line = P(AXES)
    return jax.shard_map(
        body,
        mesh=fine,
        in_specs=(rows, rows, line, line) + (P(),) * 8 + (rows, rows),
        out_specs=(rows,) * 4 + (P(),) * 8,
        check_vma=False,
    )
```

```python
import functools

import jax
import jax.numpy as jnp
from jax import lax
from jax.experimental import pallas as pl
from jax.experimental.pallas import tpu as pltpu
from jax.sharding import Mesh
from jax.sharding import PartitionSpec as P

DILATION_STEP = 256
AXES = ("outer", "core", "far", "near")
HALVES = 2
NEAR = 4
LANES = 128
ROWS = 512
ONES = 16
F32 = jnp.float32
BF16 = jnp.bfloat16
MEGA = 1 << 20
COSTS = {
    "load": 8, "head": 2, "near_sum_0": 7, "mine_1": 2, "near_part_0": 1,
    "near_part_1": 2, "near_sum_1": 4, "near_join_0_1": 2, "near_join_1_1": 4, "far_join_0": 4,
}
FLOPS = 10**9


def dot(left, right):
    return jnp.dot(left, right, preferred_element_type=F32)


def across(left, right):
    return lax.dot_general(left, right, (((0,), (0,)), ((), ())), preferred_element_type=F32)


def against(left, weight):
    return lax.dot_general(left, weight, (((1,), (1,)), ((), ())), preferred_element_type=F32)


def column(lines):
    turned = lines.astype(F32).T
    return jnp.concatenate([turned[:, k : k + 1] for k in range(lines.shape[0])], axis=0)


def row(lines):
    return jnp.concatenate([lines[k : k + 1] for k in range(lines.shape[0])], axis=1)


def tap_of(lines):
    return jnp.where(lines >= DILATION_STEP, 1, 0)


def lines_of(ref, rows):
    return ref[rows.start // LANES : rows.stop // LANES, :]


def picked(pieces, rows):
    found, at = [], 0
    for ref in pieces:
        low, high = max(rows.start, at), min(rows.stop, at + ref.shape[0])
        if low < high:
            found.append(ref[low - at : high - at, :])
        at += ref.shape[0]
    return found[0] if len(found) == 1 else jnp.concatenate(found, axis=0)


def call(kernel, name, in_specs, out_specs, out_shape, scratch=(), aliases=None, grid=(), vmem=24):
    return pl.pallas_call(
        kernel,
        grid=grid,
        in_specs=in_specs,
        out_specs=out_specs,
        out_shape=out_shape,
        scratch_shapes=list(scratch),
        input_output_aliases=aliases or {},
        cost_estimate=pl.CostEstimate(
            flops=1 + int(FLOPS * COSTS.get(name, COSTS.get(name.split("_")[0], 0))), bytes_accessed=1, transcendentals=0
        ),
        name=name,
        compiler_params=pltpu.CompilerParams(vmem_limit_bytes=vmem * MEGA),
    )


VMEM = pl.BlockSpec(memory_space=pltpu.VMEM)
ANYWHERE = pl.BlockSpec(memory_space=pl.ANY)
MARK = jax.ShapeDtypeStruct((8, LANES), F32)


def beside(*parts):
    return jnp.concatenate(parts, axis=1)


def below(*parts):
    return jnp.concatenate(parts, axis=0)


def gate_product(half, k, rows, past, sig, feats, w_in, w_cond, b_conv):
    width = sig.shape[1]
    part = w_in.shape[1] // 2
    here = slice(k * part, (k + 1) * part)
    there = slice((k * HALVES + half) * part, (k * HALVES + half + 1) * part)
    own = dot(past, w_in[:width, here]) + dot(sig[rows, :], w_in[width:, here])
    return own + across(feats, w_cond[:, there]) + b_conv[:, there]


def back_product(rows, gout, gskip, w_res, w_skip):
    return against(gout[rows, :], w_res[...]) + against(gskip[rows, :], w_skip[...])


def weight_copies(half, w_past, w_now, w_res, w_skip, w_in_to, w_res_to, w_skip_to):
    width = w_past.shape[0]
    part = w_res_to.shape[0]
    pairs = []
    for k in range(2):
        here = pl.ds((k * HALVES + half) * part, part)
        for i, ref in enumerate((w_past, w_now)):
            pairs.append((ref.at[:, here], w_in_to.at[pl.ds(i * width, width), pl.ds(k * part, part)]))
    rows = pl.ds(half * part, part)
    return pairs + [(w_res.at[rows], w_res_to), (w_skip.at[rows], w_skip_to)]


def half_weights(w_past, w_res, w_skip):
    part = w_res.shape[0] // HALVES
    shapes = ((2 * w_past.shape[0], 2 * part), (part, w_res.shape[1]), (part, w_skip.shape[1]))
    return [jax.ShapeDtypeStruct(shape, BF16) for shape in shapes]


def finish(pre_a, pre_s, dgated, valid_lines):
    act = jnp.tanh(pre_a)
    gate = 0.5 + 0.5 * jnp.tanh(0.5 * pre_s)
    slope = (column(valid_lines) * dgated) * gate
    dpre = beside(slope * (1.0 - act * act), slope * act * (1.0 - gate)).astype(BF16)
    gated = (act * gate).astype(BF16)
    return gated, gated.T * row(valid_lines.astype(BF16)), dpre


def forward_tiles(half, tiles, prepare, arrive, valid, past, sig, x_turned, gout, gskip, weights, outs, base):
    w_in, w_cond, b_conv, w_res, w_skip = weights
    gated_out, kept_out, dpre_out = outs
    cond = w_cond.shape[0]
    width = sig.shape[1]

    def product(rows, k):
        if arrive:
            arrive(rows, k)
        if k == 2:
            return back_product(rows, gout, gskip, w_res, w_skip)
        feats = x_turned[2 * width : 2 * width + cond, rows]
        return gate_product(half, k, rows, past[rows, :], sig, feats, w_in, w_cond, b_conv)

    def done(rows, made):
        there = slice(rows.start - base, rows.stop - base)
        gated_out[there, :], kept_out[:, there], dpre_out[there, :] = finish(*made, lines_of(valid, rows))

    ahead = None
    for rows in tiles:
        if prepare:
            prepare(rows)
        made = [product(rows, k) for k in range(3)]
        if ahead:
            done(*ahead)
        ahead = (rows, made)
    done(*ahead)


def tiles_of(start, stop):
    return [slice(a, a + DILATION_STEP) for a in range(start, stop, DILATION_STEP)]


def load_body(
    valid, pos, b_conv, feat, w_cond, w_res, w_skip, w_past, w_now, sig, gout, gskip,
    valid_to, pos_to, b_conv_to, w_cond_to, w_in, w_res_to, w_skip_to, past, sig_to, x_turned,
    gout_to, gskip_to, gated_rest, kept_rest, dpre_rest, sems,
):
    rows_all, width = sig.shape
    cond = feat.shape[0]
    count = 0

    def start(source, target):
        nonlocal count
        copy = pltpu.make_async_copy(source, target, sems.at[count])
        copy.start()
        count += 1
        return copy

    def tile(i, source, target):
        rows = pl.ds(i * ROWS, ROWS)
        return start(source.at[rows], target.at[rows])

    weights = weight_copies(0, w_past, w_now, w_res, w_skip, w_in, w_res_to, w_skip_to)
    signals = [[tile(0, sig, sig_to)]]
    needs = [
        [
            start(pos, pos_to),
            *(start(*pair) for pair in weights[:2]),
            start(feat, x_turned.at[pl.ds(2 * width, cond)]),
            start(w_cond, w_cond_to),
            start(b_conv, b_conv_to),
        ],
        [start(*pair) for pair in weights[2:4]],
        [start(valid, valid_to), *(start(*pair) for pair in weights[4:])],
    ]
    cotangents = [[tile(0, gout, gout_to), tile(0, gskip, gskip_to)]]
    for i in range(1, rows_all // ROWS):
        signals.append([tile(i, sig, sig_to)])
        cotangents.append([tile(i, gout, gout_to), tile(i, gskip, gskip_to)])

    def wait(copies):
        for copy in copies:
            copy.wait()
        copies.clear()

    def prepare(rows):
        i = rows.start // ROWS
        wait(signals[i])
        wait(needs[0])
        whole = rows if i else slice(0, rows.stop)
        before = slice(rows.start - DILATION_STEP, rows.stop - DILATION_STEP)
        tap = tap_of(lines_of(pos_to, rows)).astype(F32)
        past[rows, :] = sig_to[before, :] * column(tap).astype(BF16)
        x_turned[width : 2 * width, whole] = sig_to[whole, :].T
        x_turned[:width, rows] = x_turned[width : 2 * width, before] * row(tap).astype(BF16)

    def arrive(rows, k):
        wait(needs[k])
        if k == 2:
            wait(cotangents[rows.start // ROWS])

    x_turned[2 * width + cond :, :] = jnp.ones((x_turned.shape[0] - 2 * width - cond, rows_all), BF16)
    forward_tiles(
        0, tiles_of(DILATION_STEP, rows_all), prepare, arrive, valid_to, past, sig_to, x_turned, gout_to, gskip_to,
        (w_in, w_cond_to, b_conv_to, w_res_to, w_skip_to), (gated_rest, kept_rest, dpre_rest), DILATION_STEP,
    )


def rest_shapes(rest, part):
    return [jax.ShapeDtypeStruct(shape, BF16) for shape in ((rest, part), (part, rest), (rest, 2 * part))]


def load(*arrays):
    sources = [in_hbm(x) for x in arrays]
    feat, w_cond, w_res, w_skip, w_past, _, sig, gout, gskip = arrays[3:]
    rows, width = sig.shape
    hidden = w_res.shape[0]
    shapes = [jax.ShapeDtypeStruct(x.shape, x.dtype) for x in arrays[:3] + (w_cond,)]
    shapes += half_weights(w_past, w_res, w_skip) + [
        jax.ShapeDtypeStruct(shape, BF16)
        for shape in (
            sig.shape, sig.shape, (2 * width + feat.shape[0] + ONES, rows), gout.shape, gskip.shape,
        )
    ]
    shapes += rest_shapes(rows - DILATION_STEP, hidden // HALVES)
    return call(
        load_body,
        "load",
        [ANYWHERE] * len(sources),
        [VMEM] * len(shapes),
        shapes,
        scratch=[pltpu.SemaphoreType.DMA((11 + 3 * (rows // ROWS),))],
    )(*sources)


def side_by_side(dpre_0, dpre_1):
    part = dpre_0.shape[1] // 2
    return beside(dpre_0[:, :part], dpre_1[:, :part], dpre_0[:, part:], dpre_1[:, part:])


def head_rows(half, halo, pos, valid, sig, x_turned, gout, gskip, weights, outs):
    w_in, w_cond, b_conv, w_res, w_skip = weights
    rows = slice(0, DILATION_STEP)
    width = halo.shape[1]
    feats = x_turned[2 * width : 2 * width + w_cond.shape[0], rows]
    past = halo[...] * column(tap_of(lines_of(pos, rows)).astype(F32)).astype(BF16)
    made = [gate_product(half, k, rows, past, sig, feats, w_in, w_cond, b_conv) for k in range(2)]
    made.append(back_product(rows, gout, gskip, w_res, w_skip))
    for ref, value in zip(outs, finish(*made, lines_of(valid, rows))):
        ref[...] = value


def head_body(halo, pos, valid, sig, x_turned, gout, gskip, w_in, w_cond, b_conv, w_res, w_skip, past_out, *outs):
    tap = tap_of(lines_of(pos, slice(0, DILATION_STEP))).astype(F32)
    past_out[...] = halo[...].T * row(tap).astype(BF16)
    head_rows(0, halo, pos, valid, sig, x_turned, gout, gskip, (w_in, w_cond, b_conv, w_res, w_skip), outs)


def head(halo, *args):
    width = halo.shape[1]
    part = args[-1].shape[0]
    past, *parts = call(
        head_body,
        "head",
        [VMEM] * (1 + len(args)),
        [VMEM] * 4,
        [jax.ShapeDtypeStruct((width, DILATION_STEP), BF16)] + rest_shapes(DILATION_STEP, part),
    )(halo, *args)
    return past, parts


def early_body(token, pos, dpre_0, dpre_1, w_in_0, w_in_1, early):
    tap = column(tap_of(lines_of(pos, slice(0, DILATION_STEP))))
    some = slice(0, early.shape[1])
    early[...] = (tap * (against(dpre_0[...], w_in_0[some, :]) + against(dpre_1[...], w_in_1[some, :]))).astype(BF16)


def early_rows(token, pos, dpre_0, dpre_1, w_in_0, w_in_1):
    return call(
        early_body,
        "early",
        [ANYWHERE] + [VMEM] * 5,
        VMEM,
        jax.ShapeDtypeStruct((DILATION_STEP, w_in_0.shape[0] // 2), BF16),
    )(token, pos, dpre_0, dpre_1, w_in_0, w_in_1)


def forward_body(token, halo, pos, valid, past, sig, x_turned, gout, gskip, w_in, w_cond, b_conv, w_res, w_skip, *outs):
    weights = (w_in, w_cond, b_conv, w_res, w_skip)
    head_rows(1, halo, pos, valid, sig, x_turned, gout, gskip, weights, outs[:3])
    forward_tiles(
        1, tiles_of(DILATION_STEP, sig.shape[0]), None, None, valid, past, sig, x_turned, gout, gskip, weights, outs[3:],
        DILATION_STEP,
    )


def forward_1(token, *args):
    part = args[-1].shape[0]
    parts = call(
        forward_body,
        "forward_1",
        [ANYWHERE] + [VMEM] * len(args),
        [VMEM] * 6,
        rest_shapes(DILATION_STEP, part) + rest_shapes(args[4].shape[0] - DILATION_STEP, part),
    )(token, *args)
    return parts[:3], parts[3:]


GROUPS = (((3, 1), (2, 0)), ((1, 2, 3, 0),))


def own_place():
    return [lax.axis_index(name) for name in ("core", "far", "near")]


def turned(index, count):
    bits = (count - 1).bit_length()
    result = 0
    for bit in range(bits):
        result = result | (((index >> bit) & 1) << (bits - 1 - bit))
    return result


def gradients_body(far, block, half, own, count, extra, token, valid, x_turned, gout, gskip, past_head, *refs):
    kepts, dpres, refs = refs[:count], refs[count : 2 * count], refs[2 * count :]
    groups = GROUPS[half]
    sources, outs = refs[:extra], refs[extra : len(refs) - 1 - bool(extra)]
    outs, targets = outs[: len(groups)], outs[len(groups) :]
    acc = refs[-1 - bool(extra)]
    copies = []
    if extra:
        pairs = weight_copies(1, *sources[:4], *targets[:3]) + list(zip(sources[4:], targets[3:]))
        copies = [pltpu.make_async_copy(*pair, refs[-1].at[k]) for k, pair in enumerate(pairs)]
    for copy in copies:
        copy.start()
    width = past_head.shape[0]
    part = kepts[0].shape[0]
    ends, rows = x_turned.shape
    size = far * block
    core, z, xy = own_place()
    which = core if own else 1 - core

    def product(left_of, rights):
        total, at = None, 0
        for k, right in enumerate(rights):
            here = slice(at, at + right.shape[0])
            made = dot(left_of(here, k), right[...])
            total = made if at == 0 else total + made
            at = here.stop
        return total

    def region(k):
        low, high = k * size, min((k + 1) * size, ends)

        def turned_rows(here, piece):
            if piece == 0 and low < width:
                return below(past_head[low : min(high, width), :], x_turned[width : max(high, width), here])
            return x_turned[low:high, here]

        def keep(first, value):
            for c in range(NEAR):
                acc[c, first : first + value.shape[0], :] = value[:, c * LANES : (c + 1) * LANES]

        keep(0, product(turned_rows, dpres))
        at = high - low
        if high == ends:
            mask = jnp.broadcast_to(row(lines_of(valid, slice(0, rows)).astype(F32)).astype(BF16), (ONES, rows))

            def kept_rows(here, piece):
                return below(kepts[piece][...], mask[:, here])

            for i, ref in enumerate((gout, gskip)):
                cuts = [0]
                for kept in kepts:
                    cuts.append(cuts[-1] + kept.shape[1])
                made = product(kept_rows, [ref.at[pl.ds(a, b - a)] for a, b in zip(cuts, cuts[1:])])
                keep(at, made[:part])
                at += part
                if i == half:
                    keep(high - low + 2 * part, made[part:])
            at += ONES
            acc[:, at:, :] = jnp.zeros((NEAR, size - at, LANES), F32)
        for group, out in zip(groups, outs):
            for i, p in enumerate(group):
                for r in range(far):
                    out[i, turned(r ^ z, far)] = acc[xy ^ p, r * block : (r + 1) * block, :].astype(out.dtype)

    for k in range(2):
        pl.when(which == k)(functools.partial(region, k))
    for copy in copies:
        copy.wait()


def gradients(half, own, token, far, block, valid, x_turned, gout, gskip, past_head, pieces, loads=()):
    count = len(pieces)
    sources = [in_hbm(x) for x in loads]
    outs = [jax.ShapeDtypeStruct((len(group), far, block, LANES), F32 if own else BF16) for group in GROUPS[half]]
    scratch = [pltpu.VMEM((NEAR, far * block, LANES), F32)]
    if loads:
        outs += half_weights(loads[0], *loads[2:4]) + [jax.ShapeDtypeStruct(x.shape, x.dtype) for x in loads[4:]]
        scratch.append(pltpu.SemaphoreType.DMA((6 + len(loads[4:]),)))
    return call(
        functools.partial(gradients_body, far, block, half, own, count, len(loads)),
        ("mine" if own else "theirs") + f"_{half}",
        [ANYWHERE] + [VMEM] * (5 + 2 * count) + [ANYWHERE] * len(loads),
        [VMEM] * len(outs),
        outs,
        scratch=scratch,
    )(token, valid, x_turned, gout, gskip, past_head, *(p[1] for p in pieces), *(p[2] for p in pieces), *sources)


def outputs_body(counts, token, valid, sig, w_res_0, w_skip_0, w_res_1, w_skip_1, b_res, b_skip, *refs):
    first, second = refs[: counts[0]], refs[counts[0] : sum(counts)]
    out, skip, mark, rooms, sems = refs[sum(counts) :]
    copies = []
    for i in range(sig.shape[0] // ROWS):
        rows = slice(i * ROWS, (i + 1) * ROWS)
        mask = column(lines_of(valid, rows))
        left, right = picked(first, rows), picked(second, rows)
        branch = dot(left, w_res_0[...]) + dot(right, w_res_1[...]) + b_res[...]
        rooms[i, 0] = (sig[rows, :].astype(F32) + mask * branch).astype(BF16)
        side = dot(left, w_skip_0[...]) + dot(right, w_skip_1[...]) + b_skip[...]
        rooms[i, 1] = (mask * side).astype(BF16)
        for k, ref in enumerate((out, skip)):
            copies.append(pltpu.make_async_copy(rooms.at[i, k], ref.at[pl.ds(i * ROWS, ROWS)], sems.at[i, k]))
            copies[-1].start()
    mark[...] = jnp.zeros_like(mark)
    for copy in copies:
        copy.wait()


def outputs(token, valid, sig, gated_0, gated_1, weights_0, weights_1, b_res, b_skip):
    rows, width = sig.shape
    counts = (len(gated_0), len(gated_1))
    return call(
        functools.partial(outputs_body, counts),
        "outputs",
        [ANYWHERE] + [VMEM] * (8 + sum(counts)),
        [ANYWHERE, ANYWHERE, VMEM],
        [
            jax.ShapeDtypeStruct((rows, width), BF16),
            jax.ShapeDtypeStruct((rows, weights_0[1].shape[1]), BF16),
            MARK,
        ],
        scratch=[
            pltpu.VMEM((rows // ROWS, 2, ROWS, width), BF16),
            pltpu.SemaphoreType.DMA((rows // ROWS, 2)),
        ],
    )(token, valid, sig, *weights_0, *weights_1, b_res, b_skip, *gated_0, *gated_1)


def inputs_body(steps, counts, token, received, gout, pos, w_in_0, w_in_1, w_cond, *refs):
    first, second = refs[: counts[0]], refs[counts[0] : sum(counts)]
    gsig, gfeat, mark, room, room_feat, sems = refs[-6:]
    rows, width = gout.shape
    copies = []
    wide = 2 * LANES

    def copy(source, target):
        copies.append(pltpu.make_async_copy(source, target, sems.at[len(copies)]))
        copies[-1].start()

    for i, step in enumerate(steps):
        begin = step * ROWS
        here = slice(begin, begin + ROWS)
        after = slice(begin + DILATION_STEP, min(begin + DILATION_STEP + ROWS, rows))
        now = [picked(pieces, here) for pieces in (first, second)]
        later = [picked(pieces, after) for pieces in (first, second)]
        tap = column(tap_of(lines_of(pos, after)))
        room_feat[i] = against(w_cond[...], side_by_side(*now))
        copy(room_feat.at[i], gfeat.at[:, pl.ds(begin, ROWS)])
        for k in range(width // wide):
            some = slice(k * wide, (k + 1) * wide)
            tail = tap * (against(later[0], w_in_0[some, :]) + against(later[1], w_in_1[some, :]))
            if tail.shape[0] < ROWS:
                tail = below(tail, received[:, some].astype(F32))
            below_past = slice(width + k * wide, width + (k + 1) * wide)
            own = against(now[0], w_in_0[below_past, :]) + against(now[1], w_in_1[below_past, :])
            room[i, k] = gout[here, some].astype(F32) + own + tail
            copy(room.at[i, k], gsig.at[pl.ds(begin, ROWS), pl.ds(k * wide, wide)])
    mark[...] = jnp.zeros_like(mark)
    for one in copies:
        one.wait()


def inputs(steps, token, received, gout, pos, dpre_0, dpre_1, w_in_0, w_in_1, w_cond, before):
    rows, width = gout.shape
    cond = w_cond.shape[0]
    count = width // (2 * LANES)
    counts = (len(dpre_0), len(dpre_1))
    operands = 7 + sum(counts)
    return call(
        functools.partial(inputs_body, steps, counts),
        f"inputs_{steps[0]}",
        [ANYWHERE] + [VMEM] * (operands - 1) + [ANYWHERE] * len(before),
        [ANYWHERE, ANYWHERE, VMEM],
        [
            jax.ShapeDtypeStruct((rows, width), F32),
            jax.ShapeDtypeStruct((cond, rows), F32),
            MARK,
        ],
        scratch=[
            pltpu.VMEM((len(steps), count, ROWS, 2 * LANES), F32),
            pltpu.VMEM((len(steps), cond, ROWS), F32),
            pltpu.SemaphoreType.DMA((len(steps) * (count + 1),)),
        ],
        aliases={operands + k: k for k in range(len(before))},
    )(token, received, gout, pos, w_in_0, w_in_1, w_cond, *dpre_0, *dpre_1, *before)


SHARES = ((0, 3), (1, 2))


def unpack_body(far, block, token, *refs):
    blocks, arrays, (mark, room) = refs[: 2 * len(SHARES)], refs[-9:-2], refs[-2:]
    mine, theirs = blocks[: len(SHARES)], blocks[len(SHARES) :]
    mark[...] = jnp.zeros_like(mark)
    core, z, xy = own_place()

    @pl.when(pl.program_id(0) == 0)
    def _():
        for k, parts in ((core, mine), (1 - core, theirs)):
            for share, ref in zip(SHARES, parts):
                for i, c in enumerate(share):
                    for r in range(far):
                        rows = pl.ds(pl.multiple_of((k * far + (r ^ z)) * block, 16), block)
                        room[c ^ xy, rows, :] = ref[i, turned(r, far)]

    for j in range(NEAR // 2):
        c = pl.program_id(0) * (NEAR // 2) + j
        here = pl.ds(j * LANES, LANES)
        top = 0
        for ref in arrays:
            count = ref.shape[0]
            size = max(count, ONES)
            ref[:, here] = room[c, top : top + size, :].astype(F32)[:count]
            top += size


def unpack(half, token, far, block, mine, theirs, width, cond, hidden, skip_width, before):
    part = hidden // HALVES
    gates = 2 * hidden
    own = (width, skip_width)[half]

    def wide(size):
        return pl.BlockSpec((size, part), lambda s: (0, HALVES * s + half))

    def tall(size):
        return pl.BlockSpec((part, size // 2), lambda s: (half, s))

    specs = [wide(width), wide(width), wide(cond), wide(1), tall(width), tall(skip_width), pl.BlockSpec((1, own // 2), lambda s: (0, s))]
    shapes = [(width, gates), (width, gates), (cond, gates), (1, gates), (hidden, width), (hidden, skip_width), (1, own)]
    blocks = [pl.BlockSpec(x.shape, lambda s: (0,) * 4) for x in (*mine, *theirs)]
    return call(
        functools.partial(unpack_body, far, block),
        f"unpack_{half}",
        [ANYWHERE, *blocks] + [ANYWHERE] * len(before),
        specs + [pl.BlockSpec(MARK.shape, lambda s: (0, 0))],
        [jax.ShapeDtypeStruct(shape, F32) for shape in shapes] + [MARK],
        scratch=[pltpu.VMEM((NEAR, 2 * far * block, LANES), BF16)],
        aliases={1 + len(blocks) + k: k for k in range(len(before))},
        grid=(2,),
    )(token, *mine, *theirs, *before)


def swapped(x, axis, k):
    return lax.ppermute(x, axis, [(i, i ^ k) for i in range(lax.axis_size(axis))])


def exchanged(blocks):
    return [swapped(block, "near", k + 1) for k, block in enumerate(blocks)]


def add_body(sizes, token, *refs):
    count = len(sizes)
    kept, got, outs = refs[0], refs[1:-count], refs[-count:]
    at = 0
    for out, size in zip(outs, sizes):
        for k in range(size):
            total = kept[at + k].astype(F32)
            for ref in got:
                total = total + ref[at + k].astype(F32)
            out[k] = total.astype(out.dtype)
        at += size


def added(name, token, kept, got, outs):
    sizes = [size for size, _ in outs]
    result = call(
        functools.partial(add_body, sizes),
        name,
        [ANYWHERE] + [VMEM] * (1 + len(got)),
        [VMEM] * len(outs),
        [jax.ShapeDtypeStruct((size, *kept.shape[1:]), dtype) for size, dtype in outs],
    )(token, kept, *got)
    return result


def mirror_body(token, mine, got, out):
    count = mine.shape[0]
    for k in range(count):
        out[k] = (mine[k].astype(F32) + got[count - 1 - k].astype(F32)).astype(out.dtype)


def mirrored(name, token, mine, got):
    return call(
        mirror_body,
        name,
        [ANYWHERE, VMEM, VMEM],
        VMEM,
        jax.ShapeDtypeStruct(mine.shape, BF16),
    )(token, mine, got)


def join_body(token, *refs):
    out = refs[-1]
    at = 0
    for ref in refs[:-1]:
        out[at : at + ref.shape[0]] = ref[...]
        at += ref.shape[0]


def joined(name, token, parts):
    count = sum(part.shape[0] for part in parts)
    return call(
        join_body,
        name,
        [ANYWHERE] + [VMEM] * len(parts),
        VMEM,
        jax.ShapeDtypeStruct((count, *parts[0].shape[1:]), BF16),
    )(token, *parts)


def over_outer(total):
    for bit in range((lax.axis_size("outer") - 1).bit_length()):
        total = (total.astype(F32) + swapped(total, "outer", 1 << bit).astype(F32)).astype(BF16)
    return total


def passed_along(x, by):
    peers = lax.axis_size(AXES)
    pairs = [(i, i + by) for i in range(peers) if 0 <= i + by < peers]
    return lax.ppermute(x, AXES, pairs)


def in_hbm(x):
    return pltpu.with_memory_space_constraint(x, pltpu.HBM)


def body(
    signal,
    features,
    position,
    valid,
    w_past,
    w_now,
    b_conv,
    w_cond,
    w_res,
    b_res,
    w_skip,
    b_skip,
    grad_out,
    grad_skip,
):
    rows, width = signal.shape
    features = features.T
    cond = features.shape[0]
    hidden = w_res.shape[0]
    skip_width = w_skip.shape[1]
    far = lax.axis_size("far")
    far_bits = (far - 1).bit_length()
    used = 2 * width + cond + ONES + 2 * (hidden // HALVES) + ONES
    block = -(-used // (2 * far * 16)) * 16
    lines = (rows // LANES, LANES)
    pos, val = position.reshape(lines), valid.reshape(lines)
    b_conv, b_res, b_skip = (b.reshape(1, -1) for b in (b_conv, b_res, b_skip))

    def core_sum(half, token, theirs, mine):
        got = {}
        for k, group in enumerate(GROUPS[half]):
            blocks = added(
                f"core_sum_{half}_{k}", token, mine[k], [swapped(theirs[k], "core", 1)],
                [(1, BF16 if p else F32) for p in group],
            )
            token = blocks[0]
            for p, part in zip(group, blocks):
                got[p] = swapped(part[0], "near", p) if p else part[0]
        return got[0], [got[p] for p in range(1, NEAR)]

    def near_sum(half, token, kept, got):
        kept, sent = added(f"near_sum_{half}", token, kept, got, [(far // 2, F32), (far // 2, BF16)])
        return kept, swapped(sent, "far", 1)

    def far_sum(half, token, kept, got):
        for bit in range(1, far_bits - 1):
            size = kept.shape[0] // 2
            kept, sent = added(f"far_sum_{half}_{bit}", token, kept, [got], [(size, F32), (size, BF16)])
            got = swapped(sent, "far", 1 << bit)
        (mine,) = added(f"far_sum_{half}", token, kept, [got], [(kept.shape[0], BF16)])
        return mine, swapped(mine, "far", 1 << (far_bits - 1))

    def far_end(half, token, mine, got):
        total = over_outer(mirrored(f"far_end_{half}", token, mine, got))
        return total, swapped(total, "far", 1 << (far_bits - 2))

    def far_join(half, token, mine, got):
        total = joined(f"far_join_{half}", token, [mine, got])
        for bit in reversed(range(far_bits - 2)):
            total = joined(f"far_join_{half}_{bit}", token, [total, swapped(total, "far", 1 << bit)])
        return total, exchanged([total] * (NEAR - 1))

    def near_join(half, k, token, mine, got):
        blocks = [mine, *got]
        total = joined(f"near_join_{half}_{k}", token, [blocks[c][None] for c in SHARES[k]])
        return total, swapped(total, "core", 1)

    def input_gradients(steps, token, before):
        last = (steps[-1] + 1) * ROWS == rows
        return inputs(steps, token, received if last else head_0[0], grad_out, pos, dpre_0, dpre_1, w_in_0, w_in_1, w_cond, before)

    halo = passed_along(signal[rows - DILATION_STEP :], 1)
    loads = (w_past, w_now, w_res, w_skip, b_res, b_skip)
    val, pos, b_conv, w_cond, w_in_0, *outer_0, past, signal, x_turned, grad_out, grad_skip, a, b, c = load(
        val, pos, b_conv, features, w_cond, w_res, w_skip, w_past, w_now, signal, grad_out, grad_skip
    )
    rest_0 = (a, b, c)
    common = (signal, x_turned, grad_out, grad_skip)
    past_head, head_0 = head(halo, pos, val, *common, w_in_0, w_cond, b_conv, *outer_0)
    made_0 = (head_0, rest_0)
    fixed = (far, block, val, x_turned, grad_out, grad_skip, past_head)
    *theirs_0, w_in_1, w_res_1, w_skip_1, b_res, b_skip = gradients(0, False, past_head, *fixed, made_0, loads)
    outer_1 = (w_res_1, w_skip_1)
    weights_1 = (w_in_1, w_cond, b_conv, *outer_1)
    mine_0 = gradients(0, True, theirs_0[0], *fixed, made_0)
    kept_0, got_0 = core_sum(0, mine_0[0], theirs_0, mine_0)
    made_1 = forward_1(kept_0, halo, pos, val, past, *common, *weights_1)
    dpre_0, dpre_1 = ([p[2] for p in made] for made in (made_0, made_1))
    theirs_1 = gradients(1, False, kept_0, *fixed, made_1)
    mine_1 = gradients(1, True, theirs_1[0], *fixed, made_1)
    (part,) = added("near_part_0", mine_1[0], got_0[2], [got_0[0]], [(far, F32)])
    kept_0, got_0 = near_sum(0, part, kept_0, [part, got_0[1]])
    kept_1, got_1 = core_sum(1, kept_0, theirs_1, mine_1)
    ends_0, got_0 = far_sum(0, kept_1, kept_0, got_0)
    *grads, mark = input_gradients((0, 1), ends_0, [])
    ends_0, got_0 = far_end(0, mark, ends_0, got_0)
    (part,) = added("near_part_1", ends_0, got_1[2], [got_1[1]], [(far, F32)])
    kept_1, got_1 = near_sum(1, part, kept_1, [part, got_1[0]])
    ends_0, got_0 = far_join(0, kept_1, ends_0, got_0)
    ends_1, got_1 = far_sum(1, ends_0, kept_1, got_1)
    output, skip_out, mark = outputs(
        ends_1, val, signal, [p[0] for p in made_0], [p[0] for p in made_1], outer_0, outer_1, b_res, b_skip
    )
    ends_1, got_1 = far_end(1, mark, ends_1, got_1)
    early = early_rows(ends_1, pos, dpre_0[0], dpre_1[0], w_in_0, w_in_1)
    received = passed_along(early, -1)
    first = near_join(0, 0, early, ends_0, got_0)
    second = near_join(0, 1, first[0], ends_0, got_0)
    pairs_0 = [first, second]
    ends_1, got_1 = far_join(1, second[0], ends_1, got_1)
    *grads, mark = input_gradients((2, 3), ends_1, grads)
    first = near_join(1, 0, mark, ends_1, got_1)
    second = near_join(1, 1, first[0], ends_1, got_1)
    pairs_1 = [first, second]
    sizes = (width, cond, hidden, skip_width)
    *done, own_0, mark = unpack(0, first[1], far, block, *zip(*pairs_0), *sizes, [])
    *done, own_1, _ = unpack(1, mark, far, block, *zip(*pairs_1), *sizes, done)
    g_past, g_now, g_cond, g_bias, g_res, g_skip = done
    grad_signal, grad_features = grads
    return (
        output,
        skip_out,
        grad_signal,
        grad_features.T,
        g_past,
        g_now,
        g_bias.reshape(-1),
        g_cond,
        g_res,
        own_0.reshape(-1),
        g_skip,
        own_1.reshape(-1),
    )


def solution(mesh):
    row, col = mesh.shape["row"], mesh.shape["col"]
    fine = Mesh(mesh.devices.reshape(row // 2, 2, col // NEAR, NEAR), AXES)
    rows = P(AXES, None)
    line = P(AXES)
    return jax.shard_map(
        body,
        mesh=fine,
        in_specs=(rows, rows, line, line) + (P(),) * 8 + (rows, rows),
        out_specs=(rows,) * 4 + (P(),) * 8,
        check_vma=False,
    )
```

```python
import functools

import jax
import jax.numpy as jnp
from jax import lax
from jax.experimental import pallas as pl
from jax.experimental.pallas import tpu as pltpu
from jax.sharding import Mesh
from jax.sharding import PartitionSpec as P

DILATION_STEP = 256
AXES = ("outer", "core", "far", "near")
HALVES = 2
NEAR = 4
LANES = 128
ROWS = 512
ONES = 16
F32 = jnp.float32
BF16 = jnp.bfloat16
MEGA = 1 << 20
COSTS = {
    "load": 8, "head": 2, "near_sum_0": 7, "mine_1": 2, "near_part_0": 1,
    "near_part_1": 2, "near_sum_1": 4, "near_join_0_1": 2, "near_join_1_1": 4, "far_join_0": 4,
}
FLOPS = 10**9


def dot(left, right):
    return jnp.dot(left, right, preferred_element_type=F32)


def across(left, right):
    return lax.dot_general(left, right, (((0,), (0,)), ((), ())), preferred_element_type=F32)


def against(left, weight):
    return lax.dot_general(left, weight, (((1,), (1,)), ((), ())), preferred_element_type=F32)


def column(lines):
    turned = lines.astype(F32).T
    return jnp.concatenate([turned[:, k : k + 1] for k in range(lines.shape[0])], axis=0)


def row(lines):
    return jnp.concatenate([lines[k : k + 1] for k in range(lines.shape[0])], axis=1)


def tap_of(lines):
    return jnp.where(lines >= DILATION_STEP, 1, 0)


def lines_of(ref, rows):
    return ref[rows.start // LANES : rows.stop // LANES, :]


def picked(pieces, rows):
    found, at = [], 0
    for ref in pieces:
        low, high = max(rows.start, at), min(rows.stop, at + ref.shape[0])
        if low < high:
            found.append(ref[low - at : high - at, :])
        at += ref.shape[0]
    return found[0] if len(found) == 1 else jnp.concatenate(found, axis=0)


def call(kernel, name, in_specs, out_specs, out_shape, scratch=(), aliases=None, grid=(), vmem=24):
    return pl.pallas_call(
        kernel,
        grid=grid,
        in_specs=in_specs,
        out_specs=out_specs,
        out_shape=out_shape,
        scratch_shapes=list(scratch),
        input_output_aliases=aliases or {},
        cost_estimate=pl.CostEstimate(
            flops=1 + int(FLOPS * COSTS.get(name, COSTS.get(name.split("_")[0], 0))), bytes_accessed=1, transcendentals=0
        ),
        name=name,
        compiler_params=pltpu.CompilerParams(vmem_limit_bytes=vmem * MEGA),
    )


VMEM = pl.BlockSpec(memory_space=pltpu.VMEM)
ANYWHERE = pl.BlockSpec(memory_space=pl.ANY)
MARK = jax.ShapeDtypeStruct((8, LANES), F32)


def beside(*parts):
    return jnp.concatenate(parts, axis=1)


def below(*parts):
    return jnp.concatenate(parts, axis=0)


def gate_product(half, k, rows, past, sig, feats, w_in, w_cond, b_conv):
    width = sig.shape[1]
    part = w_in.shape[1] // 2
    here = slice(k * part, (k + 1) * part)
    there = slice((k * HALVES + half) * part, (k * HALVES + half + 1) * part)
    own = dot(past, w_in[:width, here]) + dot(sig[rows, :], w_in[width:, here])
    return own + across(feats, w_cond[:, there]) + b_conv[:, there]


def back_product(rows, gout, gskip, w_res, w_skip):
    return against(gout[rows, :], w_res[...]) + against(gskip[rows, :], w_skip[...])


def weight_copies(half, w_past, w_now, w_res, w_skip, w_in_to, w_res_to, w_skip_to):
    width = w_past.shape[0]
    part = w_res_to.shape[0]
    pairs = []
    for k in range(2):
        here = pl.ds((k * HALVES + half) * part, part)
        for i, ref in enumerate((w_past, w_now)):
            pairs.append((ref.at[:, here], w_in_to.at[pl.ds(i * width, width), pl.ds(k * part, part)]))
    rows = pl.ds(half * part, part)
    return pairs + [(w_res.at[rows], w_res_to), (w_skip.at[rows], w_skip_to)]


def half_weights(w_past, w_res, w_skip):
    part = w_res.shape[0] // HALVES
    shapes = ((2 * w_past.shape[0], 2 * part), (part, w_res.shape[1]), (part, w_skip.shape[1]))
    return [jax.ShapeDtypeStruct(shape, BF16) for shape in shapes]


def finish(pre_a, pre_s, dgated, valid_lines):
    act = jnp.tanh(pre_a)
    gate = 0.5 + 0.5 * jnp.tanh(0.5 * pre_s)
    slope = (column(valid_lines) * dgated) * gate
    dpre = beside(slope * (1.0 - act * act), slope * act * (1.0 - gate)).astype(BF16)
    gated = (act * gate).astype(BF16)
    return gated, gated.T * row(valid_lines.astype(BF16)), dpre


def forward_tiles(half, tiles, prepare, arrive, valid, past, sig, x_turned, gout, gskip, weights, outs, base):
    w_in, w_cond, b_conv, w_res, w_skip = weights
    gated_out, kept_out, dpre_out = outs
    cond = w_cond.shape[0]
    width = sig.shape[1]

    def product(rows, k):
        if arrive:
            arrive(rows, k)
        if k == 2:
            return back_product(rows, gout, gskip, w_res, w_skip)
        feats = x_turned[2 * width : 2 * width + cond, rows]
        return gate_product(half, k, rows, past[rows, :], sig, feats, w_in, w_cond, b_conv)

    def done(rows, made):
        there = slice(rows.start - base, rows.stop - base)
        gated_out[there, :], kept_out[:, there], dpre_out[there, :] = finish(*made, lines_of(valid, rows))

    ahead = None
    for rows in tiles:
        if prepare:
            prepare(rows)
        made = [product(rows, k) for k in range(3)]
        if ahead:
            done(*ahead)
        ahead = (rows, made)
    done(*ahead)


def tiles_of(start, stop):
    return [slice(a, a + DILATION_STEP) for a in range(start, stop, DILATION_STEP)]


def load_body(
    valid, pos, b_conv, feat, w_cond, w_res, w_skip, w_past, w_now, sig, gout, gskip,
    valid_to, pos_to, b_conv_to, w_cond_to, w_in, w_res_to, w_skip_to, past, sig_to, x_turned,
    gout_to, gskip_to, gated_rest, kept_rest, dpre_rest, sems,
):
    rows_all, width = sig.shape
    cond = feat.shape[0]
    count = 0

    def start(source, target):
        nonlocal count
        copy = pltpu.make_async_copy(source, target, sems.at[count])
        copy.start()
        count += 1
        return copy

    def tile(i, source, target):
        rows = pl.ds(i * ROWS, ROWS)
        return start(source.at[rows], target.at[rows])

    weights = weight_copies(0, w_past, w_now, w_res, w_skip, w_in, w_res_to, w_skip_to)
    signals = [[tile(0, sig, sig_to)]]
    needs = [
        [
            start(pos, pos_to),
            *(start(*pair) for pair in weights[:2]),
            start(feat, x_turned.at[pl.ds(2 * width, cond)]),
            start(w_cond, w_cond_to),
            start(b_conv, b_conv_to),
        ],
        [start(*pair) for pair in weights[2:4]],
        [start(valid, valid_to), *(start(*pair) for pair in weights[4:])],
    ]
    cotangents = [[tile(0, gout, gout_to), tile(0, gskip, gskip_to)]]
    for i in range(1, rows_all // ROWS):
        signals.append([tile(i, sig, sig_to)])
        cotangents.append([tile(i, gout, gout_to), tile(i, gskip, gskip_to)])

    def wait(copies):
        for copy in copies:
            copy.wait()
        copies.clear()

    def prepare(rows):
        i = rows.start // ROWS
        wait(signals[i])
        wait(needs[0])
        whole = rows if i else slice(0, rows.stop)
        before = slice(rows.start - DILATION_STEP, rows.stop - DILATION_STEP)
        tap = tap_of(lines_of(pos_to, rows)).astype(F32)
        past[rows, :] = sig_to[before, :] * column(tap).astype(BF16)
        x_turned[width : 2 * width, whole] = sig_to[whole, :].T
        x_turned[:width, rows] = x_turned[width : 2 * width, before] * row(tap).astype(BF16)

    def arrive(rows, k):
        wait(needs[k])
        if k == 2:
            wait(cotangents[rows.start // ROWS])

    x_turned[2 * width + cond :, :] = jnp.ones((x_turned.shape[0] - 2 * width - cond, rows_all), BF16)
    forward_tiles(
        0, tiles_of(DILATION_STEP, rows_all), prepare, arrive, valid_to, past, sig_to, x_turned, gout_to, gskip_to,
        (w_in, w_cond_to, b_conv_to, w_res_to, w_skip_to), (gated_rest, kept_rest, dpre_rest), DILATION_STEP,
    )


def rest_shapes(rest, part):
    return [jax.ShapeDtypeStruct(shape, BF16) for shape in ((rest, part), (part, rest), (rest, 2 * part))]


def load(*arrays):
    sources = [in_hbm(x) for x in arrays]
    feat, w_cond, w_res, w_skip, w_past, _, sig, gout, gskip = arrays[3:]
    rows, width = sig.shape
    hidden = w_res.shape[0]
    shapes = [jax.ShapeDtypeStruct(x.shape, x.dtype) for x in arrays[:3] + (w_cond,)]
    shapes += half_weights(w_past, w_res, w_skip) + [
        jax.ShapeDtypeStruct(shape, BF16)
        for shape in (
            sig.shape, sig.shape, (2 * width + feat.shape[0] + ONES, rows), gout.shape, gskip.shape,
        )
    ]
    shapes += rest_shapes(rows - DILATION_STEP, hidden // HALVES)
    return call(
        load_body,
        "load",
        [ANYWHERE] * len(sources),
        [VMEM] * len(shapes),
        shapes,
        scratch=[pltpu.SemaphoreType.DMA((11 + 3 * (rows // ROWS),))],
    )(*sources)


def side_by_side(dpre_0, dpre_1):
    part = dpre_0.shape[1] // 2
    return beside(dpre_0[:, :part], dpre_1[:, :part], dpre_0[:, part:], dpre_1[:, part:])


def head_rows(half, halo, pos, valid, sig, x_turned, gout, gskip, weights, outs):
    w_in, w_cond, b_conv, w_res, w_skip = weights
    rows = slice(0, DILATION_STEP)
    width = halo.shape[1]
    feats = x_turned[2 * width : 2 * width + w_cond.shape[0], rows]
    past = halo[...] * column(tap_of(lines_of(pos, rows)).astype(F32)).astype(BF16)
    made = [gate_product(half, k, rows, past, sig, feats, w_in, w_cond, b_conv) for k in range(2)]
    made.append(back_product(rows, gout, gskip, w_res, w_skip))
    for ref, value in zip(outs, finish(*made, lines_of(valid, rows))):
        ref[...] = value


def head_body(halo, pos, valid, sig, x_turned, gout, gskip, w_in, w_cond, b_conv, w_res, w_skip, past_out, *outs):
    tap = tap_of(lines_of(pos, slice(0, DILATION_STEP))).astype(F32)
    past_out[...] = halo[...].T * row(tap).astype(BF16)
    head_rows(0, halo, pos, valid, sig, x_turned, gout, gskip, (w_in, w_cond, b_conv, w_res, w_skip), outs)


def head(halo, *args):
    width = halo.shape[1]
    part = args[-1].shape[0]
    past, *parts = call(
        head_body,
        "head",
        [VMEM] * (1 + len(args)),
        [VMEM] * 4,
        [jax.ShapeDtypeStruct((width, DILATION_STEP), BF16)] + rest_shapes(DILATION_STEP, part),
    )(halo, *args)
    return past, parts


def early_body(token, pos, dpre_0, dpre_1, w_in_0, w_in_1, early):
    tap = column(tap_of(lines_of(pos, slice(0, DILATION_STEP))))
    some = slice(0, early.shape[1])
    early[...] = (tap * (against(dpre_0[...], w_in_0[some, :]) + against(dpre_1[...], w_in_1[some, :]))).astype(BF16)


def early_rows(token, pos, dpre_0, dpre_1, w_in_0, w_in_1):
    return call(
        early_body,
        "early",
        [ANYWHERE] + [VMEM] * 5,
        VMEM,
        jax.ShapeDtypeStruct((DILATION_STEP, w_in_0.shape[0] // 2), BF16),
    )(token, pos, dpre_0, dpre_1, w_in_0, w_in_1)


def forward_body(token, halo, pos, valid, past, sig, x_turned, gout, gskip, w_in, w_cond, b_conv, w_res, w_skip, *outs):
    weights = (w_in, w_cond, b_conv, w_res, w_skip)
    head_rows(1, halo, pos, valid, sig, x_turned, gout, gskip, weights, outs[:3])
    forward_tiles(
        1, tiles_of(DILATION_STEP, sig.shape[0]), None, None, valid, past, sig, x_turned, gout, gskip, weights, outs[3:],
        DILATION_STEP,
    )


def forward_1(token, *args):
    part = args[-1].shape[0]
    parts = call(
        forward_body,
        "forward_1",
        [ANYWHERE] + [VMEM] * len(args),
        [VMEM] * 6,
        rest_shapes(DILATION_STEP, part) + rest_shapes(args[4].shape[0] - DILATION_STEP, part),
    )(token, *args)
    return parts[:3], parts[3:]


GROUPS = (((3, 1), (2, 0)), ((1, 2, 3, 0),))


def own_place():
    return [lax.axis_index(name) for name in ("core", "far", "near")]


def turned(index, count):
    bits = (count - 1).bit_length()
    result = 0
    for bit in range(bits):
        result = result | (((index >> bit) & 1) << (bits - 1 - bit))
    return result


def gradients_body(far, block, half, own, count, extra, token, valid, x_turned, gout, gskip, past_head, *refs):
    kepts, dpres, refs = refs[:count], refs[count : 2 * count], refs[2 * count :]
    groups = GROUPS[half]
    sources, outs = refs[:extra], refs[extra : len(refs) - 1 - bool(extra)]
    outs, targets = outs[: len(groups)], outs[len(groups) :]
    acc = refs[-1 - bool(extra)]
    copies = []
    if extra:
        pairs = weight_copies(1, *sources[:4], *targets[:3]) + list(zip(sources[4:], targets[3:]))
        copies = [pltpu.make_async_copy(*pair, refs[-1].at[k]) for k, pair in enumerate(pairs)]
    for copy in copies:
        copy.start()
    width = past_head.shape[0]
    part = kepts[0].shape[0]
    ends, rows = x_turned.shape
    size = far * block
    core, z, xy = own_place()
    which = core if own else 1 - core

    def product(left_of, rights):
        total, at = None, 0
        for k, right in enumerate(rights):
            here = slice(at, at + right.shape[0])
            made = dot(left_of(here, k), right[...])
            total = made if at == 0 else total + made
            at = here.stop
        return total

    def region(k):
        low, high = k * size, min((k + 1) * size, ends)

        def turned_rows(here, piece):
            if piece == 0 and low < width:
                return below(past_head[low : min(high, width), :], x_turned[width : max(high, width), here])
            return x_turned[low:high, here]

        def keep(first, value):
            for c in range(NEAR):
                acc[c, first : first + value.shape[0], :] = value[:, c * LANES : (c + 1) * LANES]

        keep(0, product(turned_rows, dpres))
        at = high - low
        if high == ends:
            mask = jnp.broadcast_to(row(lines_of(valid, slice(0, rows)).astype(F32)).astype(BF16), (ONES, rows))

            def kept_rows(here, piece):
                return below(kepts[piece][...], mask[:, here])

            for i, ref in enumerate((gout, gskip)):
                cuts = [0]
                for kept in kepts:
                    cuts.append(cuts[-1] + kept.shape[1])
                made = product(kept_rows, [ref.at[pl.ds(a, b - a)] for a, b in zip(cuts, cuts[1:])])
                keep(at, made[:part])
                at += part
                if i == half:
                    keep(high - low + 2 * part, made[part:])
            at += ONES
            acc[:, at:, :] = jnp.zeros((NEAR, size - at, LANES), F32)
        for group, out in zip(groups, outs):
            for i, p in enumerate(group):
                for r in range(far):
                    out[i, turned(r ^ z, far)] = acc[xy ^ p, r * block : (r + 1) * block, :].astype(out.dtype)

    for k in range(2):
        pl.when(which == k)(functools.partial(region, k))
    for copy in copies:
        copy.wait()


def gradients(half, own, token, far, block, valid, x_turned, gout, gskip, past_head, pieces, loads=()):
    count = len(pieces)
    sources = [in_hbm(x) for x in loads]
    outs = [jax.ShapeDtypeStruct((len(group), far, block, LANES), F32 if own else BF16) for group in GROUPS[half]]
    scratch = [pltpu.VMEM((NEAR, far * block, LANES), F32)]
    if loads:
        outs += half_weights(loads[0], *loads[2:4]) + [jax.ShapeDtypeStruct(x.shape, x.dtype) for x in loads[4:]]
        scratch.append(pltpu.SemaphoreType.DMA((6 + len(loads[4:]),)))
    return call(
        functools.partial(gradients_body, far, block, half, own, count, len(loads)),
        ("mine" if own else "theirs") + f"_{half}",
        [ANYWHERE] + [VMEM] * (5 + 2 * count) + [ANYWHERE] * len(loads),
        [VMEM] * len(outs),
        outs,
        scratch=scratch,
    )(token, valid, x_turned, gout, gskip, past_head, *(p[1] for p in pieces), *(p[2] for p in pieces), *sources)


def outputs_body(counts, token, valid, sig, w_res_0, w_skip_0, w_res_1, w_skip_1, b_res, b_skip, *refs):
    first, second = refs[: counts[0]], refs[counts[0] : sum(counts)]
    out, skip, mark, rooms, sems = refs[sum(counts) :]
    copies = []
    for i in range(sig.shape[0] // ROWS):
        rows = slice(i * ROWS, (i + 1) * ROWS)
        mask = column(lines_of(valid, rows))
        left, right = picked(first, rows), picked(second, rows)
        branch = dot(left, w_res_0[...]) + dot(right, w_res_1[...]) + b_res[...]
        rooms[i, 0] = (sig[rows, :].astype(F32) + mask * branch).astype(BF16)
        side = dot(left, w_skip_0[...]) + dot(right, w_skip_1[...]) + b_skip[...]
        rooms[i, 1] = (mask * side).astype(BF16)
        for k, ref in enumerate((out, skip)):
            copies.append(pltpu.make_async_copy(rooms.at[i, k], ref.at[pl.ds(i * ROWS, ROWS)], sems.at[i, k]))
            copies[-1].start()
    mark[...] = jnp.zeros_like(mark)
    for copy in copies:
        copy.wait()


def outputs(token, valid, sig, gated_0, gated_1, weights_0, weights_1, b_res, b_skip):
    rows, width = sig.shape
    counts = (len(gated_0), len(gated_1))
    return call(
        functools.partial(outputs_body, counts),
        "outputs",
        [ANYWHERE] + [VMEM] * (8 + sum(counts)),
        [ANYWHERE, ANYWHERE, VMEM],
        [
            jax.ShapeDtypeStruct((rows, width), BF16),
            jax.ShapeDtypeStruct((rows, weights_0[1].shape[1]), BF16),
            MARK,
        ],
        scratch=[
            pltpu.VMEM((rows // ROWS, 2, ROWS, width), BF16),
            pltpu.SemaphoreType.DMA((rows // ROWS, 2)),
        ],
    )(token, valid, sig, *weights_0, *weights_1, b_res, b_skip, *gated_0, *gated_1)


def inputs_body(steps, counts, token, received, gout, pos, w_in_0, w_in_1, w_cond, *refs):
    first, second = refs[: counts[0]], refs[counts[0] : sum(counts)]
    gsig, gfeat, mark, room, room_feat, sems = refs[-6:]
    rows, width = gout.shape
    copies = []
    wide = 2 * LANES

    def copy(source, target):
        copies.append(pltpu.make_async_copy(source, target, sems.at[len(copies)]))
        copies[-1].start()

    for i, step in enumerate(steps):
        begin = step * ROWS
        here = slice(begin, begin + ROWS)
        after = slice(begin + DILATION_STEP, min(begin + DILATION_STEP + ROWS, rows))
        now = [picked(pieces, here) for pieces in (first, second)]
        later = [picked(pieces, after) for pieces in (first, second)]
        tap = column(tap_of(lines_of(pos, after)))
        room_feat[i] = against(w_cond[...], side_by_side(*now))
        copy(room_feat.at[i], gfeat.at[:, pl.ds(begin, ROWS)])
        for k in range(width // wide):
            some = slice(k * wide, (k + 1) * wide)
            tail = tap * (against(later[0], w_in_0[some, :]) + against(later[1], w_in_1[some, :]))
            if tail.shape[0] < ROWS:
                tail = below(tail, received[:, some].astype(F32))
            below_past = slice(width + k * wide, width + (k + 1) * wide)
            own = against(now[0], w_in_0[below_past, :]) + against(now[1], w_in_1[below_past, :])
            room[i, k] = gout[here, some].astype(F32) + own + tail
            copy(room.at[i, k], gsig.at[pl.ds(begin, ROWS), pl.ds(k * wide, wide)])
    mark[...] = jnp.zeros_like(mark)
    for one in copies:
        one.wait()


def inputs(steps, token, received, gout, pos, dpre_0, dpre_1, w_in_0, w_in_1, w_cond, before):
    rows, width = gout.shape
    cond = w_cond.shape[0]
    count = width // (2 * LANES)
    counts = (len(dpre_0), len(dpre_1))
    operands = 7 + sum(counts)
    return call(
        functools.partial(inputs_body, steps, counts),
        f"inputs_{steps[0]}",
        [ANYWHERE] + [VMEM] * (operands - 1) + [ANYWHERE] * len(before),
        [ANYWHERE, ANYWHERE, VMEM],
        [
            jax.ShapeDtypeStruct((rows, width), F32),
            jax.ShapeDtypeStruct((cond, rows), F32),
            MARK,
        ],
        scratch=[
            pltpu.VMEM((len(steps), count, ROWS, 2 * LANES), F32),
            pltpu.VMEM((len(steps), cond, ROWS), F32),
            pltpu.SemaphoreType.DMA((len(steps) * (count + 1),)),
        ],
        aliases={operands + k: k for k in range(len(before))},
    )(token, received, gout, pos, w_in_0, w_in_1, w_cond, *dpre_0, *dpre_1, *before)


SHARES = ((0, 3), (1, 2))


def unpack_body(far, block, token, *refs):
    blocks, arrays, (mark, room) = refs[: 2 * len(SHARES)], refs[-9:-2], refs[-2:]
    mine, theirs = blocks[: len(SHARES)], blocks[len(SHARES) :]
    mark[...] = jnp.zeros_like(mark)
    core, z, xy = own_place()

    @pl.when(pl.program_id(0) == 0)
    def _():
        for k, parts in ((core, mine), (1 - core, theirs)):
            for share, ref in zip(SHARES, parts):
                for i, c in enumerate(share):
                    for r in range(far):
                        rows = pl.ds(pl.multiple_of((k * far + (r ^ z)) * block, 16), block)
                        room[c ^ xy, rows, :] = ref[i, turned(r, far)]

    for j in range(NEAR // 2):
        c = pl.program_id(0) * (NEAR // 2) + j
        here = pl.ds(j * LANES, LANES)
        top = 0
        for ref in arrays:
            count = ref.shape[0]
            size = max(count, ONES)
            ref[:, here] = room[c, top : top + size, :].astype(F32)[:count]
            top += size


def unpack(half, token, far, block, mine, theirs, width, cond, hidden, skip_width, before):
    part = hidden // HALVES
    gates = 2 * hidden
    own = (width, skip_width)[half]

    def wide(size):
        return pl.BlockSpec((size, part), lambda s: (0, HALVES * s + half))

    def tall(size):
        return pl.BlockSpec((part, size // 2), lambda s: (half, s))

    specs = [wide(width), wide(width), wide(cond), wide(1), tall(width), tall(skip_width), pl.BlockSpec((1, own // 2), lambda s: (0, s))]
    shapes = [(width, gates), (width, gates), (cond, gates), (1, gates), (hidden, width), (hidden, skip_width), (1, own)]
    blocks = [pl.BlockSpec(x.shape, lambda s: (0,) * 4) for x in (*mine, *theirs)]
    return call(
        functools.partial(unpack_body, far, block),
        f"unpack_{half}",
        [ANYWHERE, *blocks] + [ANYWHERE] * len(before),
        specs + [pl.BlockSpec(MARK.shape, lambda s: (0, 0))],
        [jax.ShapeDtypeStruct(shape, F32) for shape in shapes] + [MARK],
        scratch=[pltpu.VMEM((NEAR, 2 * far * block, LANES), BF16)],
        aliases={1 + len(blocks) + k: k for k in range(len(before))},
        grid=(2,),
    )(token, *mine, *theirs, *before)


def swapped(x, axis, k):
    return lax.ppermute(x, axis, [(i, i ^ k) for i in range(lax.axis_size(axis))])


def exchanged(blocks):
    return [swapped(block, "near", k + 1) for k, block in enumerate(blocks)]


def add_body(sizes, token, *refs):
    count = len(sizes)
    kept, got, outs = refs[0], refs[1:-count], refs[-count:]
    at = 0
    for out, size in zip(outs, sizes):
        for k in range(size):
            total = kept[at + k].astype(F32)
            for ref in got:
                total = total + ref[at + k].astype(F32)
            out[k] = total.astype(out.dtype)
        at += size


def added(name, token, kept, got, outs):
    sizes = [size for size, _ in outs]
    result = call(
        functools.partial(add_body, sizes),
        name,
        [ANYWHERE] + [VMEM] * (1 + len(got)),
        [VMEM] * len(outs),
        [jax.ShapeDtypeStruct((size, *kept.shape[1:]), dtype) for size, dtype in outs],
    )(token, kept, *got)
    return result


def mirror_body(token, mine, got, out):
    count = mine.shape[0]
    for k in range(count):
        out[k] = (mine[k].astype(F32) + got[count - 1 - k].astype(F32)).astype(out.dtype)


def mirrored(name, token, mine, got):
    return call(
        mirror_body,
        name,
        [ANYWHERE, VMEM, VMEM],
        VMEM,
        jax.ShapeDtypeStruct(mine.shape, BF16),
    )(token, mine, got)


def join_body(token, *refs):
    out = refs[-1]
    at = 0
    for ref in refs[:-1]:
        out[at : at + ref.shape[0]] = ref[...]
        at += ref.shape[0]


def joined(name, token, parts):
    count = sum(part.shape[0] for part in parts)
    return call(
        join_body,
        name,
        [ANYWHERE] + [VMEM] * len(parts),
        VMEM,
        jax.ShapeDtypeStruct((count, *parts[0].shape[1:]), BF16),
    )(token, *parts)


def over_outer(total):
    for bit in range((lax.axis_size("outer") - 1).bit_length()):
        total = (total.astype(F32) + swapped(total, "outer", 1 << bit).astype(F32)).astype(BF16)
    return total


def passed_along(x, by):
    peers = lax.axis_size(AXES)
    pairs = [(i, i + by) for i in range(peers) if 0 <= i + by < peers]
    return lax.ppermute(x, AXES, pairs)


def in_hbm(x):
    return pltpu.with_memory_space_constraint(x, pltpu.HBM)


def body(
    signal,
    features,
    position,
    valid,
    w_past,
    w_now,
    b_conv,
    w_cond,
    w_res,
    b_res,
    w_skip,
    b_skip,
    grad_out,
    grad_skip,
):
    rows, width = signal.shape
    features = features.T
    cond = features.shape[0]
    hidden = w_res.shape[0]
    skip_width = w_skip.shape[1]
    far = lax.axis_size("far")
    far_bits = (far - 1).bit_length()
    used = 2 * width + cond + ONES + 2 * (hidden // HALVES) + ONES
    block = -(-used // (2 * far * 16)) * 16
    lines = (rows // LANES, LANES)
    pos, val = position.reshape(lines), valid.reshape(lines)
    b_conv, b_res, b_skip = (b.reshape(1, -1) for b in (b_conv, b_res, b_skip))

    def core_sum(half, token, theirs, mine):
        got = {}
        for k, group in enumerate(GROUPS[half]):
            blocks = added(
                f"core_sum_{half}_{k}", token, mine[k], [swapped(theirs[k], "core", 1)],
                [(1, BF16 if p else F32) for p in group],
            )
            token = blocks[0]
            for p, part in zip(group, blocks):
                got[p] = swapped(part[0], "near", p) if p else part[0]
        return got[0], [got[p] for p in range(1, NEAR)]

    def near_sum(half, token, kept, got):
        kept, sent = added(f"near_sum_{half}", token, kept, got, [(far // 2, F32), (far // 2, BF16)])
        return kept, swapped(sent, "far", 1)

    def far_sum(half, token, kept, got):
        for bit in range(1, far_bits - 1):
            size = kept.shape[0] // 2
            kept, sent = added(f"far_sum_{half}_{bit}", token, kept, [got], [(size, F32), (size, BF16)])
            got = swapped(sent, "far", 1 << bit)
        (mine,) = added(f"far_sum_{half}", token, kept, [got], [(kept.shape[0], BF16)])
        return mine, swapped(mine, "far", 1 << (far_bits - 1))

    def far_end(half, token, mine, got):
        total = over_outer(mirrored(f"far_end_{half}", token, mine, got))
        return total, swapped(total, "far", 1 << (far_bits - 2))

    def far_join(half, token, mine, got):
        total = joined(f"far_join_{half}", token, [mine, got])
        for bit in reversed(range(far_bits - 2)):
            total = joined(f"far_join_{half}_{bit}", token, [total, swapped(total, "far", 1 << bit)])
        return total, exchanged([total] * (NEAR - 1))

    def near_join(half, k, token, mine, got):
        blocks = [mine, *got]
        total = joined(f"near_join_{half}_{k}", token, [blocks[c][None] for c in SHARES[k]])
        return total, swapped(total, "core", 1)

    def input_gradients(steps, token, before):
        last = (steps[-1] + 1) * ROWS == rows
        return inputs(steps, token, received if last else head_0[0], grad_out, pos, dpre_0, dpre_1, w_in_0, w_in_1, w_cond, before)

    halo = passed_along(signal[rows - DILATION_STEP :], 1)
    loads = (w_past, w_now, w_res, w_skip, b_res, b_skip)
    val, pos, b_conv, w_cond, w_in_0, *outer_0, past, signal, x_turned, grad_out, grad_skip, a, b, c = load(
        val, pos, b_conv, features, w_cond, w_res, w_skip, w_past, w_now, signal, grad_out, grad_skip
    )
    rest_0 = (a, b, c)
    common = (signal, x_turned, grad_out, grad_skip)
    past_head, head_0 = head(halo, pos, val, *common, w_in_0, w_cond, b_conv, *outer_0)
    made_0 = (head_0, rest_0)
    fixed = (far, block, val, x_turned, grad_out, grad_skip, past_head)
    *theirs_0, w_in_1, w_res_1, w_skip_1, b_res, b_skip = gradients(0, False, past_head, *fixed, made_0, loads)
    outer_1 = (w_res_1, w_skip_1)
    weights_1 = (w_in_1, w_cond, b_conv, *outer_1)
    mine_0 = gradients(0, True, theirs_0[0], *fixed, made_0)
    kept_0, got_0 = core_sum(0, mine_0[0], theirs_0, mine_0)
    made_1 = forward_1(kept_0, halo, pos, val, past, *common, *weights_1)
    dpre_0, dpre_1 = ([p[2] for p in made] for made in (made_0, made_1))
    theirs_1 = gradients(1, False, kept_0, *fixed, made_1)
    mine_1 = gradients(1, True, theirs_1[0], *fixed, made_1)
    (part,) = added("near_part_0", mine_1[0], got_0[2], [got_0[0]], [(far, F32)])
    kept_0, got_0 = near_sum(0, part, kept_0, [part, got_0[1]])
    kept_1, got_1 = core_sum(1, kept_0, theirs_1, mine_1)
    ends_0, got_0 = far_sum(0, kept_1, kept_0, got_0)
    *grads, mark = input_gradients((0, 1), ends_0, [])
    ends_0, got_0 = far_end(0, mark, ends_0, got_0)
    (part,) = added("near_part_1", ends_0, got_1[2], [got_1[1]], [(far, F32)])
    kept_1, got_1 = near_sum(1, part, kept_1, [part, got_1[0]])
    ends_0, got_0 = far_join(0, kept_1, ends_0, got_0)
    ends_1, got_1 = far_sum(1, ends_0, kept_1, got_1)
    *grads, mark = input_gradients((2,), ends_1, grads)
    ends_1, got_1 = far_end(1, mark, ends_1, got_1)
    early = early_rows(ends_1, pos, dpre_0[0], dpre_1[0], w_in_0, w_in_1)
    received = passed_along(early, -1)
    first = near_join(0, 0, early, ends_0, got_0)
    second = near_join(0, 1, first[0], ends_0, got_0)
    pairs_0 = [first, second]
    ends_1, got_1 = far_join(1, second[0], ends_1, got_1)
    output, skip_out, mark = outputs(
        ends_1, val, signal, [p[0] for p in made_0], [p[0] for p in made_1], outer_0, outer_1, b_res, b_skip
    )
    *grads, mark = input_gradients((3,), mark, grads)
    first = near_join(1, 0, mark, ends_1, got_1)
    second = near_join(1, 1, first[0], ends_1, got_1)
    pairs_1 = [first, second]
    sizes = (width, cond, hidden, skip_width)
    *done, own_0, mark = unpack(0, first[1], far, block, *zip(*pairs_0), *sizes, [])
    *done, own_1, _ = unpack(1, mark, far, block, *zip(*pairs_1), *sizes, done)
    g_past, g_now, g_cond, g_bias, g_res, g_skip = done
    grad_signal, grad_features = grads
    return (
        output,
        skip_out,
        grad_signal,
        grad_features.T,
        g_past,
        g_now,
        g_bias.reshape(-1),
        g_cond,
        g_res,
        own_0.reshape(-1),
        g_skip,
        own_1.reshape(-1),
    )


def solution(mesh):
    row, col = mesh.shape["row"], mesh.shape["col"]
    fine = Mesh(mesh.devices.reshape(row // 2, 2, col // NEAR, NEAR), AXES)
    rows = P(AXES, None)
    line = P(AXES)
    return jax.shard_map(
        body,
        mesh=fine,
        in_specs=(rows, rows, line, line) + (P(),) * 8 + (rows, rows),
        out_specs=(rows,) * 4 + (P(),) * 8,
        check_vma=False,
    )
```

```python
import functools

import jax
import jax.numpy as jnp
from jax import lax
from jax.experimental import pallas as pl
from jax.experimental.pallas import tpu as pltpu
from jax.sharding import Mesh
from jax.sharding import PartitionSpec as P

DILATION_STEP = 256
AXES = ("outer", "core", "far", "near")
HALVES = 2
NEAR = 4
LANES = 128
ROWS = 512
ONES = 16
F32 = jnp.float32
BF16 = jnp.bfloat16
MEGA = 1 << 20
COSTS = {
    "load": 8, "head": 2, "near_sum_0": 7, "mine_1": 2, "near_part_0": 1,
    "near_part_1": 2, "near_sum_1": 4, "outputs": 10, "touch": 4, "near_join_0_0": 2, "near_join_1_1": 4, "far_join_0": 4,
}
FLOPS = 10**9


def dot(left, right):
    return jnp.dot(left, right, preferred_element_type=F32)


def across(left, right):
    return lax.dot_general(left, right, (((0,), (0,)), ((), ())), preferred_element_type=F32)


def against(left, weight):
    return lax.dot_general(left, weight, (((1,), (1,)), ((), ())), preferred_element_type=F32)


def column(lines):
    turned = lines.astype(F32).T
    return jnp.concatenate([turned[:, k : k + 1] for k in range(lines.shape[0])], axis=0)


def row(lines):
    return jnp.concatenate([lines[k : k + 1] for k in range(lines.shape[0])], axis=1)


def tap_of(lines):
    return jnp.where(lines >= DILATION_STEP, 1, 0)


def lines_of(ref, rows):
    return ref[rows.start // LANES : rows.stop // LANES, :]


def picked(pieces, rows):
    found, at = [], 0
    for ref in pieces:
        low, high = max(rows.start, at), min(rows.stop, at + ref.shape[0])
        if low < high:
            found.append(ref[low - at : high - at, :])
        at += ref.shape[0]
    return found[0] if len(found) == 1 else jnp.concatenate(found, axis=0)


def call(kernel, name, in_specs, out_specs, out_shape, scratch=(), aliases=None, grid=(), vmem=24):
    return pl.pallas_call(
        kernel,
        grid=grid,
        in_specs=in_specs,
        out_specs=out_specs,
        out_shape=out_shape,
        scratch_shapes=list(scratch),
        input_output_aliases=aliases or {},
        cost_estimate=pl.CostEstimate(
            flops=1 + int(FLOPS * COSTS.get(name, COSTS.get(name.split("_")[0], 0))), bytes_accessed=1, transcendentals=0
        ),
        name=name,
        compiler_params=pltpu.CompilerParams(vmem_limit_bytes=vmem * MEGA),
    )


VMEM = pl.BlockSpec(memory_space=pltpu.VMEM)
ANYWHERE = pl.BlockSpec(memory_space=pl.ANY)
MARK = jax.ShapeDtypeStruct((8, LANES), F32)


def beside(*parts):
    return jnp.concatenate(parts, axis=1)


def below(*parts):
    return jnp.concatenate(parts, axis=0)


def gate_product(half, k, rows, past, sig, feats, w_in, w_cond, b_conv):
    width = sig.shape[1]
    part = w_in.shape[1] // 2
    here = slice(k * part, (k + 1) * part)
    there = slice((k * HALVES + half) * part, (k * HALVES + half + 1) * part)
    own = dot(past, w_in[:width, here]) + dot(sig[rows, :], w_in[width:, here])
    return own + across(feats, w_cond[:, there]) + b_conv[:, there]


def back_product(rows, gout, gskip, w_res, w_skip):
    return against(gout[rows, :], w_res[...]) + against(gskip[rows, :], w_skip[...])


def weight_copies(half, w_past, w_now, w_res, w_skip, w_in_to, w_res_to, w_skip_to):
    width = w_past.shape[0]
    part = w_res_to.shape[0]
    pairs = []
    for k in range(2):
        here = pl.ds((k * HALVES + half) * part, part)
        for i, ref in enumerate((w_past, w_now)):
            pairs.append((ref.at[:, here], w_in_to.at[pl.ds(i * width, width), pl.ds(k * part, part)]))
    rows = pl.ds(half * part, part)
    return pairs + [(w_res.at[rows], w_res_to), (w_skip.at[rows], w_skip_to)]


def half_weights(w_past, w_res, w_skip):
    part = w_res.shape[0] // HALVES
    shapes = ((2 * w_past.shape[0], 2 * part), (part, w_res.shape[1]), (part, w_skip.shape[1]))
    return [jax.ShapeDtypeStruct(shape, BF16) for shape in shapes]


def finish(pre_a, pre_s, dgated, valid_lines):
    act = jnp.tanh(pre_a)
    gate = 0.5 + 0.5 * jnp.tanh(0.5 * pre_s)
    slope = (column(valid_lines) * dgated) * gate
    dpre = beside(slope * (1.0 - act * act), slope * act * (1.0 - gate)).astype(BF16)
    gated = (act * gate).astype(BF16)
    return gated, gated.T * row(valid_lines.astype(BF16)), dpre


def forward_tiles(half, tiles, prepare, arrive, valid, past, sig, x_turned, gout, gskip, weights, outs, base):
    w_in, w_cond, b_conv, w_res, w_skip = weights
    gated_out, kept_out, dpre_out = outs
    cond = w_cond.shape[0]
    width = sig.shape[1]

    def product(rows, k):
        if arrive:
            arrive(rows, k)
        if k == 2:
            return back_product(rows, gout, gskip, w_res, w_skip)
        feats = x_turned[2 * width : 2 * width + cond, rows]
        return gate_product(half, k, rows, past[rows, :], sig, feats, w_in, w_cond, b_conv)

    def done(rows, made):
        there = slice(rows.start - base, rows.stop - base)
        gated_out[there, :], kept_out[:, there], dpre_out[there, :] = finish(*made, lines_of(valid, rows))

    ahead = None
    for rows in tiles:
        if prepare:
            prepare(rows)
        made = [product(rows, k) for k in range(3)]
        if ahead:
            done(*ahead)
        ahead = (rows, made)
    done(*ahead)


def tiles_of(start, stop):
    return [slice(a, a + DILATION_STEP) for a in range(start, stop, DILATION_STEP)]


def load_body(
    valid, pos, b_conv, feat, w_cond, w_res, w_skip, w_past, w_now, sig, gout, gskip,
    valid_to, pos_to, b_conv_to, w_cond_to, w_in, w_res_to, w_skip_to, past, sig_to, x_turned,
    gout_to, gskip_to, gated_rest, kept_rest, dpre_rest, sems,
):
    rows_all, width = sig.shape
    cond = feat.shape[0]
    count = 0

    def start(source, target):
        nonlocal count
        copy = pltpu.make_async_copy(source, target, sems.at[count])
        copy.start()
        count += 1
        return copy

    def tile(i, source, target):
        rows = pl.ds(i * ROWS, ROWS)
        return start(source.at[rows], target.at[rows])

    weights = weight_copies(0, w_past, w_now, w_res, w_skip, w_in, w_res_to, w_skip_to)
    signals = [[tile(0, sig, sig_to)]]
    needs = [
        [
            start(pos, pos_to),
            *(start(*pair) for pair in weights[:2]),
            start(feat, x_turned.at[pl.ds(2 * width, cond)]),
            start(w_cond, w_cond_to),
            start(b_conv, b_conv_to),
        ],
        [start(*pair) for pair in weights[2:4]],
        [start(valid, valid_to), *(start(*pair) for pair in weights[4:])],
    ]
    cotangents = [[tile(0, gout, gout_to), tile(0, gskip, gskip_to)]]
    for i in range(1, rows_all // ROWS):
        signals.append([tile(i, sig, sig_to)])
        cotangents.append([tile(i, gout, gout_to), tile(i, gskip, gskip_to)])

    def wait(copies):
        for copy in copies:
            copy.wait()
        copies.clear()

    def prepare(rows):
        i = rows.start // ROWS
        wait(signals[i])
        wait(needs[0])
        whole = rows if i else slice(0, rows.stop)
        before = slice(rows.start - DILATION_STEP, rows.stop - DILATION_STEP)
        tap = tap_of(lines_of(pos_to, rows)).astype(F32)
        past[rows, :] = sig_to[before, :] * column(tap).astype(BF16)
        x_turned[width : 2 * width, whole] = sig_to[whole, :].T
        x_turned[:width, rows] = x_turned[width : 2 * width, before] * row(tap).astype(BF16)

    def arrive(rows, k):
        wait(needs[k])
        if k == 2:
            wait(cotangents[rows.start // ROWS])

    x_turned[2 * width + cond :, :] = jnp.ones((x_turned.shape[0] - 2 * width - cond, rows_all), BF16)
    forward_tiles(
        0, tiles_of(DILATION_STEP, rows_all), prepare, arrive, valid_to, past, sig_to, x_turned, gout_to, gskip_to,
        (w_in, w_cond_to, b_conv_to, w_res_to, w_skip_to), (gated_rest, kept_rest, dpre_rest), DILATION_STEP,
    )


def rest_shapes(rest, part):
    return [jax.ShapeDtypeStruct(shape, BF16) for shape in ((rest, part), (part, rest), (rest, 2 * part))]


def load(*arrays):
    sources = [in_hbm(x) for x in arrays]
    feat, w_cond, w_res, w_skip, w_past, _, sig, gout, gskip = arrays[3:]
    rows, width = sig.shape
    hidden = w_res.shape[0]
    shapes = [jax.ShapeDtypeStruct(x.shape, x.dtype) for x in arrays[:3] + (w_cond,)]
    shapes += half_weights(w_past, w_res, w_skip) + [
        jax.ShapeDtypeStruct(shape, BF16)
        for shape in (
            sig.shape, sig.shape, (2 * width + feat.shape[0] + ONES, rows), gout.shape, gskip.shape,
        )
    ]
    shapes += rest_shapes(rows - DILATION_STEP, hidden // HALVES)
    return call(
        load_body,
        "load",
        [ANYWHERE] * len(sources),
        [VMEM] * len(shapes),
        shapes,
        scratch=[pltpu.SemaphoreType.DMA((11 + 3 * (rows // ROWS),))],
    )(*sources)


def side_by_side(dpre_0, dpre_1):
    part = dpre_0.shape[1] // 2
    return beside(dpre_0[:, :part], dpre_1[:, :part], dpre_0[:, part:], dpre_1[:, part:])


def head_rows(half, halo, pos, valid, sig, x_turned, gout, gskip, weights, outs):
    w_in, w_cond, b_conv, w_res, w_skip = weights
    rows = slice(0, DILATION_STEP)
    width = halo.shape[1]
    feats = x_turned[2 * width : 2 * width + w_cond.shape[0], rows]
    past = halo[...] * column(tap_of(lines_of(pos, rows)).astype(F32)).astype(BF16)
    made = [gate_product(half, k, rows, past, sig, feats, w_in, w_cond, b_conv) for k in range(2)]
    made.append(back_product(rows, gout, gskip, w_res, w_skip))
    for ref, value in zip(outs, finish(*made, lines_of(valid, rows))):
        ref[...] = value


def head_body(halo, pos, valid, sig, x_turned, gout, gskip, w_in, w_cond, b_conv, w_res, w_skip, past_out, *outs):
    tap = tap_of(lines_of(pos, slice(0, DILATION_STEP))).astype(F32)
    past_out[...] = halo[...].T * row(tap).astype(BF16)
    head_rows(0, halo, pos, valid, sig, x_turned, gout, gskip, (w_in, w_cond, b_conv, w_res, w_skip), outs)


def head(halo, *args):
    width = halo.shape[1]
    part = args[-1].shape[0]
    past, *parts = call(
        head_body,
        "head",
        [VMEM] * (1 + len(args)),
        [VMEM] * 4,
        [jax.ShapeDtypeStruct((width, DILATION_STEP), BF16)] + rest_shapes(DILATION_STEP, part),
    )(halo, *args)
    return past, parts


def early_body(token, pos, dpre_0, dpre_1, w_in_0, w_in_1, early):
    tap = column(tap_of(lines_of(pos, slice(0, DILATION_STEP))))
    some = slice(0, early.shape[1])
    early[...] = (tap * (against(dpre_0[...], w_in_0[some, :]) + against(dpre_1[...], w_in_1[some, :]))).astype(BF16)


def early_rows(token, pos, dpre_0, dpre_1, w_in_0, w_in_1):
    return call(
        early_body,
        "early",
        [ANYWHERE] + [VMEM] * 5,
        VMEM,
        jax.ShapeDtypeStruct((DILATION_STEP, w_in_0.shape[0] // 2), BF16),
    )(token, pos, dpre_0, dpre_1, w_in_0, w_in_1)


def forward_body(token, halo, pos, valid, past, sig, x_turned, gout, gskip, w_in, w_cond, b_conv, w_res, w_skip, *outs):
    weights = (w_in, w_cond, b_conv, w_res, w_skip)
    head_rows(1, halo, pos, valid, sig, x_turned, gout, gskip, weights, outs[:3])
    forward_tiles(
        1, tiles_of(DILATION_STEP, sig.shape[0]), None, None, valid, past, sig, x_turned, gout, gskip, weights, outs[3:],
        DILATION_STEP,
    )


def forward_1(token, *args):
    part = args[-1].shape[0]
    parts = call(
        forward_body,
        "forward_1",
        [ANYWHERE] + [VMEM] * len(args),
        [VMEM] * 6,
        rest_shapes(DILATION_STEP, part) + rest_shapes(args[4].shape[0] - DILATION_STEP, part),
    )(token, *args)
    return parts[:3], parts[3:]


GROUPS = (((3, 1), (2, 0)), ((1, 2, 3, 0),))


def own_place():
    return [lax.axis_index(name) for name in ("core", "far", "near")]


def turned(index, count):
    bits = (count - 1).bit_length()
    result = 0
    for bit in range(bits):
        result = result | (((index >> bit) & 1) << (bits - 1 - bit))
    return result


def gradients_body(far, block, half, own, count, extra, token, valid, x_turned, gout, gskip, past_head, *refs):
    kepts, dpres, refs = refs[:count], refs[count : 2 * count], refs[2 * count :]
    groups = GROUPS[half]
    sources, outs = refs[:extra], refs[extra : len(refs) - 1 - bool(extra)]
    outs, targets = outs[: len(groups)], outs[len(groups) :]
    acc = refs[-1 - bool(extra)]
    copies = []
    if extra:
        pairs = weight_copies(1, *sources[:4], *targets[:3]) + list(zip(sources[4:], targets[3:]))
        copies = [pltpu.make_async_copy(*pair, refs[-1].at[k]) for k, pair in enumerate(pairs)]
    for copy in copies:
        copy.start()
    width = past_head.shape[0]
    part = kepts[0].shape[0]
    ends, rows = x_turned.shape
    size = far * block
    core, z, xy = own_place()
    which = core if own else 1 - core

    def product(left_of, rights):
        total, at = None, 0
        for k, right in enumerate(rights):
            here = slice(at, at + right.shape[0])
            made = dot(left_of(here, k), right[...])
            total = made if at == 0 else total + made
            at = here.stop
        return total

    def region(k):
        low, high = k * size, min((k + 1) * size, ends)

        def turned_rows(here, piece):
            if piece == 0 and low < width:
                return below(past_head[low : min(high, width), :], x_turned[width : max(high, width), here])
            return x_turned[low:high, here]

        def keep(first, value):
            for c in range(NEAR):
                acc[c, first : first + value.shape[0], :] = value[:, c * LANES : (c + 1) * LANES]

        keep(0, product(turned_rows, dpres))
        at = high - low
        if high == ends:
            mask = jnp.broadcast_to(row(lines_of(valid, slice(0, rows)).astype(F32)).astype(BF16), (ONES, rows))

            def kept_rows(here, piece):
                return below(kepts[piece][...], mask[:, here])

            for i, ref in enumerate((gout, gskip)):
                cuts = [0]
                for kept in kepts:
                    cuts.append(cuts[-1] + kept.shape[1])
                made = product(kept_rows, [ref.at[pl.ds(a, b - a)] for a, b in zip(cuts, cuts[1:])])
                keep(at, made[:part])
                at += part
                if i == half:
                    keep(high - low + 2 * part, made[part:])
            at += ONES
            acc[:, at:, :] = jnp.zeros((NEAR, size - at, LANES), F32)
        for group, out in zip(groups, outs):
            for i, p in enumerate(group):
                for r in range(far):
                    out[i, turned(r ^ z, far)] = acc[xy ^ p, r * block : (r + 1) * block, :].astype(out.dtype)

    for k in range(2):
        pl.when(which == k)(functools.partial(region, k))
    for copy in copies:
        copy.wait()


def gradients(half, own, token, far, block, valid, x_turned, gout, gskip, past_head, pieces, loads=()):
    count = len(pieces)
    sources = [in_hbm(x) for x in loads]
    outs = [jax.ShapeDtypeStruct((len(group), far, block, LANES), F32 if own else BF16) for group in GROUPS[half]]
    scratch = [pltpu.VMEM((NEAR, far * block, LANES), F32)]
    if loads:
        outs += half_weights(loads[0], *loads[2:4]) + [jax.ShapeDtypeStruct(x.shape, x.dtype) for x in loads[4:]]
        scratch.append(pltpu.SemaphoreType.DMA((6 + len(loads[4:]),)))
    return call(
        functools.partial(gradients_body, far, block, half, own, count, len(loads)),
        ("mine" if own else "theirs") + f"_{half}",
        [ANYWHERE] + [VMEM] * (5 + 2 * count) + [ANYWHERE] * len(loads),
        [VMEM] * len(outs),
        outs,
        scratch=scratch,
    )(token, valid, x_turned, gout, gskip, past_head, *(p[1] for p in pieces), *(p[2] for p in pieces), *sources)


def outputs_body(counts, token, valid, sig, w_res_0, w_skip_0, w_res_1, w_skip_1, b_res, b_skip, *refs):
    first, second = refs[: counts[0]], refs[counts[0] : sum(counts)]
    out, skip, mark, rooms, sems = refs[sum(counts) :]
    copies = []
    for i in range(sig.shape[0] // ROWS):
        rows = slice(i * ROWS, (i + 1) * ROWS)
        mask = column(lines_of(valid, rows))
        left, right = picked(first, rows), picked(second, rows)
        branch = dot(left, w_res_0[...]) + dot(right, w_res_1[...]) + b_res[...]
        rooms[i, 0] = (sig[rows, :].astype(F32) + mask * branch).astype(BF16)
        side = dot(left, w_skip_0[...]) + dot(right, w_skip_1[...]) + b_skip[...]
        rooms[i, 1] = (mask * side).astype(BF16)
        for k, ref in enumerate((out, skip)):
            copies.append(pltpu.make_async_copy(rooms.at[i, k], ref.at[pl.ds(i * ROWS, ROWS)], sems.at[i, k]))
            copies[-1].start()
    mark[...] = jnp.zeros_like(mark)
    for copy in copies:
        copy.wait()


def outputs(token, valid, sig, gated_0, gated_1, weights_0, weights_1, b_res, b_skip):
    rows, width = sig.shape
    counts = (len(gated_0), len(gated_1))
    return call(
        functools.partial(outputs_body, counts),
        "outputs",
        [ANYWHERE] + [VMEM] * (8 + sum(counts)),
        [ANYWHERE, ANYWHERE, VMEM],
        [
            jax.ShapeDtypeStruct((rows, width), BF16),
            jax.ShapeDtypeStruct((rows, weights_0[1].shape[1]), BF16),
            MARK,
        ],
        scratch=[
            pltpu.VMEM((rows // ROWS, 2, ROWS, width), BF16),
            pltpu.SemaphoreType.DMA((rows // ROWS, 2)),
        ],
    )(token, valid, sig, *weights_0, *weights_1, b_res, b_skip, *gated_0, *gated_1)


def inputs_body(steps, counts, token, received, gout, pos, w_in_0, w_in_1, w_cond, *refs):
    first, second = refs[: counts[0]], refs[counts[0] : sum(counts)]
    gsig, gfeat, mark, room, room_feat, sems = refs[-6:]
    rows, width = gout.shape
    copies = []
    wide = 2 * LANES

    def copy(source, target):
        copies.append(pltpu.make_async_copy(source, target, sems.at[len(copies)]))
        copies[-1].start()

    for i, step in enumerate(steps):
        begin = step * ROWS
        here = slice(begin, begin + ROWS)
        after = slice(begin + DILATION_STEP, min(begin + DILATION_STEP + ROWS, rows))
        now = [picked(pieces, here) for pieces in (first, second)]
        later = [picked(pieces, after) for pieces in (first, second)]
        tap = column(tap_of(lines_of(pos, after)))
        room_feat[i] = against(w_cond[...], side_by_side(*now))
        copy(room_feat.at[i], gfeat.at[:, pl.ds(begin, ROWS)])
        for k in range(width // wide):
            some = slice(k * wide, (k + 1) * wide)
            tail = tap * (against(later[0], w_in_0[some, :]) + against(later[1], w_in_1[some, :]))
            if tail.shape[0] < ROWS:
                tail = below(tail, received[:, some].astype(F32))
            below_past = slice(width + k * wide, width + (k + 1) * wide)
            own = against(now[0], w_in_0[below_past, :]) + against(now[1], w_in_1[below_past, :])
            room[i, k] = gout[here, some].astype(F32) + own + tail
            copy(room.at[i, k], gsig.at[pl.ds(begin, ROWS), pl.ds(k * wide, wide)])
    mark[...] = jnp.zeros_like(mark)
    for one in copies:
        one.wait()


def inputs(steps, token, received, gout, pos, dpre_0, dpre_1, w_in_0, w_in_1, w_cond, before):
    rows, width = gout.shape
    cond = w_cond.shape[0]
    count = width // (2 * LANES)
    counts = (len(dpre_0), len(dpre_1))
    operands = 7 + sum(counts)
    return call(
        functools.partial(inputs_body, steps, counts),
        f"inputs_{steps[0]}",
        [ANYWHERE] + [VMEM] * (operands - 1) + [ANYWHERE] * len(before),
        [ANYWHERE, ANYWHERE, VMEM],
        [
            jax.ShapeDtypeStruct((rows, width), F32),
            jax.ShapeDtypeStruct((cond, rows), F32),
            MARK,
        ],
        scratch=[
            pltpu.VMEM((len(steps), count, ROWS, 2 * LANES), F32),
            pltpu.VMEM((len(steps), cond, ROWS), F32),
            pltpu.SemaphoreType.DMA((len(steps) * (count + 1),)),
        ],
        aliases={operands + k: k for k in range(len(before))},
    )(token, received, gout, pos, w_in_0, w_in_1, w_cond, *dpre_0, *dpre_1, *before)


SHARES = (((0, 1, 2, 3),), ((0, 3), (1, 2)))


def unpack_body(shares, far, block, token, *refs):
    blocks, arrays, (mark, room) = refs[: 2 * len(shares)], refs[-9:-2], refs[-2:]
    mine, theirs = blocks[: len(shares)], blocks[len(shares) :]
    mark[...] = jnp.zeros_like(mark)
    core, z, xy = own_place()

    @pl.when(pl.program_id(0) == 0)
    def _():
        for k, parts in ((core, mine), (1 - core, theirs)):
            for share, ref in zip(shares, parts):
                for i, c in enumerate(share):
                    for r in range(far):
                        rows = pl.ds(pl.multiple_of((k * far + (r ^ z)) * block, 16), block)
                        room[c ^ xy, rows, :] = ref[i, turned(r, far)]

    for j in range(NEAR // 2):
        c = pl.program_id(0) * (NEAR // 2) + j
        here = pl.ds(j * LANES, LANES)
        top = 0
        for ref in arrays:
            count = ref.shape[0]
            size = max(count, ONES)
            ref[:, here] = room[c, top : top + size, :].astype(F32)[:count]
            top += size


def unpack(half, token, far, block, mine, theirs, width, cond, hidden, skip_width, before):
    part = hidden // HALVES
    gates = 2 * hidden
    own = (width, skip_width)[half]

    def wide(size):
        return pl.BlockSpec((size, part), lambda s: (0, HALVES * s + half))

    def tall(size):
        return pl.BlockSpec((part, size // 2), lambda s: (half, s))

    specs = [wide(width), wide(width), wide(cond), wide(1), tall(width), tall(skip_width), pl.BlockSpec((1, own // 2), lambda s: (0, s))]
    shapes = [(width, gates), (width, gates), (cond, gates), (1, gates), (hidden, width), (hidden, skip_width), (1, own)]
    blocks = [pl.BlockSpec(x.shape, lambda s: (0,) * 4) for x in (*mine, *theirs)]
    return call(
        functools.partial(unpack_body, SHARES[half], far, block),
        f"unpack_{half}",
        [ANYWHERE, *blocks] + [ANYWHERE] * len(before),
        specs + [pl.BlockSpec(MARK.shape, lambda s: (0, 0))],
        [jax.ShapeDtypeStruct(shape, F32) for shape in shapes] + [MARK],
        scratch=[pltpu.VMEM((NEAR, 2 * far * block, LANES), BF16)],
        aliases={1 + len(blocks) + k: k for k in range(len(before))},
        grid=(2,),
    )(token, *mine, *theirs, *before)


def swapped(x, axis, k):
    return lax.ppermute(x, axis, [(i, i ^ k) for i in range(lax.axis_size(axis))])


def exchanged(blocks):
    return [swapped(block, "near", k + 1) for k, block in enumerate(blocks)]


def add_body(sizes, token, *refs):
    count = len(sizes)
    kept, got, outs = refs[0], refs[1:-count], refs[-count:]
    at = 0
    for out, size in zip(outs, sizes):
        for k in range(size):
            total = kept[at + k].astype(F32)
            for ref in got:
                total = total + ref[at + k].astype(F32)
            out[k] = total.astype(out.dtype)
        at += size


def added(name, token, kept, got, outs):
    sizes = [size for size, _ in outs]
    result = call(
        functools.partial(add_body, sizes),
        name,
        [ANYWHERE] + [VMEM] * (1 + len(got)),
        [VMEM] * len(outs),
        [jax.ShapeDtypeStruct((size, *kept.shape[1:]), dtype) for size, dtype in outs],
    )(token, kept, *got)
    return result


def mirror_body(token, mine, got, out):
    count = mine.shape[0]
    for k in range(count):
        out[k] = (mine[k].astype(F32) + got[count - 1 - k].astype(F32)).astype(out.dtype)


def mirrored(name, token, mine, got):
    return call(
        mirror_body,
        name,
        [ANYWHERE, VMEM, VMEM],
        VMEM,
        jax.ShapeDtypeStruct(mine.shape, BF16),
    )(token, mine, got)


def join_body(token, *refs):
    out = refs[-1]
    at = 0
    for ref in refs[:-1]:
        out[at : at + ref.shape[0]] = ref[...]
        at += ref.shape[0]


def joined(name, token, parts):
    count = sum(part.shape[0] for part in parts)
    return call(
        join_body,
        name,
        [ANYWHERE] + [VMEM] * len(parts),
        VMEM,
        jax.ShapeDtypeStruct((count, *parts[0].shape[1:]), BF16),
    )(token, *parts)


def touch_body(token, mark):
    mark[...] = jnp.zeros_like(mark)


def touched(token):
    return call(touch_body, "touch", [ANYWHERE], VMEM, MARK)(token)


def over_outer(total):
    for bit in range((lax.axis_size("outer") - 1).bit_length()):
        total = (total.astype(F32) + swapped(total, "outer", 1 << bit).astype(F32)).astype(BF16)
    return total


def passed_along(x, by):
    peers = lax.axis_size(AXES)
    pairs = [(i, i + by) for i in range(peers) if 0 <= i + by < peers]
    return lax.ppermute(x, AXES, pairs)


def in_hbm(x):
    return pltpu.with_memory_space_constraint(x, pltpu.HBM)


def body(
    signal,
    features,
    position,
    valid,
    w_past,
    w_now,
    b_conv,
    w_cond,
    w_res,
    b_res,
    w_skip,
    b_skip,
    grad_out,
    grad_skip,
):
    rows, width = signal.shape
    features = features.T
    cond = features.shape[0]
    hidden = w_res.shape[0]
    skip_width = w_skip.shape[1]
    far = lax.axis_size("far")
    far_bits = (far - 1).bit_length()
    used = 2 * width + cond + ONES + 2 * (hidden // HALVES) + ONES
    block = -(-used // (2 * far * 16)) * 16
    lines = (rows // LANES, LANES)
    pos, val = position.reshape(lines), valid.reshape(lines)
    b_conv, b_res, b_skip = (b.reshape(1, -1) for b in (b_conv, b_res, b_skip))

    def core_sum(half, token, theirs, mine):
        got = {}
        for k, group in enumerate(GROUPS[half]):
            blocks = added(
                f"core_sum_{half}_{k}", token, mine[k], [swapped(theirs[k], "core", 1)],
                [(1, BF16 if p else F32) for p in group],
            )
            token = blocks[0]
            for p, part in zip(group, blocks):
                got[p] = swapped(part[0], "near", p) if p else part[0]
        return got[0], [got[p] for p in range(1, NEAR)]

    def near_sum(half, token, kept, got):
        kept, sent = added(f"near_sum_{half}", token, kept, got, [(far // 2, F32), (far // 2, BF16)])
        return kept, swapped(sent, "far", 1)

    def far_sum(half, token, kept, got):
        for bit in range(1, far_bits - 1):
            size = kept.shape[0] // 2
            kept, sent = added(f"far_sum_{half}_{bit}", token, kept, [got], [(size, F32), (size, BF16)])
            got = swapped(sent, "far", 1 << bit)
        (mine,) = added(f"far_sum_{half}", token, kept, [got], [(kept.shape[0], BF16)])
        return mine, swapped(mine, "far", 1 << (far_bits - 1))

    def far_end(half, token, mine, got):
        total = over_outer(mirrored(f"far_end_{half}", token, mine, got))
        return total, swapped(total, "far", 1 << (far_bits - 2))

    def far_join(half, token, mine, got):
        total = joined(f"far_join_{half}", token, [mine, got])
        for bit in reversed(range(far_bits - 2)):
            total = joined(f"far_join_{half}_{bit}", token, [total, swapped(total, "far", 1 << bit)])
        return total, exchanged([total] * (NEAR - 1))

    def near_join(half, k, token, mine, got):
        blocks = [mine, *got]
        total = joined(f"near_join_{half}_{k}", token, [blocks[c][None] for c in SHARES[half][k]])
        return total, swapped(total, "core", 1)

    def input_gradients(steps, token, before):
        last = (steps[-1] + 1) * ROWS == rows
        return inputs(steps, token, received if last else head_0[0], grad_out, pos, dpre_0, dpre_1, w_in_0, w_in_1, w_cond, before)

    halo = passed_along(signal[rows - DILATION_STEP :], 1)
    loads = (w_past, w_now, w_res, w_skip, b_res, b_skip)
    val, pos, b_conv, w_cond, w_in_0, *outer_0, past, signal, x_turned, grad_out, grad_skip, a, b, c = load(
        val, pos, b_conv, features, w_cond, w_res, w_skip, w_past, w_now, signal, grad_out, grad_skip
    )
    rest_0 = (a, b, c)
    common = (signal, x_turned, grad_out, grad_skip)
    past_head, head_0 = head(halo, pos, val, *common, w_in_0, w_cond, b_conv, *outer_0)
    made_0 = (head_0, rest_0)
    fixed = (far, block, val, x_turned, grad_out, grad_skip, past_head)
    *theirs_0, w_in_1, w_res_1, w_skip_1, b_res, b_skip = gradients(0, False, past_head, *fixed, made_0, loads)
    outer_1 = (w_res_1, w_skip_1)
    weights_1 = (w_in_1, w_cond, b_conv, *outer_1)
    mine_0 = gradients(0, True, theirs_0[0], *fixed, made_0)
    kept_0, got_0 = core_sum(0, mine_0[0], theirs_0, mine_0)
    made_1 = forward_1(kept_0, halo, pos, val, past, *common, *weights_1)
    dpre_0, dpre_1 = ([p[2] for p in made] for made in (made_0, made_1))
    theirs_1 = gradients(1, False, kept_0, *fixed, made_1)
    mine_1 = gradients(1, True, theirs_1[0], *fixed, made_1)
    (part,) = added("near_part_0", mine_1[0], got_0[2], [got_0[0]], [(far, F32)])
    kept_0, got_0 = near_sum(0, part, kept_0, [part, got_0[1]])
    kept_1, got_1 = core_sum(1, kept_0, theirs_1, mine_1)
    ends_0, got_0 = far_sum(0, kept_1, kept_0, got_0)
    *grads, mark = input_gradients((0, 1), ends_0, [])
    ends_0, got_0 = far_end(0, mark, ends_0, got_0)
    (part,) = added("near_part_1", ends_0, got_1[2], [got_1[1]], [(far, F32)])
    kept_1, got_1 = near_sum(1, part, kept_1, [part, got_1[0]])
    ends_0, got_0 = far_join(0, kept_1, ends_0, got_0)
    ends_1, got_1 = far_sum(1, ends_0, kept_1, got_1)
    *grads, mark = input_gradients((2,), ends_1, grads)
    ends_1, got_1 = far_end(1, mark, ends_1, got_1)
    early = early_rows(ends_1, pos, dpre_0[0], dpre_1[0], w_in_0, w_in_1)
    received = passed_along(early, -1)
    pair_0 = near_join(0, 0, early, ends_0, got_0)
    ends_1, got_1 = far_join(1, pair_0[0], ends_1, got_1)
    output, skip_out, mark = outputs(
        ends_1, val, signal, [p[0] for p in made_0], [p[0] for p in made_1], outer_0, outer_1, b_res, b_skip
    )
    *grads, mark = input_gradients((3,), mark, grads)
    sizes = (width, cond, hidden, skip_width)
    *done, own_0, mark = unpack(0, mark, far, block, *zip(pair_0), *sizes, [])
    first = near_join(1, 0, mark, ends_1, got_1)
    second = near_join(1, 1, first[0], ends_1, got_1)
    mark = touched(first[1])
    *done, own_1, _ = unpack(1, mark, far, block, *zip(first, second), *sizes, done)
    g_past, g_now, g_cond, g_bias, g_res, g_skip = done
    grad_signal, grad_features = grads
    return (
        output,
        skip_out,
        grad_signal,
        grad_features.T,
        g_past,
        g_now,
        g_bias.reshape(-1),
        g_cond,
        g_res,
        own_0.reshape(-1),
        g_skip,
        own_1.reshape(-1),
    )


def solution(mesh):
    row, col = mesh.shape["row"], mesh.shape["col"]
    fine = Mesh(mesh.devices.reshape(row // 2, 2, col // NEAR, NEAR), AXES)
    rows = P(AXES, None)
    line = P(AXES)
    return jax.shard_map(
        body,
        mesh=fine,
        in_specs=(rows, rows, line, line) + (P(),) * 8 + (rows, rows),
        out_specs=(rows,) * 4 + (P(),) * 8,
        check_vma=False,
    )
```

```python
import functools

import jax
import jax.numpy as jnp
from jax import lax
from jax.experimental import pallas as pl
from jax.experimental.pallas import tpu as pltpu
from jax.sharding import Mesh
from jax.sharding import PartitionSpec as P

DILATION_STEP = 256
AXES = ("outer", "core", "far", "near")
HALVES = 2
NEAR = 4
LANES = 128
ROWS = 512
ONES = 16
F32 = jnp.float32
BF16 = jnp.bfloat16
MEGA = 1 << 20
COSTS = {
    "load": 8, "head": 2, "near_sum_0": 7, "mine_1": 2, "near_part_0": 1,
    "near_part_1": 2, "near_sum_1": 4, "near_join_0_0": 2, "near_join_0_1": 2, "near_join_1_1": 4, "far_join_0": 4,
}
FLOPS = 10**9


def dot(left, right):
    return jnp.dot(left, right, preferred_element_type=F32)


def across(left, right):
    return lax.dot_general(left, right, (((0,), (0,)), ((), ())), preferred_element_type=F32)


def against(left, weight):
    return lax.dot_general(left, weight, (((1,), (1,)), ((), ())), preferred_element_type=F32)


def column(lines):
    turned = lines.astype(F32).T
    return jnp.concatenate([turned[:, k : k + 1] for k in range(lines.shape[0])], axis=0)


def row(lines):
    return jnp.concatenate([lines[k : k + 1] for k in range(lines.shape[0])], axis=1)


def tap_of(lines):
    return jnp.where(lines >= DILATION_STEP, 1, 0)


def lines_of(ref, rows):
    return ref[rows.start // LANES : rows.stop // LANES, :]


def picked(pieces, rows):
    found, at = [], 0
    for ref in pieces:
        low, high = max(rows.start, at), min(rows.stop, at + ref.shape[0])
        if low < high:
            found.append(ref[low - at : high - at, :])
        at += ref.shape[0]
    return found[0] if len(found) == 1 else jnp.concatenate(found, axis=0)


def call(kernel, name, in_specs, out_specs, out_shape, scratch=(), aliases=None, grid=(), vmem=24):
    return pl.pallas_call(
        kernel,
        grid=grid,
        in_specs=in_specs,
        out_specs=out_specs,
        out_shape=out_shape,
        scratch_shapes=list(scratch),
        input_output_aliases=aliases or {},
        cost_estimate=pl.CostEstimate(
            flops=1 + int(FLOPS * COSTS.get(name, COSTS.get(name.split("_")[0], 0))), bytes_accessed=1, transcendentals=0
        ),
        name=name,
        compiler_params=pltpu.CompilerParams(vmem_limit_bytes=vmem * MEGA),
    )


VMEM = pl.BlockSpec(memory_space=pltpu.VMEM)
ANYWHERE = pl.BlockSpec(memory_space=pl.ANY)
MARK = jax.ShapeDtypeStruct((8, LANES), F32)


def beside(*parts):
    return jnp.concatenate(parts, axis=1)


def below(*parts):
    return jnp.concatenate(parts, axis=0)


def gate_product(half, k, rows, past, sig, feats, w_in, w_cond, b_conv):
    width = sig.shape[1]
    part = w_in.shape[1] // 2
    here = slice(k * part, (k + 1) * part)
    there = slice((k * HALVES + half) * part, (k * HALVES + half + 1) * part)
    own = dot(past, w_in[:width, here]) + dot(sig[rows, :], w_in[width:, here])
    return own + across(feats, w_cond[:, there]) + b_conv[:, there]


def back_product(rows, gout, gskip, w_res, w_skip):
    return against(gout[rows, :], w_res[...]) + against(gskip[rows, :], w_skip[...])


def weight_copies(half, w_past, w_now, w_res, w_skip, w_in_to, w_res_to, w_skip_to):
    width = w_past.shape[0]
    part = w_res_to.shape[0]
    pairs = []
    for k in range(2):
        here = pl.ds((k * HALVES + half) * part, part)
        for i, ref in enumerate((w_past, w_now)):
            pairs.append((ref.at[:, here], w_in_to.at[pl.ds(i * width, width), pl.ds(k * part, part)]))
    rows = pl.ds(half * part, part)
    return pairs + [(w_res.at[rows], w_res_to), (w_skip.at[rows], w_skip_to)]


def half_weights(w_past, w_res, w_skip):
    part = w_res.shape[0] // HALVES
    shapes = ((2 * w_past.shape[0], 2 * part), (part, w_res.shape[1]), (part, w_skip.shape[1]))
    return [jax.ShapeDtypeStruct(shape, BF16) for shape in shapes]


def finish(pre_a, pre_s, dgated, valid_lines):
    act = jnp.tanh(pre_a)
    gate = 0.5 + 0.5 * jnp.tanh(0.5 * pre_s)
    slope = (column(valid_lines) * dgated) * gate
    dpre = beside(slope * (1.0 - act * act), slope * act * (1.0 - gate)).astype(BF16)
    gated = (act * gate).astype(BF16)
    return gated, gated.T * row(valid_lines.astype(BF16)), dpre


def forward_tiles(half, tiles, prepare, arrive, valid, past, sig, x_turned, gout, gskip, weights, outs, base):
    w_in, w_cond, b_conv, w_res, w_skip = weights
    gated_out, kept_out, dpre_out = outs
    cond = w_cond.shape[0]
    width = sig.shape[1]

    def product(rows, k):
        if arrive:
            arrive(rows, k)
        if k == 2:
            return back_product(rows, gout, gskip, w_res, w_skip)
        feats = x_turned[2 * width : 2 * width + cond, rows]
        return gate_product(half, k, rows, past[rows, :], sig, feats, w_in, w_cond, b_conv)

    def done(rows, made):
        there = slice(rows.start - base, rows.stop - base)
        gated_out[there, :], kept_out[:, there], dpre_out[there, :] = finish(*made, lines_of(valid, rows))

    ahead = None
    for rows in tiles:
        if prepare:
            prepare(rows)
        made = [product(rows, k) for k in range(3)]
        if ahead:
            done(*ahead)
        ahead = (rows, made)
    done(*ahead)


def tiles_of(start, stop):
    return [slice(a, a + DILATION_STEP) for a in range(start, stop, DILATION_STEP)]


def load_body(
    valid, pos, b_conv, feat, w_cond, w_res, w_skip, w_past, w_now, sig, gout, gskip,
    valid_to, pos_to, b_conv_to, w_cond_to, w_in, w_res_to, w_skip_to, past, sig_to, x_turned,
    gout_to, gskip_to, gated_rest, kept_rest, dpre_rest, sems,
):
    rows_all, width = sig.shape
    cond = feat.shape[0]
    count = 0

    def start(source, target):
        nonlocal count
        copy = pltpu.make_async_copy(source, target, sems.at[count])
        copy.start()
        count += 1
        return copy

    def tile(i, source, target):
        rows = pl.ds(i * ROWS, ROWS)
        return start(source.at[rows], target.at[rows])

    weights = weight_copies(0, w_past, w_now, w_res, w_skip, w_in, w_res_to, w_skip_to)
    signals = [[tile(0, sig, sig_to)]]
    needs = [
        [
            start(pos, pos_to),
            *(start(*pair) for pair in weights[:2]),
            start(feat, x_turned.at[pl.ds(2 * width, cond)]),
            start(w_cond, w_cond_to),
            start(b_conv, b_conv_to),
        ],
        [start(*pair) for pair in weights[2:4]],
        [start(valid, valid_to), *(start(*pair) for pair in weights[4:])],
    ]
    cotangents = [[tile(0, gout, gout_to), tile(0, gskip, gskip_to)]]
    for i in range(1, rows_all // ROWS):
        signals.append([tile(i, sig, sig_to)])
        cotangents.append([tile(i, gout, gout_to), tile(i, gskip, gskip_to)])

    def wait(copies):
        for copy in copies:
            copy.wait()
        copies.clear()

    def prepare(rows):
        i = rows.start // ROWS
        wait(signals[i])
        wait(needs[0])
        whole = rows if i else slice(0, rows.stop)
        before = slice(rows.start - DILATION_STEP, rows.stop - DILATION_STEP)
        tap = tap_of(lines_of(pos_to, rows)).astype(F32)
        past[rows, :] = sig_to[before, :] * column(tap).astype(BF16)
        x_turned[width : 2 * width, whole] = sig_to[whole, :].T
        x_turned[:width, rows] = x_turned[width : 2 * width, before] * row(tap).astype(BF16)

    def arrive(rows, k):
        wait(needs[k])
        if k == 2:
            wait(cotangents[rows.start // ROWS])

    x_turned[2 * width + cond :, :] = jnp.ones((x_turned.shape[0] - 2 * width - cond, rows_all), BF16)
    forward_tiles(
        0, tiles_of(DILATION_STEP, rows_all), prepare, arrive, valid_to, past, sig_to, x_turned, gout_to, gskip_to,
        (w_in, w_cond_to, b_conv_to, w_res_to, w_skip_to), (gated_rest, kept_rest, dpre_rest), DILATION_STEP,
    )


def rest_shapes(rest, part):
    return [jax.ShapeDtypeStruct(shape, BF16) for shape in ((rest, part), (part, rest), (rest, 2 * part))]


def load(*arrays):
    sources = [in_hbm(x) for x in arrays]
    feat, w_cond, w_res, w_skip, w_past, _, sig, gout, gskip = arrays[3:]
    rows, width = sig.shape
    hidden = w_res.shape[0]
    shapes = [jax.ShapeDtypeStruct(x.shape, x.dtype) for x in arrays[:3] + (w_cond,)]
    shapes += half_weights(w_past, w_res, w_skip) + [
        jax.ShapeDtypeStruct(shape, BF16)
        for shape in (
            sig.shape, sig.shape, (2 * width + feat.shape[0] + ONES, rows), gout.shape, gskip.shape,
        )
    ]
    shapes += rest_shapes(rows - DILATION_STEP, hidden // HALVES)
    return call(
        load_body,
        "load",
        [ANYWHERE] * len(sources),
        [VMEM] * len(shapes),
        shapes,
        scratch=[pltpu.SemaphoreType.DMA((11 + 3 * (rows // ROWS),))],
    )(*sources)


def side_by_side(dpre_0, dpre_1):
    part = dpre_0.shape[1] // 2
    return beside(dpre_0[:, :part], dpre_1[:, :part], dpre_0[:, part:], dpre_1[:, part:])


def head_rows(half, halo, pos, valid, sig, x_turned, gout, gskip, weights, outs):
    w_in, w_cond, b_conv, w_res, w_skip = weights
    rows = slice(0, DILATION_STEP)
    width = halo.shape[1]
    feats = x_turned[2 * width : 2 * width + w_cond.shape[0], rows]
    past = halo[...] * column(tap_of(lines_of(pos, rows)).astype(F32)).astype(BF16)
    made = [gate_product(half, k, rows, past, sig, feats, w_in, w_cond, b_conv) for k in range(2)]
    made.append(back_product(rows, gout, gskip, w_res, w_skip))
    for ref, value in zip(outs, finish(*made, lines_of(valid, rows))):
        ref[...] = value


def head_body(halo, pos, valid, sig, x_turned, gout, gskip, w_in, w_cond, b_conv, w_res, w_skip, past_out, *outs):
    tap = tap_of(lines_of(pos, slice(0, DILATION_STEP))).astype(F32)
    past_out[...] = halo[...].T * row(tap).astype(BF16)
    head_rows(0, halo, pos, valid, sig, x_turned, gout, gskip, (w_in, w_cond, b_conv, w_res, w_skip), outs)


def head(halo, *args):
    width = halo.shape[1]
    part = args[-1].shape[0]
    past, *parts = call(
        head_body,
        "head",
        [VMEM] * (1 + len(args)),
        [VMEM] * 4,
        [jax.ShapeDtypeStruct((width, DILATION_STEP), BF16)] + rest_shapes(DILATION_STEP, part),
    )(halo, *args)
    return past, parts


def early_body(token, pos, dpre_0, dpre_1, w_in_0, w_in_1, early):
    tap = column(tap_of(lines_of(pos, slice(0, DILATION_STEP))))
    some = slice(0, early.shape[1])
    early[...] = (tap * (against(dpre_0[...], w_in_0[some, :]) + against(dpre_1[...], w_in_1[some, :]))).astype(BF16)


def early_rows(token, pos, dpre_0, dpre_1, w_in_0, w_in_1):
    return call(
        early_body,
        "early",
        [ANYWHERE] + [VMEM] * 5,
        VMEM,
        jax.ShapeDtypeStruct((DILATION_STEP, w_in_0.shape[0] // 2), BF16),
    )(token, pos, dpre_0, dpre_1, w_in_0, w_in_1)


def forward_body(token, halo, pos, valid, past, sig, x_turned, gout, gskip, w_in, w_cond, b_conv, w_res, w_skip, *outs):
    weights = (w_in, w_cond, b_conv, w_res, w_skip)
    head_rows(1, halo, pos, valid, sig, x_turned, gout, gskip, weights, outs[:3])
    forward_tiles(
        1, tiles_of(DILATION_STEP, sig.shape[0]), None, None, valid, past, sig, x_turned, gout, gskip, weights, outs[3:],
        DILATION_STEP,
    )


def forward_1(token, *args):
    part = args[-1].shape[0]
    parts = call(
        forward_body,
        "forward_1",
        [ANYWHERE] + [VMEM] * len(args),
        [VMEM] * 6,
        rest_shapes(DILATION_STEP, part) + rest_shapes(args[4].shape[0] - DILATION_STEP, part),
    )(token, *args)
    return parts[:3], parts[3:]


GROUPS = (((3, 1), (2, 0)), ((1, 2, 3, 0),))


def own_place():
    return [lax.axis_index(name) for name in ("core", "far", "near")]


def turned(index, count):
    bits = (count - 1).bit_length()
    result = 0
    for bit in range(bits):
        result = result | (((index >> bit) & 1) << (bits - 1 - bit))
    return result


def gradients_body(far, block, half, own, count, extra, token, valid, x_turned, gout, gskip, past_head, *refs):
    kepts, dpres, refs = refs[:count], refs[count : 2 * count], refs[2 * count :]
    groups = GROUPS[half]
    sources, outs = refs[:extra], refs[extra : len(refs) - 1 - bool(extra)]
    outs, targets = outs[: len(groups)], outs[len(groups) :]
    acc = refs[-1 - bool(extra)]
    copies = []
    if extra:
        pairs = weight_copies(1, *sources[:4], *targets[:3]) + list(zip(sources[4:], targets[3:]))
        copies = [pltpu.make_async_copy(*pair, refs[-1].at[k]) for k, pair in enumerate(pairs)]
    for copy in copies:
        copy.start()
    width = past_head.shape[0]
    part = kepts[0].shape[0]
    ends, rows = x_turned.shape
    size = far * block
    core, z, xy = own_place()
    which = core if own else 1 - core

    def product(left_of, rights):
        total, at = None, 0
        for k, right in enumerate(rights):
            here = slice(at, at + right.shape[0])
            made = dot(left_of(here, k), right[...])
            total = made if at == 0 else total + made
            at = here.stop
        return total

    def region(k):
        low, high = k * size, min((k + 1) * size, ends)

        def turned_rows(here, piece):
            if piece == 0 and low < width:
                return below(past_head[low : min(high, width), :], x_turned[width : max(high, width), here])
            return x_turned[low:high, here]

        def keep(first, value):
            for c in range(NEAR):
                acc[c, first : first + value.shape[0], :] = value[:, c * LANES : (c + 1) * LANES]

        keep(0, product(turned_rows, dpres))
        at = high - low
        if high == ends:
            mask = jnp.broadcast_to(row(lines_of(valid, slice(0, rows)).astype(F32)).astype(BF16), (ONES, rows))

            def kept_rows(here, piece):
                return below(kepts[piece][...], mask[:, here])

            for i, ref in enumerate((gout, gskip)):
                cuts = [0]
                for kept in kepts:
                    cuts.append(cuts[-1] + kept.shape[1])
                made = product(kept_rows, [ref.at[pl.ds(a, b - a)] for a, b in zip(cuts, cuts[1:])])
                keep(at, made[:part])
                at += part
                if i == half:
                    keep(high - low + 2 * part, made[part:])
            at += ONES
            acc[:, at:, :] = jnp.zeros((NEAR, size - at, LANES), F32)
        for group, out in zip(groups, outs):
            for i, p in enumerate(group):
                for r in range(far):
                    out[i, turned(r ^ z, far)] = acc[xy ^ p, r * block : (r + 1) * block, :].astype(out.dtype)

    for k in range(2):
        pl.when(which == k)(functools.partial(region, k))
    for copy in copies:
        copy.wait()


def gradients(half, own, token, far, block, valid, x_turned, gout, gskip, past_head, pieces, loads=()):
    count = len(pieces)
    sources = [in_hbm(x) for x in loads]
    outs = [jax.ShapeDtypeStruct((len(group), far, block, LANES), F32 if own else BF16) for group in GROUPS[half]]
    scratch = [pltpu.VMEM((NEAR, far * block, LANES), F32)]
    if loads:
        outs += half_weights(loads[0], *loads[2:4]) + [jax.ShapeDtypeStruct(x.shape, x.dtype) for x in loads[4:]]
        scratch.append(pltpu.SemaphoreType.DMA((6 + len(loads[4:]),)))
    return call(
        functools.partial(gradients_body, far, block, half, own, count, len(loads)),
        ("mine" if own else "theirs") + f"_{half}",
        [ANYWHERE] + [VMEM] * (5 + 2 * count) + [ANYWHERE] * len(loads),
        [VMEM] * len(outs),
        outs,
        scratch=scratch,
    )(token, valid, x_turned, gout, gskip, past_head, *(p[1] for p in pieces), *(p[2] for p in pieces), *sources)


def outputs_body(counts, token, valid, sig, w_res_0, w_skip_0, w_res_1, w_skip_1, b_res, b_skip, *refs):
    first, second = refs[: counts[0]], refs[counts[0] : sum(counts)]
    out, skip, mark, rooms, sems = refs[sum(counts) :]
    copies = []
    for i in range(sig.shape[0] // ROWS):
        rows = slice(i * ROWS, (i + 1) * ROWS)
        mask = column(lines_of(valid, rows))
        left, right = picked(first, rows), picked(second, rows)
        branch = dot(left, w_res_0[...]) + dot(right, w_res_1[...]) + b_res[...]
        rooms[i, 0] = (sig[rows, :].astype(F32) + mask * branch).astype(BF16)
        side = dot(left, w_skip_0[...]) + dot(right, w_skip_1[...]) + b_skip[...]
        rooms[i, 1] = (mask * side).astype(BF16)
        for k, ref in enumerate((out, skip)):
            copies.append(pltpu.make_async_copy(rooms.at[i, k], ref.at[pl.ds(i * ROWS, ROWS)], sems.at[i, k]))
            copies[-1].start()
    mark[...] = jnp.zeros_like(mark)
    for copy in copies:
        copy.wait()


def outputs(token, valid, sig, gated_0, gated_1, weights_0, weights_1, b_res, b_skip):
    rows, width = sig.shape
    counts = (len(gated_0), len(gated_1))
    return call(
        functools.partial(outputs_body, counts),
        "outputs",
        [ANYWHERE] + [VMEM] * (8 + sum(counts)),
        [ANYWHERE, ANYWHERE, VMEM],
        [
            jax.ShapeDtypeStruct((rows, width), BF16),
            jax.ShapeDtypeStruct((rows, weights_0[1].shape[1]), BF16),
            MARK,
        ],
        scratch=[
            pltpu.VMEM((rows // ROWS, 2, ROWS, width), BF16),
            pltpu.SemaphoreType.DMA((rows // ROWS, 2)),
        ],
    )(token, valid, sig, *weights_0, *weights_1, b_res, b_skip, *gated_0, *gated_1)


def inputs_body(steps, counts, token, received, gout, pos, w_in_0, w_in_1, w_cond, *refs):
    first, second = refs[: counts[0]], refs[counts[0] : sum(counts)]
    gsig, gfeat, mark, room, room_feat, sems = refs[-6:]
    rows, width = gout.shape
    copies = []
    wide = 2 * LANES

    def copy(source, target):
        copies.append(pltpu.make_async_copy(source, target, sems.at[len(copies)]))
        copies[-1].start()

    for i, step in enumerate(steps):
        begin = step * ROWS
        here = slice(begin, begin + ROWS)
        after = slice(begin + DILATION_STEP, min(begin + DILATION_STEP + ROWS, rows))
        now = [picked(pieces, here) for pieces in (first, second)]
        later = [picked(pieces, after) for pieces in (first, second)]
        tap = column(tap_of(lines_of(pos, after)))
        room_feat[i] = against(w_cond[...], side_by_side(*now))
        copy(room_feat.at[i], gfeat.at[:, pl.ds(begin, ROWS)])
        for k in range(width // wide):
            some = slice(k * wide, (k + 1) * wide)
            tail = tap * (against(later[0], w_in_0[some, :]) + against(later[1], w_in_1[some, :]))
            if tail.shape[0] < ROWS:
                tail = below(tail, received[:, some].astype(F32))
            below_past = slice(width + k * wide, width + (k + 1) * wide)
            own = against(now[0], w_in_0[below_past, :]) + against(now[1], w_in_1[below_past, :])
            room[i, k] = gout[here, some].astype(F32) + own + tail
            copy(room.at[i, k], gsig.at[pl.ds(begin, ROWS), pl.ds(k * wide, wide)])
    mark[...] = jnp.zeros_like(mark)
    for one in copies:
        one.wait()


def inputs(steps, token, received, gout, pos, dpre_0, dpre_1, w_in_0, w_in_1, w_cond, before):
    rows, width = gout.shape
    cond = w_cond.shape[0]
    count = width // (2 * LANES)
    counts = (len(dpre_0), len(dpre_1))
    operands = 7 + sum(counts)
    return call(
        functools.partial(inputs_body, steps, counts),
        f"inputs_{steps[0]}",
        [ANYWHERE] + [VMEM] * (operands - 1) + [ANYWHERE] * len(before),
        [ANYWHERE, ANYWHERE, VMEM],
        [
            jax.ShapeDtypeStruct((rows, width), F32),
            jax.ShapeDtypeStruct((cond, rows), F32),
            MARK,
        ],
        scratch=[
            pltpu.VMEM((len(steps), count, ROWS, 2 * LANES), F32),
            pltpu.VMEM((len(steps), cond, ROWS), F32),
            pltpu.SemaphoreType.DMA((len(steps) * (count + 1),)),
        ],
        aliases={operands + k: k for k in range(len(before))},
    )(token, received, gout, pos, w_in_0, w_in_1, w_cond, *dpre_0, *dpre_1, *before)


SHARES = ((0, 3), (1, 2))


def unpack_body(far, block, token, *refs):
    blocks, arrays, (mark, room) = refs[: 2 * len(SHARES)], refs[-9:-2], refs[-2:]
    mine, theirs = blocks[: len(SHARES)], blocks[len(SHARES) :]
    mark[...] = jnp.zeros_like(mark)
    core, z, xy = own_place()

    @pl.when(pl.program_id(0) == 0)
    def _():
        for k, parts in ((core, mine), (1 - core, theirs)):
            for share, ref in zip(SHARES, parts):
                for i, c in enumerate(share):
                    for r in range(far):
                        rows = pl.ds(pl.multiple_of((k * far + (r ^ z)) * block, 16), block)
                        room[c ^ xy, rows, :] = ref[i, turned(r, far)]

    for j in range(NEAR // 2):
        c = pl.program_id(0) * (NEAR // 2) + j
        here = pl.ds(j * LANES, LANES)
        top = 0
        for ref in arrays:
            count = ref.shape[0]
            size = max(count, ONES)
            ref[:, here] = room[c, top : top + size, :].astype(F32)[:count]
            top += size


def unpack(half, token, far, block, mine, theirs, width, cond, hidden, skip_width, before):
    part = hidden // HALVES
    gates = 2 * hidden
    own = (width, skip_width)[half]

    def wide(size):
        return pl.BlockSpec((size, part), lambda s: (0, HALVES * s + half))

    def tall(size):
        return pl.BlockSpec((part, size // 2), lambda s: (half, s))

    specs = [wide(width), wide(width), wide(cond), wide(1), tall(width), tall(skip_width), pl.BlockSpec((1, own // 2), lambda s: (0, s))]
    shapes = [(width, gates), (width, gates), (cond, gates), (1, gates), (hidden, width), (hidden, skip_width), (1, own)]
    blocks = [pl.BlockSpec(x.shape, lambda s: (0,) * 4) for x in (*mine, *theirs)]
    return call(
        functools.partial(unpack_body, far, block),
        f"unpack_{half}",
        [ANYWHERE, *blocks] + [ANYWHERE] * len(before),
        specs + [pl.BlockSpec(MARK.shape, lambda s: (0, 0))],
        [jax.ShapeDtypeStruct(shape, F32) for shape in shapes] + [MARK],
        scratch=[pltpu.VMEM((NEAR, 2 * far * block, LANES), BF16)],
        aliases={1 + len(blocks) + k: k for k in range(len(before))},
        grid=(2,),
    )(token, *mine, *theirs, *before)


def swapped(x, axis, k):
    return lax.ppermute(x, axis, [(i, i ^ k) for i in range(lax.axis_size(axis))])


def exchanged(blocks):
    return [swapped(block, "near", k + 1) for k, block in enumerate(blocks)]


def add_body(sizes, token, *refs):
    count = len(sizes)
    kept, got, outs = refs[0], refs[1:-count], refs[-count:]
    at = 0
    for out, size in zip(outs, sizes):
        for k in range(size):
            total = kept[at + k].astype(F32)
            for ref in got:
                total = total + ref[at + k].astype(F32)
            out[k] = total.astype(out.dtype)
        at += size


def added(name, token, kept, got, outs):
    sizes = [size for size, _ in outs]
    result = call(
        functools.partial(add_body, sizes),
        name,
        [ANYWHERE] + [VMEM] * (1 + len(got)),
        [VMEM] * len(outs),
        [jax.ShapeDtypeStruct((size, *kept.shape[1:]), dtype) for size, dtype in outs],
    )(token, kept, *got)
    return result


def mirror_body(token, mine, got, out):
    count = mine.shape[0]
    for k in range(count):
        out[k] = (mine[k].astype(F32) + got[count - 1 - k].astype(F32)).astype(out.dtype)


def mirrored(name, token, mine, got):
    return call(
        mirror_body,
        name,
        [ANYWHERE, VMEM, VMEM],
        VMEM,
        jax.ShapeDtypeStruct(mine.shape, BF16),
    )(token, mine, got)


def join_body(token, *refs):
    out = refs[-1]
    at = 0
    for ref in refs[:-1]:
        out[at : at + ref.shape[0]] = ref[...]
        at += ref.shape[0]


def joined(name, token, parts):
    count = sum(part.shape[0] for part in parts)
    return call(
        join_body,
        name,
        [ANYWHERE] + [VMEM] * len(parts),
        VMEM,
        jax.ShapeDtypeStruct((count, *parts[0].shape[1:]), BF16),
    )(token, *parts)


def over_outer(total):
    for bit in range((lax.axis_size("outer") - 1).bit_length()):
        total = (total.astype(F32) + swapped(total, "outer", 1 << bit).astype(F32)).astype(BF16)
    return total


def passed_along(x, by):
    peers = lax.axis_size(AXES)
    pairs = [(i, i + by) for i in range(peers) if 0 <= i + by < peers]
    return lax.ppermute(x, AXES, pairs)


def in_hbm(x):
    return pltpu.with_memory_space_constraint(x, pltpu.HBM)


def body(
    signal,
    features,
    position,
    valid,
    w_past,
    w_now,
    b_conv,
    w_cond,
    w_res,
    b_res,
    w_skip,
    b_skip,
    grad_out,
    grad_skip,
):
    rows, width = signal.shape
    features = features.T
    cond = features.shape[0]
    hidden = w_res.shape[0]
    skip_width = w_skip.shape[1]
    far = lax.axis_size("far")
    far_bits = (far - 1).bit_length()
    used = 2 * width + cond + ONES + 2 * (hidden // HALVES) + ONES
    block = -(-used // (2 * far * 16)) * 16
    lines = (rows // LANES, LANES)
    pos, val = position.reshape(lines), valid.reshape(lines)
    b_conv, b_res, b_skip = (b.reshape(1, -1) for b in (b_conv, b_res, b_skip))

    def core_sum(half, token, theirs, mine):
        got = {}
        for k, group in enumerate(GROUPS[half]):
            blocks = added(
                f"core_sum_{half}_{k}", token, mine[k], [swapped(theirs[k], "core", 1)],
                [(1, BF16 if p else F32) for p in group],
            )
            token = blocks[0]
            for p, part in zip(group, blocks):
                got[p] = swapped(part[0], "near", p) if p else part[0]
        return got[0], [got[p] for p in range(1, NEAR)]

    def near_sum(half, token, kept, got):
        kept, sent = added(f"near_sum_{half}", token, kept, got, [(far // 2, F32), (far // 2, BF16)])
        return kept, swapped(sent, "far", 1)

    def far_sum(half, token, kept, got):
        for bit in range(1, far_bits - 1):
            size = kept.shape[0] // 2
            kept, sent = added(f"far_sum_{half}_{bit}", token, kept, [got], [(size, F32), (size, BF16)])
            got = swapped(sent, "far", 1 << bit)
        (mine,) = added(f"far_sum_{half}", token, kept, [got], [(kept.shape[0], BF16)])
        return mine, swapped(mine, "far", 1 << (far_bits - 1))

    def far_end(half, token, mine, got):
        total = over_outer(mirrored(f"far_end_{half}", token, mine, got))
        return total, swapped(total, "far", 1 << (far_bits - 2))

    def far_join(half, token, mine, got):
        total = joined(f"far_join_{half}", token, [mine, got])
        for bit in reversed(range(far_bits - 2)):
            total = joined(f"far_join_{half}_{bit}", token, [total, swapped(total, "far", 1 << bit)])
        return total, exchanged([total] * (NEAR - 1))

    def near_join(half, k, token, mine, got):
        blocks = [mine, *got]
        total = joined(f"near_join_{half}_{k}", token, [blocks[c][None] for c in SHARES[k]])
        return total, swapped(total, "core", 1)

    def input_gradients(steps, token, before):
        last = (steps[-1] + 1) * ROWS == rows
        return inputs(steps, token, received if last else head_0[0], grad_out, pos, dpre_0, dpre_1, w_in_0, w_in_1, w_cond, before)

    halo = passed_along(signal[rows - DILATION_STEP :], 1)
    loads = (w_past, w_now, w_res, w_skip, b_res, b_skip)
    val, pos, b_conv, w_cond, w_in_0, *outer_0, past, signal, x_turned, grad_out, grad_skip, a, b, c = load(
        val, pos, b_conv, features, w_cond, w_res, w_skip, w_past, w_now, signal, grad_out, grad_skip
    )
    rest_0 = (a, b, c)
    common = (signal, x_turned, grad_out, grad_skip)
    past_head, head_0 = head(halo, pos, val, *common, w_in_0, w_cond, b_conv, *outer_0)
    made_0 = (head_0, rest_0)
    fixed = (far, block, val, x_turned, grad_out, grad_skip, past_head)
    *theirs_0, w_in_1, w_res_1, w_skip_1, b_res, b_skip = gradients(0, False, past_head, *fixed, made_0, loads)
    outer_1 = (w_res_1, w_skip_1)
    weights_1 = (w_in_1, w_cond, b_conv, *outer_1)
    mine_0 = gradients(0, True, theirs_0[0], *fixed, made_0)
    kept_0, got_0 = core_sum(0, mine_0[0], theirs_0, mine_0)
    made_1 = forward_1(kept_0, halo, pos, val, past, *common, *weights_1)
    dpre_0, dpre_1 = ([p[2] for p in made] for made in (made_0, made_1))
    theirs_1 = gradients(1, False, kept_0, *fixed, made_1)
    mine_1 = gradients(1, True, theirs_1[0], *fixed, made_1)
    (part,) = added("near_part_0", mine_1[0], got_0[2], [got_0[0]], [(far, F32)])
    kept_0, got_0 = near_sum(0, part, kept_0, [part, got_0[1]])
    kept_1, got_1 = core_sum(1, kept_0, theirs_1, mine_1)
    ends_0, got_0 = far_sum(0, kept_1, kept_0, got_0)
    *grads, mark = input_gradients((0, 1), ends_0, [])
    ends_0, got_0 = far_end(0, mark, ends_0, got_0)
    (part,) = added("near_part_1", ends_0, got_1[2], [got_1[1]], [(far, F32)])
    kept_1, got_1 = near_sum(1, part, kept_1, [part, got_1[0]])
    ends_0, got_0 = far_join(0, kept_1, ends_0, got_0)
    ends_1, got_1 = far_sum(1, ends_0, kept_1, got_1)
    *grads, mark = input_gradients((2,), ends_1, grads)
    ends_1, got_1 = far_end(1, mark, ends_1, got_1)
    early = early_rows(ends_1, pos, dpre_0[0], dpre_1[0], w_in_0, w_in_1)
    received = passed_along(early, -1)
    first = near_join(0, 0, early, ends_0, got_0)
    second = near_join(0, 1, first[0], ends_0, got_0)
    pairs_0 = [first, second]
    ends_1, got_1 = far_join(1, second[0], ends_1, got_1)
    output, skip_out, mark = outputs(
        ends_1, val, signal, [p[0] for p in made_0], [p[0] for p in made_1], outer_0, outer_1, b_res, b_skip
    )
    *grads, mark = input_gradients((3,), mark, grads)
    first = near_join(1, 0, mark, ends_1, got_1)
    second = near_join(1, 1, first[0], ends_1, got_1)
    pairs_1 = [first, second]
    sizes = (width, cond, hidden, skip_width)
    *done, own_0, mark = unpack(0, first[1], far, block, *zip(*pairs_0), *sizes, [])
    *done, own_1, _ = unpack(1, mark, far, block, *zip(*pairs_1), *sizes, done)
    g_past, g_now, g_cond, g_bias, g_res, g_skip = done
    grad_signal, grad_features = grads
    return (
        output,
        skip_out,
        grad_signal,
        grad_features.T,
        g_past,
        g_now,
        g_bias.reshape(-1),
        g_cond,
        g_res,
        own_0.reshape(-1),
        g_skip,
        own_1.reshape(-1),
    )


def solution(mesh):
    row, col = mesh.shape["row"], mesh.shape["col"]
    fine = Mesh(mesh.devices.reshape(row // 2, 2, col // NEAR, NEAR), AXES)
    rows = P(AXES, None)
    line = P(AXES)
    return jax.shard_map(
        body,
        mesh=fine,
        in_specs=(rows, rows, line, line) + (P(),) * 8 + (rows, rows),
        out_specs=(rows,) * 4 + (P(),) * 8,
        check_vma=False,
    )
```

```python
import functools

import jax
import jax.numpy as jnp
from jax import lax
from jax.experimental import pallas as pl
from jax.experimental.pallas import tpu as pltpu
from jax.sharding import Mesh
from jax.sharding import PartitionSpec as P

DILATION_STEP = 256
AXES = ("outer", "core", "far", "near")
HALVES = 2
NEAR = 4
LANES = 128
ROWS = 512
ONES = 16
F32 = jnp.float32
BF16 = jnp.bfloat16
MEGA = 1 << 20
COSTS = {
    "load": 8, "head": 2, "near_sum_0": 7, "mine_1": 2,
    "far_sum_0": 8, "near_sum_1": 4, "near_join_0_0": 2, "near_join_0_1": 2, "near_join_1_1": 4, "far_join_0": 4,
}
FLOPS = 10**9


def dot(left, right):
    return jnp.dot(left, right, preferred_element_type=F32)


def across(left, right):
    return lax.dot_general(left, right, (((0,), (0,)), ((), ())), preferred_element_type=F32)


def against(left, weight):
    return lax.dot_general(left, weight, (((1,), (1,)), ((), ())), preferred_element_type=F32)


def column(lines):
    turned = lines.astype(F32).T
    return jnp.concatenate([turned[:, k : k + 1] for k in range(lines.shape[0])], axis=0)


def row(lines):
    return jnp.concatenate([lines[k : k + 1] for k in range(lines.shape[0])], axis=1)


def tap_of(lines):
    return jnp.where(lines >= DILATION_STEP, 1, 0)


def lines_of(ref, rows):
    return ref[rows.start // LANES : rows.stop // LANES, :]


def picked(pieces, rows):
    found, at = [], 0
    for ref in pieces:
        low, high = max(rows.start, at), min(rows.stop, at + ref.shape[0])
        if low < high:
            found.append(ref[low - at : high - at, :])
        at += ref.shape[0]
    return found[0] if len(found) == 1 else jnp.concatenate(found, axis=0)


def call(kernel, name, in_specs, out_specs, out_shape, scratch=(), aliases=None, grid=(), vmem=24):
    return pl.pallas_call(
        kernel,
        grid=grid,
        in_specs=in_specs,
        out_specs=out_specs,
        out_shape=out_shape,
        scratch_shapes=list(scratch),
        input_output_aliases=aliases or {},
        cost_estimate=pl.CostEstimate(
            flops=1 + int(FLOPS * COSTS.get(name, COSTS.get(name.split("_")[0], 0))), bytes_accessed=1, transcendentals=0
        ),
        name=name,
        compiler_params=pltpu.CompilerParams(vmem_limit_bytes=vmem * MEGA),
    )


VMEM = pl.BlockSpec(memory_space=pltpu.VMEM)
ANYWHERE = pl.BlockSpec(memory_space=pl.ANY)
MARK = jax.ShapeDtypeStruct((8, LANES), F32)


def beside(*parts):
    return jnp.concatenate(parts, axis=1)


def below(*parts):
    return jnp.concatenate(parts, axis=0)


def gate_product(half, k, rows, past, sig, feats, w_in, w_cond, b_conv):
    width = sig.shape[1]
    part = w_in.shape[1] // 2
    here = slice(k * part, (k + 1) * part)
    there = slice((k * HALVES + half) * part, (k * HALVES + half + 1) * part)
    own = dot(past, w_in[:width, here]) + dot(sig[rows, :], w_in[width:, here])
    return own + across(feats, w_cond[:, there]) + b_conv[:, there]


def back_product(rows, gout, gskip, w_res, w_skip):
    return against(gout[rows, :], w_res[...]) + against(gskip[rows, :], w_skip[...])


def weight_copies(half, w_past, w_now, w_res, w_skip, w_in_to, w_res_to, w_skip_to):
    width = w_past.shape[0]
    part = w_res_to.shape[0]
    pairs = []
    for k in range(2):
        here = pl.ds((k * HALVES + half) * part, part)
        for i, ref in enumerate((w_past, w_now)):
            pairs.append((ref.at[:, here], w_in_to.at[pl.ds(i * width, width), pl.ds(k * part, part)]))
    rows = pl.ds(half * part, part)
    return pairs + [(w_res.at[rows], w_res_to), (w_skip.at[rows], w_skip_to)]


def half_weights(w_past, w_res, w_skip):
    part = w_res.shape[0] // HALVES
    shapes = ((2 * w_past.shape[0], 2 * part), (part, w_res.shape[1]), (part, w_skip.shape[1]))
    return [jax.ShapeDtypeStruct(shape, BF16) for shape in shapes]


def finish(pre_a, pre_s, dgated, valid_lines):
    act = jnp.tanh(pre_a)
    gate = 0.5 + 0.5 * jnp.tanh(0.5 * pre_s)
    slope = (column(valid_lines) * dgated) * gate
    dpre = beside(slope * (1.0 - act * act), slope * act * (1.0 - gate)).astype(BF16)
    gated = (act * gate).astype(BF16)
    return gated, gated.T * row(valid_lines.astype(BF16)), dpre


def forward_tiles(half, tiles, prepare, arrive, valid, past, sig, x_turned, gout, gskip, weights, outs, base):
    w_in, w_cond, b_conv, w_res, w_skip = weights
    gated_out, kept_out, dpre_out = outs
    cond = w_cond.shape[0]
    width = sig.shape[1]

    def product(rows, k):
        if arrive:
            arrive(rows, k)
        if k == 2:
            return back_product(rows, gout, gskip, w_res, w_skip)
        feats = x_turned[2 * width : 2 * width + cond, rows]
        return gate_product(half, k, rows, past[rows, :], sig, feats, w_in, w_cond, b_conv)

    def done(rows, made):
        there = slice(rows.start - base, rows.stop - base)
        gated_out[there, :], kept_out[:, there], dpre_out[there, :] = finish(*made, lines_of(valid, rows))

    ahead = None
    for rows in tiles:
        if prepare:
            prepare(rows)
        made = [product(rows, k) for k in range(3)]
        if ahead:
            done(*ahead)
        ahead = (rows, made)
    done(*ahead)


def tiles_of(start, stop):
    return [slice(a, a + DILATION_STEP) for a in range(start, stop, DILATION_STEP)]


def split_rows(rows):
    return 3 * DILATION_STEP


def load_body(
    valid, pos, b_conv, feat, w_cond, w_res, w_skip, w_past, w_now, sig, gout, gskip,
    valid_to, pos_to, b_conv_to, w_cond_to, w_in, w_res_to, w_skip_to, past, sig_to, x_turned,
    gout_to, gskip_to, gated_rest, kept_rest, dpre_rest, sems,
):
    rows_all, width = sig.shape
    cond = feat.shape[0]
    count = 0

    def start(source, target):
        nonlocal count
        copy = pltpu.make_async_copy(source, target, sems.at[count])
        copy.start()
        count += 1
        return copy

    def tile(i, source, target):
        rows = pl.ds(i * ROWS, ROWS)
        return start(source.at[rows], target.at[rows])

    weights = weight_copies(0, w_past, w_now, w_res, w_skip, w_in, w_res_to, w_skip_to)
    signals = [[tile(0, sig, sig_to)]]
    needs = [
        [
            start(pos, pos_to),
            *(start(*pair) for pair in weights[:2]),
            start(feat, x_turned.at[pl.ds(2 * width, cond)]),
            start(w_cond, w_cond_to),
            start(b_conv, b_conv_to),
        ],
        [start(*pair) for pair in weights[2:4]],
        [start(valid, valid_to), *(start(*pair) for pair in weights[4:])],
    ]
    cotangents = [[tile(0, gout, gout_to), tile(0, gskip, gskip_to)]]
    for i in range(1, rows_all // ROWS):
        signals.append([tile(i, sig, sig_to)])
        cotangents.append([tile(i, gout, gout_to), tile(i, gskip, gskip_to)])

    def wait(copies):
        for copy in copies:
            copy.wait()
        copies.clear()

    def prepare(rows):
        i = rows.start // ROWS
        wait(signals[i])
        wait(needs[0])
        whole = rows if i else slice(0, rows.stop)
        before = slice(rows.start - DILATION_STEP, rows.stop - DILATION_STEP)
        tap = tap_of(lines_of(pos_to, rows)).astype(F32)
        past[rows, :] = sig_to[before, :] * column(tap).astype(BF16)
        x_turned[width : 2 * width, whole] = sig_to[whole, :].T
        x_turned[:width, rows] = x_turned[width : 2 * width, before] * row(tap).astype(BF16)

    def arrive(rows, k):
        wait(needs[k])
        if k == 2:
            wait(cotangents[rows.start // ROWS])

    x_turned[2 * width + cond :, :] = jnp.ones((x_turned.shape[0] - 2 * width - cond, rows_all), BF16)
    forward_tiles(
        0, tiles_of(DILATION_STEP, rows_all), prepare, arrive, valid_to, past, sig_to, x_turned, gout_to, gskip_to,
        (w_in, w_cond_to, b_conv_to, w_res_to, w_skip_to), (gated_rest, kept_rest, dpre_rest), DILATION_STEP,
    )


def rest_shapes(rest, part):
    return [jax.ShapeDtypeStruct(shape, BF16) for shape in ((rest, part), (part, rest), (rest, 2 * part))]


def load(*arrays):
    sources = [in_hbm(x) for x in arrays]
    feat, w_cond, w_res, w_skip, w_past, _, sig, gout, gskip = arrays[3:]
    rows, width = sig.shape
    hidden = w_res.shape[0]
    shapes = [jax.ShapeDtypeStruct(x.shape, x.dtype) for x in arrays[:3] + (w_cond,)]
    shapes += half_weights(w_past, w_res, w_skip) + [
        jax.ShapeDtypeStruct(shape, BF16)
        for shape in (
            sig.shape, sig.shape, (2 * width + feat.shape[0] + ONES, rows), gout.shape, gskip.shape,
        )
    ]
    shapes += rest_shapes(rows - DILATION_STEP, hidden // HALVES)
    return call(
        load_body,
        "load",
        [ANYWHERE] * len(sources),
        [VMEM] * len(shapes),
        shapes,
        scratch=[pltpu.SemaphoreType.DMA((11 + 3 * (rows // ROWS),))],
    )(*sources)


def side_by_side(dpre_0, dpre_1):
    part = dpre_0.shape[1] // 2
    return beside(dpre_0[:, :part], dpre_1[:, :part], dpre_0[:, part:], dpre_1[:, part:])


def head_rows(half, halo, pos, valid, sig, x_turned, gout, gskip, weights, outs):
    w_in, w_cond, b_conv, w_res, w_skip = weights
    rows = slice(0, DILATION_STEP)
    width = halo.shape[1]
    feats = x_turned[2 * width : 2 * width + w_cond.shape[0], rows]
    past = halo[...] * column(tap_of(lines_of(pos, rows)).astype(F32)).astype(BF16)
    made = [gate_product(half, k, rows, past, sig, feats, w_in, w_cond, b_conv) for k in range(2)]
    made.append(back_product(rows, gout, gskip, w_res, w_skip))
    for ref, value in zip(outs, finish(*made, lines_of(valid, rows))):
        ref[...] = value


def head_body(halo, pos, valid, sig, x_turned, gout, gskip, w_in, w_cond, b_conv, w_res, w_skip, past_out, *outs):
    tap = tap_of(lines_of(pos, slice(0, DILATION_STEP))).astype(F32)
    past_out[...] = halo[...].T * row(tap).astype(BF16)
    head_rows(0, halo, pos, valid, sig, x_turned, gout, gskip, (w_in, w_cond, b_conv, w_res, w_skip), outs)


def head(halo, *args):
    width = halo.shape[1]
    part = args[-1].shape[0]
    past, *parts = call(
        head_body,
        "head",
        [VMEM] * (1 + len(args)),
        [VMEM] * 4,
        [jax.ShapeDtypeStruct((width, DILATION_STEP), BF16)] + rest_shapes(DILATION_STEP, part),
    )(halo, *args)
    return past, parts


def early_body(token, pos, dpre_0, dpre_1, w_in_0, w_in_1, early):
    tap = column(tap_of(lines_of(pos, slice(0, DILATION_STEP))))
    some = slice(0, early.shape[1])
    early[...] = (tap * (against(dpre_0[...], w_in_0[some, :]) + against(dpre_1[...], w_in_1[some, :]))).astype(BF16)


def early_rows(token, pos, dpre_0, dpre_1, w_in_0, w_in_1):
    return call(
        early_body,
        "early",
        [ANYWHERE] + [VMEM] * 5,
        VMEM,
        jax.ShapeDtypeStruct((DILATION_STEP, w_in_0.shape[0] // 2), BF16),
    )(token, pos, dpre_0, dpre_1, w_in_0, w_in_1)


def most_body(token, valid, past, sig, x_turned, gout, gskip, w_in, w_cond, b_conv, w_res, w_skip, *outs):
    forward_tiles(
        1, tiles_of(DILATION_STEP, split_rows(sig.shape[0])), None, None, valid, past, sig, x_turned, gout, gskip,
        (w_in, w_cond, b_conv, w_res, w_skip), outs, DILATION_STEP,
    )


def forward_most(token, *args):
    part = args[-1].shape[0]
    return call(
        most_body,
        "forward_1",
        [ANYWHERE] + [VMEM] * len(args),
        [VMEM] * 3,
        rest_shapes(split_rows(args[2].shape[0]) - DILATION_STEP, part),
    )(token, *args)


def ends_body(token, halo, pos, valid, past, sig, x_turned, gout, gskip, w_in, w_cond, b_conv, w_res, w_skip, *outs):
    weights = (w_in, w_cond, b_conv, w_res, w_skip)
    rows = sig.shape[0]
    head_rows(1, halo, pos, valid, sig, x_turned, gout, gskip, weights, outs[:3])
    forward_tiles(
        1, tiles_of(split_rows(rows), rows), None, None, valid, past, sig, x_turned, gout, gskip, weights, outs[3:],
        split_rows(rows),
    )


def forward_ends(token, *args):
    part = args[-1].shape[0]
    rows = args[4].shape[0]
    parts = call(
        ends_body,
        "ends_1",
        [ANYWHERE] + [VMEM] * len(args),
        [VMEM] * 6,
        rest_shapes(DILATION_STEP, part) + rest_shapes(rows - split_rows(rows), part),
    )(token, *args)
    return parts[:3], parts[3:]


def own_place():
    return [lax.axis_index(name) for name in ("core", "far", "near")]


def turned(index, count):
    bits = (count - 1).bit_length()
    result = 0
    for bit in range(bits):
        result = result | (((index >> bit) & 1) << (bits - 1 - bit))
    return result


def gradients_body(far, block, half, own, count, extra, token, valid, x_turned, gout, gskip, past_head, *refs):
    kepts, dpres, refs = refs[:count], refs[count : 2 * count], refs[2 * count :]
    sources, (out, *targets) = refs[:extra], refs[extra : len(refs) - 1 - bool(extra)]
    acc = refs[-1 - bool(extra)]
    copies = []
    if extra:
        pairs = weight_copies(1, *sources[:4], *targets[:3]) + list(zip(sources[4:], targets[3:]))
        copies = [pltpu.make_async_copy(*pair, refs[-1].at[k]) for k, pair in enumerate(pairs)]
    for copy in copies:
        copy.start()
    width = past_head.shape[0]
    part = kepts[0].shape[0]
    ends, rows = x_turned.shape
    size = far * block
    core, z, xy = own_place()
    which = core if own else 1 - core

    def product(left_of, rights):
        total, at = None, 0
        for k, right in enumerate(rights):
            here = slice(at, at + right.shape[0])
            made = dot(left_of(here, k), right[...])
            total = made if at == 0 else total + made
            at = here.stop
        return total

    def region(k):
        low, high = k * size, min((k + 1) * size, ends)

        def turned_rows(here, piece):
            if piece == 0 and low < width:
                return below(past_head[low : min(high, width), :], x_turned[width : max(high, width), here])
            return x_turned[low:high, here]

        acc[: high - low, :] = product(turned_rows, dpres)
        at = high - low
        if high == ends:
            mask = jnp.broadcast_to(row(lines_of(valid, slice(0, rows)).astype(F32)).astype(BF16), (ONES, rows))

            def kept_rows(here, piece):
                return below(kepts[piece][...], mask[:, here])

            for i, ref in enumerate((gout, gskip)):
                cuts = [0]
                for kept in kepts:
                    cuts.append(cuts[-1] + kept.shape[1])
                made = product(kept_rows, [ref.at[pl.ds(a, b - a)] for a, b in zip(cuts, cuts[1:])])
                acc[at : at + part, :] = made[:part]
                at += part
                if i == half:
                    acc[high - low + 2 * part : high - low + 2 * part + ONES, :] = made[part:]
            at += ONES
            acc[at:, :] = jnp.zeros((size - at, acc.shape[1]), F32)
        for r in range(far):
            for c in range(NEAR):
                value = acc[r * block : (r + 1) * block, c * LANES : (c + 1) * LANES]
                out[c ^ xy, turned(r ^ z, far)] = value.astype(out.dtype)

    for k in range(2):
        pl.when(which == k)(functools.partial(region, k))
    for copy in copies:
        copy.wait()


def gradients(half, own, token, far, block, valid, x_turned, gout, gskip, past_head, pieces, loads=()):
    packed = (NEAR, far, block, LANES)
    wide = pieces[0][2].shape[1]
    count = len(pieces)
    sources = [in_hbm(x) for x in loads]
    outs = [jax.ShapeDtypeStruct(packed, F32 if own else BF16)]
    scratch = [pltpu.VMEM((far * block, wide), F32)]
    if loads:
        outs += half_weights(loads[0], *loads[2:4]) + [jax.ShapeDtypeStruct(x.shape, x.dtype) for x in loads[4:]]
        scratch.append(pltpu.SemaphoreType.DMA((6 + len(loads[4:]),)))
    return call(
        functools.partial(gradients_body, far, block, half, own, count, len(loads)),
        ("mine" if own else "theirs") + f"_{half}",
        [ANYWHERE] + [VMEM] * (5 + 2 * count) + [ANYWHERE] * len(loads),
        [VMEM] * len(outs),
        outs,
        scratch=scratch,
    )(token, valid, x_turned, gout, gskip, past_head, *(p[1] for p in pieces), *(p[2] for p in pieces), *sources)


def outputs_body(counts, token, valid, sig, w_res_0, w_skip_0, w_res_1, w_skip_1, b_res, b_skip, *refs):
    first, second = refs[: counts[0]], refs[counts[0] : sum(counts)]
    out, skip, mark, rooms, sems = refs[sum(counts) :]
    copies = []
    for i in range(sig.shape[0] // ROWS):
        rows = slice(i * ROWS, (i + 1) * ROWS)
        mask = column(lines_of(valid, rows))
        left, right = picked(first, rows), picked(second, rows)
        branch = dot(left, w_res_0[...]) + dot(right, w_res_1[...]) + b_res[...]
        rooms[i, 0] = (sig[rows, :].astype(F32) + mask * branch).astype(BF16)
        side = dot(left, w_skip_0[...]) + dot(right, w_skip_1[...]) + b_skip[...]
        rooms[i, 1] = (mask * side).astype(BF16)
        for k, ref in enumerate((out, skip)):
            copies.append(pltpu.make_async_copy(rooms.at[i, k], ref.at[pl.ds(i * ROWS, ROWS)], sems.at[i, k]))
            copies[-1].start()
    mark[...] = jnp.zeros_like(mark)
    for copy in copies:
        copy.wait()


def outputs(token, valid, sig, gated_0, gated_1, weights_0, weights_1, b_res, b_skip):
    rows, width = sig.shape
    counts = (len(gated_0), len(gated_1))
    return call(
        functools.partial(outputs_body, counts),
        "outputs",
        [ANYWHERE] + [VMEM] * (8 + sum(counts)),
        [ANYWHERE, ANYWHERE, VMEM],
        [
            jax.ShapeDtypeStruct((rows, width), BF16),
            jax.ShapeDtypeStruct((rows, weights_0[1].shape[1]), BF16),
            MARK,
        ],
        scratch=[
            pltpu.VMEM((rows // ROWS, 2, ROWS, width), BF16),
            pltpu.SemaphoreType.DMA((rows // ROWS, 2)),
        ],
    )(token, valid, sig, *weights_0, *weights_1, b_res, b_skip, *gated_0, *gated_1)


def inputs_body(steps, counts, token, received, gout, pos, w_in_0, w_in_1, w_cond, *refs):
    first, second = refs[: counts[0]], refs[counts[0] : sum(counts)]
    gsig, gfeat, mark, room, room_feat, sems = refs[-6:]
    rows, width = gout.shape
    copies = []
    wide = 2 * LANES

    def copy(source, target):
        copies.append(pltpu.make_async_copy(source, target, sems.at[len(copies)]))
        copies[-1].start()

    for i, step in enumerate(steps):
        begin = step * ROWS
        here = slice(begin, begin + ROWS)
        after = slice(begin + DILATION_STEP, min(begin + DILATION_STEP + ROWS, rows))
        now = [picked(pieces, here) for pieces in (first, second)]
        later = [picked(pieces, after) for pieces in (first, second)]
        tap = column(tap_of(lines_of(pos, after)))
        room_feat[i] = against(w_cond[...], side_by_side(*now))
        copy(room_feat.at[i], gfeat.at[:, pl.ds(begin, ROWS)])
        for k in range(width // wide):
            some = slice(k * wide, (k + 1) * wide)
            tail = tap * (against(later[0], w_in_0[some, :]) + against(later[1], w_in_1[some, :]))
            if tail.shape[0] < ROWS:
                tail = below(tail, received[:, some].astype(F32))
            below_past = slice(width + k * wide, width + (k + 1) * wide)
            own = against(now[0], w_in_0[below_past, :]) + against(now[1], w_in_1[below_past, :])
            room[i, k] = gout[here, some].astype(F32) + own + tail
            copy(room.at[i, k], gsig.at[pl.ds(begin, ROWS), pl.ds(k * wide, wide)])
    mark[...] = jnp.zeros_like(mark)
    for one in copies:
        one.wait()


def inputs(steps, token, received, gout, pos, dpre_0, dpre_1, w_in_0, w_in_1, w_cond, before):
    rows, width = gout.shape
    cond = w_cond.shape[0]
    count = width // (2 * LANES)
    counts = (len(dpre_0), len(dpre_1))
    operands = 7 + sum(counts)
    return call(
        functools.partial(inputs_body, steps, counts),
        f"inputs_{steps[0]}",
        [ANYWHERE] + [VMEM] * (operands - 1) + [ANYWHERE] * len(before),
        [ANYWHERE, ANYWHERE, VMEM],
        [
            jax.ShapeDtypeStruct((rows, width), F32),
            jax.ShapeDtypeStruct((cond, rows), F32),
            MARK,
        ],
        scratch=[
            pltpu.VMEM((len(steps), count, ROWS, 2 * LANES), F32),
            pltpu.VMEM((len(steps), cond, ROWS), F32),
            pltpu.SemaphoreType.DMA((len(steps) * (count + 1),)),
        ],
        aliases={operands + k: k for k in range(len(before))},
    )(token, received, gout, pos, w_in_0, w_in_1, w_cond, *dpre_0, *dpre_1, *before)


SHARES = ((0, 3), (1, 2))


def unpack_body(far, block, token, *refs):
    blocks, arrays, (mark, room) = refs[: 2 * len(SHARES)], refs[-9:-2], refs[-2:]
    mine, theirs = blocks[: len(SHARES)], blocks[len(SHARES) :]
    mark[...] = jnp.zeros_like(mark)
    core, z, xy = own_place()

    @pl.when(pl.program_id(0) == 0)
    def _():
        for k, parts in ((core, mine), (1 - core, theirs)):
            for share, ref in zip(SHARES, parts):
                for i, c in enumerate(share):
                    for r in range(far):
                        rows = pl.ds(pl.multiple_of((k * far + (r ^ z)) * block, 16), block)
                        room[c ^ xy, rows, :] = ref[i, turned(r, far)]

    for j in range(NEAR // 2):
        c = pl.program_id(0) * (NEAR // 2) + j
        here = pl.ds(j * LANES, LANES)
        top = 0
        for ref in arrays:
            count = ref.shape[0]
            size = max(count, ONES)
            ref[:, here] = room[c, top : top + size, :].astype(F32)[:count]
            top += size


def unpack(half, token, far, block, mine, theirs, width, cond, hidden, skip_width, before):
    part = hidden // HALVES
    gates = 2 * hidden
    own = (width, skip_width)[half]

    def wide(size):
        return pl.BlockSpec((size, part), lambda s: (0, HALVES * s + half))

    def tall(size):
        return pl.BlockSpec((part, size // 2), lambda s: (half, s))

    specs = [wide(width), wide(width), wide(cond), wide(1), tall(width), tall(skip_width), pl.BlockSpec((1, own // 2), lambda s: (0, s))]
    shapes = [(width, gates), (width, gates), (cond, gates), (1, gates), (hidden, width), (hidden, skip_width), (1, own)]
    blocks = [pl.BlockSpec(x.shape, lambda s: (0,) * 4) for x in (*mine, *theirs)]
    return call(
        functools.partial(unpack_body, far, block),
        f"unpack_{half}",
        [ANYWHERE, *blocks] + [ANYWHERE] * len(before),
        specs + [pl.BlockSpec(MARK.shape, lambda s: (0, 0))],
        [jax.ShapeDtypeStruct(shape, F32) for shape in shapes] + [MARK],
        scratch=[pltpu.VMEM((NEAR, 2 * far * block, LANES), BF16)],
        aliases={1 + len(blocks) + k: k for k in range(len(before))},
        grid=(2,),
    )(token, *mine, *theirs, *before)


def swapped(x, axis, k):
    return lax.ppermute(x, axis, [(i, i ^ k) for i in range(lax.axis_size(axis))])


def exchanged(blocks):
    return [swapped(block, "near", k + 1) for k, block in enumerate(blocks)]


def add_body(sizes, token, *refs):
    count = len(sizes)
    kept, got, outs = refs[0], refs[1:-count], refs[-count:]
    at = 0
    for out, size in zip(outs, sizes):
        for k in range(size):
            total = kept[at + k].astype(F32)
            for ref in got:
                total = total + ref[at + k].astype(F32)
            out[k] = total.astype(out.dtype)
        at += size


def added(name, token, kept, got, outs):
    sizes = [size for size, _ in outs]
    result = call(
        functools.partial(add_body, sizes),
        name,
        [ANYWHERE] + [VMEM] * (1 + len(got)),
        [VMEM] * len(outs),
        [jax.ShapeDtypeStruct((size, *kept.shape[1:]), dtype) for size, dtype in outs],
    )(token, kept, *got)
    return result


def mirror_body(token, mine, got, out):
    count = mine.shape[0]
    for k in range(count):
        out[k] = (mine[k].astype(F32) + got[count - 1 - k].astype(F32)).astype(out.dtype)


def mirrored(name, token, mine, got):
    return call(
        mirror_body,
        name,
        [ANYWHERE, VMEM, VMEM],
        VMEM,
        jax.ShapeDtypeStruct(mine.shape, BF16),
    )(token, mine, got)


def join_body(token, *refs):
    out = refs[-1]
    at = 0
    for ref in refs[:-1]:
        out[at : at + ref.shape[0]] = ref[...]
        at += ref.shape[0]


def joined(name, token, parts):
    count = sum(part.shape[0] for part in parts)
    return call(
        join_body,
        name,
        [ANYWHERE] + [VMEM] * len(parts),
        VMEM,
        jax.ShapeDtypeStruct((count, *parts[0].shape[1:]), BF16),
    )(token, *parts)


def over_outer(total):
    for bit in range((lax.axis_size("outer") - 1).bit_length()):
        total = (total.astype(F32) + swapped(total, "outer", 1 << bit).astype(F32)).astype(BF16)
    return total


def passed_along(x, by):
    peers = lax.axis_size(AXES)
    pairs = [(i, i + by) for i in range(peers) if 0 <= i + by < peers]
    return lax.ppermute(x, AXES, pairs)


def in_hbm(x):
    return pltpu.with_memory_space_constraint(x, pltpu.HBM)


def body(
    signal,
    features,
    position,
    valid,
    w_past,
    w_now,
    b_conv,
    w_cond,
    w_res,
    b_res,
    w_skip,
    b_skip,
    grad_out,
    grad_skip,
):
    rows, width = signal.shape
    features = features.T
    cond = features.shape[0]
    hidden = w_res.shape[0]
    skip_width = w_skip.shape[1]
    far = lax.axis_size("far")
    far_bits = (far - 1).bit_length()
    used = 2 * width + cond + ONES + 2 * (hidden // HALVES) + ONES
    block = -(-used // (2 * far * 16)) * 16
    lines = (rows // LANES, LANES)
    pos, val = position.reshape(lines), valid.reshape(lines)
    b_conv, b_res, b_skip = (b.reshape(1, -1) for b in (b_conv, b_res, b_skip))

    def core_sum(half, token, theirs, mine):
        kept, *sent = added(
            f"core_sum_{half}", token, mine, [swapped(theirs, "core", 1)], [(1, F32)] + [(1, BF16)] * (NEAR - 1)
        )
        return kept[0], exchanged([x[0] for x in sent])

    def near_sum(half, token, kept, got):
        kept, sent = added(f"near_sum_{half}", token, kept, got, [(far // 2, F32), (far // 2, BF16)])
        return kept, swapped(sent, "far", 1)

    def far_sum(half, token, kept, got):
        for bit in range(1, far_bits - 1):
            size = kept.shape[0] // 2
            kept, sent = added(f"far_sum_{half}_{bit}", token, kept, [got], [(size, F32), (size, BF16)])
            got = swapped(sent, "far", 1 << bit)
        (mine,) = added(f"far_sum_{half}", token, kept, [got], [(kept.shape[0], BF16)])
        return mine, swapped(mine, "far", 1 << (far_bits - 1))

    def far_end(half, token, mine, got):
        total = over_outer(mirrored(f"far_end_{half}", token, mine, got))
        return total, swapped(total, "far", 1 << (far_bits - 2))

    def far_join(half, token, mine, got):
        total = joined(f"far_join_{half}", token, [mine, got])
        for bit in reversed(range(far_bits - 2)):
            total = joined(f"far_join_{half}_{bit}", token, [total, swapped(total, "far", 1 << bit)])
        return total, exchanged([total] * (NEAR - 1))

    def near_join(half, k, token, mine, got):
        blocks = [mine, *got]
        total = joined(f"near_join_{half}_{k}", token, [blocks[c][None] for c in SHARES[k]])
        return total, swapped(total, "core", 1)

    def input_gradients(steps, token, before):
        last = (steps[-1] + 1) * ROWS == rows
        return inputs(steps, token, received if last else head_0[0], grad_out, pos, dpre_0, dpre_1, w_in_0, w_in_1, w_cond, before)

    halo = passed_along(signal[rows - DILATION_STEP :], 1)
    loads = (w_past, w_now, w_res, w_skip, b_res, b_skip)
    val, pos, b_conv, w_cond, w_in_0, *outer_0, past, signal, x_turned, grad_out, grad_skip, a, b, c = load(
        val, pos, b_conv, features, w_cond, w_res, w_skip, w_past, w_now, signal, grad_out, grad_skip
    )
    rest_0 = (a, b, c)
    common = (signal, x_turned, grad_out, grad_skip)
    past_head, head_0 = head(halo, pos, val, *common, w_in_0, w_cond, b_conv, *outer_0)
    made_0 = (head_0, rest_0)
    fixed = (far, block, val, x_turned, grad_out, grad_skip, past_head)
    theirs_0, w_in_1, *outer_1, b_res, b_skip = gradients(0, False, past_head, *fixed, made_0, loads)
    weights_1 = (w_in_1, w_cond, b_conv, *outer_1)
    (mine_0,) = gradients(0, True, theirs_0, *fixed, made_0)
    most_1 = forward_most(mine_0, val, past, *common, *weights_1)
    kept_0, got_0 = core_sum(0, most_1[0], theirs_0, mine_0)
    head_1, last_1 = forward_ends(kept_0, halo, pos, val, past, *common, *weights_1)
    made_1 = (head_1, most_1, last_1)
    dpre_0, dpre_1 = ([p[2] for p in made] for made in (made_0, made_1))
    (theirs_1,) = gradients(1, False, kept_0, *fixed, made_1)
    (mine_1,) = gradients(1, True, theirs_1, *fixed, made_1)
    kept_0, got_0 = near_sum(0, mine_1, kept_0, got_0)
    kept_1, got_1 = core_sum(1, kept_0, theirs_1, mine_1)
    ends_0, got_0 = far_sum(0, kept_1, kept_0, got_0)
    *grads, mark = input_gradients((0, 1), ends_0, [])
    ends_0, got_0 = far_end(0, mark, ends_0, got_0)
    kept_1, got_1 = near_sum(1, ends_0, kept_1, got_1)
    ends_0, got_0 = far_join(0, kept_1, ends_0, got_0)
    ends_1, got_1 = far_sum(1, ends_0, kept_1, got_1)
    *grads, mark = input_gradients((2,), ends_1, grads)
    ends_1, got_1 = far_end(1, mark, ends_1, got_1)
    early = early_rows(ends_1, pos, head_0[2], head_1[2], w_in_0, w_in_1)
    received = passed_along(early, -1)
    first = near_join(0, 0, early, ends_0, got_0)
    second = near_join(0, 1, first[0], ends_0, got_0)
    pairs_0 = [first, second]
    ends_1, got_1 = far_join(1, second[0], ends_1, got_1)
    output, skip_out, mark = outputs(
        ends_1, val, signal, [p[0] for p in made_0], [p[0] for p in made_1], outer_0, outer_1, b_res, b_skip
    )
    *grads, mark = input_gradients((3,), mark, grads)
    first = near_join(1, 0, mark, ends_1, got_1)
    second = near_join(1, 1, first[0], ends_1, got_1)
    pairs_1 = [first, second]
    sizes = (width, cond, hidden, skip_width)
    *done, own_0, mark = unpack(0, first[1], far, block, *zip(*pairs_0), *sizes, [])
    *done, own_1, _ = unpack(1, mark, far, block, *zip(*pairs_1), *sizes, done)
    g_past, g_now, g_cond, g_bias, g_res, g_skip = done
    grad_signal, grad_features = grads
    return (
        output,
        skip_out,
        grad_signal,
        grad_features.T,
        g_past,
        g_now,
        g_bias.reshape(-1),
        g_cond,
        g_res,
        own_0.reshape(-1),
        g_skip,
        own_1.reshape(-1),
    )


def solution(mesh):
    row, col = mesh.shape["row"], mesh.shape["col"]
    fine = Mesh(mesh.devices.reshape(row // 2, 2, col // NEAR, NEAR), AXES)
    rows = P(AXES, None)
    line = P(AXES)
    return jax.shard_map(
        body,
        mesh=fine,
        in_specs=(rows, rows, line, line) + (P(),) * 8 + (rows, rows),
        out_specs=(rows,) * 4 + (P(),) * 8,
        check_vma=False,
    )
```

```python
import functools

import jax
import jax.numpy as jnp
from jax import lax
from jax.experimental import pallas as pl
from jax.experimental.pallas import tpu as pltpu
from jax.sharding import Mesh
from jax.sharding import PartitionSpec as P

DILATION_STEP = 256
AXES = ("outer", "core", "far", "near")
HALVES = 2
NEAR = 4
LANES = 128
ROWS = 512
ONES = 16
F32 = jnp.float32
BF16 = jnp.bfloat16
MEGA = 1 << 20
COSTS = {
    "load": 8, "head": 2, "near_sum_0": 7, "mine_1": 2,
    "near_part_1": 2, "near_sum_1": 4, "near_join_0_0": 2, "near_join_0_1": 2, "near_join_1_1": 4, "far_join_0": 4,
}
FLOPS = 10**9


def dot(left, right):
    return jnp.dot(left, right, preferred_element_type=F32)


def across(left, right):
    return lax.dot_general(left, right, (((0,), (0,)), ((), ())), preferred_element_type=F32)


def against(left, weight):
    return lax.dot_general(left, weight, (((1,), (1,)), ((), ())), preferred_element_type=F32)


def column(lines):
    turned = lines.astype(F32).T
    return jnp.concatenate([turned[:, k : k + 1] for k in range(lines.shape[0])], axis=0)


def row(lines):
    return jnp.concatenate([lines[k : k + 1] for k in range(lines.shape[0])], axis=1)


def tap_of(lines):
    return jnp.where(lines >= DILATION_STEP, 1, 0)


def lines_of(ref, rows):
    return ref[rows.start // LANES : rows.stop // LANES, :]


def picked(pieces, rows):
    found, at = [], 0
    for ref in pieces:
        low, high = max(rows.start, at), min(rows.stop, at + ref.shape[0])
        if low < high:
            found.append(ref[low - at : high - at, :])
        at += ref.shape[0]
    return found[0] if len(found) == 1 else jnp.concatenate(found, axis=0)


def call(kernel, name, in_specs, out_specs, out_shape, scratch=(), aliases=None, grid=(), vmem=24):
    return pl.pallas_call(
        kernel,
        grid=grid,
        in_specs=in_specs,
        out_specs=out_specs,
        out_shape=out_shape,
        scratch_shapes=list(scratch),
        input_output_aliases=aliases or {},
        cost_estimate=pl.CostEstimate(
            flops=1 + int(FLOPS * COSTS.get(name, COSTS.get(name.split("_")[0], 0))), bytes_accessed=1, transcendentals=0
        ),
        name=name,
        compiler_params=pltpu.CompilerParams(vmem_limit_bytes=vmem * MEGA),
    )


VMEM = pl.BlockSpec(memory_space=pltpu.VMEM)
ANYWHERE = pl.BlockSpec(memory_space=pl.ANY)
MARK = jax.ShapeDtypeStruct((8, LANES), F32)


def beside(*parts):
    return jnp.concatenate(parts, axis=1)


def below(*parts):
    return jnp.concatenate(parts, axis=0)


def gate_product(half, k, rows, past, sig, feats, w_in, w_cond, b_conv):
    width = sig.shape[1]
    part = w_in.shape[1] // 2
    here = slice(k * part, (k + 1) * part)
    there = slice((k * HALVES + half) * part, (k * HALVES + half + 1) * part)
    own = dot(past, w_in[:width, here]) + dot(sig[rows, :], w_in[width:, here])
    return own + across(feats, w_cond[:, there]) + b_conv[:, there]


def back_product(rows, gout, gskip, w_res, w_skip):
    return against(gout[rows, :], w_res[...]) + against(gskip[rows, :], w_skip[...])


def weight_copies(half, w_past, w_now, w_res, w_skip, w_in_to, w_res_to, w_skip_to):
    width = w_past.shape[0]
    part = w_res_to.shape[0]
    pairs = []
    for k in range(2):
        here = pl.ds((k * HALVES + half) * part, part)
        for i, ref in enumerate((w_past, w_now)):
            pairs.append((ref.at[:, here], w_in_to.at[pl.ds(i * width, width), pl.ds(k * part, part)]))
    rows = pl.ds(half * part, part)
    return pairs + [(w_res.at[rows], w_res_to), (w_skip.at[rows], w_skip_to)]


def half_weights(w_past, w_res, w_skip):
    part = w_res.shape[0] // HALVES
    shapes = ((2 * w_past.shape[0], 2 * part), (part, w_res.shape[1]), (part, w_skip.shape[1]))
    return [jax.ShapeDtypeStruct(shape, BF16) for shape in shapes]


def finish(pre_a, pre_s, dgated, valid_lines):
    act = jnp.tanh(pre_a)
    gate = 0.5 + 0.5 * jnp.tanh(0.5 * pre_s)
    slope = (column(valid_lines) * dgated) * gate
    dpre = beside(slope * (1.0 - act * act), slope * act * (1.0 - gate)).astype(BF16)
    gated = (act * gate).astype(BF16)
    return gated, gated.T * row(valid_lines.astype(BF16)), dpre


def forward_tiles(half, tiles, prepare, arrive, valid, past, sig, x_turned, gout, gskip, weights, outs, base):
    w_in, w_cond, b_conv, w_res, w_skip = weights
    gated_out, kept_out, dpre_out = outs
    cond = w_cond.shape[0]
    width = sig.shape[1]

    def product(rows, k):
        if arrive:
            arrive(rows, k)
        if k == 2:
            return back_product(rows, gout, gskip, w_res, w_skip)
        feats = x_turned[2 * width : 2 * width + cond, rows]
        return gate_product(half, k, rows, past[rows, :], sig, feats, w_in, w_cond, b_conv)

    def done(rows, made):
        there = slice(rows.start - base, rows.stop - base)
        gated_out[there, :], kept_out[:, there], dpre_out[there, :] = finish(*made, lines_of(valid, rows))

    ahead = None
    for rows in tiles:
        if prepare:
            prepare(rows)
        made = [product(rows, k) for k in range(3)]
        if ahead:
            done(*ahead)
        ahead = (rows, made)
    done(*ahead)


def tiles_of(start, stop):
    return [slice(a, a + DILATION_STEP) for a in range(start, stop, DILATION_STEP)]


def split_rows(rows):
    return 3 * DILATION_STEP


def load_body(
    valid, pos, b_conv, feat, w_cond, w_res, w_skip, w_past, w_now, sig, gout, gskip,
    valid_to, pos_to, b_conv_to, w_cond_to, w_in, w_res_to, w_skip_to, past, sig_to, x_turned,
    gout_to, gskip_to, gated_rest, kept_rest, dpre_rest, sems,
):
    rows_all, width = sig.shape
    cond = feat.shape[0]
    count = 0

    def start(source, target):
        nonlocal count
        copy = pltpu.make_async_copy(source, target, sems.at[count])
        copy.start()
        count += 1
        return copy

    def tile(i, source, target):
        rows = pl.ds(i * ROWS, ROWS)
        return start(source.at[rows], target.at[rows])

    weights = weight_copies(0, w_past, w_now, w_res, w_skip, w_in, w_res_to, w_skip_to)
    signals = [[tile(0, sig, sig_to)]]
    needs = [
        [
            start(pos, pos_to),
            *(start(*pair) for pair in weights[:2]),
            start(feat, x_turned.at[pl.ds(2 * width, cond)]),
            start(w_cond, w_cond_to),
            start(b_conv, b_conv_to),
        ],
        [start(*pair) for pair in weights[2:4]],
        [start(valid, valid_to), *(start(*pair) for pair in weights[4:])],
    ]
    cotangents = [[tile(0, gout, gout_to), tile(0, gskip, gskip_to)]]
    for i in range(1, rows_all // ROWS):
        signals.append([tile(i, sig, sig_to)])
        cotangents.append([tile(i, gout, gout_to), tile(i, gskip, gskip_to)])

    def wait(copies):
        for copy in copies:
            copy.wait()
        copies.clear()

    def prepare(rows):
        i = rows.start // ROWS
        wait(signals[i])
        wait(needs[0])
        whole = rows if i else slice(0, rows.stop)
        before = slice(rows.start - DILATION_STEP, rows.stop - DILATION_STEP)
        tap = tap_of(lines_of(pos_to, rows)).astype(F32)
        past[rows, :] = sig_to[before, :] * column(tap).astype(BF16)
        x_turned[width : 2 * width, whole] = sig_to[whole, :].T
        x_turned[:width, rows] = x_turned[width : 2 * width, before] * row(tap).astype(BF16)

    def arrive(rows, k):
        wait(needs[k])
        if k == 2:
            wait(cotangents[rows.start // ROWS])

    x_turned[2 * width + cond :, :] = jnp.ones((x_turned.shape[0] - 2 * width - cond, rows_all), BF16)
    forward_tiles(
        0, tiles_of(DILATION_STEP, rows_all), prepare, arrive, valid_to, past, sig_to, x_turned, gout_to, gskip_to,
        (w_in, w_cond_to, b_conv_to, w_res_to, w_skip_to), (gated_rest, kept_rest, dpre_rest), DILATION_STEP,
    )


def rest_shapes(rest, part):
    return [jax.ShapeDtypeStruct(shape, BF16) for shape in ((rest, part), (part, rest), (rest, 2 * part))]


def load(*arrays):
    sources = [in_hbm(x) for x in arrays]
    feat, w_cond, w_res, w_skip, w_past, _, sig, gout, gskip = arrays[3:]
    rows, width = sig.shape
    hidden = w_res.shape[0]
    shapes = [jax.ShapeDtypeStruct(x.shape, x.dtype) for x in arrays[:3] + (w_cond,)]
    shapes += half_weights(w_past, w_res, w_skip) + [
        jax.ShapeDtypeStruct(shape, BF16)
        for shape in (
            sig.shape, sig.shape, (2 * width + feat.shape[0] + ONES, rows), gout.shape, gskip.shape,
        )
    ]
    shapes += rest_shapes(rows - DILATION_STEP, hidden // HALVES)
    return call(
        load_body,
        "load",
        [ANYWHERE] * len(sources),
        [VMEM] * len(shapes),
        shapes,
        scratch=[pltpu.SemaphoreType.DMA((11 + 3 * (rows // ROWS),))],
    )(*sources)


def side_by_side(dpre_0, dpre_1):
    part = dpre_0.shape[1] // 2
    return beside(dpre_0[:, :part], dpre_1[:, :part], dpre_0[:, part:], dpre_1[:, part:])


def head_rows(half, halo, pos, valid, sig, x_turned, gout, gskip, weights, outs):
    w_in, w_cond, b_conv, w_res, w_skip = weights
    rows = slice(0, DILATION_STEP)
    width = halo.shape[1]
    feats = x_turned[2 * width : 2 * width + w_cond.shape[0], rows]
    past = halo[...] * column(tap_of(lines_of(pos, rows)).astype(F32)).astype(BF16)
    made = [gate_product(half, k, rows, past, sig, feats, w_in, w_cond, b_conv) for k in range(2)]
    made.append(back_product(rows, gout, gskip, w_res, w_skip))
    for ref, value in zip(outs, finish(*made, lines_of(valid, rows))):
        ref[...] = value


def head_body(halo, pos, valid, sig, x_turned, gout, gskip, w_in, w_cond, b_conv, w_res, w_skip, past_out, *outs):
    tap = tap_of(lines_of(pos, slice(0, DILATION_STEP))).astype(F32)
    past_out[...] = halo[...].T * row(tap).astype(BF16)
    head_rows(0, halo, pos, valid, sig, x_turned, gout, gskip, (w_in, w_cond, b_conv, w_res, w_skip), outs)


def head(halo, *args):
    width = halo.shape[1]
    part = args[-1].shape[0]
    past, *parts = call(
        head_body,
        "head",
        [VMEM] * (1 + len(args)),
        [VMEM] * 4,
        [jax.ShapeDtypeStruct((width, DILATION_STEP), BF16)] + rest_shapes(DILATION_STEP, part),
    )(halo, *args)
    return past, parts


def early_body(token, pos, dpre_0, dpre_1, w_in_0, w_in_1, early):
    tap = column(tap_of(lines_of(pos, slice(0, DILATION_STEP))))
    some = slice(0, early.shape[1])
    early[...] = (tap * (against(dpre_0[...], w_in_0[some, :]) + against(dpre_1[...], w_in_1[some, :]))).astype(BF16)


def early_rows(token, pos, dpre_0, dpre_1, w_in_0, w_in_1):
    return call(
        early_body,
        "early",
        [ANYWHERE] + [VMEM] * 5,
        VMEM,
        jax.ShapeDtypeStruct((DILATION_STEP, w_in_0.shape[0] // 2), BF16),
    )(token, pos, dpre_0, dpre_1, w_in_0, w_in_1)


def most_body(token, valid, past, sig, x_turned, gout, gskip, w_in, w_cond, b_conv, w_res, w_skip, *outs):
    forward_tiles(
        1, tiles_of(DILATION_STEP, split_rows(sig.shape[0])), None, None, valid, past, sig, x_turned, gout, gskip,
        (w_in, w_cond, b_conv, w_res, w_skip), outs, DILATION_STEP,
    )


def forward_most(token, *args):
    part = args[-1].shape[0]
    return call(
        most_body,
        "forward_1",
        [ANYWHERE] + [VMEM] * len(args),
        [VMEM] * 3,
        rest_shapes(split_rows(args[2].shape[0]) - DILATION_STEP, part),
    )(token, *args)


def ends_body(token, halo, pos, valid, past, sig, x_turned, gout, gskip, w_in, w_cond, b_conv, w_res, w_skip, *outs):
    weights = (w_in, w_cond, b_conv, w_res, w_skip)
    rows = sig.shape[0]
    head_rows(1, halo, pos, valid, sig, x_turned, gout, gskip, weights, outs[:3])
    forward_tiles(
        1, tiles_of(split_rows(rows), rows), None, None, valid, past, sig, x_turned, gout, gskip, weights, outs[3:],
        split_rows(rows),
    )


def forward_ends(token, *args):
    part = args[-1].shape[0]
    rows = args[4].shape[0]
    parts = call(
        ends_body,
        "ends_1",
        [ANYWHERE] + [VMEM] * len(args),
        [VMEM] * 6,
        rest_shapes(DILATION_STEP, part) + rest_shapes(rows - split_rows(rows), part),
    )(token, *args)
    return parts[:3], parts[3:]


def own_place():
    return [lax.axis_index(name) for name in ("core", "far", "near")]


def turned(index, count):
    bits = (count - 1).bit_length()
    result = 0
    for bit in range(bits):
        result = result | (((index >> bit) & 1) << (bits - 1 - bit))
    return result


def gradients_body(far, block, half, own, count, extra, token, valid, x_turned, gout, gskip, past_head, *refs):
    kepts, dpres, refs = refs[:count], refs[count : 2 * count], refs[2 * count :]
    sources, (out, *targets) = refs[:extra], refs[extra : len(refs) - 1 - bool(extra)]
    acc = refs[-1 - bool(extra)]
    copies = []
    if extra:
        pairs = weight_copies(1, *sources[:4], *targets[:3]) + list(zip(sources[4:], targets[3:]))
        copies = [pltpu.make_async_copy(*pair, refs[-1].at[k]) for k, pair in enumerate(pairs)]
    for copy in copies:
        copy.start()
    width = past_head.shape[0]
    part = kepts[0].shape[0]
    ends, rows = x_turned.shape
    size = far * block
    core, z, xy = own_place()
    which = core if own else 1 - core

    def product(left_of, rights):
        total, at = None, 0
        for k, right in enumerate(rights):
            here = slice(at, at + right.shape[0])
            made = dot(left_of(here, k), right[...])
            total = made if at == 0 else total + made
            at = here.stop
        return total

    def region(k):
        low, high = k * size, min((k + 1) * size, ends)

        def turned_rows(here, piece):
            if piece == 0 and low < width:
                return below(past_head[low : min(high, width), :], x_turned[width : max(high, width), here])
            return x_turned[low:high, here]

        acc[: high - low, :] = product(turned_rows, dpres)
        at = high - low
        if high == ends:
            mask = jnp.broadcast_to(row(lines_of(valid, slice(0, rows)).astype(F32)).astype(BF16), (ONES, rows))

            def kept_rows(here, piece):
                return below(kepts[piece][...], mask[:, here])

            for i, ref in enumerate((gout, gskip)):
                cuts = [0]
                for kept in kepts:
                    cuts.append(cuts[-1] + kept.shape[1])
                made = product(kept_rows, [ref.at[pl.ds(a, b - a)] for a, b in zip(cuts, cuts[1:])])
                acc[at : at + part, :] = made[:part]
                at += part
                if i == half:
                    acc[high - low + 2 * part : high - low + 2 * part + ONES, :] = made[part:]
            at += ONES
            acc[at:, :] = jnp.zeros((size - at, acc.shape[1]), F32)
        for r in range(far):
            for c in range(NEAR):
                value = acc[r * block : (r + 1) * block, c * LANES : (c + 1) * LANES]
                out[c ^ xy, turned(r ^ z, far)] = value.astype(out.dtype)

    for k in range(2):
        pl.when(which == k)(functools.partial(region, k))
    for copy in copies:
        copy.wait()


def gradients(half, own, token, far, block, valid, x_turned, gout, gskip, past_head, pieces, loads=()):
    packed = (NEAR, far, block, LANES)
    wide = pieces[0][2].shape[1]
    count = len(pieces)
    sources = [in_hbm(x) for x in loads]
    outs = [jax.ShapeDtypeStruct(packed, F32 if own else BF16)]
    scratch = [pltpu.VMEM((far * block, wide), F32)]
    if loads:
        outs += half_weights(loads[0], *loads[2:4]) + [jax.ShapeDtypeStruct(x.shape, x.dtype) for x in loads[4:]]
        scratch.append(pltpu.SemaphoreType.DMA((6 + len(loads[4:]),)))
    return call(
        functools.partial(gradients_body, far, block, half, own, count, len(loads)),
        ("mine" if own else "theirs") + f"_{half}",
        [ANYWHERE] + [VMEM] * (5 + 2 * count) + [ANYWHERE] * len(loads),
        [VMEM] * len(outs),
        outs,
        scratch=scratch,
    )(token, valid, x_turned, gout, gskip, past_head, *(p[1] for p in pieces), *(p[2] for p in pieces), *sources)


def outputs_body(counts, token, valid, sig, w_res_0, w_skip_0, w_res_1, w_skip_1, b_res, b_skip, *refs):
    first, second = refs[: counts[0]], refs[counts[0] : sum(counts)]
    out, skip, mark, rooms, sems = refs[sum(counts) :]
    copies = []
    for i in range(sig.shape[0] // ROWS):
        rows = slice(i * ROWS, (i + 1) * ROWS)
        mask = column(lines_of(valid, rows))
        left, right = picked(first, rows), picked(second, rows)
        branch = dot(left, w_res_0[...]) + dot(right, w_res_1[...]) + b_res[...]
        rooms[i, 0] = (sig[rows, :].astype(F32) + mask * branch).astype(BF16)
        side = dot(left, w_skip_0[...]) + dot(right, w_skip_1[...]) + b_skip[...]
        rooms[i, 1] = (mask * side).astype(BF16)
        for k, ref in enumerate((out, skip)):
            copies.append(pltpu.make_async_copy(rooms.at[i, k], ref.at[pl.ds(i * ROWS, ROWS)], sems.at[i, k]))
            copies[-1].start()
    mark[...] = jnp.zeros_like(mark)
    for copy in copies:
        copy.wait()


def outputs(token, valid, sig, gated_0, gated_1, weights_0, weights_1, b_res, b_skip):
    rows, width = sig.shape
    counts = (len(gated_0), len(gated_1))
    return call(
        functools.partial(outputs_body, counts),
        "outputs",
        [ANYWHERE] + [VMEM] * (8 + sum(counts)),
        [ANYWHERE, ANYWHERE, VMEM],
        [
            jax.ShapeDtypeStruct((rows, width), BF16),
            jax.ShapeDtypeStruct((rows, weights_0[1].shape[1]), BF16),
            MARK,
        ],
        scratch=[
            pltpu.VMEM((rows // ROWS, 2, ROWS, width), BF16),
            pltpu.SemaphoreType.DMA((rows // ROWS, 2)),
        ],
    )(token, valid, sig, *weights_0, *weights_1, b_res, b_skip, *gated_0, *gated_1)


def inputs_body(steps, counts, token, received, gout, pos, w_in_0, w_in_1, w_cond, *refs):
    first, second = refs[: counts[0]], refs[counts[0] : sum(counts)]
    gsig, gfeat, mark, room, room_feat, sems = refs[-6:]
    rows, width = gout.shape
    copies = []
    wide = 2 * LANES

    def copy(source, target):
        copies.append(pltpu.make_async_copy(source, target, sems.at[len(copies)]))
        copies[-1].start()

    for i, step in enumerate(steps):
        begin = step * ROWS
        here = slice(begin, begin + ROWS)
        after = slice(begin + DILATION_STEP, min(begin + DILATION_STEP + ROWS, rows))
        now = [picked(pieces, here) for pieces in (first, second)]
        later = [picked(pieces, after) for pieces in (first, second)]
        tap = column(tap_of(lines_of(pos, after)))
        room_feat[i] = against(w_cond[...], side_by_side(*now))
        copy(room_feat.at[i], gfeat.at[:, pl.ds(begin, ROWS)])
        for k in range(width // wide):
            some = slice(k * wide, (k + 1) * wide)
            tail = tap * (against(later[0], w_in_0[some, :]) + against(later[1], w_in_1[some, :]))
            if tail.shape[0] < ROWS:
                tail = below(tail, received[:, some].astype(F32))
            below_past = slice(width + k * wide, width + (k + 1) * wide)
            own = against(now[0], w_in_0[below_past, :]) + against(now[1], w_in_1[below_past, :])
            room[i, k] = gout[here, some].astype(F32) + own + tail
            copy(room.at[i, k], gsig.at[pl.ds(begin, ROWS), pl.ds(k * wide, wide)])
    mark[...] = jnp.zeros_like(mark)
    for one in copies:
        one.wait()


def inputs(steps, token, received, gout, pos, dpre_0, dpre_1, w_in_0, w_in_1, w_cond, before):
    rows, width = gout.shape
    cond = w_cond.shape[0]
    count = width // (2 * LANES)
    counts = (len(dpre_0), len(dpre_1))
    operands = 7 + sum(counts)
    return call(
        functools.partial(inputs_body, steps, counts),
        f"inputs_{steps[0]}",
        [ANYWHERE] + [VMEM] * (operands - 1) + [ANYWHERE] * len(before),
        [ANYWHERE, ANYWHERE, VMEM],
        [
            jax.ShapeDtypeStruct((rows, width), F32),
            jax.ShapeDtypeStruct((cond, rows), F32),
            MARK,
        ],
        scratch=[
            pltpu.VMEM((len(steps), count, ROWS, 2 * LANES), F32),
            pltpu.VMEM((len(steps), cond, ROWS), F32),
            pltpu.SemaphoreType.DMA((len(steps) * (count + 1),)),
        ],
        aliases={operands + k: k for k in range(len(before))},
    )(token, received, gout, pos, w_in_0, w_in_1, w_cond, *dpre_0, *dpre_1, *before)


SHARES = ((0, 3), (1, 2))


def unpack_body(far, block, token, *refs):
    blocks, arrays, (mark, room) = refs[: 2 * len(SHARES)], refs[-9:-2], refs[-2:]
    mine, theirs = blocks[: len(SHARES)], blocks[len(SHARES) :]
    mark[...] = jnp.zeros_like(mark)
    core, z, xy = own_place()

    @pl.when(pl.program_id(0) == 0)
    def _():
        for k, parts in ((core, mine), (1 - core, theirs)):
            for share, ref in zip(SHARES, parts):
                for i, c in enumerate(share):
                    for r in range(far):
                        rows = pl.ds(pl.multiple_of((k * far + (r ^ z)) * block, 16), block)
                        room[c ^ xy, rows, :] = ref[i, turned(r, far)]

    for j in range(NEAR // 2):
        c = pl.program_id(0) * (NEAR // 2) + j
        here = pl.ds(j * LANES, LANES)
        top = 0
        for ref in arrays:
            count = ref.shape[0]
            size = max(count, ONES)
            ref[:, here] = room[c, top : top + size, :].astype(F32)[:count]
            top += size


def unpack(half, token, far, block, mine, theirs, width, cond, hidden, skip_width, before):
    part = hidden // HALVES
    gates = 2 * hidden
    own = (width, skip_width)[half]

    def wide(size):
        return pl.BlockSpec((size, part), lambda s: (0, HALVES * s + half))

    def tall(size):
        return pl.BlockSpec((part, size // 2), lambda s: (half, s))

    specs = [wide(width), wide(width), wide(cond), wide(1), tall(width), tall(skip_width), pl.BlockSpec((1, own // 2), lambda s: (0, s))]
    shapes = [(width, gates), (width, gates), (cond, gates), (1, gates), (hidden, width), (hidden, skip_width), (1, own)]
    blocks = [pl.BlockSpec(x.shape, lambda s: (0,) * 4) for x in (*mine, *theirs)]
    return call(
        functools.partial(unpack_body, far, block),
        f"unpack_{half}",
        [ANYWHERE, *blocks] + [ANYWHERE] * len(before),
        specs + [pl.BlockSpec(MARK.shape, lambda s: (0, 0))],
        [jax.ShapeDtypeStruct(shape, F32) for shape in shapes] + [MARK],
        scratch=[pltpu.VMEM((NEAR, 2 * far * block, LANES), BF16)],
        aliases={1 + len(blocks) + k: k for k in range(len(before))},
        grid=(2,),
    )(token, *mine, *theirs, *before)


def swapped(x, axis, k):
    return lax.ppermute(x, axis, [(i, i ^ k) for i in range(lax.axis_size(axis))])


def exchanged(blocks):
    return [swapped(block, "near", k + 1) for k, block in enumerate(blocks)]


def add_body(sizes, token, *refs):
    count = len(sizes)
    kept, got, outs = refs[0], refs[1:-count], refs[-count:]
    at = 0
    for out, size in zip(outs, sizes):
        for k in range(size):
            total = kept[at + k].astype(F32)
            for ref in got:
                total = total + ref[at + k].astype(F32)
            out[k] = total.astype(out.dtype)
        at += size


def added(name, token, kept, got, outs):
    sizes = [size for size, _ in outs]
    result = call(
        functools.partial(add_body, sizes),
        name,
        [ANYWHERE] + [VMEM] * (1 + len(got)),
        [VMEM] * len(outs),
        [jax.ShapeDtypeStruct((size, *kept.shape[1:]), dtype) for size, dtype in outs],
    )(token, kept, *got)
    return result


def mirror_body(token, mine, got, out):
    count = mine.shape[0]
    for k in range(count):
        out[k] = (mine[k].astype(F32) + got[count - 1 - k].astype(F32)).astype(out.dtype)


def mirrored(name, token, mine, got):
    return call(
        mirror_body,
        name,
        [ANYWHERE, VMEM, VMEM],
        VMEM,
        jax.ShapeDtypeStruct(mine.shape, BF16),
    )(token, mine, got)


def join_body(token, *refs):
    out = refs[-1]
    at = 0
    for ref in refs[:-1]:
        out[at : at + ref.shape[0]] = ref[...]
        at += ref.shape[0]


def joined(name, token, parts):
    count = sum(part.shape[0] for part in parts)
    return call(
        join_body,
        name,
        [ANYWHERE] + [VMEM] * len(parts),
        VMEM,
        jax.ShapeDtypeStruct((count, *parts[0].shape[1:]), BF16),
    )(token, *parts)


def over_outer(total):
    for bit in range((lax.axis_size("outer") - 1).bit_length()):
        total = (total.astype(F32) + swapped(total, "outer", 1 << bit).astype(F32)).astype(BF16)
    return total


def passed_along(x, by):
    peers = lax.axis_size(AXES)
    pairs = [(i, i + by) for i in range(peers) if 0 <= i + by < peers]
    return lax.ppermute(x, AXES, pairs)


def in_hbm(x):
    return pltpu.with_memory_space_constraint(x, pltpu.HBM)


def body(
    signal,
    features,
    position,
    valid,
    w_past,
    w_now,
    b_conv,
    w_cond,
    w_res,
    b_res,
    w_skip,
    b_skip,
    grad_out,
    grad_skip,
):
    rows, width = signal.shape
    features = features.T
    cond = features.shape[0]
    hidden = w_res.shape[0]
    skip_width = w_skip.shape[1]
    far = lax.axis_size("far")
    far_bits = (far - 1).bit_length()
    used = 2 * width + cond + ONES + 2 * (hidden // HALVES) + ONES
    block = -(-used // (2 * far * 16)) * 16
    lines = (rows // LANES, LANES)
    pos, val = position.reshape(lines), valid.reshape(lines)
    b_conv, b_res, b_skip = (b.reshape(1, -1) for b in (b_conv, b_res, b_skip))

    def core_sum(half, token, theirs, mine):
        kept, *sent = added(
            f"core_sum_{half}", token, mine, [swapped(theirs, "core", 1)], [(1, F32)] + [(1, BF16)] * (NEAR - 1)
        )
        return kept[0], exchanged([x[0] for x in sent])

    def near_sum(half, token, kept, got):
        kept, sent = added(f"near_sum_{half}", token, kept, got, [(far // 2, F32), (far // 2, BF16)])
        return kept, swapped(sent, "far", 1)

    def far_sum(half, token, kept, got):
        for bit in range(1, far_bits - 1):
            size = kept.shape[0] // 2
            kept, sent = added(f"far_sum_{half}_{bit}", token, kept, [got], [(size, F32), (size, BF16)])
            got = swapped(sent, "far", 1 << bit)
        (mine,) = added(f"far_sum_{half}", token, kept, [got], [(kept.shape[0], BF16)])
        return mine, swapped(mine, "far", 1 << (far_bits - 1))

    def far_end(half, token, mine, got):
        total = over_outer(mirrored(f"far_end_{half}", token, mine, got))
        return total, swapped(total, "far", 1 << (far_bits - 2))

    def far_join(half, token, mine, got):
        total = joined(f"far_join_{half}", token, [mine, got])
        for bit in reversed(range(far_bits - 2)):
            total = joined(f"far_join_{half}_{bit}", token, [total, swapped(total, "far", 1 << bit)])
        return total, exchanged([total] * (NEAR - 1))

    def near_join(half, k, token, mine, got):
        blocks = [mine, *got]
        total = joined(f"near_join_{half}_{k}", token, [blocks[c][None] for c in SHARES[k]])
        return total, swapped(total, "core", 1)

    def input_gradients(steps, token, before):
        last = (steps[-1] + 1) * ROWS == rows
        return inputs(steps, token, received if last else head_0[0], grad_out, pos, dpre_0, dpre_1, w_in_0, w_in_1, w_cond, before)

    halo = passed_along(signal[rows - DILATION_STEP :], 1)
    loads = (w_past, w_now, w_res, w_skip, b_res, b_skip)
    val, pos, b_conv, w_cond, w_in_0, *outer_0, past, signal, x_turned, grad_out, grad_skip, a, b, c = load(
        val, pos, b_conv, features, w_cond, w_res, w_skip, w_past, w_now, signal, grad_out, grad_skip
    )
    rest_0 = (a, b, c)
    common = (signal, x_turned, grad_out, grad_skip)
    past_head, head_0 = head(halo, pos, val, *common, w_in_0, w_cond, b_conv, *outer_0)
    made_0 = (head_0, rest_0)
    fixed = (far, block, val, x_turned, grad_out, grad_skip, past_head)
    theirs_0, w_in_1, *outer_1, b_res, b_skip = gradients(0, False, past_head, *fixed, made_0, loads)
    weights_1 = (w_in_1, w_cond, b_conv, *outer_1)
    (mine_0,) = gradients(0, True, theirs_0, *fixed, made_0)
    most_1 = forward_most(mine_0, val, past, *common, *weights_1)
    kept_0, got_0 = core_sum(0, most_1[0], theirs_0, mine_0)
    head_1, last_1 = forward_ends(kept_0, halo, pos, val, past, *common, *weights_1)
    made_1 = (head_1, most_1, last_1)
    dpre_0, dpre_1 = ([p[2] for p in made] for made in (made_0, made_1))
    (theirs_1,) = gradients(1, False, kept_0, *fixed, made_1)
    (mine_1,) = gradients(1, True, theirs_1, *fixed, made_1)
    kept_0, got_0 = near_sum(0, mine_1, kept_0, got_0)
    kept_1, got_1 = core_sum(1, kept_0, theirs_1, mine_1)
    ends_0, got_0 = far_sum(0, kept_1, kept_0, got_0)
    *grads, mark = input_gradients((0, 1), ends_0, [])
    ends_0, got_0 = far_end(0, mark, ends_0, got_0)
    (part,) = added("near_part_1", ends_0, got_1[2], [got_1[1]], [(far, F32)])
    kept_1, got_1 = near_sum(1, part, kept_1, [part, got_1[0]])
    ends_0, got_0 = far_join(0, kept_1, ends_0, got_0)
    ends_1, got_1 = far_sum(1, ends_0, kept_1, got_1)
    *grads, mark = input_gradients((2,), ends_1, grads)
    ends_1, got_1 = far_end(1, mark, ends_1, got_1)
    early = early_rows(ends_1, pos, head_0[2], head_1[2], w_in_0, w_in_1)
    received = passed_along(early, -1)
    first = near_join(0, 0, early, ends_0, got_0)
    second = near_join(0, 1, first[0], ends_0, got_0)
    pairs_0 = [first, second]
    ends_1, got_1 = far_join(1, second[0], ends_1, got_1)
    output, skip_out, mark = outputs(
        ends_1, val, signal, [p[0] for p in made_0], [p[0] for p in made_1], outer_0, outer_1, b_res, b_skip
    )
    *grads, mark = input_gradients((3,), mark, grads)
    first = near_join(1, 0, mark, ends_1, got_1)
    second = near_join(1, 1, first[0], ends_1, got_1)
    pairs_1 = [first, second]
    sizes = (width, cond, hidden, skip_width)
    *done, own_0, mark = unpack(0, first[1], far, block, *zip(*pairs_0), *sizes, [])
    *done, own_1, _ = unpack(1, mark, far, block, *zip(*pairs_1), *sizes, done)
    g_past, g_now, g_cond, g_bias, g_res, g_skip = done
    grad_signal, grad_features = grads
    return (
        output,
        skip_out,
        grad_signal,
        grad_features.T,
        g_past,
        g_now,
        g_bias.reshape(-1),
        g_cond,
        g_res,
        own_0.reshape(-1),
        g_skip,
        own_1.reshape(-1),
    )


def solution(mesh):
    row, col = mesh.shape["row"], mesh.shape["col"]
    fine = Mesh(mesh.devices.reshape(row // 2, 2, col // NEAR, NEAR), AXES)
    rows = P(AXES, None)
    line = P(AXES)
    return jax.shard_map(
        body,
        mesh=fine,
        in_specs=(rows, rows, line, line) + (P(),) * 8 + (rows, rows),
        out_specs=(rows,) * 4 + (P(),) * 8,
        check_vma=False,
    )
```
